32 devices in a mesh: blk: 4 (over y, core), batch: 8 (over z, x).
Axes of the slice: x: 2, y: 2, z: 4, core: 2. Of those that a mesh axis runs over, the one named last changes fastest.
Arguments:
- tokens: bfloat16 [32, 512, 768], P('batch', 'blk'), may hold values from -6 to 6
- cotangent: bfloat16 [32, 512, 768], P('batch', 'blk'), may hold values from -6 to 6
- span_mask: int32 [32, 512], P('batch', 'blk'), may hold values from 0 to 1, as said below
- attention_weight: float32 [4, 768, 768], P(None, 'blk', 'batch'), may hold values from -2 to 2
- expand_weight: float32 [768, 3072], P('blk', 'batch'), may hold values from -0.21875 to 0.21875
- reduce_weight: float32 [3072, 768], P('blk', 'batch'), may hold values from -0.109375 to 0.109375
- vectors: float32 [12, 768], P('blk', 'batch'), may hold values from -2 to 2
- attention_first: float32 [4, 768, 768], P(None, 'blk', 'batch'), may hold values from -40 to 40
- attention_second: float32 [4, 768, 768], P(None, 'blk', 'batch'), may hold values from 0 to 11
- expand_first: float32 [768, 3072], P('blk', 'batch'), may hold values from -40 to 40
- expand_second: float32 [768, 3072], P('blk', 'batch'), may hold values from 0 to 11
- reduce_first: float32 [3072, 768], P('blk', 'batch'), may hold values from -40 to 40
- reduce_second: float32 [3072, 768], P('blk', 'batch'), may hold values from 0 to 11
- vector_first: float32 [12, 768], P('blk', 'batch'), may hold values from -40 to 40
- vector_second: float32 [12, 768], P('blk', 'batch'), may hold values from 0 to 11
Outputs:
- out_tokens: bfloat16 [32, 512, 768], P('batch', 'blk')
- input_grad: float32 [32, 512, 768], P('batch', 'blk')
- attention_new: float32 [4, 768, 768], P(None, 'blk', 'batch')
- attention_moment_one: float32 [4, 768, 768], P(None, 'blk', 'batch')
- attention_moment_two: float32 [4, 768, 768], P(None, 'blk', 'batch')
- expand_new: float32 [768, 3072], P('blk', 'batch')
- expand_moment_one: float32 [768, 3072], P('blk', 'batch')
- expand_moment_two: float32 [768, 3072], P('blk', 'batch')
- reduce_new: float32 [3072, 768], P('blk', 'batch')
- reduce_moment_one: float32 [3072, 768], P('blk', 'batch')
- reduce_moment_two: float32 [3072, 768], P('blk', 'batch')
- vector_new: float32 [12, 768], P('blk', 'batch')
- vector_moment_one: float32 [12, 768], P('blk', 'batch')
- vector_moment_two: float32 [12, 768], P('blk', 'batch')
The draws below stay inside these ranges and needn't reach their ends.
Inputs may be any that keep to these rules, and one draw needn't show every extreme that they name: `span_mask`: 1 marks a character inside a masked span; spans are aligned runs of 8 characters, each masked with a probability of 5 to 25 percent drawn for its row.
All inputs are finite; a program needn't handle non-finite values.
Results may differ from the reference program's by a relative error of at most 0.019.
Values may be sent and summed in bfloat16 or wider, within the bound.
A program may use at most 192 MiB of HBM per device.

```python
import math
import jax
import jax.numpy as jnp
from jax import lax

D = 768
HEADS = 12
HEAD = 64
FF = 3072
LEN = 512
SPAN = 8
STEP = 10
SEQS = 32
TOKENS = 16384


def state_first(key, shape, size):
    return jnp.clip(jax.random.normal(key, shape, jnp.float32), -4.0, 4.0) * (size / 9.0)


def state_second(key, shape, size):
    factor = jnp.exp(jax.random.uniform(key, shape, jnp.float32, 0.0, math.log(4.0)))
    return factor * (size * size * 0.001 / 0.999)


def draw_span_mask(key, part):
    key = jax.random.fold_in(key, 5)
    key_rate, key_roll = jax.random.split(key)
    share = jax.random.randint(key_rate, (SEQS, 1), 5, 26)
    rolls = jax.random.randint(key_roll, (SEQS, LEN // SPAN), 0, 100)
    marked = (rolls < share).astype(jnp.int32)
    return jnp.repeat(marked, SPAN, axis=1)


def draw_attention_weight(key, part):
    key = jax.random.fold_in(key, 1)
    raw = jnp.clip(jax.random.normal(key, (4, D, D), jnp.float32), -4.0, 4.0)
    scales = jnp.array([1.4, 1.4, 1.0, 3.0], jnp.float32) / math.sqrt(D)
    return raw * scales[:, None, None]


def draw_vectors(key, part):
    key = jax.random.fold_in(key, 2)
    raw = jnp.clip(jax.random.normal(key, (12, D), jnp.float32), -4.0, 4.0)
    rows = jnp.arange(12)[:, None]
    is_gain = (rows == 0) | (rows == 5)
    return jnp.where(is_gain, 1.0 + 0.15 * raw, 0.3 * raw)


def draw_attention_first(key, part):
    key = jax.random.fold_in(key, 11)
    return state_first(key, (4, D, D), 0.2 * math.sqrt(TOKENS))


def draw_attention_second(key, part):
    key = jax.random.fold_in(key, 12)
    return state_second(key, (4, D, D), 0.2 * math.sqrt(TOKENS))


def draw_expand_first(key, part):
    key = jax.random.fold_in(key, 13)
    return state_first(key, (D, FF), 0.1 * math.sqrt(TOKENS))


def draw_expand_second(key, part):
    key = jax.random.fold_in(key, 14)
    return state_second(key, (D, FF), 0.1 * math.sqrt(TOKENS))


def draw_reduce_first(key, part):
    key = jax.random.fold_in(key, 15)
    return state_first(key, (FF, D), 0.2 * math.sqrt(TOKENS))


def draw_reduce_second(key, part):
    key = jax.random.fold_in(key, 16)
    return state_second(key, (FF, D), 0.2 * math.sqrt(TOKENS))


def draw_vector_first(key, part):
    key = jax.random.fold_in(key, 17)
    return state_first(key, (12, D), 0.4 * math.sqrt(TOKENS))


def draw_vector_second(key, part):
    key = jax.random.fold_in(key, 18)
    return state_second(key, (12, D), 0.4 * math.sqrt(TOKENS))


def level_of(stream_key, dims, cuts, smallest, top_value):
    def one(dim, shards_of):
        draws = jax.random.uniform(jax.random.fold_in(jax.random.fold_in(stream_key, 6), dim), (shards_of,), jnp.float32, smallest / len(cuts), top_value / len(cuts))
        return jnp.repeat(jnp.exp(draws), dims[dim] // shards_of).reshape((-1,) + (1,) * (len(dims) - dim - 1))

    gain = one(*cuts[0])
    for cut in cuts[1:]:
        gain = gain * one(*cut)
    return gain


def bell_draw(rng, extent, spread, bound, shards=(), kind=jnp.bfloat16):
    values = jax.random.normal(rng, extent, jnp.float32) * spread
    if len(shards) > 0:
        values = level_of(rng, extent, shards, -0.22, 0.18) * values
    return jnp.clip(values, min=-bound, max=bound).astype(kind)


def setup_inputs(seed: int = 0) -> dict:
    seeds = jax.random.split(jax.random.key(seed), 16)
    return {
        "tokens": bell_draw(seeds[0], (SEQS, LEN, D), 1.0, 6.0, ((0, 8), (1, 4))),
        "cotangent": bell_draw(seeds[1], (SEQS, LEN, D), 1.0, 6.0, ((0, 8), (1, 4))),
        "span_mask": draw_span_mask(jax.random.fold_in(seeds[15], 71), 0),
        "attention_weight": draw_attention_weight(jax.random.fold_in(seeds[15], 71), 0),
        "expand_weight": bell_draw(seeds[4], (D, FF), D ** -0.5, 0.21875, ((0, 4), (1, 8)), jnp.float32),
        "reduce_weight": bell_draw(seeds[5], (FF, D), FF ** -0.5, 0.109375, ((0, 4), (1, 8)), jnp.float32),
        "vectors": draw_vectors(jax.random.fold_in(seeds[15], 71), 0),
        "attention_first": draw_attention_first(jax.random.fold_in(seeds[15], 71), 0),
        "attention_second": draw_attention_second(jax.random.fold_in(seeds[15], 71), 0),
        "expand_first": draw_expand_first(jax.random.fold_in(seeds[15], 71), 0),
        "expand_second": draw_expand_second(jax.random.fold_in(seeds[15], 71), 0),
        "reduce_first": draw_reduce_first(jax.random.fold_in(seeds[15], 71), 0),
        "reduce_second": draw_reduce_second(jax.random.fold_in(seeds[15], 71), 0),
        "vector_first": draw_vector_first(jax.random.fold_in(seeds[15], 71), 0),
        "vector_second": draw_vector_second(jax.random.fold_in(seeds[15], 71), 0),
    }


@jax.custom_vjp
def low(v):
    return lax.optimization_barrier(v.astype(jnp.bfloat16)).astype(jnp.float32)

@jax.custom_vjp
def low_back(v):
    return v

def low_keep(v):
    return (low(v), None)

def low_pass(kept, grad):
    return (grad,)

def back_keep(v):
    return (v, None)

def back_low(kept, grad):
    return (low(grad),)
low.defvjp(low_keep, low_pass)
low_back.defvjp(back_keep, back_low)
norm_epsilon = 1e-05
beta_one = 0.9
beta_two = 0.999
adam_epsilon = 1e-08
decay_weight = 0.1
rate_attention = 0.05
rate_expand = 0.03
rate_reduce = 0.015
rate_vector = 0.4

def layer_norm(value, gain_row, bias_row):
    average = lax.optimization_barrier(jnp.mean(value, axis=-1, keepdims=True))
    centered = value - average
    variance = lax.optimization_barrier(jnp.mean(centered * centered, axis=-1, keepdims=True))
    return centered * lax.rsqrt(variance + norm_epsilon) * gain_row + bias_row

def matmul_high(left, right):
    return jnp.matmul(left, right, precision=lax.Precision.HIGHEST)

def adamw(weight, moment_one, moment_two, gradient, step_rate):
    moment_one = beta_one * moment_one + (1.0 - beta_one) * gradient
    moment_two = beta_two * moment_two + (1.0 - beta_two) * gradient * gradient
    corrected_one = moment_one / (1.0 - beta_one ** STEP)
    corrected_two = moment_two / (1.0 - beta_two ** STEP)
    updated = weight - step_rate * (corrected_one / (jnp.sqrt(corrected_two) + adam_epsilon) + decay_weight * weight)
    return (updated, moment_one, moment_two)

def forward(inputs, attention_weight, expand_weight, reduce_weight, vectors):
    attention = low(attention_weight)
    expand = low(expand_weight)
    shrink = low(reduce_weight)
    vec_low = low(vectors)
    group_size, length, width = inputs.shape
    normed = low(layer_norm(inputs, vec_low[0], vec_low[1]))
    queries = low(low_back(matmul_high(normed, attention[0]) + vec_low[2])).reshape(group_size, length, HEADS, HEAD)
    key_rows = low(low_back(matmul_high(normed, attention[1]))).reshape(group_size, length, HEADS, HEAD)
    value_rows = low(low_back(matmul_high(normed, attention[2]) + vec_low[3])).reshape(group_size, length, HEADS, HEAD)
    scores = low_back(jnp.einsum('gqhd,gkhd->ghqk', queries, key_rows, precision=lax.Precision.HIGHEST) * HEAD ** (-0.5))
    highest = lax.optimization_barrier(jnp.max(scores, axis=-1, keepdims=True))
    expo = jnp.exp(scores - highest)
    probs = low(expo / lax.optimization_barrier(jnp.sum(expo, axis=-1, keepdims=True)))
    mixed = jnp.einsum('ghqk,gkhd->gqhd', probs, value_rows, precision=lax.Precision.HIGHEST)
    mixed = low(low_back(mixed.reshape(group_size, length, width)))
    branch = low_back(matmul_high(mixed, attention[3]) + vec_low[4])
    hidden = inputs + branch
    normed_two = low(layer_norm(hidden, vec_low[5], vec_low[6]))
    inner = low_back(matmul_high(normed_two, expand) + vec_low[8:12].reshape(FF))
    activated = low(jax.nn.gelu(inner, approximate=True))
    return hidden + low_back(matmul_high(activated, shrink) + vec_low[7])

def reference(tokens, cotangent, span_mask, attention_weight, expand_weight, reduce_weight, vectors, attention_first, attention_second, expand_first, expand_second, reduce_first, reduce_second, vector_first, vector_second):
    group = max(1, min(SEQS, 4096 // LEN))
    count = SEQS // group
    inputs = tokens.astype(jnp.float32).reshape(count, group, LEN, D)
    incoming = (cotangent.astype(jnp.float32) * span_mask[..., None].astype(jnp.float32)).reshape(count, group, LEN, D)
    parameters = (attention_weight, expand_weight, reduce_weight, vectors)

    def group_step(carry_in, group_item):
        group_in, group_cot = group_item
        result, pullback = jax.vjp(forward, group_in, *parameters)
        gradients = pullback(group_cot)
        summed = tuple((held + fresh for held, fresh in zip(carry_in, gradients[1:])))
        return (summed, (result.astype(jnp.bfloat16), gradients[0]))
    zero_sums = tuple((jnp.zeros(item.shape, jnp.float32) for item in parameters))
    totals, (outputs, input_grads) = lax.scan(group_step, zero_sums, (inputs, incoming))
    attention_new, attention_one, attention_two = adamw(attention_weight, attention_first, attention_second, totals[0], rate_attention)
    expand_new, expand_one, expand_two = adamw(expand_weight, expand_first, expand_second, totals[1], rate_expand)
    reduce_new, reduce_one, reduce_two = adamw(reduce_weight, reduce_first, reduce_second, totals[2], rate_reduce)
    vector_new, vector_one, vector_two = adamw(vectors, vector_first, vector_second, totals[3], rate_vector)
    return (outputs.reshape(SEQS, LEN, D), input_grads.reshape(SEQS, LEN, D), attention_new, attention_one, attention_two, expand_new, expand_one, expand_two, reduce_new, reduce_one, reduce_two, vector_new, vector_one, vector_two)
```

```python
import functools
import math

import jax
import jax.numpy as jnp
from jax import lax
from jax.experimental import pallas as pl
from jax.experimental.pallas import tpu as pltpu
from jax.sharding import PartitionSpec as P

HEADS = 12
HEAD = 64
STEP = 10
GROUPS = 8

norm_epsilon = 1e-05
beta_one = 0.9
beta_two = 0.999
adam_epsilon = 1e-08
decay_weight = 0.1
rate_attention = 0.05
rate_expand = 0.03
rate_reduce = 0.015
rate_vector = 0.4

F32 = jnp.float32
BF16 = jnp.bfloat16
MESH = pl.DeviceIdType.MESH
GELU_SCALE = math.sqrt(2.0 / math.pi)
GELU_CUBE = 0.044715


def adamw(weight, moment_one, moment_two, gradient, step_rate):
    moment_one = beta_one * moment_one + (1.0 - beta_one) * gradient
    moment_two = beta_two * moment_two + (1.0 - beta_two) * gradient * gradient
    corrected_one = moment_one / (1.0 - beta_one**STEP)
    corrected_two = moment_two / (1.0 - beta_two**STEP)
    updated = weight - step_rate * (
        corrected_one / (jnp.sqrt(corrected_two) + adam_epsilon) + decay_weight * weight
    )
    return (updated, moment_one, moment_two)


def dot_nn(left, right):
    return lax.dot_general(left, right, (((1,), (0,)), ((), ())), preferred_element_type=F32)


def dot_nt(left, right):
    return lax.dot_general(left, right, (((1,), (1,)), ((), ())), preferred_element_type=F32)


def lane_tiles(ref, count=6):
    return jnp.concatenate([ref[t] for t in range(count)], axis=1)


class Unit:
    def __init__(self, order, half, whole, own, core_in, long_in, mid_in, line_in, total):
        self.order = order
        self.half = half
        self.u = whole.at[half]
        self.own = own.at[half]
        self.core_in = core_in.at[half]
        self.long_in = long_in.at[half]
        self.mid_in = mid_in.at[half]
        self.line_in = line_in.at[half]
        self.total = total.at[half]


def kernel(sub, zs, *refs):
    (tok, cot, vec_in, a_in, w1_in, w2_in,
     out, ig, ga, g1, g2, gvec,
     ua, uw1, uw2,
     rca, rcw1, rcw2, r8a, r8w1, r8w2, r4a, r4w1, r4w2, r3a, r3w1, r3w2,
     x_in, cot_in, stage, vec, vin, gin,
     at, n1, q6, k6, v6, o6, pt, h1, acc, n2, act, gp, ta, tb, tc, d6,
     local_sem, ag_send, ag_recv, rs_send, rs_recv, a2a_send, a2a_recv, v_send, v_recv) = refs

    i = lax.axis_index("blk")
    b = lax.axis_index("batch")
    c, y = lax.rem(i, 2), lax.div(i, 2)
    g, r = lax.div(b, sub), lax.rem(b, sub)
    x, z = lax.rem(g, 2), lax.div(g, 2)

    def device(c_=c, y_=y, x_=x, z_=z):
        return {"blk": 2 * y_ + c_, "batch": (2 * z_ + x_) * sub + r}

    def z_at(k):
        return lax.rem(z + k, zs)

    def block_at(k):
        return lax.rem(i + k, 4)

    def copy(src, dst, send, recv, to):
        return pltpu.make_async_remote_copy(
            src_ref=src, dst_ref=dst, send_sem=send, recv_sem=recv, device_id=to, device_id_type=MESH
        )

    partners = [device(z_=z_at(k)) for k in range(1, zs)]
    partners += [device(x_=1 - x), device(y_=1 - y), device(c_=1 - c), device(c_=1 - c, y_=1 - y)]
    barrier = pltpu.get_barrier_semaphore()
    for partner in partners:
        pl.semaphore_signal(barrier, inc=1, device_id=partner, device_id_type=MESH)
    pl.semaphore_wait(barrier, len(partners))

    pieces = (
        (ua, a_in, rca, r8a, r4a, r3a, ga),
        (uw1, w1_in, rcw1, r8w1, r4w1, r3w1, g1),
        (uw2, w2_in, rcw2, r8w2, r4w2, r3w2, g2),
    )
    units = [Unit(2 * n + half, half, *pieces[n]) for n in range(3) for half in range(2)]
    unit_a, unit_w1, unit_w2 = units[0:2], units[2:4], units[4:6]

    def ag_line_copy(n, k):
        u = n.u.at[c, y, x]
        return copy(u.at[z], u.at[z], ag_send.at[n.order, k - 1], ag_recv.at[n.order, k - 1],
                    device(z_=z_at(k)))

    def ag_line_landed(n, k):
        u = n.u.at[c, y, x]
        source = z_at(zs - k)
        return copy(u.at[source], u.at[source], ag_send.at[n.order, k - 1],
                    ag_recv.at[n.order, k - 1], device())

    def ag_line(n):
        for k in range(1, zs):
            ag_line_copy(n, k).start()

    def ag_step(n, name, landed=False):
        slot = {"mid": zs - 1, "long": zs, "core": zs + 1}[name]
        if name == "core":
            src, dst, to = n.u.at[c], n.u.at[1 - c], device(c_=1 - c)
        elif name == "mid" and n.half == 0:
            src, dst, to = n.u.at[c, y, x], n.u.at[c, y, 1 - x], device(x_=1 - x)
        elif name == "mid":
            src, dst, to = n.u.at[c, y, x], n.u.at[c, 1 - y, x], device(y_=1 - y)
        elif n.half == 0:
            src, dst, to = n.u.at[c, y], n.u.at[c, 1 - y], device(y_=1 - y)
        else:
            src, dst, to = n.u.at[c, :, x], n.u.at[c, :, 1 - x], device(x_=1 - x)
        send, recv = ag_send.at[n.order, slot], ag_recv.at[n.order, slot]
        ref = dst if landed else src
        return copy(ref, ref, send, recv, to)

    def ag_mid(n):
        for k in range(1, zs):
            ag_line_landed(n, k).wait_recv()
        ag_step(n, "mid").start()

    def ag_long(n):
        ag_step(n, "mid", True).wait_recv()
        ag_step(n, "long").start()

    def ag_core(n):
        ag_step(n, "long", True).wait_recv()
        ag_step(n, "core").start()

    def ag_done(n):
        ag_step(n, "core", True).wait_recv()
        for k in range(1, zs):
            ag_line_copy(n, k).wait_send()
        for name in ("mid", "long", "core"):
            ag_step(n, name).wait_send()

    def rs_step(n, name):
        slot = {"core": 0, "long": 1, "mid": 2}[name]
        if name == "core":
            src, dst, to = n.u.at[1 - c], n.core_in, device(c_=1 - c)
        elif name == "long" and n.half == 0:
            src, dst, to = n.u.at[c, 1 - y], n.long_in, device(y_=1 - y)
        elif name == "long":
            src, dst, to = n.u.at[c, :, 1 - x], n.long_in, device(x_=1 - x)
        elif n.half == 0:
            src, dst, to = n.u.at[c, y, 1 - x], n.mid_in, device(x_=1 - x)
        else:
            src, dst, to = n.u.at[c, 1 - y, x], n.mid_in, device(y_=1 - y)
        return copy(src, dst, rs_send.at[n.order, slot], rs_recv.at[n.order, slot], to)

    def rs_line_copy(n, k):
        return copy(n.u.at[c, y, x, z_at(k)], n.line_in.at[k - 1],
                    rs_send.at[n.order, 2 + k], rs_recv.at[n.order, 2 + k], device(z_=z_at(k)))

    def add_into(dst, src):
        dst[...] = (dst[...].astype(F32) + src[...].astype(F32)).astype(BF16)

    def rs_core(n):
        rs_step(n, "core").start()

    def rs_long(n):
        rs_step(n, "core").wait_recv()

        def body(s, carry):
            for yy in range(2):
                for xx in range(2):
                    add_into(n.u.at[c, yy, xx, s], n.core_in.at[yy, xx, s])
            return carry

        lax.fori_loop(0, zs, body, 0)
        rs_step(n, "long").start()

    def rs_mid(n):
        rs_step(n, "long").wait_recv()

        def body(s, carry):
            for e in range(2):
                mine = n.u.at[c, y, e, s] if n.half == 0 else n.u.at[c, e, x, s]
                add_into(mine, n.long_in.at[e, s])
            return carry

        lax.fori_loop(0, zs, body, 0)
        rs_step(n, "mid").start()

    def rs_line(n):
        rs_step(n, "mid").wait_recv()

        def body(s, carry):
            add_into(n.u.at[c, y, x, s], n.mid_in.at[s])
            return carry

        lax.fori_loop(0, zs, body, 0)
        for k in range(1, zs):
            rs_line_copy(n, k).start()

    def rs_done(n):
        for k in range(1, zs):
            rs_line_copy(n, k).wait_recv()
        value = n.u[c, y, x, z].astype(F32)
        for k in range(1, zs):
            value = value + n.line_in[k - 1].astype(F32)
        n.total[...] = value
        for name in ("core", "long", "mid"):
            rs_step(n, name).wait_send()
        for k in range(1, zs):
            rs_line_copy(n, k).wait_send()

    def small_copy(ref, slots, which, slot, to):
        return copy(ref, slots.at[slot], v_send.at[which, slot], v_recv.at[which, slot], to)

    def small_sum(ref, slots, which):
        for slot, to in enumerate((device(c_=1 - c), device(y_=1 - y), device(x_=1 - x))):
            moved = small_copy(ref, slots, which, slot, to)
            moved.start()
            moved.wait()
            ref[...] = ref[...] + slots[slot]
        copies = [small_copy(ref, slots, which, 2 + k, device(z_=z_at(k))) for k in range(1, zs)]
        for moved in copies:
            moved.start()
        for moved in copies:
            moved.wait()
        value = ref[...]
        for k in range(1, zs):
            value = value + slots[2 + k]
        ref[...] = value

    def exchange(src, dst, which):
        return [copy(src.at[block_at(k)], dst.at[i], a2a_send.at[which, k - 1],
                     a2a_recv.at[which, k - 1], {"blk": block_at(k), "batch": b})
                for k in range(1, 4)]

    def exchange_landed(dst, which):
        return [copy(dst.at[block_at(4 - k)], dst.at[block_at(4 - k)], a2a_send.at[which, k - 1],
                     a2a_recv.at[which, k - 1], {"blk": block_at(4 - k), "batch": b})
                for k in range(1, 4)]

    own_copies = [
        pltpu.make_async_copy(tok.at[i], x_in.at[i], local_sem.at[0]),
        pltpu.make_async_copy(cot.at[i], cot_in.at[i], local_sem.at[1]),
    ]
    for moved in own_copies:
        moved.start()
    tokens_out = exchange(tok, x_in, 0)
    for moved in tokens_out:
        moved.start()

    for n in units:
        n.u[c, y, x, z] = n.own[...]
    for n in unit_a:
        ag_line(n)
    vec[...] = vec_in[...]
    small_sum(vec, vin, 0)
    for n in unit_a:
        ag_mid(n)
    for n in unit_w1:
        ag_line(n)
    cot_out = exchange(cot, cot_in, 1)
    for moved in cot_out:
        moved.start()
    for n in unit_a:
        ag_long(n)
    for n in unit_w1:
        ag_mid(n)
    for n in unit_w2:
        ag_line(n)

    for moved in exchange_landed(x_in, 0):
        moved.wait_recv()
    own_copies[0].wait()

    def normalise(value):
        centered = value - jnp.mean(value, axis=-1, keepdims=True)
        scale = lax.rsqrt(jnp.mean(centered * centered, axis=-1, keepdims=True) + norm_epsilon)
        return centered * scale, scale

    def first_norm(s, carry):
        unit, _ = normalise(x_in[s].astype(F32))
        n1[pl.ds(pl.multiple_of(s * 128, 128), 128), :] = (unit * vec[0:1, :] + vec[1:2, :]).astype(BF16)
        return carry

    lax.fori_loop(0, 4, first_norm, 0)

    for n in unit_a:
        ag_core(n)
    for n in unit_w1:
        ag_long(n)
    for n in unit_w2:
        ag_mid(n)
    for n in unit_a:
        ag_done(n)

    lanes = lax.broadcasted_iota(jnp.int32, (96, 128), 1)

    def unpack(s, carry):
        for p in range(2):
            for xx in range(2):
                rows = pl.ds(pl.multiple_of((2 * s + xx) * 96, 96), 96)
                for yy in range(2):
                    first, second = ua.at[p, 0, yy, xx, s], ua.at[p, 1, yy, xx, s]
                    lo, hi = 384 * yy, 384 * yy + 256
                    for m in range(2):
                        at[2 * p + m, rows, lo : lo + 128] = first[96 * m : 96 * m + 96, :]
                        at[2 * p + m, rows, hi : hi + 128] = second[96 * m : 96 * m + 96, :]
                    rest_first = first[192:288, :].astype(F32)
                    rest_second = second[192:288, :].astype(F32)
                    even = jnp.where(lanes < 64, rest_first, rest_second)
                    odd = pltpu.roll(jnp.where(lanes < 64, rest_second, rest_first), 64, 1)
                    at[2 * p, rows, lo + 128 : lo + 256] = even.astype(BF16)
                    at[2 * p + 1, rows, lo + 128 : lo + 256] = odd.astype(BF16)
        return carry

    lax.fori_loop(0, zs, unpack, 0)

    for m, dst, bias in ((0, q6, 2), (1, k6, None), (2, v6, 3)):
        for n in range(3):
            value = dot_nt(n1[...], at[m, 256 * n : 256 * n + 256, :])
            if bias is not None:
                value = value + vec[bias : bias + 1, 256 * n : 256 * n + 256]
            value = value.astype(BF16)
            if m == 0:
                value = value * jnp.asarray(HEAD ** (-0.5), BF16)
            dst[2 * n] = value[:, 0:128]
            dst[2 * n + 1] = value[:, 128:256]

    for n in unit_w1:
        ag_core(n)

    half_lane = lax.broadcasted_iota(jnp.int32, (512, 128), 1) // HEAD

    def half_of(value, which):
        return jnp.where(half_lane == which, value, jnp.zeros_like(value))

    def attend(p, carry):
        queries, keys = q6[p], k6[p]
        values_t = v6[p].astype(F32).T.astype(BF16)
        mixed = []
        for which in range(2):
            scores = dot_nt(half_of(keys, which), queries)
            expo = jnp.exp(scores - jnp.max(scores, axis=0, keepdims=True))
            probs = (expo * (1.0 / jnp.sum(expo, axis=0, keepdims=True))).astype(BF16)
            pt[2 * p + which] = probs
            mixed.append(dot_nn(values_t[64 * which : 64 * which + 64, :], probs))
        o6[p] = jnp.concatenate(mixed, axis=0).T.astype(BF16)
        return carry

    lax.fori_loop(0, 6, attend, 0)

    for n in unit_w2:
        ag_long(n)

    for n in range(3):
        cols = slice(256 * n, 256 * n + 256)
        value = dot_nt(lane_tiles(o6), at[3, cols, :]) + vec[4:5, cols]
        for s in range(4):
            h1[128 * s : 128 * s + 128, cols] = x_in[s, :, cols].astype(F32) + value[128 * s : 128 * s + 128]

    def second_norm(s, carry):
        rows = pl.ds(pl.multiple_of(s * 128, 128), 128)
        unit, _ = normalise(h1[rows, :])
        n2[rows, :] = (unit * vec[5:6, :] + vec[6:7, :]).astype(BF16)
        return carry

    lax.fori_loop(0, 4, second_norm, 0)

    for n in unit_w1:
        ag_done(n)
    for n in unit_w2:
        ag_core(n)

    def expand_piece(s, xx):
        return jnp.concatenate(
            [uw1[h, cc, yy, xx, s] for yy in range(2) for cc in range(2) for h in range(2)], axis=0
        )

    def reduce_block(s):
        yy, cc = lax.div(s, 2), lax.rem(s, 2)
        return jnp.concatenate(
            [uw2[h, cc, yy, xx, zz] for zz in range(zs) for xx in range(2) for h in range(2)], axis=0
        )

    def block_rows(s):
        return pl.ds(pl.multiple_of(s * 512, 512), 512)

    def expand(s, carry):
        for xx in range(2):
            cols = slice(384 * xx, 384 * xx + 384)
            inner = dot_nn(n2[...], expand_piece(s, xx)) + vec[pl.ds(8 + s, 1), cols]
            square = inner * inner
            tanh = jnp.tanh(GELU_SCALE * inner * (1.0 + GELU_CUBE * square))
            act[block_rows(s), cols] = (0.5 * inner * (1.0 + tanh)).astype(BF16)
            slope = 0.5 * (1.0 + tanh) + 0.5 * inner * (1.0 - tanh * tanh) * (
                GELU_SCALE * (1.0 + 3.0 * GELU_CUBE * square)
            )
            gp[block_rows(s), cols] = slope.astype(BF16)
        return carry

    lax.fori_loop(0, 4, expand, 0)

    for n in unit_w2:
        ag_done(n)

    acc[...] = h1[...] + vec[7:8, :]

    def reduce(s, carry):
        acc[...] += dot_nt(act[block_rows(s), :], reduce_block(s))
        return carry

    lax.fori_loop(0, 4, reduce, 0)
    for s in range(4):
        stage[s] = acc[128 * s : 128 * s + 128, :].astype(BF16)
    own_copies.append(pltpu.make_async_copy(stage.at[i], out.at[i], local_sem.at[2]))
    own_copies[2].start()
    result_out = exchange(stage, out, 2)
    for moved in result_out:
        moved.start()

    for moved in exchange_landed(cot_in, 1):
        moved.wait_recv()
    own_copies[1].wait()
    gvec[...] = jnp.zeros_like(gvec)

    def cotangent_rows():
        return jnp.concatenate([cot_in[s] for s in range(4)], axis=0)

    def inner_back(s, carry):
        grad = dot_nn(cotangent_rows(), reduce_block(s)) * gp[block_rows(s), :].astype(F32)
        low = grad.astype(BF16)
        gp[block_rows(s), :] = low
        gvec[pl.ds(8 + s, 1), :] = jnp.sum(low.astype(F32), axis=0, keepdims=True)
        return carry

    lax.fori_loop(0, 4, inner_back, 0)

    def transpose_rows(dst, s, value):
        dst[:, 128 * s : 128 * s + 128] = value.astype(F32).T.astype(BF16)

    total = jnp.zeros((1, 768), F32)
    for s in range(4):
        transpose_rows(ta, s, cot_in[s])
        total = total + jnp.sum(cot_in[s].astype(F32), axis=0, keepdims=True)
    gvec[7:8, :] = total

    def reduce_back(s, carry):
        yy, cc = lax.div(s, 2), lax.rem(s, 2)
        grad = dot_nn(ta[...], act[block_rows(s), :]).astype(BF16)
        for zz in range(zs):
            for xx in range(2):
                for h in range(2):
                    row = 96 * (2 * zz + xx) + 48 * h
                    uw2[h, cc, yy, xx, zz] = grad[row : row + 48, :]
        return carry

    lax.fori_loop(0, 4, reduce_back, 0)
    for n in unit_w2:
        rs_core(n)

    def norm_back(s, carry):
        whole = jnp.concatenate([expand_piece(s, 0), expand_piece(s, 1)], axis=1)
        part = dot_nt(gp[block_rows(s), :], whole)

        @pl.when(s == 0)
        def _():
            acc[...] = part

        @pl.when(s > 0)
        def _():
            acc[...] += part

        return carry

    lax.fori_loop(0, 4, norm_back, 0)
    for n in unit_w2:
        rs_long(n)

    for s in range(4):
        transpose_rows(tb, s, n2[128 * s : 128 * s + 128, :])

    def expand_back(s, carry):
        for xx in range(2):
            grad = dot_nn(tb[...], gp[block_rows(s), 384 * xx : 384 * xx + 384]).astype(BF16)
            for yy in range(2):
                for cc in range(2):
                    for h in range(2):
                        row = 192 * (2 * yy + cc) + 96 * h
                        uw1[h, cc, yy, xx, s] = grad[row : row + 96, :]
        return carry

    lax.fori_loop(0, 4, expand_back, 0)
    for n in unit_w1:
        rs_core(n)

    def norm_gradient(value, scale_row, grad):
        unit, scale = normalise(value)
        gain_sum = jnp.sum(grad * unit, axis=0, keepdims=True)
        bias_sum = jnp.sum(grad, axis=0, keepdims=True)
        inner = grad * scale_row
        mean = jnp.mean(inner, axis=-1, keepdims=True)
        along = jnp.mean(inner * unit, axis=-1, keepdims=True)
        return scale * (inner - mean - unit * along), gain_sum, bias_sum

    def hidden_back(s, carry):
        rows = pl.ds(pl.multiple_of(s * 128, 128), 128)
        grad, gain_sum, bias_sum = norm_gradient(h1[rows, :], vec[5:6, :], acc[rows, :])
        grad = grad + cot_in[s].astype(F32)
        h1[rows, :] = grad
        low = grad.astype(BF16)
        n2[rows, :] = low
        gvec[5:6, :] += gain_sum
        gvec[6:7, :] += bias_sum
        gvec[4:5, :] += jnp.sum(low.astype(F32), axis=0, keepdims=True)
        return carry

    lax.fori_loop(0, 4, hidden_back, 0)
    for n in unit_w2:
        rs_mid(n)
    for n in unit_w1:
        rs_long(n)

    for n in range(3):
        value = dot_nn(n2[...], at[3, :, 256 * n : 256 * n + 256]).astype(BF16)
        d6[2 * n] = value[:, 0:128]
        d6[2 * n + 1] = value[:, 128:256]
    for s in range(4):
        transpose_rows(tc, s, n2[128 * s : 128 * s + 128, :])
    act[768:1536, :] = dot_nn(tc[...], lane_tiles(o6)).astype(BF16)
    for n in unit_w2:
        rs_line(n)

    def attend_back(p, carry):
        rows = pl.ds(pl.multiple_of(p * 128, 128), 128)
        queries, keys, values, grads = q6[p], k6[p], v6[p], d6[p]
        keys_t = keys.astype(F32).T.astype(BF16)
        grad_query, grad_key, grad_value = [], 0.0, 0.0
        for which in range(2):
            probs = pt[2 * p + which]
            wide = probs.astype(F32)
            grad_probs = dot_nt(half_of(values, which), grads)
            inner = jnp.sum(wide * grad_probs, axis=0, keepdims=True)
            grad_scores = (wide * (grad_probs - inner)).astype(BF16)
            grad_query.append(dot_nn(keys_t[64 * which : 64 * which + 64, :], grad_scores))
            grad_key = grad_key + dot_nn(grad_scores, half_of(queries, which))
            grad_value = grad_value + dot_nn(probs, half_of(grads, which))
        grad_query = jnp.concatenate(grad_query, axis=0) * HEAD ** (-0.5)
        low_key, low_value = grad_key.astype(BF16), grad_value.astype(BF16)
        ta[rows, :] = grad_query.astype(BF16)
        tb[rows, :] = grad_key.T.astype(BF16)
        tc[rows, :] = grad_value.T.astype(BF16)
        q6[p] = grad_query.T.astype(BF16)
        k6[p] = low_key
        v6[p] = low_value
        return carry

    lax.fori_loop(0, 6, attend_back, 0)
    for n in unit_w2:
        rs_done(n)
    for n in unit_w1:
        rs_mid(n)

    def pack(p, first_row, second_row):
        def body(s, carry):
            for xx in range(2):
                offset = (2 * s + xx) * 96
                rows = [pl.ds(pl.multiple_of(first_row + offset, 96), 96),
                        pl.ds(pl.multiple_of(second_row + offset, 96), 96)]
                for yy in range(2):
                    lo, mid, hi = 384 * yy, 384 * yy + 128, 384 * yy + 256
                    for m in range(2):
                        ua[p, 0, yy, xx, s, 96 * m : 96 * m + 96, :] = act[rows[m], lo : lo + 128]
                        ua[p, 1, yy, xx, s, 96 * m : 96 * m + 96, :] = act[rows[m], hi : hi + 128]
                    even = act[rows[0], mid : mid + 128].astype(F32)
                    odd = pltpu.roll(act[rows[1], mid : mid + 128].astype(F32), 64, 1)
                    ua[p, 0, yy, xx, s, 192:288, :] = jnp.where(lanes < 64, even, odd).astype(BF16)
                    ua[p, 1, yy, xx, s, 192:288, :] = jnp.where(lanes < 64, odd, even).astype(BF16)
            return carry

        lax.fori_loop(0, zs, body, 0)

    act[0:768, :] = dot_nn(tc[...], n1[...]).astype(BF16)
    pack(1, 0, 768)
    rs_core(unit_a[1])
    act[0:768, :] = dot_nn(ta[...], n1[...]).astype(BF16)
    act[768:1536, :] = dot_nn(tb[...], n1[...]).astype(BF16)
    pack(0, 0, 768)
    rs_core(unit_a[0])
    for n in unit_w1:
        rs_line(n)
    rs_long(unit_a[1])
    rs_long(unit_a[0])

    acc[...] = dot_nn(lane_tiles(q6), at[0])
    acc[...] += dot_nn(lane_tiles(k6), at[1])
    acc[...] += dot_nn(lane_tiles(v6), at[2])
    gvec[2:3, :] = jnp.sum(lane_tiles(q6).astype(F32), axis=0, keepdims=True)
    gvec[3:4, :] = jnp.sum(lane_tiles(v6).astype(F32), axis=0, keepdims=True)

    for moved in result_out:
        moved.wait_send()
    own_copies[2].wait()

    def input_back(s, carry):
        rows = pl.ds(pl.multiple_of(s * 128, 128), 128)
        grad, gain_sum, bias_sum = norm_gradient(x_in[s].astype(F32), vec[0:1, :], acc[rows, :])
        stage[s] = (grad + h1[rows, :]).astype(BF16)
        gvec[0:1, :] += gain_sum
        gvec[1:2, :] += bias_sum
        return carry

    lax.fori_loop(0, 4, input_back, 0)
    own_copies.append(pltpu.make_async_copy(stage.at[i], ig.at[i], local_sem.at[3]))
    own_copies[3].start()
    grad_out = exchange(stage, ig, 3)
    for moved in grad_out:
        moved.start()

    for n in unit_a:
        rs_mid(n)
    for n in unit_w1:
        rs_done(n)
    small_sum(gvec, gin, 1)
    for n in unit_a:
        rs_line(n)
    for n in unit_a:
        rs_done(n)

    own_copies[3].wait()
    for moved in tokens_out + cot_out + grad_out:
        moved.wait_send()
    for moved in exchange_landed(out, 2) + exchange_landed(ig, 3):
        moved.wait_recv()


def exchange_kernel(sub, tokens, masked, vec, a_own, w1_own, w2_own):
    zs = GROUPS // 2
    seqs, block, width = tokens.shape
    rows = seqs * block
    vmem = lambda shape, dtype: pltpu.VMEM(shape, dtype)
    shapes = (a_own.shape[1:], w1_own.shape[1:], w2_own.shape[1:])
    scratch = [vmem((2, 2, 2, 2, zs) + s, BF16) for s in shapes]
    scratch += [vmem((2, 2, 2, zs) + s, BF16) for s in shapes]
    scratch += [vmem((2, 2, zs) + s, BF16) for s in shapes]
    scratch += [vmem((2, zs) + s, BF16) for s in shapes]
    scratch += [vmem((2, zs - 1) + s, BF16) for s in shapes]
    scratch += [vmem(tokens.shape, BF16)] * 3
    scratch += [vmem((16, width), F32)]
    scratch += [vmem((zs + 2, 16, width), F32)] * 2
    tiles = vmem((width // 128, rows, 128), BF16)
    flat = vmem((rows, width), BF16)
    turned = vmem((width, rows), BF16)
    scratch += [vmem((4, width, width), BF16), flat, tiles, tiles, tiles, tiles]
    scratch += [vmem((HEADS, rows, rows), BF16), vmem((rows, width), F32), vmem((rows, width), F32)]
    scratch += [flat, vmem((4 * rows, width), BF16), vmem((4 * rows, width), BF16)]
    scratch += [turned, turned, turned, tiles]
    scratch += [pltpu.SemaphoreType.DMA((4,))]
    scratch += [pltpu.SemaphoreType.DMA((6, zs + 2))] * 4
    scratch += [pltpu.SemaphoreType.DMA((4, 3))] * 2
    scratch += [pltpu.SemaphoreType.DMA((2, zs + 2))] * 2
    in_vmem = pl.BlockSpec(memory_space=pltpu.VMEM)
    anywhere = pl.BlockSpec(memory_space=pl.ANY)
    return pl.pallas_call(
        functools.partial(kernel, sub, zs),
        out_shape=(
            jax.ShapeDtypeStruct(tokens.shape, BF16),
            jax.ShapeDtypeStruct(tokens.shape, BF16),
            jax.ShapeDtypeStruct(a_own.shape, F32),
            jax.ShapeDtypeStruct(w1_own.shape, F32),
            jax.ShapeDtypeStruct(w2_own.shape, F32),
            jax.ShapeDtypeStruct(vec.shape, F32),
        ),
        in_specs=[anywhere, anywhere] + [in_vmem] * 4,
        out_specs=(anywhere, anywhere) + (in_vmem,) * 4,
        scratch_shapes=scratch,
        compiler_params=pltpu.CompilerParams(
            collective_id=0, has_side_effects=True, vmem_limit_bytes=63 * 1024 * 1024
        ),
    )(tokens, masked, vec, a_own, w1_own, w2_own)


def local(
    sub,
    tokens,
    cotangent,
    span_mask,
    attention_weight,
    expand_weight,
    reduce_weight,
    vectors,
    attention_first,
    attention_second,
    expand_first,
    expand_second,
    reduce_first,
    reduce_second,
    vector_first,
    vector_second,
):
    core = lax.rem(lax.axis_index("blk"), 2)
    together = [[n * sub + m for m in range(sub)] for n in range(GROUPS)]

    def widen(value, axis):
        if sub == 1:
            return value
        return lax.all_gather(value, "batch", axis=axis, tiled=True, axis_index_groups=together)

    def narrow(value, axis):
        if sub == 1:
            return value
        return lax.psum_scatter(
            value, "batch", scatter_dimension=axis, tiled=True, axis_index_groups=together
        )

    masked = (cotangent.astype(F32) * span_mask[..., None].astype(F32)).astype(BF16)

    a_low = jnp.swapaxes(widen(attention_weight.astype(BF16), 2), 1, 2)
    columns, depth = a_low.shape[1:]
    main = jnp.where(core == 0, a_low[:, :, :128], a_low[:, :, 64:])
    rest = jnp.where(core == 0, a_low[:, :, 128:], a_low[:, :, :64])
    rest = rest.reshape(2, 2, columns, 64)
    rest = jnp.where(
        core == 0,
        jnp.concatenate([rest[:, 0], rest[:, 1]], axis=-1),
        jnp.concatenate([rest[:, 1], rest[:, 0]], axis=-1),
    )
    a_own = jnp.concatenate([main.reshape(2, 2 * columns, 128), rest], axis=1)
    w1_low = widen(expand_weight.astype(BF16), 1)
    w1_own = w1_low.reshape(2, w1_low.shape[0] // 2, w1_low.shape[1])
    w2_low = widen(reduce_weight.astype(BF16), 1).T
    w2_own = w2_low.reshape(2, w2_low.shape[0] // 2, w2_low.shape[1])
    vec_low = widen(vectors.astype(BF16), 1).astype(F32)
    row = vec_low.shape[0] * lax.axis_index("blk")
    column = vec_low.shape[1] * lax.div(lax.axis_index("batch"), sub)
    vec = lax.dynamic_update_slice(jnp.zeros((16, tokens.shape[2]), F32), vec_low, (row, column))

    out_tokens, input_grad, ga, gw1, gw2, gvec = exchange_kernel(
        sub, tokens, masked, vec, a_own, w1_own, w2_own
    )

    main, rest = ga[:, : 2 * columns].reshape(4, columns, 128), ga[:, 2 * columns :]
    low, high = rest[:, :, :64], rest[:, :, 64:]
    rest = jnp.where(core == 0, jnp.stack([low, high], axis=1), jnp.stack([high, low], axis=1))
    rest = rest.reshape(4, columns, 64)
    attention_sum = jnp.where(
        core == 0,
        jnp.concatenate([main, rest], axis=-1),
        jnp.concatenate([rest, main], axis=-1),
    )
    attention_sum = narrow(jnp.swapaxes(attention_sum, 1, 2), 2)
    expand_sum = narrow(gw1.reshape(w1_low.shape), 1)
    reduce_sum = narrow(gw2.reshape(w2_low.shape).T, 1)
    vector_sum = narrow(lax.dynamic_slice(gvec, (row, column), vec_low.shape), 1)

    attention_new, attention_one, attention_two = adamw(
        attention_weight, attention_first, attention_second, attention_sum, rate_attention
    )
    expand_new, expand_one, expand_two = adamw(
        expand_weight, expand_first, expand_second, expand_sum, rate_expand
    )
    reduce_new, reduce_one, reduce_two = adamw(
        reduce_weight, reduce_first, reduce_second, reduce_sum, rate_reduce
    )
    vector_new, vector_one, vector_two = adamw(
        vectors, vector_first, vector_second, vector_sum, rate_vector
    )
    return (
        out_tokens,
        input_grad.astype(F32),
        attention_new,
        attention_one,
        attention_two,
        expand_new,
        expand_one,
        expand_two,
        reduce_new,
        reduce_one,
        reduce_two,
        vector_new,
        vector_one,
        vector_two,
    )


def solution(mesh):
    sub = mesh.shape["batch"] // GROUPS
    sequences = P("batch", "blk", None)
    attention = P(None, "blk", "batch")
    matrix = P("blk", "batch")
    return jax.shard_map(
        functools.partial(local, sub),
        mesh=mesh,
        in_specs=(sequences, sequences, P("batch", "blk"), attention, matrix, matrix, matrix)
        + (attention,) * 2
        + (matrix,) * 6,
        out_specs=(sequences,) * 2 + (attention,) * 3 + (matrix,) * 9,
        check_vma=False,
    )
```

```python
import functools
import math

import jax
import jax.numpy as jnp
from jax import lax
from jax.experimental import pallas as pl
from jax.experimental.pallas import tpu as pltpu
from jax.sharding import PartitionSpec as P

HEADS = 12
HEAD = 64
STEP = 10
GROUPS = 8

norm_epsilon = 1e-05
beta_one = 0.9
beta_two = 0.999
adam_epsilon = 1e-08
decay_weight = 0.1
rate_attention = 0.05
rate_expand = 0.03
rate_reduce = 0.015
rate_vector = 0.4

F32 = jnp.float32
BF16 = jnp.bfloat16
MESH = pl.DeviceIdType.MESH
GELU_SCALE = math.sqrt(2.0 / math.pi)
GELU_CUBE = 0.044715


def adamw(weight, moment_one, moment_two, gradient, step_rate):
    moment_one = beta_one * moment_one + (1.0 - beta_one) * gradient
    moment_two = beta_two * moment_two + (1.0 - beta_two) * gradient * gradient
    corrected_one = moment_one / (1.0 - beta_one**STEP)
    corrected_two = moment_two / (1.0 - beta_two**STEP)
    updated = weight - step_rate * (
        corrected_one / (jnp.sqrt(corrected_two) + adam_epsilon) + decay_weight * weight
    )
    return (updated, moment_one, moment_two)


def dot_nn(left, right):
    return lax.dot_general(left, right, (((1,), (0,)), ((), ())), preferred_element_type=F32)


def dot_nt(left, right):
    return lax.dot_general(left, right, (((1,), (1,)), ((), ())), preferred_element_type=F32)


def lane_tiles(ref, count=6):
    return jnp.concatenate([ref[t] for t in range(count)], axis=1)


class Unit:
    def __init__(self, order, u, own, long_axis, fine):
        self.order, self.u, self.own, self.long_axis, self.fine = order, u, own, long_axis, fine


class Gradient:
    def __init__(self, order, u, long_axis, first, count, whole, core_in, long_in, mid_in, line_in, total):
        self.order, self.long_axis, self.first, self.count, self.whole = order, long_axis, first, count, whole
        self.u, self.core_in, self.long_in, self.mid_in, self.line_in = u, core_in, long_in, mid_in, line_in
        self.total = total


def kernel(sub, zs, *refs):
    (tok, cot, vec_in, a_in, w1_in, w2_in,
     out, ig, ga, g1, g2, gvec,
     ubuf, core_in, long_in, mid_in, line_in,
     x_in, cot_in, stage, vec, vin, gin,
     at, n1, q6, k6, v6, o6, pt, h1, acc, n2, act, gp, ta, tb, tc, d6,
     local_sem, ag_send, ag_recv, rs_send, rs_recv, a2a_send, a2a_recv, v_send, v_recv) = refs

    i = lax.axis_index("blk")
    b = lax.axis_index("batch")
    c, y = lax.rem(i, 2), lax.div(i, 2)
    g, r = lax.div(b, sub), lax.rem(b, sub)
    x, z = lax.rem(g, 2), lax.div(g, 2)

    def device(c_=c, y_=y, x_=x, z_=z):
        return {"blk": 2 * y_ + c_, "batch": (2 * z_ + x_) * sub + r}

    def z_at(k):
        return lax.rem(z + k, zs)

    def block_at(k):
        return lax.rem(i + k, 4)

    def copy(src, dst, send, recv, to):
        return pltpu.make_async_remote_copy(
            src_ref=src, dst_ref=dst, send_sem=send, recv_sem=recv, device_id=to, device_id_type=MESH
        )

    def loop(count, body, hooks=()):
        def step(s, carry):
            body(s)
            for k, *todo in hooks:

                @pl.when(s == k)
                def _():
                    for f in todo:
                        f()

            return carry

        lax.fori_loop(0, count, step, 0)

    partners = [device(z_=z_at(k)) for k in range(1, zs)]
    partners += [device(x_=1 - x), device(y_=1 - y), device(c_=1 - c), device(c_=1 - c, y_=1 - y)]
    barrier = pltpu.get_barrier_semaphore()
    for partner in partners:
        pl.semaphore_signal(barrier, inc=1, device_id=partner, device_id_type=MESH)
    pl.semaphore_wait(barrier, len(partners))

    def ag_sems(n, slot):
        return ag_send.at[n.order, slot], ag_recv.at[n.order, slot]

    def group(n, u, long_off, mid_off, cut=None):
        yy = y if (long_off if n.long_axis == "y" else mid_off) == 0 else 1 - y
        xx = x if (long_off if n.long_axis == "x" else mid_off) == 0 else 1 - x
        return u.at[c, yy, xx] if cut is None else u.at[c, yy, xx, cut]

    def partner_of(n, step):
        axis = n.long_axis if step == "long" else {"x": "y", "y": "x"}[n.long_axis]
        return device(x_=1 - x) if axis == "x" else device(y_=1 - y)

    LINE, MID, LONG, LAST, CORE = 0, zs - 1, 2 * zs - 1, 3 * zs - 1, 3 * zs

    def ag_line(n, k, landed=False):
        ref = group(n, n.u, 0, 0, z_at(zs - k) if landed else z)
        return copy(ref, ref, *ag_sems(n, LINE + k - 1), device(z_=z_at(k)))

    def ag_first(n, step, k, landed=False):
        cut = z_at(zs - k) if n.fine else None
        off = (0, 1) if step == "mid" else (1, 0)
        ref = group(n, n.u, *(off if landed else (0, 0)), cut)
        return copy(ref, ref, *ag_sems(n, (MID if step == "mid" else LONG) + k), partner_of(n, step))

    def ag_last(n, landed=False):
        ref = group(n, n.u, 1 if landed else 0, 1)
        return copy(ref, ref, *ag_sems(n, LAST), partner_of(n, "long"))

    def ag_core(n, long_off, mid_off, landed=False):
        ref = group(n, n.u, long_off, mid_off)
        if landed:
            yy = y if (long_off if n.long_axis == "y" else mid_off) == 0 else 1 - y
            xx = x if (long_off if n.long_axis == "x" else mid_off) == 0 else 1 - x
            ref = n.u.at[1 - c, yy, xx]
        return copy(ref, ref, *ag_sems(n, CORE + 2 * long_off + mid_off), device(c_=1 - c))

    def parts(n):
        return range(zs) if n.fine else range(1)

    def ag_start(n):
        if n.fine:
            for step in ("mid", "long"):
                ag_first(n, step, 0).start()
        for k in range(1, zs):
            ag_line(n, k).start()

    def ag_piece(n, k):
        ag_line(n, k, True).wait_recv()
        for step in ("mid", "long"):
            ag_first(n, step, k).start()

    def ag_one(n):
        if not n.fine:
            for k in range(1, zs):
                ag_line(n, k, True).wait_recv()
            for step in ("mid", "long"):
                ag_first(n, step, 0).start()
        ag_core(n, 0, 0).start()

    def ag_two(n):
        for k in parts(n):
            ag_first(n, "mid", k, True).wait_recv()
        ag_last(n).start()
        ag_core(n, 0, 1).start()

    def ag_three(n):
        for k in parts(n):
            ag_first(n, "long", k, True).wait_recv()
        ag_core(n, 1, 0).start()

    def ag_four(n):
        ag_last(n, True).wait_recv()
        ag_core(n, 1, 1).start()

    def ag_done(n):
        for off in ((0, 0), (0, 1), (1, 0), (1, 1)):
            ag_core(n, *off, True).wait_recv()
        for k in range(1, zs):
            ag_line(n, k).wait_send()
        for step in ("mid", "long"):
            for k in parts(n):
                ag_first(n, step, k).wait_send()
        ag_last(n).wait_send()
        for off in ((0, 0), (0, 1), (1, 0), (1, 1)):
            ag_core(n, *off).wait_send()

    def rs_sems(n, slot):
        return rs_send.at[n.order, slot], rs_recv.at[n.order, slot]

    def cut_of(n):
        return slice(None) if n.count == zs else pl.ds(n.first, n.count)

    def rs_core(n, long_off):
        place = 1 - (y if n.long_axis == "y" else x) if long_off else (y if n.long_axis == "y" else x)
        where = (place, slice(None)) if n.long_axis == "y" else (slice(None), place)
        return copy(n.u.at[(1 - c,) + where + (cut_of(n),)], n.core_in.at[where],
                    *rs_sems(n, long_off), device(c_=1 - c))

    def rs_long(n):
        where = (1 - y, slice(None)) if n.long_axis == "y" else (slice(None), 1 - x)
        return copy(n.u.at[(c,) + where + (cut_of(n),)], n.long_in, *rs_sems(n, 2), partner_of(n, "long"))

    def rs_mid(n):
        return copy(group(n, n.u, 0, 1, cut_of(n)), n.mid_in, *rs_sems(n, 3), partner_of(n, "mid"))

    def rs_line(n, k):
        return copy(group(n, n.u, 0, 0, z_at(k)), n.line_in.at[k - 1], *rs_sems(n, 3 + k), device(z_=z_at(k)))

    def within(n, place):
        return jnp.logical_and(place >= n.first, place < n.first + n.count)

    def when_within(n, place, f):
        if n.whole:
            f()
        else:
            pl.when(within(n, place))(f)

    def gather_terms(n, long_off, mid_off, names):
        yy = y if (long_off if n.long_axis == "y" else mid_off) == 0 else 1 - y
        xx = x if (long_off if n.long_axis == "x" else mid_off) == 0 else 1 - x

        def body(s):
            mine = n.u.at[c, yy, xx, n.first + s]
            value = mine[...].astype(F32) + n.core_in[yy, xx, s].astype(F32)
            if "long" in names:
                value = value + n.long_in[xx if n.long_axis == "y" else yy, s].astype(F32)
            if "mid" in names:
                value = value + n.mid_in[s].astype(F32)
            mine[...] = value.astype(BF16)

        loop(n.count, body)

    def rs_zero(n):
        rs_core(n, 1).start()
        rs_core(n, 0).start()

    def rs_one(n):
        rs_core(n, 1).wait_recv()
        gather_terms(n, 1, 0, ())
        gather_terms(n, 1, 1, ())
        rs_long(n).start()

    def rs_two(n):
        rs_core(n, 0).wait_recv()
        rs_long(n).wait_recv()
        gather_terms(n, 0, 1, ("long",))
        rs_mid(n).start()

    def rs_three(n):
        rs_mid(n).wait_recv()
        gather_terms(n, 0, 0, ("long", "mid"))
        for k in range(1, zs):
            when_within(n, z_at(k), lambda k=k: rs_line(n, k).start())

    def rs_done(n):
        def finish():
            for k in range(1, zs):
                rs_line(n, k).wait_recv()
            value = n.u[c, y, x, z].astype(F32)
            for k in range(1, zs):
                value = value + n.line_in[k - 1].astype(F32)
            n.total[...] = value

        when_within(n, z, finish)
        for moved in (rs_core(n, 0), rs_core(n, 1), rs_long(n), rs_mid(n)):
            moved.wait_send()
        for k in range(1, zs):
            when_within(n, z_at(k), lambda k=k: rs_line(n, k).wait_send())

    def small_sum(ref, slots, which):
        to = (device(c_=1 - c), device(y_=1 - y), device(x_=1 - x))
        to += tuple(device(z_=z_at(k)) for k in range(1, zs))

        def moved(slot):
            return copy(ref, slots.at[slot], v_send.at[which, slot], v_recv.at[which, slot], to[slot])

        def land(last):
            moved(last).wait()
            ref[...] = ref[...] + slots[last]

        def step(n):
            def run():
                if n > 0:
                    land(n - 1)
                moved(n).start()

            return run

        def line():
            land(2)
            for k in range(1, zs):
                moved(2 + k).start()

        def finish():
            for k in range(1, zs):
                moved(2 + k).wait()
            value = ref[...]
            for k in range(1, zs):
                value = value + slots[2 + k]
            ref[...] = value

        return [step(0), step(1), step(2), line, finish]

    def exchange(src, dst, which):
        return [copy(src.at[block_at(k)], dst.at[i], a2a_send.at[which, k - 1],
                     a2a_recv.at[which, k - 1], {"blk": block_at(k), "batch": b})
                for k in range(1, 4)]

    def exchange_landed(dst, which):
        return [copy(dst.at[block_at(4 - k)], dst.at[block_at(4 - k)], a2a_send.at[which, k - 1],
                     a2a_recv.at[which, k - 1], {"blk": block_at(4 - k), "batch": b})
                for k in range(1, 4)]

    units = [Unit(2 * n + half, ubuf.at[n, half], own.at[half], axes[half], n == 0)
             for n, (own, axes) in enumerate(((a_in, "xx"), (w1_in, "yx"), (w2_in, "yx")))
             for half in range(2)]
    unit_a, unit_w1, unit_w2 = units[0:2], units[2:4], units[4:6]
    grads = []
    half_zs = zs // 2
    for n, (source, total, axes) in enumerate(((0, g2, "yx"), (2, g1, "yx"))):
        for half in range(2):
            order = 2 * n + half
            grads.append(Gradient(order, ubuf.at[source, half], axes[half], 0, zs, True,
                                  core_in.at[order], long_in.at[order], mid_in.at[order],
                                  line_in.at[order], total.at[half]))
    for part in range(2):
        for half in range(2):
            cut = pl.ds(part * half_zs, half_zs)
            grads.append(Gradient(4 + 2 * part + half, ubuf.at[1, half], "x", part * half_zs, half_zs, False,
                                  core_in.at[4 + half, :, :, cut], long_in.at[4 + half, :, cut],
                                  mid_in.at[4 + half, cut], line_in.at[4 + half], ga.at[half]))
    grad_w2, grad_w1, grad_a = grads[0:2], grads[2:4], (grads[4:6], grads[6:8])

    def each(f, which):
        def run():
            for n in which:
                f(n)

        return run

    for n in units:
        n.u[c, y, x, z] = n.own[...]
    own_tokens = pltpu.make_async_copy(tok.at[i], x_in.at[i], local_sem.at[0])
    own_cot = pltpu.make_async_copy(cot.at[i], cot_in.at[i], local_sem.at[1])
    vec[...] = vec_in[...]
    vec_steps = small_sum(vec, vin, 0)
    vec_steps[0]()
    each(ag_start, unit_a)()
    own_tokens.start()
    own_cot.start()
    tokens_out = exchange(tok, x_in, 0)
    for moved in tokens_out:
        moved.start()
    for k in range(1, zs):
        if k < 4:
            vec_steps[k]()
        for n in unit_a:
            ag_piece(n, k)
    each(ag_one, unit_a)()
    each(ag_start, unit_w1)()
    vec_steps[4]()

    for moved in exchange_landed(x_in, 0):
        moved.wait_recv()
    own_tokens.wait()

    def normalise(value):
        centered = value - jnp.mean(value, axis=-1, keepdims=True)
        scale = lax.rsqrt(jnp.mean(centered * centered, axis=-1, keepdims=True) + norm_epsilon)
        return centered * scale, scale

    def rows_of(s):
        return pl.ds(pl.multiple_of(s * 128, 128), 128)

    def first_norm(s):
        unit, _ = normalise(x_in[s].astype(F32))
        n1[rows_of(s), :] = (unit * vec[0:1, :] + vec[1:2, :]).astype(BF16)

    each(ag_two, unit_a)()
    cot_out = exchange(cot, cot_in, 1)
    for moved in cot_out:
        moved.start()
    loop(4, first_norm)
    each(ag_three, unit_a)()
    each(ag_one, unit_w1)()
    each(ag_start, unit_w2)()
    each(ag_four, unit_a)()
    each(ag_done, unit_a)()

    lanes = lax.broadcasted_iota(jnp.int32, (96, 128), 1)

    def unpack(s):
        for p in range(2):
            for xx in range(2):
                rows = pl.ds(pl.multiple_of((2 * s + xx) * 96, 96), 96)
                for yy in range(2):
                    first, second = ubuf.at[0, p, 0, yy, xx, s], ubuf.at[0, p, 1, yy, xx, s]
                    lo, hi = 384 * yy, 384 * yy + 256
                    for m in range(2):
                        at[2 * p + m, rows, lo : lo + 128] = first[96 * m : 96 * m + 96, :]
                        at[2 * p + m, rows, hi : hi + 128] = second[96 * m : 96 * m + 96, :]
                    rest_first = first[192:288, :].astype(F32)
                    rest_second = second[192:288, :].astype(F32)
                    even = jnp.where(lanes < 64, rest_first, rest_second)
                    odd = pltpu.roll(jnp.where(lanes < 64, rest_second, rest_first), 64, 1)
                    at[2 * p, rows, lo + 128 : lo + 256] = even.astype(BF16)
                    at[2 * p + 1, rows, lo + 128 : lo + 256] = odd.astype(BF16)

    loop(zs, unpack)

    for m, dst, bias in ((0, q6, 2), (1, k6, None), (2, v6, 3)):
        for n in range(3):
            value = dot_nt(n1[...], at[m, 256 * n : 256 * n + 256, :])
            if bias is not None:
                value = value + vec[bias : bias + 1, 256 * n : 256 * n + 256]
            value = value.astype(BF16)
            if m == 0:
                value = value * jnp.asarray(HEAD ** (-0.5), BF16)
            dst[2 * n] = value[:, 0:128]
            dst[2 * n + 1] = value[:, 128:256]

    half_lane = lax.broadcasted_iota(jnp.int32, (512, 128), 1) // HEAD

    def half_of(value, which):
        return jnp.where(half_lane == which, value, jnp.zeros_like(value))

    def attend(p):
        queries, keys = q6[p], k6[p]
        values_t = v6[p].astype(F32).T.astype(BF16)
        mixed = []
        for which in range(2):
            scores = dot_nt(half_of(keys, which), queries)
            expo = jnp.exp(scores - jnp.max(scores, axis=0, keepdims=True))
            probs = (expo * (1.0 / jnp.sum(expo, axis=0, keepdims=True))).astype(BF16)
            pt[2 * p + which] = probs
            mixed.append(dot_nn(values_t[64 * which : 64 * which + 64, :], probs))
        o6[p] = jnp.concatenate(mixed, axis=0).T.astype(BF16)

    loop(6, attend, (
        (0, each(ag_two, unit_w1)),
        (2, each(ag_three, unit_w1)),
        (3, each(ag_one, unit_w2)),
        (5, each(ag_four, unit_w1)),
    ))

    for n in range(3):
        cols = slice(256 * n, 256 * n + 256)
        value = dot_nt(lane_tiles(o6), at[3, cols, :]) + vec[4:5, cols]
        for s in range(4):
            h1[128 * s : 128 * s + 128, cols] = x_in[s, :, cols].astype(F32) + value[128 * s : 128 * s + 128]

    def second_norm(s):
        unit, _ = normalise(h1[rows_of(s), :])
        n2[rows_of(s), :] = (unit * vec[5:6, :] + vec[6:7, :]).astype(BF16)

    loop(4, second_norm)
    each(ag_two, unit_w2)()
    each(ag_done, unit_w1)()

    def expand_piece(s, xx):
        def piece(ref):
            return jnp.concatenate([ref[96 * t : 96 * t + 96, :] for t in range(3)], axis=1)

        return jnp.concatenate(
            [piece(ubuf.at[1, h, cc, yy, xx, s]) for yy in range(2) for cc in range(2) for h in range(2)],
            axis=0,
        )

    def reduce_block(s):
        yy, cc = lax.div(s, 2), lax.rem(s, 2)

        def piece(ref):
            return jnp.concatenate([ref[48 * t : 48 * t + 48, :] for t in range(6)], axis=1)

        return jnp.concatenate(
            [piece(ubuf.at[2, h, cc, yy, xx, zz]) for zz in range(zs) for xx in range(2) for h in range(2)],
            axis=0,
        )

    def block_rows(s):
        return pl.ds(pl.multiple_of(s * 512, 512), 512)

    def expand(s):
        for xx in range(2):
            cols = slice(384 * xx, 384 * xx + 384)
            inner = dot_nn(n2[...], expand_piece(s, xx)) + vec[pl.ds(8 + s, 1), cols]
            square = inner * inner
            tanh = jnp.tanh(GELU_SCALE * inner * (1.0 + GELU_CUBE * square))
            act[block_rows(s), cols] = (0.5 * inner * (1.0 + tanh)).astype(BF16)
            slope = 0.5 * (1.0 + tanh) + 0.5 * inner * (1.0 - tanh * tanh) * (
                GELU_SCALE * (1.0 + 3.0 * GELU_CUBE * square)
            )
            gp[block_rows(s), cols] = slope.astype(BF16)

    loop(4, expand)
    each(ag_three, unit_w2)()

    for moved in exchange_landed(cot_in, 1):
        moved.wait_recv()
    own_cot.wait()
    gvec[...] = jnp.zeros_like(gvec)

    def transpose_rows(dst, s, value):
        dst[:, 128 * s : 128 * s + 128] = value.astype(F32).T.astype(BF16)

    total = jnp.zeros((1, 768), F32)
    for s in range(4):
        transpose_rows(ta, s, cot_in[s])
        total = total + jnp.sum(cot_in[s].astype(F32), axis=0, keepdims=True)
    gvec[7:8, :] = total

    def reduce_back(s):
        yy, cc = lax.div(s, 2), lax.rem(s, 2)
        grad = dot_nn(ta[...], act[block_rows(s), :]).astype(BF16)
        for zz in range(zs):
            for xx in range(2):
                for h in range(2):
                    row = 96 * (2 * zz + xx) + 48 * h
                    for t in range(6):
                        ubuf[0, h, cc, yy, xx, zz, 48 * t : 48 * t + 48, :] = grad[
                            row : row + 48, 128 * t : 128 * t + 128
                        ]

    loop(4, reduce_back)
    each(rs_zero, grad_w2)()
    each(ag_four, unit_w2)()
    each(rs_one, grad_w2)()
    each(ag_done, unit_w2)()

    def cotangent_rows():
        return jnp.concatenate([cot_in[s] for s in range(4)], axis=0)

    def inner_back(s):
        grad = dot_nn(cotangent_rows(), reduce_block(s)) * gp[block_rows(s), :].astype(F32)
        low = grad.astype(BF16)
        gp[block_rows(s), :] = low
        gvec[pl.ds(8 + s, 1), :] = jnp.sum(low.astype(F32), axis=0, keepdims=True)

    loop(4, inner_back)

    acc[...] = h1[...] + vec[7:8, :]

    def reduce(s):
        acc[...] += dot_nt(act[block_rows(s), :], reduce_block(s))

    loop(4, reduce)
    for s in range(4):
        stage[s] = acc[128 * s : 128 * s + 128, :].astype(BF16)
    own_out = pltpu.make_async_copy(stage.at[i], out.at[i], local_sem.at[2])
    own_out.start()
    result_out = exchange(stage, out, 2)
    for moved in result_out:
        moved.start()

    for s in range(4):
        transpose_rows(tb, s, n2[128 * s : 128 * s + 128, :])

    def expand_back(s):
        for xx in range(2):
            grad = dot_nn(tb[...], gp[block_rows(s), 384 * xx : 384 * xx + 384]).astype(BF16)
            for yy in range(2):
                for cc in range(2):
                    for h in range(2):
                        row = 192 * (2 * yy + cc) + 96 * h
                        for t in range(3):
                            ubuf[2, h, cc, yy, xx, s, 96 * t : 96 * t + 96, :] = grad[
                                row : row + 96, 128 * t : 128 * t + 128
                            ]

    loop(4, expand_back)
    each(rs_zero, grad_w1)()
    each(rs_two, grad_w2)()

    def norm_back(s):
        whole = jnp.concatenate([expand_piece(s, 0), expand_piece(s, 1)], axis=1)
        part = dot_nt(gp[block_rows(s), :], whole)

        @pl.when(s == 0)
        def _():
            acc[...] = part

        @pl.when(s > 0)
        def _():
            acc[...] += part

    loop(4, norm_back, ((1, each(rs_one, grad_w1)),))

    def norm_gradient(value, scale_row, grad):
        unit, scale = normalise(value)
        gain_sum = jnp.sum(grad * unit, axis=0, keepdims=True)
        bias_sum = jnp.sum(grad, axis=0, keepdims=True)
        inner = grad * scale_row
        mean = jnp.mean(inner, axis=-1, keepdims=True)
        along = jnp.mean(inner * unit, axis=-1, keepdims=True)
        return scale * (inner - mean - unit * along), gain_sum, bias_sum

    def hidden_back(s):
        rows = rows_of(s)
        grad, gain_sum, bias_sum = norm_gradient(h1[rows, :], vec[5:6, :], acc[rows, :])
        grad = grad + cot_in[s].astype(F32)
        h1[rows, :] = grad
        low = grad.astype(BF16)
        n2[rows, :] = low
        gvec[5:6, :] += gain_sum
        gvec[6:7, :] += bias_sum
        gvec[4:5, :] += jnp.sum(low.astype(F32), axis=0, keepdims=True)

    loop(4, hidden_back)

    for n in range(3):
        value = dot_nn(n2[...], at[3, :, 256 * n : 256 * n + 256]).astype(BF16)
        d6[2 * n] = value[:, 0:128]
        d6[2 * n + 1] = value[:, 128:256]
    for s in range(4):
        transpose_rows(tc, s, n2[128 * s : 128 * s + 128, :])
    act[768:1536, :] = dot_nn(tc[...], lane_tiles(o6)).astype(BF16)
    each(rs_three, grad_w2)()

    def attend_back(p):
        rows = rows_of(p)
        queries, keys, values, grads_in = q6[p], k6[p], v6[p], d6[p]
        keys_t = keys.astype(F32).T.astype(BF16)
        grad_query, grad_key, grad_value = [], 0.0, 0.0
        for which in range(2):
            probs = pt[2 * p + which]
            wide = probs.astype(F32)
            grad_probs = dot_nt(half_of(values, which), grads_in)
            inner = jnp.sum(wide * grad_probs, axis=0, keepdims=True)
            grad_scores = (wide * (grad_probs - inner)).astype(BF16)
            grad_query.append(dot_nn(keys_t[64 * which : 64 * which + 64, :], grad_scores))
            grad_key = grad_key + dot_nn(grad_scores, half_of(queries, which))
            grad_value = grad_value + dot_nn(probs, half_of(grads_in, which))
        grad_query = jnp.concatenate(grad_query, axis=0) * HEAD ** (-0.5)
        ta[rows, :] = grad_query.astype(BF16)
        tb[rows, :] = grad_key.T.astype(BF16)
        tc[rows, :] = grad_value.T.astype(BF16)
        q6[p] = grad_query.T.astype(BF16)
        k6[p] = grad_key.astype(BF16)
        v6[p] = grad_value.astype(BF16)

    def pack(p, part, first_row, second_row):
        def body(s):
            for xx in range(2):
                offset = (2 * s + xx) * 96
                rows = [pl.ds(pl.multiple_of(first_row + offset, 96), 96),
                        pl.ds(pl.multiple_of(second_row + offset, 96), 96)]
                first = ubuf.at[1, p, 0, :, xx, part * half_zs + s]
                second = ubuf.at[1, p, 1, :, xx, part * half_zs + s]
                for yy in range(2):
                    lo, mid, hi = 384 * yy, 384 * yy + 128, 384 * yy + 256
                    for m in range(2):
                        first[yy, 96 * m : 96 * m + 96, :] = act[rows[m], lo : lo + 128]
                        second[yy, 96 * m : 96 * m + 96, :] = act[rows[m], hi : hi + 128]
                    even = act[rows[0], mid : mid + 128].astype(F32)
                    odd = pltpu.roll(act[rows[1], mid : mid + 128].astype(F32), 64, 1)
                    first[yy, 192:288, :] = jnp.where(lanes < 64, even, odd).astype(BF16)
                    second[yy, 192:288, :] = jnp.where(lanes < 64, odd, even).astype(BF16)

        loop(half_zs, body)

    def attention_gradients(part):
        rows = slice(384 * part, 384 * part + 384)
        act[1536:1920, :] = dot_nn(tc[rows, :], n1[...]).astype(BF16)
        pack(1, part, 1536, 768 + 384 * part)
        rs_zero(grad_a[part][1])
        act[0:384, :] = dot_nn(ta[rows, :], n1[...]).astype(BF16)
        act[384:768, :] = dot_nn(tb[rows, :], n1[...]).astype(BF16)
        pack(0, part, 0, 384)
        rs_zero(grad_a[part][0])

    loop(3, attend_back, ((0, each(rs_two, grad_w1)), (1, each(rs_done, grad_w2))))
    attention_gradients(0)
    loop(3, lambda p: attend_back(p + 3), (
        (0, each(rs_one, grad_a[0])),
        (1, each(rs_three, grad_w1)),
        (2, each(rs_two, grad_a[0])),
    ))
    attention_gradients(1)
    each(rs_one, grad_a[1])()
    each(rs_done, grad_w1)()

    acc[...] = dot_nn(lane_tiles(q6), at[0])
    acc[...] += dot_nn(lane_tiles(k6), at[1])
    acc[...] += dot_nn(lane_tiles(v6), at[2])
    gvec[2:3, :] = jnp.sum(lane_tiles(q6).astype(F32), axis=0, keepdims=True)
    gvec[3:4, :] = jnp.sum(lane_tiles(v6).astype(F32), axis=0, keepdims=True)
    each(rs_three, grad_a[0])()

    for moved in result_out:
        moved.wait_send()
    own_out.wait()

    def input_back(s):
        rows = rows_of(s)
        grad, gain_sum, bias_sum = norm_gradient(x_in[s].astype(F32), vec[0:1, :], acc[rows, :])
        stage[s] = (grad + h1[rows, :]).astype(BF16)
        gvec[0:1, :] += gain_sum
        gvec[1:2, :] += bias_sum

    loop(4, input_back)
    own_grad = pltpu.make_async_copy(stage.at[i], ig.at[i], local_sem.at[3])
    own_grad.start()
    grad_out = exchange(stage, ig, 3)
    for moved in grad_out:
        moved.start()

    gvec_steps = small_sum(gvec, gin, 1)
    gvec_steps[0]()
    each(rs_two, grad_a[1])()
    gvec_steps[1]()
    each(rs_done, grad_a[0])()
    gvec_steps[2]()
    gvec_steps[3]()
    each(rs_three, grad_a[1])()
    gvec_steps[4]()
    each(rs_done, grad_a[1])()

    own_grad.wait()
    for moved in tokens_out + cot_out + grad_out:
        moved.wait_send()
    for moved in exchange_landed(out, 2) + exchange_landed(ig, 3):
        moved.wait_recv()


def exchange_kernel(sub, tokens, masked, vec, a_own, w1_own, w2_own):
    zs = GROUPS // 2
    seqs, block, width = tokens.shape
    rows = seqs * block
    vmem = lambda shape, dtype: pltpu.VMEM(shape, dtype)
    piece = a_own.shape[1:]
    scratch = [vmem((3, 2, 2, 2, 2, zs) + piece, BF16)]
    scratch += [vmem((6, 2, 2, zs) + piece, BF16), vmem((6, 2, zs) + piece, BF16)]
    scratch += [vmem((6, zs) + piece, BF16), vmem((6, zs - 1) + piece, BF16)]
    scratch += [vmem(tokens.shape, BF16)] * 3
    scratch += [vmem((16, width), F32)]
    scratch += [vmem((zs + 2, 16, width), F32)] * 2
    tiles = vmem((width // 128, rows, 128), BF16)
    flat = vmem((rows, width), BF16)
    turned = vmem((width, rows), BF16)
    scratch += [vmem((4, width, width), BF16), flat, tiles, tiles, tiles, tiles]
    scratch += [vmem((HEADS, rows, rows), BF16), vmem((rows, width), F32), vmem((rows, width), F32)]
    scratch += [flat, vmem((4 * rows, width), BF16), vmem((4 * rows, width), BF16)]
    scratch += [turned, turned, turned, tiles]
    scratch += [pltpu.SemaphoreType.DMA((4,))]
    scratch += [pltpu.SemaphoreType.DMA((6, 3 * zs + 4))] * 2
    scratch += [pltpu.SemaphoreType.DMA((8, zs + 3))] * 2
    scratch += [pltpu.SemaphoreType.DMA((4, 3))] * 2
    scratch += [pltpu.SemaphoreType.DMA((2, zs + 2))] * 2
    in_vmem = pl.BlockSpec(memory_space=pltpu.VMEM)
    anywhere = pl.BlockSpec(memory_space=pl.ANY)
    return pl.pallas_call(
        functools.partial(kernel, sub, zs),
        out_shape=(
            jax.ShapeDtypeStruct(tokens.shape, BF16),
            jax.ShapeDtypeStruct(tokens.shape, BF16),
            jax.ShapeDtypeStruct(a_own.shape, F32),
            jax.ShapeDtypeStruct(w1_own.shape, F32),
            jax.ShapeDtypeStruct(w2_own.shape, F32),
            jax.ShapeDtypeStruct(vec.shape, F32),
        ),
        in_specs=[anywhere, anywhere] + [in_vmem] * 4,
        out_specs=(anywhere, anywhere) + (in_vmem,) * 4,
        scratch_shapes=scratch,
        compiler_params=pltpu.CompilerParams(
            collective_id=0, has_side_effects=True, vmem_limit_bytes=63 * 1024 * 1024
        ),
    )(tokens, masked, vec, a_own, w1_own, w2_own)


def to_pieces(matrix):
    rows, columns = matrix.shape
    value = matrix.reshape(2, rows // 2, columns // 128, 128)
    return jnp.swapaxes(value, 1, 2).reshape(2, -1, 128)


def from_pieces(pieces, shape):
    rows, columns = shape
    value = pieces.reshape(2, columns // 128, rows // 2, 128)
    return jnp.swapaxes(value, 1, 2).reshape(shape)


def local(
    sub,
    tokens,
    cotangent,
    span_mask,
    attention_weight,
    expand_weight,
    reduce_weight,
    vectors,
    attention_first,
    attention_second,
    expand_first,
    expand_second,
    reduce_first,
    reduce_second,
    vector_first,
    vector_second,
):
    core = lax.rem(lax.axis_index("blk"), 2)
    together = [[n * sub + m for m in range(sub)] for n in range(GROUPS)]

    def widen(value, axis):
        if sub == 1:
            return value
        return lax.all_gather(value, "batch", axis=axis, tiled=True, axis_index_groups=together)

    def narrow(value, axis):
        if sub == 1:
            return value
        return lax.psum_scatter(
            value, "batch", scatter_dimension=axis, tiled=True, axis_index_groups=together
        )

    masked = (cotangent.astype(F32) * span_mask[..., None].astype(F32)).astype(BF16)

    a_low = jnp.swapaxes(widen(attention_weight.astype(BF16), 2), 1, 2)
    columns, depth = a_low.shape[1:]
    main = jnp.where(core == 0, a_low[:, :, :128], a_low[:, :, 64:])
    rest = jnp.where(core == 0, a_low[:, :, 128:], a_low[:, :, :64])
    rest = rest.reshape(2, 2, columns, 64)
    rest = jnp.where(
        core == 0,
        jnp.concatenate([rest[:, 0], rest[:, 1]], axis=-1),
        jnp.concatenate([rest[:, 1], rest[:, 0]], axis=-1),
    )
    a_own = jnp.concatenate([main.reshape(2, 2 * columns, 128), rest], axis=1)
    w1_low = widen(expand_weight.astype(BF16), 1)
    w1_own = to_pieces(w1_low)
    w2_low = widen(reduce_weight.astype(BF16), 1).T
    w2_own = to_pieces(w2_low)
    vec_low = widen(vectors.astype(BF16), 1).astype(F32)
    row = vec_low.shape[0] * lax.axis_index("blk")
    column = vec_low.shape[1] * lax.div(lax.axis_index("batch"), sub)
    vec = lax.dynamic_update_slice(jnp.zeros((16, tokens.shape[2]), F32), vec_low, (row, column))

    out_tokens, input_grad, ga, gw1, gw2, gvec = exchange_kernel(
        sub, tokens, masked, vec, a_own, w1_own, w2_own
    )

    main, rest = ga[:, : 2 * columns].reshape(4, columns, 128), ga[:, 2 * columns :]
    low, high = rest[:, :, :64], rest[:, :, 64:]
    rest = jnp.where(core == 0, jnp.stack([low, high], axis=1), jnp.stack([high, low], axis=1))
    rest = rest.reshape(4, columns, 64)
    attention_sum = jnp.where(
        core == 0,
        jnp.concatenate([main, rest], axis=-1),
        jnp.concatenate([rest, main], axis=-1),
    )
    attention_sum = narrow(jnp.swapaxes(attention_sum, 1, 2), 2)
    expand_sum = narrow(from_pieces(gw1, w1_low.shape), 1)
    reduce_sum = narrow(from_pieces(gw2, w2_low.shape).T, 1)
    vector_sum = narrow(lax.dynamic_slice(gvec, (row, column), vec_low.shape), 1)

    attention_new, attention_one, attention_two = adamw(
        attention_weight, attention_first, attention_second, attention_sum, rate_attention
    )
    expand_new, expand_one, expand_two = adamw(
        expand_weight, expand_first, expand_second, expand_sum, rate_expand
    )
    reduce_new, reduce_one, reduce_two = adamw(
        reduce_weight, reduce_first, reduce_second, reduce_sum, rate_reduce
    )
    vector_new, vector_one, vector_two = adamw(
        vectors, vector_first, vector_second, vector_sum, rate_vector
    )
    return (
        out_tokens,
        input_grad.astype(F32),
        attention_new,
        attention_one,
        attention_two,
        expand_new,
        expand_one,
        expand_two,
        reduce_new,
        reduce_one,
        reduce_two,
        vector_new,
        vector_one,
        vector_two,
    )


def solution(mesh):
    sub = mesh.shape["batch"] // GROUPS
    sequences = P("batch", "blk", None)
    attention = P(None, "blk", "batch")
    matrix = P("blk", "batch")
    return jax.shard_map(
        functools.partial(local, sub),
        mesh=mesh,
        in_specs=(sequences, sequences, P("batch", "blk"), attention, matrix, matrix, matrix)
        + (attention,) * 2
        + (matrix,) * 6,
        out_specs=(sequences,) * 2 + (attention,) * 3 + (matrix,) * 9,
        check_vma=False,
    )
```

```python
import functools
import math

import jax
import jax.numpy as jnp
from jax import lax
from jax.experimental import pallas as pl
from jax.experimental.pallas import tpu as pltpu
from jax.sharding import PartitionSpec as P

HEADS = 12
HEAD = 64
STEP = 10
GROUPS = 8

norm_epsilon = 1e-05
beta_one = 0.9
beta_two = 0.999
adam_epsilon = 1e-08
decay_weight = 0.1
rate_attention = 0.05
rate_expand = 0.03
rate_reduce = 0.015
rate_vector = 0.4

F32 = jnp.float32
BF16 = jnp.bfloat16
MESH = pl.DeviceIdType.MESH
GELU_SCALE = math.sqrt(2.0 / math.pi)
GELU_CUBE = 0.044715


def adamw(weight, moment_one, moment_two, gradient, step_rate):
    moment_one = beta_one * moment_one + (1.0 - beta_one) * gradient
    moment_two = beta_two * moment_two + (1.0 - beta_two) * gradient * gradient
    corrected_one = moment_one / (1.0 - beta_one**STEP)
    corrected_two = moment_two / (1.0 - beta_two**STEP)
    updated = weight - step_rate * (
        corrected_one / (jnp.sqrt(corrected_two) + adam_epsilon) + decay_weight * weight
    )
    return (updated, moment_one, moment_two)


def dot_nn(left, right):
    return lax.dot_general(left, right, (((1,), (0,)), ((), ())), preferred_element_type=F32)


def dot_nt(left, right):
    return lax.dot_general(left, right, (((1,), (1,)), ((), ())), preferred_element_type=F32)


def lane_tiles(ref, count=6):
    return jnp.concatenate([ref[t] for t in range(count)], axis=1)


class Unit:
    def __init__(self, order, u, long_axis, fine):
        self.order, self.u, self.long_axis, self.fine = order, u, long_axis, fine


class Gradient:
    def __init__(self, order, u, long_axis, first, count, whole, core_in, long_in, mid_in, line_in, finish):
        self.order, self.long_axis, self.first, self.count, self.whole = order, long_axis, first, count, whole
        self.u, self.core_in, self.long_in, self.mid_in, self.line_in = u, core_in, long_in, mid_in, line_in
        self.finish = finish


def kernel(sub, zs, *refs):
    (tok, cot, mask_in, vec_in, a_in, w1_in, w2_in,
     out, ig, ga, g1, g2, gv,
     ubuf, core_in, long_in, mid_in, line_in,
     x_in, cot_in, stage, vec, gvec, vin, gin, narrow_rows,
     at, n1, q6, k6, v6, o6, pt, h1, acc, n2, act, gp, ta, tb, tc, d6,
     local_sem, ag_send, ag_recv, rs_send, rs_recv, a2a_send, a2a_recv, v_send, v_recv) = refs

    i = lax.axis_index("blk")
    b = lax.axis_index("batch")
    c, y = lax.rem(i, 2), lax.div(i, 2)
    g, r = lax.div(b, sub), lax.rem(b, sub)
    x, z = lax.rem(g, 2), lax.div(g, 2)

    def device(c_=c, y_=y, x_=x, z_=z):
        return {"blk": 2 * y_ + c_, "batch": (2 * z_ + x_) * sub + r}

    def z_at(k):
        return lax.rem(z + k, zs)

    def block_at(k):
        return lax.rem(i + k, 4)

    def copy(src, dst, send, recv, to):
        return pltpu.make_async_remote_copy(
            src_ref=src, dst_ref=dst, send_sem=send, recv_sem=recv, device_id=to, device_id_type=MESH
        )

    def loop(count, body, hooks=()):
        def step(s, carry):
            body(s)
            for k, *todo in hooks:

                @pl.when(s == k)
                def _():
                    for f in todo:
                        f()

            return carry

        lax.fori_loop(0, count, step, 0)

    partners = [device(z_=z_at(k)) for k in range(1, zs)]
    partners += [device(x_=1 - x), device(y_=1 - y), device(c_=1 - c), device(c_=1 - c, y_=1 - y)]
    barrier = pltpu.get_barrier_semaphore()
    for partner in partners:
        pl.semaphore_signal(barrier, inc=1, device_id=partner, device_id_type=MESH)
    pl.semaphore_wait(barrier, len(partners))

    def ag_sems(n, slot):
        return ag_send.at[n.order, slot], ag_recv.at[n.order, slot]

    def group(n, u, long_off, mid_off, cut=None):
        yy = y if (long_off if n.long_axis == "y" else mid_off) == 0 else 1 - y
        xx = x if (long_off if n.long_axis == "x" else mid_off) == 0 else 1 - x
        return u.at[c, yy, xx] if cut is None else u.at[c, yy, xx, cut]

    def partner_of(n, step):
        axis = n.long_axis if step == "long" else {"x": "y", "y": "x"}[n.long_axis]
        return device(x_=1 - x) if axis == "x" else device(y_=1 - y)

    LINE, MID, LONG, LAST, CORE = 0, zs - 1, 2 * zs - 1, 3 * zs - 1, 3 * zs

    def ag_line(n, k, landed=False):
        ref = group(n, n.u, 0, 0, z_at(zs - k) if landed else z)
        return copy(ref, ref, *ag_sems(n, LINE + k - 1), device(z_=z_at(k)))

    def ag_first(n, step, k, landed=False):
        cut = z_at(zs - k) if n.fine else None
        off = (0, 1) if step == "mid" else (1, 0)
        ref = group(n, n.u, *(off if landed else (0, 0)), cut)
        return copy(ref, ref, *ag_sems(n, (MID if step == "mid" else LONG) + k), partner_of(n, step))

    def ag_last(n, landed=False):
        ref = group(n, n.u, 1 if landed else 0, 1)
        return copy(ref, ref, *ag_sems(n, LAST), partner_of(n, "long"))

    def ag_core(n, long_off, mid_off, landed=False):
        ref = group(n, n.u, long_off, mid_off)
        if landed:
            yy = y if (long_off if n.long_axis == "y" else mid_off) == 0 else 1 - y
            xx = x if (long_off if n.long_axis == "x" else mid_off) == 0 else 1 - x
            ref = n.u.at[1 - c, yy, xx]
        return copy(ref, ref, *ag_sems(n, CORE + 2 * long_off + mid_off), device(c_=1 - c))

    def parts(n):
        return range(zs) if n.fine else range(1)

    def ag_start(n):
        if n.fine:
            for step in ("mid", "long"):
                ag_first(n, step, 0).start()
        for k in range(1, zs):
            ag_line(n, k).start()

    def ag_piece(n, k):
        ag_line(n, k, True).wait_recv()
        for step in ("mid", "long"):
            ag_first(n, step, k).start()

    def ag_one(n):
        if not n.fine:
            for k in range(1, zs):
                ag_line(n, k, True).wait_recv()
            for step in ("mid", "long"):
                ag_first(n, step, 0).start()
        ag_core(n, 0, 0).start()

    def ag_two(n):
        for k in parts(n):
            ag_first(n, "mid", k, True).wait_recv()
        ag_last(n).start()
        ag_core(n, 0, 1).start()

    def ag_three(n):
        for k in parts(n):
            ag_first(n, "long", k, True).wait_recv()
        ag_core(n, 1, 0).start()

    def ag_four(n):
        ag_last(n, True).wait_recv()
        ag_core(n, 1, 1).start()

    def ag_done(n):
        for off in ((0, 0), (0, 1), (1, 0), (1, 1)):
            ag_core(n, *off, True).wait_recv()
        for k in range(1, zs):
            ag_line(n, k).wait_send()
        for step in ("mid", "long"):
            for k in parts(n):
                ag_first(n, step, k).wait_send()
        ag_last(n).wait_send()
        for off in ((0, 0), (0, 1), (1, 0), (1, 1)):
            ag_core(n, *off).wait_send()

    def rs_sems(n, slot):
        return rs_send.at[n.order, slot], rs_recv.at[n.order, slot]

    def cut_of(n):
        return slice(None) if n.count == zs else pl.ds(n.first, n.count)

    def rs_core(n, long_off):
        place = 1 - (y if n.long_axis == "y" else x) if long_off else (y if n.long_axis == "y" else x)
        where = (place, slice(None)) if n.long_axis == "y" else (slice(None), place)
        return copy(n.u.at[(1 - c,) + where + (cut_of(n),)], n.core_in.at[where],
                    *rs_sems(n, long_off), device(c_=1 - c))

    def rs_long(n):
        where = (1 - y, slice(None)) if n.long_axis == "y" else (slice(None), 1 - x)
        return copy(n.u.at[(c,) + where + (cut_of(n),)], n.long_in, *rs_sems(n, 2), partner_of(n, "long"))

    def rs_mid(n):
        return copy(group(n, n.u, 0, 1, cut_of(n)), n.mid_in, *rs_sems(n, 3), partner_of(n, "mid"))

    def rs_line(n, k):
        return copy(group(n, n.u, 0, 0, z_at(k)), n.line_in.at[k - 1], *rs_sems(n, 3 + k), device(z_=z_at(k)))

    def within(n, place):
        return jnp.logical_and(place >= n.first, place < n.first + n.count)

    def when_within(n, place, f):
        if n.whole:
            f()
        else:
            pl.when(within(n, place))(f)

    def gather_terms(n, long_off, mid_off, names):
        yy = y if (long_off if n.long_axis == "y" else mid_off) == 0 else 1 - y
        xx = x if (long_off if n.long_axis == "x" else mid_off) == 0 else 1 - x

        def body(s):
            mine = n.u.at[c, yy, xx, n.first + s]
            value = mine[...].astype(F32) + n.core_in[yy, xx, s].astype(F32)
            if "long" in names:
                value = value + n.long_in[xx if n.long_axis == "y" else yy, s].astype(F32)
            if "mid" in names:
                value = value + n.mid_in[s].astype(F32)
            mine[...] = value.astype(BF16)

        loop(n.count, body)

    def rs_zero(n):
        rs_core(n, 1).start()
        rs_core(n, 0).start()

    def rs_one(n):
        rs_core(n, 1).wait_recv()
        gather_terms(n, 1, 0, ())
        gather_terms(n, 1, 1, ())
        rs_long(n).start()

    def rs_two(n):
        rs_core(n, 0).wait_recv()
        rs_long(n).wait_recv()
        gather_terms(n, 0, 1, ("long",))
        rs_mid(n).start()

    def rs_three(n):
        rs_mid(n).wait_recv()
        gather_terms(n, 0, 0, ("long", "mid"))
        for k in range(1, zs):
            when_within(n, z_at(k), lambda k=k: rs_line(n, k).start())

    def rs_done(n):
        def finish():
            for k in range(1, zs):
                rs_line(n, k).wait_recv()
            value = n.u[c, y, x, z].astype(F32)
            for k in range(1, zs):
                value = value + n.line_in[k - 1].astype(F32)
            n.finish(value)

        when_within(n, z, finish)
        for moved in (rs_core(n, 0), rs_core(n, 1), rs_long(n), rs_mid(n)):
            moved.wait_send()
        for k in range(1, zs):
            when_within(n, z_at(k), lambda k=k: rs_line(n, k).wait_send())

    def small_sum(ref, slots, which):
        to = (device(y_=1 - y), device(c_=1 - c), device(x_=1 - x))
        to += tuple(device(z_=z_at(k)) for k in range(1, zs))

        def moved(slot):
            return copy(ref, slots.at[slot], v_send.at[which, slot], v_recv.at[which, slot], to[slot])

        def land(last):
            moved(last).wait()
            ref[...] = ref[...] + slots[last]

        def step(n):
            def run():
                if n > 0:
                    land(n - 1)
                moved(n).start()

            return run

        def line():
            land(2)
            for k in range(1, zs):
                moved(2 + k).start()

        def finish():
            for k in range(1, zs):
                moved(2 + k).wait()
            value = ref[...]
            for k in range(1, zs):
                value = value + slots[2 + k]
            ref[...] = value

        return [step(0), step(1), step(2), line, finish]

    def exchange(src, dst, which):
        return [copy(src.at[block_at(k)], dst.at[i], a2a_send.at[which, k - 1],
                     a2a_recv.at[which, k - 1], {"blk": block_at(k), "batch": b})
                for k in range(1, 4)]

    def exchange_landed(dst, which):
        return [copy(dst.at[block_at(4 - k)], dst.at[block_at(4 - k)], a2a_send.at[which, k - 1],
                     a2a_recv.at[which, k - 1], {"blk": block_at(4 - k), "batch": b})
                for k in range(1, 4)]

    units = [Unit(2 * n + half, ubuf.at[n, half], axes[half], n == 0)
             for n, axes in enumerate(("xy", "yx", "yx")) for half in range(2)]
    unit_qk, unit_vo, unit_w1, unit_w2 = units[0], units[1], units[2:4], units[4:6]

    def rest_rows(matrix):
        return a_in[matrix, pl.ds(pl.multiple_of(128 * (1 - c), 64), 64), :]

    def own_attention(p):
        mine = ubuf.at[0, p, c, y, x, z]
        for m in range(2):
            main = a_in[2 * p + m, pl.ds(pl.multiple_of(64 * c, 64), 128), :]
            mine[96 * m : 96 * m + 96, :] = main.T.astype(BF16)
        rest = jnp.concatenate([rest_rows(2 * p + c), rest_rows(2 * p + 1 - c)], axis=0)
        mine[192:288, :] = rest.T.astype(BF16)

    def own_feed_forward():
        for h in range(2):
            for t in range(3):
                ubuf[1, h, c, y, x, z, 96 * t : 96 * t + 96, :] = w1_in[
                    96 * h : 96 * h + 96, 128 * t : 128 * t + 128
                ].astype(BF16)
            for t in range(6):
                ubuf[2, h, c, y, x, z, 48 * t : 48 * t + 48, :] = w2_in[
                    48 * h : 48 * h + 48, 128 * t : 128 * t + 128
                ].astype(BF16)

    columns = a_in.shape[2]
    placed = lax.broadcasted_iota(jnp.int32, (columns, 768), 1) == (
        lax.broadcasted_iota(jnp.int32, (columns, 768), 0) + columns * g
    )

    def own_vectors():
        vec[...] = jnp.zeros_like(vec)
        rows = dot_nn(vec_in[...].astype(BF16), jnp.where(placed, 1.0, 0.0).astype(BF16))
        for j in range(3):
            vec[pl.ds(3 * i + j, 1), :] = rows[j : j + 1, :]

    def masked_cotangent():
        eye = lax.broadcasted_iota(jnp.int32, (128, 128), 0) == lax.broadcasted_iota(jnp.int32, (128, 128), 1)
        for s in range(4):
            row = jnp.broadcast_to(mask_in[s : s + 1, :].astype(F32), (128, 128))
            column = jnp.sum(jnp.where(eye, row, 0.0), axis=1, keepdims=True)
            stage[s] = (cot[s].astype(F32) * column).astype(BF16)

    def finish_attention(p):
        def finish(value):
            for m in range(2):
                ga[2 * p + m, pl.ds(pl.multiple_of(64 * c, 64), 128), :] = value[96 * m : 96 * m + 96, :].T
            rest = value[192:288, :].T
            rows = pl.ds(pl.multiple_of(128 * (1 - c), 64), 64)
            ga[2 * p + c, rows, :] = rest[0:64, :]
            ga[2 * p + 1 - c, rows, :] = rest[64:128, :]

        return finish

    def finish_expand(h):
        def finish(value):
            for t in range(3):
                g1[96 * h : 96 * h + 96, 128 * t : 128 * t + 128] = value[96 * t : 96 * t + 96, :]

        return finish

    def finish_reduce(h):
        def finish(value):
            for t in range(6):
                g2[48 * h : 48 * h + 48, 128 * t : 128 * t + 128] = value[48 * t : 48 * t + 48, :]

        return finish

    def finish_vectors():
        value, total = gvec[...], 0.0
        for _ in range(3):
            part = value.astype(BF16)
            total = total + dot_nt(part, jnp.where(placed, 1.0, 0.0).astype(BF16))
            value = value - part.astype(F32)
        narrow_rows[...] = total
        for j in range(3):
            gv[j : j + 1, :] = narrow_rows[pl.ds(3 * i + j, 1), :]

    grads = []
    half_zs = zs // 2
    for n, (source, finish) in enumerate(((0, finish_reduce), (2, finish_expand))):
        for half in range(2):
            order = 2 * n + half
            grads.append(Gradient(order, ubuf.at[source, half], "yx"[half], 0, zs, True,
                                  core_in.at[order], long_in.at[order], mid_in.at[order],
                                  line_in.at[order], finish(half)))
    for part in range(2):
        for half in range(2):
            cut = pl.ds(part * half_zs, half_zs)
            grads.append(Gradient(4 + 2 * part + half, ubuf.at[1, half], "xy"[half], part * half_zs, half_zs,
                                  False, core_in.at[4 + half, :, :, cut], long_in.at[4 + half, :, cut],
                                  mid_in.at[4 + half, cut], line_in.at[4 + half], finish_attention(half)))
    grad_w2, grad_w1, grad_a = grads[0:2], grads[2:4], (grads[4:6], grads[6:8])

    def each(f, which):
        def run():
            for n in which:
                f(n)

        return run

    own_attention(0)
    ag_start(unit_qk)
    own_vectors()
    vec_steps = small_sum(vec, vin, 0)
    vec_steps[0]()
    own_tokens = pltpu.make_async_copy(tok.at[i], x_in.at[i], local_sem.at[0])
    own_tokens.start()
    tokens_out = exchange(tok, x_in, 0)
    for moved in tokens_out:
        moved.start()
    own_attention(1)
    own_feed_forward()
    for k in range(1, zs):
        ag_piece(unit_qk, k)
    ag_one(unit_qk)
    ag_start(unit_vo)
    vec_steps[1]()
    masked_cotangent()
    ag_two(unit_qk)
    vec_steps[2]()
    for k in range(1, zs):
        ag_piece(unit_vo, k)
    ag_one(unit_vo)
    vec_steps[3]()
    each(ag_start, unit_w1)()
    ag_three(unit_qk)

    for moved in exchange_landed(x_in, 0):
        moved.wait_recv()
    own_tokens.wait()
    vec_steps[4]()

    def normalise(value):
        centered = value - jnp.mean(value, axis=-1, keepdims=True)
        scale = lax.rsqrt(jnp.mean(centered * centered, axis=-1, keepdims=True) + norm_epsilon)
        return centered * scale, scale

    def rows_of(s):
        return pl.ds(pl.multiple_of(s * 128, 128), 128)

    def first_norm(s):
        unit, _ = normalise(x_in[s].astype(F32))
        n1[rows_of(s), :] = (unit * vec[0:1, :] + vec[1:2, :]).astype(BF16)

    loop(4, first_norm)
    ag_four(unit_qk)
    ag_two(unit_vo)
    own_cot = pltpu.make_async_copy(stage.at[i], cot_in.at[i], local_sem.at[1])
    own_cot.start()
    cot_out = exchange(stage, cot_in, 1)
    for moved in cot_out:
        moved.start()
    ag_done(unit_qk)

    lanes = lax.broadcasted_iota(jnp.int32, (96, 128), 1)

    def unpack(p, s):
        for xx in range(2):
            rows = pl.ds(pl.multiple_of((2 * s + xx) * 96, 96), 96)
            for yy in range(2):
                first, second = ubuf.at[0, p, 0, yy, xx, s], ubuf.at[0, p, 1, yy, xx, s]
                lo, hi = 384 * yy, 384 * yy + 256
                for m in range(2):
                    at[2 * p + m, rows, lo : lo + 128] = first[96 * m : 96 * m + 96, :]
                    at[2 * p + m, rows, hi : hi + 128] = second[96 * m : 96 * m + 96, :]
                rest_first = first[192:288, :].astype(F32)
                rest_second = second[192:288, :].astype(F32)
                even = jnp.where(lanes < 64, rest_first, rest_second)
                odd = pltpu.roll(jnp.where(lanes < 64, rest_second, rest_first), 64, 1)
                at[2 * p, rows, lo + 128 : lo + 256] = even.astype(BF16)
                at[2 * p + 1, rows, lo + 128 : lo + 256] = odd.astype(BF16)

    def project(m, dst, bias):
        for n in range(3):
            value = dot_nt(n1[...], at[m, 256 * n : 256 * n + 256, :])
            if bias is not None:
                value = value + vec[bias : bias + 1, 256 * n : 256 * n + 256]
            value = value.astype(BF16)
            if m == 0:
                value = value * jnp.asarray(HEAD ** (-0.5), BF16)
            dst[2 * n] = value[:, 0:128]
            dst[2 * n + 1] = value[:, 128:256]

    loop(zs, functools.partial(unpack, 0))
    project(0, q6, 2)
    project(1, k6, None)

    half_lane = lax.broadcasted_iota(jnp.int32, (1, 128), 1) // HEAD
    half_rows = [jnp.where(half_lane == which, 1.0, 0.0).astype(BF16) for which in range(2)]

    def half_of(value, which):
        return value * half_rows[which]

    def attend(p):
        queries, keys = q6[p], k6[p]
        for which in range(2):
            scores = dot_nt(half_of(keys, which), queries)
            expo = jnp.exp(scores - jnp.max(scores, axis=0, keepdims=True))
            probs = (expo * (1.0 / jnp.sum(expo, axis=0, keepdims=True))).astype(BF16)
            pt[2 * p + which] = probs

    def mix(p):
        values_t = v6[p].T
        mixed = [dot_nn(values_t[64 * which : 64 * which + 64, :], pt[2 * p + which]) for which in range(2)]
        o6[p] = jnp.concatenate(mixed, axis=0).T.astype(BF16)

    loop(6, attend, (
        (2, lambda: ag_three(unit_vo)),
        (4, lambda: ag_four(unit_vo), each(ag_one, unit_w1)),
    ))
    ag_done(unit_vo)
    each(ag_start, unit_w2)()
    loop(zs, functools.partial(unpack, 1))
    project(2, v6, 3)
    each(ag_two, unit_w1)()
    loop(6, mix, (
        (3, each(ag_three, unit_w1)),
        (5, each(ag_four, unit_w1), each(ag_one, unit_w2)),
    ))

    for n in range(3):
        cols = slice(256 * n, 256 * n + 256)
        value = dot_nt(lane_tiles(o6), at[3, cols, :]) + vec[4:5, cols]
        for s in range(4):
            h1[128 * s : 128 * s + 128, cols] = x_in[s, :, cols].astype(F32) + value[128 * s : 128 * s + 128]

    def second_norm(s):
        unit, _ = normalise(h1[rows_of(s), :])
        n2[rows_of(s), :] = (unit * vec[5:6, :] + vec[6:7, :]).astype(BF16)

    loop(4, second_norm)
    each(ag_two, unit_w2)()
    each(ag_done, unit_w1)()

    def expand_piece(s, xx):
        def piece(ref):
            return jnp.concatenate([ref[96 * t : 96 * t + 96, :] for t in range(3)], axis=1)

        return jnp.concatenate(
            [piece(ubuf.at[1, h, cc, yy, xx, s]) for yy in range(2) for cc in range(2) for h in range(2)],
            axis=0,
        )

    def reduce_block(s):
        yy, cc = lax.div(s, 2), lax.rem(s, 2)

        def piece(ref):
            return jnp.concatenate([ref[48 * t : 48 * t + 48, :] for t in range(6)], axis=1)

        return jnp.concatenate(
            [piece(ubuf.at[2, h, cc, yy, xx, zz]) for zz in range(zs) for xx in range(2) for h in range(2)],
            axis=0,
        )

    def block_rows(s):
        return pl.ds(pl.multiple_of(s * 512, 512), 512)

    def expand(s):
        for xx in range(2):
            cols = slice(384 * xx, 384 * xx + 384)
            inner = dot_nn(n2[...], expand_piece(s, xx)) + vec[pl.ds(8 + s, 1), cols]
            square = inner * inner
            tanh = jnp.tanh(GELU_SCALE * inner * (1.0 + GELU_CUBE * square))
            act[block_rows(s), cols] = (0.5 * inner * (1.0 + tanh)).astype(BF16)
            slope = 0.5 * (1.0 + tanh) + 0.5 * inner * (1.0 - tanh * tanh) * (
                GELU_SCALE * (1.0 + 3.0 * GELU_CUBE * square)
            )
            gp[block_rows(s), cols] = slope.astype(BF16)

    loop(4, expand)
    each(ag_three, unit_w2)()

    for moved in exchange_landed(cot_in, 1):
        moved.wait_recv()
    own_cot.wait()
    gvec[...] = jnp.zeros_like(gvec)

    def transpose_rows(dst, s, value):
        dst[:, 128 * s : 128 * s + 128] = value.T

    total = jnp.zeros((1, 768), F32)
    for s in range(4):
        transpose_rows(ta, s, cot_in[s])
        total = total + jnp.sum(cot_in[s].astype(F32), axis=0, keepdims=True)
    gvec[7:8, :] = total

    def reduce_back(s):
        yy, cc = lax.div(s, 2), lax.rem(s, 2)
        grad = dot_nn(ta[...], act[block_rows(s), :]).astype(BF16)
        for zz in range(zs):
            for xx in range(2):
                for h in range(2):
                    row = 96 * (2 * zz + xx) + 48 * h
                    for t in range(6):
                        ubuf[0, h, cc, yy, xx, zz, 48 * t : 48 * t + 48, :] = grad[
                            row : row + 48, 128 * t : 128 * t + 128
                        ]

    loop(4, reduce_back)
    each(rs_zero, grad_w2)()
    each(ag_four, unit_w2)()
    each(rs_one, grad_w2)()
    each(ag_done, unit_w2)()

    def cotangent_rows():
        return jnp.concatenate([cot_in[s] for s in range(4)], axis=0)

    def inner_back(s):
        grad = dot_nn(cotangent_rows(), reduce_block(s)) * gp[block_rows(s), :].astype(F32)
        low = grad.astype(BF16)
        gp[block_rows(s), :] = low
        gvec[pl.ds(8 + s, 1), :] = jnp.sum(low.astype(F32), axis=0, keepdims=True)

    loop(4, inner_back)

    acc[...] = h1[...] + vec[7:8, :]

    def reduce(s):
        acc[...] += dot_nt(act[block_rows(s), :], reduce_block(s))

    loop(4, reduce)
    for moved in cot_out:
        moved.wait_send()
    for s in range(4):
        stage[s] = acc[128 * s : 128 * s + 128, :].astype(BF16)
    own_out = pltpu.make_async_copy(stage.at[i], out.at[i], local_sem.at[2])
    own_out.start()
    result_out = exchange(stage, out, 2)
    for moved in result_out:
        moved.start()

    for s in range(4):
        transpose_rows(tb, s, n2[128 * s : 128 * s + 128, :])

    def expand_back(s):
        for xx in range(2):
            grad = dot_nn(tb[...], gp[block_rows(s), 384 * xx : 384 * xx + 384]).astype(BF16)
            for yy in range(2):
                for cc in range(2):
                    for h in range(2):
                        row = 192 * (2 * yy + cc) + 96 * h
                        for t in range(3):
                            ubuf[2, h, cc, yy, xx, s, 96 * t : 96 * t + 96, :] = grad[
                                row : row + 96, 128 * t : 128 * t + 128
                            ]

    loop(4, expand_back)
    each(rs_zero, grad_w1)()
    each(rs_two, grad_w2)()

    def norm_back(s):
        whole = jnp.concatenate([expand_piece(s, 0), expand_piece(s, 1)], axis=1)
        part = dot_nt(gp[block_rows(s), :], whole)

        @pl.when(s == 0)
        def _():
            acc[...] = part

        @pl.when(s > 0)
        def _():
            acc[...] += part

    loop(4, norm_back, ((1, each(rs_one, grad_w1)),))

    def norm_gradient(value, scale_row, grad):
        unit, scale = normalise(value)
        gain_sum = jnp.sum(grad * unit, axis=0, keepdims=True)
        bias_sum = jnp.sum(grad, axis=0, keepdims=True)
        inner = grad * scale_row
        mean = jnp.mean(inner, axis=-1, keepdims=True)
        along = jnp.mean(inner * unit, axis=-1, keepdims=True)
        return scale * (inner - mean - unit * along), gain_sum, bias_sum

    def hidden_back(s):
        rows = rows_of(s)
        grad, gain_sum, bias_sum = norm_gradient(h1[rows, :], vec[5:6, :], acc[rows, :])
        grad = grad + cot_in[s].astype(F32)
        h1[rows, :] = grad
        low = grad.astype(BF16)
        n2[rows, :] = low
        gvec[5:6, :] += gain_sum
        gvec[6:7, :] += bias_sum
        gvec[4:5, :] += jnp.sum(low.astype(F32), axis=0, keepdims=True)

    loop(4, hidden_back)

    for n in range(3):
        value = dot_nn(n2[...], at[3, :, 256 * n : 256 * n + 256]).astype(BF16)
        d6[2 * n] = value[:, 0:128]
        d6[2 * n + 1] = value[:, 128:256]
    for s in range(4):
        transpose_rows(tc, s, n2[128 * s : 128 * s + 128, :])
    act[768:1536, :] = dot_nn(tc[...], lane_tiles(o6)).astype(BF16)
    each(rs_three, grad_w2)()

    def attend_back(p):
        rows = rows_of(p)
        queries, keys, values, grads_in = q6[p], k6[p], v6[p], d6[p]
        keys_t = keys.T
        grad_query, grad_key, grad_value = [], 0.0, 0.0
        for which in range(2):
            probs = pt[2 * p + which]
            wide = probs.astype(F32)
            grad_probs = dot_nt(half_of(values, which), grads_in)
            inner = jnp.sum(wide * grad_probs, axis=0, keepdims=True)
            grad_scores = (wide * (grad_probs - inner)).astype(BF16)
            grad_query.append(dot_nn(keys_t[64 * which : 64 * which + 64, :], grad_scores))
            grad_key = grad_key + dot_nn(grad_scores, half_of(queries, which))
            grad_value = grad_value + dot_nn(probs, half_of(grads_in, which))
        grad_query = jnp.concatenate(grad_query, axis=0) * HEAD ** (-0.5)
        grad_query = grad_query.astype(BF16)
        grad_key, grad_value = grad_key.astype(BF16), grad_value.astype(BF16)
        ta[rows, :] = grad_query
        tb[rows, :] = grad_key.T
        tc[rows, :] = grad_value.T
        q6[p] = grad_query.T
        k6[p] = grad_key
        v6[p] = grad_value

    def pack(p, part, first_row, second_row):
        def body(s):
            for xx in range(2):
                offset = (2 * s + xx) * 96
                rows = [pl.ds(pl.multiple_of(first_row + offset, 96), 96),
                        pl.ds(pl.multiple_of(second_row + offset, 96), 96)]
                first = ubuf.at[1, p, 0, :, xx, part * half_zs + s]
                second = ubuf.at[1, p, 1, :, xx, part * half_zs + s]
                for yy in range(2):
                    lo, mid, hi = 384 * yy, 384 * yy + 128, 384 * yy + 256
                    for m in range(2):
                        first[yy, 96 * m : 96 * m + 96, :] = act[rows[m], lo : lo + 128]
                        second[yy, 96 * m : 96 * m + 96, :] = act[rows[m], hi : hi + 128]
                    even = act[rows[0], mid : mid + 128].astype(F32)
                    odd = pltpu.roll(act[rows[1], mid : mid + 128].astype(F32), 64, 1)
                    first[yy, 192:288, :] = jnp.where(lanes < 64, even, odd).astype(BF16)
                    second[yy, 192:288, :] = jnp.where(lanes < 64, odd, even).astype(BF16)

        loop(half_zs, body)

    def attention_gradients(part):
        rows = slice(384 * part, 384 * part + 384)
        act[1536:1920, :] = dot_nn(tc[rows, :], n1[...]).astype(BF16)
        pack(1, part, 1536, 768 + 384 * part)
        rs_zero(grad_a[part][1])
        act[0:384, :] = dot_nn(ta[rows, :], n1[...]).astype(BF16)
        act[384:768, :] = dot_nn(tb[rows, :], n1[...]).astype(BF16)
        pack(0, part, 0, 384)
        rs_zero(grad_a[part][0])

    loop(3, attend_back, ((0, each(rs_two, grad_w1)), (1, each(rs_done, grad_w2))))
    attention_gradients(0)
    loop(3, lambda p: attend_back(p + 3), (
        (0, each(rs_one, grad_a[0])),
        (1, each(rs_three, grad_w1)),
        (2, each(rs_two, grad_a[0])),
    ))
    attention_gradients(1)
    each(rs_one, grad_a[1])()
    each(rs_done, grad_w1)()

    acc[...] = dot_nn(lane_tiles(q6), at[0])
    acc[...] += dot_nn(lane_tiles(k6), at[1])
    acc[...] += dot_nn(lane_tiles(v6), at[2])
    gvec[2:3, :] = jnp.sum(lane_tiles(q6).astype(F32), axis=0, keepdims=True)
    gvec[3:4, :] = jnp.sum(lane_tiles(v6).astype(F32), axis=0, keepdims=True)
    each(rs_three, grad_a[0])()

    for moved in result_out:
        moved.wait_send()
    own_out.wait()

    def input_back(s):
        rows = rows_of(s)
        grad, gain_sum, bias_sum = norm_gradient(x_in[s].astype(F32), vec[0:1, :], acc[rows, :])
        stage[s] = (grad + h1[rows, :]).astype(BF16)
        gvec[0:1, :] += gain_sum
        gvec[1:2, :] += bias_sum

    loop(4, input_back)
    gvec_steps = small_sum(gvec, gin, 1)
    gvec_steps[0]()
    own_grad = pltpu.make_async_copy(stage.at[i], ig.at[i], local_sem.at[3])
    own_grad.start()
    grad_out = exchange(stage, ig, 3)
    for moved in grad_out:
        moved.start()

    gvec_steps[1]()
    each(rs_two, grad_a[1])()
    gvec_steps[2]()
    each(rs_done, grad_a[0])()
    gvec_steps[3]()
    each(rs_three, grad_a[1])()
    gvec_steps[4]()
    finish_vectors()
    each(rs_done, grad_a[1])()

    own_grad.wait()
    for moved in tokens_out + grad_out:
        moved.wait_send()
    for moved in exchange_landed(out, 2) + exchange_landed(ig, 3):
        moved.wait_recv()


def layer(sub, tokens, cotangent, span_mask, vectors, attention, expand, reduce_t):
    zs = GROUPS // 2
    seqs, block, width = tokens.shape
    rows = seqs * block
    columns = attention.shape[2]
    piece = (3 * columns, 128)
    vmem = lambda shape, dtype: pltpu.VMEM(shape, dtype)
    scratch = [vmem((3, 2, 2, 2, 2, zs) + piece, BF16)]
    scratch += [vmem((6, 2, 2, zs) + piece, BF16), vmem((6, 2, zs) + piece, BF16)]
    scratch += [vmem((6, zs) + piece, BF16), vmem((6, zs - 1) + piece, BF16)]
    scratch += [vmem(tokens.shape, BF16)] * 3
    scratch += [vmem((16, width), F32)] * 2
    scratch += [vmem((zs + 2, 16, width), F32)] * 2
    scratch += [vmem((16, columns), F32)]
    tiles = vmem((width // 128, rows, 128), BF16)
    flat = vmem((rows, width), BF16)
    turned = vmem((width, rows), BF16)
    scratch += [vmem((4, width, width), BF16), flat, tiles, tiles, tiles, tiles]
    scratch += [vmem((HEADS, rows, rows), BF16), vmem((rows, width), F32), vmem((rows, width), F32)]
    scratch += [flat, vmem((4 * rows, width), BF16), vmem((4 * rows, width), BF16)]
    scratch += [turned, turned, turned, tiles]
    scratch += [pltpu.SemaphoreType.DMA((4,))]
    scratch += [pltpu.SemaphoreType.DMA((6, 3 * zs + 4))] * 2
    scratch += [pltpu.SemaphoreType.DMA((8, zs + 3))] * 2
    scratch += [pltpu.SemaphoreType.DMA((4, 3))] * 2
    scratch += [pltpu.SemaphoreType.DMA((2, zs + 2))] * 2
    in_vmem = pl.BlockSpec(memory_space=pltpu.VMEM)
    anywhere = pl.BlockSpec(memory_space=pl.ANY)
    return pl.pallas_call(
        functools.partial(kernel, sub, zs),
        out_shape=(
            jax.ShapeDtypeStruct(tokens.shape, BF16),
            jax.ShapeDtypeStruct(tokens.shape, BF16),
            jax.ShapeDtypeStruct(attention.shape, F32),
            jax.ShapeDtypeStruct(expand.shape, F32),
            jax.ShapeDtypeStruct(reduce_t.shape, F32),
            jax.ShapeDtypeStruct(vectors.shape, F32),
        ),
        in_specs=[anywhere] + [in_vmem] * 6,
        out_specs=(anywhere, anywhere) + (in_vmem,) * 4,
        scratch_shapes=scratch,
        compiler_params=pltpu.CompilerParams(
            collective_id=0, has_side_effects=True, vmem_limit_bytes=63 * 1024 * 1024
        ),
    )(tokens, cotangent, span_mask, vectors, attention, expand, reduce_t)


def update_kernel(rates, *refs):
    count = len(rates)
    ins, (result, grad) = refs[: 4 * count], refs[4 * count : 4 * count + 2]
    outs, (result_out, grad_out) = refs[4 * count + 2 : 7 * count + 2], refs[7 * count + 2 : 7 * count + 4]
    held, (low, wide) = refs[7 * count + 4 : 11 * count + 4], refs[11 * count + 4 : 11 * count + 6]
    in_sems, out_sems = refs[11 * count + 6 :]
    loads = [pltpu.make_async_copy(ins[n], held[n], in_sems.at[n]) for n in range(4 * count)]
    stores = [pltpu.make_async_copy(held[4 * n + m], outs[3 * n + m], out_sems.at[3 * n + m])
              for n in range(count) for m in range(3)]
    load_grad = pltpu.make_async_copy(grad, low, in_sems.at[4 * count])
    store_grad = pltpu.make_async_copy(wide, grad_out, out_sems.at[3 * count])
    move = pltpu.make_async_copy(result, result_out, out_sems.at[3 * count + 1])
    load_grad.start()
    for copy in loads:
        copy.start()
    move.start()
    load_grad.wait()

    def widen(s, carry):
        wide[s] = low[s].astype(F32)
        return carry

    lax.fori_loop(0, low.shape[0], widen, 0)
    store_grad.start()
    for n in range(count):
        for m in range(4):
            loads[4 * n + m].wait()
        weight, one, two, gradient = held[4 * n : 4 * n + 4]
        values = adamw(weight[...], one[...], two[...], gradient[...], rates[n])
        for ref, value in zip((weight, one, two), values):
            ref[...] = value
        for m in range(3):
            stores[3 * n + m].start()
    for copy in stores + [store_grad, move]:
        copy.wait()


def update(rates, arrays, result, grad):
    flat = [value for group in arrays for value in group]
    new = [jax.ShapeDtypeStruct(value.shape, F32) for group in arrays for value in group[:3]]
    new += [jax.ShapeDtypeStruct(result.shape, BF16), jax.ShapeDtypeStruct(grad.shape, F32)]
    anywhere = pl.BlockSpec(memory_space=pl.ANY)
    scratch = [pltpu.VMEM(value.shape, F32) for value in flat]
    scratch += [pltpu.VMEM(grad.shape, BF16), pltpu.VMEM(grad.shape, F32)]
    scratch += [pltpu.SemaphoreType.DMA((len(flat) + 1,)), pltpu.SemaphoreType.DMA((len(new),))]
    return pl.pallas_call(
        functools.partial(update_kernel, rates),
        out_shape=tuple(new),
        in_specs=[anywhere] * (len(flat) + 2),
        out_specs=(anywhere,) * len(new),
        scratch_shapes=scratch,
        compiler_params=pltpu.CompilerParams(vmem_limit_bytes=32 * 1024 * 1024),
    )(*flat, result, grad)


def local(
    sub,
    tokens,
    cotangent,
    span_mask,
    attention_weight,
    expand_weight,
    reduce_weight,
    vectors,
    attention_first,
    attention_second,
    expand_first,
    expand_second,
    reduce_first,
    reduce_second,
    vector_first,
    vector_second,
):
    together = [[n * sub + m for m in range(sub)] for n in range(GROUPS)]

    def widen(value, axis):
        if sub == 1:
            return value
        low = lax.all_gather(
            value.astype(BF16), "batch", axis=axis, tiled=True, axis_index_groups=together
        )
        return low.astype(F32)

    def narrow(value, axis):
        if sub == 1:
            return value
        return lax.psum_scatter(
            value, "batch", scatter_dimension=axis, tiled=True, axis_index_groups=together
        )

    out_tokens, input_grad, ga, g1, g2, gv = layer(
        sub,
        tokens,
        cotangent,
        span_mask,
        widen(vectors, 1),
        widen(attention_weight, 2),
        widen(expand_weight, 1),
        widen(reduce_weight.T, 0),
    )
    arrays = (
        (attention_weight, attention_first, attention_second, narrow(ga, 2)),
        (expand_weight, expand_first, expand_second, narrow(g1, 1)),
        (reduce_weight.T, reduce_first.T, reduce_second.T, narrow(g2, 0)),
        (vectors, vector_first, vector_second, narrow(gv, 1)),
    )
    rates = (rate_attention, rate_expand, rate_reduce, rate_vector)
    new = update(rates, arrays, out_tokens, input_grad)
    return new[-2:] + new[0:6] + tuple(value.T for value in new[6:9]) + new[9:12]


def solution(mesh):
    sub = mesh.shape["batch"] // GROUPS
    sequences = P("batch", "blk", None)
    attention = P(None, "blk", "batch")
    matrix = P("blk", "batch")
    return jax.shard_map(
        functools.partial(local, sub),
        mesh=mesh,
        in_specs=(sequences, sequences, P("batch", "blk"), attention, matrix, matrix, matrix)
        + (attention,) * 2
        + (matrix,) * 6,
        out_specs=(sequences,) * 2 + (attention,) * 3 + (matrix,) * 9,
        check_vma=False,
    )
```

```python
import functools
import math

import jax
import jax.numpy as jnp
from jax import lax
from jax.experimental import pallas as pl
from jax.experimental.pallas import tpu as pltpu
from jax.sharding import PartitionSpec as P

HEADS = 12
HEAD = 64
STEP = 10
GROUPS = 8

norm_epsilon = 1e-05
beta_one = 0.9
beta_two = 0.999
adam_epsilon = 1e-08
decay_weight = 0.1
rate_attention = 0.05
rate_expand = 0.03
rate_reduce = 0.015
rate_vector = 0.4

F32 = jnp.float32
BF16 = jnp.bfloat16
MESH = pl.DeviceIdType.MESH
GELU_SCALE = math.sqrt(2.0 / math.pi)
GELU_CUBE = 0.044715


def adamw(weight, moment_one, moment_two, gradient, step_rate):
    moment_one = beta_one * moment_one + (1.0 - beta_one) * gradient
    moment_two = beta_two * moment_two + (1.0 - beta_two) * gradient * gradient
    corrected_one = moment_one / (1.0 - beta_one**STEP)
    corrected_two = moment_two / (1.0 - beta_two**STEP)
    updated = weight - step_rate * (
        corrected_one / (jnp.sqrt(corrected_two) + adam_epsilon) + decay_weight * weight
    )
    return (updated, moment_one, moment_two)


def dot_nn(left, right):
    return lax.dot_general(left, right, (((1,), (0,)), ((), ())), preferred_element_type=F32)


def dot_nt(left, right):
    return lax.dot_general(left, right, (((1,), (1,)), ((), ())), preferred_element_type=F32)


def lane_tiles(ref, count=6):
    return jnp.concatenate([ref[t] for t in range(count)], axis=1)


class Unit:
    def __init__(self, order, u, long_axis, fine):
        self.order, self.u, self.long_axis, self.fine = order, u, long_axis, fine


class Gradient:
    def __init__(self, order, u, long_axis, first, count, whole, core_in, long_in, mid_in, line_in, finish):
        self.order, self.long_axis, self.first, self.count, self.whole = order, long_axis, first, count, whole
        self.u, self.core_in, self.long_in, self.mid_in, self.line_in = u, core_in, long_in, mid_in, line_in
        self.finish = finish


def kernel(sub, zs, *refs):
    (tok, cot, mask_in, vec_in, a_in, w1_in, w2_in,
     out, ig, ga, g1, g2, gv,
     ubuf, core_in, long_in, mid_in, line_in,
     x_in, cot_in, stage, vec, gvec, vin, gin, narrow_rows,
     at, n1, q6, k6, v6, o6, pt, h1, acc, n2, act, gp, ta, tb, tc, d6,
     local_sem, ag_send, ag_recv, rs_send, rs_recv, a2a_send, a2a_recv, v_send, v_recv) = refs

    i = lax.axis_index("blk")
    b = lax.axis_index("batch")
    c, y = lax.rem(i, 2), lax.div(i, 2)
    g, r = lax.div(b, sub), lax.rem(b, sub)
    x, z = lax.rem(g, 2), lax.div(g, 2)

    def device(c_=c, y_=y, x_=x, z_=z):
        return {"blk": 2 * y_ + c_, "batch": (2 * z_ + x_) * sub + r}

    def z_at(k):
        return lax.rem(z + k, zs)

    def block_at(k):
        return lax.rem(i + k, 4)

    def copy(src, dst, send, recv, to):
        return pltpu.make_async_remote_copy(
            src_ref=src, dst_ref=dst, send_sem=send, recv_sem=recv, device_id=to, device_id_type=MESH
        )

    def loop(count, body, hooks=()):
        def step(s, carry):
            body(s)
            for k, *todo in hooks:

                @pl.when(s == k)
                def _():
                    for f in todo:
                        f()

            return carry

        lax.fori_loop(0, count, step, 0)

    partners = [device(z_=z_at(k)) for k in range(1, zs)]
    partners += [device(x_=1 - x), device(y_=1 - y), device(c_=1 - c), device(c_=1 - c, y_=1 - y)]
    barrier = pltpu.get_barrier_semaphore()
    for partner in partners:
        pl.semaphore_signal(barrier, inc=1, device_id=partner, device_id_type=MESH)
    pl.semaphore_wait(barrier, len(partners))

    def ag_sems(n, slot):
        return ag_send.at[n.order, slot], ag_recv.at[n.order, slot]

    def group(n, u, long_off, mid_off, cut=None):
        yy = y if (long_off if n.long_axis == "y" else mid_off) == 0 else 1 - y
        xx = x if (long_off if n.long_axis == "x" else mid_off) == 0 else 1 - x
        return u.at[c, yy, xx] if cut is None else u.at[c, yy, xx, cut]

    def partner_of(n, step):
        axis = n.long_axis if step == "long" else {"x": "y", "y": "x"}[n.long_axis]
        return device(x_=1 - x) if axis == "x" else device(y_=1 - y)

    LINE, MID, LONG, LAST, CORE = 0, zs - 1, 2 * zs - 1, 3 * zs - 1, 3 * zs

    def ag_line(n, k, landed=False):
        ref = group(n, n.u, 0, 0, z_at(zs - k) if landed else z)
        return copy(ref, ref, *ag_sems(n, LINE + k - 1), device(z_=z_at(k)))

    def ag_first(n, step, k, landed=False):
        cut = z_at(zs - k) if n.fine else None
        off = (0, 1) if step == "mid" else (1, 0)
        ref = group(n, n.u, *(off if landed else (0, 0)), cut)
        return copy(ref, ref, *ag_sems(n, (MID if step == "mid" else LONG) + k), partner_of(n, step))

    def ag_last(n, landed=False):
        ref = group(n, n.u, 1 if landed else 0, 1)
        return copy(ref, ref, *ag_sems(n, LAST), partner_of(n, "long"))

    def ag_core(n, long_off, mid_off, landed=False):
        ref = group(n, n.u, long_off, mid_off)
        if landed:
            yy = y if (long_off if n.long_axis == "y" else mid_off) == 0 else 1 - y
            xx = x if (long_off if n.long_axis == "x" else mid_off) == 0 else 1 - x
            ref = n.u.at[1 - c, yy, xx]
        return copy(ref, ref, *ag_sems(n, CORE + 2 * long_off + mid_off), device(c_=1 - c))

    def parts(n):
        return range(zs) if n.fine else range(1)

    def ag_start(n):
        if n.fine:
            for step in ("mid", "long"):
                ag_first(n, step, 0).start()
        for k in range(1, zs):
            ag_line(n, k).start()

    def ag_piece(n, k):
        ag_line(n, k, True).wait_recv()
        for step in ("mid", "long"):
            ag_first(n, step, k).start()

    def ag_one(n):
        if not n.fine:
            for k in range(1, zs):
                ag_line(n, k, True).wait_recv()
            for step in ("mid", "long"):
                ag_first(n, step, 0).start()
        ag_core(n, 0, 0).start()

    def ag_two(n):
        for k in parts(n):
            ag_first(n, "mid", k, True).wait_recv()
        ag_last(n).start()
        ag_core(n, 0, 1).start()

    def ag_three(n):
        for k in parts(n):
            ag_first(n, "long", k, True).wait_recv()
        ag_core(n, 1, 0).start()

    def ag_four(n):
        ag_last(n, True).wait_recv()
        ag_core(n, 1, 1).start()

    def ag_done(n):
        for off in ((0, 0), (0, 1), (1, 0), (1, 1)):
            ag_core(n, *off, True).wait_recv()
        for k in range(1, zs):
            ag_line(n, k).wait_send()
        for step in ("mid", "long"):
            for k in parts(n):
                ag_first(n, step, k).wait_send()
        ag_last(n).wait_send()
        for off in ((0, 0), (0, 1), (1, 0), (1, 1)):
            ag_core(n, *off).wait_send()

    def rs_sems(n, slot):
        return rs_send.at[n.order, slot], rs_recv.at[n.order, slot]

    def cut_of(n):
        return slice(None) if n.count == zs else pl.ds(n.first, n.count)

    def rs_core(n, long_off):
        place = 1 - (y if n.long_axis == "y" else x) if long_off else (y if n.long_axis == "y" else x)
        where = (place, slice(None)) if n.long_axis == "y" else (slice(None), place)
        return copy(n.u.at[(1 - c,) + where + (cut_of(n),)], n.core_in.at[where],
                    *rs_sems(n, long_off), device(c_=1 - c))

    def rs_long(n):
        where = (1 - y, slice(None)) if n.long_axis == "y" else (slice(None), 1 - x)
        return copy(n.u.at[(c,) + where + (cut_of(n),)], n.long_in, *rs_sems(n, 2), partner_of(n, "long"))

    def rs_mid(n):
        return copy(group(n, n.u, 0, 1, cut_of(n)), n.mid_in, *rs_sems(n, 3), partner_of(n, "mid"))

    def rs_line(n, k):
        return copy(group(n, n.u, 0, 0, z_at(k)), n.line_in.at[k - 1], *rs_sems(n, 3 + k), device(z_=z_at(k)))

    def within(n, place):
        return jnp.logical_and(place >= n.first, place < n.first + n.count)

    def when_within(n, place, f):
        if n.whole:
            f()
        else:
            pl.when(within(n, place))(f)

    def gather_terms(n, long_off, mid_off, names):
        yy = y if (long_off if n.long_axis == "y" else mid_off) == 0 else 1 - y
        xx = x if (long_off if n.long_axis == "x" else mid_off) == 0 else 1 - x

        def body(s):
            mine = n.u.at[c, yy, xx, n.first + s]
            value = mine[...].astype(F32) + n.core_in[yy, xx, s].astype(F32)
            if "long" in names:
                value = value + n.long_in[xx if n.long_axis == "y" else yy, s].astype(F32)
            if "mid" in names:
                value = value + n.mid_in[s].astype(F32)
            mine[...] = value.astype(BF16)

        loop(n.count, body)

    def rs_zero(n):
        rs_core(n, 1).start()
        rs_core(n, 0).start()

    def rs_one(n):
        rs_core(n, 1).wait_recv()
        gather_terms(n, 1, 0, ())
        gather_terms(n, 1, 1, ())
        rs_long(n).start()

    def rs_two(n):
        rs_core(n, 0).wait_recv()
        rs_long(n).wait_recv()
        gather_terms(n, 0, 1, ("long",))
        rs_mid(n).start()

    def rs_three(n):
        rs_mid(n).wait_recv()
        gather_terms(n, 0, 0, ("long", "mid"))
        for k in range(1, zs):
            when_within(n, z_at(k), lambda k=k: rs_line(n, k).start())

    def rs_done(n):
        def finish():
            for k in range(1, zs):
                rs_line(n, k).wait_recv()
            value = n.u[c, y, x, z].astype(F32)
            for k in range(1, zs):
                value = value + n.line_in[k - 1].astype(F32)
            n.finish(value)

        when_within(n, z, finish)
        for moved in (rs_core(n, 0), rs_core(n, 1), rs_long(n), rs_mid(n)):
            moved.wait_send()
        for k in range(1, zs):
            when_within(n, z_at(k), lambda k=k: rs_line(n, k).wait_send())

    def small_sum(ref, slots, which):
        to = (device(y_=1 - y), device(c_=1 - c), device(x_=1 - x))
        to += tuple(device(z_=z_at(k)) for k in range(1, zs))

        def moved(slot):
            return copy(ref, slots.at[slot], v_send.at[which, slot], v_recv.at[which, slot], to[slot])

        def land(last):
            moved(last).wait()
            ref[...] = ref[...] + slots[last]

        def step(n):
            def run():
                if n > 0:
                    land(n - 1)
                moved(n).start()

            return run

        def line():
            land(2)
            for k in range(1, zs):
                moved(2 + k).start()

        def finish():
            for k in range(1, zs):
                moved(2 + k).wait()
            value = ref[...]
            for k in range(1, zs):
                value = value + slots[2 + k]
            ref[...] = value

        return [step(0), step(1), step(2), line, finish]

    def exchange(src, dst, which):
        return [copy(src.at[block_at(k)], dst.at[i], a2a_send.at[which, k - 1],
                     a2a_recv.at[which, k - 1], {"blk": block_at(k), "batch": b})
                for k in range(1, 4)]

    def exchange_landed(dst, which):
        return [copy(dst.at[block_at(4 - k)], dst.at[block_at(4 - k)], a2a_send.at[which, k - 1],
                     a2a_recv.at[which, k - 1], {"blk": block_at(4 - k), "batch": b})
                for k in range(1, 4)]

    units = [Unit(2 * n + half, ubuf.at[n, half], axes[half], n == 0)
             for n, axes in enumerate(("xy", "xy", "xx")) for half in range(2)]
    unit_qk, unit_vo, unit_w1, unit_w2 = units[0], units[1], units[2:4], units[4:6]

    def rest_rows(matrix):
        return a_in[matrix, pl.ds(pl.multiple_of(128 * (1 - c), 64), 64), :]

    def own_attention(p):
        mine = ubuf.at[0, p, c, y, x, z]
        for m in range(2):
            main = a_in[2 * p + m, pl.ds(pl.multiple_of(64 * c, 64), 128), :]
            mine[96 * m : 96 * m + 96, :] = main.T.astype(BF16)
        rest = jnp.concatenate([rest_rows(2 * p + c), rest_rows(2 * p + 1 - c)], axis=0)
        mine[192:288, :] = rest.T.astype(BF16)

    def own_feed_forward():
        for h in range(2):
            for t in range(3):
                ubuf[1, h, c, y, x, z, 96 * t : 96 * t + 96, :] = w1_in[
                    96 * h : 96 * h + 96, 128 * t : 128 * t + 128
                ].astype(BF16)
            for t in range(6):
                ubuf[2, h, c, y, x, z, 48 * t : 48 * t + 48, :] = w2_in[
                    48 * h : 48 * h + 48, 128 * t : 128 * t + 128
                ].astype(BF16)

    columns = a_in.shape[2]
    placed = lax.broadcasted_iota(jnp.int32, (columns, 768), 1) == (
        lax.broadcasted_iota(jnp.int32, (columns, 768), 0) + columns * g
    )

    def own_vectors():
        vec[...] = jnp.zeros_like(vec)
        rows = dot_nn(vec_in[...].astype(BF16), jnp.where(placed, 1.0, 0.0).astype(BF16))
        for j in range(3):
            vec[pl.ds(3 * i + j, 1), :] = rows[j : j + 1, :]

    def masked_cotangent():
        eye = lax.broadcasted_iota(jnp.int32, (128, 128), 0) == lax.broadcasted_iota(jnp.int32, (128, 128), 1)
        for s in range(4):
            row = jnp.broadcast_to(mask_in[s : s + 1, :].astype(F32), (128, 128))
            column = jnp.sum(jnp.where(eye, row, 0.0), axis=1, keepdims=True)
            stage[s] = (cot[s].astype(F32) * column).astype(BF16)

    def finish_attention(p):
        def finish(value):
            for m in range(2):
                ga[2 * p + m, pl.ds(pl.multiple_of(64 * c, 64), 128), :] = value[96 * m : 96 * m + 96, :].T
            rest = value[192:288, :].T
            rows = pl.ds(pl.multiple_of(128 * (1 - c), 64), 64)
            ga[2 * p + c, rows, :] = rest[0:64, :]
            ga[2 * p + 1 - c, rows, :] = rest[64:128, :]

        return finish

    def finish_expand(h):
        def finish(value):
            for t in range(3):
                g1[96 * h : 96 * h + 96, 128 * t : 128 * t + 128] = value[96 * t : 96 * t + 96, :]

        return finish

    def finish_reduce(h):
        def finish(value):
            for t in range(6):
                g2[48 * h : 48 * h + 48, 128 * t : 128 * t + 128] = value[48 * t : 48 * t + 48, :]

        return finish

    def finish_vectors():
        value, total = gvec[...], 0.0
        for _ in range(3):
            part = value.astype(BF16)
            total = total + dot_nt(part, jnp.where(placed, 1.0, 0.0).astype(BF16))
            value = value - part.astype(F32)
        narrow_rows[...] = total
        for j in range(3):
            gv[j : j + 1, :] = narrow_rows[pl.ds(3 * i + j, 1), :]

    grads = []
    half_zs = zs // 2
    for n, (source, finish, axes) in enumerate(((0, finish_reduce, "xx"), (2, finish_expand, "yx"))):
        for half in range(2):
            order = 2 * n + half
            grads.append(Gradient(order, ubuf.at[source, half], axes[half], 0, zs, True,
                                  core_in.at[order], long_in.at[order], mid_in.at[order],
                                  line_in.at[order], finish(half)))
    for part in range(2):
        for half in range(2):
            cut = pl.ds(part * half_zs, half_zs)
            grads.append(Gradient(4 + 2 * part + half, ubuf.at[1, half], "xy"[half], part * half_zs, half_zs,
                                  False, core_in.at[4 + half, :, :, cut], long_in.at[4 + half, :, cut],
                                  mid_in.at[4 + half, cut], line_in.at[4 + half], finish_attention(half)))
    grad_w2, grad_w1, grad_a = grads[0:2], grads[2:4], (grads[4:6], grads[6:8])

    def each(f, which):
        def run():
            for n in which:
                f(n)

        return run

    own_attention(0)
    ag_start(unit_qk)
    own_vectors()
    vec_steps = small_sum(vec, vin, 0)
    vec_steps[0]()
    own_tokens = pltpu.make_async_copy(tok.at[i], x_in.at[i], local_sem.at[0])
    own_tokens.start()
    tokens_out = exchange(tok, x_in, 0)
    for moved in tokens_out:
        moved.start()
    own_attention(1)
    own_feed_forward()
    for k in range(1, zs):
        ag_piece(unit_qk, k)
    ag_one(unit_qk)
    ag_start(unit_vo)
    ag_start(unit_w1[0])
    vec_steps[1]()
    masked_cotangent()
    ag_two(unit_qk)
    vec_steps[2]()
    for k in range(1, zs):
        ag_piece(unit_vo, k)
    ag_one(unit_vo)
    ag_start(unit_w1[1])
    vec_steps[3]()
    ag_three(unit_qk)

    for moved in exchange_landed(x_in, 0):
        moved.wait_recv()
    own_tokens.wait()
    vec_steps[4]()

    def normalise(value):
        centered = value - jnp.mean(value, axis=-1, keepdims=True)
        scale = lax.rsqrt(jnp.mean(centered * centered, axis=-1, keepdims=True) + norm_epsilon)
        return centered * scale, scale

    def rows_of(s):
        return pl.ds(pl.multiple_of(s * 128, 128), 128)

    def first_norm(s):
        unit, _ = normalise(x_in[s].astype(F32))
        n1[rows_of(s), :] = (unit * vec[0:1, :] + vec[1:2, :]).astype(BF16)

    loop(4, first_norm)
    ag_four(unit_qk)
    own_cot = pltpu.make_async_copy(stage.at[i], cot_in.at[i], local_sem.at[1])
    own_cot.start()
    cot_out = exchange(stage, cot_in, 1)
    for moved in cot_out:
        moved.start()
    ag_done(unit_qk)

    lanes = lax.broadcasted_iota(jnp.int32, (96, 128), 1)

    def unpack(p, s):
        for xx in range(2):
            rows = pl.ds(pl.multiple_of((2 * s + xx) * 96, 96), 96)
            for yy in range(2):
                first, second = ubuf.at[0, p, 0, yy, xx, s], ubuf.at[0, p, 1, yy, xx, s]
                lo, hi = 384 * yy, 384 * yy + 256
                for m in range(2):
                    at[2 * p + m, rows, lo : lo + 128] = first[96 * m : 96 * m + 96, :]
                    at[2 * p + m, rows, hi : hi + 128] = second[96 * m : 96 * m + 96, :]
                rest_first = first[192:288, :].astype(F32)
                rest_second = second[192:288, :].astype(F32)
                even = jnp.where(lanes < 64, rest_first, rest_second)
                odd = pltpu.roll(jnp.where(lanes < 64, rest_second, rest_first), 64, 1)
                at[2 * p, rows, lo + 128 : lo + 256] = even.astype(BF16)
                at[2 * p + 1, rows, lo + 128 : lo + 256] = odd.astype(BF16)

    def project(m, dst, bias):
        for n in range(3):
            value = dot_nt(n1[...], at[m, 256 * n : 256 * n + 256, :])
            if bias is not None:
                value = value + vec[bias : bias + 1, 256 * n : 256 * n + 256]
            value = value.astype(BF16)
            if m == 0:
                value = value * jnp.asarray(HEAD ** (-0.5), BF16)
            dst[2 * n] = value[:, 0:128]
            dst[2 * n + 1] = value[:, 128:256]

    loop(zs, functools.partial(unpack, 0))
    project(0, q6, 2)
    ag_two(unit_vo)
    project(1, k6, None)
    ag_one(unit_w1[0])

    half_lane = lax.broadcasted_iota(jnp.int32, (1, 128), 1) // HEAD
    half_rows = [jnp.where(half_lane == which, 1.0, 0.0).astype(BF16) for which in range(2)]

    def half_of(value, which):
        return value * half_rows[which]

    def attend(p):
        queries, keys = q6[p], k6[p]
        for which in range(2):
            scores = dot_nt(half_of(keys, which), queries)
            expo = jnp.exp(scores - jnp.max(scores, axis=0, keepdims=True))
            probs = (expo * (1.0 / jnp.sum(expo, axis=0, keepdims=True))).astype(BF16)
            pt[2 * p + which] = probs

    def mix(p):
        values_t = v6[p].T
        mixed = [dot_nn(values_t[64 * which : 64 * which + 64, :], pt[2 * p + which]) for which in range(2)]
        o6[p] = jnp.concatenate(mixed, axis=0).T.astype(BF16)

    loop(6, attend, (
        (1, lambda: ag_three(unit_vo)),
        (2, lambda: ag_one(unit_w1[1]), each(ag_start, unit_w2)),
        (3, lambda: ag_four(unit_vo), lambda: ag_two(unit_w1[0])),
    ))
    ag_two(unit_w1[1])
    ag_done(unit_vo)
    loop(zs, functools.partial(unpack, 1))
    project(2, v6, 3)
    each(ag_three, unit_w1)()
    loop(6, mix, (
        (1, lambda: ag_one(unit_w2[0])),
        (3, each(ag_four, unit_w1), lambda: ag_one(unit_w2[1])),
        (5, lambda: ag_two(unit_w2[0])),
    ))

    for n in range(3):
        cols = slice(256 * n, 256 * n + 256)
        value = dot_nt(lane_tiles(o6), at[3, cols, :]) + vec[4:5, cols]
        for s in range(4):
            h1[128 * s : 128 * s + 128, cols] = x_in[s, :, cols].astype(F32) + value[128 * s : 128 * s + 128]

    def second_norm(s):
        unit, _ = normalise(h1[rows_of(s), :])
        n2[rows_of(s), :] = (unit * vec[5:6, :] + vec[6:7, :]).astype(BF16)

    loop(4, second_norm)
    each(ag_done, unit_w1)()
    ag_two(unit_w2[1])

    def expand_piece(s, xx):
        def piece(ref):
            return jnp.concatenate([ref[96 * t : 96 * t + 96, :] for t in range(3)], axis=1)

        return jnp.concatenate(
            [piece(ubuf.at[1, h, cc, yy, xx, s]) for yy in range(2) for cc in range(2) for h in range(2)],
            axis=0,
        )

    def reduce_block(s):
        yy, cc = lax.div(s, 2), lax.rem(s, 2)

        def piece(ref):
            return jnp.concatenate([ref[48 * t : 48 * t + 48, :] for t in range(6)], axis=1)

        return jnp.concatenate(
            [piece(ubuf.at[2, h, cc, yy, xx, zz]) for zz in range(zs) for xx in range(2) for h in range(2)],
            axis=0,
        )

    def block_rows(s):
        return pl.ds(pl.multiple_of(s * 512, 512), 512)

    def expand(s):
        for xx in range(2):
            cols = slice(384 * xx, 384 * xx + 384)
            inner = dot_nn(n2[...], expand_piece(s, xx)) + vec[pl.ds(8 + s, 1), cols]
            square = inner * inner
            tanh = jnp.tanh(GELU_SCALE * inner * (1.0 + GELU_CUBE * square))
            act[block_rows(s), cols] = (0.5 * inner * (1.0 + tanh)).astype(BF16)
            slope = 0.5 * (1.0 + tanh) + 0.5 * inner * (1.0 - tanh * tanh) * (
                GELU_SCALE * (1.0 + 3.0 * GELU_CUBE * square)
            )
            gp[block_rows(s), cols] = slope.astype(BF16)

    loop(4, expand, (
        (1, each(ag_three, unit_w2)),
        (3, lambda: ag_four(unit_w2[0])),
    ))

    for moved in exchange_landed(cot_in, 1):
        moved.wait_recv()
    own_cot.wait()
    gvec[...] = jnp.zeros_like(gvec)

    def transpose_rows(dst, s, value):
        dst[:, 128 * s : 128 * s + 128] = value.T

    total = jnp.zeros((1, 768), F32)
    for s in range(4):
        transpose_rows(ta, s, cot_in[s])
        total = total + jnp.sum(cot_in[s].astype(F32), axis=0, keepdims=True)
    gvec[7:8, :] = total

    def reduce_back(s):
        yy, cc = lax.div(s, 2), lax.rem(s, 2)
        grad = dot_nn(ta[...], act[block_rows(s), :]).astype(BF16)
        for zz in range(zs):
            for xx in range(2):
                for h in range(2):
                    row = 96 * (2 * zz + xx) + 48 * h
                    for t in range(6):
                        ubuf[0, h, cc, yy, xx, zz, 48 * t : 48 * t + 48, :] = grad[
                            row : row + 48, 128 * t : 128 * t + 128
                        ]

    loop(4, reduce_back)
    each(rs_zero, grad_w2)()
    ag_four(unit_w2[1])
    each(rs_one, grad_w2)()
    each(ag_done, unit_w2)()

    def cotangent_rows():
        return jnp.concatenate([cot_in[s] for s in range(4)], axis=0)

    def inner_back(s):
        grad = dot_nn(cotangent_rows(), reduce_block(s)) * gp[block_rows(s), :].astype(F32)
        low = grad.astype(BF16)
        gp[block_rows(s), :] = low
        gvec[pl.ds(8 + s, 1), :] = jnp.sum(low.astype(F32), axis=0, keepdims=True)

    loop(4, inner_back)

    acc[...] = h1[...] + vec[7:8, :]

    def reduce(s):
        acc[...] += dot_nt(act[block_rows(s), :], reduce_block(s))

    loop(4, reduce)
    for moved in cot_out:
        moved.wait_send()
    for s in range(4):
        stage[s] = acc[128 * s : 128 * s + 128, :].astype(BF16)
    own_out = pltpu.make_async_copy(stage.at[i], out.at[i], local_sem.at[2])
    own_out.start()
    result_out = exchange(stage, out, 2)
    for moved in result_out:
        moved.start()

    for s in range(4):
        transpose_rows(tb, s, n2[128 * s : 128 * s + 128, :])

    def expand_back(s):
        for xx in range(2):
            grad = dot_nn(tb[...], gp[block_rows(s), 384 * xx : 384 * xx + 384]).astype(BF16)
            for yy in range(2):
                for cc in range(2):
                    for h in range(2):
                        row = 192 * (2 * yy + cc) + 96 * h
                        for t in range(3):
                            ubuf[2, h, cc, yy, xx, s, 96 * t : 96 * t + 96, :] = grad[
                                row : row + 96, 128 * t : 128 * t + 128
                            ]

    loop(4, expand_back)
    each(rs_zero, grad_w1)()
    each(rs_two, grad_w2)()

    def norm_back(s):
        whole = jnp.concatenate([expand_piece(s, 0), expand_piece(s, 1)], axis=1)
        part = dot_nt(gp[block_rows(s), :], whole)

        @pl.when(s == 0)
        def _():
            acc[...] = part

        @pl.when(s > 0)
        def _():
            acc[...] += part

    loop(4, norm_back, ((1, each(rs_one, grad_w1)),))

    def norm_gradient(value, scale_row, grad):
        unit, scale = normalise(value)
        gain_sum = jnp.sum(grad * unit, axis=0, keepdims=True)
        bias_sum = jnp.sum(grad, axis=0, keepdims=True)
        inner = grad * scale_row
        mean = jnp.mean(inner, axis=-1, keepdims=True)
        along = jnp.mean(inner * unit, axis=-1, keepdims=True)
        return scale * (inner - mean - unit * along), gain_sum, bias_sum

    def hidden_back(s):
        rows = rows_of(s)
        grad, gain_sum, bias_sum = norm_gradient(h1[rows, :], vec[5:6, :], acc[rows, :])
        grad = grad + cot_in[s].astype(F32)
        h1[rows, :] = grad
        low = grad.astype(BF16)
        n2[rows, :] = low
        gvec[5:6, :] += gain_sum
        gvec[6:7, :] += bias_sum
        gvec[4:5, :] += jnp.sum(low.astype(F32), axis=0, keepdims=True)

    loop(4, hidden_back)

    for n in range(3):
        value = dot_nn(n2[...], at[3, :, 256 * n : 256 * n + 256]).astype(BF16)
        d6[2 * n] = value[:, 0:128]
        d6[2 * n + 1] = value[:, 128:256]
    for s in range(4):
        transpose_rows(tc, s, n2[128 * s : 128 * s + 128, :])
    act[768:1536, :] = dot_nn(tc[...], lane_tiles(o6)).astype(BF16)
    each(rs_three, grad_w2)()

    def attend_back(p):
        rows = rows_of(p)
        queries, keys, values, grads_in = q6[p], k6[p], v6[p], d6[p]
        keys_t = keys.T
        grad_query, grad_key, grad_value = [], 0.0, 0.0
        for which in range(2):
            probs = pt[2 * p + which]
            wide = probs.astype(F32)
            grad_probs = dot_nt(half_of(values, which), grads_in)
            inner = jnp.sum(wide * grad_probs, axis=0, keepdims=True)
            grad_scores = (wide * (grad_probs - inner)).astype(BF16)
            grad_query.append(dot_nn(keys_t[64 * which : 64 * which + 64, :], grad_scores))
            grad_key = grad_key + dot_nn(grad_scores, half_of(queries, which))
            grad_value = grad_value + dot_nn(probs, half_of(grads_in, which))
        grad_query = jnp.concatenate(grad_query, axis=0) * HEAD ** (-0.5)
        grad_query = grad_query.astype(BF16)
        grad_key, grad_value = grad_key.astype(BF16), grad_value.astype(BF16)
        ta[rows, :] = grad_query
        tb[rows, :] = grad_key.T
        tc[rows, :] = grad_value.T
        q6[p] = grad_query.T
        k6[p] = grad_key
        v6[p] = grad_value

    def pack(p, part, first_row, second_row):
        def body(s):
            for xx in range(2):
                offset = (2 * s + xx) * 96
                rows = [pl.ds(pl.multiple_of(first_row + offset, 96), 96),
                        pl.ds(pl.multiple_of(second_row + offset, 96), 96)]
                first = ubuf.at[1, p, 0, :, xx, part * half_zs + s]
                second = ubuf.at[1, p, 1, :, xx, part * half_zs + s]
                for yy in range(2):
                    lo, mid, hi = 384 * yy, 384 * yy + 128, 384 * yy + 256
                    for m in range(2):
                        first[yy, 96 * m : 96 * m + 96, :] = act[rows[m], lo : lo + 128]
                        second[yy, 96 * m : 96 * m + 96, :] = act[rows[m], hi : hi + 128]
                    even = act[rows[0], mid : mid + 128].astype(F32)
                    odd = pltpu.roll(act[rows[1], mid : mid + 128].astype(F32), 64, 1)
                    first[yy, 192:288, :] = jnp.where(lanes < 64, even, odd).astype(BF16)
                    second[yy, 192:288, :] = jnp.where(lanes < 64, odd, even).astype(BF16)

        loop(half_zs, body)

    def attention_gradients(part):
        rows = slice(384 * part, 384 * part + 384)
        act[1536:1920, :] = dot_nn(tc[rows, :], n1[...]).astype(BF16)
        pack(1, part, 1536, 768 + 384 * part)
        rs_zero(grad_a[part][1])
        act[0:384, :] = dot_nn(ta[rows, :], n1[...]).astype(BF16)
        act[384:768, :] = dot_nn(tb[rows, :], n1[...]).astype(BF16)
        pack(0, part, 0, 384)
        rs_zero(grad_a[part][0])

    loop(3, attend_back, ((0, each(rs_two, grad_w1)), (1, each(rs_done, grad_w2))))
    attention_gradients(0)
    loop(3, lambda p: attend_back(p + 3), (
        (0, each(rs_one, grad_a[0])),
        (1, each(rs_three, grad_w1)),
        (2, each(rs_two, grad_a[0])),
    ))
    attention_gradients(1)
    each(rs_one, grad_a[1])()
    each(rs_done, grad_w1)()

    acc[...] = dot_nn(lane_tiles(q6), at[0])
    acc[...] += dot_nn(lane_tiles(k6), at[1])
    acc[...] += dot_nn(lane_tiles(v6), at[2])
    gvec[2:3, :] = jnp.sum(lane_tiles(q6).astype(F32), axis=0, keepdims=True)
    gvec[3:4, :] = jnp.sum(lane_tiles(v6).astype(F32), axis=0, keepdims=True)
    each(rs_three, grad_a[0])()

    for moved in result_out:
        moved.wait_send()
    own_out.wait()

    def input_back(s):
        rows = rows_of(s)
        grad, gain_sum, bias_sum = norm_gradient(x_in[s].astype(F32), vec[0:1, :], acc[rows, :])
        stage[s] = (grad + h1[rows, :]).astype(BF16)
        gvec[0:1, :] += gain_sum
        gvec[1:2, :] += bias_sum

    loop(4, input_back)
    gvec_steps = small_sum(gvec, gin, 1)
    gvec_steps[0]()
    own_grad = pltpu.make_async_copy(stage.at[i], ig.at[i], local_sem.at[3])
    own_grad.start()
    grad_out = exchange(stage, ig, 3)
    for moved in grad_out:
        moved.start()

    gvec_steps[1]()
    each(rs_two, grad_a[1])()
    gvec_steps[2]()
    each(rs_done, grad_a[0])()
    gvec_steps[3]()
    each(rs_three, grad_a[1])()
    gvec_steps[4]()
    finish_vectors()
    each(rs_done, grad_a[1])()

    own_grad.wait()
    for moved in tokens_out + grad_out:
        moved.wait_send()
    for moved in exchange_landed(out, 2) + exchange_landed(ig, 3):
        moved.wait_recv()


def layer(sub, tokens, cotangent, span_mask, vectors, attention, expand, reduce_t):
    zs = GROUPS // 2
    seqs, block, width = tokens.shape
    rows = seqs * block
    columns = attention.shape[2]
    piece = (3 * columns, 128)
    vmem = lambda shape, dtype: pltpu.VMEM(shape, dtype)
    scratch = [vmem((3, 2, 2, 2, 2, zs) + piece, BF16)]
    scratch += [vmem((6, 2, 2, zs) + piece, BF16), vmem((6, 2, zs) + piece, BF16)]
    scratch += [vmem((6, zs) + piece, BF16), vmem((6, zs - 1) + piece, BF16)]
    scratch += [vmem(tokens.shape, BF16)] * 3
    scratch += [vmem((16, width), F32)] * 2
    scratch += [vmem((zs + 2, 16, width), F32)] * 2
    scratch += [vmem((16, columns), F32)]
    tiles = vmem((width // 128, rows, 128), BF16)
    flat = vmem((rows, width), BF16)
    turned = vmem((width, rows), BF16)
    scratch += [vmem((4, width, width), BF16), flat, tiles, tiles, tiles, tiles]
    scratch += [vmem((HEADS, rows, rows), BF16), vmem((rows, width), F32), vmem((rows, width), F32)]
    scratch += [flat, vmem((4 * rows, width), BF16), vmem((4 * rows, width), BF16)]
    scratch += [turned, turned, turned, tiles]
    scratch += [pltpu.SemaphoreType.DMA((4,))]
    scratch += [pltpu.SemaphoreType.DMA((6, 3 * zs + 4))] * 2
    scratch += [pltpu.SemaphoreType.DMA((8, zs + 3))] * 2
    scratch += [pltpu.SemaphoreType.DMA((4, 3))] * 2
    scratch += [pltpu.SemaphoreType.DMA((2, zs + 2))] * 2
    in_vmem = pl.BlockSpec(memory_space=pltpu.VMEM)
    anywhere = pl.BlockSpec(memory_space=pl.ANY)
    return pl.pallas_call(
        functools.partial(kernel, sub, zs),
        out_shape=(
            jax.ShapeDtypeStruct(tokens.shape, BF16),
            jax.ShapeDtypeStruct(tokens.shape, BF16),
            jax.ShapeDtypeStruct(attention.shape, F32),
            jax.ShapeDtypeStruct(expand.shape, F32),
            jax.ShapeDtypeStruct(reduce_t.shape, F32),
            jax.ShapeDtypeStruct(vectors.shape, F32),
        ),
        in_specs=[anywhere] + [in_vmem] * 6,
        out_specs=(anywhere, anywhere) + (in_vmem,) * 4,
        scratch_shapes=scratch,
        compiler_params=pltpu.CompilerParams(
            collective_id=0, has_side_effects=True, vmem_limit_bytes=63 * 1024 * 1024
        ),
    )(tokens, cotangent, span_mask, vectors, attention, expand, reduce_t)


def update_kernel(rates, *refs):
    count = len(rates)
    ins, (result, grad) = refs[: 4 * count], refs[4 * count : 4 * count + 2]
    outs, (result_out, grad_out) = refs[4 * count + 2 : 7 * count + 2], refs[7 * count + 2 : 7 * count + 4]
    held, (low, wide) = refs[7 * count + 4 : 11 * count + 4], refs[11 * count + 4 : 11 * count + 6]
    in_sems, out_sems = refs[11 * count + 6 :]
    loads = [pltpu.make_async_copy(ins[n], held[n], in_sems.at[n]) for n in range(4 * count)]
    stores = [pltpu.make_async_copy(held[4 * n + m], outs[3 * n + m], out_sems.at[3 * n + m])
              for n in range(count) for m in range(3)]
    load_grad = pltpu.make_async_copy(grad, low, in_sems.at[4 * count])
    store_grad = pltpu.make_async_copy(wide, grad_out, out_sems.at[3 * count])
    move = pltpu.make_async_copy(result, result_out, out_sems.at[3 * count + 1])
    load_grad.start()
    for copy in loads:
        copy.start()
    move.start()
    load_grad.wait()

    def widen(s, carry):
        wide[s] = low[s].astype(F32)
        return carry

    lax.fori_loop(0, low.shape[0], widen, 0)
    store_grad.start()
    for n in range(count):
        for m in range(4):
            loads[4 * n + m].wait()
        weight, one, two, gradient = held[4 * n : 4 * n + 4]
        values = adamw(weight[...], one[...], two[...], gradient[...], rates[n])
        for ref, value in zip((weight, one, two), values):
            ref[...] = value
        for m in range(3):
            stores[3 * n + m].start()
    for copy in stores + [store_grad, move]:
        copy.wait()


def update(rates, arrays, result, grad):
    flat = [value for group in arrays for value in group]
    new = [jax.ShapeDtypeStruct(value.shape, F32) for group in arrays for value in group[:3]]
    new += [jax.ShapeDtypeStruct(result.shape, BF16), jax.ShapeDtypeStruct(grad.shape, F32)]
    anywhere = pl.BlockSpec(memory_space=pl.ANY)
    scratch = [pltpu.VMEM(value.shape, F32) for value in flat]
    scratch += [pltpu.VMEM(grad.shape, BF16), pltpu.VMEM(grad.shape, F32)]
    scratch += [pltpu.SemaphoreType.DMA((len(flat) + 1,)), pltpu.SemaphoreType.DMA((len(new),))]
    return pl.pallas_call(
        functools.partial(update_kernel, rates),
        out_shape=tuple(new),
        in_specs=[anywhere] * (len(flat) + 2),
        out_specs=(anywhere,) * len(new),
        scratch_shapes=scratch,
        compiler_params=pltpu.CompilerParams(vmem_limit_bytes=63 * 1024 * 1024),
    )(*flat, result, grad)


def local(
    sub,
    tokens,
    cotangent,
    span_mask,
    attention_weight,
    expand_weight,
    reduce_weight,
    vectors,
    attention_first,
    attention_second,
    expand_first,
    expand_second,
    reduce_first,
    reduce_second,
    vector_first,
    vector_second,
):
    together = [[n * sub + m for m in range(sub)] for n in range(GROUPS)]

    def widen(value, axis):
        if sub == 1:
            return value
        low = lax.all_gather(
            value.astype(BF16), "batch", axis=axis, tiled=True, axis_index_groups=together
        )
        return low.astype(F32)

    def narrow(value, axis):
        if sub == 1:
            return value
        return lax.psum_scatter(
            value, "batch", scatter_dimension=axis, tiled=True, axis_index_groups=together
        )

    out_tokens, input_grad, ga, g1, g2, gv = layer(
        sub,
        tokens,
        cotangent,
        span_mask,
        widen(vectors, 1),
        widen(attention_weight, 2),
        widen(expand_weight, 1),
        widen(reduce_weight.T, 0),
    )
    arrays = (
        (attention_weight, attention_first, attention_second, narrow(ga, 2)),
        (expand_weight, expand_first, expand_second, narrow(g1, 1)),
        (reduce_weight.T, reduce_first.T, reduce_second.T, narrow(g2, 0)),
        (vectors, vector_first, vector_second, narrow(gv, 1)),
    )
    rates = (rate_attention, rate_expand, rate_reduce, rate_vector)
    new = update(rates, arrays, out_tokens, input_grad)
    return new[-2:] + new[0:6] + tuple(value.T for value in new[6:9]) + new[9:12]


def solution(mesh):
    sub = mesh.shape["batch"] // GROUPS
    sequences = P("batch", "blk", None)
    attention = P(None, "blk", "batch")
    matrix = P("blk", "batch")
    return jax.shard_map(
        functools.partial(local, sub),
        mesh=mesh,
        in_specs=(sequences, sequences, P("batch", "blk"), attention, matrix, matrix, matrix)
        + (attention,) * 2
        + (matrix,) * 6,
        out_specs=(sequences,) * 2 + (attention,) * 3 + (matrix,) * 9,
        check_vma=False,
    )
```

```python
import functools
import math

import jax
import jax.numpy as jnp
from jax import lax
from jax.experimental import pallas as pl
from jax.experimental.pallas import tpu as pltpu
from jax.sharding import PartitionSpec as P

HEADS = 12
HEAD = 64
STEP = 10
GROUPS = 8

norm_epsilon = 1e-05
beta_one = 0.9
beta_two = 0.999
adam_epsilon = 1e-08
decay_weight = 0.1
rate_attention = 0.05
rate_expand = 0.03
rate_reduce = 0.015
rate_vector = 0.4

F32 = jnp.float32
BF16 = jnp.bfloat16
MESH = pl.DeviceIdType.MESH
GELU_SCALE = math.sqrt(2.0 / math.pi)
GELU_CUBE = 0.044715


def adamw(weight, moment_one, moment_two, gradient, step_rate):
    moment_one = beta_one * moment_one + (1.0 - beta_one) * gradient
    moment_two = beta_two * moment_two + (1.0 - beta_two) * gradient * gradient
    corrected_one = moment_one / (1.0 - beta_one**STEP)
    corrected_two = moment_two / (1.0 - beta_two**STEP)
    updated = weight - step_rate * (
        corrected_one / (jnp.sqrt(corrected_two) + adam_epsilon) + decay_weight * weight
    )
    return (updated, moment_one, moment_two)


def dot_nn(left, right):
    return lax.dot_general(left, right, (((1,), (0,)), ((), ())), preferred_element_type=F32)


def dot_nt(left, right):
    return lax.dot_general(left, right, (((1,), (1,)), ((), ())), preferred_element_type=F32)


def lane_tiles(ref, count=6):
    return jnp.concatenate([ref[t] for t in range(count)], axis=1)


class Unit:
    def __init__(self, order, u, long_axis, fine):
        self.order, self.u, self.long_axis, self.fine = order, u, long_axis, fine


class Gradient:
    def __init__(self, order, u, long_axis, first, count, whole, core_in, long_in, mid_in, line_in, finish):
        self.order, self.long_axis, self.first, self.count, self.whole = order, long_axis, first, count, whole
        self.u, self.core_in, self.long_in, self.mid_in, self.line_in = u, core_in, long_in, mid_in, line_in
        self.finish = finish


def kernel(sub, zs, *refs):
    (tok, cot, mask_in, vec_in, a_in, w1_in, w2_in,
     out, ig, ga, g1, g2, gv,
     ubuf, core_in, long_in, mid_in, line_in,
     x_in, cot_in, stage, vec, gvec, vin, gin, narrow_rows,
     at, n1, q6, k6, v6, o6, pt, h1, acc, n2, act, gp, ta, tb, tc, d6,
     local_sem, ag_send, ag_recv, rs_send, rs_recv, a2a_send, a2a_recv, v_send, v_recv) = refs

    i = lax.axis_index("blk")
    b = lax.axis_index("batch")
    c, y = lax.rem(i, 2), lax.div(i, 2)
    g, r = lax.div(b, sub), lax.rem(b, sub)
    x, z = lax.rem(g, 2), lax.div(g, 2)

    def device(c_=c, y_=y, x_=x, z_=z):
        return {"blk": 2 * y_ + c_, "batch": (2 * z_ + x_) * sub + r}

    def z_at(k):
        return lax.rem(z + k, zs)

    def block_at(k):
        return lax.rem(i + k, 4)

    def copy(src, dst, send, recv, to):
        return pltpu.make_async_remote_copy(
            src_ref=src, dst_ref=dst, send_sem=send, recv_sem=recv, device_id=to, device_id_type=MESH
        )

    def loop(count, body, hooks=()):
        def step(s, carry):
            body(s)
            for k, *todo in hooks:

                @pl.when(s == k)
                def _():
                    for f in todo:
                        f()

            return carry

        lax.fori_loop(0, count, step, 0)

    partners = [device(z_=z_at(k)) for k in range(1, zs)]
    partners += [device(x_=1 - x), device(y_=1 - y), device(c_=1 - c), device(c_=1 - c, y_=1 - y)]
    barrier = pltpu.get_barrier_semaphore()
    for partner in partners:
        pl.semaphore_signal(barrier, inc=1, device_id=partner, device_id_type=MESH)
    pl.semaphore_wait(barrier, len(partners))

    def ag_sems(n, slot):
        return ag_send.at[n.order, slot], ag_recv.at[n.order, slot]

    def group(n, u, long_off, mid_off, cut=None):
        yy = y if (long_off if n.long_axis == "y" else mid_off) == 0 else 1 - y
        xx = x if (long_off if n.long_axis == "x" else mid_off) == 0 else 1 - x
        return u.at[c, yy, xx] if cut is None else u.at[c, yy, xx, cut]

    def partner_of(n, step):
        axis = n.long_axis if step == "long" else {"x": "y", "y": "x"}[n.long_axis]
        return device(x_=1 - x) if axis == "x" else device(y_=1 - y)

    LINE, MID, LONG, LAST, CORE = 0, zs - 1, 2 * zs - 1, 3 * zs - 1, 3 * zs

    def ag_line(n, k, landed=False):
        ref = group(n, n.u, 0, 0, z_at(zs - k) if landed else z)
        return copy(ref, ref, *ag_sems(n, LINE + k - 1), device(z_=z_at(k)))

    def ag_first(n, step, k, landed=False):
        cut = z_at(zs - k) if n.fine else None
        off = (0, 1) if step == "mid" else (1, 0)
        ref = group(n, n.u, *(off if landed else (0, 0)), cut)
        return copy(ref, ref, *ag_sems(n, (MID if step == "mid" else LONG) + k), partner_of(n, step))

    def ag_last(n, landed=False):
        ref = group(n, n.u, 1 if landed else 0, 1)
        return copy(ref, ref, *ag_sems(n, LAST), partner_of(n, "long"))

    def ag_core(n, long_off, mid_off, landed=False):
        ref = group(n, n.u, long_off, mid_off)
        if landed:
            yy = y if (long_off if n.long_axis == "y" else mid_off) == 0 else 1 - y
            xx = x if (long_off if n.long_axis == "x" else mid_off) == 0 else 1 - x
            ref = n.u.at[1 - c, yy, xx]
        return copy(ref, ref, *ag_sems(n, CORE + 2 * long_off + mid_off), device(c_=1 - c))

    def parts(n):
        return range(zs) if n.fine else range(1)

    def ag_start(n):
        if n.fine:
            for step in ("mid", "long"):
                ag_first(n, step, 0).start()
        for k in range(1, zs):
            ag_line(n, k).start()

    def ag_piece(n, k):
        ag_line(n, k, True).wait_recv()
        for step in ("mid", "long"):
            ag_first(n, step, k).start()

    def ag_one(n):
        if not n.fine:
            for k in range(1, zs):
                ag_line(n, k, True).wait_recv()
            for step in ("mid", "long"):
                ag_first(n, step, 0).start()
        ag_core(n, 0, 0).start()

    def ag_two(n):
        for k in parts(n):
            ag_first(n, "mid", k, True).wait_recv()
        ag_last(n).start()
        ag_core(n, 0, 1).start()

    def ag_three(n):
        for k in parts(n):
            ag_first(n, "long", k, True).wait_recv()
        ag_core(n, 1, 0).start()

    def ag_four(n):
        ag_last(n, True).wait_recv()
        ag_core(n, 1, 1).start()

    def ag_done(n):
        for off in ((0, 0), (0, 1), (1, 0), (1, 1)):
            ag_core(n, *off, True).wait_recv()
        for k in range(1, zs):
            ag_line(n, k).wait_send()
        for step in ("mid", "long"):
            for k in parts(n):
                ag_first(n, step, k).wait_send()
        ag_last(n).wait_send()
        for off in ((0, 0), (0, 1), (1, 0), (1, 1)):
            ag_core(n, *off).wait_send()

    def rs_sems(n, slot):
        return rs_send.at[n.order, slot], rs_recv.at[n.order, slot]

    def cut_of(n):
        return slice(None) if n.count == zs else pl.ds(n.first, n.count)

    def rs_core(n, long_off):
        place = 1 - (y if n.long_axis == "y" else x) if long_off else (y if n.long_axis == "y" else x)
        where = (place, slice(None)) if n.long_axis == "y" else (slice(None), place)
        return copy(n.u.at[(1 - c,) + where + (cut_of(n),)], n.core_in.at[where],
                    *rs_sems(n, long_off), device(c_=1 - c))

    def rs_long(n):
        where = (1 - y, slice(None)) if n.long_axis == "y" else (slice(None), 1 - x)
        return copy(n.u.at[(c,) + where + (cut_of(n),)], n.long_in, *rs_sems(n, 2), partner_of(n, "long"))

    def rs_mid(n):
        return copy(group(n, n.u, 0, 1, cut_of(n)), n.mid_in, *rs_sems(n, 3), partner_of(n, "mid"))

    def rs_line(n, k):
        return copy(group(n, n.u, 0, 0, z_at(k)), n.line_in.at[k - 1], *rs_sems(n, 3 + k), device(z_=z_at(k)))

    def within(n, place):
        return jnp.logical_and(place >= n.first, place < n.first + n.count)

    def when_within(n, place, f):
        if n.whole:
            f()
        else:
            pl.when(within(n, place))(f)

    def gather_terms(n, long_off, mid_off, names):
        yy = y if (long_off if n.long_axis == "y" else mid_off) == 0 else 1 - y
        xx = x if (long_off if n.long_axis == "x" else mid_off) == 0 else 1 - x

        def body(s):
            mine = n.u.at[c, yy, xx, n.first + s]
            value = mine[...].astype(F32) + n.core_in[yy, xx, s].astype(F32)
            if "long" in names:
                value = value + n.long_in[xx if n.long_axis == "y" else yy, s].astype(F32)
            if "mid" in names:
                value = value + n.mid_in[s].astype(F32)
            mine[...] = value.astype(BF16)

        loop(n.count, body)

    def rs_zero(n):
        rs_core(n, 1).start()
        rs_core(n, 0).start()

    def rs_one(n):
        rs_core(n, 1).wait_recv()
        gather_terms(n, 1, 0, ())
        gather_terms(n, 1, 1, ())
        rs_long(n).start()

    def rs_two(n):
        rs_core(n, 0).wait_recv()
        rs_long(n).wait_recv()
        gather_terms(n, 0, 1, ("long",))
        rs_mid(n).start()

    def rs_three(n):
        rs_mid(n).wait_recv()
        gather_terms(n, 0, 0, ("long", "mid"))
        for k in range(1, zs):
            when_within(n, z_at(k), lambda k=k: rs_line(n, k).start())

    def rs_done(n):
        def finish():
            for k in range(1, zs):
                rs_line(n, k).wait_recv()
            value = n.u[c, y, x, z].astype(F32)
            for k in range(1, zs):
                value = value + n.line_in[k - 1].astype(F32)
            n.finish(value)

        when_within(n, z, finish)
        for moved in (rs_core(n, 0), rs_core(n, 1), rs_long(n), rs_mid(n)):
            moved.wait_send()
        for k in range(1, zs):
            when_within(n, z_at(k), lambda k=k: rs_line(n, k).wait_send())

    def small_sum(ref, slots, which):
        to = (device(y_=1 - y), device(c_=1 - c), device(x_=1 - x))
        to += tuple(device(z_=z_at(k)) for k in range(1, zs))

        def moved(slot):
            return copy(ref, slots.at[slot], v_send.at[which, slot], v_recv.at[which, slot], to[slot])

        def land(last):
            moved(last).wait()
            ref[...] = ref[...] + slots[last]

        def step(n):
            def run():
                if n > 0:
                    land(n - 1)
                moved(n).start()

            return run

        def line():
            land(2)
            for k in range(1, zs):
                moved(2 + k).start()

        def finish():
            for k in range(1, zs):
                moved(2 + k).wait()
            value = ref[...]
            for k in range(1, zs):
                value = value + slots[2 + k]
            ref[...] = value

        return [step(0), step(1), step(2), line, finish]

    def exchange(src, dst, which):
        return [copy(src.at[block_at(k)], dst.at[i], a2a_send.at[which, k - 1],
                     a2a_recv.at[which, k - 1], {"blk": block_at(k), "batch": b})
                for k in range(1, 4)]

    def exchange_landed(dst, which):
        return [copy(dst.at[block_at(4 - k)], dst.at[block_at(4 - k)], a2a_send.at[which, k - 1],
                     a2a_recv.at[which, k - 1], {"blk": block_at(4 - k), "batch": b})
                for k in range(1, 4)]

    units = [Unit(2 * n + half, ubuf.at[n, half], axes[half], n == 0)
             for n, axes in enumerate(("xy", "xy", "xx")) for half in range(2)]
    unit_qk, unit_vo, unit_w1, unit_w2 = units[0], units[1], units[2:4], units[4:6]

    def rest_rows(matrix):
        return a_in[matrix, pl.ds(pl.multiple_of(128 * (1 - c), 64), 64), :]

    def own_attention(p):
        mine = ubuf.at[0, p, c, y, x, z]
        for m in range(2):
            main = a_in[2 * p + m, pl.ds(pl.multiple_of(64 * c, 64), 128), :]
            mine[96 * m : 96 * m + 96, :] = main.T.astype(BF16)
        rest = jnp.concatenate([rest_rows(2 * p + c), rest_rows(2 * p + 1 - c)], axis=0)
        mine[192:288, :] = rest.T.astype(BF16)

    def own_feed_forward():
        for h in range(2):
            for t in range(3):
                ubuf[1, h, c, y, x, z, 96 * t : 96 * t + 96, :] = w1_in[
                    96 * h : 96 * h + 96, 128 * t : 128 * t + 128
                ].astype(BF16)
            for t in range(6):
                ubuf[2, h, c, y, x, z, 48 * t : 48 * t + 48, :] = w2_in[
                    48 * h : 48 * h + 48, 128 * t : 128 * t + 128
                ].astype(BF16)

    columns = a_in.shape[2]
    placed = lax.broadcasted_iota(jnp.int32, (columns, 768), 1) == (
        lax.broadcasted_iota(jnp.int32, (columns, 768), 0) + columns * g
    )

    def own_vectors():
        vec[...] = jnp.zeros_like(vec)
        rows = dot_nn(vec_in[...].astype(BF16), jnp.where(placed, 1.0, 0.0).astype(BF16))
        for j in range(3):
            vec[pl.ds(3 * i + j, 1), :] = rows[j : j + 1, :]

    def masked_cotangent():
        eye = lax.broadcasted_iota(jnp.int32, (128, 128), 0) == lax.broadcasted_iota(jnp.int32, (128, 128), 1)
        for s in range(4):
            row = jnp.broadcast_to(mask_in[s : s + 1, :].astype(F32), (128, 128))
            column = jnp.sum(jnp.where(eye, row, 0.0), axis=1, keepdims=True)
            stage[s] = (cot[s].astype(F32) * column).astype(BF16)

    def finish_attention(p):
        def finish(value):
            for m in range(2):
                ga[2 * p + m, pl.ds(pl.multiple_of(64 * c, 64), 128), :] = value[96 * m : 96 * m + 96, :].T
            rest = value[192:288, :].T
            rows = pl.ds(pl.multiple_of(128 * (1 - c), 64), 64)
            ga[2 * p + c, rows, :] = rest[0:64, :]
            ga[2 * p + 1 - c, rows, :] = rest[64:128, :]

        return finish

    def finish_expand(h):
        def finish(value):
            for t in range(3):
                g1[96 * h : 96 * h + 96, 128 * t : 128 * t + 128] = value[96 * t : 96 * t + 96, :]

        return finish

    def finish_reduce(h):
        def finish(value):
            for t in range(6):
                g2[48 * h : 48 * h + 48, 128 * t : 128 * t + 128] = value[48 * t : 48 * t + 48, :]

        return finish

    def finish_vectors():
        value, total = gvec[...], 0.0
        for _ in range(3):
            part = value.astype(BF16)
            total = total + dot_nt(part, jnp.where(placed, 1.0, 0.0).astype(BF16))
            value = value - part.astype(F32)
        narrow_rows[...] = total
        for j in range(3):
            gv[j : j + 1, :] = narrow_rows[pl.ds(3 * i + j, 1), :]

    grads = []
    half_zs = zs // 2
    for n, (source, finish, axes) in enumerate(((0, finish_reduce, "xx"), (2, finish_expand, "yx"))):
        for half in range(2):
            order = 2 * n + half
            grads.append(Gradient(order, ubuf.at[source, half], axes[half], 0, zs, True,
                                  core_in.at[order], long_in.at[order], mid_in.at[order],
                                  line_in.at[order], finish(half)))
    for part in range(2):
        for half in range(2):
            cut = pl.ds(part * half_zs, half_zs)
            grads.append(Gradient(4 + 2 * part + half, ubuf.at[1, half], "xy"[half], part * half_zs, half_zs,
                                  False, core_in.at[4 + half, :, :, cut], long_in.at[4 + half, :, cut],
                                  mid_in.at[4 + half, cut], line_in.at[4 + half], finish_attention(half)))
    grad_w2, grad_w1, grad_a = grads[0:2], grads[2:4], (grads[4:6], grads[6:8])

    def each(f, which):
        def run():
            for n in which:
                f(n)

        return run

    own_attention(0)
    ag_start(unit_qk)
    own_vectors()
    vec_steps = small_sum(vec, vin, 0)
    vec_steps[0]()
    own_tokens = pltpu.make_async_copy(tok.at[i], x_in.at[i], local_sem.at[0])
    own_tokens.start()
    tokens_out = exchange(tok, x_in, 0)
    for moved in tokens_out:
        moved.start()
    own_attention(1)
    own_feed_forward()
    for k in range(1, zs):
        ag_piece(unit_qk, k)
    ag_one(unit_qk)
    ag_start(unit_vo)
    ag_start(unit_w1[0])
    vec_steps[1]()
    masked_cotangent()
    ag_two(unit_qk)
    vec_steps[2]()
    for k in range(1, zs):
        ag_piece(unit_vo, k)
    ag_one(unit_vo)
    ag_start(unit_w1[1])
    vec_steps[3]()
    ag_three(unit_qk)

    for moved in exchange_landed(x_in, 0):
        moved.wait_recv()
    own_tokens.wait()
    vec_steps[4]()

    def normalise(value):
        centered = value - jnp.mean(value, axis=-1, keepdims=True)
        scale = lax.rsqrt(jnp.mean(centered * centered, axis=-1, keepdims=True) + norm_epsilon)
        return centered * scale, scale

    def rows_of(s):
        return pl.ds(pl.multiple_of(s * 128, 128), 128)

    def first_norm(s):
        unit, _ = normalise(x_in[s].astype(F32))
        n1[rows_of(s), :] = (unit * vec[0:1, :] + vec[1:2, :]).astype(BF16)

    loop(4, first_norm)
    ag_four(unit_qk)
    own_cot = pltpu.make_async_copy(stage.at[i], cot_in.at[i], local_sem.at[1])
    own_cot.start()
    cot_out = exchange(stage, cot_in, 1)
    for moved in cot_out:
        moved.start()
    ag_done(unit_qk)

    lanes = lax.broadcasted_iota(jnp.int32, (96, 128), 1)

    def unpack(p, s):
        for xx in range(2):
            rows = pl.ds(pl.multiple_of((2 * s + xx) * 96, 96), 96)
            for yy in range(2):
                first, second = ubuf.at[0, p, 0, yy, xx, s], ubuf.at[0, p, 1, yy, xx, s]
                lo, hi = 384 * yy, 384 * yy + 256
                for m in range(2):
                    at[2 * p + m, rows, lo : lo + 128] = first[96 * m : 96 * m + 96, :]
                    at[2 * p + m, rows, hi : hi + 128] = second[96 * m : 96 * m + 96, :]
                rest_first = first[192:288, :].astype(F32)
                rest_second = second[192:288, :].astype(F32)
                even = jnp.where(lanes < 64, rest_first, rest_second)
                odd = pltpu.roll(jnp.where(lanes < 64, rest_second, rest_first), 64, 1)
                at[2 * p, rows, lo + 128 : lo + 256] = even.astype(BF16)
                at[2 * p + 1, rows, lo + 128 : lo + 256] = odd.astype(BF16)

    def project(m, dst, bias):
        for n in range(3):
            value = dot_nt(n1[...], at[m, 256 * n : 256 * n + 256, :])
            if bias is not None:
                value = value + vec[bias : bias + 1, 256 * n : 256 * n + 256]
            value = value.astype(BF16)
            if m == 0:
                value = value * jnp.asarray(HEAD ** (-0.5), BF16)
            dst[2 * n] = value[:, 0:128]
            dst[2 * n + 1] = value[:, 128:256]

    loop(zs, functools.partial(unpack, 0))
    project(0, q6, 2)
    ag_two(unit_vo)
    project(1, k6, None)
    ag_one(unit_w1[0])

    half_lane = lax.broadcasted_iota(jnp.int32, (512, 128), 1) // HEAD

    def half_of(value, which):
        return jnp.where(half_lane == which, value, jnp.zeros_like(value))

    def turn(value):
        return value.astype(F32).T.astype(BF16)

    def attend(p):
        queries, keys = q6[p], k6[p]
        for which in range(2):
            scores = dot_nt(half_of(keys, which), queries)
            expo = jnp.exp(scores - jnp.max(scores, axis=0, keepdims=True))
            probs = (expo * (1.0 / jnp.sum(expo, axis=0, keepdims=True))).astype(BF16)
            pt[2 * p + which] = probs

    def mix(p):
        values_t = turn(v6[p])
        mixed = [dot_nn(values_t[64 * which : 64 * which + 64, :], pt[2 * p + which]) for which in range(2)]
        o6[p] = jnp.concatenate(mixed, axis=0).T.astype(BF16)

    loop(6, attend, (
        (1, lambda: ag_three(unit_vo)),
        (2, lambda: ag_one(unit_w1[1]), each(ag_start, unit_w2)),
        (3, lambda: ag_four(unit_vo), lambda: ag_two(unit_w1[0])),
    ))
    ag_two(unit_w1[1])
    ag_done(unit_vo)
    loop(zs, functools.partial(unpack, 1))
    project(2, v6, 3)
    each(ag_three, unit_w1)()
    loop(6, mix, (
        (1, lambda: ag_one(unit_w2[0])),
        (3, each(ag_four, unit_w1), lambda: ag_one(unit_w2[1])),
        (5, lambda: ag_two(unit_w2[0])),
    ))

    for n in range(3):
        cols = slice(256 * n, 256 * n + 256)
        value = dot_nt(lane_tiles(o6), at[3, cols, :]) + vec[4:5, cols]
        for s in range(4):
            h1[128 * s : 128 * s + 128, cols] = x_in[s, :, cols].astype(F32) + value[128 * s : 128 * s + 128]

    def second_norm(s):
        unit, _ = normalise(h1[rows_of(s), :])
        n2[rows_of(s), :] = (unit * vec[5:6, :] + vec[6:7, :]).astype(BF16)

    loop(4, second_norm)
    each(ag_done, unit_w1)()
    ag_two(unit_w2[1])

    def expand_piece(s, xx):
        def piece(ref):
            return jnp.concatenate([ref[96 * t : 96 * t + 96, :] for t in range(3)], axis=1)

        return jnp.concatenate(
            [piece(ubuf.at[1, h, cc, yy, xx, s]) for yy in range(2) for cc in range(2) for h in range(2)],
            axis=0,
        )

    def reduce_block(s):
        yy, cc = lax.div(s, 2), lax.rem(s, 2)

        def piece(ref):
            return jnp.concatenate([ref[48 * t : 48 * t + 48, :] for t in range(6)], axis=1)

        return jnp.concatenate(
            [piece(ubuf.at[2, h, cc, yy, xx, zz]) for zz in range(zs) for xx in range(2) for h in range(2)],
            axis=0,
        )

    def block_rows(s):
        return pl.ds(pl.multiple_of(s * 512, 512), 512)

    def expand(s):
        for xx in range(2):
            cols = slice(384 * xx, 384 * xx + 384)
            inner = dot_nn(n2[...], expand_piece(s, xx)) + vec[pl.ds(8 + s, 1), cols]
            square = inner * inner
            tanh = jnp.tanh(GELU_SCALE * inner * (1.0 + GELU_CUBE * square))
            act[block_rows(s), cols] = (0.5 * inner * (1.0 + tanh)).astype(BF16)
            slope = 0.5 * (1.0 + tanh) + 0.5 * inner * (1.0 - tanh * tanh) * (
                GELU_SCALE * (1.0 + 3.0 * GELU_CUBE * square)
            )
            gp[block_rows(s), cols] = slope.astype(BF16)

    loop(4, expand, (
        (1, each(ag_three, unit_w2)),
        (3, lambda: ag_four(unit_w2[0])),
    ))

    for moved in exchange_landed(cot_in, 1):
        moved.wait_recv()
    own_cot.wait()
    gvec[...] = jnp.zeros_like(gvec)

    def transpose_rows(dst, s, value):
        dst[:, 128 * s : 128 * s + 128] = turn(value)

    total = jnp.zeros((1, 768), F32)
    for s in range(4):
        transpose_rows(ta, s, cot_in[s])
        total = total + jnp.sum(cot_in[s].astype(F32), axis=0, keepdims=True)
    gvec[7:8, :] = total

    def reduce_back(s):
        yy, cc = lax.div(s, 2), lax.rem(s, 2)
        grad = dot_nn(ta[...], act[block_rows(s), :]).astype(BF16)
        for zz in range(zs):
            for xx in range(2):
                for h in range(2):
                    row = 96 * (2 * zz + xx) + 48 * h
                    for t in range(6):
                        ubuf[0, h, cc, yy, xx, zz, 48 * t : 48 * t + 48, :] = grad[
                            row : row + 48, 128 * t : 128 * t + 128
                        ]

    loop(4, reduce_back)
    each(rs_zero, grad_w2)()
    ag_four(unit_w2[1])
    each(rs_one, grad_w2)()
    each(ag_done, unit_w2)()

    def cotangent_rows():
        return jnp.concatenate([cot_in[s] for s in range(4)], axis=0)

    def inner_back(s):
        grad = dot_nn(cotangent_rows(), reduce_block(s)) * gp[block_rows(s), :].astype(F32)
        low = grad.astype(BF16)
        gp[block_rows(s), :] = low
        gvec[pl.ds(8 + s, 1), :] = jnp.sum(low.astype(F32), axis=0, keepdims=True)

    loop(4, inner_back)

    acc[...] = h1[...] + vec[7:8, :]

    def reduce(s):
        acc[...] += dot_nt(act[block_rows(s), :], reduce_block(s))

    loop(4, reduce)
    for moved in cot_out:
        moved.wait_send()
    for s in range(4):
        stage[s] = acc[128 * s : 128 * s + 128, :].astype(BF16)
    own_out = pltpu.make_async_copy(stage.at[i], out.at[i], local_sem.at[2])
    own_out.start()
    result_out = exchange(stage, out, 2)
    for moved in result_out:
        moved.start()

    for s in range(4):
        transpose_rows(tb, s, n2[128 * s : 128 * s + 128, :])

    def expand_back(s):
        for xx in range(2):
            grad = dot_nn(tb[...], gp[block_rows(s), 384 * xx : 384 * xx + 384]).astype(BF16)
            for yy in range(2):
                for cc in range(2):
                    for h in range(2):
                        row = 192 * (2 * yy + cc) + 96 * h
                        for t in range(3):
                            ubuf[2, h, cc, yy, xx, s, 96 * t : 96 * t + 96, :] = grad[
                                row : row + 96, 128 * t : 128 * t + 128
                            ]

    loop(4, expand_back)
    each(rs_zero, grad_w1)()
    each(rs_two, grad_w2)()

    def norm_back(s):
        whole = jnp.concatenate([expand_piece(s, 0), expand_piece(s, 1)], axis=1)
        part = dot_nt(gp[block_rows(s), :], whole)

        @pl.when(s == 0)
        def _():
            acc[...] = part

        @pl.when(s > 0)
        def _():
            acc[...] += part

    loop(4, norm_back, ((1, each(rs_one, grad_w1)),))

    def norm_gradient(value, scale_row, grad):
        unit, scale = normalise(value)
        gain_sum = jnp.sum(grad * unit, axis=0, keepdims=True)
        bias_sum = jnp.sum(grad, axis=0, keepdims=True)
        inner = grad * scale_row
        mean = jnp.mean(inner, axis=-1, keepdims=True)
        along = jnp.mean(inner * unit, axis=-1, keepdims=True)
        return scale * (inner - mean - unit * along), gain_sum, bias_sum

    def hidden_back(s):
        rows = rows_of(s)
        grad, gain_sum, bias_sum = norm_gradient(h1[rows, :], vec[5:6, :], acc[rows, :])
        grad = grad + cot_in[s].astype(F32)
        h1[rows, :] = grad
        low = grad.astype(BF16)
        n2[rows, :] = low
        gvec[5:6, :] += gain_sum
        gvec[6:7, :] += bias_sum
        gvec[4:5, :] += jnp.sum(low.astype(F32), axis=0, keepdims=True)

    loop(4, hidden_back)

    for n in range(3):
        value = dot_nn(n2[...], at[3, :, 256 * n : 256 * n + 256]).astype(BF16)
        d6[2 * n] = value[:, 0:128]
        d6[2 * n + 1] = value[:, 128:256]
    for s in range(4):
        transpose_rows(tc, s, n2[128 * s : 128 * s + 128, :])
    act[768:1536, :] = dot_nn(tc[...], lane_tiles(o6)).astype(BF16)
    each(rs_three, grad_w2)()

    def attend_back(p):
        rows = rows_of(p)
        queries, keys, values, grads_in = q6[p], k6[p], v6[p], d6[p]
        keys_t = turn(keys)
        grad_query, grad_key, grad_value = [], 0.0, 0.0
        for which in range(2):
            probs = pt[2 * p + which]
            wide = probs.astype(F32)
            grad_probs = dot_nt(half_of(values, which), grads_in)
            inner = jnp.sum(wide * grad_probs, axis=0, keepdims=True)
            grad_scores = (wide * (grad_probs - inner)).astype(BF16)
            grad_query.append(dot_nn(keys_t[64 * which : 64 * which + 64, :], grad_scores))
            grad_key = grad_key + dot_nn(grad_scores, half_of(queries, which))
            grad_value = grad_value + dot_nn(probs, half_of(grads_in, which))
        grad_query = jnp.concatenate(grad_query, axis=0) * HEAD ** (-0.5)
        ta[rows, :] = grad_query.astype(BF16)
        tb[rows, :] = grad_key.T.astype(BF16)
        tc[rows, :] = grad_value.T.astype(BF16)
        q6[p] = grad_query.T.astype(BF16)
        k6[p] = grad_key.astype(BF16)
        v6[p] = grad_value.astype(BF16)

    def pack(p, part, first_row, second_row):
        def body(s):
            for xx in range(2):
                offset = (2 * s + xx) * 96
                rows = [pl.ds(pl.multiple_of(first_row + offset, 96), 96),
                        pl.ds(pl.multiple_of(second_row + offset, 96), 96)]
                first = ubuf.at[1, p, 0, :, xx, part * half_zs + s]
                second = ubuf.at[1, p, 1, :, xx, part * half_zs + s]
                for yy in range(2):
                    lo, mid, hi = 384 * yy, 384 * yy + 128, 384 * yy + 256
                    for m in range(2):
                        first[yy, 96 * m : 96 * m + 96, :] = act[rows[m], lo : lo + 128]
                        second[yy, 96 * m : 96 * m + 96, :] = act[rows[m], hi : hi + 128]
                    even = act[rows[0], mid : mid + 128].astype(F32)
                    odd = pltpu.roll(act[rows[1], mid : mid + 128].astype(F32), 64, 1)
                    first[yy, 192:288, :] = jnp.where(lanes < 64, even, odd).astype(BF16)
                    second[yy, 192:288, :] = jnp.where(lanes < 64, odd, even).astype(BF16)

        loop(half_zs, body)

    def attention_gradients(part):
        rows = slice(384 * part, 384 * part + 384)
        act[1536:1920, :] = dot_nn(tc[rows, :], n1[...]).astype(BF16)
        pack(1, part, 1536, 768 + 384 * part)
        rs_zero(grad_a[part][1])
        act[0:384, :] = dot_nn(ta[rows, :], n1[...]).astype(BF16)
        act[384:768, :] = dot_nn(tb[rows, :], n1[...]).astype(BF16)
        pack(0, part, 0, 384)
        rs_zero(grad_a[part][0])

    loop(3, attend_back, ((0, each(rs_two, grad_w1)), (1, each(rs_done, grad_w2))))
    attention_gradients(0)
    loop(3, lambda p: attend_back(p + 3), (
        (0, each(rs_one, grad_a[0])),
        (1, each(rs_three, grad_w1)),
        (2, each(rs_two, grad_a[0])),
    ))
    attention_gradients(1)
    each(rs_one, grad_a[1])()
    each(rs_done, grad_w1)()

    acc[...] = dot_nn(lane_tiles(q6), at[0])
    acc[...] += dot_nn(lane_tiles(k6), at[1])
    acc[...] += dot_nn(lane_tiles(v6), at[2])
    gvec[2:3, :] = jnp.sum(lane_tiles(q6).astype(F32), axis=0, keepdims=True)
    gvec[3:4, :] = jnp.sum(lane_tiles(v6).astype(F32), axis=0, keepdims=True)
    each(rs_three, grad_a[0])()

    for moved in result_out:
        moved.wait_send()
    own_out.wait()

    def input_back(s):
        rows = rows_of(s)
        grad, gain_sum, bias_sum = norm_gradient(x_in[s].astype(F32), vec[0:1, :], acc[rows, :])
        stage[s] = (grad + h1[rows, :]).astype(BF16)
        gvec[0:1, :] += gain_sum
        gvec[1:2, :] += bias_sum

    loop(4, input_back)
    gvec_steps = small_sum(gvec, gin, 1)
    gvec_steps[0]()
    own_grad = pltpu.make_async_copy(stage.at[i], ig.at[i], local_sem.at[3])
    own_grad.start()
    grad_out = exchange(stage, ig, 3)
    for moved in grad_out:
        moved.start()

    gvec_steps[1]()
    each(rs_two, grad_a[1])()
    gvec_steps[2]()
    each(rs_done, grad_a[0])()
    gvec_steps[3]()
    each(rs_three, grad_a[1])()
    gvec_steps[4]()
    finish_vectors()
    each(rs_done, grad_a[1])()

    own_grad.wait()
    for moved in tokens_out + grad_out:
        moved.wait_send()
    for moved in exchange_landed(out, 2) + exchange_landed(ig, 3):
        moved.wait_recv()


def layer(sub, tokens, cotangent, span_mask, vectors, attention, expand, reduce_t):
    zs = GROUPS // 2
    seqs, block, width = tokens.shape
    rows = seqs * block
    columns = attention.shape[2]
    piece = (3 * columns, 128)
    vmem = lambda shape, dtype: pltpu.VMEM(shape, dtype)
    scratch = [vmem((3, 2, 2, 2, 2, zs) + piece, BF16)]
    scratch += [vmem((6, 2, 2, zs) + piece, BF16), vmem((6, 2, zs) + piece, BF16)]
    scratch += [vmem((6, zs) + piece, BF16), vmem((6, zs - 1) + piece, BF16)]
    scratch += [vmem(tokens.shape, BF16)] * 3
    scratch += [vmem((16, width), F32)] * 2
    scratch += [vmem((zs + 2, 16, width), F32)] * 2
    scratch += [vmem((16, columns), F32)]
    tiles = vmem((width // 128, rows, 128), BF16)
    flat = vmem((rows, width), BF16)
    turned = vmem((width, rows), BF16)
    scratch += [vmem((4, width, width), BF16), flat, tiles, tiles, tiles, tiles]
    scratch += [vmem((HEADS, rows, rows), BF16), vmem((rows, width), F32), vmem((rows, width), F32)]
    scratch += [flat, vmem((4 * rows, width), BF16), vmem((4 * rows, width), BF16)]
    scratch += [turned, turned, turned, tiles]
    scratch += [pltpu.SemaphoreType.DMA((4,))]
    scratch += [pltpu.SemaphoreType.DMA((6, 3 * zs + 4))] * 2
    scratch += [pltpu.SemaphoreType.DMA((8, zs + 3))] * 2
    scratch += [pltpu.SemaphoreType.DMA((4, 3))] * 2
    scratch += [pltpu.SemaphoreType.DMA((2, zs + 2))] * 2
    in_vmem = pl.BlockSpec(memory_space=pltpu.VMEM)
    anywhere = pl.BlockSpec(memory_space=pl.ANY)
    return pl.pallas_call(
        functools.partial(kernel, sub, zs),
        out_shape=(
            jax.ShapeDtypeStruct(tokens.shape, BF16),
            jax.ShapeDtypeStruct(tokens.shape, BF16),
            jax.ShapeDtypeStruct(attention.shape, F32),
            jax.ShapeDtypeStruct(expand.shape, F32),
            jax.ShapeDtypeStruct(reduce_t.shape, F32),
            jax.ShapeDtypeStruct(vectors.shape, F32),
        ),
        in_specs=[anywhere] + [in_vmem] * 6,
        out_specs=(anywhere, anywhere) + (in_vmem,) * 4,
        scratch_shapes=scratch,
        compiler_params=pltpu.CompilerParams(
            collective_id=0, has_side_effects=True, vmem_limit_bytes=63 * 1024 * 1024
        ),
    )(tokens, cotangent, span_mask, vectors, attention, expand, reduce_t)


def update_kernel(rates, *refs):
    count = len(rates)
    ins, (result, grad) = refs[: 4 * count], refs[4 * count : 4 * count + 2]
    outs, (result_out, grad_out) = refs[4 * count + 2 : 7 * count + 2], refs[7 * count + 2 : 7 * count + 4]
    held, (low, wide, passed) = refs[7 * count + 4 : 11 * count + 4], refs[11 * count + 4 : 11 * count + 7]
    in_sems, out_sems = refs[11 * count + 7 :]
    loads = [pltpu.make_async_copy(ins[n], held[n], in_sems.at[n]) for n in range(4 * count)]
    stores = [pltpu.make_async_copy(held[4 * n + m], outs[3 * n + m], out_sems.at[3 * n + m])
              for n in range(count) for m in range(3)]
    load_grad = pltpu.make_async_copy(grad, low, in_sems.at[4 * count])
    store_grad = pltpu.make_async_copy(wide, grad_out, out_sems.at[3 * count])
    load_result = pltpu.make_async_copy(result, passed, in_sems.at[4 * count + 1])
    store_result = pltpu.make_async_copy(passed, result_out, out_sems.at[3 * count + 1])
    load_grad.start()
    load_result.start()
    for copy in loads:
        copy.start()
    load_result.wait()
    store_result.start()
    load_grad.wait()

    def widen(s, carry):
        wide[s] = low[s].astype(F32)
        return carry

    lax.fori_loop(0, low.shape[0], widen, 0)
    store_grad.start()
    for n in range(count):
        for m in range(4):
            loads[4 * n + m].wait()
        weight, one, two, gradient = held[4 * n : 4 * n + 4]
        values = adamw(weight[...], one[...], two[...], gradient[...], rates[n])
        for ref, value in zip((weight, one, two), values):
            ref[...] = value
        for m in range(3):
            stores[3 * n + m].start()
    for copy in stores + [store_grad, store_result]:
        copy.wait()


def update(rates, arrays, result, grad):
    flat = [value for group in arrays for value in group]
    new = [jax.ShapeDtypeStruct(value.shape, F32) for group in arrays for value in group[:3]]
    new += [jax.ShapeDtypeStruct(result.shape, BF16), jax.ShapeDtypeStruct(grad.shape, F32)]
    anywhere = pl.BlockSpec(memory_space=pl.ANY)
    scratch = [pltpu.VMEM(value.shape, F32) for value in flat]
    scratch += [pltpu.VMEM(grad.shape, BF16), pltpu.VMEM(grad.shape, F32), pltpu.VMEM(result.shape, BF16)]
    scratch += [pltpu.SemaphoreType.DMA((len(flat) + 2,)), pltpu.SemaphoreType.DMA((len(new),))]
    return pl.pallas_call(
        functools.partial(update_kernel, rates),
        out_shape=tuple(new),
        in_specs=[anywhere] * (len(flat) + 2),
        out_specs=(anywhere,) * len(new),
        scratch_shapes=scratch,
        compiler_params=pltpu.CompilerParams(vmem_limit_bytes=63 * 1024 * 1024),
    )(*flat, result, grad)


def local(
    sub,
    tokens,
    cotangent,
    span_mask,
    attention_weight,
    expand_weight,
    reduce_weight,
    vectors,
    attention_first,
    attention_second,
    expand_first,
    expand_second,
    reduce_first,
    reduce_second,
    vector_first,
    vector_second,
):
    together = [[n * sub + m for m in range(sub)] for n in range(GROUPS)]

    def widen(value, axis):
        if sub == 1:
            return value
        low = lax.all_gather(
            value.astype(BF16), "batch", axis=axis, tiled=True, axis_index_groups=together
        )
        return low.astype(F32)

    def narrow(value, axis):
        if sub == 1:
            return value
        return lax.psum_scatter(
            value, "batch", scatter_dimension=axis, tiled=True, axis_index_groups=together
        )

    out_tokens, input_grad, ga, g1, g2, gv = layer(
        sub,
        tokens,
        cotangent,
        span_mask,
        widen(vectors, 1),
        widen(attention_weight, 2),
        widen(expand_weight, 1),
        widen(reduce_weight.T, 0),
    )
    arrays = (
        (attention_weight, attention_first, attention_second, narrow(ga, 2)),
        (expand_weight, expand_first, expand_second, narrow(g1, 1)),
        (reduce_weight.T, reduce_first.T, reduce_second.T, narrow(g2, 0)),
        (vectors, vector_first, vector_second, narrow(gv, 1)),
    )
    rates = (rate_attention, rate_expand, rate_reduce, rate_vector)
    new = update(rates, arrays, out_tokens, input_grad)
    return new[-2:] + new[0:6] + tuple(value.T for value in new[6:9]) + new[9:12]


def solution(mesh):
    sub = mesh.shape["batch"] // GROUPS
    sequences = P("batch", "blk", None)
    attention = P(None, "blk", "batch")
    matrix = P("blk", "batch")
    return jax.shard_map(
        functools.partial(local, sub),
        mesh=mesh,
        in_specs=(sequences, sequences, P("batch", "blk"), attention, matrix, matrix, matrix)
        + (attention,) * 2
        + (matrix,) * 6,
        out_specs=(sequences,) * 2 + (attention,) * 3 + (matrix,) * 9,
        check_vma=False,
    )
```

```python
import functools
import math

import jax
import jax.numpy as jnp
from jax import lax
from jax.experimental import pallas as pl
from jax.experimental.pallas import tpu as pltpu
from jax.sharding import PartitionSpec as P

HEADS = 12
HEAD = 64
STEP = 10
GROUPS = 8

norm_epsilon = 1e-05
beta_one = 0.9
beta_two = 0.999
adam_epsilon = 1e-08
decay_weight = 0.1
rate_attention = 0.05
rate_expand = 0.03
rate_reduce = 0.015
rate_vector = 0.4

F32 = jnp.float32
BF16 = jnp.bfloat16
MESH = pl.DeviceIdType.MESH
GELU_SCALE = math.sqrt(2.0 / math.pi)
GELU_CUBE = 0.044715


def adamw(weight, moment_one, moment_two, gradient, step_rate):
    moment_one = beta_one * moment_one + (1.0 - beta_one) * gradient
    moment_two = beta_two * moment_two + (1.0 - beta_two) * gradient * gradient
    corrected_one = moment_one / (1.0 - beta_one**STEP)
    corrected_two = moment_two / (1.0 - beta_two**STEP)
    updated = weight - step_rate * (
        corrected_one / (jnp.sqrt(corrected_two) + adam_epsilon) + decay_weight * weight
    )
    return (updated, moment_one, moment_two)


def dot_nn(left, right):
    return lax.dot_general(left, right, (((1,), (0,)), ((), ())), preferred_element_type=F32)


def dot_nt(left, right):
    return lax.dot_general(left, right, (((1,), (1,)), ((), ())), preferred_element_type=F32)


def lane_tiles(ref, count=6):
    return jnp.concatenate([ref[t] for t in range(count)], axis=1)


class Unit:
    def __init__(self, order, u, long_axis, fine):
        self.order, self.u, self.long_axis, self.fine = order, u, long_axis, fine


class Gradient:
    def __init__(self, order, u, long_axis, first, count, whole, core_in, long_in, mid_in, line_in, finish):
        self.order, self.long_axis, self.first, self.count, self.whole = order, long_axis, first, count, whole
        self.u, self.core_in, self.long_in, self.mid_in, self.line_in = u, core_in, long_in, mid_in, line_in
        self.finish = finish


def kernel(sub, zs, *refs):
    (tok, cot, mask_in, vec_in, a_in, w1_in, w2_in,
     out, ig, ga, g1, g2, gv,
     ubuf, core_in, long_in, mid_in, line_in,
     x_in, cot_in, stage, vec, gvec, vin, gin, narrow_rows,
     at, n1, q6, k6, v6, o6, pt, h1, acc, n2, act, gp, ta, tb, tc, d6,
     local_sem, ag_send, ag_recv, rs_send, rs_recv, a2a_send, a2a_recv, v_send, v_recv) = refs

    i = lax.axis_index("blk")
    b = lax.axis_index("batch")
    c, y = lax.rem(i, 2), lax.div(i, 2)
    g, r = lax.div(b, sub), lax.rem(b, sub)
    x, z = lax.rem(g, 2), lax.div(g, 2)

    def device(c_=c, y_=y, x_=x, z_=z):
        return {"blk": 2 * y_ + c_, "batch": (2 * z_ + x_) * sub + r}

    def z_at(k):
        return lax.rem(z + k, zs)

    def block_at(k):
        return lax.rem(i + k, 4)

    def copy(src, dst, send, recv, to):
        return pltpu.make_async_remote_copy(
            src_ref=src, dst_ref=dst, send_sem=send, recv_sem=recv, device_id=to, device_id_type=MESH
        )

    class Spread:
        def __init__(self, src, dst, send, recv, to):
            self.args = (src, dst, send, recv, to)

        def start(self):
            src, dst, send, recv, to = self.args
            lead = src.shape[:-2]
            for flat in range(math.prod(lead)):
                at, rest = [], flat
                for size in reversed(lead):
                    at.insert(0, rest % size)
                    rest //= size
                copy(src.at[tuple(at)], dst.at[tuple(at)], send, recv, to).start()

        def wait_send(self):
            copy(*self.args).wait_send()

        def wait_recv(self):
            copy(*self.args).wait_recv()

    def loop(count, body, hooks=()):
        def step(s, carry):
            body(s)
            for k, *todo in hooks:

                @pl.when(s == k)
                def _():
                    for f in todo:
                        f()

            return carry

        lax.fori_loop(0, count, step, 0)

    partners = [device(z_=z_at(k)) for k in range(1, zs)]
    partners += [device(x_=1 - x), device(y_=1 - y), device(c_=1 - c), device(c_=1 - c, y_=1 - y)]
    barrier = pltpu.get_barrier_semaphore()
    for partner in partners:
        pl.semaphore_signal(barrier, inc=1, device_id=partner, device_id_type=MESH)
    pl.semaphore_wait(barrier, len(partners))

    def ag_sems(n, slot):
        return ag_send.at[n.order, slot], ag_recv.at[n.order, slot]

    def group(n, u, long_off, mid_off, cut=None):
        yy = y if (long_off if n.long_axis == "y" else mid_off) == 0 else 1 - y
        xx = x if (long_off if n.long_axis == "x" else mid_off) == 0 else 1 - x
        return u.at[c, yy, xx] if cut is None else u.at[c, yy, xx, cut]

    def partner_of(n, step):
        axis = n.long_axis if step == "long" else {"x": "y", "y": "x"}[n.long_axis]
        return device(x_=1 - x) if axis == "x" else device(y_=1 - y)

    LINE, MID, LONG, LAST, CORE = 0, zs - 1, 2 * zs - 1, 3 * zs - 1, 3 * zs

    def ag_line(n, k, landed=False):
        ref = group(n, n.u, 0, 0, z_at(zs - k) if landed else z)
        return copy(ref, ref, *ag_sems(n, LINE + k - 1), device(z_=z_at(k)))

    def ag_first(n, step, k, landed=False):
        cut = z_at(zs - k) if n.fine else None
        off = (0, 1) if step == "mid" else (1, 0)
        ref = group(n, n.u, *(off if landed else (0, 0)), cut)
        return Spread(ref, ref, *ag_sems(n, (MID if step == "mid" else LONG) + k), partner_of(n, step))

    def ag_last(n, landed=False):
        ref = group(n, n.u, 1 if landed else 0, 1)
        return Spread(ref, ref, *ag_sems(n, LAST), partner_of(n, "long"))

    def ag_core(n, long_off, mid_off, landed=False):
        ref = group(n, n.u, long_off, mid_off)
        if landed:
            yy = y if (long_off if n.long_axis == "y" else mid_off) == 0 else 1 - y
            xx = x if (long_off if n.long_axis == "x" else mid_off) == 0 else 1 - x
            ref = n.u.at[1 - c, yy, xx]
        return Spread(ref, ref, *ag_sems(n, CORE + 2 * long_off + mid_off), device(c_=1 - c))

    def parts(n):
        return range(zs) if n.fine else range(1)

    def ag_start(n):
        if n.fine:
            for step in ("mid", "long"):
                ag_first(n, step, 0).start()
        for k in range(1, zs):
            ag_line(n, k).start()

    def ag_piece(n, k):
        ag_line(n, k, True).wait_recv()
        for step in ("mid", "long"):
            ag_first(n, step, k).start()

    def ag_one(n):
        if not n.fine:
            for k in range(1, zs):
                ag_line(n, k, True).wait_recv()
            for step in ("mid", "long"):
                ag_first(n, step, 0).start()
        ag_core(n, 0, 0).start()

    def ag_two(n):
        for k in parts(n):
            ag_first(n, "mid", k, True).wait_recv()
        ag_last(n).start()
        ag_core(n, 0, 1).start()

    def ag_three(n):
        for k in parts(n):
            ag_first(n, "long", k, True).wait_recv()
        ag_core(n, 1, 0).start()

    def ag_four(n):
        ag_last(n, True).wait_recv()
        ag_core(n, 1, 1).start()

    def ag_done(n):
        for off in ((0, 0), (0, 1), (1, 0), (1, 1)):
            ag_core(n, *off, True).wait_recv()
        for k in range(1, zs):
            ag_line(n, k).wait_send()
        for step in ("mid", "long"):
            for k in parts(n):
                ag_first(n, step, k).wait_send()
        ag_last(n).wait_send()
        for off in ((0, 0), (0, 1), (1, 0), (1, 1)):
            ag_core(n, *off).wait_send()

    def rs_sems(n, slot):
        return rs_send.at[n.order, slot], rs_recv.at[n.order, slot]

    def cut_of(n):
        return slice(None) if n.count == zs else pl.ds(n.first, n.count)

    def rs_core(n, long_off):
        place = 1 - (y if n.long_axis == "y" else x) if long_off else (y if n.long_axis == "y" else x)
        where = (place, slice(None)) if n.long_axis == "y" else (slice(None), place)
        return Spread(n.u.at[(1 - c,) + where + (cut_of(n),)], n.core_in.at[where],
                      *rs_sems(n, long_off), device(c_=1 - c))

    def rs_long(n):
        where = (1 - y, slice(None)) if n.long_axis == "y" else (slice(None), 1 - x)
        return Spread(n.u.at[(c,) + where + (cut_of(n),)], n.long_in, *rs_sems(n, 2), partner_of(n, "long"))

    def rs_mid(n):
        return Spread(group(n, n.u, 0, 1, cut_of(n)), n.mid_in, *rs_sems(n, 3), partner_of(n, "mid"))

    def rs_line(n, k):
        return copy(group(n, n.u, 0, 0, z_at(k)), n.line_in.at[k - 1], *rs_sems(n, 3 + k), device(z_=z_at(k)))

    def within(n, place):
        return jnp.logical_and(place >= n.first, place < n.first + n.count)

    def when_within(n, place, f):
        if n.whole:
            f()
        else:
            pl.when(within(n, place))(f)

    def gather_terms(n, long_off, mid_off, names):
        yy = y if (long_off if n.long_axis == "y" else mid_off) == 0 else 1 - y
        xx = x if (long_off if n.long_axis == "x" else mid_off) == 0 else 1 - x

        def body(s):
            mine = n.u.at[c, yy, xx, n.first + s]
            value = mine[...].astype(F32) + n.core_in[yy, xx, s].astype(F32)
            if "long" in names:
                value = value + n.long_in[xx if n.long_axis == "y" else yy, s].astype(F32)
            if "mid" in names:
                value = value + n.mid_in[s].astype(F32)
            mine[...] = value.astype(BF16)

        loop(n.count, body)

    def rs_zero(n):
        rs_core(n, 1).start()
        rs_core(n, 0).start()

    def rs_one(n):
        rs_core(n, 1).wait_recv()
        gather_terms(n, 1, 0, ())
        gather_terms(n, 1, 1, ())
        rs_long(n).start()

    def rs_two(n):
        rs_core(n, 0).wait_recv()
        rs_long(n).wait_recv()
        gather_terms(n, 0, 1, ("long",))
        rs_mid(n).start()

    def rs_three(n):
        rs_mid(n).wait_recv()
        gather_terms(n, 0, 0, ("long", "mid"))
        for k in range(1, zs):
            when_within(n, z_at(k), lambda k=k: rs_line(n, k).start())

    def rs_done(n):
        def finish():
            for k in range(1, zs):
                rs_line(n, k).wait_recv()
            value = n.u[c, y, x, z].astype(F32)
            for k in range(1, zs):
                value = value + n.line_in[k - 1].astype(F32)
            n.finish(value)

        when_within(n, z, finish)
        for moved in (rs_core(n, 0), rs_core(n, 1), rs_long(n), rs_mid(n)):
            moved.wait_send()
        for k in range(1, zs):
            when_within(n, z_at(k), lambda k=k: rs_line(n, k).wait_send())

    def small_sum(ref, slots, which):
        to = (device(y_=1 - y), device(c_=1 - c), device(x_=1 - x))
        to += tuple(device(z_=z_at(k)) for k in range(1, zs))

        def moved(slot):
            return copy(ref, slots.at[slot], v_send.at[which, slot], v_recv.at[which, slot], to[slot])

        def land(last):
            moved(last).wait()
            ref[...] = ref[...] + slots[last]

        def step(n):
            def run():
                if n > 0:
                    land(n - 1)
                moved(n).start()

            return run

        def line():
            land(2)
            for k in range(1, zs):
                moved(2 + k).start()

        def finish():
            for k in range(1, zs):
                moved(2 + k).wait()
            value = ref[...]
            for k in range(1, zs):
                value = value + slots[2 + k]
            ref[...] = value

        return [step(0), step(1), step(2), line, finish]

    def exchange(src, dst, which):
        return [copy(src.at[block_at(k)], dst.at[i], a2a_send.at[which, k - 1],
                     a2a_recv.at[which, k - 1], {"blk": block_at(k), "batch": b})
                for k in range(1, 4)]

    def exchange_landed(dst, which):
        return [copy(dst.at[block_at(4 - k)], dst.at[block_at(4 - k)], a2a_send.at[which, k - 1],
                     a2a_recv.at[which, k - 1], {"blk": block_at(4 - k), "batch": b})
                for k in range(1, 4)]

    units = [Unit(2 * n + half, ubuf.at[n, half], axes[half], n == 0)
             for n, axes in enumerate(("xy", "xy", "xx")) for half in range(2)]
    unit_qk, unit_vo, unit_w1, unit_w2 = units[0], units[1], units[2:4], units[4:6]

    def rest_rows(matrix):
        return a_in[matrix, pl.ds(pl.multiple_of(128 * (1 - c), 64), 64), :]

    def own_attention(p):
        mine = ubuf.at[0, p, c, y, x, z]
        for m in range(2):
            main = a_in[2 * p + m, pl.ds(pl.multiple_of(64 * c, 64), 128), :]
            mine[96 * m : 96 * m + 96, :] = main.T.astype(BF16)
        rest = jnp.concatenate([rest_rows(2 * p + c), rest_rows(2 * p + 1 - c)], axis=0)
        mine[192:288, :] = rest.T.astype(BF16)

    def own_feed_forward():
        for h in range(2):
            for t in range(3):
                ubuf[1, h, c, y, x, z, 96 * t : 96 * t + 96, :] = w1_in[
                    96 * h : 96 * h + 96, 128 * t : 128 * t + 128
                ].astype(BF16)
            for t in range(6):
                ubuf[2, h, c, y, x, z, 48 * t : 48 * t + 48, :] = w2_in[
                    48 * h : 48 * h + 48, 128 * t : 128 * t + 128
                ].astype(BF16)

    columns = a_in.shape[2]
    placed = lax.broadcasted_iota(jnp.int32, (columns, 768), 1) == (
        lax.broadcasted_iota(jnp.int32, (columns, 768), 0) + columns * g
    )

    def own_vectors():
        vec[...] = jnp.zeros_like(vec)
        rows = dot_nn(vec_in[...].astype(BF16), jnp.where(placed, 1.0, 0.0).astype(BF16))
        for j in range(3):
            vec[pl.ds(3 * i + j, 1), :] = rows[j : j + 1, :]

    def masked_cotangent():
        eye = lax.broadcasted_iota(jnp.int32, (128, 128), 0) == lax.broadcasted_iota(jnp.int32, (128, 128), 1)
        for s in range(4):
            row = jnp.broadcast_to(mask_in[s : s + 1, :].astype(F32), (128, 128))
            column = jnp.sum(jnp.where(eye, row, 0.0), axis=1, keepdims=True)
            stage[s] = (cot[s].astype(F32) * column).astype(BF16)

    def finish_attention(p):
        def finish(value):
            for m in range(2):
                ga[2 * p + m, pl.ds(pl.multiple_of(64 * c, 64), 128), :] = value[96 * m : 96 * m + 96, :].T
            rest = value[192:288, :].T
            rows = pl.ds(pl.multiple_of(128 * (1 - c), 64), 64)
            ga[2 * p + c, rows, :] = rest[0:64, :]
            ga[2 * p + 1 - c, rows, :] = rest[64:128, :]

        return finish

    def finish_expand(h):
        def finish(value):
            for t in range(3):
                g1[96 * h : 96 * h + 96, 128 * t : 128 * t + 128] = value[96 * t : 96 * t + 96, :]

        return finish

    def finish_reduce(h):
        def finish(value):
            for t in range(6):
                g2[48 * h : 48 * h + 48, 128 * t : 128 * t + 128] = value[48 * t : 48 * t + 48, :]

        return finish

    def finish_vectors():
        value, total = gvec[...], 0.0
        for _ in range(3):
            part = value.astype(BF16)
            total = total + dot_nt(part, jnp.where(placed, 1.0, 0.0).astype(BF16))
            value = value - part.astype(F32)
        narrow_rows[...] = total
        for j in range(3):
            gv[j : j + 1, :] = narrow_rows[pl.ds(3 * i + j, 1), :]

    grads = []
    half_zs = zs // 2
    for n, (source, finish, axes) in enumerate(((0, finish_reduce, "xx"), (2, finish_expand, "yx"))):
        for half in range(2):
            order = 2 * n + half
            grads.append(Gradient(order, ubuf.at[source, half], axes[half], 0, zs, True,
                                  core_in.at[order], long_in.at[order], mid_in.at[order],
                                  line_in.at[order], finish(half)))
    for part in range(2):
        for half in range(2):
            cut = pl.ds(part * half_zs, half_zs)
            grads.append(Gradient(4 + 2 * part + half, ubuf.at[1, half], "xy"[half], part * half_zs, half_zs,
                                  False, core_in.at[4 + half, :, :, cut], long_in.at[4 + half, :, cut],
                                  mid_in.at[4 + half, cut], line_in.at[4 + half], finish_attention(half)))
    grad_w2, grad_w1, grad_a = grads[0:2], grads[2:4], (grads[4:6], grads[6:8])

    def each(f, which):
        def run():
            for n in which:
                f(n)

        return run

    own_attention(0)
    ag_start(unit_qk)
    own_vectors()
    vec_steps = small_sum(vec, vin, 0)
    vec_steps[0]()
    own_tokens = pltpu.make_async_copy(tok.at[i], x_in.at[i], local_sem.at[0])
    own_tokens.start()
    tokens_out = exchange(tok, x_in, 0)
    for moved in tokens_out:
        moved.start()
    own_attention(1)
    own_feed_forward()
    for k in range(1, zs):
        ag_piece(unit_qk, k)
    ag_one(unit_qk)
    ag_start(unit_vo)
    ag_start(unit_w1[0])
    vec_steps[1]()
    masked_cotangent()
    ag_two(unit_qk)
    vec_steps[2]()
    for k in range(1, zs):
        ag_piece(unit_vo, k)
    ag_one(unit_vo)
    ag_start(unit_w1[1])
    vec_steps[3]()
    ag_three(unit_qk)

    for moved in exchange_landed(x_in, 0):
        moved.wait_recv()
    own_tokens.wait()
    vec_steps[4]()

    def normalise(value):
        centered = value - jnp.mean(value, axis=-1, keepdims=True)
        scale = lax.rsqrt(jnp.mean(centered * centered, axis=-1, keepdims=True) + norm_epsilon)
        return centered * scale, scale

    def rows_of(s):
        return pl.ds(pl.multiple_of(s * 128, 128), 128)

    def first_norm(s):
        unit, _ = normalise(x_in[s].astype(F32))
        n1[rows_of(s), :] = (unit * vec[0:1, :] + vec[1:2, :]).astype(BF16)

    loop(4, first_norm)
    ag_four(unit_qk)
    own_cot = pltpu.make_async_copy(stage.at[i], cot_in.at[i], local_sem.at[1])
    own_cot.start()
    cot_out = exchange(stage, cot_in, 1)
    for moved in cot_out:
        moved.start()
    ag_done(unit_qk)

    lanes = lax.broadcasted_iota(jnp.int32, (96, 128), 1)

    def unpack(p, s):
        for xx in range(2):
            rows = pl.ds(pl.multiple_of((2 * s + xx) * 96, 96), 96)
            for yy in range(2):
                first, second = ubuf.at[0, p, 0, yy, xx, s], ubuf.at[0, p, 1, yy, xx, s]
                lo, hi = 384 * yy, 384 * yy + 256
                for m in range(2):
                    at[2 * p + m, rows, lo : lo + 128] = first[96 * m : 96 * m + 96, :]
                    at[2 * p + m, rows, hi : hi + 128] = second[96 * m : 96 * m + 96, :]
                rest_first = first[192:288, :].astype(F32)
                rest_second = second[192:288, :].astype(F32)
                even = jnp.where(lanes < 64, rest_first, rest_second)
                odd = pltpu.roll(jnp.where(lanes < 64, rest_second, rest_first), 64, 1)
                at[2 * p, rows, lo + 128 : lo + 256] = even.astype(BF16)
                at[2 * p + 1, rows, lo + 128 : lo + 256] = odd.astype(BF16)

    def project(m, dst, bias):
        for n in range(3):
            value = dot_nt(n1[...], at[m, 256 * n : 256 * n + 256, :])
            if bias is not None:
                value = value + vec[bias : bias + 1, 256 * n : 256 * n + 256]
            value = value.astype(BF16)
            if m == 0:
                value = value * jnp.asarray(HEAD ** (-0.5), BF16)
            dst[2 * n] = value[:, 0:128]
            dst[2 * n + 1] = value[:, 128:256]

    loop(zs, functools.partial(unpack, 0))
    project(0, q6, 2)
    ag_two(unit_vo)
    project(1, k6, None)
    ag_one(unit_w1[0])

    half_lane = lax.broadcasted_iota(jnp.int32, (512, 128), 1) // HEAD

    def half_of(value, which):
        return jnp.where(half_lane == which, value, jnp.zeros_like(value))

    def turn(value):
        return value.astype(F32).T.astype(BF16)

    def attend(p):
        queries, keys = q6[p], k6[p]
        for which in range(2):
            scores = dot_nt(half_of(keys, which), queries)
            expo = jnp.exp(scores - jnp.max(scores, axis=0, keepdims=True))
            probs = (expo * (1.0 / jnp.sum(expo, axis=0, keepdims=True))).astype(BF16)
            pt[2 * p + which] = probs

    def mix(p):
        values_t = turn(v6[p])
        mixed = [dot_nn(values_t[64 * which : 64 * which + 64, :], pt[2 * p + which]) for which in range(2)]
        o6[p] = jnp.concatenate(mixed, axis=0).T.astype(BF16)

    loop(6, attend, (
        (1, lambda: ag_three(unit_vo)),
        (2, lambda: ag_one(unit_w1[1]), each(ag_start, unit_w2)),
        (3, lambda: ag_four(unit_vo), lambda: ag_two(unit_w1[0])),
    ))
    ag_two(unit_w1[1])
    ag_done(unit_vo)
    loop(zs, functools.partial(unpack, 1))
    project(2, v6, 3)
    each(ag_three, unit_w1)()
    loop(6, mix, (
        (1, lambda: ag_one(unit_w2[0])),
        (3, each(ag_four, unit_w1), lambda: ag_one(unit_w2[1])),
        (5, lambda: ag_two(unit_w2[0])),
    ))

    for n in range(3):
        cols = slice(256 * n, 256 * n + 256)
        value = dot_nt(lane_tiles(o6), at[3, cols, :]) + vec[4:5, cols]
        for s in range(4):
            h1[128 * s : 128 * s + 128, cols] = x_in[s, :, cols].astype(F32) + value[128 * s : 128 * s + 128]

    def second_norm(s):
        unit, _ = normalise(h1[rows_of(s), :])
        n2[rows_of(s), :] = (unit * vec[5:6, :] + vec[6:7, :]).astype(BF16)

    loop(4, second_norm)
    each(ag_done, unit_w1)()
    ag_two(unit_w2[1])

    def expand_piece(s, xx):
        def piece(ref):
            return jnp.concatenate([ref[96 * t : 96 * t + 96, :] for t in range(3)], axis=1)

        return jnp.concatenate(
            [piece(ubuf.at[1, h, cc, yy, xx, s]) for yy in range(2) for cc in range(2) for h in range(2)],
            axis=0,
        )

    def reduce_block(s):
        yy, cc = lax.div(s, 2), lax.rem(s, 2)

        def piece(ref):
            return jnp.concatenate([ref[48 * t : 48 * t + 48, :] for t in range(6)], axis=1)

        return jnp.concatenate(
            [piece(ubuf.at[2, h, cc, yy, xx, zz]) for zz in range(zs) for xx in range(2) for h in range(2)],
            axis=0,
        )

    def block_rows(s):
        return pl.ds(pl.multiple_of(s * 512, 512), 512)

    def expand(s):
        for xx in range(2):
            cols = slice(384 * xx, 384 * xx + 384)
            inner = dot_nn(n2[...], expand_piece(s, xx)) + vec[pl.ds(8 + s, 1), cols]
            square = inner * inner
            tanh = jnp.tanh(GELU_SCALE * inner * (1.0 + GELU_CUBE * square))
            act[block_rows(s), cols] = (0.5 * inner * (1.0 + tanh)).astype(BF16)
            slope = 0.5 * (1.0 + tanh) + 0.5 * inner * (1.0 - tanh * tanh) * (
                GELU_SCALE * (1.0 + 3.0 * GELU_CUBE * square)
            )
            gp[block_rows(s), cols] = slope.astype(BF16)

    loop(4, expand, (
        (1, each(ag_three, unit_w2)),
        (3, lambda: ag_four(unit_w2[0])),
    ))

    for moved in exchange_landed(cot_in, 1):
        moved.wait_recv()
    own_cot.wait()
    gvec[...] = jnp.zeros_like(gvec)

    def transpose_rows(dst, s, value):
        dst[:, 128 * s : 128 * s + 128] = turn(value)

    total = jnp.zeros((1, 768), F32)
    for s in range(4):
        transpose_rows(ta, s, cot_in[s])
        total = total + jnp.sum(cot_in[s].astype(F32), axis=0, keepdims=True)
    gvec[7:8, :] = total

    def reduce_back(s):
        yy, cc = lax.div(s, 2), lax.rem(s, 2)
        grad = dot_nn(ta[...], act[block_rows(s), :]).astype(BF16)
        for zz in range(zs):
            for xx in range(2):
                for h in range(2):
                    row = 96 * (2 * zz + xx) + 48 * h
                    for t in range(6):
                        ubuf[0, h, cc, yy, xx, zz, 48 * t : 48 * t + 48, :] = grad[
                            row : row + 48, 128 * t : 128 * t + 128
                        ]

    loop(4, reduce_back)
    each(rs_zero, grad_w2)()
    ag_four(unit_w2[1])
    each(rs_one, grad_w2)()
    each(ag_done, unit_w2)()

    def cotangent_rows():
        return jnp.concatenate([cot_in[s] for s in range(4)], axis=0)

    def inner_back(s):
        grad = dot_nn(cotangent_rows(), reduce_block(s)) * gp[block_rows(s), :].astype(F32)
        low = grad.astype(BF16)
        gp[block_rows(s), :] = low
        gvec[pl.ds(8 + s, 1), :] = jnp.sum(low.astype(F32), axis=0, keepdims=True)

    loop(4, inner_back)

    acc[...] = h1[...] + vec[7:8, :]

    def reduce(s):
        acc[...] += dot_nt(act[block_rows(s), :], reduce_block(s))

    loop(4, reduce)
    for moved in cot_out:
        moved.wait_send()
    for s in range(4):
        stage[s] = acc[128 * s : 128 * s + 128, :].astype(BF16)
    own_out = pltpu.make_async_copy(stage.at[i], out.at[i], local_sem.at[2])
    own_out.start()
    result_out = exchange(stage, out, 2)
    for moved in result_out:
        moved.start()

    for s in range(4):
        transpose_rows(tb, s, n2[128 * s : 128 * s + 128, :])

    def expand_back(s):
        for xx in range(2):
            grad = dot_nn(tb[...], gp[block_rows(s), 384 * xx : 384 * xx + 384]).astype(BF16)
            for yy in range(2):
                for cc in range(2):
                    for h in range(2):
                        row = 192 * (2 * yy + cc) + 96 * h
                        for t in range(3):
                            ubuf[2, h, cc, yy, xx, s, 96 * t : 96 * t + 96, :] = grad[
                                row : row + 96, 128 * t : 128 * t + 128
                            ]

    loop(4, expand_back)
    each(rs_zero, grad_w1)()
    each(rs_two, grad_w2)()

    def norm_back(s):
        whole = jnp.concatenate([expand_piece(s, 0), expand_piece(s, 1)], axis=1)
        part = dot_nt(gp[block_rows(s), :], whole)

        @pl.when(s == 0)
        def _():
            acc[...] = part

        @pl.when(s > 0)
        def _():
            acc[...] += part

    loop(4, norm_back, ((1, each(rs_one, grad_w1)),))

    def norm_gradient(value, scale_row, grad):
        unit, scale = normalise(value)
        gain_sum = jnp.sum(grad * unit, axis=0, keepdims=True)
        bias_sum = jnp.sum(grad, axis=0, keepdims=True)
        inner = grad * scale_row
        mean = jnp.mean(inner, axis=-1, keepdims=True)
        along = jnp.mean(inner * unit, axis=-1, keepdims=True)
        return scale * (inner - mean - unit * along), gain_sum, bias_sum

    def hidden_back(s):
        rows = rows_of(s)
        grad, gain_sum, bias_sum = norm_gradient(h1[rows, :], vec[5:6, :], acc[rows, :])
        grad = grad + cot_in[s].astype(F32)
        h1[rows, :] = grad
        low = grad.astype(BF16)
        n2[rows, :] = low
        gvec[5:6, :] += gain_sum
        gvec[6:7, :] += bias_sum
        gvec[4:5, :] += jnp.sum(low.astype(F32), axis=0, keepdims=True)

    loop(4, hidden_back)

    for n in range(3):
        value = dot_nn(n2[...], at[3, :, 256 * n : 256 * n + 256]).astype(BF16)
        d6[2 * n] = value[:, 0:128]
        d6[2 * n + 1] = value[:, 128:256]
    for s in range(4):
        transpose_rows(tc, s, n2[128 * s : 128 * s + 128, :])
    act[768:1536, :] = dot_nn(tc[...], lane_tiles(o6)).astype(BF16)
    each(rs_three, grad_w2)()

    def attend_back(p):
        rows = rows_of(p)
        queries, keys, values, grads_in = q6[p], k6[p], v6[p], d6[p]
        keys_t = turn(keys)
        grad_query, grad_key, grad_value = [], 0.0, 0.0
        for which in range(2):
            probs = pt[2 * p + which]
            wide = probs.astype(F32)
            grad_probs = dot_nt(half_of(values, which), grads_in)
            inner = jnp.sum(wide * grad_probs, axis=0, keepdims=True)
            grad_scores = (wide * (grad_probs - inner)).astype(BF16)
            grad_query.append(dot_nn(keys_t[64 * which : 64 * which + 64, :], grad_scores))
            grad_key = grad_key + dot_nn(grad_scores, half_of(queries, which))
            grad_value = grad_value + dot_nn(probs, half_of(grads_in, which))
        grad_query = jnp.concatenate(grad_query, axis=0) * HEAD ** (-0.5)
        ta[rows, :] = grad_query.astype(BF16)
        tb[rows, :] = grad_key.T.astype(BF16)
        tc[rows, :] = grad_value.T.astype(BF16)
        q6[p] = grad_query.T.astype(BF16)
        k6[p] = grad_key.astype(BF16)
        v6[p] = grad_value.astype(BF16)

    def pack(p, part, first_row, second_row):
        def body(s):
            for xx in range(2):
                offset = (2 * s + xx) * 96
                rows = [pl.ds(pl.multiple_of(first_row + offset, 96), 96),
                        pl.ds(pl.multiple_of(second_row + offset, 96), 96)]
                first = ubuf.at[1, p, 0, :, xx, part * half_zs + s]
                second = ubuf.at[1, p, 1, :, xx, part * half_zs + s]
                for yy in range(2):
                    lo, mid, hi = 384 * yy, 384 * yy + 128, 384 * yy + 256
                    for m in range(2):
                        first[yy, 96 * m : 96 * m + 96, :] = act[rows[m], lo : lo + 128]
                        second[yy, 96 * m : 96 * m + 96, :] = act[rows[m], hi : hi + 128]
                    even = act[rows[0], mid : mid + 128].astype(F32)
                    odd = pltpu.roll(act[rows[1], mid : mid + 128].astype(F32), 64, 1)
                    first[yy, 192:288, :] = jnp.where(lanes < 64, even, odd).astype(BF16)
                    second[yy, 192:288, :] = jnp.where(lanes < 64, odd, even).astype(BF16)

        loop(half_zs, body)

    def attention_gradients(part):
        rows = slice(384 * part, 384 * part + 384)
        act[1536:1920, :] = dot_nn(tc[rows, :], n1[...]).astype(BF16)
        pack(1, part, 1536, 768 + 384 * part)
        rs_zero(grad_a[part][1])
        act[0:384, :] = dot_nn(ta[rows, :], n1[...]).astype(BF16)
        act[384:768, :] = dot_nn(tb[rows, :], n1[...]).astype(BF16)
        pack(0, part, 0, 384)
        rs_zero(grad_a[part][0])

    loop(3, attend_back, ((0, each(rs_two, grad_w1)), (1, each(rs_done, grad_w2))))
    attention_gradients(0)
    loop(3, lambda p: attend_back(p + 3), (
        (0, each(rs_one, grad_a[0])),
        (1, each(rs_three, grad_w1)),
        (2, each(rs_two, grad_a[0])),
    ))
    attention_gradients(1)
    each(rs_one, grad_a[1])()
    each(rs_done, grad_w1)()

    acc[...] = dot_nn(lane_tiles(q6), at[0])
    acc[...] += dot_nn(lane_tiles(k6), at[1])
    acc[...] += dot_nn(lane_tiles(v6), at[2])
    gvec[2:3, :] = jnp.sum(lane_tiles(q6).astype(F32), axis=0, keepdims=True)
    gvec[3:4, :] = jnp.sum(lane_tiles(v6).astype(F32), axis=0, keepdims=True)
    each(rs_three, grad_a[0])()

    for moved in result_out:
        moved.wait_send()
    own_out.wait()

    def input_back(s):
        rows = rows_of(s)
        grad, gain_sum, bias_sum = norm_gradient(x_in[s].astype(F32), vec[0:1, :], acc[rows, :])
        stage[s] = (grad + h1[rows, :]).astype(BF16)
        gvec[0:1, :] += gain_sum
        gvec[1:2, :] += bias_sum

    loop(4, input_back)
    gvec_steps = small_sum(gvec, gin, 1)
    gvec_steps[0]()
    own_grad = pltpu.make_async_copy(stage.at[i], ig.at[i], local_sem.at[3])
    own_grad.start()
    grad_out = exchange(stage, ig, 3)
    for moved in grad_out:
        moved.start()

    gvec_steps[1]()
    each(rs_two, grad_a[1])()
    gvec_steps[2]()
    each(rs_done, grad_a[0])()
    gvec_steps[3]()
    each(rs_three, grad_a[1])()
    gvec_steps[4]()
    finish_vectors()
    each(rs_done, grad_a[1])()

    own_grad.wait()
    for moved in tokens_out + grad_out:
        moved.wait_send()
    for moved in exchange_landed(out, 2) + exchange_landed(ig, 3):
        moved.wait_recv()


def layer(sub, tokens, cotangent, span_mask, vectors, attention, expand, reduce_t):
    zs = GROUPS // 2
    seqs, block, width = tokens.shape
    rows = seqs * block
    columns = attention.shape[2]
    piece = (3 * columns, 128)
    vmem = lambda shape, dtype: pltpu.VMEM(shape, dtype)
    scratch = [vmem((3, 2, 2, 2, 2, zs) + piece, BF16)]
    scratch += [vmem((6, 2, 2, zs) + piece, BF16), vmem((6, 2, zs) + piece, BF16)]
    scratch += [vmem((6, zs) + piece, BF16), vmem((6, zs - 1) + piece, BF16)]
    scratch += [vmem(tokens.shape, BF16)] * 3
    scratch += [vmem((16, width), F32)] * 2
    scratch += [vmem((zs + 2, 16, width), F32)] * 2
    scratch += [vmem((16, columns), F32)]
    tiles = vmem((width // 128, rows, 128), BF16)
    flat = vmem((rows, width), BF16)
    turned = vmem((width, rows), BF16)
    scratch += [vmem((4, width, width), BF16), flat, tiles, tiles, tiles, tiles]
    scratch += [vmem((HEADS, rows, rows), BF16), vmem((rows, width), F32), vmem((rows, width), F32)]
    scratch += [flat, vmem((4 * rows, width), BF16), vmem((4 * rows, width), BF16)]
    scratch += [turned, turned, turned, tiles]
    scratch += [pltpu.SemaphoreType.DMA((4,))]
    scratch += [pltpu.SemaphoreType.DMA((6, 3 * zs + 4))] * 2
    scratch += [pltpu.SemaphoreType.DMA((8, zs + 3))] * 2
    scratch += [pltpu.SemaphoreType.DMA((4, 3))] * 2
    scratch += [pltpu.SemaphoreType.DMA((2, zs + 2))] * 2
    in_vmem = pl.BlockSpec(memory_space=pltpu.VMEM)
    anywhere = pl.BlockSpec(memory_space=pl.ANY)
    return pl.pallas_call(
        functools.partial(kernel, sub, zs),
        out_shape=(
            jax.ShapeDtypeStruct(tokens.shape, BF16),
            jax.ShapeDtypeStruct(tokens.shape, BF16),
            jax.ShapeDtypeStruct(attention.shape, F32),
            jax.ShapeDtypeStruct(expand.shape, F32),
            jax.ShapeDtypeStruct(reduce_t.shape, F32),
            jax.ShapeDtypeStruct(vectors.shape, F32),
        ),
        in_specs=[anywhere] + [in_vmem] * 6,
        out_specs=(anywhere, anywhere) + (in_vmem,) * 4,
        scratch_shapes=scratch,
        compiler_params=pltpu.CompilerParams(
            collective_id=0, has_side_effects=True, vmem_limit_bytes=63 * 1024 * 1024
        ),
    )(tokens, cotangent, span_mask, vectors, attention, expand, reduce_t)


def update_kernel(rates, *refs):
    count = len(rates)
    ins, (result, grad) = refs[: 4 * count], refs[4 * count : 4 * count + 2]
    outs, (result_out, grad_out) = refs[4 * count + 2 : 7 * count + 2], refs[7 * count + 2 : 7 * count + 4]
    held, (low, wide, passed) = refs[7 * count + 4 : 11 * count + 4], refs[11 * count + 4 : 11 * count + 7]
    in_sems, out_sems = refs[11 * count + 7 :]
    loads = [pltpu.make_async_copy(ins[n], held[n], in_sems.at[n]) for n in range(4 * count)]
    stores = [pltpu.make_async_copy(held[4 * n + m], outs[3 * n + m], out_sems.at[3 * n + m])
              for n in range(count) for m in range(3)]
    load_grad = pltpu.make_async_copy(grad, low, in_sems.at[4 * count])
    store_grad = pltpu.make_async_copy(wide, grad_out, out_sems.at[3 * count])
    load_result = pltpu.make_async_copy(result, passed, in_sems.at[4 * count + 1])
    store_result = pltpu.make_async_copy(passed, result_out, out_sems.at[3 * count + 1])
    load_grad.start()
    load_result.start()
    for copy in loads:
        copy.start()
    load_result.wait()
    store_result.start()
    load_grad.wait()

    def widen(s, carry):
        wide[s] = low[s].astype(F32)
        return carry

    lax.fori_loop(0, low.shape[0], widen, 0)
    store_grad.start()
    for n in range(count):
        for m in range(4):
            loads[4 * n + m].wait()
        weight, one, two, gradient = held[4 * n : 4 * n + 4]
        values = adamw(weight[...], one[...], two[...], gradient[...], rates[n])
        for ref, value in zip((weight, one, two), values):
            ref[...] = value
        for m in range(3):
            stores[3 * n + m].start()
    for copy in stores + [store_grad, store_result]:
        copy.wait()


def update(rates, arrays, result, grad):
    flat = [value for group in arrays for value in group]
    new = [jax.ShapeDtypeStruct(value.shape, F32) for group in arrays for value in group[:3]]
    new += [jax.ShapeDtypeStruct(result.shape, BF16), jax.ShapeDtypeStruct(grad.shape, F32)]
    anywhere = pl.BlockSpec(memory_space=pl.ANY)
    scratch = [pltpu.VMEM(value.shape, F32) for value in flat]
    scratch += [pltpu.VMEM(grad.shape, BF16), pltpu.VMEM(grad.shape, F32), pltpu.VMEM(result.shape, BF16)]
    scratch += [pltpu.SemaphoreType.DMA((len(flat) + 2,)), pltpu.SemaphoreType.DMA((len(new),))]
    return pl.pallas_call(
        functools.partial(update_kernel, rates),
        out_shape=tuple(new),
        in_specs=[anywhere] * (len(flat) + 2),
        out_specs=(anywhere,) * len(new),
        scratch_shapes=scratch,
        compiler_params=pltpu.CompilerParams(vmem_limit_bytes=63 * 1024 * 1024),
    )(*flat, result, grad)


def local(
    sub,
    tokens,
    cotangent,
    span_mask,
    attention_weight,
    expand_weight,
    reduce_weight,
    vectors,
    attention_first,
    attention_second,
    expand_first,
    expand_second,
    reduce_first,
    reduce_second,
    vector_first,
    vector_second,
):
    together = [[n * sub + m for m in range(sub)] for n in range(GROUPS)]

    def widen(value, axis):
        if sub == 1:
            return value
        low = lax.all_gather(
            value.astype(BF16), "batch", axis=axis, tiled=True, axis_index_groups=together
        )
        return low.astype(F32)

    def narrow(value, axis):
        if sub == 1:
            return value
        return lax.psum_scatter(
            value, "batch", scatter_dimension=axis, tiled=True, axis_index_groups=together
        )

    out_tokens, input_grad, ga, g1, g2, gv = layer(
        sub,
        tokens,
        cotangent,
        span_mask,
        widen(vectors, 1),
        widen(attention_weight, 2),
        widen(expand_weight, 1),
        widen(reduce_weight.T, 0),
    )
    arrays = (
        (attention_weight, attention_first, attention_second, narrow(ga, 2)),
        (expand_weight, expand_first, expand_second, narrow(g1, 1)),
        (reduce_weight.T, reduce_first.T, reduce_second.T, narrow(g2, 0)),
        (vectors, vector_first, vector_second, narrow(gv, 1)),
    )
    rates = (rate_attention, rate_expand, rate_reduce, rate_vector)
    new = update(rates, arrays, out_tokens, input_grad)
    return new[-2:] + new[0:6] + tuple(value.T for value in new[6:9]) + new[9:12]


def solution(mesh):
    sub = mesh.shape["batch"] // GROUPS
    sequences = P("batch", "blk", None)
    attention = P(None, "blk", "batch")
    matrix = P("blk", "batch")
    return jax.shard_map(
        functools.partial(local, sub),
        mesh=mesh,
        in_specs=(sequences, sequences, P("batch", "blk"), attention, matrix, matrix, matrix)
        + (attention,) * 2
        + (matrix,) * 6,
        out_specs=(sequences,) * 2 + (attention,) * 3 + (matrix,) * 9,
        check_vma=False,
    )
```

```python
import functools
import math

import jax
import jax.numpy as jnp
from jax import lax
from jax.experimental import pallas as pl
from jax.experimental.pallas import tpu as pltpu
from jax.sharding import PartitionSpec as P

HEADS = 12
HEAD = 64
STEP = 10
GROUPS = 8

norm_epsilon = 1e-05
beta_one = 0.9
beta_two = 0.999
adam_epsilon = 1e-08
decay_weight = 0.1
rate_attention = 0.05
rate_expand = 0.03
rate_reduce = 0.015
rate_vector = 0.4

F32 = jnp.float32
BF16 = jnp.bfloat16
MESH = pl.DeviceIdType.MESH
GELU_SCALE = math.sqrt(2.0 / math.pi)
GELU_CUBE = 0.044715


def adamw(weight, moment_one, moment_two, gradient, step_rate):
    moment_one = beta_one * moment_one + (1.0 - beta_one) * gradient
    moment_two = beta_two * moment_two + (1.0 - beta_two) * gradient * gradient
    corrected_one = moment_one / (1.0 - beta_one**STEP)
    corrected_two = moment_two / (1.0 - beta_two**STEP)
    updated = weight - step_rate * (
        corrected_one / (jnp.sqrt(corrected_two) + adam_epsilon) + decay_weight * weight
    )
    return (updated, moment_one, moment_two)


def dot_nn(left, right):
    return lax.dot_general(left, right, (((1,), (0,)), ((), ())), preferred_element_type=F32)


def dot_nt(left, right):
    return lax.dot_general(left, right, (((1,), (1,)), ((), ())), preferred_element_type=F32)


def lane_tiles(ref, count=6):
    return jnp.concatenate([ref[t] for t in range(count)], axis=1)


class Unit:
    def __init__(self, order, u, long_axis, fine):
        self.order, self.u, self.long_axis, self.fine = order, u, long_axis, fine


class Gradient:
    def __init__(self, order, u, long_axis, first, count, whole, core_in, long_in, mid_in, line_in, finish):
        self.order, self.long_axis, self.first, self.count, self.whole = order, long_axis, first, count, whole
        self.u, self.core_in, self.long_in, self.mid_in, self.line_in = u, core_in, long_in, mid_in, line_in
        self.finish = finish


def kernel(sub, zs, *refs):
    (tok, cot, mask_in, vec_in, a_in, w1_in, w2_in,
     out, ig, ga, g1, g2, gv,
     ubuf, core_in, long_in, mid_in, line_in,
     x_in, cot_in, stage, vec, gvec, vin, gin, narrow_rows,
     at, n1, q6, k6, v6, o6, pt, h1, acc, n2, act, gp, ta, tb, tc, d6,
     local_sem, ag_send, ag_recv, rs_send, rs_recv, a2a_send, a2a_recv, v_send, v_recv) = refs

    i = lax.axis_index("blk")
    b = lax.axis_index("batch")
    c, y = lax.rem(i, 2), lax.div(i, 2)
    g, r = lax.div(b, sub), lax.rem(b, sub)
    x, z = lax.rem(g, 2), lax.div(g, 2)

    def device(c_=c, y_=y, x_=x, z_=z):
        return {"blk": 2 * y_ + c_, "batch": (2 * z_ + x_) * sub + r}

    def z_at(k):
        return lax.rem(z + k, zs)

    def block_at(k):
        return lax.rem(i + k, 4)

    def copy(src, dst, send, recv, to):
        return pltpu.make_async_remote_copy(
            src_ref=src, dst_ref=dst, send_sem=send, recv_sem=recv, device_id=to, device_id_type=MESH
        )

    def loop(count, body, hooks=()):
        def step(s, carry):
            body(s)
            for k, *todo in hooks:

                @pl.when(s == k)
                def _():
                    for f in todo:
                        f()

            return carry

        lax.fori_loop(0, count, step, 0)

    partners = [device(z_=z_at(k)) for k in range(1, zs)]
    partners += [device(x_=1 - x), device(y_=1 - y), device(c_=1 - c), device(c_=1 - c, y_=1 - y)]
    barrier = pltpu.get_barrier_semaphore()
    for partner in partners:
        pl.semaphore_signal(barrier, inc=1, device_id=partner, device_id_type=MESH)
    pl.semaphore_wait(barrier, len(partners))

    def ag_sems(n, slot):
        return ag_send.at[n.order, slot], ag_recv.at[n.order, slot]

    def group(n, u, long_off, mid_off, cut=None):
        yy = y if (long_off if n.long_axis == "y" else mid_off) == 0 else 1 - y
        xx = x if (long_off if n.long_axis == "x" else mid_off) == 0 else 1 - x
        return u.at[c, yy, xx] if cut is None else u.at[c, yy, xx, cut]

    def partner_of(n, step):
        axis = n.long_axis if step == "long" else {"x": "y", "y": "x"}[n.long_axis]
        return device(x_=1 - x) if axis == "x" else device(y_=1 - y)

    LINE, MID, LONG, LAST, CORE = 0, zs - 1, 2 * zs - 1, 3 * zs - 1, 3 * zs

    def ag_line(n, k, landed=False):
        ref = group(n, n.u, 0, 0, z_at(zs - k) if landed else z)
        return copy(ref, ref, *ag_sems(n, LINE + k - 1), device(z_=z_at(k)))

    def ag_first(n, step, k, landed=False):
        cut = z_at(zs - k) if n.fine else None
        off = (0, 1) if step == "mid" else (1, 0)
        ref = group(n, n.u, *(off if landed else (0, 0)), cut)
        return copy(ref, ref, *ag_sems(n, (MID if step == "mid" else LONG) + k), partner_of(n, step))

    def ag_last(n, landed=False):
        ref = group(n, n.u, 1 if landed else 0, 1)
        return copy(ref, ref, *ag_sems(n, LAST), partner_of(n, "long"))

    def ag_core(n, long_off, mid_off, landed=False):
        ref = group(n, n.u, long_off, mid_off)
        if landed:
            yy = y if (long_off if n.long_axis == "y" else mid_off) == 0 else 1 - y
            xx = x if (long_off if n.long_axis == "x" else mid_off) == 0 else 1 - x
            ref = n.u.at[1 - c, yy, xx]
        return copy(ref, ref, *ag_sems(n, CORE + 2 * long_off + mid_off), device(c_=1 - c))

    def parts(n):
        return range(zs) if n.fine else range(1)

    def ag_start(n):
        if n.fine:
            for step in ("mid", "long"):
                ag_first(n, step, 0).start()
        for k in range(1, zs):
            ag_line(n, k).start()

    def ag_piece(n, k):
        ag_line(n, k, True).wait_recv()
        for step in ("mid", "long"):
            ag_first(n, step, k).start()

    def ag_one(n):
        if not n.fine:
            for k in range(1, zs):
                ag_line(n, k, True).wait_recv()
            for step in ("mid", "long"):
                ag_first(n, step, 0).start()
        ag_core(n, 0, 0).start()

    def ag_two(n):
        for k in parts(n):
            ag_first(n, "mid", k, True).wait_recv()
        ag_last(n).start()
        ag_core(n, 0, 1).start()

    def ag_three(n):
        for k in parts(n):
            ag_first(n, "long", k, True).wait_recv()
        ag_core(n, 1, 0).start()

    def ag_four(n):
        ag_last(n, True).wait_recv()
        ag_core(n, 1, 1).start()

    def ag_done(n):
        for off in ((0, 0), (0, 1), (1, 0), (1, 1)):
            ag_core(n, *off, True).wait_recv()
        for k in range(1, zs):
            ag_line(n, k).wait_send()
        for step in ("mid", "long"):
            for k in parts(n):
                ag_first(n, step, k).wait_send()
        ag_last(n).wait_send()
        for off in ((0, 0), (0, 1), (1, 0), (1, 1)):
            ag_core(n, *off).wait_send()

    def rs_sems(n, slot):
        return rs_send.at[n.order, slot], rs_recv.at[n.order, slot]

    def cut_of(n):
        return slice(None) if n.count == zs else pl.ds(n.first, n.count)

    def rs_core(n, long_off):
        place = 1 - (y if n.long_axis == "y" else x) if long_off else (y if n.long_axis == "y" else x)
        where = (place, slice(None)) if n.long_axis == "y" else (slice(None), place)
        return copy(n.u.at[(1 - c,) + where + (cut_of(n),)], n.core_in.at[where],
                    *rs_sems(n, long_off), device(c_=1 - c))

    def rs_long(n):
        where = (1 - y, slice(None)) if n.long_axis == "y" else (slice(None), 1 - x)
        return copy(n.u.at[(c,) + where + (cut_of(n),)], n.long_in, *rs_sems(n, 2), partner_of(n, "long"))

    def rs_mid(n):
        return copy(group(n, n.u, 0, 1, cut_of(n)), n.mid_in, *rs_sems(n, 3), partner_of(n, "mid"))

    def rs_line(n, k):
        return copy(group(n, n.u, 0, 0, z_at(k)), n.line_in.at[k - 1], *rs_sems(n, 3 + k), device(z_=z_at(k)))

    def within(n, place):
        return jnp.logical_and(place >= n.first, place < n.first + n.count)

    def when_within(n, place, f):
        if n.whole:
            f()
        else:
            pl.when(within(n, place))(f)

    def gather_terms(n, long_off, mid_off, names):
        yy = y if (long_off if n.long_axis == "y" else mid_off) == 0 else 1 - y
        xx = x if (long_off if n.long_axis == "x" else mid_off) == 0 else 1 - x

        def body(s):
            mine = n.u.at[c, yy, xx, n.first + s]
            value = mine[...].astype(F32) + n.core_in[yy, xx, s].astype(F32)
            if "long" in names:
                value = value + n.long_in[xx if n.long_axis == "y" else yy, s].astype(F32)
            if "mid" in names:
                value = value + n.mid_in[s].astype(F32)
            mine[...] = value.astype(BF16)

        loop(n.count, body)

    def rs_zero(n):
        rs_core(n, 1).start()
        rs_core(n, 0).start()

    def rs_one(n):
        rs_core(n, 1).wait_recv()
        gather_terms(n, 1, 0, ())
        gather_terms(n, 1, 1, ())
        rs_long(n).start()

    def rs_two(n):
        rs_core(n, 0).wait_recv()
        rs_long(n).wait_recv()
        gather_terms(n, 0, 1, ("long",))
        rs_mid(n).start()

    def rs_three(n):
        rs_mid(n).wait_recv()
        gather_terms(n, 0, 0, ("long", "mid"))
        for k in range(1, zs):
            when_within(n, z_at(k), lambda k=k: rs_line(n, k).start())

    def rs_done(n):
        def finish():
            for k in range(1, zs):
                rs_line(n, k).wait_recv()
            value = n.u[c, y, x, z].astype(F32)
            for k in range(1, zs):
                value = value + n.line_in[k - 1].astype(F32)
            n.finish(value)

        when_within(n, z, finish)
        for moved in (rs_core(n, 0), rs_core(n, 1), rs_long(n), rs_mid(n)):
            moved.wait_send()
        for k in range(1, zs):
            when_within(n, z_at(k), lambda k=k: rs_line(n, k).wait_send())

    def small_sum(ref, slots, which):
        to = (device(y_=1 - y), device(c_=1 - c), device(x_=1 - x))
        to += tuple(device(z_=z_at(k)) for k in range(1, zs))

        def moved(slot):
            return copy(ref, slots.at[slot], v_send.at[which, slot], v_recv.at[which, slot], to[slot])

        def land(last):
            moved(last).wait()
            ref[...] = ref[...] + slots[last]

        def step(n):
            def run():
                if n > 0:
                    land(n - 1)
                moved(n).start()

            return run

        def line():
            land(2)
            for k in range(1, zs):
                moved(2 + k).start()

        def finish():
            for k in range(1, zs):
                moved(2 + k).wait()
            value = ref[...]
            for k in range(1, zs):
                value = value + slots[2 + k]
            ref[...] = value

        return [step(0), step(1), step(2), line, finish]

    def exchange(src, dst, which):
        return [copy(src.at[block_at(k)], dst.at[i], a2a_send.at[which, k - 1],
                     a2a_recv.at[which, k - 1], {"blk": block_at(k), "batch": b})
                for k in range(1, 4)]

    def exchange_landed(dst, which):
        return [copy(dst.at[block_at(4 - k)], dst.at[block_at(4 - k)], a2a_send.at[which, k - 1],
                     a2a_recv.at[which, k - 1], {"blk": block_at(4 - k), "batch": b})
                for k in range(1, 4)]

    units = [Unit(2 * n + half, ubuf.at[n, half], axes[half], n == 0)
             for n, axes in enumerate(("xy", "xy", "xx")) for half in range(2)]
    unit_qk, unit_vo, unit_w1, unit_w2 = units[0], units[1], units[2:4], units[4:6]

    def rest_rows(matrix):
        return a_in[matrix, pl.ds(pl.multiple_of(128 * (1 - c), 64), 64), :]

    def own_attention(p):
        mine = ubuf.at[0, p, c, y, x, z]
        for m in range(2):
            main = a_in[2 * p + m, pl.ds(pl.multiple_of(64 * c, 64), 128), :]
            mine[96 * m : 96 * m + 96, :] = main.T.astype(BF16)
        rest = jnp.concatenate([rest_rows(2 * p + c), rest_rows(2 * p + 1 - c)], axis=0)
        mine[192:288, :] = rest.T.astype(BF16)

    def own_feed_forward():
        for h in range(2):
            for t in range(3):
                ubuf[1, h, c, y, x, z, 96 * t : 96 * t + 96, :] = w1_in[
                    96 * h : 96 * h + 96, 128 * t : 128 * t + 128
                ].astype(BF16)
            for t in range(6):
                ubuf[2, h, c, y, x, z, 48 * t : 48 * t + 48, :] = w2_in[
                    48 * h : 48 * h + 48, 128 * t : 128 * t + 128
                ].astype(BF16)

    columns = a_in.shape[2]
    placed = lax.broadcasted_iota(jnp.int32, (columns, 768), 1) == (
        lax.broadcasted_iota(jnp.int32, (columns, 768), 0) + columns * g
    )

    def own_vectors():
        vec[...] = jnp.zeros_like(vec)
        rows = dot_nn(vec_in[...].astype(BF16), jnp.where(placed, 1.0, 0.0).astype(BF16))
        for j in range(3):
            vec[pl.ds(3 * i + j, 1), :] = rows[j : j + 1, :]

    def masked_cotangent():
        eye = lax.broadcasted_iota(jnp.int32, (128, 128), 0) == lax.broadcasted_iota(jnp.int32, (128, 128), 1)
        for s in range(4):
            row = jnp.broadcast_to(mask_in[s : s + 1, :].astype(F32), (128, 128))
            column = jnp.sum(jnp.where(eye, row, 0.0), axis=1, keepdims=True)
            stage[s] = (cot[s].astype(F32) * column).astype(BF16)

    def finish_attention(p):
        def finish(value):
            for m in range(2):
                ga[2 * p + m, pl.ds(pl.multiple_of(64 * c, 64), 128), :] = value[96 * m : 96 * m + 96, :].T
            rest = value[192:288, :].T
            rows = pl.ds(pl.multiple_of(128 * (1 - c), 64), 64)
            ga[2 * p + c, rows, :] = rest[0:64, :]
            ga[2 * p + 1 - c, rows, :] = rest[64:128, :]

        return finish

    def finish_expand(h):
        def finish(value):
            for t in range(3):
                g1[96 * h : 96 * h + 96, 128 * t : 128 * t + 128] = value[96 * t : 96 * t + 96, :]

        return finish

    def finish_reduce(h):
        def finish(value):
            for t in range(6):
                g2[48 * h : 48 * h + 48, 128 * t : 128 * t + 128] = value[48 * t : 48 * t + 48, :]

        return finish

    def finish_vectors():
        value, total = gvec[...], 0.0
        for _ in range(3):
            part = value.astype(BF16)
            total = total + dot_nt(part, jnp.where(placed, 1.0, 0.0).astype(BF16))
            value = value - part.astype(F32)
        narrow_rows[...] = total
        for j in range(3):
            gv[j : j + 1, :] = narrow_rows[pl.ds(3 * i + j, 1), :]

    grads = []
    half_zs = zs // 2
    for n, (source, finish, axes) in enumerate(((0, finish_reduce, "xx"), (2, finish_expand, "yx"))):
        for half in range(2):
            order = 2 * n + half
            grads.append(Gradient(order, ubuf.at[source, half], axes[half], 0, zs, True,
                                  core_in.at[order], long_in.at[order], mid_in.at[order],
                                  line_in.at[order], finish(half)))
    for part in range(2):
        for half in range(2):
            cut = pl.ds(part * half_zs, half_zs)
            grads.append(Gradient(4 + 2 * part + half, ubuf.at[1, half], "xy"[half], part * half_zs, half_zs,
                                  False, core_in.at[4 + half, :, :, cut], long_in.at[4 + half, :, cut],
                                  mid_in.at[4 + half, cut], line_in.at[4 + half], finish_attention(half)))
    grad_w2, grad_w1, grad_a = grads[0:2], grads[2:4], (grads[4:6], grads[6:8])

    def each(f, which):
        def run():
            for n in which:
                f(n)

        return run

    own_attention(0)
    ag_start(unit_qk)
    own_vectors()
    vec_steps = small_sum(vec, vin, 0)
    vec_steps[0]()
    own_tokens = pltpu.make_async_copy(tok.at[i], x_in.at[i], local_sem.at[0])
    own_tokens.start()
    tokens_out = exchange(tok, x_in, 0)
    for moved in tokens_out:
        moved.start()
    own_attention(1)
    ag_start(unit_vo)
    own_feed_forward()
    each(ag_start, unit_w1 + unit_w2)()
    for k in range(1, zs):
        ag_piece(unit_qk, k)
    ag_one(unit_qk)
    vec_steps[1]()
    masked_cotangent()
    ag_two(unit_qk)
    vec_steps[2]()
    for k in range(1, zs):
        ag_piece(unit_vo, k)
    ag_one(unit_vo)
    vec_steps[3]()
    ag_three(unit_qk)

    for moved in exchange_landed(x_in, 0):
        moved.wait_recv()
    own_tokens.wait()
    vec_steps[4]()

    def normalise(value):
        centered = value - jnp.mean(value, axis=-1, keepdims=True)
        scale = lax.rsqrt(jnp.mean(centered * centered, axis=-1, keepdims=True) + norm_epsilon)
        return centered * scale, scale

    def rows_of(s):
        return pl.ds(pl.multiple_of(s * 128, 128), 128)

    def first_norm(s):
        unit, _ = normalise(x_in[s].astype(F32))
        n1[rows_of(s), :] = (unit * vec[0:1, :] + vec[1:2, :]).astype(BF16)

    loop(4, first_norm)
    ag_four(unit_qk)
    own_cot = pltpu.make_async_copy(stage.at[i], cot_in.at[i], local_sem.at[1])
    own_cot.start()
    cot_out = exchange(stage, cot_in, 1)
    for moved in cot_out:
        moved.start()
    ag_done(unit_qk)

    lanes = lax.broadcasted_iota(jnp.int32, (96, 128), 1)

    def unpack(p, s):
        for xx in range(2):
            rows = pl.ds(pl.multiple_of((2 * s + xx) * 96, 96), 96)
            for yy in range(2):
                first, second = ubuf.at[0, p, 0, yy, xx, s], ubuf.at[0, p, 1, yy, xx, s]
                lo, hi = 384 * yy, 384 * yy + 256
                for m in range(2):
                    at[2 * p + m, rows, lo : lo + 128] = first[96 * m : 96 * m + 96, :]
                    at[2 * p + m, rows, hi : hi + 128] = second[96 * m : 96 * m + 96, :]
                rest_first = first[192:288, :].astype(F32)
                rest_second = second[192:288, :].astype(F32)
                even = jnp.where(lanes < 64, rest_first, rest_second)
                odd = pltpu.roll(jnp.where(lanes < 64, rest_second, rest_first), 64, 1)
                at[2 * p, rows, lo + 128 : lo + 256] = even.astype(BF16)
                at[2 * p + 1, rows, lo + 128 : lo + 256] = odd.astype(BF16)

    def project(m, dst, bias):
        for n in range(3):
            value = dot_nt(n1[...], at[m, 256 * n : 256 * n + 256, :])
            if bias is not None:
                value = value + vec[bias : bias + 1, 256 * n : 256 * n + 256]
            value = value.astype(BF16)
            if m == 0:
                value = value * jnp.asarray(HEAD ** (-0.5), BF16)
            dst[2 * n] = value[:, 0:128]
            dst[2 * n + 1] = value[:, 128:256]

    loop(zs, functools.partial(unpack, 0))
    project(0, q6, 2)
    ag_two(unit_vo)
    project(1, k6, None)
    ag_one(unit_w1[0])

    half_lane = lax.broadcasted_iota(jnp.int32, (512, 128), 1) // HEAD

    def half_of(value, which):
        return jnp.where(half_lane == which, value, jnp.zeros_like(value))

    def turn(value):
        return value.astype(F32).T.astype(BF16)

    def attend(p):
        queries, keys = q6[p], k6[p]
        for which in range(2):
            scores = dot_nt(half_of(keys, which), queries)
            expo = jnp.exp(scores - jnp.max(scores, axis=0, keepdims=True))
            probs = (expo * (1.0 / jnp.sum(expo, axis=0, keepdims=True))).astype(BF16)
            pt[2 * p + which] = probs

    def mix(p):
        values_t = turn(v6[p])
        mixed = [dot_nn(values_t[64 * which : 64 * which + 64, :], pt[2 * p + which]) for which in range(2)]
        o6[p] = jnp.concatenate(mixed, axis=0).T.astype(BF16)

    loop(6, attend, (
        (1, lambda: ag_three(unit_vo)),
        (2, lambda: ag_one(unit_w1[1])),
        (3, lambda: ag_four(unit_vo), lambda: ag_two(unit_w1[0])),
    ))
    ag_two(unit_w1[1])
    ag_done(unit_vo)
    loop(zs, functools.partial(unpack, 1))
    project(2, v6, 3)
    each(ag_three, unit_w1)()
    loop(6, mix, (
        (1, lambda: ag_one(unit_w2[0])),
        (3, each(ag_four, unit_w1), lambda: ag_one(unit_w2[1])),
        (5, lambda: ag_two(unit_w2[0])),
    ))

    for n in range(3):
        cols = slice(256 * n, 256 * n + 256)
        value = dot_nt(lane_tiles(o6), at[3, cols, :]) + vec[4:5, cols]
        for s in range(4):
            h1[128 * s : 128 * s + 128, cols] = x_in[s, :, cols].astype(F32) + value[128 * s : 128 * s + 128]

    def second_norm(s):
        unit, _ = normalise(h1[rows_of(s), :])
        n2[rows_of(s), :] = (unit * vec[5:6, :] + vec[6:7, :]).astype(BF16)

    loop(4, second_norm)
    each(ag_done, unit_w1)()
    ag_two(unit_w2[1])

    def expand_piece(s, xx):
        def piece(ref):
            return jnp.concatenate([ref[96 * t : 96 * t + 96, :] for t in range(3)], axis=1)

        return jnp.concatenate(
            [piece(ubuf.at[1, h, cc, yy, xx, s]) for yy in range(2) for cc in range(2) for h in range(2)],
            axis=0,
        )

    def reduce_block(s):
        yy, cc = lax.div(s, 2), lax.rem(s, 2)

        def piece(ref):
            return jnp.concatenate([ref[48 * t : 48 * t + 48, :] for t in range(6)], axis=1)

        return jnp.concatenate(
            [piece(ubuf.at[2, h, cc, yy, xx, zz]) for zz in range(zs) for xx in range(2) for h in range(2)],
            axis=0,
        )

    def block_rows(s):
        return pl.ds(pl.multiple_of(s * 512, 512), 512)

    def expand(s):
        for xx in range(2):
            cols = slice(384 * xx, 384 * xx + 384)
            inner = dot_nn(n2[...], expand_piece(s, xx)) + vec[pl.ds(8 + s, 1), cols]
            square = inner * inner
            tanh = jnp.tanh(GELU_SCALE * inner * (1.0 + GELU_CUBE * square))
            act[block_rows(s), cols] = (0.5 * inner * (1.0 + tanh)).astype(BF16)
            slope = 0.5 * (1.0 + tanh) + 0.5 * inner * (1.0 - tanh * tanh) * (
                GELU_SCALE * (1.0 + 3.0 * GELU_CUBE * square)
            )
            gp[block_rows(s), cols] = slope.astype(BF16)

    loop(4, expand, (
        (1, each(ag_three, unit_w2)),
        (3, lambda: ag_four(unit_w2[0])),
    ))

    for moved in exchange_landed(cot_in, 1):
        moved.wait_recv()
    own_cot.wait()
    gvec[...] = jnp.zeros_like(gvec)

    def transpose_rows(dst, s, value):
        dst[:, 128 * s : 128 * s + 128] = turn(value)

    total = jnp.zeros((1, 768), F32)
    for s in range(4):
        transpose_rows(ta, s, cot_in[s])
        total = total + jnp.sum(cot_in[s].astype(F32), axis=0, keepdims=True)
    gvec[7:8, :] = total

    def reduce_back(s):
        yy, cc = lax.div(s, 2), lax.rem(s, 2)
        grad = dot_nn(ta[...], act[block_rows(s), :]).astype(BF16)
        for zz in range(zs):
            for xx in range(2):
                for h in range(2):
                    row = 96 * (2 * zz + xx) + 48 * h
                    for t in range(6):
                        ubuf[0, h, cc, yy, xx, zz, 48 * t : 48 * t + 48, :] = grad[
                            row : row + 48, 128 * t : 128 * t + 128
                        ]

    loop(4, reduce_back)
    each(rs_zero, grad_w2)()
    ag_four(unit_w2[1])
    each(rs_one, grad_w2)()
    each(ag_done, unit_w2)()

    def cotangent_rows():
        return jnp.concatenate([cot_in[s] for s in range(4)], axis=0)

    def inner_back(s):
        grad = dot_nn(cotangent_rows(), reduce_block(s)) * gp[block_rows(s), :].astype(F32)
        low = grad.astype(BF16)
        gp[block_rows(s), :] = low
        gvec[pl.ds(8 + s, 1), :] = jnp.sum(low.astype(F32), axis=0, keepdims=True)

    loop(4, inner_back)

    acc[...] = h1[...] + vec[7:8, :]

    def reduce(s):
        acc[...] += dot_nt(act[block_rows(s), :], reduce_block(s))

    loop(4, reduce)
    for moved in cot_out:
        moved.wait_send()
    for s in range(4):
        stage[s] = acc[128 * s : 128 * s + 128, :].astype(BF16)
    own_out = pltpu.make_async_copy(stage.at[i], out.at[i], local_sem.at[2])
    own_out.start()
    result_out = exchange(stage, out, 2)
    for moved in result_out:
        moved.start()

    for s in range(4):
        transpose_rows(tb, s, n2[128 * s : 128 * s + 128, :])

    def expand_back(s):
        for xx in range(2):
            grad = dot_nn(tb[...], gp[block_rows(s), 384 * xx : 384 * xx + 384]).astype(BF16)
            for yy in range(2):
                for cc in range(2):
                    for h in range(2):
                        row = 192 * (2 * yy + cc) + 96 * h
                        for t in range(3):
                            ubuf[2, h, cc, yy, xx, s, 96 * t : 96 * t + 96, :] = grad[
                                row : row + 96, 128 * t : 128 * t + 128
                            ]

    loop(4, expand_back)
    each(rs_zero, grad_w1)()
    each(rs_two, grad_w2)()

    def norm_back(s):
        whole = jnp.concatenate([expand_piece(s, 0), expand_piece(s, 1)], axis=1)
        part = dot_nt(gp[block_rows(s), :], whole)

        @pl.when(s == 0)
        def _():
            acc[...] = part

        @pl.when(s > 0)
        def _():
            acc[...] += part

    loop(4, norm_back, ((1, each(rs_one, grad_w1)),))

    def norm_gradient(value, scale_row, grad):
        unit, scale = normalise(value)
        gain_sum = jnp.sum(grad * unit, axis=0, keepdims=True)
        bias_sum = jnp.sum(grad, axis=0, keepdims=True)
        inner = grad * scale_row
        mean = jnp.mean(inner, axis=-1, keepdims=True)
        along = jnp.mean(inner * unit, axis=-1, keepdims=True)
        return scale * (inner - mean - unit * along), gain_sum, bias_sum

    def hidden_back(s):
        rows = rows_of(s)
        grad, gain_sum, bias_sum = norm_gradient(h1[rows, :], vec[5:6, :], acc[rows, :])
        grad = grad + cot_in[s].astype(F32)
        h1[rows, :] = grad
        low = grad.astype(BF16)
        n2[rows, :] = low
        gvec[5:6, :] += gain_sum
        gvec[6:7, :] += bias_sum
        gvec[4:5, :] += jnp.sum(low.astype(F32), axis=0, keepdims=True)

    loop(4, hidden_back)

    for n in range(3):
        value = dot_nn(n2[...], at[3, :, 256 * n : 256 * n + 256]).astype(BF16)
        d6[2 * n] = value[:, 0:128]
        d6[2 * n + 1] = value[:, 128:256]
    for s in range(4):
        transpose_rows(tc, s, n2[128 * s : 128 * s + 128, :])
    act[768:1536, :] = dot_nn(tc[...], lane_tiles(o6)).astype(BF16)
    each(rs_three, grad_w2)()

    def attend_back(p):
        rows = rows_of(p)
        queries, keys, values, grads_in = q6[p], k6[p], v6[p], d6[p]
        keys_t = turn(keys)
        grad_query, grad_key, grad_value = [], 0.0, 0.0
        for which in range(2):
            probs = pt[2 * p + which]
            wide = probs.astype(F32)
            grad_probs = dot_nt(half_of(values, which), grads_in)
            inner = jnp.sum(wide * grad_probs, axis=0, keepdims=True)
            grad_scores = (wide * (grad_probs - inner)).astype(BF16)
            grad_query.append(dot_nn(keys_t[64 * which : 64 * which + 64, :], grad_scores))
            grad_key = grad_key + dot_nn(grad_scores, half_of(queries, which))
            grad_value = grad_value + dot_nn(probs, half_of(grads_in, which))
        grad_query = jnp.concatenate(grad_query, axis=0) * HEAD ** (-0.5)
        ta[rows, :] = grad_query.astype(BF16)
        tb[rows, :] = grad_key.T.astype(BF16)
        tc[rows, :] = grad_value.T.astype(BF16)
        q6[p] = grad_query.T.astype(BF16)
        k6[p] = grad_key.astype(BF16)
        v6[p] = grad_value.astype(BF16)

    def pack(p, part, first_row, second_row):
        def body(s):
            for xx in range(2):
                offset = (2 * s + xx) * 96
                rows = [pl.ds(pl.multiple_of(first_row + offset, 96), 96),
                        pl.ds(pl.multiple_of(second_row + offset, 96), 96)]
                first = ubuf.at[1, p, 0, :, xx, part * half_zs + s]
                second = ubuf.at[1, p, 1, :, xx, part * half_zs + s]
                for yy in range(2):
                    lo, mid, hi = 384 * yy, 384 * yy + 128, 384 * yy + 256
                    for m in range(2):
                        first[yy, 96 * m : 96 * m + 96, :] = act[rows[m], lo : lo + 128]
                        second[yy, 96 * m : 96 * m + 96, :] = act[rows[m], hi : hi + 128]
                    even = act[rows[0], mid : mid + 128].astype(F32)
                    odd = pltpu.roll(act[rows[1], mid : mid + 128].astype(F32), 64, 1)
                    first[yy, 192:288, :] = jnp.where(lanes < 64, even, odd).astype(BF16)
                    second[yy, 192:288, :] = jnp.where(lanes < 64, odd, even).astype(BF16)

        loop(half_zs, body)

    def attention_gradients(part):
        rows = slice(384 * part, 384 * part + 384)
        act[1536:1920, :] = dot_nn(tc[rows, :], n1[...]).astype(BF16)
        pack(1, part, 1536, 768 + 384 * part)
        rs_zero(grad_a[part][1])
        act[0:384, :] = dot_nn(ta[rows, :], n1[...]).astype(BF16)
        act[384:768, :] = dot_nn(tb[rows, :], n1[...]).astype(BF16)
        pack(0, part, 0, 384)
        rs_zero(grad_a[part][0])

    loop(3, attend_back, ((0, each(rs_two, grad_w1)), (1, each(rs_done, grad_w2))))
    attention_gradients(0)
    loop(3, lambda p: attend_back(p + 3), (
        (0, each(rs_one, grad_a[0])),
        (1, each(rs_three, grad_w1)),
        (2, each(rs_two, grad_a[0])),
    ))
    attention_gradients(1)
    each(rs_one, grad_a[1])()
    each(rs_done, grad_w1)()

    acc[...] = dot_nn(lane_tiles(q6), at[0])
    acc[...] += dot_nn(lane_tiles(k6), at[1])
    acc[...] += dot_nn(lane_tiles(v6), at[2])
    gvec[2:3, :] = jnp.sum(lane_tiles(q6).astype(F32), axis=0, keepdims=True)
    gvec[3:4, :] = jnp.sum(lane_tiles(v6).astype(F32), axis=0, keepdims=True)
    each(rs_three, grad_a[0])()

    for moved in result_out:
        moved.wait_send()
    own_out.wait()

    def input_back(s):
        rows = rows_of(s)
        grad, gain_sum, bias_sum = norm_gradient(x_in[s].astype(F32), vec[0:1, :], acc[rows, :])
        stage[s] = (grad + h1[rows, :]).astype(BF16)
        gvec[0:1, :] += gain_sum
        gvec[1:2, :] += bias_sum

    loop(4, input_back)
    gvec_steps = small_sum(gvec, gin, 1)
    gvec_steps[0]()
    own_grad = pltpu.make_async_copy(stage.at[i], ig.at[i], local_sem.at[3])
    own_grad.start()
    grad_out = exchange(stage, ig, 3)
    for moved in grad_out:
        moved.start()

    gvec_steps[1]()
    each(rs_two, grad_a[1])()
    gvec_steps[2]()
    each(rs_done, grad_a[0])()
    gvec_steps[3]()
    each(rs_three, grad_a[1])()
    gvec_steps[4]()
    finish_vectors()
    each(rs_done, grad_a[1])()

    own_grad.wait()
    for moved in tokens_out + grad_out:
        moved.wait_send()
    for moved in exchange_landed(out, 2) + exchange_landed(ig, 3):
        moved.wait_recv()


def layer(sub, tokens, cotangent, span_mask, vectors, attention, expand, reduce_t):
    zs = GROUPS // 2
    seqs, block, width = tokens.shape
    rows = seqs * block
    columns = attention.shape[2]
    piece = (3 * columns, 128)
    vmem = lambda shape, dtype: pltpu.VMEM(shape, dtype)
    scratch = [vmem((3, 2, 2, 2, 2, zs) + piece, BF16)]
    scratch += [vmem((6, 2, 2, zs) + piece, BF16), vmem((6, 2, zs) + piece, BF16)]
    scratch += [vmem((6, zs) + piece, BF16), vmem((6, zs - 1) + piece, BF16)]
    scratch += [vmem(tokens.shape, BF16)] * 3
    scratch += [vmem((16, width), F32)] * 2
    scratch += [vmem((zs + 2, 16, width), F32)] * 2
    scratch += [vmem((16, columns), F32)]
    tiles = vmem((width // 128, rows, 128), BF16)
    flat = vmem((rows, width), BF16)
    turned = vmem((width, rows), BF16)
    scratch += [vmem((4, width, width), BF16), flat, tiles, tiles, tiles, tiles]
    scratch += [vmem((HEADS, rows, rows), BF16), vmem((rows, width), F32), vmem((rows, width), F32)]
    scratch += [flat, vmem((4 * rows, width), BF16), vmem((4 * rows, width), BF16)]
    scratch += [turned, turned, turned, tiles]
    scratch += [pltpu.SemaphoreType.DMA((4,))]
    scratch += [pltpu.SemaphoreType.DMA((6, 3 * zs + 4))] * 2
    scratch += [pltpu.SemaphoreType.DMA((8, zs + 3))] * 2
    scratch += [pltpu.SemaphoreType.DMA((4, 3))] * 2
    scratch += [pltpu.SemaphoreType.DMA((2, zs + 2))] * 2
    in_vmem = pl.BlockSpec(memory_space=pltpu.VMEM)
    anywhere = pl.BlockSpec(memory_space=pl.ANY)
    return pl.pallas_call(
        functools.partial(kernel, sub, zs),
        out_shape=(
            jax.ShapeDtypeStruct(tokens.shape, BF16),
            jax.ShapeDtypeStruct(tokens.shape, BF16),
            jax.ShapeDtypeStruct(attention.shape, F32),
            jax.ShapeDtypeStruct(expand.shape, F32),
            jax.ShapeDtypeStruct(reduce_t.shape, F32),
            jax.ShapeDtypeStruct(vectors.shape, F32),
        ),
        in_specs=[anywhere] + [in_vmem] * 6,
        out_specs=(anywhere, anywhere) + (in_vmem,) * 4,
        scratch_shapes=scratch,
        compiler_params=pltpu.CompilerParams(
            collective_id=0, has_side_effects=True, vmem_limit_bytes=63 * 1024 * 1024
        ),
    )(tokens, cotangent, span_mask, vectors, attention, expand, reduce_t)


def update_kernel(rates, *refs):
    count = len(rates)
    ins, (result, grad) = refs[: 4 * count], refs[4 * count : 4 * count + 2]
    outs, (result_out, grad_out) = refs[4 * count + 2 : 7 * count + 2], refs[7 * count + 2 : 7 * count + 4]
    held, (low, wide, passed) = refs[7 * count + 4 : 11 * count + 4], refs[11 * count + 4 : 11 * count + 7]
    in_sems, out_sems = refs[11 * count + 7 :]
    loads = [pltpu.make_async_copy(ins[n], held[n], in_sems.at[n]) for n in range(4 * count)]
    stores = [pltpu.make_async_copy(held[4 * n + m], outs[3 * n + m], out_sems.at[3 * n + m])
              for n in range(count) for m in range(3)]
    load_grad = pltpu.make_async_copy(grad, low, in_sems.at[4 * count])
    store_grad = pltpu.make_async_copy(wide, grad_out, out_sems.at[3 * count])
    load_result = pltpu.make_async_copy(result, passed, in_sems.at[4 * count + 1])
    store_result = pltpu.make_async_copy(passed, result_out, out_sems.at[3 * count + 1])
    load_grad.start()
    load_result.start()
    for copy in loads:
        copy.start()
    load_result.wait()
    store_result.start()
    load_grad.wait()

    def widen(s, carry):
        wide[s] = low[s].astype(F32)
        return carry

    lax.fori_loop(0, low.shape[0], widen, 0)
    store_grad.start()
    for n in range(count):
        for m in range(4):
            loads[4 * n + m].wait()
        weight, one, two, gradient = held[4 * n : 4 * n + 4]
        values = adamw(weight[...], one[...], two[...], gradient[...], rates[n])
        for ref, value in zip((weight, one, two), values):
            ref[...] = value
        for m in range(3):
            stores[3 * n + m].start()
    for copy in stores + [store_grad, store_result]:
        copy.wait()


def update(rates, arrays, result, grad):
    flat = [value for group in arrays for value in group]
    new = [jax.ShapeDtypeStruct(value.shape, F32) for group in arrays for value in group[:3]]
    new += [jax.ShapeDtypeStruct(result.shape, BF16), jax.ShapeDtypeStruct(grad.shape, F32)]
    anywhere = pl.BlockSpec(memory_space=pl.ANY)
    scratch = [pltpu.VMEM(value.shape, F32) for value in flat]
    scratch += [pltpu.VMEM(grad.shape, BF16), pltpu.VMEM(grad.shape, F32), pltpu.VMEM(result.shape, BF16)]
    scratch += [pltpu.SemaphoreType.DMA((len(flat) + 2,)), pltpu.SemaphoreType.DMA((len(new),))]
    return pl.pallas_call(
        functools.partial(update_kernel, rates),
        out_shape=tuple(new),
        in_specs=[anywhere] * (len(flat) + 2),
        out_specs=(anywhere,) * len(new),
        scratch_shapes=scratch,
        compiler_params=pltpu.CompilerParams(vmem_limit_bytes=63 * 1024 * 1024),
    )(*flat, result, grad)


def local(
    sub,
    tokens,
    cotangent,
    span_mask,
    attention_weight,
    expand_weight,
    reduce_weight,
    vectors,
    attention_first,
    attention_second,
    expand_first,
    expand_second,
    reduce_first,
    reduce_second,
    vector_first,
    vector_second,
):
    together = [[n * sub + m for m in range(sub)] for n in range(GROUPS)]

    def widen(value, axis):
        if sub == 1:
            return value
        low = lax.all_gather(
            value.astype(BF16), "batch", axis=axis, tiled=True, axis_index_groups=together
        )
        return low.astype(F32)

    def narrow(value, axis):
        if sub == 1:
            return value
        return lax.psum_scatter(
            value, "batch", scatter_dimension=axis, tiled=True, axis_index_groups=together
        )

    out_tokens, input_grad, ga, g1, g2, gv = layer(
        sub,
        tokens,
        cotangent,
        span_mask,
        widen(vectors, 1),
        widen(attention_weight, 2),
        widen(expand_weight, 1),
        widen(reduce_weight.T, 0),
    )
    arrays = (
        (attention_weight, attention_first, attention_second, narrow(ga, 2)),
        (expand_weight, expand_first, expand_second, narrow(g1, 1)),
        (reduce_weight.T, reduce_first.T, reduce_second.T, narrow(g2, 0)),
        (vectors, vector_first, vector_second, narrow(gv, 1)),
    )
    rates = (rate_attention, rate_expand, rate_reduce, rate_vector)
    new = update(rates, arrays, out_tokens, input_grad)
    return new[-2:] + new[0:6] + tuple(value.T for value in new[6:9]) + new[9:12]


def solution(mesh):
    sub = mesh.shape["batch"] // GROUPS
    sequences = P("batch", "blk", None)
    attention = P(None, "blk", "batch")
    matrix = P("blk", "batch")
    return jax.shard_map(
        functools.partial(local, sub),
        mesh=mesh,
        in_specs=(sequences, sequences, P("batch", "blk"), attention, matrix, matrix, matrix)
        + (attention,) * 2
        + (matrix,) * 6,
        out_specs=(sequences,) * 2 + (attention,) * 3 + (matrix,) * 9,
        check_vma=False,
    )
```

```python
import functools
import math

import jax
import jax.numpy as jnp
from jax import lax
from jax.experimental import pallas as pl
from jax.experimental.pallas import tpu as pltpu
from jax.sharding import PartitionSpec as P

HEADS = 12
HEAD = 64
STEP = 10
GROUPS = 8

norm_epsilon = 1e-05
beta_one = 0.9
beta_two = 0.999
adam_epsilon = 1e-08
decay_weight = 0.1
rate_attention = 0.05
rate_expand = 0.03
rate_reduce = 0.015
rate_vector = 0.4

F32 = jnp.float32
BF16 = jnp.bfloat16
MESH = pl.DeviceIdType.MESH
GELU_SCALE = math.sqrt(2.0 / math.pi)
GELU_CUBE = 0.044715


def adamw(weight, moment_one, moment_two, gradient, step_rate):
    moment_one = beta_one * moment_one + (1.0 - beta_one) * gradient
    moment_two = beta_two * moment_two + (1.0 - beta_two) * gradient * gradient
    corrected_one = moment_one / (1.0 - beta_one**STEP)
    corrected_two = moment_two / (1.0 - beta_two**STEP)
    updated = weight - step_rate * (
        corrected_one / (jnp.sqrt(corrected_two) + adam_epsilon) + decay_weight * weight
    )
    return (updated, moment_one, moment_two)


def dot_nn(left, right):
    return lax.dot_general(left, right, (((1,), (0,)), ((), ())), preferred_element_type=F32)


def dot_nt(left, right):
    return lax.dot_general(left, right, (((1,), (1,)), ((), ())), preferred_element_type=F32)


def lane_tiles(ref, count=6):
    return jnp.concatenate([ref[t] for t in range(count)], axis=1)


class Unit:
    def __init__(self, order, u, other, long_axis, fine):
        self.order, self.u, self.other, self.long_axis, self.fine = order, u, other, long_axis, fine


class Gradient:
    def __init__(self, order, u, other, long_axis, first, count, whole, core_in, long_in, mid_in, line_in, finish):
        self.order, self.long_axis, self.first, self.count, self.whole = order, long_axis, first, count, whole
        self.u, self.other, self.core_in, self.long_in, self.mid_in = u, other, core_in, long_in, mid_in
        self.line_in, self.finish = line_in, finish


def kernel(sub, zs, *refs):
    (tok, cot, mask_in, vec_in, a_in, w1_in, w2_in,
     out, ig, ga, g1, g2, gv,
     ua, uw1, uw2, gw1, gw2, core_in, long_in, mid_in, line_in,
     x_in, cot_in, stage, vec, gvec, vin, gin, narrow_rows,
     at, n1, q6, k6, v6, o6, pt, h1, acc, n2, act, gp, ta, tb, tc, d6,
     w1_other, w2_other, n2_other, cot_other, back_in, ahead_in,
     lines, b1, gb1, tot1, tot2, turned1, got1, got2,
     local_sem, ag_send, ag_recv, rs_send, rs_recv, a2a_send, a2a_recv, v_send, v_recv,
     pair_send, pair_recv) = refs

    i = lax.axis_index("blk")
    b = lax.axis_index("batch")
    c, y = lax.rem(i, 2), lax.div(i, 2)
    g, r = lax.div(b, sub), lax.rem(b, sub)
    x, z = lax.rem(g, 2), lax.div(g, 2)

    def device(c_=c, y_=y, x_=x, z_=z):
        return {"blk": 2 * y_ + c_, "batch": (2 * z_ + x_) * sub + r}

    def z_at(k):
        return lax.rem(z + k, zs)

    def block_at(k):
        return lax.rem(i + k, 4)

    def copy(src, dst, send, recv, to):
        return pltpu.make_async_remote_copy(
            src_ref=src, dst_ref=dst, send_sem=send, recv_sem=recv, device_id=to, device_id_type=MESH
        )

    def loop(count, body, hooks=()):
        def step(s, carry):
            body(s)
            for k, *todo in hooks:

                @pl.when(s == k)
                def _():
                    for f in todo:
                        f()

            return carry

        lax.fori_loop(0, count, step, 0)

    partners = [device(z_=z_at(k)) for k in range(1, zs)]
    partners += [device(x_=1 - x), device(y_=1 - y), device(c_=1 - c), device(c_=1 - c, y_=1 - y)]
    barrier = pltpu.get_barrier_semaphore()
    for partner in partners:
        pl.semaphore_signal(barrier, inc=1, device_id=partner, device_id_type=MESH)
    pl.semaphore_wait(barrier, len(partners))

    def ag_sems(n, slot):
        return ag_send.at[n.order, slot], ag_recv.at[n.order, slot]

    def places(n, long_off, mid_off):
        yy = y if (long_off if n.long_axis == "y" else mid_off) == 0 else 1 - y
        xx = x if (long_off if n.long_axis == "x" else mid_off) == 0 else 1 - x
        return yy, xx

    def group(n, u, long_off, mid_off, cut=None):
        where = places(n, long_off, mid_off)
        return u.at[where] if cut is None else u.at[where + (cut,)]

    def partner_of(n, step):
        axis = n.long_axis if step == "long" else {"x": "y", "y": "x"}[n.long_axis]
        return device(x_=1 - x) if axis == "x" else device(y_=1 - y)

    LINE, MID, LONG, LAST, CORE = 0, zs - 1, 2 * zs - 1, 3 * zs - 1, 3 * zs

    def ag_line(n, k, landed=False):
        ref = group(n, n.u, 0, 0, z_at(zs - k) if landed else z)
        return copy(ref, ref, *ag_sems(n, LINE + k - 1), device(z_=z_at(k)))

    def ag_first(n, step, k, landed=False):
        cut = z_at(zs - k) if n.fine else None
        off = (0, 1) if step == "mid" else (1, 0)
        ref = group(n, n.u, *(off if landed else (0, 0)), cut)
        return copy(ref, ref, *ag_sems(n, (MID if step == "mid" else LONG) + k), partner_of(n, step))

    def ag_last(n, landed=False):
        ref = group(n, n.u, 1 if landed else 0, 1)
        return copy(ref, ref, *ag_sems(n, LAST), partner_of(n, "long"))

    def ag_core(n, long_off, mid_off, landed=False):
        ref = group(n, n.other if landed else n.u, long_off, mid_off)
        return copy(ref, ref, *ag_sems(n, CORE + 2 * long_off + mid_off), device(c_=1 - c))

    def ag_core_start(n, long_off, mid_off):
        if n.other is not None:
            ag_core(n, long_off, mid_off).start()

    def parts(n):
        return range(zs) if n.fine else range(1)

    def ag_start(n):
        if n.fine:
            for step in ("mid", "long"):
                ag_first(n, step, 0).start()
        for k in range(1, zs):
            ag_line(n, k).start()

    def ag_piece(n, k):
        ag_line(n, k, True).wait_recv()
        for step in ("mid", "long"):
            ag_first(n, step, k).start()

    def ag_one(n):
        if not n.fine:
            for k in range(1, zs):
                ag_line(n, k, True).wait_recv()
            for step in ("mid", "long"):
                ag_first(n, step, 0).start()
        ag_core_start(n, 0, 0)

    def ag_two(n):
        for k in parts(n):
            ag_first(n, "mid", k, True).wait_recv()
        ag_last(n).start()
        ag_core_start(n, 0, 1)

    def ag_three(n):
        for k in parts(n):
            ag_first(n, "long", k, True).wait_recv()
        ag_core_start(n, 1, 0)

    def ag_four(n):
        ag_last(n, True).wait_recv()
        ag_core_start(n, 1, 1)

    def ag_done(n):
        offs = ((0, 0), (0, 1), (1, 0), (1, 1)) if n.other is not None else ()
        for off in offs:
            ag_core(n, *off, True).wait_recv()
        for k in range(1, zs):
            ag_line(n, k).wait_send()
        for step in ("mid", "long"):
            for k in parts(n):
                ag_first(n, step, k).wait_send()
        ag_last(n).wait_send()
        for off in offs:
            ag_core(n, *off).wait_send()

    def rs_sems(n, slot):
        return rs_send.at[n.order, slot], rs_recv.at[n.order, slot]

    def cut_of(n):
        return slice(None) if n.count == zs else pl.ds(n.first, n.count)

    def rs_core(n, long_off):
        place = 1 - (y if n.long_axis == "y" else x) if long_off else (y if n.long_axis == "y" else x)
        where = (place, slice(None)) if n.long_axis == "y" else (slice(None), place)
        return copy(n.other.at[where + (cut_of(n),)], n.core_in.at[where],
                    *rs_sems(n, long_off), device(c_=1 - c))

    def rs_long(n):
        where = (1 - y, slice(None)) if n.long_axis == "y" else (slice(None), 1 - x)
        return copy(n.u.at[where + (cut_of(n),)], n.long_in, *rs_sems(n, 2), partner_of(n, "long"))

    def rs_mid(n):
        return copy(group(n, n.u, 0, 1, cut_of(n)), n.mid_in, *rs_sems(n, 3), partner_of(n, "mid"))

    def rs_line(n, k):
        return copy(group(n, n.u, 0, 0, z_at(k)), n.line_in.at[k - 1], *rs_sems(n, 3 + k), device(z_=z_at(k)))

    def within(n, place):
        return jnp.logical_and(place >= n.first, place < n.first + n.count)

    def when_within(n, place, f):
        if n.whole:
            f()
        else:
            pl.when(within(n, place))(f)

    def gather_terms(n, long_off, mid_off, names):
        yy, xx = places(n, long_off, mid_off)

        def body(s):
            mine = n.u.at[yy, xx, n.first + s]
            value = mine[...].astype(F32)
            if n.other is not None:
                value = value + n.core_in[yy, xx, s].astype(F32)
            if "long" in names:
                value = value + n.long_in[xx if n.long_axis == "y" else yy, s].astype(F32)
            if "mid" in names:
                value = value + n.mid_in[s].astype(F32)
            mine[...] = value.astype(BF16)

        loop(n.count, body)

    def rs_zero(n):
        rs_core(n, 1).start()
        rs_core(n, 0).start()

    def rs_one(n):
        if n.other is not None:
            rs_core(n, 1).wait_recv()
            gather_terms(n, 1, 0, ())
            gather_terms(n, 1, 1, ())
        rs_long(n).start()

    def rs_two(n):
        if n.other is not None:
            rs_core(n, 0).wait_recv()
        rs_long(n).wait_recv()
        gather_terms(n, 0, 1, ("long",))
        rs_mid(n).start()

    def rs_three(n):
        rs_mid(n).wait_recv()
        gather_terms(n, 0, 0, ("long", "mid"))
        for k in range(1, zs):
            when_within(n, z_at(k), lambda k=k: rs_line(n, k).start())

    def rs_done(n):
        def finish():
            for k in range(1, zs):
                rs_line(n, k).wait_recv()
            value = n.u[y, x, z].astype(F32)
            for k in range(1, zs):
                value = value + n.line_in[k - 1].astype(F32)
            n.finish(value)

        when_within(n, z, finish)
        if n.other is not None:
            rs_core(n, 0).wait_send()
            rs_core(n, 1).wait_send()
        rs_long(n).wait_send()
        rs_mid(n).wait_send()
        for k in range(1, zs):
            when_within(n, z_at(k), lambda k=k: rs_line(n, k).wait_send())

    def small_sum(ref, slots, which):
        to = (device(y_=1 - y), device(c_=1 - c), device(x_=1 - x))
        to += tuple(device(z_=z_at(k)) for k in range(1, zs))

        def moved(slot):
            return copy(ref, slots.at[slot], v_send.at[which, slot], v_recv.at[which, slot], to[slot])

        def land(last):
            moved(last).wait()
            ref[...] = ref[...] + slots[last]

        def step(n):
            def run():
                if n > 0:
                    land(n - 1)
                moved(n).start()

            return run

        def line():
            land(2)
            for k in range(1, zs):
                moved(2 + k).start()

        def finish():
            for k in range(1, zs):
                moved(2 + k).wait()
            value = ref[...]
            for k in range(1, zs):
                value = value + slots[2 + k]
            ref[...] = value

        return [step(0), step(1), step(2), line, finish]

    def exchange(src, dst, which):
        return [copy(src.at[block_at(k)], dst.at[i], a2a_send.at[which, k - 1],
                     a2a_recv.at[which, k - 1], {"blk": block_at(k), "batch": b})
                for k in range(1, 4)]

    def exchange_landed(dst, which):
        return [copy(dst.at[block_at(4 - k)], dst.at[block_at(4 - k)], a2a_send.at[which, k - 1],
                     a2a_recv.at[which, k - 1], {"blk": block_at(4 - k), "batch": b})
                for k in range(1, 4)]

    unit_qk, unit_vo = [Unit(half, ua.at[half, c], ua.at[half, 1 - c], "xy"[half], True) for half in range(2)]
    unit_w1 = [Unit(2 + half, uw1.at[half], None, "xy"[half], False) for half in range(2)]
    unit_w2 = [Unit(4 + half, uw2.at[half], None, "xx"[half], False) for half in range(2)]

    def pair(slot, src, dst):
        return copy(src, dst, pair_send.at[slot], pair_recv.at[slot], device(c_=1 - c))

    w1_swap, w2_swap = pair(0, w1_in, w1_other), pair(1, w2_in, w2_other)

    def each_core(f):
        for q in range(2):
            pl.when(c == q)(functools.partial(f, q))

    def rest_rows(matrix):
        return a_in[matrix, pl.ds(pl.multiple_of(128 * (1 - c), 64), 64), :]

    def own_attention(p):
        mine = ua.at[p, c, y, x, z]
        for m in range(2):
            main = a_in[2 * p + m, pl.ds(pl.multiple_of(64 * c, 64), 128), :]
            mine[96 * m : 96 * m + 96, :] = main.T.astype(BF16)
        rest = jnp.concatenate([rest_rows(2 * p + c), rest_rows(2 * p + 1 - c)], axis=0)
        mine[192:288, :] = rest.T.astype(BF16)

    def own_expand(q):
        both = (w1_in, w1_other) if q == 0 else (w1_other, w1_in)
        cols = slice(192 * q, 192 * q + 192)
        blocks = (
            both[0][0:128, cols],
            jnp.concatenate([both[0][128:192, cols], both[1][0:64, cols]], axis=0),
            both[1][64:192, cols],
        )
        for t, block in enumerate(blocks):
            value = block.T.astype(BF16)
            for h in range(2):
                uw1[h, y, x, z, 96 * t : 96 * t + 96, :] = value[96 * h : 96 * h + 96, :]

    def own_reduce(q):
        both = (w2_in, w2_other) if q == 0 else (w2_other, w2_in)
        for cc in range(2):
            for part_of in range(2):
                start = 384 * part_of + 192 * q
                lines[:, 192 * part_of : 192 * part_of + 192] = both[cc][:, start : start + 192]
            for t in range(3):
                uw2[cc, y, x, z, 96 * t : 96 * t + 96, :] = lines[:, 128 * t : 128 * t + 128].astype(BF16)

    def own_hidden_bias(q):
        for zz in range(zs):
            for xx in range(2):
                col = 384 * (zz % 2) + 192 * xx
                start = 384 * xx + 192 * q
                b1[zz // 2 : zz // 2 + 1, col : col + 192] = vec[8 + zz : 9 + zz, start : start + 192]

    def hidden_bias_gradient(q):
        for zz in range(zs):
            for xx in range(2):
                col = 384 * (zz % 2) + 192 * xx
                start = 384 * xx + 192 * q
                gvec[8 + zz : 9 + zz, start : start + 192] = gb1[zz // 2 : zz // 2 + 1, col : col + 192]

    columns = a_in.shape[2]
    placed = lax.broadcasted_iota(jnp.int32, (columns, 768), 1) == (
        lax.broadcasted_iota(jnp.int32, (columns, 768), 0) + columns * g
    )

    def own_vectors():
        vec[...] = jnp.zeros_like(vec)
        rows = dot_nn(vec_in[...].astype(BF16), jnp.where(placed, 1.0, 0.0).astype(BF16))
        for j in range(3):
            vec[pl.ds(3 * i + j, 1), :] = rows[j : j + 1, :]

    load_cot = pltpu.make_async_copy(cot, stage, local_sem.at[4])

    def masked_cotangent():
        load_cot.wait()
        eye = lax.broadcasted_iota(jnp.int32, (128, 128), 0) == lax.broadcasted_iota(jnp.int32, (128, 128), 1)
        for s in range(4):
            row = jnp.broadcast_to(mask_in[s : s + 1, :].astype(F32), (128, 128))
            column = jnp.sum(jnp.where(eye, row, 0.0), axis=1, keepdims=True)
            stage[s] = (stage[s].astype(F32) * column).astype(BF16)

    def finish_attention(p):
        def finish(value):
            for m in range(2):
                ga[2 * p + m, pl.ds(pl.multiple_of(64 * c, 64), 128), :] = value[96 * m : 96 * m + 96, :].T
            rest = value[192:288, :].T
            rows = pl.ds(pl.multiple_of(128 * (1 - c), 64), 64)
            ga[2 * p + c, rows, :] = rest[0:64, :]
            ga[2 * p + 1 - c, rows, :] = rest[64:128, :]

        return finish

    def finish_expand(h):
        def finish(value):
            tot1[h] = value

        return finish

    def finish_reduce(h):
        def finish(value):
            tot2[h] = value

        return finish

    w1_back = pair(6, turned1.at[pl.ds(pl.multiple_of(192 * (1 - c), 64), 192)], got1)
    w2_back = pair(7, tot2.at[1 - c], got2)

    def turn_expand():
        for h in range(2):
            for t in range(3):
                turned1[128 * t : 128 * t + 128, 96 * h : 96 * h + 96] = tot1[h, 96 * t : 96 * t + 96, :].T
        w1_back.start()

    def join_expand(q):
        g1[:, 192 * q : 192 * q + 192] = turned1[192 * q : 192 * q + 192, :]
        g1[:, 192 * (1 - q) : 192 * (1 - q) + 192] = got1[...]

    def join_reduce(q):
        for half, value in ((q, tot2.at[q]), (1 - q, got2)):
            for t in range(3):
                lines[:, 128 * t : 128 * t + 128] = value[96 * t : 96 * t + 96, :]
            for part_of in range(2):
                start = 384 * part_of + 192 * half
                g2[:, start : start + 192] = lines[:, 192 * part_of : 192 * part_of + 192]

    def finish_vectors():
        value, total = gvec[...], 0.0
        for _ in range(3):
            part = value.astype(BF16)
            total = total + dot_nt(part, jnp.where(placed, 1.0, 0.0).astype(BF16))
            value = value - part.astype(F32)
        narrow_rows[...] = total
        for j in range(3):
            gv[j : j + 1, :] = narrow_rows[pl.ds(3 * i + j, 1), :]

    grads = []
    half_zs = zs // 2
    for n, (source, finish, axes) in enumerate(((gw2, finish_reduce, "xy"), (gw1, finish_expand, "yx"))):
        for half in range(2):
            order = 2 * n + half
            grads.append(Gradient(order, source.at[half], None, axes[half], 0, zs, True,
                                  None, long_in.at[order], mid_in.at[order],
                                  line_in.at[order], finish(half)))
    for part_of in range(2):
        for half in range(2):
            cut = pl.ds(part_of * half_zs, half_zs)
            grads.append(Gradient(4 + 2 * part_of + half, ua.at[half, c], ua.at[half, 1 - c], "xy"[half],
                                  part_of * half_zs, half_zs, False,
                                  core_in.at[half, :, :, cut], long_in.at[4 + half, :, cut],
                                  mid_in.at[4 + half, cut], line_in.at[4 + half], finish_attention(half)))
    grad_w2, grad_w1, grad_a = grads[0:2], grads[2:4], (grads[4:6], grads[6:8])

    def each(f, which):
        def run():
            for n in which:
                f(n)

        return run

    load_cot.start()
    own_attention(0)
    ag_start(unit_qk)
    w1_swap.start()
    w2_swap.start()
    own_vectors()
    vec_steps = small_sum(vec, vin, 0)
    vec_steps[0]()
    own_tokens = pltpu.make_async_copy(tok.at[i], x_in.at[i], local_sem.at[0])
    own_tokens.start()
    tokens_out = exchange(tok, x_in, 0)
    for moved in tokens_out:
        moved.start()
    own_attention(1)
    w1_swap.wait()
    each_core(own_expand)
    w2_swap.wait()
    each_core(own_reduce)
    for k in range(1, zs):
        ag_piece(unit_qk, k)
    ag_one(unit_qk)
    ag_start(unit_vo)
    ag_start(unit_w1[0])
    vec_steps[1]()
    masked_cotangent()
    ag_two(unit_qk)
    vec_steps[2]()
    for k in range(1, zs):
        ag_piece(unit_vo, k)
    ag_one(unit_vo)
    ag_start(unit_w1[1])
    vec_steps[3]()
    ag_three(unit_qk)

    for moved in exchange_landed(x_in, 0):
        moved.wait_recv()
    own_tokens.wait()
    vec_steps[4]()
    each_core(own_hidden_bias)

    def normalise(value):
        centered = value - jnp.mean(value, axis=-1, keepdims=True)
        scale = lax.rsqrt(jnp.mean(centered * centered, axis=-1, keepdims=True) + norm_epsilon)
        return centered * scale, scale

    def rows_of(s):
        return pl.ds(pl.multiple_of(s * 128, 128), 128)

    def first_norm(s):
        unit, _ = normalise(x_in[s].astype(F32))
        n1[rows_of(s), :] = (unit * vec[0:1, :] + vec[1:2, :]).astype(BF16)

    loop(4, first_norm)
    ag_four(unit_qk)
    own_cot = pltpu.make_async_copy(stage.at[i], cot_in.at[i], local_sem.at[1])
    own_cot.start()
    cot_out = exchange(stage, cot_in, 1)
    for moved in cot_out:
        moved.start()
    ag_done(unit_qk)

    lanes = lax.broadcasted_iota(jnp.int32, (96, 128), 1)

    def unpack(p, s):
        for xx in range(2):
            rows = pl.ds(pl.multiple_of((2 * s + xx) * 96, 96), 96)
            for yy in range(2):
                first, second = ua.at[p, 0, yy, xx, s], ua.at[p, 1, yy, xx, s]
                lo, hi = 384 * yy, 384 * yy + 256
                for m in range(2):
                    at[2 * p + m, rows, lo : lo + 128] = first[96 * m : 96 * m + 96, :]
                    at[2 * p + m, rows, hi : hi + 128] = second[96 * m : 96 * m + 96, :]
                rest_first = first[192:288, :].astype(F32)
                rest_second = second[192:288, :].astype(F32)
                even = jnp.where(lanes < 64, rest_first, rest_second)
                odd = pltpu.roll(jnp.where(lanes < 64, rest_second, rest_first), 64, 1)
                at[2 * p, rows, lo + 128 : lo + 256] = even.astype(BF16)
                at[2 * p + 1, rows, lo + 128 : lo + 256] = odd.astype(BF16)

    def project(m, dst, bias):
        for n in range(3):
            value = dot_nt(n1[...], at[m, 256 * n : 256 * n + 256, :])
            if bias is not None:
                value = value + vec[bias : bias + 1, 256 * n : 256 * n + 256]
            value = value.astype(BF16)
            if m == 0:
                value = value * jnp.asarray(HEAD ** (-0.5), BF16)
            dst[2 * n] = value[:, 0:128]
            dst[2 * n + 1] = value[:, 128:256]

    loop(zs, functools.partial(unpack, 0))
    project(0, q6, 2)
    ag_two(unit_vo)
    project(1, k6, None)
    ag_one(unit_w1[0])

    half_lane = lax.broadcasted_iota(jnp.int32, (512, 128), 1) // HEAD

    def half_of(value, which):
        return jnp.where(half_lane == which, value, jnp.zeros_like(value))

    def turn(value):
        return value.astype(F32).T.astype(BF16)

    def attend(p):
        queries, keys = q6[p], k6[p]
        for which in range(2):
            scores = dot_nt(half_of(keys, which), queries)
            expo = jnp.exp(scores - jnp.max(scores, axis=0, keepdims=True))
            probs = (expo * (1.0 / jnp.sum(expo, axis=0, keepdims=True))).astype(BF16)
            pt[2 * p + which] = probs

    def mix(p):
        values_t = turn(v6[p])
        mixed = [dot_nn(values_t[64 * which : 64 * which + 64, :], pt[2 * p + which]) for which in range(2)]
        o6[p] = jnp.concatenate(mixed, axis=0).T.astype(BF16)

    loop(6, attend, (
        (1, lambda: ag_three(unit_vo)),
        (2, lambda: ag_one(unit_w1[1]), each(ag_start, unit_w2)),
        (3, lambda: ag_four(unit_vo), lambda: ag_two(unit_w1[0])),
    ))
    ag_two(unit_w1[1])
    ag_done(unit_vo)
    loop(zs, functools.partial(unpack, 1))
    project(2, v6, 3)
    each(ag_three, unit_w1)()
    loop(6, mix, (
        (1, lambda: ag_one(unit_w2[0])),
        (3, each(ag_four, unit_w1), lambda: ag_one(unit_w2[1])),
        (5, lambda: ag_two(unit_w2[0])),
    ))

    for n in range(3):
        cols = slice(256 * n, 256 * n + 256)
        value = dot_nt(lane_tiles(o6), at[3, cols, :]) + vec[4:5, cols]
        for s in range(4):
            h1[128 * s : 128 * s + 128, cols] = x_in[s, :, cols].astype(F32) + value[128 * s : 128 * s + 128]

    def second_norm(s):
        unit, _ = normalise(h1[rows_of(s), :])
        n2[rows_of(s), :] = (unit * vec[5:6, :] + vec[6:7, :]).astype(BF16)

    loop(4, second_norm)
    n2_swap = pair(2, n2, n2_other)
    n2_swap.start()
    for moved in exchange_landed(cot_in, 1):
        moved.wait_recv()
    own_cot.wait()
    cot_swap = pair(3, cot_in, cot_other)
    cot_swap.start()
    each(ag_done, unit_w1)()
    ag_two(unit_w2[1])

    def expand_block(s):
        def piece(ref):
            return jnp.concatenate([ref[96 * t : 96 * t + 96, :] for t in range(3)], axis=1)

        return jnp.concatenate(
            [jnp.concatenate([piece(uw1.at[h, yy, xx, 2 * s + zz]) for yy in range(2)], axis=1)
             for zz in range(2) for xx in range(2) for h in range(2)],
            axis=0,
        )

    def reduce_block(s):
        def piece(ref):
            return jnp.concatenate([ref[96 * t : 96 * t + 96, :] for t in range(3)], axis=1)

        return jnp.concatenate(
            [jnp.concatenate([piece(uw2.at[cc, s, xx, zz]) for cc in range(2)], axis=1)
             for zz in range(zs) for xx in range(2)],
            axis=0,
        )

    def block_rows(owner, s):
        return pl.ds(pl.multiple_of((2 * owner + s) * 512, 512), 512)

    def expand(owner, normed, s):
        rows = block_rows(owner, s)
        inner = dot_nt(normed[...], expand_block(s)) + b1[pl.ds(s, 1), :]
        square = inner * inner
        tanh = jnp.tanh(GELU_SCALE * inner * (1.0 + GELU_CUBE * square))
        act[rows, :] = (0.5 * inner * (1.0 + tanh)).astype(BF16)
        slope = 0.5 * (1.0 + tanh) + 0.5 * inner * (1.0 - tanh * tanh) * (
            GELU_SCALE * (1.0 + 3.0 * GELU_CUBE * square)
        )
        gp[rows, :] = slope.astype(BF16)

    loop(2, functools.partial(expand, 0, n2))
    each(ag_three, unit_w2)()
    n2_swap.wait()
    loop(2, functools.partial(expand, 1, n2_other))
    ag_four(unit_w2[0])

    gvec[...] = jnp.zeros_like(gvec)

    def transpose_rows(dst, s, value):
        dst[:, 128 * s : 128 * s + 128] = turn(value)

    total = jnp.zeros((1, 768), F32)
    for s in range(4):
        transpose_rows(ta, s, cot_in[s])
        total = total + jnp.sum(cot_in[s].astype(F32), axis=0, keepdims=True)
    gvec[7:8, :] = total
    cot_swap.wait()
    for s in range(4):
        transpose_rows(tb, s, cot_other[s])

    def both_rows(ref, s):
        return jnp.concatenate([ref[block_rows(0, s), :], ref[block_rows(1, s), :]], axis=0)

    def reduce_back(s):
        grad = dot_nn(jnp.concatenate([ta[...], tb[...]], axis=1), both_rows(act, s)).astype(BF16)
        for zz in range(zs):
            for xx in range(2):
                row = 96 * (2 * zz + xx)
                for cc in range(2):
                    for t in range(3):
                        col = 384 * cc + 128 * t
                        gw2[cc, s, xx, zz, 96 * t : 96 * t + 96, :] = grad[row : row + 96, col : col + 128]

    loop(2, reduce_back)
    each(rs_one, grad_w2)()
    ag_four(unit_w2[1])
    each(ag_done, unit_w2)()

    def rows_together(ref):
        return jnp.concatenate([ref[s] for s in range(4)], axis=0)

    def inner_back(owner, cotangent_rows, s):
        rows = block_rows(owner, s)
        grad = dot_nn(rows_together(cotangent_rows), reduce_block(s)) * gp[rows, :].astype(F32)
        low = grad.astype(BF16)
        gp[rows, :] = low
        sums = jnp.sum(low.astype(F32), axis=0, keepdims=True)
        gb1[pl.ds(s, 1), :] = sums if owner == 1 else gb1[pl.ds(s, 1), :] + sums

    def norm_back(owner):
        acc[...] = dot_nn(gp[block_rows(owner, 0), :], expand_block(0))
        acc[...] += dot_nn(gp[block_rows(owner, 1), :], expand_block(1))

    loop(2, functools.partial(inner_back, 1, cot_other))
    norm_back(1)
    for t in range(6):
        d6[t] = acc[:, 128 * t : 128 * t + 128].astype(BF16)
    back_swap = pair(4, d6, back_in)
    back_swap.start()
    loop(2, functools.partial(inner_back, 0, cot_in))
    each_core(hidden_bias_gradient)
    norm_back(0)

    def expand_back(s):
        turned = jnp.concatenate([turn(gp[block_rows(owner, s), :]) for owner in range(2)], axis=1)
        normed = jnp.concatenate([n2[...], n2_other[...]], axis=0)
        grad = dot_nn(turned, normed).astype(BF16)
        for zz in range(2):
            for xx in range(2):
                for h in range(2):
                    row = 384 * zz + 192 * xx + 96 * h
                    for yy in range(2):
                        for t in range(3):
                            col = 384 * yy + 128 * t
                            gw1[h, yy, xx, 2 * s + zz, 96 * t : 96 * t + 96, :] = grad[
                                row : row + 96, col : col + 128
                            ]

    loop(2, expand_back)
    each(rs_one, grad_w1)()
    each(rs_two, grad_w2)()
    back_swap.wait()

    def norm_gradient(value, scale_row, grad):
        unit, scale = normalise(value)
        gain_sum = jnp.sum(grad * unit, axis=0, keepdims=True)
        bias_sum = jnp.sum(grad, axis=0, keepdims=True)
        inner = grad * scale_row
        mean = jnp.mean(inner, axis=-1, keepdims=True)
        along = jnp.mean(inner * unit, axis=-1, keepdims=True)
        return scale * (inner - mean - unit * along), gain_sum, bias_sum

    def hidden_back(s):
        rows = rows_of(s)
        grad_in = jnp.concatenate([back_in[t, rows, :] for t in range(6)], axis=1)
        grad_in = acc[rows, :] + grad_in.astype(F32)
        grad, gain_sum, bias_sum = norm_gradient(h1[rows, :], vec[5:6, :], grad_in)
        grad = grad + cot_in[s].astype(F32)
        acc[rows, :] = grad
        low = grad.astype(BF16)
        n2[rows, :] = low
        gvec[5:6, :] += gain_sum
        gvec[6:7, :] += bias_sum
        gvec[4:5, :] += jnp.sum(low.astype(F32), axis=0, keepdims=True)

    loop(4, hidden_back)

    for n in range(3):
        value = dot_nn(n2[...], at[3, :, 256 * n : 256 * n + 256]).astype(BF16)
        d6[2 * n] = value[:, 0:128]
        d6[2 * n + 1] = value[:, 128:256]
    for s in range(4):
        transpose_rows(tc, s, n2[128 * s : 128 * s + 128, :])
    gp[768:1536, :] = dot_nn(tc[...], lane_tiles(o6)).astype(BF16)
    each(rs_three, grad_w2)()

    def attend_back(p):
        rows = rows_of(p)
        queries, keys, values, grads_in = q6[p], k6[p], v6[p], d6[p]
        keys_t = turn(keys)
        grad_query, grad_key, grad_value = [], 0.0, 0.0
        for which in range(2):
            probs = pt[2 * p + which]
            wide = probs.astype(F32)
            grad_probs = dot_nt(half_of(values, which), grads_in)
            inner = jnp.sum(wide * grad_probs, axis=0, keepdims=True)
            grad_scores = (wide * (grad_probs - inner)).astype(BF16)
            grad_query.append(dot_nn(keys_t[64 * which : 64 * which + 64, :], grad_scores))
            grad_key = grad_key + dot_nn(grad_scores, half_of(queries, which))
            grad_value = grad_value + dot_nn(probs, half_of(grads_in, which))
        grad_query = jnp.concatenate(grad_query, axis=0) * HEAD ** (-0.5)
        ta[rows, :] = grad_query.astype(BF16)
        tb[rows, :] = grad_key.T.astype(BF16)
        tc[rows, :] = grad_value.T.astype(BF16)
        q6[p] = grad_query.T.astype(BF16)
        k6[p] = grad_key.astype(BF16)
        v6[p] = grad_value.astype(BF16)

    def pack(p, half, first_row, second_row):
        def body(s):
            for xx in range(2):
                offset = (2 * s + xx) * 96
                rows = [pl.ds(pl.multiple_of(first_row + offset, 96), 96),
                        pl.ds(pl.multiple_of(second_row + offset, 96), 96)]
                first = ua.at[p, 0, :, xx, half * half_zs + s]
                second = ua.at[p, 1, :, xx, half * half_zs + s]
                for yy in range(2):
                    lo, mid, hi = 384 * yy, 384 * yy + 128, 384 * yy + 256
                    for m in range(2):
                        first[yy, 96 * m : 96 * m + 96, :] = gp[rows[m], lo : lo + 128]
                        second[yy, 96 * m : 96 * m + 96, :] = gp[rows[m], hi : hi + 128]
                    even = gp[rows[0], mid : mid + 128].astype(F32)
                    odd = pltpu.roll(gp[rows[1], mid : mid + 128].astype(F32), 64, 1)
                    first[yy, 192:288, :] = jnp.where(lanes < 64, even, odd).astype(BF16)
                    second[yy, 192:288, :] = jnp.where(lanes < 64, odd, even).astype(BF16)

        loop(half_zs, body)

    def attention_gradients(half):
        rows = slice(384 * half, 384 * half + 384)
        gp[1536:1920, :] = dot_nn(tc[rows, :], n1[...]).astype(BF16)
        pack(1, half, 1536, 768 + 384 * half)
        rs_zero(grad_a[half][1])
        gp[0:384, :] = dot_nn(ta[rows, :], n1[...]).astype(BF16)
        gp[384:768, :] = dot_nn(tb[rows, :], n1[...]).astype(BF16)
        pack(0, half, 0, 384)
        rs_zero(grad_a[half][0])

    loop(3, attend_back, ((0, each(rs_two, grad_w1)), (1, each(rs_done, grad_w2))))
    attention_gradients(0)

    def reduce(owner):
        value = dot_nt(act[block_rows(owner, 0), :], reduce_block(0))
        return value + dot_nt(act[block_rows(owner, 1), :], reduce_block(1))

    n2[...] = reduce(1).astype(BF16)
    ahead_swap = pair(5, n2, ahead_in)
    ahead_swap.start()
    h1[...] = h1[...] + vec[7:8, :] + reduce(0)
    for moved in cot_out:
        moved.wait_send()
    ahead_swap.wait()
    for s in range(4):
        rows = slice(128 * s, 128 * s + 128)
        stage[s] = (h1[rows, :] + ahead_in[rows, :].astype(F32)).astype(BF16)
    own_out = pltpu.make_async_copy(stage.at[i], out.at[i], local_sem.at[2])
    own_out.start()
    result_out = exchange(stage, out, 2)
    for moved in result_out:
        moved.start()

    loop(3, lambda p: attend_back(p + 3), (
        (0, each(rs_one, grad_a[0])),
        (1, each(rs_three, grad_w1)),
        (2, each(rs_two, grad_a[0])),
    ))
    attention_gradients(1)
    each(rs_one, grad_a[1])()
    each(rs_done, grad_w1)()
    turn_expand()
    w2_back.start()

    h1[...] = dot_nn(lane_tiles(q6), at[0])
    h1[...] += dot_nn(lane_tiles(k6), at[1])
    h1[...] += dot_nn(lane_tiles(v6), at[2])
    gvec[2:3, :] = jnp.sum(lane_tiles(q6).astype(F32), axis=0, keepdims=True)
    gvec[3:4, :] = jnp.sum(lane_tiles(v6).astype(F32), axis=0, keepdims=True)
    each(rs_three, grad_a[0])()

    for moved in result_out:
        moved.wait_send()
    own_out.wait()

    def input_back(s):
        rows = rows_of(s)
        grad, gain_sum, bias_sum = norm_gradient(x_in[s].astype(F32), vec[0:1, :], h1[rows, :])
        stage[s] = (grad + acc[rows, :]).astype(BF16)
        gvec[0:1, :] += gain_sum
        gvec[1:2, :] += bias_sum

    loop(4, input_back)
    gvec_steps = small_sum(gvec, gin, 1)
    gvec_steps[0]()
    own_grad = pltpu.make_async_copy(stage.at[i], ig.at[i], local_sem.at[3])
    own_grad.start()
    grad_out = exchange(stage, ig, 3)
    for moved in grad_out:
        moved.start()

    gvec_steps[1]()
    each(rs_two, grad_a[1])()
    gvec_steps[2]()
    each(rs_done, grad_a[0])()
    gvec_steps[3]()
    each(rs_three, grad_a[1])()
    gvec_steps[4]()
    finish_vectors()
    w1_back.wait()
    each_core(join_expand)
    w2_back.wait()
    each_core(join_reduce)
    each(rs_done, grad_a[1])()

    own_grad.wait()
    for moved in tokens_out + grad_out:
        moved.wait_send()
    for moved in exchange_landed(out, 2) + exchange_landed(ig, 3):
        moved.wait_recv()


def layer(sub, tokens, cotangent, span_mask, vectors, attention, expand, reduce_t):
    zs = GROUPS // 2
    seqs, block, width = tokens.shape
    rows = seqs * block
    columns = attention.shape[2]
    piece = (3 * columns, 128)
    vmem = lambda shape, dtype: pltpu.VMEM(shape, dtype)
    half = (2, 2, 2, zs) + piece
    scratch = [vmem((2,) + half, BF16)] + [vmem(half, BF16)] * 4
    scratch += [vmem((2, 2, 2, zs) + piece, BF16), vmem((6, 2, zs) + piece, BF16)]
    scratch += [vmem((6, zs) + piece, BF16), vmem((6, zs - 1) + piece, BF16)]
    scratch += [vmem(tokens.shape, BF16)] * 3
    scratch += [vmem((16, width), F32)] * 2
    scratch += [vmem((zs + 2, 16, width), F32)] * 2
    scratch += [vmem((16, columns), F32)]
    tiles = vmem((width // 128, rows, 128), BF16)
    flat = vmem((rows, width), BF16)
    turned = vmem((width, rows), BF16)
    scratch += [vmem((4, width, width), BF16), flat, tiles, tiles, tiles, tiles]
    scratch += [vmem((HEADS, rows, rows), BF16), vmem((rows, width), F32), vmem((rows, width), F32)]
    scratch += [flat, vmem((4 * rows, width), BF16), vmem((4 * rows, width), BF16)]
    scratch += [turned, turned, turned, tiles]
    scratch += [vmem(expand.shape, F32), vmem(reduce_t.shape, F32), flat, vmem(tokens.shape, BF16)]
    scratch += [tiles, flat, vmem((columns, width // 2), F32), vmem((2, width), F32), vmem((2, width), F32)]
    scratch += [vmem((2,) + piece, F32), vmem((2,) + piece, F32), vmem((width // 2, 2 * columns), F32)]
    scratch += [vmem((2 * columns, 2 * columns), F32), vmem(piece, F32)]
    scratch += [pltpu.SemaphoreType.DMA((5,))]
    scratch += [pltpu.SemaphoreType.DMA((6, 3 * zs + 4))] * 2
    scratch += [pltpu.SemaphoreType.DMA((8, zs + 3))] * 2
    scratch += [pltpu.SemaphoreType.DMA((4, 3))] * 2
    scratch += [pltpu.SemaphoreType.DMA((2, zs + 2))] * 2
    scratch += [pltpu.SemaphoreType.DMA((8,))] * 2
    in_vmem = pl.BlockSpec(memory_space=pltpu.VMEM)
    anywhere = pl.BlockSpec(memory_space=pl.ANY)
    return pl.pallas_call(
        functools.partial(kernel, sub, zs),
        out_shape=(
            jax.ShapeDtypeStruct(tokens.shape, BF16),
            jax.ShapeDtypeStruct(tokens.shape, BF16),
            jax.ShapeDtypeStruct(attention.shape, F32),
            jax.ShapeDtypeStruct(expand.shape, F32),
            jax.ShapeDtypeStruct(reduce_t.shape, F32),
            jax.ShapeDtypeStruct(vectors.shape, F32),
        ),
        in_specs=[anywhere] * 2 + [in_vmem] * 5,
        out_specs=(anywhere, anywhere) + (in_vmem,) * 4,
        scratch_shapes=scratch,
        compiler_params=pltpu.CompilerParams(
            collective_id=0, has_side_effects=True, vmem_limit_bytes=63 * 1024 * 1024
        ),
    )(tokens, cotangent, span_mask, vectors, attention, expand, reduce_t)


def update_kernel(rates, *refs):
    count = len(rates)
    ins, (result, grad) = refs[: 4 * count], refs[4 * count : 4 * count + 2]
    outs, (result_out, grad_out) = refs[4 * count + 2 : 7 * count + 2], refs[7 * count + 2 : 7 * count + 4]
    held, (low, wide, passed) = refs[7 * count + 4 : 11 * count + 4], refs[11 * count + 4 : 11 * count + 7]
    in_sems, out_sems = refs[11 * count + 7 :]
    loads = [pltpu.make_async_copy(ins[n], held[n], in_sems.at[n]) for n in range(4 * count)]
    stores = [pltpu.make_async_copy(held[4 * n + m], outs[3 * n + m], out_sems.at[3 * n + m])
              for n in range(count) for m in range(3)]
    load_grad = pltpu.make_async_copy(grad, low, in_sems.at[4 * count])
    store_grad = pltpu.make_async_copy(wide, grad_out, out_sems.at[3 * count])
    load_result = pltpu.make_async_copy(result, passed, in_sems.at[4 * count + 1])
    store_result = pltpu.make_async_copy(passed, result_out, out_sems.at[3 * count + 1])
    load_grad.start()
    load_result.start()
    for copy in loads:
        copy.start()
    load_result.wait()
    store_result.start()
    load_grad.wait()

    def widen(s, carry):
        wide[s] = low[s].astype(F32)
        return carry

    lax.fori_loop(0, low.shape[0], widen, 0)
    store_grad.start()
    for n in range(count):
        for m in range(4):
            loads[4 * n + m].wait()
        weight, one, two, gradient = held[4 * n : 4 * n + 4]
        values = adamw(weight[...], one[...], two[...], gradient[...], rates[n])
        for ref, value in zip((weight, one, two), values):
            ref[...] = value
        for m in range(3):
            stores[3 * n + m].start()
    for copy in stores + [store_grad, store_result]:
        copy.wait()


def update(rates, arrays, result, grad):
    flat = [value for group in arrays for value in group]
    new = [jax.ShapeDtypeStruct(value.shape, F32) for group in arrays for value in group[:3]]
    new += [jax.ShapeDtypeStruct(result.shape, BF16), jax.ShapeDtypeStruct(grad.shape, F32)]
    anywhere = pl.BlockSpec(memory_space=pl.ANY)
    scratch = [pltpu.VMEM(value.shape, F32) for value in flat]
    scratch += [pltpu.VMEM(grad.shape, BF16), pltpu.VMEM(grad.shape, F32), pltpu.VMEM(result.shape, BF16)]
    scratch += [pltpu.SemaphoreType.DMA((len(flat) + 2,)), pltpu.SemaphoreType.DMA((len(new),))]
    return pl.pallas_call(
        functools.partial(update_kernel, rates),
        out_shape=tuple(new),
        in_specs=[anywhere] * (len(flat) + 2),
        out_specs=(anywhere,) * len(new),
        scratch_shapes=scratch,
        compiler_params=pltpu.CompilerParams(vmem_limit_bytes=63 * 1024 * 1024),
    )(*flat, result, grad)


def local(
    sub,
    tokens,
    cotangent,
    span_mask,
    attention_weight,
    expand_weight,
    reduce_weight,
    vectors,
    attention_first,
    attention_second,
    expand_first,
    expand_second,
    reduce_first,
    reduce_second,
    vector_first,
    vector_second,
):
    together = [[n * sub + m for m in range(sub)] for n in range(GROUPS)]

    def widen(value, axis):
        if sub == 1:
            return value
        low = lax.all_gather(
            value.astype(BF16), "batch", axis=axis, tiled=True, axis_index_groups=together
        )
        return low.astype(F32)

    def narrow(value, axis):
        if sub == 1:
            return value
        return lax.psum_scatter(
            value, "batch", scatter_dimension=axis, tiled=True, axis_index_groups=together
        )

    out_tokens, input_grad, ga, g1, g2, gv = layer(
        sub,
        tokens,
        cotangent,
        span_mask,
        widen(vectors, 1),
        widen(attention_weight, 2),
        widen(expand_weight, 1),
        widen(reduce_weight.T, 0),
    )
    arrays = (
        (attention_weight, attention_first, attention_second, narrow(ga, 2)),
        (expand_weight, expand_first, expand_second, narrow(g1, 1)),
        (reduce_weight.T, reduce_first.T, reduce_second.T, narrow(g2, 0)),
        (vectors, vector_first, vector_second, narrow(gv, 1)),
    )
    rates = (rate_attention, rate_expand, rate_reduce, rate_vector)
    new = update(rates, arrays, out_tokens, input_grad)
    return new[-2:] + new[0:6] + tuple(value.T for value in new[6:9]) + new[9:12]


def solution(mesh):
    sub = mesh.shape["batch"] // GROUPS
    sequences = P("batch", "blk", None)
    attention = P(None, "blk", "batch")
    matrix = P("blk", "batch")
    return jax.shard_map(
        functools.partial(local, sub),
        mesh=mesh,
        in_specs=(sequences, sequences, P("batch", "blk"), attention, matrix, matrix, matrix)
        + (attention,) * 2
        + (matrix,) * 6,
        out_specs=(sequences,) * 2 + (attention,) * 3 + (matrix,) * 9,
        check_vma=False,
    )
```

```python
import functools
import math

import jax
import jax.numpy as jnp
from jax import lax
from jax.experimental import pallas as pl
from jax.experimental.pallas import tpu as pltpu
from jax.sharding import PartitionSpec as P

HEADS = 12
HEAD = 64
STEP = 10
GROUPS = 8

norm_epsilon = 1e-05
beta_one = 0.9
beta_two = 0.999
adam_epsilon = 1e-08
decay_weight = 0.1
rate_attention = 0.05
rate_expand = 0.03
rate_reduce = 0.015
rate_vector = 0.4

F32 = jnp.float32
BF16 = jnp.bfloat16
MESH = pl.DeviceIdType.MESH
GELU_SCALE = math.sqrt(2.0 / math.pi)
GELU_CUBE = 0.044715


def adamw(weight, moment_one, moment_two, gradient, step_rate):
    moment_one = beta_one * moment_one + (1.0 - beta_one) * gradient
    moment_two = beta_two * moment_two + (1.0 - beta_two) * gradient * gradient
    corrected_one = moment_one / (1.0 - beta_one**STEP)
    corrected_two = moment_two / (1.0 - beta_two**STEP)
    updated = weight - step_rate * (
        corrected_one / (jnp.sqrt(corrected_two) + adam_epsilon) + decay_weight * weight
    )
    return (updated, moment_one, moment_two)


def dot_nn(left, right):
    return lax.dot_general(left, right, (((1,), (0,)), ((), ())), preferred_element_type=F32)


def dot_nt(left, right):
    return lax.dot_general(left, right, (((1,), (1,)), ((), ())), preferred_element_type=F32)


def lane_tiles(ref, count=6):
    return jnp.concatenate([ref[t] for t in range(count)], axis=1)


class Unit:
    def __init__(self, order, u, long_axis, fine):
        self.order, self.u, self.long_axis, self.fine = order, u, long_axis, fine


class Gradient:
    def __init__(self, order, u, long_axis, first, count, whole, core_in, long_in, mid_in, line_in, finish):
        self.order, self.long_axis, self.first, self.count, self.whole = order, long_axis, first, count, whole
        self.u, self.core_in, self.long_in, self.mid_in, self.line_in = u, core_in, long_in, mid_in, line_in
        self.finish = finish


def kernel(sub, zs, *refs):
    (tok, cot, mask_in, vec_in, a_in, w1_in, w2_in,
     out, ig, ga, g1, g2, gv,
     ubuf, core_in, long_in, mid_in, line_in,
     x_in, cot_in, stage, vec, gvec, vin, gin, narrow_rows,
     at, n1, q6, k6, v6, o6, pt, h1, acc, n2, act, gp, ta, tb, tc, d6,
     local_sem, ag_send, ag_recv, rs_send, rs_recv, a2a_send, a2a_recv, v_send, v_recv) = refs

    i = lax.axis_index("blk")
    b = lax.axis_index("batch")
    c, y = lax.rem(i, 2), lax.div(i, 2)
    g, r = lax.div(b, sub), lax.rem(b, sub)
    x, z = lax.rem(g, 2), lax.div(g, 2)

    def device(c_=c, y_=y, x_=x, z_=z):
        return {"blk": 2 * y_ + c_, "batch": (2 * z_ + x_) * sub + r}

    def z_at(k):
        return lax.rem(z + k, zs)

    def block_at(k):
        return lax.rem(i + k, 4)

    def copy(src, dst, send, recv, to):
        return pltpu.make_async_remote_copy(
            src_ref=src, dst_ref=dst, send_sem=send, recv_sem=recv, device_id=to, device_id_type=MESH
        )

    def loop(count, body, hooks=()):
        def step(s, carry):
            body(s)
            for k, *todo in hooks:

                @pl.when(s == k)
                def _():
                    for f in todo:
                        f()

            return carry

        lax.fori_loop(0, count, step, 0)

    partners = [device(z_=z_at(k)) for k in range(1, zs)]
    partners += [device(x_=1 - x), device(y_=1 - y), device(c_=1 - c), device(c_=1 - c, y_=1 - y)]
    barrier = pltpu.get_barrier_semaphore()
    for partner in partners:
        pl.semaphore_signal(barrier, inc=1, device_id=partner, device_id_type=MESH)
    pl.semaphore_wait(barrier, len(partners))

    def ag_sems(n, slot):
        return ag_send.at[n.order, slot], ag_recv.at[n.order, slot]

    def group(n, u, long_off, mid_off, cut=None):
        yy = y if (long_off if n.long_axis == "y" else mid_off) == 0 else 1 - y
        xx = x if (long_off if n.long_axis == "x" else mid_off) == 0 else 1 - x
        return u.at[c, yy, xx] if cut is None else u.at[c, yy, xx, cut]

    def partner_of(n, step):
        axis = n.long_axis if step == "long" else {"x": "y", "y": "x"}[n.long_axis]
        return device(x_=1 - x) if axis == "x" else device(y_=1 - y)

    LINE, MID, LONG, LAST, CORE = 0, zs - 1, 2 * zs - 1, 3 * zs - 1, 3 * zs

    def ag_line(n, k, landed=False):
        ref = group(n, n.u, 0, 0, z_at(zs - k) if landed else z)
        return copy(ref, ref, *ag_sems(n, LINE + k - 1), device(z_=z_at(k)))

    def ag_first(n, step, k, landed=False):
        cut = z_at(zs - k) if n.fine else None
        off = (0, 1) if step == "mid" else (1, 0)
        ref = group(n, n.u, *(off if landed else (0, 0)), cut)
        return copy(ref, ref, *ag_sems(n, (MID if step == "mid" else LONG) + k), partner_of(n, step))

    def ag_last(n, landed=False):
        ref = group(n, n.u, 1 if landed else 0, 1)
        return copy(ref, ref, *ag_sems(n, LAST), partner_of(n, "long"))

    def ag_core(n, long_off, mid_off, landed=False):
        ref = group(n, n.u, long_off, mid_off)
        if landed:
            yy = y if (long_off if n.long_axis == "y" else mid_off) == 0 else 1 - y
            xx = x if (long_off if n.long_axis == "x" else mid_off) == 0 else 1 - x
            ref = n.u.at[1 - c, yy, xx]
        return copy(ref, ref, *ag_sems(n, CORE + 2 * long_off + mid_off), device(c_=1 - c))

    def parts(n):
        return range(zs) if n.fine else range(1)

    def ag_start(n):
        if n.fine:
            for step in ("mid", "long"):
                ag_first(n, step, 0).start()
        for k in range(1, zs):
            ag_line(n, k).start()

    def ag_piece(n, k):
        ag_line(n, k, True).wait_recv()
        for step in ("mid", "long"):
            ag_first(n, step, k).start()

    def ag_one(n):
        if not n.fine:
            for k in range(1, zs):
                ag_line(n, k, True).wait_recv()
            for step in ("mid", "long"):
                ag_first(n, step, 0).start()
        ag_core(n, 0, 0).start()

    def ag_two(n):
        for k in parts(n):
            ag_first(n, "mid", k, True).wait_recv()
        ag_last(n).start()
        ag_core(n, 0, 1).start()

    def ag_three(n):
        for k in parts(n):
            ag_first(n, "long", k, True).wait_recv()
        ag_core(n, 1, 0).start()

    def ag_four(n):
        ag_last(n, True).wait_recv()
        ag_core(n, 1, 1).start()

    def ag_done(n):
        for off in ((0, 0), (0, 1), (1, 0), (1, 1)):
            ag_core(n, *off, True).wait_recv()
        for k in range(1, zs):
            ag_line(n, k).wait_send()
        for step in ("mid", "long"):
            for k in parts(n):
                ag_first(n, step, k).wait_send()
        ag_last(n).wait_send()
        for off in ((0, 0), (0, 1), (1, 0), (1, 1)):
            ag_core(n, *off).wait_send()

    def rs_sems(n, slot):
        return rs_send.at[n.order, slot], rs_recv.at[n.order, slot]

    def cut_of(n):
        return slice(None) if n.count == zs else pl.ds(n.first, n.count)

    def rs_core(n, long_off):
        place = 1 - (y if n.long_axis == "y" else x) if long_off else (y if n.long_axis == "y" else x)
        where = (place, slice(None)) if n.long_axis == "y" else (slice(None), place)
        return copy(n.u.at[(1 - c,) + where + (cut_of(n),)], n.core_in.at[where],
                    *rs_sems(n, long_off), device(c_=1 - c))

    def rs_long(n):
        where = (1 - y, slice(None)) if n.long_axis == "y" else (slice(None), 1 - x)
        return copy(n.u.at[(c,) + where + (cut_of(n),)], n.long_in, *rs_sems(n, 2), partner_of(n, "long"))

    def rs_mid(n):
        return copy(group(n, n.u, 0, 1, cut_of(n)), n.mid_in, *rs_sems(n, 3), partner_of(n, "mid"))

    def rs_line(n, k):
        return copy(group(n, n.u, 0, 0, z_at(k)), n.line_in.at[k - 1], *rs_sems(n, 3 + k), device(z_=z_at(k)))

    def within(n, place):
        return jnp.logical_and(place >= n.first, place < n.first + n.count)

    def when_within(n, place, f):
        if n.whole:
            f()
        else:
            pl.when(within(n, place))(f)

    def gather_terms(n, long_off, mid_off, names):
        yy = y if (long_off if n.long_axis == "y" else mid_off) == 0 else 1 - y
        xx = x if (long_off if n.long_axis == "x" else mid_off) == 0 else 1 - x

        def body(s):
            mine = n.u.at[c, yy, xx, n.first + s]
            value = mine[...].astype(F32) + n.core_in[yy, xx, s].astype(F32)
            if "long" in names:
                value = value + n.long_in[xx if n.long_axis == "y" else yy, s].astype(F32)
            if "mid" in names:
                value = value + n.mid_in[s].astype(F32)
            mine[...] = value.astype(BF16)

        loop(n.count, body)

    def rs_zero(n):
        rs_core(n, 1).start()
        rs_core(n, 0).start()

    def rs_one(n):
        rs_core(n, 1).wait_recv()
        gather_terms(n, 1, 0, ())
        gather_terms(n, 1, 1, ())
        rs_long(n).start()

    def rs_two(n):
        rs_core(n, 0).wait_recv()
        rs_long(n).wait_recv()
        gather_terms(n, 0, 1, ("long",))
        rs_mid(n).start()

    def rs_three(n):
        rs_mid(n).wait_recv()
        gather_terms(n, 0, 0, ("long", "mid"))
        for k in range(1, zs):
            when_within(n, z_at(k), lambda k=k: rs_line(n, k).start())

    def rs_done(n):
        def finish():
            for k in range(1, zs):
                rs_line(n, k).wait_recv()
            value = n.u[c, y, x, z].astype(F32)
            for k in range(1, zs):
                value = value + n.line_in[k - 1].astype(F32)
            n.finish(value)

        when_within(n, z, finish)
        for moved in (rs_core(n, 0), rs_core(n, 1), rs_long(n), rs_mid(n)):
            moved.wait_send()
        for k in range(1, zs):
            when_within(n, z_at(k), lambda k=k: rs_line(n, k).wait_send())

    def small_sum(ref, slots, which):
        to = (device(y_=1 - y), device(c_=1 - c), device(x_=1 - x))
        to += tuple(device(z_=z_at(k)) for k in range(1, zs))

        def moved(slot):
            return copy(ref, slots.at[slot], v_send.at[which, slot], v_recv.at[which, slot], to[slot])

        def land(last):
            moved(last).wait()
            ref[...] = ref[...] + slots[last]

        def step(n):
            def run():
                if n > 0:
                    land(n - 1)
                moved(n).start()

            return run

        def line():
            land(2)
            for k in range(1, zs):
                moved(2 + k).start()

        def finish():
            for k in range(1, zs):
                moved(2 + k).wait()
            value = ref[...]
            for k in range(1, zs):
                value = value + slots[2 + k]
            ref[...] = value

        return [step(0), step(1), step(2), line, finish]

    def rows_of(s):
        return pl.ds(pl.multiple_of(s * 128, 128), 128)

    def exchange(src, dst, which):
        return [copy(src.at[block_at(k)], dst.at[i], a2a_send.at[which, k - 1],
                     a2a_recv.at[which, k - 1], {"blk": block_at(k), "batch": b})
                for k in range(1, 4)]

    def exchange_landed(dst, which):
        return [copy(dst.at[block_at(4 - k)], dst.at[block_at(4 - k)], a2a_send.at[which, k - 1],
                     a2a_recv.at[which, k - 1], {"blk": block_at(4 - k), "batch": b})
                for k in range(1, 4)]

    units = [Unit(2 * n + half, ubuf.at[n, half], axes[half], n == 0)
             for n, axes in enumerate(("xy", "xy", "xx")) for half in range(2)]
    unit_qk, unit_vo, unit_w1, unit_w2 = units[0], units[1], units[2:4], units[4:6]

    def rest_rows(matrix):
        return a_in[matrix, pl.ds(pl.multiple_of(128 * (1 - c), 64), 64), :]

    def own_attention(p):
        mine = ubuf.at[0, p, c, y, x, z]
        for m in range(2):
            main = a_in[2 * p + m, pl.ds(pl.multiple_of(64 * c, 64), 128), :]
            mine[96 * m : 96 * m + 96, :] = main.T.astype(BF16)
        rest = jnp.concatenate([rest_rows(2 * p + c), rest_rows(2 * p + 1 - c)], axis=0)
        mine[192:288, :] = rest.T.astype(BF16)

    def own_feed_forward():
        for h in range(2):
            for t in range(3):
                ubuf[1, h, c, y, x, z, 96 * t : 96 * t + 96, :] = w1_in[
                    96 * h : 96 * h + 96, 128 * t : 128 * t + 128
                ].astype(BF16)
            for t in range(6):
                ubuf[2, h, c, y, x, z, 48 * t : 48 * t + 48, :] = w2_in[
                    48 * h : 48 * h + 48, 128 * t : 128 * t + 128
                ].astype(BF16)

    columns = a_in.shape[2]
    placed = lax.broadcasted_iota(jnp.int32, (columns, 768), 1) == (
        lax.broadcasted_iota(jnp.int32, (columns, 768), 0) + columns * g
    )

    def own_vectors():
        vec[...] = jnp.zeros_like(vec)
        rows = dot_nn(vec_in[...].astype(BF16), jnp.where(placed, 1.0, 0.0).astype(BF16))
        for j in range(3):
            vec[pl.ds(3 * i + j, 1), :] = rows[j : j + 1, :]

    load_cot = pltpu.make_async_copy(cot, stage, local_sem.at[4])

    def masked_cotangent():
        load_cot.wait()
        eye = lax.broadcasted_iota(jnp.int32, (128, 128), 0) == lax.broadcasted_iota(jnp.int32, (128, 128), 1)
        for s in range(4):
            row = jnp.broadcast_to(mask_in[s : s + 1, :].astype(F32), (128, 128))
            column = jnp.sum(jnp.where(eye, row, 0.0), axis=1, keepdims=True)
            stage[s] = (stage[s].astype(F32) * column).astype(BF16)

    def finish_attention(p):
        def finish(value):
            for m in range(2):
                ga[2 * p + m, pl.ds(pl.multiple_of(64 * c, 64), 128), :] = value[96 * m : 96 * m + 96, :].T
            rest = value[192:288, :].T
            rows = pl.ds(pl.multiple_of(128 * (1 - c), 64), 64)
            ga[2 * p + c, rows, :] = rest[0:64, :]
            ga[2 * p + 1 - c, rows, :] = rest[64:128, :]

        return finish

    def finish_expand(h):
        def finish(value):
            for t in range(3):
                g1[96 * h : 96 * h + 96, 128 * t : 128 * t + 128] = value[96 * t : 96 * t + 96, :]

        return finish

    def finish_reduce(h):
        def finish(value):
            for t in range(6):
                g2[48 * h : 48 * h + 48, 128 * t : 128 * t + 128] = value[48 * t : 48 * t + 48, :]

        return finish

    def finish_vectors():
        value, total = gvec[...], 0.0
        for _ in range(3):
            part = value.astype(BF16)
            total = total + dot_nt(part, jnp.where(placed, 1.0, 0.0).astype(BF16))
            value = value - part.astype(F32)
        narrow_rows[...] = total
        for j in range(3):
            gv[j : j + 1, :] = narrow_rows[pl.ds(3 * i + j, 1), :]

    grads = []
    half_zs = zs // 2
    for n, (source, finish, axes) in enumerate(((0, finish_reduce, "xx"), (2, finish_expand, "yx"))):
        for half in range(2):
            order = 2 * n + half
            grads.append(Gradient(order, ubuf.at[source, half], axes[half], 0, zs, True,
                                  core_in.at[order], long_in.at[order], mid_in.at[order],
                                  line_in.at[order], finish(half)))
    for part in range(2):
        for half in range(2):
            cut = pl.ds(part * half_zs, half_zs)
            grads.append(Gradient(4 + 2 * part + half, ubuf.at[1, half], "xy"[half], part * half_zs, half_zs,
                                  False, core_in.at[4 + half, :, :, cut], long_in.at[4 + half, :, cut],
                                  mid_in.at[4 + half, cut], line_in.at[4 + half], finish_attention(half)))
    grad_w2, grad_w1, grad_a = grads[0:2], grads[2:4], (grads[4:6], grads[6:8])

    def each(f, which):
        def run():
            for n in which:
                f(n)

        return run

    load_tokens = [pltpu.make_async_copy(tok.at[s], n2.at[128 * s : 128 * s + 128], local_sem.at[5 + s])
                   for s in range(4)]
    for s in range(4):
        load_tokens[s].start()
    load_cot.start()
    own_attention(0)
    ag_start(unit_qk)
    own_vectors()
    vec_steps = small_sum(vec, vin, 0)
    vec_steps[0]()
    for s in range(4):
        load_tokens[s].wait()
    own_tokens = pltpu.make_async_copy(n2.at[rows_of(i)], x_in.at[i], local_sem.at[0])
    own_tokens.start()
    tokens_out = [copy(n2.at[rows_of(block_at(k))], x_in.at[i], a2a_send.at[0, k - 1], a2a_recv.at[0, k - 1],
                       {"blk": block_at(k), "batch": b}) for k in range(1, 4)]
    for moved in tokens_out:
        moved.start()
    own_attention(1)
    own_feed_forward()
    for k in range(1, zs):
        ag_piece(unit_qk, k)
    ag_one(unit_qk)
    ag_start(unit_vo)
    ag_start(unit_w1[0])
    vec_steps[1]()
    masked_cotangent()
    ag_two(unit_qk)
    vec_steps[2]()
    for k in range(1, zs):
        ag_piece(unit_vo, k)
    ag_one(unit_vo)
    ag_start(unit_w1[1])
    vec_steps[3]()
    ag_three(unit_qk)

    for moved in exchange_landed(x_in, 0):
        moved.wait_recv()
    own_tokens.wait()
    vec_steps[4]()

    def normalise(value):
        centered = value - jnp.mean(value, axis=-1, keepdims=True)
        scale = lax.rsqrt(jnp.mean(centered * centered, axis=-1, keepdims=True) + norm_epsilon)
        return centered * scale, scale

    def first_norm(s):
        unit, _ = normalise(x_in[s].astype(F32))
        n1[rows_of(s), :] = (unit * vec[0:1, :] + vec[1:2, :]).astype(BF16)

    loop(4, first_norm)
    ag_four(unit_qk)
    own_cot = pltpu.make_async_copy(stage.at[i], cot_in.at[i], local_sem.at[1])
    own_cot.start()
    cot_out = exchange(stage, cot_in, 1)
    for moved in cot_out:
        moved.start()
    ag_done(unit_qk)

    lanes = lax.broadcasted_iota(jnp.int32, (96, 128), 1)

    def unpack(p, s):
        for xx in range(2):
            rows = pl.ds(pl.multiple_of((2 * s + xx) * 96, 96), 96)
            for yy in range(2):
                first, second = ubuf.at[0, p, 0, yy, xx, s], ubuf.at[0, p, 1, yy, xx, s]
                lo, hi = 384 * yy, 384 * yy + 256
                for m in range(2):
                    at[2 * p + m, rows, lo : lo + 128] = first[96 * m : 96 * m + 96, :]
                    at[2 * p + m, rows, hi : hi + 128] = second[96 * m : 96 * m + 96, :]
                rest_first = first[192:288, :].astype(F32)
                rest_second = second[192:288, :].astype(F32)
                even = jnp.where(lanes < 64, rest_first, rest_second)
                odd = pltpu.roll(jnp.where(lanes < 64, rest_second, rest_first), 64, 1)
                at[2 * p, rows, lo + 128 : lo + 256] = even.astype(BF16)
                at[2 * p + 1, rows, lo + 128 : lo + 256] = odd.astype(BF16)

    def project(m, dst, bias):
        for n in range(3):
            value = dot_nt(n1[...], at[m, 256 * n : 256 * n + 256, :])
            if bias is not None:
                value = value + vec[bias : bias + 1, 256 * n : 256 * n + 256]
            value = value.astype(BF16)
            if m == 0:
                value = value * jnp.asarray(HEAD ** (-0.5), BF16)
            dst[2 * n] = value[:, 0:128]
            dst[2 * n + 1] = value[:, 128:256]

    loop(zs, functools.partial(unpack, 0))
    project(0, q6, 2)
    ag_two(unit_vo)
    project(1, k6, None)
    ag_one(unit_w1[0])

    half_lane = lax.broadcasted_iota(jnp.int32, (512, 128), 1) // HEAD

    def half_of(value, which):
        return jnp.where(half_lane == which, value, jnp.zeros_like(value))

    def turn(value):
        return value.astype(F32).T.astype(BF16)

    def attend(p):
        queries, keys = q6[p], k6[p]
        for which in range(2):
            scores = dot_nt(half_of(keys, which), queries)
            expo = jnp.exp(scores - jnp.max(scores, axis=0, keepdims=True))
            probs = (expo * (1.0 / jnp.sum(expo, axis=0, keepdims=True))).astype(BF16)
            pt[2 * p + which] = probs

    def mix(p):
        values_t = turn(v6[p])
        mixed = [dot_nn(values_t[64 * which : 64 * which + 64, :], pt[2 * p + which]) for which in range(2)]
        o6[p] = jnp.concatenate(mixed, axis=0).T.astype(BF16)

    loop(6, attend, (
        (1, lambda: ag_three(unit_vo)),
        (2, lambda: ag_one(unit_w1[1]), each(ag_start, unit_w2)),
        (3, lambda: ag_four(unit_vo), lambda: ag_two(unit_w1[0])),
    ))
    ag_two(unit_w1[1])
    ag_done(unit_vo)
    loop(zs, functools.partial(unpack, 1))
    project(2, v6, 3)
    each(ag_three, unit_w1)()
    loop(6, mix, (
        (1, lambda: ag_one(unit_w2[0])),
        (3, each(ag_four, unit_w1), lambda: ag_one(unit_w2[1])),
        (5, lambda: ag_two(unit_w2[0])),
    ))

    for n in range(3):
        cols = slice(256 * n, 256 * n + 256)
        value = dot_nt(lane_tiles(o6), at[3, cols, :]) + vec[4:5, cols]
        for s in range(4):
            h1[128 * s : 128 * s + 128, cols] = x_in[s, :, cols].astype(F32) + value[128 * s : 128 * s + 128]

    def second_norm(s):
        unit, _ = normalise(h1[rows_of(s), :])
        n2[rows_of(s), :] = (unit * vec[5:6, :] + vec[6:7, :]).astype(BF16)

    for moved in tokens_out:
        moved.wait_send()
    loop(4, second_norm)
    each(ag_done, unit_w1)()
    ag_two(unit_w2[1])

    def expand_piece(s, xx):
        def piece(ref):
            return jnp.concatenate([ref[96 * t : 96 * t + 96, :] for t in range(3)], axis=1)

        return jnp.concatenate(
            [piece(ubuf.at[1, h, cc, yy, xx, s]) for yy in range(2) for cc in range(2) for h in range(2)],
            axis=0,
        )

    def reduce_block(s):
        yy, cc = lax.div(s, 2), lax.rem(s, 2)

        def piece(ref):
            return jnp.concatenate([ref[48 * t : 48 * t + 48, :] for t in range(6)], axis=1)

        return jnp.concatenate(
            [piece(ubuf.at[2, h, cc, yy, xx, zz]) for zz in range(zs) for xx in range(2) for h in range(2)],
            axis=0,
        )

    def block_rows(s):
        return pl.ds(pl.multiple_of(s * 512, 512), 512)

    def expand(s):
        for xx in range(2):
            cols = slice(384 * xx, 384 * xx + 384)
            inner = dot_nn(n2[...], expand_piece(s, xx)) + vec[pl.ds(8 + s, 1), cols]
            square = inner * inner
            tanh = jnp.tanh(GELU_SCALE * inner * (1.0 + GELU_CUBE * square))
            act[block_rows(s), cols] = (0.5 * inner * (1.0 + tanh)).astype(BF16)
            slope = 0.5 * (1.0 + tanh) + 0.5 * inner * (1.0 - tanh * tanh) * (
                GELU_SCALE * (1.0 + 3.0 * GELU_CUBE * square)
            )
            gp[block_rows(s), cols] = slope.astype(BF16)

    loop(4, expand, (
        (1, each(ag_three, unit_w2)),
        (3, lambda: ag_four(unit_w2[0])),
    ))

    for moved in exchange_landed(cot_in, 1):
        moved.wait_recv()
    own_cot.wait()
    gvec[...] = jnp.zeros_like(gvec)

    def transpose_rows(dst, s, value):
        dst[:, 128 * s : 128 * s + 128] = turn(value)

    total = jnp.zeros((1, 768), F32)
    for s in range(4):
        transpose_rows(ta, s, cot_in[s])
        total = total + jnp.sum(cot_in[s].astype(F32), axis=0, keepdims=True)
    gvec[7:8, :] = total

    def reduce_back(s):
        yy, cc = lax.div(s, 2), lax.rem(s, 2)
        grad = dot_nn(ta[...], act[block_rows(s), :]).astype(BF16)
        for zz in range(zs):
            for xx in range(2):
                for h in range(2):
                    row = 96 * (2 * zz + xx) + 48 * h
                    for t in range(6):
                        ubuf[0, h, cc, yy, xx, zz, 48 * t : 48 * t + 48, :] = grad[
                            row : row + 48, 128 * t : 128 * t + 128
                        ]

    loop(4, reduce_back)
    each(rs_zero, grad_w2)()
    ag_four(unit_w2[1])
    each(rs_one, grad_w2)()
    each(ag_done, unit_w2)()

    def cotangent_rows():
        return jnp.concatenate([cot_in[s] for s in range(4)], axis=0)

    def inner_back(s):
        grad = dot_nn(cotangent_rows(), reduce_block(s)) * gp[block_rows(s), :].astype(F32)
        low = grad.astype(BF16)
        gp[block_rows(s), :] = low
        gvec[pl.ds(8 + s, 1), :] = jnp.sum(low.astype(F32), axis=0, keepdims=True)

    loop(4, inner_back)

    acc[...] = h1[...] + vec[7:8, :]

    def reduce(s):
        acc[...] += dot_nt(act[block_rows(s), :], reduce_block(s))

    loop(4, reduce)
    for moved in cot_out:
        moved.wait_send()
    for s in range(4):
        stage[s] = acc[128 * s : 128 * s + 128, :].astype(BF16)
    own_out = pltpu.make_async_copy(stage.at[i], out.at[i], local_sem.at[2])
    own_out.start()
    result_out = exchange(stage, out, 2)
    for moved in result_out:
        moved.start()

    for s in range(4):
        transpose_rows(tb, s, n2[128 * s : 128 * s + 128, :])

    def expand_back(s):
        for xx in range(2):
            grad = dot_nn(tb[...], gp[block_rows(s), 384 * xx : 384 * xx + 384]).astype(BF16)
            for yy in range(2):
                for cc in range(2):
                    for h in range(2):
                        row = 192 * (2 * yy + cc) + 96 * h
                        for t in range(3):
                            ubuf[2, h, cc, yy, xx, s, 96 * t : 96 * t + 96, :] = grad[
                                row : row + 96, 128 * t : 128 * t + 128
                            ]

    loop(4, expand_back)
    each(rs_zero, grad_w1)()
    each(rs_two, grad_w2)()

    def norm_back(s):
        whole = jnp.concatenate([expand_piece(s, 0), expand_piece(s, 1)], axis=1)
        part = dot_nt(gp[block_rows(s), :], whole)

        @pl.when(s == 0)
        def _():
            acc[...] = part

        @pl.when(s > 0)
        def _():
            acc[...] += part

    loop(4, norm_back, ((1, each(rs_one, grad_w1)),))

    def norm_gradient(value, scale_row, grad):
        unit, scale = normalise(value)
        gain_sum = jnp.sum(grad * unit, axis=0, keepdims=True)
        bias_sum = jnp.sum(grad, axis=0, keepdims=True)
        inner = grad * scale_row
        mean = jnp.mean(inner, axis=-1, keepdims=True)
        along = jnp.mean(inner * unit, axis=-1, keepdims=True)
        return scale * (inner - mean - unit * along), gain_sum, bias_sum

    def hidden_back(s):
        rows = rows_of(s)
        grad, gain_sum, bias_sum = norm_gradient(h1[rows, :], vec[5:6, :], acc[rows, :])
        grad = grad + cot_in[s].astype(F32)
        h1[rows, :] = grad
        low = grad.astype(BF16)
        n2[rows, :] = low
        gvec[5:6, :] += gain_sum
        gvec[6:7, :] += bias_sum
        gvec[4:5, :] += jnp.sum(low.astype(F32), axis=0, keepdims=True)

    loop(4, hidden_back)

    for n in range(3):
        value = dot_nn(n2[...], at[3, :, 256 * n : 256 * n + 256]).astype(BF16)
        d6[2 * n] = value[:, 0:128]
        d6[2 * n + 1] = value[:, 128:256]
    for s in range(4):
        transpose_rows(tc, s, n2[128 * s : 128 * s + 128, :])
    act[768:1536, :] = dot_nn(tc[...], lane_tiles(o6)).astype(BF16)
    each(rs_three, grad_w2)()

    def attend_back(p):
        rows = rows_of(p)
        queries, keys, values, grads_in = q6[p], k6[p], v6[p], d6[p]
        keys_t = turn(keys)
        grad_query, grad_key, grad_value = [], 0.0, 0.0
        for which in range(2):
            probs = pt[2 * p + which]
            wide = probs.astype(F32)
            grad_probs = dot_nt(half_of(values, which), grads_in)
            inner = jnp.sum(wide * grad_probs, axis=0, keepdims=True)
            grad_scores = (wide * (grad_probs - inner)).astype(BF16)
            grad_query.append(dot_nn(keys_t[64 * which : 64 * which + 64, :], grad_scores))
            grad_key = grad_key + dot_nn(grad_scores, half_of(queries, which))
            grad_value = grad_value + dot_nn(probs, half_of(grads_in, which))
        grad_query = jnp.concatenate(grad_query, axis=0) * HEAD ** (-0.5)
        ta[rows, :] = grad_query.astype(BF16)
        tb[rows, :] = grad_key.T.astype(BF16)
        tc[rows, :] = grad_value.T.astype(BF16)
        q6[p] = grad_query.T.astype(BF16)
        k6[p] = grad_key.astype(BF16)
        v6[p] = grad_value.astype(BF16)

    def pack(p, part, first_row, second_row):
        def body(s):
            for xx in range(2):
                offset = (2 * s + xx) * 96
                rows = [pl.ds(pl.multiple_of(first_row + offset, 96), 96),
                        pl.ds(pl.multiple_of(second_row + offset, 96), 96)]
                first = ubuf.at[1, p, 0, :, xx, part * half_zs + s]
                second = ubuf.at[1, p, 1, :, xx, part * half_zs + s]
                for yy in range(2):
                    lo, mid, hi = 384 * yy, 384 * yy + 128, 384 * yy + 256
                    for m in range(2):
                        first[yy, 96 * m : 96 * m + 96, :] = act[rows[m], lo : lo + 128]
                        second[yy, 96 * m : 96 * m + 96, :] = act[rows[m], hi : hi + 128]
                    even = act[rows[0], mid : mid + 128].astype(F32)
                    odd = pltpu.roll(act[rows[1], mid : mid + 128].astype(F32), 64, 1)
                    first[yy, 192:288, :] = jnp.where(lanes < 64, even, odd).astype(BF16)
                    second[yy, 192:288, :] = jnp.where(lanes < 64, odd, even).astype(BF16)

        loop(half_zs, body)

    def attention_gradients(part):
        rows = slice(384 * part, 384 * part + 384)
        act[1536:1920, :] = dot_nn(tc[rows, :], n1[...]).astype(BF16)
        pack(1, part, 1536, 768 + 384 * part)
        rs_zero(grad_a[part][1])
        act[0:384, :] = dot_nn(ta[rows, :], n1[...]).astype(BF16)
        act[384:768, :] = dot_nn(tb[rows, :], n1[...]).astype(BF16)
        pack(0, part, 0, 384)
        rs_zero(grad_a[part][0])

    loop(3, attend_back, ((0, each(rs_two, grad_w1)), (1, each(rs_done, grad_w2))))
    attention_gradients(0)
    loop(3, lambda p: attend_back(p + 3), (
        (0, each(rs_one, grad_a[0])),
        (1, each(rs_three, grad_w1)),
        (2, each(rs_two, grad_a[0])),
    ))
    attention_gradients(1)
    each(rs_one, grad_a[1])()
    each(rs_done, grad_w1)()

    acc[...] = dot_nn(lane_tiles(q6), at[0])
    acc[...] += dot_nn(lane_tiles(k6), at[1])
    acc[...] += dot_nn(lane_tiles(v6), at[2])
    gvec[2:3, :] = jnp.sum(lane_tiles(q6).astype(F32), axis=0, keepdims=True)
    gvec[3:4, :] = jnp.sum(lane_tiles(v6).astype(F32), axis=0, keepdims=True)
    each(rs_three, grad_a[0])()

    for moved in result_out:
        moved.wait_send()
    own_out.wait()

    def input_back(s):
        rows = rows_of(s)
        grad, gain_sum, bias_sum = norm_gradient(x_in[s].astype(F32), vec[0:1, :], acc[rows, :])
        stage[s] = (grad + h1[rows, :]).astype(BF16)
        gvec[0:1, :] += gain_sum
        gvec[1:2, :] += bias_sum

    loop(4, input_back)
    gvec_steps = small_sum(gvec, gin, 1)
    gvec_steps[0]()
    own_grad = pltpu.make_async_copy(stage.at[i], ig.at[i], local_sem.at[3])
    own_grad.start()
    grad_out = exchange(stage, ig, 3)
    for moved in grad_out:
        moved.start()

    gvec_steps[1]()
    each(rs_two, grad_a[1])()
    gvec_steps[2]()
    each(rs_done, grad_a[0])()
    gvec_steps[3]()
    each(rs_three, grad_a[1])()
    gvec_steps[4]()
    finish_vectors()
    each(rs_done, grad_a[1])()

    own_grad.wait()
    for moved in grad_out:
        moved.wait_send()
    for moved in exchange_landed(out, 2) + exchange_landed(ig, 3):
        moved.wait_recv()


def layer(sub, tokens, cotangent, span_mask, vectors, attention, expand, reduce_t):
    zs = GROUPS // 2
    seqs, block, width = tokens.shape
    rows = seqs * block
    columns = attention.shape[2]
    piece = (3 * columns, 128)
    vmem = lambda shape, dtype: pltpu.VMEM(shape, dtype)
    scratch = [vmem((3, 2, 2, 2, 2, zs) + piece, BF16)]
    scratch += [vmem((6, 2, 2, zs) + piece, BF16), vmem((6, 2, zs) + piece, BF16)]
    scratch += [vmem((6, zs) + piece, BF16), vmem((6, zs - 1) + piece, BF16)]
    scratch += [vmem(tokens.shape, BF16)] * 3
    scratch += [vmem((16, width), F32)] * 2
    scratch += [vmem((zs + 2, 16, width), F32)] * 2
    scratch += [vmem((16, columns), F32)]
    tiles = vmem((width // 128, rows, 128), BF16)
    flat = vmem((rows, width), BF16)
    turned = vmem((width, rows), BF16)
    scratch += [vmem((4, width, width), BF16), flat, tiles, tiles, tiles, tiles]
    scratch += [vmem((HEADS, rows, rows), BF16), vmem((rows, width), F32), vmem((rows, width), F32)]
    scratch += [flat, vmem((4 * rows, width), BF16), vmem((4 * rows, width), BF16)]
    scratch += [turned, turned, turned, tiles]
    scratch += [pltpu.SemaphoreType.DMA((9,))]
    scratch += [pltpu.SemaphoreType.DMA((6, 3 * zs + 4))] * 2
    scratch += [pltpu.SemaphoreType.DMA((8, zs + 3))] * 2
    scratch += [pltpu.SemaphoreType.DMA((4, 3))] * 2
    scratch += [pltpu.SemaphoreType.DMA((2, zs + 2))] * 2
    in_vmem = pl.BlockSpec(memory_space=pltpu.VMEM)
    anywhere = pl.BlockSpec(memory_space=pl.ANY)
    return pl.pallas_call(
        functools.partial(kernel, sub, zs),
        out_shape=(
            jax.ShapeDtypeStruct(tokens.shape, BF16),
            jax.ShapeDtypeStruct(tokens.shape, BF16),
            jax.ShapeDtypeStruct(attention.shape, F32),
            jax.ShapeDtypeStruct(expand.shape, F32),
            jax.ShapeDtypeStruct(reduce_t.shape, F32),
            jax.ShapeDtypeStruct(vectors.shape, F32),
        ),
        in_specs=[anywhere] * 2 + [in_vmem] * 5,
        out_specs=(in_vmem,) * 6,
        scratch_shapes=scratch,
        compiler_params=pltpu.CompilerParams(
            collective_id=0, has_side_effects=True, vmem_limit_bytes=65400 * 1024
        ),
    )(tokens, cotangent, span_mask, vectors, attention, expand, reduce_t)


def update_kernel(rates, *refs):
    count = len(rates)
    ins, (result, grad) = refs[: 4 * count], refs[4 * count : 4 * count + 2]
    outs, (result_out, grad_out) = refs[4 * count + 2 : 7 * count + 2], refs[7 * count + 2 : 7 * count + 4]
    held, (low, wide, passed) = refs[7 * count + 4 : 11 * count + 4], refs[11 * count + 4 : 11 * count + 7]
    in_sems, out_sems = refs[11 * count + 7 :]
    loads = [pltpu.make_async_copy(ins[n], held[n], in_sems.at[n]) for n in range(4 * count)]
    stores = [pltpu.make_async_copy(held[4 * n + m], outs[3 * n + m], out_sems.at[3 * n + m])
              for n in range(count) for m in range(3)]
    load_grad = pltpu.make_async_copy(grad, low, in_sems.at[4 * count])
    store_grad = pltpu.make_async_copy(wide, grad_out, out_sems.at[3 * count])
    load_result = pltpu.make_async_copy(result, passed, in_sems.at[4 * count + 1])
    store_result = pltpu.make_async_copy(passed, result_out, out_sems.at[3 * count + 1])
    load_grad.start()
    load_result.start()
    for copy in loads:
        copy.start()
    load_result.wait()
    store_result.start()
    load_grad.wait()

    def widen(s, carry):
        wide[s] = low[s].astype(F32)
        return carry

    lax.fori_loop(0, low.shape[0], widen, 0)
    store_grad.start()
    for n in range(count):
        for m in range(4):
            loads[4 * n + m].wait()
        weight, one, two, gradient = held[4 * n : 4 * n + 4]
        values = adamw(weight[...], one[...], two[...], gradient[...], rates[n])
        for ref, value in zip((weight, one, two), values):
            ref[...] = value
        for m in range(3):
            stores[3 * n + m].start()
    for copy in stores + [store_grad, store_result]:
        copy.wait()


def update(rates, arrays, result, grad):
    flat = [value for group in arrays for value in group]
    new = [jax.ShapeDtypeStruct(value.shape, F32) for group in arrays for value in group[:3]]
    new += [jax.ShapeDtypeStruct(result.shape, BF16), jax.ShapeDtypeStruct(grad.shape, F32)]
    anywhere = pl.BlockSpec(memory_space=pl.ANY)
    scratch = [pltpu.VMEM(value.shape, F32) for value in flat]
    scratch += [pltpu.VMEM(grad.shape, BF16), pltpu.VMEM(grad.shape, F32), pltpu.VMEM(result.shape, BF16)]
    scratch += [pltpu.SemaphoreType.DMA((len(flat) + 2,)), pltpu.SemaphoreType.DMA((len(new),))]
    return pl.pallas_call(
        functools.partial(update_kernel, rates),
        out_shape=tuple(new),
        in_specs=[anywhere] * (len(flat) + 2),
        out_specs=(anywhere,) * len(new),
        scratch_shapes=scratch,
        compiler_params=pltpu.CompilerParams(vmem_limit_bytes=63 * 1024 * 1024),
    )(*flat, result, grad)


def local(
    sub,
    tokens,
    cotangent,
    span_mask,
    attention_weight,
    expand_weight,
    reduce_weight,
    vectors,
    attention_first,
    attention_second,
    expand_first,
    expand_second,
    reduce_first,
    reduce_second,
    vector_first,
    vector_second,
):
    together = [[n * sub + m for m in range(sub)] for n in range(GROUPS)]

    def widen(value, axis):
        if sub == 1:
            return value
        low = lax.all_gather(
            value.astype(BF16), "batch", axis=axis, tiled=True, axis_index_groups=together
        )
        return low.astype(F32)

    def narrow(value, axis):
        if sub == 1:
            return value
        return lax.psum_scatter(
            value, "batch", scatter_dimension=axis, tiled=True, axis_index_groups=together
        )

    out_tokens, input_grad, ga, g1, g2, gv = layer(
        sub,
        tokens,
        cotangent,
        span_mask,
        widen(vectors, 1),
        widen(attention_weight, 2),
        widen(expand_weight, 1),
        widen(reduce_weight.T, 0),
    )
    arrays = (
        (attention_weight, attention_first, attention_second, narrow(ga, 2)),
        (expand_weight, expand_first, expand_second, narrow(g1, 1)),
        (reduce_weight.T, reduce_first.T, reduce_second.T, narrow(g2, 0)),
        (vectors, vector_first, vector_second, narrow(gv, 1)),
    )
    rates = (rate_attention, rate_expand, rate_reduce, rate_vector)
    new = update(rates, arrays, out_tokens, input_grad)
    return new[-2:] + new[0:6] + tuple(value.T for value in new[6:9]) + new[9:12]


def solution(mesh):
    sub = mesh.shape["batch"] // GROUPS
    sequences = P("batch", "blk", None)
    attention = P(None, "blk", "batch")
    matrix = P("blk", "batch")
    return jax.shard_map(
        functools.partial(local, sub),
        mesh=mesh,
        in_specs=(sequences, sequences, P("batch", "blk"), attention, matrix, matrix, matrix)
        + (attention,) * 2
        + (matrix,) * 6,
        out_specs=(sequences,) * 2 + (attention,) * 3 + (matrix,) * 9,
        check_vma=False,
    )
```

```python
import functools
import math

import jax
import jax.numpy as jnp
from jax import lax
from jax.experimental import pallas as pl
from jax.experimental.pallas import tpu as pltpu
from jax.sharding import PartitionSpec as P

HEADS = 12
HEAD = 64
STEP = 10
GROUPS = 8

norm_epsilon = 1e-05
beta_one = 0.9
beta_two = 0.999
adam_epsilon = 1e-08
decay_weight = 0.1
rate_attention = 0.05
rate_expand = 0.03
rate_reduce = 0.015
rate_vector = 0.4

F32 = jnp.float32
BF16 = jnp.bfloat16
MESH = pl.DeviceIdType.MESH
GELU_SCALE = math.sqrt(2.0 / math.pi)
GELU_CUBE = 0.044715


def adamw(weight, moment_one, moment_two, gradient, step_rate):
    moment_one = beta_one * moment_one + (1.0 - beta_one) * gradient
    moment_two = beta_two * moment_two + (1.0 - beta_two) * gradient * gradient
    corrected_one = moment_one / (1.0 - beta_one**STEP)
    corrected_two = moment_two / (1.0 - beta_two**STEP)
    updated = weight - step_rate * (
        corrected_one / (jnp.sqrt(corrected_two) + adam_epsilon) + decay_weight * weight
    )
    return (updated, moment_one, moment_two)


def dot_nn(left, right):
    return lax.dot_general(left, right, (((1,), (0,)), ((), ())), preferred_element_type=F32)


def dot_nt(left, right):
    return lax.dot_general(left, right, (((1,), (1,)), ((), ())), preferred_element_type=F32)


X, Y, Z = 1, 2, 4
QK, VO, W10, W11, W20, W21 = range(6)
AQK, AVO, G10, G11, G20, G21 = range(6)
SEND, GOT, WHOLE, SUM, VEC, SMALL, DO = range(7)
(TOK, COT, OUT, IG, TOK_HERE, COT_HERE, OUT_HERE,
 IG_HERE, SWAP_HERE, N2S_HERE, COTS_HERE, BACKS_HERE, AHEADS_HERE) = range(13)
GATHER_ROUTE = ((Z, X, Y), (Y, Z, X), (Y, Z, X), (Z, X, Y), (Z, Y, X), (X, Z, Y))
SUM_ROUTE = ((Y, X, Z), (X, Z, Y), (X, Y, Z), (Y, X, Z), (Z, Y, X), (Y, Z, X))
PLAN = dict(
    own1=(
        (SEND, QK, 0, X), (SEND, QK, 0, Y), (SEND, QK, 0, Z),
    ),
    ownff=(
        (SEND, VO, 0, X), (DO, TOK), (DO, SWAP_HERE),
    ),
    mask=(
        (GOT, QK, X), (GOT, QK, Y), (SEND, W10, 0, X), (SEND, W10, 0, Z), (SEND, W11, 0, X),
        (SEND, W20, 0, X),
    ),
    ln1=(
        (VEC, 0), (GOT, VO, X), (SEND, QK, X, Y), (VEC, 1), (GOT, W10, X), (GOT, QK, Z), (SEND, QK, Z, X),
        (SEND, QK, Z, Y), (GOT, W11, X), (VEC, 2), (SEND, VO, 0, Z), (SEND, W21, 0, X), (GOT, W20, X),
        (DO, TOK_HERE), (GOT, QK, X | Y), (GOT, W10, Z), (SEND, W10, Z, X), (VEC, 3), (GOT, QK, Z | X),
        (SEND, QK, Z | X, Y), (SEND, W11, 0, Z),
    ),
    unp0=(
        (GOT, W21, X), (SEND, W10, 0, Y), (GOT, QK, Z | Y), (SEND, VO, 0, Y), (DO, COT), (GOT, VO, Z),
        (SEND, VO, Z, X), (GOT, W10, Z | X), (GOT, QK, Z | X | Y), (GOT, W10, Y), (SEND, W10, Y, X),
        (SEND, W10, Y, Z), (WHOLE, QK),
    ),
    projq=(
        (GOT, VO, Y), (SEND, VO, Y, X),
    ),
    attend0=(
        (GOT, W11, Z), (SEND, W11, Z, X), (SEND, VO, Y, Z), (GOT, VO, Z | X),
    ),
    attend1=(
        (SEND, W11, 0, Y),
    ),
    attend2=(
        (GOT, W10, Y | X), (SEND, W11, X, Y),
    ),
    attend3=(
        (GOT, VO, Y | X), (SEND, W11, Z, Y),
    ),
    attend5=(
        (GOT, W10, Y | Z), (SEND, W10, Y | Z, X), (SEND, W20, 0, Z), (DO, COT_HERE),
    ),
    unp1=(
        (GOT, W11, Z | X), (GOT, W11, Y), (SEND, W11, Z | X, Y), (GOT, W11, X | Y), (DO, COTS_HERE),
        (GOT, VO, Y | Z), (SEND, VO, Y | Z, X), (SEND, W21, 0, Z), (GOT, W10, Y | Z | X), (SEND, W20, 0, Y),
        (GOT, W11, Z | Y), (WHOLE, W10), (GOT, W20, Z), (SEND, W20, Z, X), (SEND, W20, Z, Y),
        (SEND, W21, X, Z), (GOT, VO, Y | Z | X), (GOT, W11, Z | X | Y), (SEND, W21, 0, Y), (GOT, W20, Y),
        (SEND, W20, Y, X), (SEND, W21, X, Y), (WHOLE, VO),
    ),
    projv=(
        (WHOLE, W11),
    ),
    mix5=(
        (GOT, W21, Z), (SEND, W21, Z, Y),
    ),
    ln2=(
        (GOT, W20, Z | X), (GOT, W20, Z | Y), (SEND, W20, Z | Y, X),
    ),
    expa0=(
        (GOT, W20, Y | X), (GOT, W21, Y),
    ),
    expa1=(
        (GOT, W21, X | Y),
    ),
    expb0=(
        (DO, N2S_HERE), (GOT, W21, X | Z), (SEND, W21, X | Z, Y),
    ),
    expb1=(
        (GOT, W20, Z | Y | X), (GOT, W21, Z | Y),
    ),
    trY=(
        (WHOLE, W20),
    ),
    gw2_1=(
        (GOT, W21, X | Z | Y),
    ),
    innb0=(
        (SUM, G20, 0), (SUM, G21, 0), (WHOLE, W21),
    ),
    gw1_0=(
        (DO, BACKS_HERE),
    ),
    hid=(
        (SUM, G10, 0), (SUM, G11, 0),
    ),
    dO=(
        (SUM, G21, 1),
    ),
    ab5=(
        (SUM, G10, 1), (SUM, G11, 1), (SUM, G20, 1),
    ),
    reda=(
        (SUM, G10, 2), (SUM, G11, 2), (SUM, AVO, 0),
    ),
    outst=(
        (SUM, AQK, 0), (SUM, G20, 2), (SUM, G21, 2), (DO, AHEADS_HERE),
    ),
    end=(
        (SUM, G10, 3), (DO, OUT), (SUM, AVO, 1), (SUM, G20, 3), (SUM, G11, 3), (SUM, AQK, 1), (SMALL, 0),
        (SUM, G21, 3), (SMALL, 1), (DO, IG), (SUM, AQK, 2), (SMALL, 2), (DO, OUT_HERE), (SUM, AVO, 2),
        (SMALL, 3), (DO, IG_HERE), (SUM, AVO, 3), (SUM, AQK, 3),
    ),
)


def lane_tiles(ref, count=6):
    return jnp.concatenate([ref[t] for t in range(count)], axis=1)


class Unit:
    def __init__(self, index, route, u, other):
        self.index, self.route, self.u, self.other = index, route, u, other


class Gradient:
    def __init__(self, index, route, u, other, core_in, got, finish):
        self.index, self.route, self.u, self.other = index, route, u, other
        self.core_in, self.got, self.finish = core_in, got, finish


def kernel(sub, zs, *refs):
    (tok, cot, mask_in, vec_in, a_in, w1_in, w2_in,
     out, ig, ga, g1, g2, gv,
     ua, uw1, uw2, gw1, gw2, core_in, got,
     x_in, cot_in, stage, vec, gvec, vin, gin, narrow_rows,
     at, n1, q6, k6, v6, o6, pt, h1, acc, n2, act, gp, ta, tb, tc, d6,
     w1_other, w2_other, n2_other, cot_other, back_in, ahead_in,
     lines, b1, gb1, tot1, tot2, turned1, got1, got2,
     local_sem, ag_send, ag_recv, core_send, core_recv, rs_send, rs_recv,
     a2a_send, a2a_recv, v_send, v_recv, pair_send, pair_recv) = refs

    i = lax.axis_index("blk")
    b = lax.axis_index("batch")
    c, y = lax.rem(i, 2), lax.div(i, 2)
    g, r = lax.div(b, sub), lax.rem(b, sub)
    x, z = lax.rem(g, 2), lax.div(g, 2)

    def device(c_=c, y_=y, x_=x, z_=z):
        return {"blk": 2 * y_ + c_, "batch": (2 * z_ + x_) * sub + r}

    def z_at(k):
        return lax.rem(z + k, zs)

    def block_at(k):
        return lax.rem(i + k, 4)

    def copy(src, dst, send, recv, to):
        return pltpu.make_async_remote_copy(
            src_ref=src, dst_ref=dst, send_sem=send, recv_sem=recv, device_id=to, device_id_type=MESH
        )

    def loop(count, body, hooks=()):
        def step(s, carry):
            body(s)
            for k, f in hooks:
                pl.when(s == k)(f)
            return carry

        lax.fori_loop(0, count, step, 0)

    partners = [device(z_=z_at(k)) for k in range(1, zs)]
    partners += [device(x_=1 - x), device(y_=1 - y), device(c_=1 - c), device(c_=1 - c, y_=1 - y)]
    barrier = pltpu.get_barrier_semaphore()
    for partner in partners:
        pl.semaphore_signal(barrier, inc=1, device_id=partner, device_id_type=MESH)
    pl.semaphore_wait(barrier, len(partners))

    def offsets(axes):
        return [(dy, dx, dz)
                for dy in ((1,) if "y" in axes else (0,))
                for dx in ((1,) if "x" in axes else (0,))
                for dz in (range(1, zs) if "z" in axes else (0,))]

    def owner(d):
        dy, dx, dz = d
        return (1 - y if dy else y, 1 - x if dx else x, z if isinstance(dz, int) and dz == 0 else z_at(zs - dz))

    def moves(d, axis):
        dy, dx, dz = d
        if axis == "y":
            return [(device(y_=1 - y), (1, dx, dz))]
        if axis == "x":
            return [(device(x_=1 - x), (dy, 1, dz))]
        return [(device(z_=z_at(k)), (dy, dx, k)) for k in range(1, zs)]

    def ag_copy(n, ref, d, to):
        slot = (d[0] * 2 + d[1]) * zs + d[2]
        return copy(ref, ref, ag_send.at[n.index, slot], ag_recv.at[n.index, slot], to)

    def core_copy(n, ref):
        return copy(ref, ref, core_send.at[n.index], core_recv.at[n.index], device(c_=1 - c))

    def ag_send_part(n, axes, axis):
        for d in offsets(axes):
            ref = n.u.at[owner(d)]
            for to, there in moves(d, axis):
                ag_copy(n, ref, there, to).start()

    def ag_wait_part(n, axes):
        for d in offsets(axes):
            ref = n.u.at[owner(d)]
            ag_copy(n, ref, d, device()).wait_recv()
            if n.other is not None:
                core_copy(n, ref).start()

    def ag_done(n):
        if n.other is not None:
            core_copy(n, n.other).wait_recv()

    def ag_drain(n):
        own = n.u.at[y, x, z]
        for d in [(dy, dx, dz) for dy in range(2) for dx in range(2) for dz in range(zs)][1:]:
            ag_copy(n, own, d, device()).wait_send()
        if n.other is not None:
            core_copy(n, n.u).wait_send()

    AXES = "yxz"

    def step_region(n, step, k):
        where = []
        for axis in AXES:
            at_step = n.route.index(axis)
            where.append(0 if at_step < step else (k if at_step == step else slice(None)))
        return n.got.at[tuple(where)]

    def step_groups(n, step):
        axis = n.route[step]
        if axis == "y":
            return [(1, 0, device(y_=1 - y))]
        if axis == "x":
            return [(1, 1, device(x_=1 - x))]
        return [(k, 1 + k, device(z_=z_at(zs - k))) for k in range(1, zs)]

    def rs_group(n, step, k, slot, to):
        ref = step_region(n, step, k)
        return copy(ref, ref, rs_send.at[n.index, slot], rs_recv.at[n.index, slot], to)

    def step_offsets(n, step, k):
        spans = []
        for axis, size in zip(AXES, (2, 2, zs)):
            at_step = n.route.index(axis)
            spans.append((0,) if at_step < step else ((k,) if at_step == step else tuple(range(size))))
        return spans

    def add_terms(n, d, step):
        dy, dx, dz = d
        value = n.u[owner(d)].astype(F32)
        if n.other is not None:
            value = value + n.core_in[dy, dx, dz].astype(F32)
        for axis in n.route[:step]:
            if axis == "y":
                value = value + n.got[1, dx, dz].astype(F32)
            elif axis == "x":
                value = value + n.got[dy, 1, dz].astype(F32)
            else:
                for k in range(1, zs):
                    value = value + n.got[dy, dx, k].astype(F32)
        return value

    def rs_start(n):
        for dy in range(2):
            for dx in range(2):
                for dz in range(zs):
                    d = (dy, dx, dz)
                    copy(n.other.at[owner(d)], n.core_in.at[d], rs_send.at[n.index, zs + 1],
                         rs_recv.at[n.index, zs + 1], device(c_=1 - c)).start()

    def rs_core_whole(n):
        return copy(n.core_in, n.core_in, rs_send.at[n.index, zs + 1], rs_recv.at[n.index, zs + 1],
                    device(c_=1 - c))

    def rs_step(n, step):
        if step == 0 and n.other is not None:
            rs_core_whole(n).wait_recv()
        if step > 0:
            for k, slot, to in step_groups(n, step - 1):
                rs_group(n, step - 1, k, slot, to).wait_recv()
        if step == 3:
            n.finish(add_terms(n, (0, 0, 0), 3))
            return
        for k, slot, to in step_groups(n, step):
            dys, dxs, dzs = step_offsets(n, step, k)
            if step > 0 or n.other is not None:

                def body(e):
                    for dy in dys:
                        for dx in dxs:
                            d = (dy, dx, dzs[0] if len(dzs) == 1 else e)
                            n.u[owner(d)] = add_terms(n, d, step).astype(BF16)

                if len(dzs) == 1:
                    body(0)
                else:
                    loop(zs, body)
            for dy in dys:
                for dx in dxs:
                    for dz in dzs:
                        d = (dy, dx, dz)
                        copy(n.u.at[owner(d)], n.got.at[d], rs_send.at[n.index, slot],
                             rs_recv.at[n.index, slot], to).start()

    def rs_drain(n):
        if n.other is not None:
            rs_core_whole(n).wait_send()
        for step in range(3):
            for group in step_groups(n, step):
                rs_group(n, step, *group).wait_send()

    def small_sum(ref, slots, which):
        to = (device(y_=1 - y), device(c_=1 - c), device(x_=1 - x))
        to += tuple(device(z_=z_at(k)) for k in range(1, zs))

        def moved(slot):
            return copy(ref, slots.at[slot], v_send.at[which, slot], v_recv.at[which, slot], to[slot])

        def land(last):
            moved(last).wait()
            ref[...] = ref[...] + slots[last]

        def step(n):
            def run():
                if n > 0:
                    land(n - 1)
                moved(n).start()

            return run

        def line():
            land(2)
            for k in range(1, zs):
                moved(2 + k).start()

        def finish():
            for k in range(1, zs):
                moved(2 + k).wait()
            value = ref[...]
            for k in range(1, zs):
                value = value + slots[2 + k]
            ref[...] = value

        return [step(0), step(1), step(2), line, finish]

    def rows_of(s):
        return pl.ds(pl.multiple_of(s * 128, 128), 128)

    def exchange(src, dst, which):
        return [copy(src.at[block_at(k)], dst.at[i], a2a_send.at[which, k - 1],
                     a2a_recv.at[which, k - 1], {"blk": block_at(k), "batch": b})
                for k in range(1, 4)]

    def exchange_landed(dst, which):
        return [copy(dst.at[block_at(4 - k)], dst.at[block_at(4 - k)], a2a_send.at[which, k - 1],
                     a2a_recv.at[which, k - 1], {"blk": block_at(4 - k), "batch": b})
                for k in range(1, 4)]

    def axes_of(mask):
        return "".join(axis for axis, bit in (("y", Y), ("x", X), ("z", Z)) if mask & bit)

    units = []
    for index, route in enumerate(GATHER_ROUTE):
        half = index % 2
        ref = (ua, uw1, uw2)[index // 2]
        pieces = (ref.at[half, c], ref.at[half, 1 - c]) if index < 2 else (ref.at[half], None)
        units.append(Unit(index, "".join(map(axes_of, route)), *pieces))

    def pair(slot, src, dst):
        return copy(src, dst, pair_send.at[slot], pair_recv.at[slot], device(c_=1 - c))

    w1_swap, w2_swap = pair(0, w1_in, w1_other), pair(1, w2_in, w2_other)

    def each_core(f):
        for q in range(2):
            pl.when(c == q)(functools.partial(f, q))

    def rest_rows(matrix):
        return a_in[matrix, pl.ds(pl.multiple_of(128 * (1 - c), 64), 64), :]

    def own_attention(p):
        mine = ua.at[p, c, y, x, z]
        for m in range(2):
            main = a_in[2 * p + m, pl.ds(pl.multiple_of(64 * c, 64), 128), :]
            mine[96 * m : 96 * m + 96, :] = main.T.astype(BF16)
        rest = jnp.concatenate([rest_rows(2 * p + c), rest_rows(2 * p + 1 - c)], axis=0)
        mine[192:288, :] = rest.T.astype(BF16)

    def own_expand(q):
        both = (w1_in, w1_other) if q == 0 else (w1_other, w1_in)
        cols = slice(192 * q, 192 * q + 192)
        blocks = (
            both[0][0:128, cols],
            jnp.concatenate([both[0][128:192, cols], both[1][0:64, cols]], axis=0),
            both[1][64:192, cols],
        )
        for t, block in enumerate(blocks):
            value = block.T.astype(BF16)
            for h in range(2):
                uw1[h, y, x, z, 96 * t : 96 * t + 96, :] = value[96 * h : 96 * h + 96, :]

    def own_reduce(q):
        both = (w2_in, w2_other) if q == 0 else (w2_other, w2_in)
        for cc in range(2):
            for part_of in range(2):
                start = 384 * part_of + 192 * q
                lines[:, 192 * part_of : 192 * part_of + 192] = both[cc][:, start : start + 192]
            for t in range(3):
                uw2[cc, y, x, z, 96 * t : 96 * t + 96, :] = lines[:, 128 * t : 128 * t + 128].astype(BF16)

    def own_hidden_bias(q):
        for zz in range(zs):
            for xx in range(2):
                col = 384 * (zz % 2) + 192 * xx
                start = 384 * xx + 192 * q
                b1[zz // 2 : zz // 2 + 1, col : col + 192] = vec[8 + zz : 9 + zz, start : start + 192]

    def hidden_bias_gradient(q):
        for zz in range(zs):
            for xx in range(2):
                col = 384 * (zz % 2) + 192 * xx
                start = 384 * xx + 192 * q
                gvec[8 + zz : 9 + zz, start : start + 192] = gb1[zz // 2 : zz // 2 + 1, col : col + 192]

    columns = a_in.shape[2]
    placed = lax.broadcasted_iota(jnp.int32, (columns, 768), 1) == (
        lax.broadcasted_iota(jnp.int32, (columns, 768), 0) + columns * g
    )

    def own_vectors():
        vec[...] = jnp.zeros_like(vec)
        rows = dot_nn(vec_in[...].astype(BF16), jnp.where(placed, 1.0, 0.0).astype(BF16))
        for j in range(3):
            vec[pl.ds(3 * i + j, 1), :] = rows[j : j + 1, :]

    load_cot = pltpu.make_async_copy(cot, stage, local_sem.at[4])

    def masked_cotangent():
        load_cot.wait()
        eye = lax.broadcasted_iota(jnp.int32, (128, 128), 0) == lax.broadcasted_iota(jnp.int32, (128, 128), 1)
        for s in range(4):
            row = jnp.broadcast_to(mask_in[s : s + 1, :].astype(F32), (128, 128))
            column = jnp.sum(jnp.where(eye, row, 0.0), axis=1, keepdims=True)
            stage[s] = (stage[s].astype(F32) * column).astype(BF16)

    def finish_attention(p):
        def finish(value):
            for m in range(2):
                ga[2 * p + m, pl.ds(pl.multiple_of(64 * c, 64), 128), :] = value[96 * m : 96 * m + 96, :].T
            rest = value[192:288, :].T
            rows = pl.ds(pl.multiple_of(128 * (1 - c), 64), 64)
            ga[2 * p + c, rows, :] = rest[0:64, :]
            ga[2 * p + 1 - c, rows, :] = rest[64:128, :]

        return finish

    def finish_expand(h):
        def finish(value):
            tot1[h] = value

        return finish

    def finish_reduce(h):
        def finish(value):
            tot2[h] = value

        return finish

    w1_back = pair(6, turned1.at[pl.ds(pl.multiple_of(192 * (1 - c), 64), 192)], got1)
    w2_back = pair(7, tot2.at[1 - c], got2)

    def turn_expand():
        for h in range(2):
            for t in range(3):
                turned1[128 * t : 128 * t + 128, 96 * h : 96 * h + 96] = tot1[h, 96 * t : 96 * t + 96, :].T
        w1_back.start()

    def join_expand(q):
        g1[:, 192 * q : 192 * q + 192] = turned1[192 * q : 192 * q + 192, :]
        g1[:, 192 * (1 - q) : 192 * (1 - q) + 192] = got1[...]

    def join_reduce(q):
        for half, value in ((q, tot2.at[q]), (1 - q, got2)):
            for t in range(3):
                lines[:, 128 * t : 128 * t + 128] = value[96 * t : 96 * t + 96, :]
            for part_of in range(2):
                start = 384 * part_of + 192 * half
                g2[:, start : start + 192] = lines[:, 192 * part_of : 192 * part_of + 192]

    def finish_vectors():
        value, total = gvec[...], 0.0
        for _ in range(3):
            part = value.astype(BF16)
            total = total + dot_nt(part, jnp.where(placed, 1.0, 0.0).astype(BF16))
            value = value - part.astype(F32)
        narrow_rows[...] = total
        for j in range(3):
            gv[j : j + 1, :] = narrow_rows[pl.ds(3 * i + j, 1), :]

    grads = []
    finishes = (finish_attention, finish_expand, finish_reduce)
    for index, route in enumerate(SUM_ROUTE):
        half = index % 2
        ref = (ua, gw1, gw2)[index // 2]
        pieces = (ref.at[half, c], ref.at[half, 1 - c], core_in.at[half]) if index < 2 else (ref.at[half], None, None)
        grads.append(Gradient(index, "".join(map(axes_of, route)), *pieces, got.at[index],
                              finishes[index // 2](half)))

    seen = set()

    def event(kind, *rest):
        if kind == SEND:
            ag_send_part(units[rest[0]], axes_of(rest[1]), axes_of(rest[2]))
        elif kind == GOT:
            ag_wait_part(units[rest[0]], axes_of(rest[1]))
        elif kind == WHOLE:
            ag_done(units[rest[0]])
        elif kind == SUM:
            rs_step(grads[rest[0]], rest[1])
            if rest[1] == 3:
                seen.add(rest[0])
                if rest[0] in (G10, G11) and {G10, G11} <= seen:
                    turn_expand()
                if rest[0] in (G20, G21) and {G20, G21} <= seen:
                    w2_back.start()
        elif kind == DO:
            actions[rest[0]]()
        else:
            (vec_steps if kind == VEC else gvec_steps)[rest[0] + 1]()

    def run(part):
        for todo in PLAN.get(part, ()):
            event(*todo)

    def parts(name, count, body):
        run(name + "0")
        hooks = [(k - 1, functools.partial(run, name + str(k))) for k in range(1, count) if name + str(k) in PLAN]
        loop(count, body, hooks)

    def started(copies):
        for moved in copies:
            moved.start()
        return copies

    def arrived(*copies):
        for moved in copies:
            moved.wait_recv()

    load_cot.start()
    own_tokens = pltpu.make_async_copy(tok.at[i], x_in.at[i], local_sem.at[0])
    own_tokens.start()
    own_cot = pltpu.make_async_copy(stage.at[i], cot_in.at[i], local_sem.at[1])
    tokens_out, cot_out = exchange(tok, x_in, 0), exchange(stage, cot_in, 1)
    result_out = exchange(stage, out, 2)
    grad_out = [copy(n1.at[rows_of(block_at(k))], ig.at[i], a2a_send.at[3, k - 1], a2a_recv.at[3, k - 1],
                     {"blk": block_at(k), "batch": b}) for k in range(1, 4)]
    own_out = pltpu.make_async_copy(stage.at[i], out.at[i], local_sem.at[2])
    own_grad = pltpu.make_async_copy(n1.at[rows_of(i)], ig.at[i], local_sem.at[3])
    n2_swap, cot_swap = pair(2, n2, n2_other), pair(3, cot_in, cot_other)
    back_swap, ahead_swap = pair(4, d6, back_in), pair(5, n2, ahead_in)
    vec_steps, gvec_steps = small_sum(vec, vin, 0), small_sum(gvec, gin, 1)

    def tokens_here():
        arrived(*exchange_landed(x_in, 0))
        own_tokens.wait()

    def cotangent_here():
        arrived(*exchange_landed(cot_in, 1))
        own_cot.wait()
        cot_swap.start()

    def swaps_here():
        w1_swap.wait()
        w2_swap.wait()

    actions = {
        TOK: lambda: started(tokens_out),
        COT: lambda: started(cot_out),
        OUT: lambda: started(result_out),
        IG: lambda: started(grad_out),
        TOK_HERE: tokens_here,
        COT_HERE: cotangent_here,
        OUT_HERE: lambda: arrived(*exchange_landed(out, 2)),
        IG_HERE: lambda: arrived(*exchange_landed(ig, 3)),
        SWAP_HERE: swaps_here,
        N2S_HERE: lambda: n2_swap.wait(),
        COTS_HERE: lambda: cot_swap.wait(),
        BACKS_HERE: lambda: back_swap.wait(),
        AHEADS_HERE: lambda: ahead_swap.wait(),
    }

    def core_own(index):
        core_copy(units[index], units[index].u.at[y, x, z]).start()

    own_attention(0)
    core_own(QK)
    w1_swap.start()
    w2_swap.start()
    own_vectors()
    vec_steps[0]()
    run("own1")
    own_attention(1)
    core_own(VO)
    run("ownff")
    each_core(own_expand)
    each_core(own_reduce)
    run("mask")
    masked_cotangent()
    own_cot.start()
    run("ln1")
    each_core(own_hidden_bias)

    def normalise(value):
        centered = value - jnp.mean(value, axis=-1, keepdims=True)
        scale = lax.rsqrt(jnp.mean(centered * centered, axis=-1, keepdims=True) + norm_epsilon)
        return centered * scale, scale

    def first_norm(s):
        unit, _ = normalise(x_in[s].astype(F32))
        n1[rows_of(s), :] = (unit * vec[0:1, :] + vec[1:2, :]).astype(BF16)

    loop(4, first_norm)
    run("unp0")

    lanes = lax.broadcasted_iota(jnp.int32, (96, 128), 1)

    def unpack(p, s):
        for xx in range(2):
            rows = pl.ds(pl.multiple_of((2 * s + xx) * 96, 96), 96)
            for yy in range(2):
                first, second = ua.at[p, 0, yy, xx, s], ua.at[p, 1, yy, xx, s]
                lo, hi = 384 * yy, 384 * yy + 256
                for m in range(2):
                    at[2 * p + m, rows, lo : lo + 128] = first[96 * m : 96 * m + 96, :]
                    at[2 * p + m, rows, hi : hi + 128] = second[96 * m : 96 * m + 96, :]
                rest_first = first[192:288, :].astype(F32)
                rest_second = second[192:288, :].astype(F32)
                even = jnp.where(lanes < 64, rest_first, rest_second)
                odd = pltpu.roll(jnp.where(lanes < 64, rest_second, rest_first), 64, 1)
                at[2 * p, rows, lo + 128 : lo + 256] = even.astype(BF16)
                at[2 * p + 1, rows, lo + 128 : lo + 256] = odd.astype(BF16)

    def project(m, dst, bias):
        for n in range(3):
            value = dot_nt(n1[...], at[m, 256 * n : 256 * n + 256, :])
            if bias is not None:
                value = value + vec[bias : bias + 1, 256 * n : 256 * n + 256]
            value = value.astype(BF16)
            if m == 0:
                value = value * jnp.asarray(HEAD ** (-0.5), BF16)
            dst[2 * n] = value[:, 0:128]
            dst[2 * n + 1] = value[:, 128:256]

    loop(zs, functools.partial(unpack, 0))
    run("projq")
    project(0, q6, 2)
    run("projk")
    project(1, k6, None)

    half_lane = lax.broadcasted_iota(jnp.int32, (512, 128), 1) // HEAD

    def half_of(value, which):
        return jnp.where(half_lane == which, value, jnp.zeros_like(value))

    def turn(value):
        return value.astype(F32).T.astype(BF16)

    def attend(p):
        queries, keys = q6[p], k6[p]
        for which in range(2):
            scores = dot_nt(half_of(keys, which), queries)
            expo = jnp.exp(scores - jnp.max(scores, axis=0, keepdims=True))
            probs = (expo * (1.0 / jnp.sum(expo, axis=0, keepdims=True))).astype(BF16)
            pt[2 * p + which] = probs

    def mix(p):
        values_t = turn(v6[p])
        mixed = [dot_nn(values_t[64 * which : 64 * which + 64, :], pt[2 * p + which]) for which in range(2)]
        o6[p] = jnp.concatenate(mixed, axis=0).T.astype(BF16)

    parts("attend", 6, attend)
    run("unp1")
    loop(zs, functools.partial(unpack, 1))
    run("projv")
    project(2, v6, 3)
    parts("mix", 6, mix)

    run("ao")
    for n in range(3):
        cols = slice(256 * n, 256 * n + 256)
        value = dot_nt(lane_tiles(o6), at[3, cols, :]) + vec[4:5, cols]
        for s in range(4):
            h1[128 * s : 128 * s + 128, cols] = x_in[s, :, cols].astype(F32) + value[128 * s : 128 * s + 128]

    def second_norm(s):
        unit, _ = normalise(h1[rows_of(s), :])
        n2[rows_of(s), :] = (unit * vec[5:6, :] + vec[6:7, :]).astype(BF16)

    run("ln2")
    loop(4, second_norm)
    n2_swap.start()

    def expand_block(s):
        def piece(ref):
            return jnp.concatenate([ref[96 * t : 96 * t + 96, :] for t in range(3)], axis=1)

        return jnp.concatenate(
            [jnp.concatenate([piece(uw1.at[h, yy, xx, 2 * s + zz]) for yy in range(2)], axis=1)
             for zz in range(2) for xx in range(2) for h in range(2)],
            axis=0,
        )

    def reduce_block(s):
        def piece(ref):
            return jnp.concatenate([ref[96 * t : 96 * t + 96, :] for t in range(3)], axis=1)

        return jnp.concatenate(
            [jnp.concatenate([piece(uw2.at[cc, s, xx, zz]) for cc in range(2)], axis=1)
             for zz in range(zs) for xx in range(2)],
            axis=0,
        )

    def block_rows(owner, s):
        return pl.ds(pl.multiple_of((2 * owner + s) * 512, 512), 512)

    def expand(owner, normed, s):
        rows = block_rows(owner, s)
        inner = dot_nt(normed[...], expand_block(s)) + b1[pl.ds(s, 1), :]
        square = inner * inner
        tanh = jnp.tanh(GELU_SCALE * inner * (1.0 + GELU_CUBE * square))
        act[rows, :] = (0.5 * inner * (1.0 + tanh)).astype(BF16)
        slope = 0.5 * (1.0 + tanh) + 0.5 * inner * (1.0 - tanh * tanh) * (
            GELU_SCALE * (1.0 + 3.0 * GELU_CUBE * square)
        )
        gp[rows, :] = slope.astype(BF16)

    parts("expa", 2, functools.partial(expand, 0, n2))
    parts("expb", 2, functools.partial(expand, 1, n2_other))

    gvec[...] = jnp.zeros_like(gvec)

    def transpose_rows(dst, s, value):
        dst[:, 128 * s : 128 * s + 128] = turn(value)

    run("trY")
    total = jnp.zeros((1, 768), F32)
    for s in range(4):
        transpose_rows(ta, s, cot_in[s])
        total = total + jnp.sum(cot_in[s].astype(F32), axis=0, keepdims=True)
    gvec[7:8, :] = total
    for s in range(4):
        transpose_rows(tb, s, cot_other[s])

    def both_rows(ref, s):
        return jnp.concatenate([ref[block_rows(0, s), :], ref[block_rows(1, s), :]], axis=0)

    def reduce_back(s):
        grad = dot_nn(jnp.concatenate([ta[...], tb[...]], axis=1), both_rows(act, s)).astype(BF16)
        for zz in range(zs):
            for xx in range(2):
                row = 96 * (2 * zz + xx)
                for cc in range(2):
                    for t in range(3):
                        col = 384 * cc + 128 * t
                        gw2[cc, s, xx, zz, 96 * t : 96 * t + 96, :] = grad[row : row + 96, col : col + 128]

    parts("gw2_", 2, reduce_back)

    def rows_together(ref):
        return jnp.concatenate([ref[s] for s in range(4)], axis=0)

    def inner_back(owner, cotangent_rows, s):
        rows = block_rows(owner, s)
        grad = dot_nn(rows_together(cotangent_rows), reduce_block(s)) * gp[rows, :].astype(F32)
        low = grad.astype(BF16)
        gp[rows, :] = low
        sums = jnp.sum(low.astype(F32), axis=0, keepdims=True)
        gb1[pl.ds(s, 1), :] = sums if owner == 1 else gb1[pl.ds(s, 1), :] + sums

    def norm_back(owner):
        acc[...] = dot_nn(gp[block_rows(owner, 0), :], expand_block(0))
        acc[...] += dot_nn(gp[block_rows(owner, 1), :], expand_block(1))

    parts("innb", 2, functools.partial(inner_back, 1, cot_other))
    run("dn2b")
    norm_back(1)
    for t in range(6):
        d6[t] = acc[:, 128 * t : 128 * t + 128].astype(BF16)
    back_swap.start()
    parts("inna", 2, functools.partial(inner_back, 0, cot_in))
    each_core(hidden_bias_gradient)
    run("dn2a")
    norm_back(0)

    def expand_back(s):
        turned = jnp.concatenate([turn(gp[block_rows(owner, s), :]) for owner in range(2)], axis=1)
        normed = jnp.concatenate([n2[...], n2_other[...]], axis=0)
        grad = dot_nn(turned, normed).astype(BF16)
        for zz in range(2):
            for xx in range(2):
                for h in range(2):
                    row = 384 * zz + 192 * xx + 96 * h
                    for yy in range(2):
                        for t in range(3):
                            col = 384 * yy + 128 * t
                            gw1[h, yy, xx, 2 * s + zz, 96 * t : 96 * t + 96, :] = grad[
                                row : row + 96, col : col + 128
                            ]

    parts("gw1_", 2, expand_back)
    run("hid")

    def norm_gradient(value, scale_row, grad):
        unit, scale = normalise(value)
        gain_sum = jnp.sum(grad * unit, axis=0, keepdims=True)
        bias_sum = jnp.sum(grad, axis=0, keepdims=True)
        inner = grad * scale_row
        mean = jnp.mean(inner, axis=-1, keepdims=True)
        along = jnp.mean(inner * unit, axis=-1, keepdims=True)
        return scale * (inner - mean - unit * along), gain_sum, bias_sum

    def hidden_back(s):
        rows = rows_of(s)
        grad_in = jnp.concatenate([back_in[t, rows, :] for t in range(6)], axis=1)
        grad_in = acc[rows, :] + grad_in.astype(F32)
        grad, gain_sum, bias_sum = norm_gradient(h1[rows, :], vec[5:6, :], grad_in)
        grad = grad + cot_in[s].astype(F32)
        acc[rows, :] = grad
        low = grad.astype(BF16)
        n2[rows, :] = low
        gvec[5:6, :] += gain_sum
        gvec[6:7, :] += bias_sum
        gvec[4:5, :] += jnp.sum(low.astype(F32), axis=0, keepdims=True)

    loop(4, hidden_back)

    run("dO")
    for n in range(3):
        value = dot_nn(n2[...], at[3, :, 256 * n : 256 * n + 256]).astype(BF16)
        d6[2 * n] = value[:, 0:128]
        d6[2 * n + 1] = value[:, 128:256]
    run("gao")
    for s in range(4):
        transpose_rows(tc, s, n2[128 * s : 128 * s + 128, :])
    gp[768:1536, :] = dot_nn(tc[...], lane_tiles(o6)).astype(BF16)

    def attend_back(p):
        rows = rows_of(p)
        queries, keys, values, grads_in = q6[p], k6[p], v6[p], d6[p]
        keys_t = turn(keys)
        grad_query, grad_key, grad_value = [], 0.0, 0.0
        for which in range(2):
            probs = pt[2 * p + which]
            wide = probs.astype(F32)
            grad_probs = dot_nt(half_of(values, which), grads_in)
            inner = jnp.sum(wide * grad_probs, axis=0, keepdims=True)
            grad_scores = (wide * (grad_probs - inner)).astype(BF16)
            grad_query.append(dot_nn(keys_t[64 * which : 64 * which + 64, :], grad_scores))
            grad_key = grad_key + dot_nn(grad_scores, half_of(queries, which))
            grad_value = grad_value + dot_nn(probs, half_of(grads_in, which))
        grad_query = jnp.concatenate(grad_query, axis=0) * HEAD ** (-0.5)
        ta[rows, :] = grad_query.astype(BF16)
        tb[rows, :] = grad_key.T.astype(BF16)
        tc[rows, :] = grad_value.T.astype(BF16)
        q6[p] = grad_query.T.astype(BF16)
        k6[p] = grad_key.astype(BF16)
        v6[p] = grad_value.astype(BF16)

    def pack(p, first_row, second_row):
        def body(s):
            for xx in range(2):
                offset = (2 * s + xx) * 96
                rows = [pl.ds(pl.multiple_of(first_row + offset, 96), 96),
                        pl.ds(pl.multiple_of(second_row + offset, 96), 96)]
                first, second = ua.at[p, 0, :, xx, s], ua.at[p, 1, :, xx, s]
                for yy in range(2):
                    lo, mid, hi = 384 * yy, 384 * yy + 128, 384 * yy + 256
                    for m in range(2):
                        first[yy, 96 * m : 96 * m + 96, :] = gp[rows[m], lo : lo + 128]
                        second[yy, 96 * m : 96 * m + 96, :] = gp[rows[m], hi : hi + 128]
                    even = gp[rows[0], mid : mid + 128].astype(F32)
                    odd = pltpu.roll(gp[rows[1], mid : mid + 128].astype(F32), 64, 1)
                    first[yy, 192:288, :] = jnp.where(lanes < 64, even, odd).astype(BF16)
                    second[yy, 192:288, :] = jnp.where(lanes < 64, odd, even).astype(BF16)

        loop(zs, body)

    parts("ab", 6, attend_back)
    run("gav")
    ag_drain(units[VO])
    gp[0:768, :] = dot_nn(tc[...], n1[...]).astype(BF16)
    pack(1, 0, 768)
    rs_start(grads[AVO])
    run("gaqk")
    ag_drain(units[QK])
    gp[0:768, :] = dot_nn(ta[...], n1[...]).astype(BF16)
    gp[768:1536, :] = dot_nn(tb[...], n1[...]).astype(BF16)
    pack(0, 0, 768)
    rs_start(grads[AQK])

    def reduce(owner):
        value = dot_nt(act[block_rows(owner, 0), :], reduce_block(0))
        return value + dot_nt(act[block_rows(owner, 1), :], reduce_block(1))

    def layer_output():
        run("redb")
        n2[...] = reduce(1).astype(BF16)
        ahead_swap.start()
        run("reda")
        h1[...] = h1[...] + vec[7:8, :] + reduce(0)
        run("outst")
        for moved in cot_out:
            moved.wait_send()
        for s in range(4):
            rows = slice(128 * s, 128 * s + 128)
            stage[s] = (h1[rows, :] + ahead_in[rows, :].astype(F32)).astype(BF16)
        own_out.start()

    layer_output()
    run("dn1")
    h1[...] = dot_nn(lane_tiles(q6), at[0])
    h1[...] += dot_nn(lane_tiles(k6), at[1])
    h1[...] += dot_nn(lane_tiles(v6), at[2])
    gvec[2:3, :] = jnp.sum(lane_tiles(q6).astype(F32), axis=0, keepdims=True)
    gvec[3:4, :] = jnp.sum(lane_tiles(v6).astype(F32), axis=0, keepdims=True)

    run("inb")

    def input_back(s):
        rows = rows_of(s)
        grad, gain_sum, bias_sum = norm_gradient(x_in[s].astype(F32), vec[0:1, :], h1[rows, :])
        n1[rows, :] = (grad + acc[rows, :]).astype(BF16)
        gvec[0:1, :] += gain_sum
        gvec[1:2, :] += bias_sum

    loop(4, input_back)
    gvec_steps[0]()
    own_grad.start()
    run("end")
    finish_vectors()
    w1_back.wait()
    each_core(join_expand)
    w2_back.wait()
    each_core(join_reduce)

    own_out.wait()
    own_grad.wait()
    for moved in tokens_out + result_out + grad_out:
        moved.wait_send()
    for n in units[W10:]:
        ag_drain(n)
    for n in grads:
        rs_drain(n)


def layer(sub, tokens, cotangent, span_mask, vectors, attention, expand, reduce_t):
    zs = GROUPS // 2
    seqs, block, width = tokens.shape
    rows = seqs * block
    columns = attention.shape[2]
    piece = (3 * columns, 128)
    vmem = lambda shape, dtype: pltpu.VMEM(shape, dtype)
    half = (2, 2, 2, zs) + piece
    scratch = [vmem((2,) + half, BF16)] + [vmem(half, BF16)] * 4
    scratch += [vmem((2, 2, 2, zs) + piece, BF16), vmem((6, 2, 2, zs) + piece, BF16)]
    scratch += [vmem(tokens.shape, BF16)] * 3
    scratch += [vmem((16, width), F32)] * 2
    scratch += [vmem((zs + 2, 16, width), F32)] * 2
    scratch += [vmem((16, columns), F32)]
    tiles = vmem((width // 128, rows, 128), BF16)
    flat = vmem((rows, width), BF16)
    turned = vmem((width, rows), BF16)
    scratch += [vmem((4, width, width), BF16), flat, tiles, tiles, tiles, tiles]
    scratch += [vmem((HEADS, rows, rows), BF16), vmem((rows, width), F32), vmem((rows, width), F32)]
    scratch += [flat, vmem((4 * rows, width), BF16), vmem((4 * rows, width), BF16)]
    scratch += [turned, turned, turned, tiles]
    scratch += [vmem(expand.shape, F32), vmem(reduce_t.shape, F32), flat, vmem(tokens.shape, BF16)]
    scratch += [tiles, flat, vmem((columns, width // 2), F32), vmem((2, width), F32), vmem((2, width), F32)]
    scratch += [vmem((2,) + piece, F32), vmem((2,) + piece, F32), vmem((width // 2, 2 * columns), F32)]
    scratch += [vmem((2 * columns, 2 * columns), F32), vmem(piece, F32)]
    scratch += [pltpu.SemaphoreType.DMA((5,))]
    scratch += [pltpu.SemaphoreType.DMA((6, 4 * zs))] * 2
    scratch += [pltpu.SemaphoreType.DMA((2,))] * 2
    scratch += [pltpu.SemaphoreType.DMA((6, zs + 2))] * 2
    scratch += [pltpu.SemaphoreType.DMA((4, 3))] * 2
    scratch += [pltpu.SemaphoreType.DMA((2, zs + 2))] * 2
    scratch += [pltpu.SemaphoreType.DMA((8,))] * 2
    in_vmem = pl.BlockSpec(memory_space=pltpu.VMEM)
    anywhere = pl.BlockSpec(memory_space=pl.ANY)
    return pl.pallas_call(
        functools.partial(kernel, sub, zs),
        out_shape=(
            jax.ShapeDtypeStruct(tokens.shape, BF16),
            jax.ShapeDtypeStruct(tokens.shape, BF16),
            jax.ShapeDtypeStruct(attention.shape, F32),
            jax.ShapeDtypeStruct(expand.shape, F32),
            jax.ShapeDtypeStruct(reduce_t.shape, F32),
            jax.ShapeDtypeStruct(vectors.shape, F32),
        ),
        in_specs=[anywhere] * 2 + [in_vmem] * 5,
        out_specs=(anywhere, anywhere) + (in_vmem,) * 4,
        scratch_shapes=scratch,
        compiler_params=pltpu.CompilerParams(
            collective_id=0, has_side_effects=True, vmem_limit_bytes=65400 * 1024
        ),
    )(tokens, cotangent, span_mask, vectors, attention, expand, reduce_t)


def update_kernel(rates, *refs):
    count = len(rates)
    ins, (result, grad) = refs[: 4 * count], refs[4 * count : 4 * count + 2]
    outs, (result_out, grad_out) = refs[4 * count + 2 : 7 * count + 2], refs[7 * count + 2 : 7 * count + 4]
    held, (low, wide, passed) = refs[7 * count + 4 : 11 * count + 4], refs[11 * count + 4 : 11 * count + 7]
    in_sems, out_sems = refs[11 * count + 7 :]
    loads = [pltpu.make_async_copy(ins[n], held[n], in_sems.at[n]) for n in range(4 * count)]
    stores = [pltpu.make_async_copy(held[4 * n + m], outs[3 * n + m], out_sems.at[3 * n + m])
              for n in range(count) for m in range(3)]
    load_grad = pltpu.make_async_copy(grad, low, in_sems.at[4 * count])
    store_grad = pltpu.make_async_copy(wide, grad_out, out_sems.at[3 * count])
    load_result = pltpu.make_async_copy(result, passed, in_sems.at[4 * count + 1])
    store_result = pltpu.make_async_copy(passed, result_out, out_sems.at[3 * count + 1])
    load_grad.start()
    load_result.start()
    for copy in loads:
        copy.start()
    load_result.wait()
    store_result.start()
    load_grad.wait()

    def widen(s, carry):
        wide[s] = low[s].astype(F32)
        return carry

    lax.fori_loop(0, low.shape[0], widen, 0)
    store_grad.start()
    for n in range(count):
        for m in range(4):
            loads[4 * n + m].wait()
        weight, one, two, gradient = held[4 * n : 4 * n + 4]
        values = adamw(weight[...], one[...], two[...], gradient[...], rates[n])
        for ref, value in zip((weight, one, two), values):
            ref[...] = value
        for m in range(3):
            stores[3 * n + m].start()
    for copy in stores + [store_grad, store_result]:
        copy.wait()


def update(rates, arrays, result, grad):
    flat = [value for group in arrays for value in group]
    new = [jax.ShapeDtypeStruct(value.shape, F32) for group in arrays for value in group[:3]]
    new += [jax.ShapeDtypeStruct(result.shape, BF16), jax.ShapeDtypeStruct(grad.shape, F32)]
    anywhere = pl.BlockSpec(memory_space=pl.ANY)
    scratch = [pltpu.VMEM(value.shape, F32) for value in flat]
    scratch += [pltpu.VMEM(grad.shape, BF16), pltpu.VMEM(grad.shape, F32), pltpu.VMEM(result.shape, BF16)]
    scratch += [pltpu.SemaphoreType.DMA((len(flat) + 2,)), pltpu.SemaphoreType.DMA((len(new),))]
    return pl.pallas_call(
        functools.partial(update_kernel, rates),
        out_shape=tuple(new),
        in_specs=[anywhere] * (len(flat) + 2),
        out_specs=(anywhere,) * len(new),
        scratch_shapes=scratch,
        compiler_params=pltpu.CompilerParams(vmem_limit_bytes=63 * 1024 * 1024),
    )(*flat, result, grad)


def local(
    sub,
    tokens,
    cotangent,
    span_mask,
    attention_weight,
    expand_weight,
    reduce_weight,
    vectors,
    attention_first,
    attention_second,
    expand_first,
    expand_second,
    reduce_first,
    reduce_second,
    vector_first,
    vector_second,
):
    together = [[n * sub + m for m in range(sub)] for n in range(GROUPS)]

    def widen(value, axis):
        if sub == 1:
            return value
        low = lax.all_gather(
            value.astype(BF16), "batch", axis=axis, tiled=True, axis_index_groups=together
        )
        return low.astype(F32)

    def narrow(value, axis):
        if sub == 1:
            return value
        return lax.psum_scatter(
            value, "batch", scatter_dimension=axis, tiled=True, axis_index_groups=together
        )

    out_tokens, input_grad, ga, g1, g2, gv = layer(
        sub,
        tokens,
        cotangent,
        span_mask,
        widen(vectors, 1),
        widen(attention_weight, 2),
        widen(expand_weight, 1),
        widen(reduce_weight.T, 0),
    )
    arrays = (
        (attention_weight, attention_first, attention_second, narrow(ga, 2)),
        (expand_weight, expand_first, expand_second, narrow(g1, 1)),
        (reduce_weight.T, reduce_first.T, reduce_second.T, narrow(g2, 0)),
        (vectors, vector_first, vector_second, narrow(gv, 1)),
    )
    rates = (rate_attention, rate_expand, rate_reduce, rate_vector)
    new = update(rates, arrays, out_tokens, input_grad)
    return new[-2:] + new[0:6] + tuple(value.T for value in new[6:9]) + new[9:12]


def solution(mesh):
    sub = mesh.shape["batch"] // GROUPS
    sequences = P("batch", "blk", None)
    attention = P(None, "blk", "batch")
    matrix = P("blk", "batch")
    return jax.shard_map(
        functools.partial(local, sub),
        mesh=mesh,
        in_specs=(sequences, sequences, P("batch", "blk"), attention, matrix, matrix, matrix)
        + (attention,) * 2
        + (matrix,) * 6,
        out_specs=(sequences,) * 2 + (attention,) * 3 + (matrix,) * 9,
        check_vma=False,
    )
```

```python
import functools
import math

import jax
import jax.numpy as jnp
from jax import lax
from jax.experimental import pallas as pl
from jax.experimental.pallas import tpu as pltpu
from jax.sharding import PartitionSpec as P

HEADS = 12
HEAD = 64
STEP = 10
GROUPS = 8

norm_epsilon = 1e-05
beta_one = 0.9
beta_two = 0.999
adam_epsilon = 1e-08
decay_weight = 0.1
rate_attention = 0.05
rate_expand = 0.03
rate_reduce = 0.015
rate_vector = 0.4

F32 = jnp.float32
BF16 = jnp.bfloat16
MESH = pl.DeviceIdType.MESH
GELU_SCALE = math.sqrt(2.0 / math.pi)
GELU_CUBE = 0.044715


def adamw(weight, moment_one, moment_two, gradient, step_rate):
    moment_one = beta_one * moment_one + (1.0 - beta_one) * gradient
    moment_two = beta_two * moment_two + (1.0 - beta_two) * gradient * gradient
    corrected_one = moment_one / (1.0 - beta_one**STEP)
    corrected_two = moment_two / (1.0 - beta_two**STEP)
    updated = weight - step_rate * (
        corrected_one / (jnp.sqrt(corrected_two) + adam_epsilon) + decay_weight * weight
    )
    return (updated, moment_one, moment_two)


def dot_nn(left, right):
    return lax.dot_general(left, right, (((1,), (0,)), ((), ())), preferred_element_type=F32)


def dot_nt(left, right):
    return lax.dot_general(left, right, (((1,), (1,)), ((), ())), preferred_element_type=F32)


X, Y, Z = 1, 2, 4
(N_QKA, N_QKB, N_VOA, N_VOB, N_W10A, N_W10B, N_W11A, N_W11B, N_W20A, N_W20B, N_W21A, N_W21B) = range(12)
(N_AQKA, N_AQKB, N_AVOA, N_AVOB, N_G10, N_G11, N_G20, N_G21) = range(8)
QK, VO = (N_QKA, N_QKB), (N_VOA, N_VOB)
AQK, AVO = (N_AQKA, N_AQKB), (N_AVOA, N_AVOB)
SEND, GOT, WHOLE, SUM, VEC, SMALL, DO = range(7)
(TOK, COT, OUT, IG, TOK_HERE, COT_HERE, OUT_HERE,
 IG_HERE, SWAP_HERE, N2S_HERE, COTS_HERE, BACKS_HERE, AHEADS_HERE) = range(13)
GATHER_ROUTES = (
    ((Z, X, Y), (Z, Y, X),),
    ((Z, Y, X), (Z, Y, X),),
    ((Y, Z, X), (Y, Z, X),),
    ((X, Z, Y), (Z, Y, X),),
    ((Z, Y, X), (Z, Y, X),),
    ((Z, X, Y), (X, Y, Z),),
)
SUM_ROUTES = (
    ((Y, X, Z), (X, Z, Y),),
    ((Y, X, Z), (X, Z, Y),),
    ((Y, X, Z),),
    ((X, Y, Z),),
    ((Z, Y, X),),
    ((Y, Z, X),),
)
PLAN = dict(
    own1=(
        (SEND, N_QKA, 0, X), (SEND, N_QKA, 0, Z), (SEND, N_QKB, 0, X), (SEND, N_QKB, 0, Y),
        (SEND, N_QKB, 0, Z),
    ),
    ownff=(
        (SEND, N_VOA, 0, X), (SEND, N_VOB, 0, X), (DO, TOK), (SEND, N_VOA, 0, Z), (VEC, 0), (DO, SWAP_HERE),
        (GOT, N_QKA, X),
    ),
    mask=(
        (GOT, N_QKB, Y), (SEND, N_QKB, Y, X), (GOT, N_QKB, X), (SEND, N_W10A, 0, X), (SEND, N_W11A, 0, X),
    ),
    ln1=(
        (GOT, N_VOA, X), (VEC, 1), (GOT, N_QKA, Z), (GOT, N_VOB, X), (SEND, N_QKA, Z, X), (SEND, N_VOB, 0, Z),
        (GOT, N_QKB, Y | X), (SEND, N_W10B, 0, X), (GOT, N_W11A, X), (VEC, 2), (SEND, N_QKA, Z, Y),
        (GOT, N_QKB, Z), (SEND, N_QKB, Z, X), (SEND, N_QKB, Z, Y), (SEND, N_W11B, 0, Z), (GOT, N_QKA, Z | X),
        (SEND, N_W11B, 0, X), (SEND, N_QKA, Z | X, Y), (GOT, N_W10A, X), (GOT, N_VOA, Z), (SEND, N_VOA, Z, X),
        (DO, TOK_HERE), (SEND, N_W10A, 0, Z), (SEND, N_QKA, 0, Y), (GOT, N_QKB, Z | X), (SEND, N_QKA, X, Y),
        (GOT, N_W10B, X), (GOT, N_QKB, Z | Y), (SEND, N_QKB, Z | Y, X), (SEND, N_VOA, Z, Y), (GOT, N_VOB, Z),
        (SEND, N_VOB, Z, X), (VEC, 3), (SEND, N_W10B, 0, Z),
    ),
    unp0=(
        (GOT, N_VOA, Z | X), (GOT, N_QKA, Z | Y), (SEND, N_VOB, Z, Y), (GOT, N_W11B, X), (SEND, N_W21B, 0, X),
        (GOT, N_W11B, Z), (SEND, N_W11B, Z, X), (GOT, N_QKA, Z | X | Y), (SEND, N_W11A, 0, Z),
        (SEND, N_VOA, 0, Y), (GOT, N_QKB, Z | Y | X), (GOT, N_QKA, Y), (SEND, N_VOB, 0, Y),
        (GOT, N_QKA, X | Y), (SEND, N_W10A, 0, Y), (SEND, N_W10B, 0, Y), (GOT, N_VOB, Z | X),
        (GOT, N_W10A, Z), (SEND, N_W10A, Z, X), (SEND, N_W11A, X, Z), (SEND, N_W11B, Z, Y), (WHOLE, N_QKA),
        (WHOLE, N_QKB), (GOT, N_VOA, Z | Y), (SEND, N_VOA, Z | Y, X),
    ),
    projk=(
        (GOT, N_W11B, Z | X), (SEND, N_W11B, 0, Y),
    ),
    attend0=(
        (GOT, N_W21B, X), (GOT, N_W10B, Z), (GOT, N_VOB, Z | Y), (SEND, N_VOB, Z | Y, X), (DO, COT),
    ),
    attend1=(
        (GOT, N_VOA, Y), (SEND, N_VOA, Y, X), (GOT, N_VOB, Y), (SEND, N_VOB, Y, X),
    ),
    attend2=(
        (GOT, N_W10A, Z | X), (SEND, N_W10B, Z, X), (GOT, N_W10A, Y), (SEND, N_W10A, Y, Z),
    ),
    attend3=(
        (GOT, N_W11A, Z), (GOT, N_W10B, Y), (SEND, N_W10B, Y, Z),
    ),
    attend4=(
        (GOT, N_VOA, Z | Y | X),
    ),
    attend5=(
        (GOT, N_W11B, Z | Y), (SEND, N_W11B, Z | Y, X), (GOT, N_W11A, X | Z), (GOT, N_W11B, Y),
        (SEND, N_W20A, 0, Z),
    ),
    unp1=(
        (GOT, N_VOB, Z | Y | X), (GOT, N_VOA, Y | X), (GOT, N_VOB, Y | X), (SEND, N_W11A, Z, Y),
        (GOT, N_W10A, Y | Z), (SEND, N_W10A, Y | Z, X), (SEND, N_W20B, 0, Z), (WHOLE, N_VOA), (WHOLE, N_VOB),
        (GOT, N_W10B, Z | X),
    ),
    projv=(
        (SEND, N_W11A, X | Z, Y),
    ),
    mix0=(
        (SEND, N_W10A, Y, X), (SEND, N_W10B, Y, X),
    ),
    mix1=(
        (GOT, N_W10B, Y | Z), (SEND, N_W10B, Y | Z, X), (SEND, N_W21A, 0, Z),
    ),
    mix3=(
        (GOT, N_W11B, Z | Y | X), (SEND, N_W11B, Y, X), (SEND, N_W11A, 0, Y),
    ),
    ao=(
        (SEND, N_W21A, 0, X), (SEND, N_W11A, X, Y),
    ),
    ln2=(
        (DO, COT_HERE),
    ),
    expa0=(
        (GOT, N_W10A, Y | Z | X), (GOT, N_W20A, Z), (SEND, N_W20A, Z, X), (SEND, N_W20A, Z, Y),
        (SEND, N_W21B, 0, Z), (GOT, N_W11A, Z | Y), (GOT, N_W10B, Y | Z | X), (DO, COTS_HERE),
        (GOT, N_W10A, Y | X), (GOT, N_W20B, Z), (SEND, N_W20B, Z, X), (SEND, N_W20B, Z, Y),
        (SEND, N_W21B, X, Z), (GOT, N_W10B, Y | X), (GOT, N_W11A, X | Z | Y), (DO, N2S_HERE),
        (SEND, N_W21B, 0, Y), (GOT, N_W11B, Y | X), (GOT, N_W11A, Y), (SEND, N_W21B, X, Y), (GOT, N_W21A, X),
        (GOT, N_W11A, X | Y), (SEND, N_W20A, 0, Y),
    ),
    expa1=(
        (GOT, N_W21A, Z), (SEND, N_W21A, Z, X), (SEND, N_W20B, 0, Y), (SEND, N_W21A, Z, Y),
        (GOT, N_W20A, Z | X), (GOT, N_W20A, Z | Y), (SEND, N_W20A, Z | Y, X),
    ),
    expb0=(
        (GOT, N_W21B, Z),
    ),
    expb1=(
        (GOT, N_W20B, Z | X), (GOT, N_W20B, Z | Y), (SEND, N_W20B, Z | Y, X), (GOT, N_W21B, Y),
        (SEND, N_W21B, Y, Z), (SEND, N_W20A, 0, X), (GOT, N_W21B, X | Y), (SEND, N_W21B, X | Y, Z),
        (SEND, N_W20B, 0, X), (SEND, N_W21A, 0, Y),
    ),
    trY=(
        (GOT, N_W21A, Z | X), (SEND, N_W21A, Z | X, Y), (GOT, N_W20A, Y), (SEND, N_W20A, Y, X),
        (GOT, N_W21B, X | Z), (SEND, N_W21A, X, Y), (GOT, N_W20B, Y), (SEND, N_W20B, Y, X),
    ),
    gw2_0=(
        (GOT, N_W20A, Z | Y | X),
    ),
    gw2_1=(
        (GOT, N_W21A, Z | Y), (GOT, N_W21B, Y | Z), (GOT, N_W20B, Z | Y | X),
    ),
    innb0=(
        (GOT, N_W20A, X), (GOT, N_W21A, Z | X | Y), (GOT, N_W20B, X), (GOT, N_W21A, Y), (SUM, N_G20, 0),
        (SUM, N_G21, 0), (GOT, N_W21B, X | Y | Z), (GOT, N_W20A, Y | X), (GOT, N_W21A, X | Y),
        (GOT, N_W20B, Y | X),
    ),
    gw1_0=(
        (DO, BACKS_HERE),
    ),
    hid=(
        (SUM, N_G10, 0), (SUM, N_G11, 0),
    ),
    dO=(
        (SUM, N_G21, 1),
    ),
    ab4=(
        (SUM, N_G20, 1),
    ),
    ab5=(
        (SUM, N_G10, 1), (SUM, N_G11, 1),
    ),
    gaqk=(
        (SUM, N_G20, 2),
    ),
    reda=(
        (SUM, N_AVOB, 0), (SUM, N_G10, 2), (SUM, N_AVOA, 0),
    ),
    outst=(
        (SUM, N_G20, 3), (SUM, N_G11, 2), (SUM, N_AQKB, 0), (SUM, N_G21, 2), (SUM, N_AQKA, 0),
        (DO, AHEADS_HERE),
    ),
    end=(
        (SUM, N_AVOB, 1), (SUM, N_AVOA, 1), (SUM, N_G10, 3), (DO, OUT), (SUM, N_AQKB, 1), (SUM, N_AQKA, 1),
        (SUM, N_G11, 3), (SMALL, 0), (SUM, N_AVOA, 2), (SMALL, 1), (DO, IG), (SUM, N_G21, 3),
        (SUM, N_AVOB, 2), (SUM, N_AQKA, 2), (SMALL, 2), (DO, OUT_HERE), (SUM, N_AQKB, 2), (SUM, N_AVOA, 3),
        (DO, IG_HERE), (SUM, N_AVOB, 3), (SUM, N_AQKB, 3), (SUM, N_AQKA, 3), (SMALL, 3),
    ),
)


def lane_tiles(ref, count=6):
    return jnp.concatenate([ref[t] for t in range(count)], axis=1)


class Unit:
    def __init__(self, index, route, rows, u, other):
        self.index, self.route, self.rows, self.u, self.other = index, route, rows, u, other


class Gradient:
    def __init__(self, index, route, rows, u, other, core_in, got, total):
        self.index, self.route, self.rows, self.u, self.other = index, route, rows, u, other
        self.core_in, self.got, self.total = core_in, got, total


def kernel(sub, zs, *refs):
    (tok, cot, mask_in, vec_in, a_in, w1_in, w2_in,
     out, ig, ga, g1, g2, gv,
     ua, uw1, uw2, gw1, gw2, core_in, got,
     x_in, cot_in, stage, vec, gvec, vin, gin, narrow_rows,
     at, n1, q6, k6, v6, o6, pt, h1, acc, n2, act, gp, ta, tb, tc, d6,
     w1_other, w2_other, n2_other, cot_other, back_in, ahead_in,
     lines, b1, gb1, totals, turned1, got1, got2,
     local_sem, ag_send, ag_recv, core_send, core_recv, rs_send, rs_recv,
     a2a_send, a2a_recv, v_send, v_recv, pair_send, pair_recv) = refs

    i = lax.axis_index("blk")
    b = lax.axis_index("batch")
    c, y = lax.rem(i, 2), lax.div(i, 2)
    g, r = lax.div(b, sub), lax.rem(b, sub)
    x, z = lax.rem(g, 2), lax.div(g, 2)

    def device(c_=c, y_=y, x_=x, z_=z):
        return {"blk": 2 * y_ + c_, "batch": (2 * z_ + x_) * sub + r}

    def z_at(k):
        return lax.rem(z + k, zs)

    def block_at(k):
        return lax.rem(i + k, 4)

    def copy(src, dst, send, recv, to):
        return pltpu.make_async_remote_copy(
            src_ref=src, dst_ref=dst, send_sem=send, recv_sem=recv, device_id=to, device_id_type=MESH
        )

    def loop(count, body, hooks=()):
        def step(s, carry):
            body(s)
            for k, f in hooks:
                pl.when(s == k)(f)
            return carry

        lax.fori_loop(0, count, step, 0)

    partners = [device(z_=z_at(k)) for k in range(1, zs)]
    partners += [device(x_=1 - x), device(y_=1 - y), device(c_=1 - c), device(c_=1 - c, y_=1 - y)]
    barrier = pltpu.get_barrier_semaphore()
    for partner in partners:
        pl.semaphore_signal(barrier, inc=1, device_id=partner, device_id_type=MESH)
    pl.semaphore_wait(barrier, len(partners))

    def offsets(axes):
        return [(dy, dx, dz)
                for dy in ((1,) if "y" in axes else (0,))
                for dx in ((1,) if "x" in axes else (0,))
                for dz in (range(1, zs) if "z" in axes else (0,))]

    def owner(d):
        dy, dx, dz = d
        return (1 - y if dy else y, 1 - x if dx else x, z if isinstance(dz, int) and dz == 0 else z_at(zs - dz))

    def moves(d, axis):
        dy, dx, dz = d
        if axis == "y":
            return [(device(y_=1 - y), (1, dx, dz))]
        if axis == "x":
            return [(device(x_=1 - x), (dy, 1, dz))]
        return [(device(z_=z_at(k)), (dy, dx, k)) for k in range(1, zs)]

    def piece(n, d):
        return n.u.at[owner(d) + (n.rows,)]

    def ag_copy(n, ref, d, to):
        slot = (d[0] * 2 + d[1]) * zs + d[2]
        return copy(ref, ref, ag_send.at[n.index, slot], ag_recv.at[n.index, slot], to)

    def core_copy(n, ref):
        return copy(ref, ref, core_send.at[n.index], core_recv.at[n.index], device(c_=1 - c))

    def ag_send_part(n, axes, axis):
        for d in offsets(axes):
            ref = piece(n, d)
            for to, there in moves(d, axis):
                ag_copy(n, ref, there, to).start()

    def ag_wait_part(n, axes):
        for d in offsets(axes):
            ref = piece(n, d)
            ag_copy(n, ref, d, device()).wait_recv()
            if n.other is not None:
                core_copy(n, ref).start()

    def ag_done(n):
        if n.other is not None:
            core_copy(n, n.other.at[:, :, :, n.rows]).wait_recv()

    def ag_drain(n):
        own = piece(n, (0, 0, 0))
        for d in [(dy, dx, dz) for dy in range(2) for dx in range(2) for dz in range(zs)][1:]:
            ag_copy(n, own, d, device()).wait_send()
        if n.other is not None:
            core_copy(n, n.u.at[:, :, :, n.rows]).wait_send()

    AXES = "yxz"

    def step_region(n, step, k):
        where = []
        for axis in AXES:
            at_step = n.route.index(axis)
            where.append(0 if at_step < step else (k if at_step == step else slice(None)))
        return n.got.at[tuple(where) + (n.rows,)]

    def step_groups(n, step):
        axis = n.route[step]
        if axis == "y":
            return [(1, 0, device(y_=1 - y))]
        if axis == "x":
            return [(1, 1, device(x_=1 - x))]
        return [(k, 1 + k, device(z_=z_at(zs - k))) for k in range(1, zs)]

    def rs_group(n, step, k, slot, to):
        ref = step_region(n, step, k)
        return copy(ref, ref, rs_send.at[n.index, slot], rs_recv.at[n.index, slot], to)

    def step_offsets(n, step, k):
        spans = []
        for axis, size in zip(AXES, (2, 2, zs)):
            at_step = n.route.index(axis)
            spans.append((0,) if at_step < step else ((k,) if at_step == step else tuple(range(size))))
        return spans

    def add_terms(n, d, step):
        dy, dx, dz = d
        value = piece(n, d)[...].astype(F32)
        if n.other is not None:
            value = value + n.core_in[dy, dx, dz, n.rows].astype(F32)
        for axis in n.route[:step]:
            if axis == "y":
                value = value + n.got[1, dx, dz, n.rows].astype(F32)
            elif axis == "x":
                value = value + n.got[dy, 1, dz, n.rows].astype(F32)
            else:
                for k in range(1, zs):
                    value = value + n.got[dy, dx, k, n.rows].astype(F32)
        return value

    def rs_start(n):
        for dy in range(2):
            for dx in range(2):
                for dz in range(zs):
                    d = (dy, dx, dz)
                    copy(n.other.at[owner(d) + (n.rows,)], n.core_in.at[d + (n.rows,)], rs_send.at[n.index, zs + 1],
                         rs_recv.at[n.index, zs + 1], device(c_=1 - c)).start()

    def rs_core_whole(n):
        ref = n.core_in.at[:, :, :, n.rows]
        return copy(ref, ref, rs_send.at[n.index, zs + 1], rs_recv.at[n.index, zs + 1], device(c_=1 - c))

    def rs_step(n, step):
        if step == 0 and n.other is not None:
            rs_core_whole(n).wait_recv()
        if step > 0:
            for k, slot, to in step_groups(n, step - 1):
                rs_group(n, step - 1, k, slot, to).wait_recv()
        if step == 3:
            n.total[n.rows, :] = add_terms(n, (0, 0, 0), 3)
            return
        for k, slot, to in step_groups(n, step):
            dys, dxs, dzs = step_offsets(n, step, k)
            if step > 0 or n.other is not None:

                def body(e):
                    for dy in dys:
                        for dx in dxs:
                            d = (dy, dx, dzs[0] if len(dzs) == 1 else e)
                            piece(n, d)[...] = add_terms(n, d, step).astype(BF16)

                if len(dzs) == 1:
                    body(0)
                else:
                    loop(zs, body)
            for dy in dys:
                for dx in dxs:
                    for dz in dzs:
                        d = (dy, dx, dz)
                        copy(piece(n, d), n.got.at[d + (n.rows,)], rs_send.at[n.index, slot],
                             rs_recv.at[n.index, slot], to).start()

    def rs_drain(n):
        if n.other is not None:
            rs_core_whole(n).wait_send()
        for step in range(3):
            for group in step_groups(n, step):
                rs_group(n, step, *group).wait_send()

    def small_sum(ref, slots, which):
        to = (device(y_=1 - y), device(c_=1 - c), device(x_=1 - x))
        to += tuple(device(z_=z_at(k)) for k in range(1, zs))

        def moved(slot):
            return copy(ref, slots.at[slot], v_send.at[which, slot], v_recv.at[which, slot], to[slot])

        def land(last):
            moved(last).wait()
            ref[...] = ref[...] + slots[last]

        def step(n):
            def run():
                if n > 0:
                    land(n - 1)
                moved(n).start()

            return run

        def line():
            land(2)
            for k in range(1, zs):
                moved(2 + k).start()

        def finish():
            for k in range(1, zs):
                moved(2 + k).wait()
            value = ref[...]
            for k in range(1, zs):
                value = value + slots[2 + k]
            ref[...] = value

        return [step(0), step(1), step(2), line, finish]

    def rows_of(s):
        return pl.ds(pl.multiple_of(s * 128, 128), 128)

    def exchange(src, dst, which):
        return [copy(src.at[block_at(k)], dst.at[i], a2a_send.at[which, k - 1],
                     a2a_recv.at[which, k - 1], {"blk": block_at(k), "batch": b})
                for k in range(1, 4)]

    def exchange_landed(dst, which):
        return [copy(dst.at[block_at(4 - k)], dst.at[block_at(4 - k)], a2a_send.at[which, k - 1],
                     a2a_recv.at[which, k - 1], {"blk": block_at(4 - k), "batch": b})
                for k in range(1, 4)]

    def axes_of(mask):
        return "".join(axis for axis, bit in (("y", Y), ("x", X), ("z", Z)) if mask & bit)

    def rows_in(part, count):
        return pl.ds(part * (288 // count), 288 // count)

    units = []
    for unit, routes in enumerate(GATHER_ROUTES):
        half = unit % 2
        ref = (ua, uw1, uw2)[unit // 2]
        pieces = (ref.at[half, c], ref.at[half, 1 - c]) if unit < 2 else (ref.at[half], None)
        for part, route in enumerate(routes):
            units.append(Unit(len(units), "".join(map(axes_of, route)), rows_in(part, len(routes)), *pieces))

    def pair(slot, src, dst):
        return copy(src, dst, pair_send.at[slot], pair_recv.at[slot], device(c_=1 - c))

    w1_swap, w2_swap = pair(0, w1_in, w1_other), pair(1, w2_in, w2_other)

    def each_core(f):
        for q in range(2):
            pl.when(c == q)(functools.partial(f, q))

    def rest_rows(matrix):
        return a_in[matrix, pl.ds(pl.multiple_of(128 * (1 - c), 64), 64), :]

    def own_attention(p):
        mine = ua.at[p, c, y, x, z]
        for m in range(2):
            main = a_in[2 * p + m, pl.ds(pl.multiple_of(64 * c, 64), 128), :]
            mine[96 * m : 96 * m + 96, :] = main.T.astype(BF16)
        rest = jnp.concatenate([rest_rows(2 * p + c), rest_rows(2 * p + 1 - c)], axis=0)
        mine[192:288, :] = rest.T.astype(BF16)

    def own_expand(q):
        both = (w1_in, w1_other) if q == 0 else (w1_other, w1_in)
        cols = slice(192 * q, 192 * q + 192)
        blocks = (
            both[0][0:128, cols],
            jnp.concatenate([both[0][128:192, cols], both[1][0:64, cols]], axis=0),
            both[1][64:192, cols],
        )
        for t, block in enumerate(blocks):
            value = block.T.astype(BF16)
            for h in range(2):
                uw1[h, y, x, z, 96 * t : 96 * t + 96, :] = value[96 * h : 96 * h + 96, :]

    def own_reduce(q):
        both = (w2_in, w2_other) if q == 0 else (w2_other, w2_in)
        for cc in range(2):
            for part_of in range(2):
                start = 384 * part_of + 192 * q
                lines[:, 192 * part_of : 192 * part_of + 192] = both[cc][:, start : start + 192]
            for t in range(3):
                uw2[cc, y, x, z, 96 * t : 96 * t + 96, :] = lines[:, 128 * t : 128 * t + 128].astype(BF16)

    def own_hidden_bias(q):
        for zz in range(zs):
            for xx in range(2):
                col = 384 * (zz % 2) + 192 * xx
                start = 384 * xx + 192 * q
                b1[zz // 2 : zz // 2 + 1, col : col + 192] = vec[8 + zz : 9 + zz, start : start + 192]

    def hidden_bias_gradient(q):
        for zz in range(zs):
            for xx in range(2):
                col = 384 * (zz % 2) + 192 * xx
                start = 384 * xx + 192 * q
                gvec[8 + zz : 9 + zz, start : start + 192] = gb1[zz // 2 : zz // 2 + 1, col : col + 192]

    columns = a_in.shape[2]
    placed = lax.broadcasted_iota(jnp.int32, (columns, 768), 1) == (
        lax.broadcasted_iota(jnp.int32, (columns, 768), 0) + columns * g
    )

    def own_vectors():
        vec[...] = jnp.zeros_like(vec)
        rows = dot_nn(vec_in[...].astype(BF16), jnp.where(placed, 1.0, 0.0).astype(BF16))
        for j in range(3):
            vec[pl.ds(3 * i + j, 1), :] = rows[j : j + 1, :]

    load_cot = pltpu.make_async_copy(cot, stage, local_sem.at[4])

    def masked_cotangent():
        load_cot.wait()
        eye = lax.broadcasted_iota(jnp.int32, (128, 128), 0) == lax.broadcasted_iota(jnp.int32, (128, 128), 1)
        for s in range(4):
            row = jnp.broadcast_to(mask_in[s : s + 1, :].astype(F32), (128, 128))
            column = jnp.sum(jnp.where(eye, row, 0.0), axis=1, keepdims=True)
            stage[s] = (stage[s].astype(F32) * column).astype(BF16)

    def finish_attention(p):
        value = totals.at[p]
        for m in range(2):
            ga[2 * p + m, pl.ds(pl.multiple_of(64 * c, 64), 128), :] = value[96 * m : 96 * m + 96, :].T
        rest = value[192:288, :].T
        rows = pl.ds(pl.multiple_of(128 * (1 - c), 64), 64)
        ga[2 * p + c, rows, :] = rest[0:64, :]
        ga[2 * p + 1 - c, rows, :] = rest[64:128, :]

    w1_back = pair(6, turned1.at[pl.ds(pl.multiple_of(192 * (1 - c), 64), 192)], got1)
    w2_back = pair(7, totals.at[5 - c], got2)

    def turn_expand():
        for h in range(2):
            for t in range(3):
                turned1[128 * t : 128 * t + 128, 96 * h : 96 * h + 96] = totals[2 + h, 96 * t : 96 * t + 96, :].T
        w1_back.start()

    def join_expand(q):
        g1[:, 192 * q : 192 * q + 192] = turned1[192 * q : 192 * q + 192, :]
        g1[:, 192 * (1 - q) : 192 * (1 - q) + 192] = got1[...]

    def join_reduce(q):
        for half, value in ((q, totals.at[4 + q]), (1 - q, got2)):
            for t in range(3):
                lines[:, 128 * t : 128 * t + 128] = value[96 * t : 96 * t + 96, :]
            for part_of in range(2):
                start = 384 * part_of + 192 * half
                g2[:, start : start + 192] = lines[:, 192 * part_of : 192 * part_of + 192]

    def finish_vectors():
        value, total = gvec[...], 0.0
        for _ in range(3):
            part = value.astype(BF16)
            total = total + dot_nt(part, jnp.where(placed, 1.0, 0.0).astype(BF16))
            value = value - part.astype(F32)
        narrow_rows[...] = total
        for j in range(3):
            gv[j : j + 1, :] = narrow_rows[pl.ds(3 * i + j, 1), :]

    grads, owners = [], []
    for unit, routes in enumerate(SUM_ROUTES):
        half = unit % 2
        ref = (ua, gw1, gw2)[unit // 2]
        pieces = (ref.at[half, c], ref.at[half, 1 - c], core_in.at[half]) if unit < 2 else (ref.at[half], None, None)
        for part, route in enumerate(routes):
            grads.append(Gradient(len(grads), "".join(map(axes_of, route)), rows_in(part, len(routes)), *pieces,
                                  got.at[unit], totals.at[unit]))
            owners.append(unit)

    def summed(unit):
        if unit < 2:
            finish_attention(unit)
        elif unit < 4 and {2, 3} <= set(whole):
            turn_expand()
        elif unit >= 4 and {4, 5} <= set(whole):
            w2_back.start()

    seen, whole = set(), []

    def event(kind, *rest):
        if kind == SEND:
            ag_send_part(units[rest[0]], axes_of(rest[1]), axes_of(rest[2]))
        elif kind == GOT:
            ag_wait_part(units[rest[0]], axes_of(rest[1]))
        elif kind == WHOLE:
            ag_done(units[rest[0]])
        elif kind == SUM:
            rs_step(grads[rest[0]], rest[1])
            if rest[1] == 3:
                seen.add(rest[0])
                unit = owners[rest[0]]
                if all(k in seen for k in range(len(grads)) if owners[k] == unit):
                    whole.append(unit)
                    summed(unit)
        elif kind == DO:
            actions[rest[0]]()
        else:
            (vec_steps if kind == VEC else gvec_steps)[rest[0] + 1]()

    def run(part):
        for todo in PLAN.get(part, ()):
            event(*todo)

    def parts(name, count, body):
        run(name + "0")
        hooks = [(k - 1, functools.partial(run, name + str(k))) for k in range(1, count) if name + str(k) in PLAN]
        loop(count, body, hooks)

    def started(copies):
        for moved in copies:
            moved.start()
        return copies

    def arrived(*copies):
        for moved in copies:
            moved.wait_recv()

    load_cot.start()
    own_tokens = pltpu.make_async_copy(tok.at[i], x_in.at[i], local_sem.at[0])
    own_tokens.start()
    own_cot = pltpu.make_async_copy(stage.at[i], cot_in.at[i], local_sem.at[1])
    tokens_out, cot_out = exchange(tok, x_in, 0), exchange(stage, cot_in, 1)
    result_out = exchange(stage, out, 2)
    grad_out = [copy(n1.at[rows_of(block_at(k))], ig.at[i], a2a_send.at[3, k - 1], a2a_recv.at[3, k - 1],
                     {"blk": block_at(k), "batch": b}) for k in range(1, 4)]
    own_out = pltpu.make_async_copy(stage.at[i], out.at[i], local_sem.at[2])
    own_grad = pltpu.make_async_copy(n1.at[rows_of(i)], ig.at[i], local_sem.at[3])
    n2_swap, cot_swap = pair(2, n2, n2_other), pair(3, cot_in, cot_other)
    back_swap, ahead_swap = pair(4, d6, back_in), pair(5, n2, ahead_in)
    vec_steps, gvec_steps = small_sum(vec, vin, 0), small_sum(gvec, gin, 1)

    def tokens_here():
        arrived(*exchange_landed(x_in, 0))
        own_tokens.wait()

    def cotangent_here():
        arrived(*exchange_landed(cot_in, 1))
        own_cot.wait()
        cot_swap.start()

    def swaps_here():
        w1_swap.wait()
        w2_swap.wait()

    actions = {
        TOK: lambda: started(tokens_out),
        COT: lambda: started(cot_out),
        OUT: lambda: started(result_out),
        IG: lambda: started(grad_out),
        TOK_HERE: tokens_here,
        COT_HERE: cotangent_here,
        OUT_HERE: lambda: arrived(*exchange_landed(out, 2)),
        IG_HERE: lambda: arrived(*exchange_landed(ig, 3)),
        SWAP_HERE: swaps_here,
        N2S_HERE: lambda: n2_swap.wait(),
        COTS_HERE: lambda: cot_swap.wait(),
        BACKS_HERE: lambda: back_swap.wait(),
        AHEADS_HERE: lambda: ahead_swap.wait(),
    }

    def core_own(first, last):
        for n in units[first : last + 1]:
            core_copy(n, piece(n, (0, 0, 0))).start()

    own_attention(0)
    core_own(*QK)
    w1_swap.start()
    w2_swap.start()
    own_vectors()
    vec_steps[0]()
    run("own1")
    own_attention(1)
    core_own(*VO)
    run("ownff")
    each_core(own_expand)
    each_core(own_reduce)
    run("mask")
    masked_cotangent()
    own_cot.start()
    run("ln1")
    each_core(own_hidden_bias)

    def normalise(value):
        centered = value - jnp.mean(value, axis=-1, keepdims=True)
        scale = lax.rsqrt(jnp.mean(centered * centered, axis=-1, keepdims=True) + norm_epsilon)
        return centered * scale, scale

    def first_norm(s):
        unit, _ = normalise(x_in[s].astype(F32))
        n1[rows_of(s), :] = (unit * vec[0:1, :] + vec[1:2, :]).astype(BF16)

    loop(4, first_norm)
    run("unp0")

    lanes = lax.broadcasted_iota(jnp.int32, (96, 128), 1)

    def unpack(p, s):
        for xx in range(2):
            rows = pl.ds(pl.multiple_of((2 * s + xx) * 96, 96), 96)
            for yy in range(2):
                first, second = ua.at[p, 0, yy, xx, s], ua.at[p, 1, yy, xx, s]
                lo, hi = 384 * yy, 384 * yy + 256
                for m in range(2):
                    at[2 * p + m, rows, lo : lo + 128] = first[96 * m : 96 * m + 96, :]
                    at[2 * p + m, rows, hi : hi + 128] = second[96 * m : 96 * m + 96, :]
                rest_first = first[192:288, :].astype(F32)
                rest_second = second[192:288, :].astype(F32)
                even = jnp.where(lanes < 64, rest_first, rest_second)
                odd = pltpu.roll(jnp.where(lanes < 64, rest_second, rest_first), 64, 1)
                at[2 * p, rows, lo + 128 : lo + 256] = even.astype(BF16)
                at[2 * p + 1, rows, lo + 128 : lo + 256] = odd.astype(BF16)

    def project(m, dst, bias):
        for n in range(3):
            value = dot_nt(n1[...], at[m, 256 * n : 256 * n + 256, :])
            if bias is not None:
                value = value + vec[bias : bias + 1, 256 * n : 256 * n + 256]
            value = value.astype(BF16)
            if m == 0:
                value = value * jnp.asarray(HEAD ** (-0.5), BF16)
            dst[2 * n] = value[:, 0:128]
            dst[2 * n + 1] = value[:, 128:256]

    loop(zs, functools.partial(unpack, 0))
    run("projq")
    project(0, q6, 2)
    run("projk")
    project(1, k6, None)

    half_lane = lax.broadcasted_iota(jnp.int32, (512, 128), 1) // HEAD

    def half_of(value, which):
        return jnp.where(half_lane == which, value, jnp.zeros_like(value))

    def turn(value):
        return value.astype(F32).T.astype(BF16)

    def attend(p):
        queries, keys = q6[p], k6[p]
        for which in range(2):
            scores = dot_nt(half_of(keys, which), queries)
            expo = jnp.exp(scores - jnp.max(scores, axis=0, keepdims=True))
            probs = (expo * (1.0 / jnp.sum(expo, axis=0, keepdims=True))).astype(BF16)
            pt[2 * p + which] = probs

    def mix(p):
        values_t = turn(v6[p])
        mixed = [dot_nn(values_t[64 * which : 64 * which + 64, :], pt[2 * p + which]) for which in range(2)]
        o6[p] = jnp.concatenate(mixed, axis=0).T.astype(BF16)

    parts("attend", 6, attend)
    run("unp1")
    loop(zs, functools.partial(unpack, 1))
    run("projv")
    project(2, v6, 3)
    parts("mix", 6, mix)

    run("ao")
    for n in range(3):
        cols = slice(256 * n, 256 * n + 256)
        value = dot_nt(lane_tiles(o6), at[3, cols, :]) + vec[4:5, cols]
        for s in range(4):
            h1[128 * s : 128 * s + 128, cols] = x_in[s, :, cols].astype(F32) + value[128 * s : 128 * s + 128]

    def second_norm(s):
        unit, _ = normalise(h1[rows_of(s), :])
        n2[rows_of(s), :] = (unit * vec[5:6, :] + vec[6:7, :]).astype(BF16)

    run("ln2")
    loop(4, second_norm)
    n2_swap.start()

    def expand_block(s):
        def piece(ref):
            return jnp.concatenate([ref[96 * t : 96 * t + 96, :] for t in range(3)], axis=1)

        return jnp.concatenate(
            [jnp.concatenate([piece(uw1.at[h, yy, xx, 2 * s + zz]) for yy in range(2)], axis=1)
             for zz in range(2) for xx in range(2) for h in range(2)],
            axis=0,
        )

    def reduce_block(s):
        def piece(ref):
            return jnp.concatenate([ref[96 * t : 96 * t + 96, :] for t in range(3)], axis=1)

        return jnp.concatenate(
            [jnp.concatenate([piece(uw2.at[cc, s, xx, zz]) for cc in range(2)], axis=1)
             for zz in range(zs) for xx in range(2)],
            axis=0,
        )

    def block_rows(owner, s):
        return pl.ds(pl.multiple_of((2 * owner + s) * 512, 512), 512)

    def expand(owner, normed, s):
        rows = block_rows(owner, s)
        inner = dot_nt(normed[...], expand_block(s)) + b1[pl.ds(s, 1), :]
        square = inner * inner
        tanh = jnp.tanh(GELU_SCALE * inner * (1.0 + GELU_CUBE * square))
        act[rows, :] = (0.5 * inner * (1.0 + tanh)).astype(BF16)
        slope = 0.5 * (1.0 + tanh) + 0.5 * inner * (1.0 - tanh * tanh) * (
            GELU_SCALE * (1.0 + 3.0 * GELU_CUBE * square)
        )
        gp[rows, :] = slope.astype(BF16)

    parts("expa", 2, functools.partial(expand, 0, n2))
    parts("expb", 2, functools.partial(expand, 1, n2_other))

    gvec[...] = jnp.zeros_like(gvec)

    def transpose_rows(dst, s, value):
        dst[:, 128 * s : 128 * s + 128] = turn(value)

    run("trY")
    total = jnp.zeros((1, 768), F32)
    for s in range(4):
        transpose_rows(ta, s, cot_in[s])
        total = total + jnp.sum(cot_in[s].astype(F32), axis=0, keepdims=True)
    gvec[7:8, :] = total
    for s in range(4):
        transpose_rows(tb, s, cot_other[s])

    def both_rows(ref, s):
        return jnp.concatenate([ref[block_rows(0, s), :], ref[block_rows(1, s), :]], axis=0)

    def reduce_back(s):
        grad = dot_nn(jnp.concatenate([ta[...], tb[...]], axis=1), both_rows(act, s)).astype(BF16)
        for zz in range(zs):
            for xx in range(2):
                row = 96 * (2 * zz + xx)
                for cc in range(2):
                    for t in range(3):
                        col = 384 * cc + 128 * t
                        gw2[cc, s, xx, zz, 96 * t : 96 * t + 96, :] = grad[row : row + 96, col : col + 128]

    parts("gw2_", 2, reduce_back)

    def rows_together(ref):
        return jnp.concatenate([ref[s] for s in range(4)], axis=0)

    def inner_back(owner, cotangent_rows, s):
        rows = block_rows(owner, s)
        grad = dot_nn(rows_together(cotangent_rows), reduce_block(s)) * gp[rows, :].astype(F32)
        low = grad.astype(BF16)
        gp[rows, :] = low
        sums = jnp.sum(low.astype(F32), axis=0, keepdims=True)
        gb1[pl.ds(s, 1), :] = sums if owner == 1 else gb1[pl.ds(s, 1), :] + sums

    def norm_back(owner):
        acc[...] = dot_nn(gp[block_rows(owner, 0), :], expand_block(0))
        acc[...] += dot_nn(gp[block_rows(owner, 1), :], expand_block(1))

    parts("innb", 2, functools.partial(inner_back, 1, cot_other))
    run("dn2b")
    norm_back(1)
    for t in range(6):
        d6[t] = acc[:, 128 * t : 128 * t + 128].astype(BF16)
    back_swap.start()
    parts("inna", 2, functools.partial(inner_back, 0, cot_in))
    each_core(hidden_bias_gradient)
    run("dn2a")
    norm_back(0)

    def expand_back(s):
        turned = jnp.concatenate([turn(gp[block_rows(owner, s), :]) for owner in range(2)], axis=1)
        normed = jnp.concatenate([n2[...], n2_other[...]], axis=0)
        grad = dot_nn(turned, normed).astype(BF16)
        for zz in range(2):
            for xx in range(2):
                for h in range(2):
                    row = 384 * zz + 192 * xx + 96 * h
                    for yy in range(2):
                        for t in range(3):
                            col = 384 * yy + 128 * t
                            gw1[h, yy, xx, 2 * s + zz, 96 * t : 96 * t + 96, :] = grad[
                                row : row + 96, col : col + 128
                            ]

    parts("gw1_", 2, expand_back)
    run("hid")

    def norm_gradient(value, scale_row, grad):
        unit, scale = normalise(value)
        gain_sum = jnp.sum(grad * unit, axis=0, keepdims=True)
        bias_sum = jnp.sum(grad, axis=0, keepdims=True)
        inner = grad * scale_row
        mean = jnp.mean(inner, axis=-1, keepdims=True)
        along = jnp.mean(inner * unit, axis=-1, keepdims=True)
        return scale * (inner - mean - unit * along), gain_sum, bias_sum

    def hidden_back(s):
        rows = rows_of(s)
        grad_in = jnp.concatenate([back_in[t, rows, :] for t in range(6)], axis=1)
        grad_in = acc[rows, :] + grad_in.astype(F32)
        grad, gain_sum, bias_sum = norm_gradient(h1[rows, :], vec[5:6, :], grad_in)
        grad = grad + cot_in[s].astype(F32)
        acc[rows, :] = grad
        low = grad.astype(BF16)
        n2[rows, :] = low
        gvec[5:6, :] += gain_sum
        gvec[6:7, :] += bias_sum
        gvec[4:5, :] += jnp.sum(low.astype(F32), axis=0, keepdims=True)

    loop(4, hidden_back)

    run("dO")
    for n in range(3):
        value = dot_nn(n2[...], at[3, :, 256 * n : 256 * n + 256]).astype(BF16)
        d6[2 * n] = value[:, 0:128]
        d6[2 * n + 1] = value[:, 128:256]
    run("gao")
    for s in range(4):
        transpose_rows(tc, s, n2[128 * s : 128 * s + 128, :])
    gp[768:1536, :] = dot_nn(tc[...], lane_tiles(o6)).astype(BF16)

    def attend_back(p):
        rows = rows_of(p)
        queries, keys, values, grads_in = q6[p], k6[p], v6[p], d6[p]
        keys_t = turn(keys)
        grad_query, grad_key, grad_value = [], 0.0, 0.0
        for which in range(2):
            probs = pt[2 * p + which]
            wide = probs.astype(F32)
            grad_probs = dot_nt(half_of(values, which), grads_in)
            inner = jnp.sum(wide * grad_probs, axis=0, keepdims=True)
            grad_scores = (wide * (grad_probs - inner)).astype(BF16)
            grad_query.append(dot_nn(keys_t[64 * which : 64 * which + 64, :], grad_scores))
            grad_key = grad_key + dot_nn(grad_scores, half_of(queries, which))
            grad_value = grad_value + dot_nn(probs, half_of(grads_in, which))
        grad_query = jnp.concatenate(grad_query, axis=0) * HEAD ** (-0.5)
        ta[rows, :] = grad_query.astype(BF16)
        tb[rows, :] = grad_key.T.astype(BF16)
        tc[rows, :] = grad_value.T.astype(BF16)
        q6[p] = grad_query.T.astype(BF16)
        k6[p] = grad_key.astype(BF16)
        v6[p] = grad_value.astype(BF16)

    def pack(p, first_row, second_row):
        def body(s):
            for xx in range(2):
                offset = (2 * s + xx) * 96
                rows = [pl.ds(pl.multiple_of(first_row + offset, 96), 96),
                        pl.ds(pl.multiple_of(second_row + offset, 96), 96)]
                first, second = ua.at[p, 0, :, xx, s], ua.at[p, 1, :, xx, s]
                for yy in range(2):
                    lo, mid, hi = 384 * yy, 384 * yy + 128, 384 * yy + 256
                    for m in range(2):
                        first[yy, 96 * m : 96 * m + 96, :] = gp[rows[m], lo : lo + 128]
                        second[yy, 96 * m : 96 * m + 96, :] = gp[rows[m], hi : hi + 128]
                    even = gp[rows[0], mid : mid + 128].astype(F32)
                    odd = pltpu.roll(gp[rows[1], mid : mid + 128].astype(F32), 64, 1)
                    first[yy, 192:288, :] = jnp.where(lanes < 64, even, odd).astype(BF16)
                    second[yy, 192:288, :] = jnp.where(lanes < 64, odd, even).astype(BF16)

        loop(zs, body)

    parts("ab", 6, attend_back)
    run("gav")
    for n in units[VO[0] : VO[1] + 1]:
        ag_drain(n)
    gp[0:768, :] = dot_nn(tc[...], n1[...]).astype(BF16)
    pack(1, 0, 768)
    for n in grads[AVO[0] : AVO[1] + 1]:
        rs_start(n)
    run("gaqk")
    for n in units[QK[0] : QK[1] + 1]:
        ag_drain(n)
    gp[0:768, :] = dot_nn(ta[...], n1[...]).astype(BF16)
    gp[768:1536, :] = dot_nn(tb[...], n1[...]).astype(BF16)
    pack(0, 0, 768)
    for n in grads[AQK[0] : AQK[1] + 1]:
        rs_start(n)

    def reduce(owner):
        value = dot_nt(act[block_rows(owner, 0), :], reduce_block(0))
        return value + dot_nt(act[block_rows(owner, 1), :], reduce_block(1))

    def layer_output():
        run("redb")
        n2[...] = reduce(1).astype(BF16)
        ahead_swap.start()
        run("reda")
        h1[...] = h1[...] + vec[7:8, :] + reduce(0)
        run("outst")
        for moved in cot_out:
            moved.wait_send()
        for s in range(4):
            rows = slice(128 * s, 128 * s + 128)
            stage[s] = (h1[rows, :] + ahead_in[rows, :].astype(F32)).astype(BF16)
        own_out.start()

    layer_output()
    run("dn1")
    h1[...] = dot_nn(lane_tiles(q6), at[0])
    h1[...] += dot_nn(lane_tiles(k6), at[1])
    h1[...] += dot_nn(lane_tiles(v6), at[2])
    gvec[2:3, :] = jnp.sum(lane_tiles(q6).astype(F32), axis=0, keepdims=True)
    gvec[3:4, :] = jnp.sum(lane_tiles(v6).astype(F32), axis=0, keepdims=True)

    run("inb")

    def input_back(s):
        rows = rows_of(s)
        grad, gain_sum, bias_sum = norm_gradient(x_in[s].astype(F32), vec[0:1, :], h1[rows, :])
        n1[rows, :] = (grad + acc[rows, :]).astype(BF16)
        gvec[0:1, :] += gain_sum
        gvec[1:2, :] += bias_sum

    loop(4, input_back)
    gvec_steps[0]()
    own_grad.start()
    run("end")
    finish_vectors()
    w1_back.wait()
    each_core(join_expand)
    w2_back.wait()
    each_core(join_reduce)

    own_out.wait()
    own_grad.wait()
    for moved in tokens_out + result_out + grad_out:
        moved.wait_send()
    for n in units[VO[1] + 1 :]:
        ag_drain(n)
    for n in grads:
        rs_drain(n)


def layer(sub, tokens, cotangent, span_mask, vectors, attention, expand, reduce_t):
    zs = GROUPS // 2
    seqs, block, width = tokens.shape
    rows = seqs * block
    columns = attention.shape[2]
    piece = (3 * columns, 128)
    vmem = lambda shape, dtype: pltpu.VMEM(shape, dtype)
    half = (2, 2, 2, zs) + piece
    scratch = [vmem((2,) + half, BF16)] + [vmem(half, BF16)] * 4
    scratch += [vmem((2, 2, 2, zs) + piece, BF16), vmem((6, 2, 2, zs) + piece, BF16)]
    scratch += [vmem(tokens.shape, BF16)] * 3
    scratch += [vmem((16, width), F32)] * 2
    scratch += [vmem((zs + 2, 16, width), F32)] * 2
    scratch += [vmem((16, columns), F32)]
    tiles = vmem((width // 128, rows, 128), BF16)
    flat = vmem((rows, width), BF16)
    turned = vmem((width, rows), BF16)
    scratch += [vmem((4, width, width), BF16), flat, tiles, tiles, tiles, tiles]
    scratch += [vmem((HEADS, rows, rows), BF16), vmem((rows, width), F32), vmem((rows, width), F32)]
    scratch += [flat, vmem((4 * rows, width), BF16), vmem((4 * rows, width), BF16)]
    scratch += [turned, turned, turned, tiles]
    scratch += [vmem(expand.shape, F32), vmem(reduce_t.shape, F32), flat, vmem(tokens.shape, BF16)]
    scratch += [tiles, flat, vmem((columns, width // 2), F32), vmem((2, width), F32), vmem((2, width), F32)]
    scratch += [vmem((6,) + piece, F32), vmem((width // 2, 2 * columns), F32)]
    scratch += [vmem((2 * columns, 2 * columns), F32), vmem(piece, F32)]
    scratch += [pltpu.SemaphoreType.DMA((5,))]
    gathered, summed = sum(map(len, GATHER_ROUTES)), sum(map(len, SUM_ROUTES))
    scratch += [pltpu.SemaphoreType.DMA((gathered, 4 * zs))] * 2
    scratch += [pltpu.SemaphoreType.DMA((gathered,))] * 2
    scratch += [pltpu.SemaphoreType.DMA((summed, zs + 2))] * 2
    scratch += [pltpu.SemaphoreType.DMA((4, 3))] * 2
    scratch += [pltpu.SemaphoreType.DMA((2, zs + 2))] * 2
    scratch += [pltpu.SemaphoreType.DMA((8,))] * 2
    in_vmem = pl.BlockSpec(memory_space=pltpu.VMEM)
    anywhere = pl.BlockSpec(memory_space=pl.ANY)
    return pl.pallas_call(
        functools.partial(kernel, sub, zs),
        out_shape=(
            jax.ShapeDtypeStruct(tokens.shape, BF16),
            jax.ShapeDtypeStruct(tokens.shape, BF16),
            jax.ShapeDtypeStruct(attention.shape, F32),
            jax.ShapeDtypeStruct(expand.shape, F32),
            jax.ShapeDtypeStruct(reduce_t.shape, F32),
            jax.ShapeDtypeStruct(vectors.shape, F32),
        ),
        in_specs=[anywhere] * 2 + [in_vmem] * 5,
        out_specs=(anywhere, anywhere) + (in_vmem,) * 4,
        scratch_shapes=scratch,
        compiler_params=pltpu.CompilerParams(
            collective_id=0, has_side_effects=True, vmem_limit_bytes=65400 * 1024
        ),
    )(tokens, cotangent, span_mask, vectors, attention, expand, reduce_t)


def update_kernel(rates, *refs):
    count = len(rates)
    ins, (result, grad) = refs[: 4 * count], refs[4 * count : 4 * count + 2]
    outs, (result_out, grad_out) = refs[4 * count + 2 : 7 * count + 2], refs[7 * count + 2 : 7 * count + 4]
    held, (low, wide, passed) = refs[7 * count + 4 : 11 * count + 4], refs[11 * count + 4 : 11 * count + 7]
    in_sems, out_sems = refs[11 * count + 7 :]
    loads = [pltpu.make_async_copy(ins[n], held[n], in_sems.at[n]) for n in range(4 * count)]
    stores = [pltpu.make_async_copy(held[4 * n + m], outs[3 * n + m], out_sems.at[3 * n + m])
              for n in range(count) for m in range(3)]
    load_grad = pltpu.make_async_copy(grad, low, in_sems.at[4 * count])
    store_grad = pltpu.make_async_copy(wide, grad_out, out_sems.at[3 * count])
    load_result = pltpu.make_async_copy(result, passed, in_sems.at[4 * count + 1])
    store_result = pltpu.make_async_copy(passed, result_out, out_sems.at[3 * count + 1])
    load_grad.start()
    load_result.start()
    for copy in loads:
        copy.start()
    load_result.wait()
    store_result.start()
    load_grad.wait()

    def widen(s, carry):
        wide[s] = low[s].astype(F32)
        return carry

    lax.fori_loop(0, low.shape[0], widen, 0)
    store_grad.start()
    for n in range(count):
        for m in range(4):
            loads[4 * n + m].wait()
        weight, one, two, gradient = held[4 * n : 4 * n + 4]
        values = adamw(weight[...], one[...], two[...], gradient[...], rates[n])
        for ref, value in zip((weight, one, two), values):
            ref[...] = value
        for m in range(3):
            stores[3 * n + m].start()
    for copy in stores + [store_grad, store_result]:
        copy.wait()


def update(rates, arrays, result, grad):
    flat = [value for group in arrays for value in group]
    new = [jax.ShapeDtypeStruct(value.shape, F32) for group in arrays for value in group[:3]]
    new += [jax.ShapeDtypeStruct(result.shape, BF16), jax.ShapeDtypeStruct(grad.shape, F32)]
    anywhere = pl.BlockSpec(memory_space=pl.ANY)
    scratch = [pltpu.VMEM(value.shape, F32) for value in flat]
    scratch += [pltpu.VMEM(grad.shape, BF16), pltpu.VMEM(grad.shape, F32), pltpu.VMEM(result.shape, BF16)]
    scratch += [pltpu.SemaphoreType.DMA((len(flat) + 2,)), pltpu.SemaphoreType.DMA((len(new),))]
    return pl.pallas_call(
        functools.partial(update_kernel, rates),
        out_shape=tuple(new),
        in_specs=[anywhere] * (len(flat) + 2),
        out_specs=(anywhere,) * len(new),
        scratch_shapes=scratch,
        compiler_params=pltpu.CompilerParams(vmem_limit_bytes=63 * 1024 * 1024),
    )(*flat, result, grad)


def local(
    sub,
    tokens,
    cotangent,
    span_mask,
    attention_weight,
    expand_weight,
    reduce_weight,
    vectors,
    attention_first,
    attention_second,
    expand_first,
    expand_second,
    reduce_first,
    reduce_second,
    vector_first,
    vector_second,
):
    together = [[n * sub + m for m in range(sub)] for n in range(GROUPS)]

    def widen(value, axis):
        if sub == 1:
            return value
        low = lax.all_gather(
            value.astype(BF16), "batch", axis=axis, tiled=True, axis_index_groups=together
        )
        return low.astype(F32)

    def narrow(value, axis):
        if sub == 1:
            return value
        return lax.psum_scatter(
            value, "batch", scatter_dimension=axis, tiled=True, axis_index_groups=together
        )

    out_tokens, input_grad, ga, g1, g2, gv = layer(
        sub,
        tokens,
        cotangent,
        span_mask,
        widen(vectors, 1),
        widen(attention_weight, 2),
        widen(expand_weight, 1),
        widen(reduce_weight.T, 0),
    )
    arrays = (
        (attention_weight, attention_first, attention_second, narrow(ga, 2)),
        (expand_weight, expand_first, expand_second, narrow(g1, 1)),
        (reduce_weight.T, reduce_first.T, reduce_second.T, narrow(g2, 0)),
        (vectors, vector_first, vector_second, narrow(gv, 1)),
    )
    rates = (rate_attention, rate_expand, rate_reduce, rate_vector)
    new = update(rates, arrays, out_tokens, input_grad)
    return new[-2:] + new[0:6] + tuple(value.T for value in new[6:9]) + new[9:12]


def solution(mesh):
    sub = mesh.shape["batch"] // GROUPS
    sequences = P("batch", "blk", None)
    attention = P(None, "blk", "batch")
    matrix = P("blk", "batch")
    return jax.shard_map(
        functools.partial(local, sub),
        mesh=mesh,
        in_specs=(sequences, sequences, P("batch", "blk"), attention, matrix, matrix, matrix)
        + (attention,) * 2
        + (matrix,) * 6,
        out_specs=(sequences,) * 2 + (attention,) * 3 + (matrix,) * 9,
        check_vma=False,
    )
```

```python
import functools
import math

import jax
import jax.numpy as jnp
from jax import lax
from jax.experimental import pallas as pl
from jax.experimental.pallas import tpu as pltpu
from jax.sharding import PartitionSpec as P

HEADS = 12
HEAD = 64
STEP = 10
GROUPS = 8

norm_epsilon = 1e-05
beta_one = 0.9
beta_two = 0.999
adam_epsilon = 1e-08
decay_weight = 0.1
rate_attention = 0.05
rate_expand = 0.03
rate_reduce = 0.015
rate_vector = 0.4

F32 = jnp.float32
BF16 = jnp.bfloat16
MESH = pl.DeviceIdType.MESH
GELU_SCALE = math.sqrt(2.0 / math.pi)
GELU_CUBE = 0.044715


def adamw(weight, moment_one, moment_two, gradient, step_rate):
    moment_one = beta_one * moment_one + (1.0 - beta_one) * gradient
    moment_two = beta_two * moment_two + (1.0 - beta_two) * gradient * gradient
    corrected_one = moment_one / (1.0 - beta_one**STEP)
    corrected_two = moment_two / (1.0 - beta_two**STEP)
    updated = weight - step_rate * (
        corrected_one / (jnp.sqrt(corrected_two) + adam_epsilon) + decay_weight * weight
    )
    return (updated, moment_one, moment_two)


def dot_nn(left, right):
    return lax.dot_general(left, right, (((1,), (0,)), ((), ())), preferred_element_type=F32)


def dot_nt(left, right):
    return lax.dot_general(left, right, (((1,), (1,)), ((), ())), preferred_element_type=F32)


X, Y, Z = 1, 2, 4
(N_QKA, N_QKB, N_VOA, N_VOB, N_W10A, N_W10B, N_W11A, N_W11B, N_W20A, N_W20B, N_W21A, N_W21B) = range(12)
(N_AQKA, N_AQKB, N_AVO, N_G10, N_G11A, N_G11B, N_G20, N_G21) = range(8)
QK, VO = (N_QKA, N_QKB), (N_VOA, N_VOB)
AQK, AVO = (N_AQKA, N_AQKB), (N_AVO, N_AVO)
SEND, GOT, WHOLE, SUM, VEC, SMALL, DO = range(7)
(TOK, COT, OUT, IG, TOK_HERE, COT_HERE, OUT_HERE,
 IG_HERE, SWAP_HERE, N2S_HERE, COTS_HERE, BACKS_HERE, AHEADS_HERE) = range(13)
GATHER_ROUTES = (
    ((Z, Y, X), (Z, Y, X),),
    ((Z, Y, X), (Z, Y, X),),
    ((Y, Z, X), (X, Z, Y),),
    ((Z, X, Y), (Y, Z, X),),
    ((X, Z, Y), (Z, X, Y),),
    ((Y, Z, X), (Z, Y, X),),
)
SUM_ROUTES = (
    ((Y, X, Z), (X, Z, Y),),
    ((Y, X, Z),),
    ((Y, X, Z),),
    ((X, Z, Y), (X, Z, Y),),
    ((Y, X, Z),),
    ((Z, X, Y),),
)
PLAN = dict(
    own1=(
        (SEND, N_QKA, 0, Z), (SEND, N_QKB, 0, Z),
    ),
    ownff=(
        (DO, TOK), (SEND, N_VOA, 0, Z), (VEC, 0), (DO, SWAP_HERE),
    ),
    mask=(
        (SEND, N_W10B, 0, X), (SEND, N_W20A, 0, X),
    ),
    ln1=(
        (VEC, 1), (GOT, N_QKA, Z), (SEND, N_QKA, Z, X), (SEND, N_QKA, Z, Y), (SEND, N_VOB, 0, Z),
        (GOT, N_W10B, X), (GOT, N_W20A, X), (GOT, N_QKB, Z), (SEND, N_QKB, Z, X), (SEND, N_QKB, Z, Y),
        (SEND, N_W11A, 0, Z), (GOT, N_QKA, Z | X), (DO, TOK_HERE), (GOT, N_VOA, Z), (SEND, N_VOA, Z, X),
        (SEND, N_VOA, Z, Y), (SEND, N_W11B, 0, Z), (GOT, N_QKB, Z | X), (VEC, 2), (GOT, N_QKA, Z | Y),
        (SEND, N_QKA, Z | Y, X), (GOT, N_VOB, Z), (SEND, N_VOB, Z, Y), (SEND, N_W10A, 0, Z),
        (GOT, N_VOA, Z | X), (GOT, N_QKB, Z | Y), (SEND, N_QKB, Z | Y, X), (SEND, N_VOB, Z, X),
        (SEND, N_W11B, 0, Y), (GOT, N_W11A, Z), (SEND, N_W10A, 0, Y), (VEC, 3), (SEND, N_W10B, 0, Z),
    ),
    unp0=(
        (DO, COT), (GOT, N_QKA, Z | Y | X), (GOT, N_VOA, Z | Y), (SEND, N_VOA, Z | Y, X), (GOT, N_W11B, Z),
        (SEND, N_W10B, X, Z), (GOT, N_QKB, Z | Y | X), (GOT, N_VOB, Z | Y), (SEND, N_VOB, Z | Y, X),
        (GOT, N_W11B, Y), (GOT, N_W10A, Z), (SEND, N_W11B, Y, Z), (GOT, N_W10A, Y), (WHOLE, N_QKA),
        (WHOLE, N_QKB),
    ),
    projq=(
        (GOT, N_VOB, Z | X), (SEND, N_W11A, Z, X),
    ),
    projk=(
        (SEND, N_W11A, Z, Y),
    ),
    attend0=(
        (GOT, N_W10B, Z), (SEND, N_W10A, Y, Z),
    ),
    attend1=(
        (GOT, N_VOA, Z | Y | X), (SEND, N_W11B, Z, X),
    ),
    attend2=(
        (SEND, N_W10B, Z, Y), (GOT, N_W10B, X | Z),
    ),
    attend3=(
        (SEND, N_W21B, 0, Z),
    ),
    attend4=(
        (GOT, N_VOB, Z | Y | X), (SEND, N_W10A, Z, X), (DO, COT_HERE), (SEND, N_W10B, X | Z, Y),
    ),
    attend5=(
        (GOT, N_W11B, Y | Z), (SEND, N_W20B, 0, Z),
    ),
    unp1=(
        (WHOLE, N_VOA), (WHOLE, N_VOB), (GOT, N_W11A, Z | X), (SEND, N_W11B, Y | Z, X),
    ),
    projv=(
        (GOT, N_W11A, Z | Y), (SEND, N_W11A, Z | X, Y), (DO, COTS_HERE),
    ),
    mix0=(
        (GOT, N_W10A, Y | Z), (SEND, N_W21A, 0, Z),
    ),
    mix5=(
        (GOT, N_W11B, Z | X),
    ),
    ao=(
        (SEND, N_W10A, Y | Z, X),
    ),
    ln2=(
        (GOT, N_W10B, Z | Y), (SEND, N_W21A, 0, Y), (GOT, N_W21B, Z),
    ),
    expa0=(
        (SEND, N_W20A, 0, Z), (SEND, N_W21B, Z, Y), (GOT, N_W10A, Z | X), (GOT, N_W10B, X | Z | Y),
        (GOT, N_W20B, Z), (SEND, N_W20B, Z, X), (SEND, N_W20A, X, Z), (SEND, N_W20B, Z, Y), (DO, N2S_HERE),
        (GOT, N_W11B, Y | Z | X), (SEND, N_W21B, Z, X), (GOT, N_W11A, Z | X | Y), (GOT, N_W21A, Z),
        (GOT, N_W21A, Y), (SEND, N_W21A, Y, Z), (GOT, N_W10A, Y | Z | X), (SEND, N_W21A, Z, X),
    ),
    expa1=(
        (GOT, N_W20A, Z), (SEND, N_W20A, Z, Y), (GOT, N_W21B, Z | Y),
    ),
    expb0=(
        (GOT, N_W20B, Z | X), (SEND, N_W20B, Z | X, Y), (SEND, N_W21B, Z | Y, X), (GOT, N_W20A, X | Z),
        (GOT, N_W20B, Z | Y),
    ),
    expb1=(
        (SEND, N_W20A, X | Z, Y), (GOT, N_W21B, Z | X),
    ),
    trY=(
        (GOT, N_W21A, Y | Z), (SEND, N_W21A, Y | Z, X), (GOT, N_W20A, Z | Y),
    ),
    gw2_0=(
        (GOT, N_W21A, Z | X),
    ),
    gw2_1=(
        (GOT, N_W20B, Z | X | Y),
    ),
    innb0=(
        (GOT, N_W21B, Z | Y | X), (SUM, N_G20, 0), (SUM, N_G21, 0), (GOT, N_W20A, X | Z | Y),
        (GOT, N_W21A, Y | Z | X),
    ),
    gw1_0=(
        (DO, BACKS_HERE),
    ),
    hid=(
        (SUM, N_G10, 0), (SUM, N_G11A, 0), (SUM, N_G11B, 0), (SUM, N_G20, 1),
    ),
    ab0=(
        (SUM, N_G11A, 1),
    ),
    ab2=(
        (SUM, N_G21, 1),
    ),
    ab3=(
        (SUM, N_AVO, 0), (SUM, N_G10, 1), (SUM, N_G11B, 1),
    ),
    gaqk=(
        (SUM, N_G11A, 2),
    ),
    redb=(
        (SUM, N_G20, 2),
    ),
    outst=(
        (SUM, N_G11B, 2), (SUM, N_AQKB, 0), (SUM, N_AQKA, 0), (SUM, N_G10, 2), (DO, AHEADS_HERE),
        (SUM, N_AVO, 1),
    ),
    inb=(
        (SUM, N_G11A, 3), (DO, OUT), (SUM, N_G21, 2), (SUM, N_G20, 3),
    ),
    end=(
        (SUM, N_AQKA, 1), (SUM, N_AQKB, 1), (SUM, N_G10, 3), (DO, IG), (SUM, N_AVO, 2), (DO, OUT_HERE),
        (SMALL, 0), (SUM, N_AQKB, 2), (SUM, N_AQKA, 2), (SMALL, 1), (SMALL, 2), (SUM, N_AVO, 3),
        (DO, IG_HERE), (SUM, N_G21, 3), (SUM, N_AQKA, 3), (SUM, N_G11B, 3), (SMALL, 3), (SUM, N_AQKB, 3),
    ),
)


def lane_tiles(ref, count=6):
    return jnp.concatenate([ref[t] for t in range(count)], axis=1)


class Unit:
    def __init__(self, index, route, rows, u, other):
        self.index, self.route, self.rows, self.u, self.other = index, route, rows, u, other


class Gradient:
    def __init__(self, index, route, rows, u, other, core_in, got, total):
        self.index, self.route, self.rows, self.u, self.other = index, route, rows, u, other
        self.core_in, self.got, self.total = core_in, got, total


def kernel(sub, zs, *refs):
    (tok, cot, mask_in, vec_in, a_in, w1_in, w2_in,
     out, ig, ga, g1, g2, gv,
     ua, uw1, uw2, gw1, gw2, core_in, got,
     x_in, cot_in, stage, vec, gvec, vin, gin, narrow_rows,
     at, n1, q6, k6, v6, o6, pt, h1, acc, n2, act, gp, ta, tb, tc, d6,
     w1_other, w2_other, n2_other, cot_other, back_in, ahead_in,
     lines, b1, gb1, totals, turned1, got1, got2,
     local_sem, ag_send, ag_recv, core_send, core_recv, rs_send, rs_recv,
     a2a_send, a2a_recv, v_send, v_recv, pair_send, pair_recv) = refs

    i = lax.axis_index("blk")
    b = lax.axis_index("batch")
    c, y = lax.rem(i, 2), lax.div(i, 2)
    g, r = lax.div(b, sub), lax.rem(b, sub)
    x, z = lax.rem(g, 2), lax.div(g, 2)

    def device(c_=c, y_=y, x_=x, z_=z):
        return {"blk": 2 * y_ + c_, "batch": (2 * z_ + x_) * sub + r}

    def z_at(k):
        return lax.rem(z + k, zs)

    def block_at(k):
        return lax.rem(i + k, 4)

    def copy(src, dst, send, recv, to):
        return pltpu.make_async_remote_copy(
            src_ref=src, dst_ref=dst, send_sem=send, recv_sem=recv, device_id=to, device_id_type=MESH
        )

    def loop(count, body, hooks=()):
        def step(s, carry):
            body(s)
            for k, f in hooks:
                pl.when(s == k)(f)
            return carry

        lax.fori_loop(0, count, step, 0)

    partners = [device(z_=z_at(k)) for k in range(1, zs)]
    partners += [device(x_=1 - x), device(y_=1 - y), device(c_=1 - c), device(c_=1 - c, y_=1 - y)]
    barrier = pltpu.get_barrier_semaphore()
    for partner in partners:
        pl.semaphore_signal(barrier, inc=1, device_id=partner, device_id_type=MESH)
    pl.semaphore_wait(barrier, len(partners))

    ME = {"y": y, "x": x, "z": z}

    def before(n, axis, other):
        return n.route.index(axis) < n.route.index(other)

    def side(n, axes, all_z):
        where = (1 - y if "y" in axes else y, 1 - x if "x" in axes else x, slice(None) if all_z else z)
        return n.u.at[where + (n.rows,)]

    def neighbour(axis):
        return device(y_=1 - y) if axis == "y" else device(x_=1 - x)

    def ag_copy(n, ref, axes, k, to):
        slot = (("y" in axes) * 2 + ("x" in axes)) * zs + k
        return copy(ref, ref, ag_send.at[n.index, slot], ag_recv.at[n.index, slot], to)

    def core_copy(n, ref):
        return copy(ref, ref, core_send.at[n.index], core_recv.at[n.index], device(c_=1 - c))

    def ag_sends(n, axes, axis):
        axes = axes.replace("z", "")
        if axis == "z":
            ref = side(n, axes, False)
            return [ag_copy(n, ref, axes, k, device(z_=z_at(k))) for k in range(1, zs)]
        ref = side(n, axes, before(n, "z", axis))
        return [ag_copy(n, ref, axes + axis, 0, neighbour(axis))]

    def ag_send_part(n, axes, axis):
        for moved in ag_sends(n, axes, axis):
            moved.start()

    def ag_wait_part(n, axes):
        last = max(axes, key=n.route.index)
        axes = axes.replace("z", "")
        if last == "z":
            yy, xx = (1 - y if "y" in axes else y), (1 - x if "x" in axes else x)
            for k in range(1, zs):
                ag_copy(n, n.u.at[yy, xx, z_at(zs - k), n.rows], axes, k, device()).wait_recv()
        else:
            ag_copy(n, side(n, axes, before(n, "z", last)), axes, 0, device()).wait_recv()
        if n.other is not None and (last == "z" or before(n, "z", last)):
            core_copy(n, side(n, axes, True)).start()

    def ag_done(n):
        if n.other is not None:
            core_copy(n, n.other.at[:, :, :, n.rows]).wait_recv()

    def ag_drain(n):
        for axis in n.route:
            earlier = [other for other in "yx" if before(n, other, axis)]
            for some in range(2 ** len(earlier)):
                axes = "".join(other for bit, other in enumerate(earlier) if some >> bit & 1)
                for moved in ag_sends(n, axes, axis):
                    moved.wait_send()
        if n.other is not None:
            core_copy(n, n.u.at[:, :, :, n.rows]).wait_send()

    AXES = "yxz"

    def rs_groups(n, step):
        axis = n.route[step]
        if axis == "z":
            return [(k, 1 + k, device(z_=z_at(zs - k))) for k in range(1, zs)]
        return [(1, "yx".index(axis), neighbour(axis))]

    def rs_where(n, step, k):
        axis, out, land = n.route[step], [], []
        for other in AXES:
            if other == axis:
                out.append(z_at(zs - k) if axis == "z" else 1 - ME[axis])
                land.append(k)
            elif before(n, other, axis):
                out.append(ME[other])
                land.append(0)
            else:
                out.append(slice(None))
                land.append(slice(None))
        return tuple(out) + (n.rows,), tuple(land) + (n.rows,)

    def rs_copy(n, step, k, slot, to):
        out, land = rs_where(n, step, k)
        return copy(n.u.at[out], n.got.at[land], rs_send.at[n.index, slot], rs_recv.at[n.index, slot], to)

    def rs_core(n):
        return copy(n.other.at[:, :, :, n.rows], n.core_in.at[:, :, :, n.rows], rs_send.at[n.index, zs + 1],
                    rs_recv.at[n.index, zs + 1], device(c_=1 - c))

    def add_terms(n, place, step):
        value = n.u[tuple(place) + (n.rows,)].astype(F32)
        if n.other is not None:
            value = value + n.core_in[tuple(place) + (n.rows,)].astype(F32)
        for axis in n.route[:step]:
            for k in range(1, zs) if axis == "z" else (1,):
                where = [k if other == axis else (0 if before(n, other, axis) else at_place)
                         for other, at_place in zip(AXES, place)]
                value = value + n.got[tuple(where) + (n.rows,)].astype(F32)
        return value

    def rs_start(n):
        rs_core(n).start()

    def rs_step(n, step):
        if step == 0 and n.other is not None:
            rs_core(n).wait_recv()
        if step > 0:
            for group in rs_groups(n, step - 1):
                rs_copy(n, step - 1, *group).wait_recv()
        if step == 3:
            n.total[n.rows, :] = add_terms(n, (y, x, z), 3)
            return
        for k, slot, to in rs_groups(n, step):
            out, _ = rs_where(n, step, k)
            if step > 0 or n.other is not None:
                spans = [range(2) if isinstance(at_place, slice) else (at_place,) for at_place in out[:2]]

                def body(zz):
                    for yy in spans[0]:
                        for xx in spans[1]:
                            n.u[yy, xx, zz, n.rows] = add_terms(n, (yy, xx, zz), step).astype(BF16)

                if isinstance(out[2], slice):
                    loop(zs, body)
                else:
                    body(out[2])
            rs_copy(n, step, k, slot, to).start()

    def rs_drain(n):
        if n.other is not None:
            rs_core(n).wait_send()
        for step in range(3):
            for group in rs_groups(n, step):
                rs_copy(n, step, *group).wait_send()

    def small_sum(ref, slots, which):
        to = (device(y_=1 - y), device(c_=1 - c), device(x_=1 - x))
        to += tuple(device(z_=z_at(k)) for k in range(1, zs))

        def moved(slot):
            return copy(ref, slots.at[slot], v_send.at[which, slot], v_recv.at[which, slot], to[slot])

        def land(last):
            moved(last).wait()
            ref[...] = ref[...] + slots[last]

        def step(n):
            def run():
                if n > 0:
                    land(n - 1)
                moved(n).start()

            return run

        def line():
            land(2)
            for k in range(1, zs):
                moved(2 + k).start()

        def finish():
            for k in range(1, zs):
                moved(2 + k).wait()
            value = ref[...]
            for k in range(1, zs):
                value = value + slots[2 + k]
            ref[...] = value

        return [step(0), step(1), step(2), line, finish]

    def rows_of(s):
        return pl.ds(pl.multiple_of(s * 128, 128), 128)

    def exchange(src, dst, which):
        return [copy(src.at[block_at(k)], dst.at[i], a2a_send.at[which, k - 1],
                     a2a_recv.at[which, k - 1], {"blk": block_at(k), "batch": b})
                for k in range(1, 4)]

    def exchange_landed(dst, which):
        return [copy(dst.at[block_at(4 - k)], dst.at[block_at(4 - k)], a2a_send.at[which, k - 1],
                     a2a_recv.at[which, k - 1], {"blk": block_at(4 - k), "batch": b})
                for k in range(1, 4)]

    def axes_of(mask):
        return "".join(axis for axis, bit in (("y", Y), ("x", X), ("z", Z)) if mask & bit)

    def rows_in(part, count):
        return pl.ds(part * (288 // count), 288 // count)

    units = []
    for unit, routes in enumerate(GATHER_ROUTES):
        half = unit % 2
        ref = (ua, uw1, uw2)[unit // 2]
        pieces = (ref.at[half, c], ref.at[half, 1 - c]) if unit < 2 else (ref.at[half], None)
        for part, route in enumerate(routes):
            units.append(Unit(len(units), "".join(map(axes_of, route)), rows_in(part, len(routes)), *pieces))

    def pair(slot, src, dst):
        return copy(src, dst, pair_send.at[slot], pair_recv.at[slot], device(c_=1 - c))

    w1_swap, w2_swap = pair(0, w1_in, w1_other), pair(1, w2_in, w2_other)

    def each_core(f):
        for q in range(2):
            pl.when(c == q)(functools.partial(f, q))

    def rest_rows(matrix):
        return a_in[matrix, pl.ds(pl.multiple_of(128 * (1 - c), 64), 64), :]

    def own_attention(p):
        mine = ua.at[p, c, y, x, z]
        for m in range(2):
            main = a_in[2 * p + m, pl.ds(pl.multiple_of(64 * c, 64), 128), :]
            mine[96 * m : 96 * m + 96, :] = main.T.astype(BF16)
        rest = jnp.concatenate([rest_rows(2 * p + c), rest_rows(2 * p + 1 - c)], axis=0)
        mine[192:288, :] = rest.T.astype(BF16)

    def own_expand(q):
        both = (w1_in, w1_other) if q == 0 else (w1_other, w1_in)
        cols = slice(192 * q, 192 * q + 192)
        blocks = (
            both[0][0:128, cols],
            jnp.concatenate([both[0][128:192, cols], both[1][0:64, cols]], axis=0),
            both[1][64:192, cols],
        )
        for t, block in enumerate(blocks):
            value = block.T.astype(BF16)
            for h in range(2):
                uw1[h, y, x, z, 96 * t : 96 * t + 96, :] = value[96 * h : 96 * h + 96, :]

    def own_reduce(q):
        both = (w2_in, w2_other) if q == 0 else (w2_other, w2_in)
        for cc in range(2):
            for part_of in range(2):
                start = 384 * part_of + 192 * q
                lines[:, 192 * part_of : 192 * part_of + 192] = both[cc][:, start : start + 192]
            for t in range(3):
                uw2[cc, y, x, z, 96 * t : 96 * t + 96, :] = lines[:, 128 * t : 128 * t + 128].astype(BF16)

    def own_hidden_bias(q):
        for zz in range(zs):
            for xx in range(2):
                col = 384 * (zz % 2) + 192 * xx
                start = 384 * xx + 192 * q
                b1[zz // 2 : zz // 2 + 1, col : col + 192] = vec[8 + zz : 9 + zz, start : start + 192]

    def hidden_bias_gradient(q):
        for zz in range(zs):
            for xx in range(2):
                col = 384 * (zz % 2) + 192 * xx
                start = 384 * xx + 192 * q
                gvec[8 + zz : 9 + zz, start : start + 192] = gb1[zz // 2 : zz // 2 + 1, col : col + 192]

    columns = a_in.shape[2]
    placed = lax.broadcasted_iota(jnp.int32, (columns, 768), 1) == (
        lax.broadcasted_iota(jnp.int32, (columns, 768), 0) + columns * g
    )

    def own_vectors():
        vec[...] = jnp.zeros_like(vec)
        rows = dot_nn(vec_in[...].astype(BF16), jnp.where(placed, 1.0, 0.0).astype(BF16))
        for j in range(3):
            vec[pl.ds(3 * i + j, 1), :] = rows[j : j + 1, :]

    load_cot = pltpu.make_async_copy(cot, stage, local_sem.at[4])

    def masked_cotangent():
        load_cot.wait()
        eye = lax.broadcasted_iota(jnp.int32, (128, 128), 0) == lax.broadcasted_iota(jnp.int32, (128, 128), 1)
        for s in range(4):
            row = jnp.broadcast_to(mask_in[s : s + 1, :].astype(F32), (128, 128))
            column = jnp.sum(jnp.where(eye, row, 0.0), axis=1, keepdims=True)
            stage[s] = (stage[s].astype(F32) * column).astype(BF16)

    def finish_attention(p):
        value = totals.at[p]
        for m in range(2):
            ga[2 * p + m, pl.ds(pl.multiple_of(64 * c, 64), 128), :] = value[96 * m : 96 * m + 96, :].T
        rest = value[192:288, :].T
        rows = pl.ds(pl.multiple_of(128 * (1 - c), 64), 64)
        ga[2 * p + c, rows, :] = rest[0:64, :]
        ga[2 * p + 1 - c, rows, :] = rest[64:128, :]

    w1_back = pair(6, turned1.at[pl.ds(pl.multiple_of(192 * (1 - c), 64), 192)], got1)
    w2_back = pair(7, totals.at[5 - c], got2)

    def turn_expand():
        for h in range(2):
            for t in range(3):
                turned1[128 * t : 128 * t + 128, 96 * h : 96 * h + 96] = totals[2 + h, 96 * t : 96 * t + 96, :].T
        w1_back.start()

    def join_expand(q):
        g1[:, 192 * q : 192 * q + 192] = turned1[192 * q : 192 * q + 192, :]
        g1[:, 192 * (1 - q) : 192 * (1 - q) + 192] = got1[...]

    def join_reduce(q):
        for half, value in ((q, totals.at[4 + q]), (1 - q, got2)):
            for t in range(3):
                lines[:, 128 * t : 128 * t + 128] = value[96 * t : 96 * t + 96, :]
            for part_of in range(2):
                start = 384 * part_of + 192 * half
                g2[:, start : start + 192] = lines[:, 192 * part_of : 192 * part_of + 192]

    def finish_vectors():
        value, total = gvec[...], 0.0
        for _ in range(3):
            part = value.astype(BF16)
            total = total + dot_nt(part, jnp.where(placed, 1.0, 0.0).astype(BF16))
            value = value - part.astype(F32)
        narrow_rows[...] = total
        for j in range(3):
            gv[j : j + 1, :] = narrow_rows[pl.ds(3 * i + j, 1), :]

    grads, owners = [], []
    for unit, routes in enumerate(SUM_ROUTES):
        half = unit % 2
        ref = (ua, gw1, gw2)[unit // 2]
        pieces = (ref.at[half, c], ref.at[half, 1 - c], core_in.at[half]) if unit < 2 else (ref.at[half], None, None)
        for part, route in enumerate(routes):
            grads.append(Gradient(len(grads), "".join(map(axes_of, route)), rows_in(part, len(routes)), *pieces,
                                  got.at[unit], totals.at[unit]))
            owners.append(unit)

    def summed(unit):
        if unit < 2:
            finish_attention(unit)
        elif unit < 4 and {2, 3} <= set(whole):
            turn_expand()
        elif unit >= 4 and {4, 5} <= set(whole):
            w2_back.start()

    seen, whole = set(), []

    def event(kind, *rest):
        if kind == SEND:
            ag_send_part(units[rest[0]], axes_of(rest[1]), axes_of(rest[2]))
        elif kind == GOT:
            ag_wait_part(units[rest[0]], axes_of(rest[1]))
        elif kind == WHOLE:
            ag_done(units[rest[0]])
        elif kind == SUM:
            rs_step(grads[rest[0]], rest[1])
            if rest[1] == 3:
                seen.add(rest[0])
                unit = owners[rest[0]]
                if all(k in seen for k in range(len(grads)) if owners[k] == unit):
                    whole.append(unit)
                    summed(unit)
        elif kind == DO:
            actions[rest[0]]()
        else:
            (vec_steps if kind == VEC else gvec_steps)[rest[0] + 1]()

    def run(part):
        for todo in PLAN.get(part, ()):
            event(*todo)

    def parts(name, count, body):
        run(name + "0")
        hooks = [(k - 1, functools.partial(run, name + str(k))) for k in range(1, count) if name + str(k) in PLAN]
        loop(count, body, hooks)

    def started(copies):
        for moved in copies:
            moved.start()
        return copies

    def arrived(*copies):
        for moved in copies:
            moved.wait_recv()

    load_cot.start()
    own_tokens = pltpu.make_async_copy(tok.at[i], x_in.at[i], local_sem.at[0])
    own_tokens.start()
    own_cot = pltpu.make_async_copy(stage.at[i], cot_in.at[i], local_sem.at[1])
    tokens_out, cot_out = exchange(tok, x_in, 0), exchange(stage, cot_in, 1)
    result_out = exchange(stage, out, 2)
    grad_out = [copy(n1.at[rows_of(block_at(k))], ig.at[i], a2a_send.at[3, k - 1], a2a_recv.at[3, k - 1],
                     {"blk": block_at(k), "batch": b}) for k in range(1, 4)]
    own_out = pltpu.make_async_copy(stage.at[i], out.at[i], local_sem.at[2])
    own_grad = pltpu.make_async_copy(n1.at[rows_of(i)], ig.at[i], local_sem.at[3])
    n2_swap, cot_swap = pair(2, n2, n2_other), pair(3, cot_in, cot_other)
    back_swap, ahead_swap = pair(4, d6, back_in), pair(5, n2, ahead_in)
    vec_steps, gvec_steps = small_sum(vec, vin, 0), small_sum(gvec, gin, 1)

    def tokens_here():
        arrived(*exchange_landed(x_in, 0))
        own_tokens.wait()

    def cotangent_here():
        arrived(*exchange_landed(cot_in, 1))
        own_cot.wait()
        cot_swap.start()

    def swaps_here():
        w1_swap.wait()
        w2_swap.wait()

    actions = {
        TOK: lambda: started(tokens_out),
        COT: lambda: started(cot_out),
        OUT: lambda: started(result_out),
        IG: lambda: started(grad_out),
        TOK_HERE: tokens_here,
        COT_HERE: cotangent_here,
        OUT_HERE: lambda: arrived(*exchange_landed(out, 2)),
        IG_HERE: lambda: arrived(*exchange_landed(ig, 3)),
        SWAP_HERE: swaps_here,
        N2S_HERE: lambda: n2_swap.wait(),
        COTS_HERE: lambda: cot_swap.wait(),
        BACKS_HERE: lambda: back_swap.wait(),
        AHEADS_HERE: lambda: ahead_swap.wait(),
    }

    own_attention(0)
    w1_swap.start()
    w2_swap.start()
    own_vectors()
    vec_steps[0]()
    run("own1")
    own_attention(1)
    run("ownff")
    each_core(own_expand)
    each_core(own_reduce)
    run("mask")
    masked_cotangent()
    own_cot.start()
    run("ln1")
    each_core(own_hidden_bias)

    def normalise(value):
        centered = value - jnp.mean(value, axis=-1, keepdims=True)
        scale = lax.rsqrt(jnp.mean(centered * centered, axis=-1, keepdims=True) + norm_epsilon)
        return centered * scale, scale

    def first_norm(s):
        unit, _ = normalise(x_in[s].astype(F32))
        n1[rows_of(s), :] = (unit * vec[0:1, :] + vec[1:2, :]).astype(BF16)

    loop(4, first_norm)
    run("unp0")

    lanes = lax.broadcasted_iota(jnp.int32, (96, 128), 1)

    def unpack(p, s):
        for xx in range(2):
            rows = pl.ds(pl.multiple_of((2 * s + xx) * 96, 96), 96)
            for yy in range(2):
                first, second = ua.at[p, 0, yy, xx, s], ua.at[p, 1, yy, xx, s]
                lo, hi = 384 * yy, 384 * yy + 256
                for m in range(2):
                    at[2 * p + m, rows, lo : lo + 128] = first[96 * m : 96 * m + 96, :]
                    at[2 * p + m, rows, hi : hi + 128] = second[96 * m : 96 * m + 96, :]
                rest_first = first[192:288, :].astype(F32)
                rest_second = second[192:288, :].astype(F32)
                even = jnp.where(lanes < 64, rest_first, rest_second)
                odd = pltpu.roll(jnp.where(lanes < 64, rest_second, rest_first), 64, 1)
                at[2 * p, rows, lo + 128 : lo + 256] = even.astype(BF16)
                at[2 * p + 1, rows, lo + 128 : lo + 256] = odd.astype(BF16)

    def project(m, dst, bias):
        for n in range(3):
            value = dot_nt(n1[...], at[m, 256 * n : 256 * n + 256, :])
            if bias is not None:
                value = value + vec[bias : bias + 1, 256 * n : 256 * n + 256]
            value = value.astype(BF16)
            if m == 0:
                value = value * jnp.asarray(HEAD ** (-0.5), BF16)
            dst[2 * n] = value[:, 0:128]
            dst[2 * n + 1] = value[:, 128:256]

    loop(zs, functools.partial(unpack, 0))
    run("projq")
    project(0, q6, 2)
    run("projk")
    project(1, k6, None)

    half_lane = lax.broadcasted_iota(jnp.int32, (512, 128), 1) // HEAD

    def half_of(value, which):
        return jnp.where(half_lane == which, value, jnp.zeros_like(value))

    def turn(value):
        return value.astype(F32).T.astype(BF16)

    def attend(p):
        queries, keys = q6[p], k6[p]
        for which in range(2):
            scores = dot_nt(half_of(keys, which), queries)
            expo = jnp.exp(scores - jnp.max(scores, axis=0, keepdims=True))
            probs = (expo * (1.0 / jnp.sum(expo, axis=0, keepdims=True))).astype(BF16)
            pt[2 * p + which] = probs

    def mix(p):
        values_t = turn(v6[p])
        mixed = [dot_nn(values_t[64 * which : 64 * which + 64, :], pt[2 * p + which]) for which in range(2)]
        o6[p] = jnp.concatenate(mixed, axis=0).T.astype(BF16)

    parts("attend", 6, attend)
    run("unp1")
    loop(zs, functools.partial(unpack, 1))
    run("projv")
    project(2, v6, 3)
    parts("mix", 6, mix)

    run("ao")
    for n in range(3):
        cols = slice(256 * n, 256 * n + 256)
        value = dot_nt(lane_tiles(o6), at[3, cols, :]) + vec[4:5, cols]
        for s in range(4):
            h1[128 * s : 128 * s + 128, cols] = x_in[s, :, cols].astype(F32) + value[128 * s : 128 * s + 128]

    def second_norm(s):
        unit, _ = normalise(h1[rows_of(s), :])
        n2[rows_of(s), :] = (unit * vec[5:6, :] + vec[6:7, :]).astype(BF16)

    run("ln2")
    loop(4, second_norm)
    n2_swap.start()

    def expand_block(s):
        def piece(ref):
            return jnp.concatenate([ref[96 * t : 96 * t + 96, :] for t in range(3)], axis=1)

        return jnp.concatenate(
            [jnp.concatenate([piece(uw1.at[h, yy, xx, 2 * s + zz]) for yy in range(2)], axis=1)
             for zz in range(2) for xx in range(2) for h in range(2)],
            axis=0,
        )

    def reduce_block(s):
        def piece(ref):
            return jnp.concatenate([ref[96 * t : 96 * t + 96, :] for t in range(3)], axis=1)

        return jnp.concatenate(
            [jnp.concatenate([piece(uw2.at[cc, s, xx, zz]) for cc in range(2)], axis=1)
             for zz in range(zs) for xx in range(2)],
            axis=0,
        )

    def block_rows(owner, s):
        return pl.ds(pl.multiple_of((2 * owner + s) * 512, 512), 512)

    def expand(owner, normed, s):
        rows = block_rows(owner, s)
        inner = dot_nt(normed[...], expand_block(s)) + b1[pl.ds(s, 1), :]
        square = inner * inner
        tanh = jnp.tanh(GELU_SCALE * inner * (1.0 + GELU_CUBE * square))
        act[rows, :] = (0.5 * inner * (1.0 + tanh)).astype(BF16)
        slope = 0.5 * (1.0 + tanh) + 0.5 * inner * (1.0 - tanh * tanh) * (
            GELU_SCALE * (1.0 + 3.0 * GELU_CUBE * square)
        )
        gp[rows, :] = slope.astype(BF16)

    parts("expa", 2, functools.partial(expand, 0, n2))
    parts("expb", 2, functools.partial(expand, 1, n2_other))

    gvec[...] = jnp.zeros_like(gvec)

    def transpose_rows(dst, s, value):
        dst[:, 128 * s : 128 * s + 128] = turn(value)

    run("trY")
    total = jnp.zeros((1, 768), F32)
    for s in range(4):
        transpose_rows(ta, s, cot_in[s])
        total = total + jnp.sum(cot_in[s].astype(F32), axis=0, keepdims=True)
    gvec[7:8, :] = total
    for s in range(4):
        transpose_rows(tb, s, cot_other[s])

    def both_rows(ref, s):
        return jnp.concatenate([ref[block_rows(0, s), :], ref[block_rows(1, s), :]], axis=0)

    def reduce_back(s):
        grad = dot_nn(jnp.concatenate([ta[...], tb[...]], axis=1), both_rows(act, s)).astype(BF16)
        for zz in range(zs):
            for xx in range(2):
                row = 96 * (2 * zz + xx)
                for cc in range(2):
                    for t in range(3):
                        col = 384 * cc + 128 * t
                        gw2[cc, s, xx, zz, 96 * t : 96 * t + 96, :] = grad[row : row + 96, col : col + 128]

    parts("gw2_", 2, reduce_back)

    def rows_together(ref):
        return jnp.concatenate([ref[s] for s in range(4)], axis=0)

    def inner_back(owner, cotangent_rows, s):
        rows = block_rows(owner, s)
        grad = dot_nn(rows_together(cotangent_rows), reduce_block(s)) * gp[rows, :].astype(F32)
        low = grad.astype(BF16)
        gp[rows, :] = low
        sums = jnp.sum(low.astype(F32), axis=0, keepdims=True)
        gb1[pl.ds(s, 1), :] = sums if owner == 1 else gb1[pl.ds(s, 1), :] + sums

    def norm_back(owner):
        acc[...] = dot_nn(gp[block_rows(owner, 0), :], expand_block(0))
        acc[...] += dot_nn(gp[block_rows(owner, 1), :], expand_block(1))

    parts("innb", 2, functools.partial(inner_back, 1, cot_other))
    run("dn2b")
    norm_back(1)
    for t in range(6):
        d6[t] = acc[:, 128 * t : 128 * t + 128].astype(BF16)
    back_swap.start()
    parts("inna", 2, functools.partial(inner_back, 0, cot_in))
    each_core(hidden_bias_gradient)
    run("dn2a")
    norm_back(0)

    def expand_back(s):
        turned = jnp.concatenate([turn(gp[block_rows(owner, s), :]) for owner in range(2)], axis=1)
        normed = jnp.concatenate([n2[...], n2_other[...]], axis=0)
        grad = dot_nn(turned, normed).astype(BF16)
        for zz in range(2):
            for xx in range(2):
                for h in range(2):
                    row = 384 * zz + 192 * xx + 96 * h
                    for yy in range(2):
                        for t in range(3):
                            col = 384 * yy + 128 * t
                            gw1[h, yy, xx, 2 * s + zz, 96 * t : 96 * t + 96, :] = grad[
                                row : row + 96, col : col + 128
                            ]

    parts("gw1_", 2, expand_back)
    run("hid")

    def norm_gradient(value, scale_row, grad):
        unit, scale = normalise(value)
        gain_sum = jnp.sum(grad * unit, axis=0, keepdims=True)
        bias_sum = jnp.sum(grad, axis=0, keepdims=True)
        inner = grad * scale_row
        mean = jnp.mean(inner, axis=-1, keepdims=True)
        along = jnp.mean(inner * unit, axis=-1, keepdims=True)
        return scale * (inner - mean - unit * along), gain_sum, bias_sum

    def hidden_back(s):
        rows = rows_of(s)
        grad_in = jnp.concatenate([back_in[t, rows, :] for t in range(6)], axis=1)
        grad_in = acc[rows, :] + grad_in.astype(F32)
        grad, gain_sum, bias_sum = norm_gradient(h1[rows, :], vec[5:6, :], grad_in)
        grad = grad + cot_in[s].astype(F32)
        acc[rows, :] = grad
        low = grad.astype(BF16)
        n2[rows, :] = low
        gvec[5:6, :] += gain_sum
        gvec[6:7, :] += bias_sum
        gvec[4:5, :] += jnp.sum(low.astype(F32), axis=0, keepdims=True)

    loop(4, hidden_back)

    run("dO")
    for n in range(3):
        value = dot_nn(n2[...], at[3, :, 256 * n : 256 * n + 256]).astype(BF16)
        d6[2 * n] = value[:, 0:128]
        d6[2 * n + 1] = value[:, 128:256]
    run("gao")
    for s in range(4):
        transpose_rows(tc, s, n2[128 * s : 128 * s + 128, :])
    gp[768:1536, :] = dot_nn(tc[...], lane_tiles(o6)).astype(BF16)

    def value_back(p):
        grads_in, grad_value = d6[p], 0.0
        for which in range(2):
            grad_value = grad_value + dot_nn(pt[2 * p + which], half_of(grads_in, which))
        tc[rows_of(p), :] = grad_value.T.astype(BF16)
        o6[p] = grad_value.astype(BF16)

    def attend_back(p):
        rows = rows_of(p)
        queries, keys, values, grads_in = q6[p], k6[p], v6[p], d6[p]
        keys_t = turn(keys)
        grad_query, grad_key = [], 0.0
        for which in range(2):
            wide = pt[2 * p + which].astype(F32)
            grad_probs = dot_nt(half_of(values, which), grads_in)
            inner = jnp.sum(wide * grad_probs, axis=0, keepdims=True)
            grad_scores = (wide * (grad_probs - inner)).astype(BF16)
            grad_query.append(dot_nn(keys_t[64 * which : 64 * which + 64, :], grad_scores))
            grad_key = grad_key + dot_nn(grad_scores, half_of(queries, which))
        grad_query = jnp.concatenate(grad_query, axis=0) * HEAD ** (-0.5)
        ta[rows, :] = grad_query.astype(BF16)
        tb[rows, :] = grad_key.T.astype(BF16)
        q6[p] = grad_query.T.astype(BF16)
        k6[p] = grad_key.astype(BF16)

    def pack(p, first_row, second_row):
        def body(s):
            for xx in range(2):
                offset = (2 * s + xx) * 96
                rows = [pl.ds(pl.multiple_of(first_row + offset, 96), 96),
                        pl.ds(pl.multiple_of(second_row + offset, 96), 96)]
                first, second = ua.at[p, 0, :, xx, s], ua.at[p, 1, :, xx, s]
                for yy in range(2):
                    lo, mid, hi = 384 * yy, 384 * yy + 128, 384 * yy + 256
                    for m in range(2):
                        first[yy, 96 * m : 96 * m + 96, :] = gp[rows[m], lo : lo + 128]
                        second[yy, 96 * m : 96 * m + 96, :] = gp[rows[m], hi : hi + 128]
                    even = gp[rows[0], mid : mid + 128].astype(F32)
                    odd = pltpu.roll(gp[rows[1], mid : mid + 128].astype(F32), 64, 1)
                    first[yy, 192:288, :] = jnp.where(lanes < 64, even, odd).astype(BF16)
                    second[yy, 192:288, :] = jnp.where(lanes < 64, odd, even).astype(BF16)

        loop(zs, body)

    parts("av", 6, value_back)
    run("gav")
    for n in units[VO[0] : VO[1] + 1]:
        ag_drain(n)
    gp[0:768, :] = dot_nn(tc[...], n1[...]).astype(BF16)
    pack(1, 0, 768)
    for n in grads[AVO[0] : AVO[1] + 1]:
        rs_start(n)
    parts("ab", 6, attend_back)
    run("gaqk")
    for n in units[QK[0] : QK[1] + 1]:
        ag_drain(n)
    gp[0:768, :] = dot_nn(ta[...], n1[...]).astype(BF16)
    gp[768:1536, :] = dot_nn(tb[...], n1[...]).astype(BF16)
    pack(0, 0, 768)
    for n in grads[AQK[0] : AQK[1] + 1]:
        rs_start(n)

    def reduce(owner):
        value = dot_nt(act[block_rows(owner, 0), :], reduce_block(0))
        return value + dot_nt(act[block_rows(owner, 1), :], reduce_block(1))

    def layer_output():
        run("redb")
        n2[...] = reduce(1).astype(BF16)
        ahead_swap.start()
        run("reda")
        h1[...] = h1[...] + vec[7:8, :] + reduce(0)
        run("outst")
        for moved in cot_out:
            moved.wait_send()
        for s in range(4):
            rows = slice(128 * s, 128 * s + 128)
            stage[s] = (h1[rows, :] + ahead_in[rows, :].astype(F32)).astype(BF16)
        own_out.start()

    layer_output()
    run("dn1")
    h1[...] = dot_nn(lane_tiles(q6), at[0])
    h1[...] += dot_nn(lane_tiles(k6), at[1])
    h1[...] += dot_nn(lane_tiles(o6), at[2])
    gvec[2:3, :] = jnp.sum(lane_tiles(q6).astype(F32), axis=0, keepdims=True)
    gvec[3:4, :] = jnp.sum(lane_tiles(o6).astype(F32), axis=0, keepdims=True)

    run("inb")

    def input_back(s):
        rows = rows_of(s)
        grad, gain_sum, bias_sum = norm_gradient(x_in[s].astype(F32), vec[0:1, :], h1[rows, :])
        n1[rows, :] = (grad + acc[rows, :]).astype(BF16)
        gvec[0:1, :] += gain_sum
        gvec[1:2, :] += bias_sum

    loop(4, input_back)
    gvec_steps[0]()
    own_grad.start()
    run("end")
    finish_vectors()
    w1_back.wait()
    each_core(join_expand)
    w2_back.wait()
    each_core(join_reduce)

    own_out.wait()
    own_grad.wait()
    for moved in tokens_out + result_out + grad_out:
        moved.wait_send()
    for n in units[VO[1] + 1 :]:
        ag_drain(n)
    for n in grads:
        rs_drain(n)


def layer(sub, tokens, cotangent, span_mask, vectors, attention, expand, reduce_t):
    zs = GROUPS // 2
    seqs, block, width = tokens.shape
    rows = seqs * block
    columns = attention.shape[2]
    piece = (3 * columns, 128)
    vmem = lambda shape, dtype: pltpu.VMEM(shape, dtype)
    half = (2, 2, 2, zs) + piece
    scratch = [vmem((2,) + half, BF16)] + [vmem(half, BF16)] * 4
    scratch += [vmem((2, 2, 2, zs) + piece, BF16), vmem((6, 2, 2, zs) + piece, BF16)]
    scratch += [vmem(tokens.shape, BF16)] * 3
    scratch += [vmem((16, width), F32)] * 2
    scratch += [vmem((zs + 2, 16, width), F32)] * 2
    scratch += [vmem((16, columns), F32)]
    tiles = vmem((width // 128, rows, 128), BF16)
    flat = vmem((rows, width), BF16)
    turned = vmem((width, rows), BF16)
    scratch += [vmem((4, width, width), BF16), flat, tiles, tiles, tiles, tiles]
    scratch += [vmem((HEADS, rows, rows), BF16), vmem((rows, width), F32), vmem((rows, width), F32)]
    scratch += [flat, vmem((4 * rows, width), BF16), vmem((4 * rows, width), BF16)]
    scratch += [turned, turned, turned, tiles]
    scratch += [vmem(expand.shape, F32), vmem(reduce_t.shape, F32), flat, vmem(tokens.shape, BF16)]
    scratch += [tiles, flat, vmem((columns, width // 2), F32), vmem((2, width), F32), vmem((2, width), F32)]
    scratch += [vmem((6,) + piece, F32), vmem((width // 2, 2 * columns), F32)]
    scratch += [vmem((2 * columns, 2 * columns), F32), vmem(piece, F32)]
    scratch += [pltpu.SemaphoreType.DMA((5,))]
    gathered, summed = sum(map(len, GATHER_ROUTES)), sum(map(len, SUM_ROUTES))
    scratch += [pltpu.SemaphoreType.DMA((gathered, 4 * zs))] * 2
    scratch += [pltpu.SemaphoreType.DMA((gathered,))] * 2
    scratch += [pltpu.SemaphoreType.DMA((summed, zs + 2))] * 2
    scratch += [pltpu.SemaphoreType.DMA((4, 3))] * 2
    scratch += [pltpu.SemaphoreType.DMA((2, zs + 2))] * 2
    scratch += [pltpu.SemaphoreType.DMA((8,))] * 2
    in_vmem = pl.BlockSpec(memory_space=pltpu.VMEM)
    anywhere = pl.BlockSpec(memory_space=pl.ANY)
    return pl.pallas_call(
        functools.partial(kernel, sub, zs),
        out_shape=(
            jax.ShapeDtypeStruct(tokens.shape, BF16),
            jax.ShapeDtypeStruct(tokens.shape, BF16),
            jax.ShapeDtypeStruct(attention.shape, F32),
            jax.ShapeDtypeStruct(expand.shape, F32),
            jax.ShapeDtypeStruct(reduce_t.shape, F32),
            jax.ShapeDtypeStruct(vectors.shape, F32),
        ),
        in_specs=[anywhere] * 2 + [in_vmem] * 5,
        out_specs=(anywhere, anywhere) + (in_vmem,) * 4,
        scratch_shapes=scratch,
        compiler_params=pltpu.CompilerParams(
            collective_id=0, has_side_effects=True, vmem_limit_bytes=65400 * 1024
        ),
    )(tokens, cotangent, span_mask, vectors, attention, expand, reduce_t)


def update_kernel(rates, *refs):
    count = len(rates)
    ins, (result, grad) = refs[: 4 * count], refs[4 * count : 4 * count + 2]
    outs, (result_out, grad_out) = refs[4 * count + 2 : 7 * count + 2], refs[7 * count + 2 : 7 * count + 4]
    held, (low, wide, passed) = refs[7 * count + 4 : 11 * count + 4], refs[11 * count + 4 : 11 * count + 7]
    in_sems, out_sems = refs[11 * count + 7 :]
    loads = [pltpu.make_async_copy(ins[n], held[n], in_sems.at[n]) for n in range(4 * count)]
    stores = [pltpu.make_async_copy(held[4 * n + m], outs[3 * n + m], out_sems.at[3 * n + m])
              for n in range(count) for m in range(3)]
    load_grad = pltpu.make_async_copy(grad, low, in_sems.at[4 * count])
    store_grad = pltpu.make_async_copy(wide, grad_out, out_sems.at[3 * count])
    load_result = pltpu.make_async_copy(result, passed, in_sems.at[4 * count + 1])
    store_result = pltpu.make_async_copy(passed, result_out, out_sems.at[3 * count + 1])
    load_grad.start()
    load_result.start()
    for copy in loads:
        copy.start()
    load_result.wait()
    store_result.start()
    load_grad.wait()

    def widen(s, carry):
        wide[s] = low[s].astype(F32)
        return carry

    lax.fori_loop(0, low.shape[0], widen, 0)
    store_grad.start()
    for n in range(count):
        for m in range(4):
            loads[4 * n + m].wait()
        weight, one, two, gradient = held[4 * n : 4 * n + 4]
        values = adamw(weight[...], one[...], two[...], gradient[...], rates[n])
        for ref, value in zip((weight, one, two), values):
            ref[...] = value
        for m in range(3):
            stores[3 * n + m].start()
    for copy in stores + [store_grad, store_result]:
        copy.wait()


def update(rates, arrays, result, grad):
    flat = [value for group in arrays for value in group]
    new = [jax.ShapeDtypeStruct(value.shape, F32) for group in arrays for value in group[:3]]
    new += [jax.ShapeDtypeStruct(result.shape, BF16), jax.ShapeDtypeStruct(grad.shape, F32)]
    anywhere = pl.BlockSpec(memory_space=pl.ANY)
    scratch = [pltpu.VMEM(value.shape, F32) for value in flat]
    scratch += [pltpu.VMEM(grad.shape, BF16), pltpu.VMEM(grad.shape, F32), pltpu.VMEM(result.shape, BF16)]
    scratch += [pltpu.SemaphoreType.DMA((len(flat) + 2,)), pltpu.SemaphoreType.DMA((len(new),))]
    return pl.pallas_call(
        functools.partial(update_kernel, rates),
        out_shape=tuple(new),
        in_specs=[anywhere] * (len(flat) + 2),
        out_specs=(anywhere,) * len(new),
        scratch_shapes=scratch,
        compiler_params=pltpu.CompilerParams(vmem_limit_bytes=63 * 1024 * 1024),
    )(*flat, result, grad)


def local(
    sub,
    tokens,
    cotangent,
    span_mask,
    attention_weight,
    expand_weight,
    reduce_weight,
    vectors,
    attention_first,
    attention_second,
    expand_first,
    expand_second,
    reduce_first,
    reduce_second,
    vector_first,
    vector_second,
):
    together = [[n * sub + m for m in range(sub)] for n in range(GROUPS)]

    def widen(value, axis):
        if sub == 1:
            return value
        low = lax.all_gather(
            value.astype(BF16), "batch", axis=axis, tiled=True, axis_index_groups=together
        )
        return low.astype(F32)

    def narrow(value, axis):
        if sub == 1:
            return value
        return lax.psum_scatter(
            value, "batch", scatter_dimension=axis, tiled=True, axis_index_groups=together
        )

    out_tokens, input_grad, ga, g1, g2, gv = layer(
        sub,
        tokens,
        cotangent,
        span_mask,
        widen(vectors, 1),
        widen(attention_weight, 2),
        widen(expand_weight, 1),
        widen(reduce_weight.T, 0),
    )
    arrays = (
        (attention_weight, attention_first, attention_second, narrow(ga, 2)),
        (expand_weight, expand_first, expand_second, narrow(g1, 1)),
        (reduce_weight.T, reduce_first.T, reduce_second.T, narrow(g2, 0)),
        (vectors, vector_first, vector_second, narrow(gv, 1)),
    )
    rates = (rate_attention, rate_expand, rate_reduce, rate_vector)
    new = update(rates, arrays, out_tokens, input_grad)
    return new[-2:] + new[0:6] + tuple(value.T for value in new[6:9]) + new[9:12]


def solution(mesh):
    sub = mesh.shape["batch"] // GROUPS
    sequences = P("batch", "blk", None)
    attention = P(None, "blk", "batch")
    matrix = P("blk", "batch")
    return jax.shard_map(
        functools.partial(local, sub),
        mesh=mesh,
        in_specs=(sequences, sequences, P("batch", "blk"), attention, matrix, matrix, matrix)
        + (attention,) * 2
        + (matrix,) * 6,
        out_specs=(sequences,) * 2 + (attention,) * 3 + (matrix,) * 9,
        check_vma=False,
    )
```

```python
import functools
import math

import jax
import jax.numpy as jnp
from jax import lax
from jax.experimental import pallas as pl
from jax.experimental.pallas import tpu as pltpu
from jax.sharding import PartitionSpec as P

HEADS = 12
HEAD = 64
STEP = 10
GROUPS = 8

norm_epsilon = 1e-05
beta_one = 0.9
beta_two = 0.999
adam_epsilon = 1e-08
decay_weight = 0.1
rate_attention = 0.05
rate_expand = 0.03
rate_reduce = 0.015
rate_vector = 0.4

F32 = jnp.float32
BF16 = jnp.bfloat16
MESH = pl.DeviceIdType.MESH
GELU_SCALE = math.sqrt(2.0 / math.pi)
GELU_CUBE = 0.044715


def adamw(weight, moment_one, moment_two, gradient, step_rate):
    moment_one = beta_one * moment_one + (1.0 - beta_one) * gradient
    moment_two = beta_two * moment_two + (1.0 - beta_two) * gradient * gradient
    corrected_one = moment_one / (1.0 - beta_one**STEP)
    corrected_two = moment_two / (1.0 - beta_two**STEP)
    updated = weight - step_rate * (
        corrected_one / (jnp.sqrt(corrected_two) + adam_epsilon) + decay_weight * weight
    )
    return (updated, moment_one, moment_two)


def dot_nn(left, right):
    return lax.dot_general(left, right, (((1,), (0,)), ((), ())), preferred_element_type=F32)


def dot_nt(left, right):
    return lax.dot_general(left, right, (((1,), (1,)), ((), ())), preferred_element_type=F32)


X, Y, Z = 1, 2, 4
(N_QKA, N_QKB, N_VOA, N_VOB, N_W10A, N_W10B, N_W11A, N_W11B, N_W20A, N_W20B, N_W21) = range(11)
(N_AQKA, N_AQKB, N_AVO, N_G10A, N_G10B, N_G11, N_G20A, N_G20B, N_G21) = range(9)
QK, VO = (N_QKA, N_QKB), (N_VOA, N_VOB)
AQK, AVO = (N_AQKA, N_AQKB), (N_AVO, N_AVO)
SEND, GOT, WHOLE, SUM, VEC, SMALL, DO = range(7)
(TOK, COT, OUT, IG, TOK_HERE, COT_HERE, OUT_HERE,
 IG_HERE, SWAP_HERE, N2S_HERE, COTS_HERE, BACKS_HERE, AHEADS_HERE) = range(13)
GATHER_ROUTES = (
    ((Z, Y, X), (Z, Y, X),),
    ((Z, X, Y), (Y, Z, X),),
    ((Y, X, Z), (Z, X, Y),),
    ((Z, Y, X), (Z, Y, X),),
    ((Y, X, Z), (Z, Y, X),),
    ((Z, X, Y),),
)
SUM_ROUTES = (
    ((X, Z, Y), (X, Z, Y),),
    ((Y, X, Z),),
    ((Z, X, Y), (X, Y, Z),),
    ((Y, X, Z),),
    ((X, Z, Y), (X, Z, Y),),
    ((Y, X, Z),),
)
PLAN = dict(
    own1=(
        (SEND, N_QKA, 0, Z), (SEND, N_QKB, 0, Z),
    ),
    ownff=(
        (DO, TOK), (SEND, N_VOA, 0, Z), (VEC, 0), (DO, SWAP_HERE),
    ),
    mask=(
        (SEND, N_W10A, 0, X), (SEND, N_W20A, 0, X),
    ),
    ln1=(
        (VEC, 1), (GOT, N_QKA, Z), (SEND, N_QKA, Z, X), (SEND, N_QKA, Z, Y), (SEND, N_VOB, 0, Z),
        (GOT, N_W10A, X), (GOT, N_W20A, X), (GOT, N_QKB, Z), (SEND, N_QKB, Z, X), (SEND, N_QKB, Z, Y),
        (SEND, N_W11A, 0, Z), (GOT, N_QKA, Z | X), (DO, TOK_HERE), (SEND, N_VOB, 0, Y), (GOT, N_VOA, Z),
        (SEND, N_VOA, Z, X), (SEND, N_VOA, Z, Y), (SEND, N_W11B, 0, Z), (GOT, N_QKB, Z | X),
        (GOT, N_QKA, Z | Y), (SEND, N_QKA, Z | Y, X), (VEC, 2), (GOT, N_VOB, Z), (GOT, N_QKB, Z | Y),
        (SEND, N_QKB, Z | Y, X), (GOT, N_VOA, Z | X), (SEND, N_VOA, Z | X, Y), (GOT, N_W11A, Z),
        (SEND, N_VOB, Z, X), (GOT, N_VOB, Y), (SEND, N_VOB, Y, Z), (SEND, N_W10A, 0, Y), (VEC, 3),
    ),
    unp0=(
        (SEND, N_W10B, 0, Z), (SEND, N_W11A, Z, Y), (GOT, N_QKA, Z | Y | X), (SEND, N_W11A, Z, X),
        (GOT, N_VOA, Z | Y), (GOT, N_W11B, Z), (SEND, N_W21, 0, Z), (SEND, N_W11B, Z, Y),
        (GOT, N_QKB, Z | Y | X), (GOT, N_VOA, Z | X | Y), (GOT, N_VOB, Y | Z), (SEND, N_VOB, Y | Z, X),
        (GOT, N_W10A, Y), (DO, COT), (WHOLE, N_QKA), (WHOLE, N_QKB),
    ),
    projq=(
        (GOT, N_VOB, Z | X),
    ),
    projk=(
        (GOT, N_W10B, Z), (SEND, N_W10B, Z, X), (GOT, N_W11A, Z | Y),
    ),
    attend0=(
        (SEND, N_W10A, 0, Z),
    ),
    attend1=(
        (GOT, N_W11A, Z | X), (SEND, N_W10A, Y, X), (SEND, N_W11B, Z, X), (GOT, N_W11B, Z | Y),
        (SEND, N_W10A, X, Z),
    ),
    attend2=(
        (GOT, N_VOB, Y | Z | X), (SEND, N_W10B, Z, Y), (SEND, N_W11A, Z | Y, X), (GOT, N_W21, Z),
    ),
    unp1=(
        (SEND, N_W10A, Y, Z), (WHOLE, N_VOA), (WHOLE, N_VOB), (GOT, N_W10B, Z | X), (SEND, N_W10B, Z | X, Y),
        (GOT, N_W10A, Y | X),
    ),
    projv=(
        (SEND, N_W11B, Z | Y, X), (GOT, N_W10A, Z), (SEND, N_W10A, Y | X, Z),
    ),
    mix1=(
        (DO, COT_HERE),
    ),
    mix2=(
        (SEND, N_W20A, 0, Y), (GOT, N_W11B, Z | X),
    ),
    ao=(
        (SEND, N_W21, Z, X), (GOT, N_W10A, X | Z), (SEND, N_W21, Z, Y),
    ),
    ln2=(
        (SEND, N_W20B, 0, Z),
    ),
    expa0=(
        (GOT, N_W10B, Z | Y), (DO, COTS_HERE), (GOT, N_W11A, Z | Y | X), (GOT, N_W10A, Y | Z),
        (SEND, N_W20A, 0, Z), (GOT, N_W10B, Z | X | Y), (GOT, N_W11B, Z | Y | X), (DO, N2S_HERE),
        (GOT, N_W20A, Y), (SEND, N_W20A, Y, X), (GOT, N_W10A, Y | X | Z),
    ),
    expa1=(
        (SEND, N_W20A, X, Z),
    ),
    expb0=(
        (GOT, N_W20B, Z), (SEND, N_W20B, Z, X), (SEND, N_W20B, Z, Y), (SEND, N_W20A, Y, Z),
    ),
    expb1=(
        (GOT, N_W21, Z | X), (SEND, N_W21, Z | X, Y), (GOT, N_W21, Z | Y), (GOT, N_W20A, Z),
        (GOT, N_W20A, Y | X), (SEND, N_W20A, Y | X, Z),
    ),
    gw2_0=(
        (GOT, N_W20B, Z | Y), (SEND, N_W20B, Z | Y, X), (GOT, N_W20A, X | Z), (GOT, N_W20B, Z | X),
    ),
    innb0=(
        (GOT, N_W20A, Y | Z), (SUM, N_G20A, 0), (SUM, N_G20B, 0), (SUM, N_G21, 0), (GOT, N_W20B, Z | Y | X),
        (GOT, N_W21, Z | X | Y), (GOT, N_W20A, Y | X | Z),
    ),
    gw1_0=(
        (SUM, N_G20A, 1), (DO, BACKS_HERE),
    ),
    hid=(
        (SUM, N_G10A, 0), (SUM, N_G10B, 0), (SUM, N_G11, 0),
    ),
    dO=(
        (SUM, N_G20B, 1), (SUM, N_G21, 1), (SUM, N_G20A, 2),
    ),
    gav=(
        (SUM, N_G10B, 1),
    ),
    ab2=(
        (SUM, N_AVO, 0), (SUM, N_G21, 2), (SUM, N_G11, 1), (SUM, N_G10A, 1),
    ),
    gaqk=(
        (SUM, N_G10B, 2),
    ),
    redb=(
        (SUM, N_G20B, 2),
    ),
    reda=(
        (SUM, N_G11, 2),
    ),
    outst=(
        (SUM, N_G10A, 2), (SUM, N_AQKA, 0), (SUM, N_AQKB, 0), (DO, AHEADS_HERE), (SUM, N_G21, 3),
    ),
    dn1=(
        (DO, OUT),
    ),
    inb=(
        (SUM, N_AVO, 1),
    ),
    end=(
        (SUM, N_G20A, 3), (DO, IG), (SUM, N_AQKA, 1), (SUM, N_G11, 3), (SUM, N_G10B, 3), (DO, OUT_HERE),
        (SUM, N_AQKB, 1), (SUM, N_AQKA, 2), (SUM, N_AVO, 2), (DO, IG_HERE), (SMALL, 0), (SUM, N_G20B, 3),
        (SUM, N_AQKB, 2), (SUM, N_G10A, 3), (SMALL, 1), (SUM, N_AQKA, 3), (SUM, N_AQKB, 3), (SMALL, 2),
        (SUM, N_AVO, 3), (SMALL, 3),
    ),
)


def lane_tiles(ref, count=6):
    return jnp.concatenate([ref[t] for t in range(count)], axis=1)


class Unit:
    def __init__(self, index, route, rows, u, other):
        self.index, self.route, self.rows, self.u, self.other = index, route, rows, u, other


class Gradient:
    def __init__(self, index, route, rows, u, other, core_in, got, total):
        self.index, self.route, self.rows, self.u, self.other = index, route, rows, u, other
        self.core_in, self.got, self.total = core_in, got, total


def kernel(sub, zs, *refs):
    (tok, cot, mask_hbm, vec_hbm, a_hbm, w1_hbm, w2_hbm,
     out, ig, ga, g1, g2, gv,
     mask_in, vec_in, a_in, w1_in, w2_in, ua, uw1, uw2, gw1, gw2, core_in, got,
     x_in, cot_in, stage, vec, gvec, vin, gin, narrow_rows,
     at, n1, q6, k6, v6, o6, pt, h1, acc, n2, act, gp, ta, tb, tc, d6,
     w1_other, w2_other, n2_other, cot_other, back_in, ahead_in,
     lines, b1, gb1, totals, turned1, got1, got2,
     local_sem, ag_send, ag_recv, core_send, core_recv, rs_send, rs_recv,
     a2a_send, a2a_recv, v_send, v_recv, pair_send, pair_recv) = refs

    i = lax.axis_index("blk")
    b = lax.axis_index("batch")
    c, y = lax.rem(i, 2), lax.div(i, 2)
    g, r = lax.div(b, sub), lax.rem(b, sub)
    x, z = lax.rem(g, 2), lax.div(g, 2)

    def device(c_=c, y_=y, x_=x, z_=z):
        return {"blk": 2 * y_ + c_, "batch": (2 * z_ + x_) * sub + r}

    def z_at(k):
        return lax.rem(z + k, zs)

    def block_at(k):
        return lax.rem(i + k, 4)

    def copy(src, dst, send, recv, to):
        return pltpu.make_async_remote_copy(
            src_ref=src, dst_ref=dst, send_sem=send, recv_sem=recv, device_id=to, device_id_type=MESH
        )

    def loop(count, body, hooks=()):
        def step(s, carry):
            body(s)
            for k, f in hooks:
                pl.when(s == k)(f)
            return carry

        lax.fori_loop(0, count, step, 0)

    partners = [device(z_=z_at(k)) for k in range(1, zs)]
    partners += [device(x_=1 - x), device(y_=1 - y), device(c_=1 - c), device(c_=1 - c, y_=1 - y)]
    barrier = pltpu.get_barrier_semaphore()
    for partner in partners:
        pl.semaphore_signal(barrier, inc=1, device_id=partner, device_id_type=MESH)

    ME = {"y": y, "x": x, "z": z}

    def before(n, axis, other):
        return n.route.index(axis) < n.route.index(other)

    def side(n, axes, all_z):
        where = (1 - y if "y" in axes else y, 1 - x if "x" in axes else x, slice(None) if all_z else z)
        return n.u.at[where + (n.rows,)]

    def neighbour(axis):
        return device(y_=1 - y) if axis == "y" else device(x_=1 - x)

    def ag_copy(n, ref, axes, k, to):
        slot = (("y" in axes) * 2 + ("x" in axes)) * zs + k
        return copy(ref, ref, ag_send.at[n.index, slot], ag_recv.at[n.index, slot], to)

    def core_copy(n, ref):
        return copy(ref, ref, core_send.at[n.index], core_recv.at[n.index], device(c_=1 - c))

    def ag_sends(n, axes, axis):
        axes = axes.replace("z", "")
        if axis == "z":
            ref = side(n, axes, False)
            return [ag_copy(n, ref, axes, k, device(z_=z_at(k))) for k in range(1, zs)]
        ref = side(n, axes, before(n, "z", axis))
        return [ag_copy(n, ref, axes + axis, 0, neighbour(axis))]

    def ag_send_part(n, axes, axis):
        for moved in ag_sends(n, axes, axis):
            moved.start()

    def ag_wait_part(n, axes):
        last = max(axes, key=n.route.index)
        axes = axes.replace("z", "")
        if last == "z":
            yy, xx = (1 - y if "y" in axes else y), (1 - x if "x" in axes else x)
            for k in range(1, zs):
                ag_copy(n, n.u.at[yy, xx, z_at(zs - k), n.rows], axes, k, device()).wait_recv()
        else:
            ag_copy(n, side(n, axes, before(n, "z", last)), axes, 0, device()).wait_recv()
        if n.other is not None and (last == "z" or before(n, "z", last)):
            core_copy(n, side(n, axes, True)).start()

    def ag_done(n):
        if n.other is not None:
            core_copy(n, n.other.at[:, :, :, n.rows]).wait_recv()

    def ag_drain(n):
        for axis in n.route:
            earlier = [other for other in "yx" if before(n, other, axis)]
            for some in range(2 ** len(earlier)):
                axes = "".join(other for bit, other in enumerate(earlier) if some >> bit & 1)
                for moved in ag_sends(n, axes, axis):
                    moved.wait_send()
        if n.other is not None:
            core_copy(n, n.u.at[:, :, :, n.rows]).wait_send()

    AXES = "yxz"

    def rs_groups(n, step):
        axis = n.route[step]
        if axis == "z":
            return [(k, 1 + k, device(z_=z_at(zs - k))) for k in range(1, zs)]
        return [(1, "yx".index(axis), neighbour(axis))]

    def rs_where(n, step, k):
        axis, out, land = n.route[step], [], []
        for other in AXES:
            if other == axis:
                out.append(z_at(zs - k) if axis == "z" else 1 - ME[axis])
                land.append(k)
            elif before(n, other, axis):
                out.append(ME[other])
                land.append(0)
            else:
                out.append(slice(None))
                land.append(slice(None))
        return tuple(out) + (n.rows,), tuple(land) + (n.rows,)

    def rs_copy(n, step, k, slot, to):
        out, land = rs_where(n, step, k)
        return copy(n.u.at[out], n.got.at[land], rs_send.at[n.index, slot], rs_recv.at[n.index, slot], to)

    def rs_core(n):
        return copy(n.other.at[:, :, :, n.rows], n.core_in.at[:, :, :, n.rows], rs_send.at[n.index, zs + 1],
                    rs_recv.at[n.index, zs + 1], device(c_=1 - c))

    def add_terms(n, place, step):
        value = n.u[tuple(place) + (n.rows,)].astype(F32)
        if n.other is not None:
            value = value + n.core_in[tuple(place) + (n.rows,)].astype(F32)
        for axis in n.route[:step]:
            for k in range(1, zs) if axis == "z" else (1,):
                where = [k if other == axis else (0 if before(n, other, axis) else at_place)
                         for other, at_place in zip(AXES, place)]
                value = value + n.got[tuple(where) + (n.rows,)].astype(F32)
        return value

    def rs_start(n):
        rs_core(n).start()

    def rs_step(n, step):
        if step == 0 and n.other is not None:
            rs_core(n).wait_recv()
        if step > 0:
            for group in rs_groups(n, step - 1):
                rs_copy(n, step - 1, *group).wait_recv()
        if step == 3:
            n.total[n.rows, :] = add_terms(n, (y, x, z), 3)
            return
        for k, slot, to in rs_groups(n, step):
            out, _ = rs_where(n, step, k)
            if step > 0 or n.other is not None:
                spans = [range(2) if isinstance(at_place, slice) else (at_place,) for at_place in out[:2]]

                def body(zz):
                    for yy in spans[0]:
                        for xx in spans[1]:
                            n.u[yy, xx, zz, n.rows] = add_terms(n, (yy, xx, zz), step).astype(BF16)

                if isinstance(out[2], slice):
                    loop(zs, body)
                else:
                    body(out[2])
            rs_copy(n, step, k, slot, to).start()

    def rs_drain(n):
        if n.other is not None:
            rs_core(n).wait_send()
        for step in range(3):
            for group in rs_groups(n, step):
                rs_copy(n, step, *group).wait_send()

    def small_sum(ref, slots, which):
        to = (device(y_=1 - y), device(c_=1 - c), device(x_=1 - x))
        to += tuple(device(z_=z_at(k)) for k in range(1, zs))

        def moved(slot):
            return copy(ref, slots.at[slot], v_send.at[which, slot], v_recv.at[which, slot], to[slot])

        def land(last):
            moved(last).wait()
            ref[...] = ref[...] + slots[last]

        def step(n):
            def run():
                if n > 0:
                    land(n - 1)
                moved(n).start()

            return run

        def line():
            land(2)
            for k in range(1, zs):
                moved(2 + k).start()

        def finish():
            for k in range(1, zs):
                moved(2 + k).wait()
            value = ref[...]
            for k in range(1, zs):
                value = value + slots[2 + k]
            ref[...] = value

        return [step(0), step(1), step(2), line, finish]

    def rows_of(s):
        return pl.ds(pl.multiple_of(s * 128, 128), 128)

    def exchange(src, dst, which):
        return [copy(src.at[block_at(k)], dst.at[i], a2a_send.at[which, k - 1],
                     a2a_recv.at[which, k - 1], {"blk": block_at(k), "batch": b})
                for k in range(1, 4)]

    def exchange_landed(dst, which):
        return [copy(dst.at[block_at(4 - k)], dst.at[block_at(4 - k)], a2a_send.at[which, k - 1],
                     a2a_recv.at[which, k - 1], {"blk": block_at(4 - k), "batch": b})
                for k in range(1, 4)]

    def axes_of(mask):
        return "".join(axis for axis, bit in (("y", Y), ("x", X), ("z", Z)) if mask & bit)

    def rows_in(part, count):
        return pl.ds(part * (288 // count), 288 // count)

    units = []
    for unit, routes in enumerate(GATHER_ROUTES):
        half = unit % 2
        ref = (ua, uw1, uw2)[unit // 2]
        pieces = (ref.at[half, c], ref.at[half, 1 - c]) if unit < 2 else (ref.at[half], None)
        for part, route in enumerate(routes):
            units.append(Unit(len(units), "".join(map(axes_of, route)), rows_in(part, len(routes)), *pieces))

    def pair(slot, src, dst):
        return copy(src, dst, pair_send.at[slot], pair_recv.at[slot], device(c_=1 - c))

    w1_swap, w2_swap = pair(0, w1_in, w1_other), pair(1, w2_in, w2_other)

    def each_core(f):
        for q in range(2):
            pl.when(c == q)(functools.partial(f, q))

    def rest_rows(matrix):
        return a_in[matrix, pl.ds(pl.multiple_of(128 * (1 - c), 64), 64), :]

    def own_attention(p):
        mine = ua.at[p, c, y, x, z]
        for m in range(2):
            main = a_in[2 * p + m, pl.ds(pl.multiple_of(64 * c, 64), 128), :]
            mine[96 * m : 96 * m + 96, :] = main.T.astype(BF16)
        rest = jnp.concatenate([rest_rows(2 * p + c), rest_rows(2 * p + 1 - c)], axis=0)
        mine[192:288, :] = rest.T.astype(BF16)

    def own_expand(q):
        both = (w1_in, w1_other) if q == 0 else (w1_other, w1_in)
        cols = slice(192 * q, 192 * q + 192)
        blocks = (
            both[0][0:128, cols],
            jnp.concatenate([both[0][128:192, cols], both[1][0:64, cols]], axis=0),
            both[1][64:192, cols],
        )
        for t, block in enumerate(blocks):
            value = block.T.astype(BF16)
            for h in range(2):
                uw1[h, y, x, z, 96 * t : 96 * t + 96, :] = value[96 * h : 96 * h + 96, :]

    def own_reduce(q):
        both = (w2_in, w2_other) if q == 0 else (w2_other, w2_in)
        for cc in range(2):
            for part_of in range(2):
                start = 384 * part_of + 192 * q
                lines[:, 192 * part_of : 192 * part_of + 192] = both[cc][:, start : start + 192]
            for t in range(3):
                uw2[cc, y, x, z, 96 * t : 96 * t + 96, :] = lines[:, 128 * t : 128 * t + 128].astype(BF16)

    def own_hidden_bias(q):
        for zz in range(zs):
            for xx in range(2):
                col = 384 * (zz % 2) + 192 * xx
                start = 384 * xx + 192 * q
                b1[zz // 2 : zz // 2 + 1, col : col + 192] = vec[8 + zz : 9 + zz, start : start + 192]

    def hidden_bias_gradient(q):
        for zz in range(zs):
            for xx in range(2):
                col = 384 * (zz % 2) + 192 * xx
                start = 384 * xx + 192 * q
                gvec[8 + zz : 9 + zz, start : start + 192] = gb1[zz // 2 : zz // 2 + 1, col : col + 192]

    columns = a_in.shape[2]
    placed = lax.broadcasted_iota(jnp.int32, (columns, 768), 1) == (
        lax.broadcasted_iota(jnp.int32, (columns, 768), 0) + columns * g
    )

    def own_vectors():
        vec[...] = jnp.zeros_like(vec)
        rows = dot_nn(vec_in[...].astype(BF16), jnp.where(placed, 1.0, 0.0).astype(BF16))
        for j in range(3):
            vec[pl.ds(3 * i + j, 1), :] = rows[j : j + 1, :]

    loads = [pltpu.make_async_copy(src, dst, local_sem.at[4 + n]) for n, (src, dst) in enumerate((
        (a_hbm, a_in), (vec_hbm, vec_in), (w1_hbm, w1_in), (w2_hbm, w2_in), (cot, stage), (mask_hbm, mask_in)
    ))]
    load_a, load_vec, load_w1, load_w2, load_cot, load_mask = loads
    for load in loads:
        load.start()

    def masked_cotangent():
        load_cot.wait()
        load_mask.wait()
        eye = lax.broadcasted_iota(jnp.int32, (128, 128), 0) == lax.broadcasted_iota(jnp.int32, (128, 128), 1)
        for s in range(4):
            row = jnp.broadcast_to(mask_in[s : s + 1, :].astype(F32), (128, 128))
            column = jnp.sum(jnp.where(eye, row, 0.0), axis=1, keepdims=True)
            stage[s] = (stage[s].astype(F32) * column).astype(BF16)

    def finish_attention(p):
        value = totals.at[p]
        for m in range(2):
            ga[2 * p + m, pl.ds(pl.multiple_of(64 * c, 64), 128), :] = value[96 * m : 96 * m + 96, :].T
        rest = value[192:288, :].T
        rows = pl.ds(pl.multiple_of(128 * (1 - c), 64), 64)
        ga[2 * p + c, rows, :] = rest[0:64, :]
        ga[2 * p + 1 - c, rows, :] = rest[64:128, :]

    w1_back = pair(6, turned1.at[pl.ds(pl.multiple_of(192 * (1 - c), 64), 192)], got1)
    w2_back = pair(7, totals.at[5 - c], got2)

    def turn_expand():
        for h in range(2):
            for t in range(3):
                turned1[128 * t : 128 * t + 128, 96 * h : 96 * h + 96] = totals[2 + h, 96 * t : 96 * t + 96, :].T
        w1_back.start()

    def join_expand(q):
        g1[:, 192 * q : 192 * q + 192] = turned1[192 * q : 192 * q + 192, :]
        g1[:, 192 * (1 - q) : 192 * (1 - q) + 192] = got1[...]

    def join_reduce(q):
        for half, value in ((q, totals.at[4 + q]), (1 - q, got2)):
            for t in range(3):
                lines[:, 128 * t : 128 * t + 128] = value[96 * t : 96 * t + 96, :]
            for part_of in range(2):
                start = 384 * part_of + 192 * half
                g2[:, start : start + 192] = lines[:, 192 * part_of : 192 * part_of + 192]

    def finish_vectors():
        value, total = gvec[...], 0.0
        for _ in range(3):
            part = value.astype(BF16)
            total = total + dot_nt(part, jnp.where(placed, 1.0, 0.0).astype(BF16))
            value = value - part.astype(F32)
        narrow_rows[...] = total
        for j in range(3):
            gv[j : j + 1, :] = narrow_rows[pl.ds(3 * i + j, 1), :]

    grads, owners = [], []
    for unit, routes in enumerate(SUM_ROUTES):
        half = unit % 2
        ref = (ua, gw1, gw2)[unit // 2]
        pieces = (ref.at[half, c], ref.at[half, 1 - c], core_in.at[half]) if unit < 2 else (ref.at[half], None, None)
        for part, route in enumerate(routes):
            grads.append(Gradient(len(grads), "".join(map(axes_of, route)), rows_in(part, len(routes)), *pieces,
                                  got.at[unit], totals.at[unit]))
            owners.append(unit)

    def summed(unit):
        if unit < 2:
            finish_attention(unit)
        elif unit < 4 and {2, 3} <= set(whole):
            turn_expand()
        elif unit >= 4 and {4, 5} <= set(whole):
            w2_back.start()

    seen, whole = set(), []

    def event(kind, *rest):
        if kind == SEND:
            ag_send_part(units[rest[0]], axes_of(rest[1]), axes_of(rest[2]))
        elif kind == GOT:
            ag_wait_part(units[rest[0]], axes_of(rest[1]))
        elif kind == WHOLE:
            ag_done(units[rest[0]])
        elif kind == SUM:
            rs_step(grads[rest[0]], rest[1])
            if rest[1] == 3:
                seen.add(rest[0])
                unit = owners[rest[0]]
                if all(k in seen for k in range(len(grads)) if owners[k] == unit):
                    whole.append(unit)
                    summed(unit)
        elif kind == DO:
            actions[rest[0]]()
        else:
            (vec_steps if kind == VEC else gvec_steps)[rest[0] + 1]()

    def run(part):
        for todo in PLAN.get(part, ()):
            event(*todo)

    def parts(name, count, body):
        run(name + "0")
        hooks = [(k - 1, functools.partial(run, name + str(k))) for k in range(1, count) if name + str(k) in PLAN]
        loop(count, body, hooks)

    def in_line(name, count, body):
        for k in range(count):
            run(name + str(k))
            body(k)

    def started(copies):
        for moved in copies:
            moved.start()
        return copies

    def arrived(*copies):
        for moved in copies:
            moved.wait_recv()

    own_tokens = pltpu.make_async_copy(tok.at[i], x_in.at[i], local_sem.at[0])
    own_tokens.start()
    own_cot = pltpu.make_async_copy(stage.at[i], cot_in.at[i], local_sem.at[1])
    tokens_out, cot_out = exchange(tok, x_in, 0), exchange(stage, cot_in, 1)
    result_out = exchange(stage, out, 2)
    grad_out = [copy(n1.at[rows_of(block_at(k))], ig.at[i], a2a_send.at[3, k - 1], a2a_recv.at[3, k - 1],
                     {"blk": block_at(k), "batch": b}) for k in range(1, 4)]
    own_out = pltpu.make_async_copy(stage.at[i], out.at[i], local_sem.at[2])
    own_grad = pltpu.make_async_copy(n1.at[rows_of(i)], ig.at[i], local_sem.at[3])
    n2_swap, cot_swap = pair(2, n2, n2_other), pair(3, cot_in, cot_other)
    back_swap, ahead_swap = pair(4, d6, back_in), pair(5, n2, ahead_in)
    vec_steps, gvec_steps = small_sum(vec, vin, 0), small_sum(gvec, gin, 1)

    def tokens_here():
        arrived(*exchange_landed(x_in, 0))
        own_tokens.wait()

    def cotangent_here():
        arrived(*exchange_landed(cot_in, 1))
        own_cot.wait()
        cot_swap.start()

    def swaps_here():
        w1_swap.wait()
        w2_swap.wait()

    actions = {
        TOK: lambda: started(tokens_out),
        COT: lambda: started(cot_out),
        OUT: lambda: started(result_out),
        IG: lambda: started(grad_out),
        TOK_HERE: tokens_here,
        COT_HERE: cotangent_here,
        OUT_HERE: lambda: arrived(*exchange_landed(out, 2)),
        IG_HERE: lambda: arrived(*exchange_landed(ig, 3)),
        SWAP_HERE: swaps_here,
        N2S_HERE: lambda: n2_swap.wait(),
        COTS_HERE: lambda: cot_swap.wait(),
        BACKS_HERE: lambda: back_swap.wait(),
        AHEADS_HERE: lambda: ahead_swap.wait(),
    }

    load_a.wait()
    own_attention(0)
    load_vec.wait()
    own_vectors()
    load_w1.wait()
    load_w2.wait()
    pl.semaphore_wait(barrier, len(partners))
    vec_steps[0]()
    w1_swap.start()
    w2_swap.start()
    run("own1")
    own_attention(1)
    run("ownff")
    each_core(own_expand)
    each_core(own_reduce)
    run("mask")
    masked_cotangent()
    own_cot.start()
    run("ln1")
    each_core(own_hidden_bias)

    def normalise(value):
        centered = value - jnp.mean(value, axis=-1, keepdims=True)
        scale = lax.rsqrt(jnp.mean(centered * centered, axis=-1, keepdims=True) + norm_epsilon)
        return centered * scale, scale

    def first_norm(s):
        unit, _ = normalise(x_in[s].astype(F32))
        n1[rows_of(s), :] = (unit * vec[0:1, :] + vec[1:2, :]).astype(BF16)

    loop(4, first_norm)
    run("unp0")

    lanes = lax.broadcasted_iota(jnp.int32, (96, 128), 1)

    def unpack(p, s):
        for xx in range(2):
            rows = pl.ds(pl.multiple_of((2 * s + xx) * 96, 96), 96)
            for yy in range(2):
                first, second = ua.at[p, 0, yy, xx, s], ua.at[p, 1, yy, xx, s]
                lo, hi = 384 * yy, 384 * yy + 256
                for m in range(2):
                    at[2 * p + m, rows, lo : lo + 128] = first[96 * m : 96 * m + 96, :]
                    at[2 * p + m, rows, hi : hi + 128] = second[96 * m : 96 * m + 96, :]
                rest_first = first[192:288, :].astype(F32)
                rest_second = second[192:288, :].astype(F32)
                even = jnp.where(lanes < 64, rest_first, rest_second)
                odd = pltpu.roll(jnp.where(lanes < 64, rest_second, rest_first), 64, 1)
                at[2 * p, rows, lo + 128 : lo + 256] = even.astype(BF16)
                at[2 * p + 1, rows, lo + 128 : lo + 256] = odd.astype(BF16)

    def project(m, dst, bias):
        for n in range(3):
            value = dot_nt(n1[...], at[m, 256 * n : 256 * n + 256, :])
            if bias is not None:
                value = value + vec[bias : bias + 1, 256 * n : 256 * n + 256]
            value = value.astype(BF16)
            if m == 0:
                value = value * jnp.asarray(HEAD ** (-0.5), BF16)
            dst[2 * n] = value[:, 0:128]
            dst[2 * n + 1] = value[:, 128:256]

    loop(zs, functools.partial(unpack, 0))
    run("projq")
    project(0, q6, 2)
    run("projk")
    project(1, k6, None)

    half_lane = lax.broadcasted_iota(jnp.int32, (512, 128), 1) // HEAD

    def half_of(value, which):
        return jnp.where(half_lane == which, value, jnp.zeros_like(value))

    def turn(value):
        return value.astype(F32).T.astype(BF16)

    def two_pairs(body):
        def both(s):
            body(2 * s)
            body(2 * s + 1)

        return both

    def attend(p):
        queries, keys = q6[p], k6[p]
        for which in range(2):
            scores = dot_nt(half_of(keys, which), queries)
            expo = jnp.exp(scores - jnp.max(scores, axis=0, keepdims=True))
            probs = (expo * (1.0 / jnp.sum(expo, axis=0, keepdims=True))).astype(BF16)
            pt[2 * p + which] = probs

    def mix(p):
        values_t = turn(v6[p])
        mixed = [dot_nn(values_t[64 * which : 64 * which + 64, :], pt[2 * p + which]) for which in range(2)]
        o6[p] = jnp.concatenate(mixed, axis=0).T.astype(BF16)

    parts("attend", 3, two_pairs(attend))
    run("unp1")
    loop(zs, functools.partial(unpack, 1))
    run("projv")
    project(2, v6, 3)
    parts("mix", 3, two_pairs(mix))

    run("ao")
    for n in range(3):
        cols = slice(256 * n, 256 * n + 256)
        value = dot_nt(lane_tiles(o6), at[3, cols, :]) + vec[4:5, cols]
        for s in range(4):
            h1[128 * s : 128 * s + 128, cols] = x_in[s, :, cols].astype(F32) + value[128 * s : 128 * s + 128]

    def second_norm(s):
        unit, _ = normalise(h1[rows_of(s), :])
        n2[rows_of(s), :] = (unit * vec[5:6, :] + vec[6:7, :]).astype(BF16)

    run("ln2")
    loop(4, second_norm)
    n2_swap.start()

    def expand_block(s):
        def piece(ref):
            return jnp.concatenate([ref[96 * t : 96 * t + 96, :] for t in range(3)], axis=1)

        return jnp.concatenate(
            [jnp.concatenate([piece(uw1.at[h, yy, xx, 2 * s + zz]) for yy in range(2)], axis=1)
             for zz in range(2) for xx in range(2) for h in range(2)],
            axis=0,
        )

    def reduce_block(s):
        def piece(ref):
            return jnp.concatenate([ref[96 * t : 96 * t + 96, :] for t in range(3)], axis=1)

        return jnp.concatenate(
            [jnp.concatenate([piece(uw2.at[cc, s, xx, zz]) for cc in range(2)], axis=1)
             for zz in range(zs) for xx in range(2)],
            axis=0,
        )

    def block_rows(owner, s):
        return slice((2 * owner + s) * 512, (2 * owner + s) * 512 + 512)

    COLUMNS = [slice(256 * n, 256 * n + 256) for n in range(3)]

    def expand(owner, normed, s):
        rows, block = block_rows(owner, s), expand_block(s)
        for cols in COLUMNS:
            inner = dot_nt(normed[...], block[cols]) + b1[s : s + 1, cols]
            square = inner * inner
            tanh = jnp.tanh(GELU_SCALE * inner * (1.0 + GELU_CUBE * square))
            act[rows, cols] = (0.5 * inner * (1.0 + tanh)).astype(BF16)
            slope = 0.5 * (1.0 + tanh) + 0.5 * inner * (1.0 - tanh * tanh) * (
                GELU_SCALE * (1.0 + 3.0 * GELU_CUBE * square)
            )
            gp[rows, cols] = slope.astype(BF16)

    in_line("expa", 2, functools.partial(expand, 0, n2))
    in_line("expb", 2, functools.partial(expand, 1, n2_other))

    gvec[...] = jnp.zeros_like(gvec)

    def transpose_rows(dst, s, value):
        dst[:, 128 * s : 128 * s + 128] = turn(value)

    run("trY")
    total = jnp.zeros((1, 768), F32)
    for s in range(4):
        transpose_rows(ta, s, cot_in[s])
        total = total + jnp.sum(cot_in[s].astype(F32), axis=0, keepdims=True)
    gvec[7:8, :] = total
    for s in range(4):
        transpose_rows(tb, s, cot_other[s])

    def both_rows(ref, s):
        return jnp.concatenate([ref[block_rows(0, s), :], ref[block_rows(1, s), :]], axis=0)

    def reduce_back(s):
        turned, rows = jnp.concatenate([ta[...], tb[...]], axis=1), both_rows(act, s)
        for n, cols in enumerate(COLUMNS):
            grad = dot_nn(turned, rows[:, cols]).astype(BF16)
            for zz in range(zs):
                for xx in range(2):
                    row = 96 * (2 * zz + xx)
                    for e in range(2):
                        cc, t = divmod(2 * n + e, 3)
                        gw2[cc, s, xx, zz, 96 * t : 96 * t + 96, :] = grad[
                            row : row + 96, 128 * e : 128 * e + 128
                        ]

    in_line("gw2_", 2, reduce_back)

    def rows_together(ref):
        return jnp.concatenate([ref[s] for s in range(4)], axis=0)

    def inner_back(owner, cotangent_rows, s):
        rows, block, left = block_rows(owner, s), reduce_block(s), rows_together(cotangent_rows)
        for cols in COLUMNS:
            grad = dot_nn(left, block[:, cols]) * gp[rows, cols].astype(F32)
            low = grad.astype(BF16)
            gp[rows, cols] = low
            sums = jnp.sum(low.astype(F32), axis=0, keepdims=True)
            gb1[s : s + 1, cols] = sums if owner == 1 else gb1[s : s + 1, cols] + sums

    def norm_back(owner):
        left = jnp.concatenate([gp[block_rows(owner, s), :] for s in range(2)], axis=1)
        right = jnp.concatenate([expand_block(s) for s in range(2)], axis=0)
        return [dot_nn(left, right[:, cols]) for cols in COLUMNS]

    in_line("innb", 2, functools.partial(inner_back, 1, cot_other))
    run("dn2b")
    for n, value in enumerate(norm_back(1)):
        low = value.astype(BF16)
        d6[2 * n] = low[:, 0:128]
        d6[2 * n + 1] = low[:, 128:256]
    back_swap.start()
    in_line("inna", 2, functools.partial(inner_back, 0, cot_in))
    each_core(hidden_bias_gradient)
    run("dn2a")
    for cols, value in zip(COLUMNS, norm_back(0)):
        acc[:, cols] = value

    def expand_back(s):
        turned = jnp.concatenate([turn(gp[block_rows(owner, s), :]) for owner in range(2)], axis=1)
        normed = jnp.concatenate([n2[...], n2_other[...]], axis=0)
        for n, cols in enumerate(COLUMNS):
            grad = dot_nn(turned, normed[:, cols]).astype(BF16)
            for zz in range(2):
                for xx in range(2):
                    for h in range(2):
                        row = 384 * zz + 192 * xx + 96 * h
                        for e in range(2):
                            yy, t = divmod(2 * n + e, 3)
                            gw1[h, yy, xx, 2 * s + zz, 96 * t : 96 * t + 96, :] = grad[
                                row : row + 96, 128 * e : 128 * e + 128
                            ]

    in_line("gw1_", 2, expand_back)
    run("hid")

    def norm_gradient(value, scale_row, grad):
        unit, scale = normalise(value)
        gain_sum = jnp.sum(grad * unit, axis=0, keepdims=True)
        bias_sum = jnp.sum(grad, axis=0, keepdims=True)
        inner = grad * scale_row
        mean = jnp.mean(inner, axis=-1, keepdims=True)
        along = jnp.mean(inner * unit, axis=-1, keepdims=True)
        return scale * (inner - mean - unit * along), gain_sum, bias_sum

    def hidden_back(s):
        rows = rows_of(s)
        grad_in = jnp.concatenate([back_in[t, rows, :] for t in range(6)], axis=1)
        grad_in = acc[rows, :] + grad_in.astype(F32)
        grad, gain_sum, bias_sum = norm_gradient(h1[rows, :], vec[5:6, :], grad_in)
        grad = grad + cot_in[s].astype(F32)
        acc[rows, :] = grad
        low = grad.astype(BF16)
        n2[rows, :] = low
        gvec[5:6, :] += gain_sum
        gvec[6:7, :] += bias_sum
        gvec[4:5, :] += jnp.sum(low.astype(F32), axis=0, keepdims=True)

    loop(4, hidden_back)

    run("dO")
    for n in range(3):
        value = dot_nn(n2[...], at[3, :, 256 * n : 256 * n + 256]).astype(BF16)
        d6[2 * n] = value[:, 0:128]
        d6[2 * n + 1] = value[:, 128:256]
    run("gao")
    for s in range(4):
        transpose_rows(tc, s, n2[128 * s : 128 * s + 128, :])
    mixed_rows = lane_tiles(o6)
    for cols in COLUMNS:
        gp[768:1536, cols] = dot_nn(tc[...], mixed_rows[:, cols]).astype(BF16)

    def value_back(p):
        grads_in, grad_value = d6[p], 0.0
        for which in range(2):
            grad_value = grad_value + dot_nn(pt[2 * p + which], half_of(grads_in, which))
        tc[rows_of(p), :] = grad_value.T.astype(BF16)
        o6[p] = grad_value.astype(BF16)

    def attend_back(p):
        rows = rows_of(p)
        queries, keys, values, grads_in = q6[p], k6[p], v6[p], d6[p]
        keys_t = turn(keys)
        grad_query, grad_key = [], 0.0
        for which in range(2):
            wide = pt[2 * p + which].astype(F32)
            grad_probs = dot_nt(half_of(values, which), grads_in)
            inner = jnp.sum(wide * grad_probs, axis=0, keepdims=True)
            grad_scores = (wide * (grad_probs - inner)).astype(BF16)
            grad_query.append(dot_nn(keys_t[64 * which : 64 * which + 64, :], grad_scores))
            grad_key = grad_key + dot_nn(grad_scores, half_of(queries, which))
        grad_query = jnp.concatenate(grad_query, axis=0) * HEAD ** (-0.5)
        ta[rows, :] = grad_query.astype(BF16)
        tb[rows, :] = grad_key.T.astype(BF16)
        q6[p] = grad_query.T.astype(BF16)
        k6[p] = grad_key.astype(BF16)

    def pack(p, first_row, second_row):
        def body(s):
            for xx in range(2):
                offset = (2 * s + xx) * 96
                rows = [pl.ds(pl.multiple_of(first_row + offset, 96), 96),
                        pl.ds(pl.multiple_of(second_row + offset, 96), 96)]
                first, second = ua.at[p, 0, :, xx, s], ua.at[p, 1, :, xx, s]
                for yy in range(2):
                    lo, mid, hi = 384 * yy, 384 * yy + 128, 384 * yy + 256
                    for m in range(2):
                        first[yy, 96 * m : 96 * m + 96, :] = gp[rows[m], lo : lo + 128]
                        second[yy, 96 * m : 96 * m + 96, :] = gp[rows[m], hi : hi + 128]
                    even = gp[rows[0], mid : mid + 128].astype(F32)
                    odd = pltpu.roll(gp[rows[1], mid : mid + 128].astype(F32), 64, 1)
                    first[yy, 192:288, :] = jnp.where(lanes < 64, even, odd).astype(BF16)
                    second[yy, 192:288, :] = jnp.where(lanes < 64, odd, even).astype(BF16)

        loop(zs, body)

    parts("av", 3, two_pairs(value_back))
    run("gav")
    for n in units[VO[0] : VO[1] + 1]:
        ag_drain(n)
    for cols in COLUMNS:
        gp[0:768, cols] = dot_nn(tc[...], n1[:, cols]).astype(BF16)
    pack(1, 0, 768)
    for n in grads[AVO[0] : AVO[1] + 1]:
        rs_start(n)
    parts("ab", 3, two_pairs(attend_back))
    run("gaqk")
    for n in units[QK[0] : QK[1] + 1]:
        ag_drain(n)
    for cols in COLUMNS:
        gp[0:768, cols] = dot_nn(ta[...], n1[:, cols]).astype(BF16)
    for cols in COLUMNS:
        gp[768:1536, cols] = dot_nn(tb[...], n1[:, cols]).astype(BF16)
    pack(0, 0, 768)
    for n in grads[AQK[0] : AQK[1] + 1]:
        rs_start(n)

    def reduce(owner):
        left = jnp.concatenate([act[block_rows(owner, s), :] for s in range(2)], axis=1)
        right = jnp.concatenate([reduce_block(s) for s in range(2)], axis=1)
        return [dot_nt(left, right[cols]) for cols in COLUMNS]

    def layer_output():
        run("redb")
        for cols, value in zip(COLUMNS, reduce(1)):
            n2[:, cols] = value.astype(BF16)
        ahead_swap.start()
        run("reda")
        for cols, value in zip(COLUMNS, reduce(0)):
            h1[:, cols] = h1[:, cols] + vec[7:8, cols] + value
        run("outst")
        for moved in cot_out:
            moved.wait_send()
        for s in range(4):
            rows = slice(128 * s, 128 * s + 128)
            stage[s] = (h1[rows, :] + ahead_in[rows, :].astype(F32)).astype(BF16)
        own_out.start()

    layer_output()
    run("dn1")
    left = jnp.concatenate([lane_tiles(q6), lane_tiles(k6), lane_tiles(o6)], axis=1)
    for cols in COLUMNS:
        h1[:, cols] = dot_nn(left, jnp.concatenate([at[m, :, cols] for m in range(3)], axis=0))
    gvec[2:3, :] = jnp.sum(lane_tiles(q6).astype(F32), axis=0, keepdims=True)
    gvec[3:4, :] = jnp.sum(lane_tiles(o6).astype(F32), axis=0, keepdims=True)

    run("inb")

    def input_back(s):
        rows = rows_of(s)
        grad, gain_sum, bias_sum = norm_gradient(x_in[s].astype(F32), vec[0:1, :], h1[rows, :])
        n1[rows, :] = (grad + acc[rows, :]).astype(BF16)
        gvec[0:1, :] += gain_sum
        gvec[1:2, :] += bias_sum

    loop(4, input_back)
    gvec_steps[0]()
    own_grad.start()
    run("end")
    finish_vectors()
    w1_back.wait()
    each_core(join_expand)
    w2_back.wait()
    each_core(join_reduce)

    own_out.wait()
    own_grad.wait()
    for moved in tokens_out + result_out + grad_out:
        moved.wait_send()
    for n in units[VO[1] + 1 :]:
        ag_drain(n)
    for n in grads:
        rs_drain(n)


def layer(sub, tokens, cotangent, span_mask, vectors, attention, expand, reduce_t):
    zs = GROUPS // 2
    seqs, block, width = tokens.shape
    rows = seqs * block
    columns = attention.shape[2]
    piece = (3 * columns, 128)
    vmem = lambda shape, dtype: pltpu.VMEM(shape, dtype)
    half = (2, 2, 2, zs) + piece
    scratch = [vmem(value.shape, value.dtype) for value in (span_mask, vectors, attention, expand, reduce_t)]
    scratch += [vmem((2,) + half, BF16)] + [vmem(half, BF16)] * 4
    scratch += [vmem((2, 2, 2, zs) + piece, BF16), vmem((6, 2, 2, zs) + piece, BF16)]
    scratch += [vmem(tokens.shape, BF16)] * 3
    scratch += [vmem((16, width), F32)] * 2
    scratch += [vmem((zs + 2, 16, width), F32)] * 2
    scratch += [vmem((16, columns), F32)]
    tiles = vmem((width // 128, rows, 128), BF16)
    flat = vmem((rows, width), BF16)
    turned = vmem((width, rows), BF16)
    scratch += [vmem((4, width, width), BF16), flat, tiles, tiles, tiles, tiles]
    scratch += [vmem((HEADS, rows, rows), BF16), vmem((rows, width), F32), vmem((rows, width), F32)]
    scratch += [flat, vmem((4 * rows, width), BF16), vmem((4 * rows, width), BF16)]
    scratch += [turned, turned, turned, tiles]
    scratch += [vmem(expand.shape, F32), vmem(reduce_t.shape, F32), flat, vmem(tokens.shape, BF16)]
    scratch += [tiles, flat, vmem((columns, width // 2), F32), vmem((2, width), F32), vmem((2, width), F32)]
    scratch += [vmem((6,) + piece, F32), vmem((width // 2, 2 * columns), F32)]
    scratch += [vmem((2 * columns, 2 * columns), F32), vmem(piece, F32)]
    scratch += [pltpu.SemaphoreType.DMA((10,))]
    gathered, summed = sum(map(len, GATHER_ROUTES)), sum(map(len, SUM_ROUTES))
    scratch += [pltpu.SemaphoreType.DMA((gathered, 4 * zs))] * 2
    scratch += [pltpu.SemaphoreType.DMA((gathered,))] * 2
    scratch += [pltpu.SemaphoreType.DMA((summed, zs + 2))] * 2
    scratch += [pltpu.SemaphoreType.DMA((4, 3))] * 2
    scratch += [pltpu.SemaphoreType.DMA((2, zs + 2))] * 2
    scratch += [pltpu.SemaphoreType.DMA((8,))] * 2
    in_vmem = pl.BlockSpec(memory_space=pltpu.VMEM)
    anywhere = pl.BlockSpec(memory_space=pl.ANY)
    return pl.pallas_call(
        functools.partial(kernel, sub, zs),
        out_shape=(
            jax.ShapeDtypeStruct(tokens.shape, BF16),
            jax.ShapeDtypeStruct(tokens.shape, BF16),
            jax.ShapeDtypeStruct(attention.shape, F32),
            jax.ShapeDtypeStruct(expand.shape, F32),
            jax.ShapeDtypeStruct(reduce_t.shape, F32),
            jax.ShapeDtypeStruct(vectors.shape, F32),
        ),
        in_specs=[anywhere] * 7,
        out_specs=(anywhere, anywhere) + (in_vmem,) * 4,
        scratch_shapes=scratch,
        compiler_params=pltpu.CompilerParams(
            collective_id=0, has_side_effects=True, vmem_limit_bytes=65400 * 1024
        ),
    )(tokens, cotangent, span_mask, vectors, attention, expand, reduce_t)


def update_kernel(rates, *refs):
    count = len(rates)
    ins, (result, grad) = refs[: 4 * count], refs[4 * count : 4 * count + 2]
    outs, (result_out, grad_out) = refs[4 * count + 2 : 7 * count + 2], refs[7 * count + 2 : 7 * count + 4]
    held, (low, wide, passed) = refs[7 * count + 4 : 11 * count + 4], refs[11 * count + 4 : 11 * count + 7]
    in_sems, out_sems = refs[11 * count + 7 :]
    loads = [pltpu.make_async_copy(ins[n], held[n], in_sems.at[n]) for n in range(4 * count)]
    stores = [pltpu.make_async_copy(held[4 * n + m], outs[3 * n + m], out_sems.at[3 * n + m])
              for n in range(count) for m in range(3)]
    load_grad = pltpu.make_async_copy(grad, low, in_sems.at[4 * count])
    store_grad = pltpu.make_async_copy(wide, grad_out, out_sems.at[3 * count])
    load_result = pltpu.make_async_copy(result, passed, in_sems.at[4 * count + 1])
    store_result = pltpu.make_async_copy(passed, result_out, out_sems.at[3 * count + 1])
    load_grad.start()
    load_result.start()
    for copy in loads:
        copy.start()
    load_result.wait()
    store_result.start()
    load_grad.wait()

    def widen(s, carry):
        wide[s] = low[s].astype(F32)
        return carry

    lax.fori_loop(0, low.shape[0], widen, 0)
    store_grad.start()
    for n in range(count):
        for m in range(4):
            loads[4 * n + m].wait()
        weight, one, two, gradient = held[4 * n : 4 * n + 4]
        values = adamw(weight[...], one[...], two[...], gradient[...], rates[n])
        for ref, value in zip((weight, one, two), values):
            ref[...] = value
        for m in range(3):
            stores[3 * n + m].start()
    for copy in stores + [store_grad, store_result]:
        copy.wait()


def update(rates, arrays, result, grad):
    flat = [value for group in arrays for value in group]
    new = [jax.ShapeDtypeStruct(value.shape, F32) for group in arrays for value in group[:3]]
    new += [jax.ShapeDtypeStruct(result.shape, BF16), jax.ShapeDtypeStruct(grad.shape, F32)]
    anywhere = pl.BlockSpec(memory_space=pl.ANY)
    scratch = [pltpu.VMEM(value.shape, F32) for value in flat]
    scratch += [pltpu.VMEM(grad.shape, BF16), pltpu.VMEM(grad.shape, F32), pltpu.VMEM(result.shape, BF16)]
    scratch += [pltpu.SemaphoreType.DMA((len(flat) + 2,)), pltpu.SemaphoreType.DMA((len(new),))]
    return pl.pallas_call(
        functools.partial(update_kernel, rates),
        out_shape=tuple(new),
        in_specs=[anywhere] * (len(flat) + 2),
        out_specs=(anywhere,) * len(new),
        scratch_shapes=scratch,
        compiler_params=pltpu.CompilerParams(vmem_limit_bytes=63 * 1024 * 1024),
    )(*flat, result, grad)


def local(
    sub,
    tokens,
    cotangent,
    span_mask,
    attention_weight,
    expand_weight,
    reduce_weight,
    vectors,
    attention_first,
    attention_second,
    expand_first,
    expand_second,
    reduce_first,
    reduce_second,
    vector_first,
    vector_second,
):
    together = [[n * sub + m for m in range(sub)] for n in range(GROUPS)]

    def widen(value, axis):
        if sub == 1:
            return value
        low = lax.all_gather(
            value.astype(BF16), "batch", axis=axis, tiled=True, axis_index_groups=together
        )
        return low.astype(F32)

    def narrow(value, axis):
        if sub == 1:
            return value
        return lax.psum_scatter(
            value, "batch", scatter_dimension=axis, tiled=True, axis_index_groups=together
        )

    out_tokens, input_grad, ga, g1, g2, gv = layer(
        sub,
        tokens,
        cotangent,
        span_mask,
        widen(vectors, 1),
        widen(attention_weight, 2),
        widen(expand_weight, 1),
        widen(reduce_weight.T, 0),
    )
    arrays = (
        (attention_weight, attention_first, attention_second, narrow(ga, 2)),
        (expand_weight, expand_first, expand_second, narrow(g1, 1)),
        (reduce_weight.T, reduce_first.T, reduce_second.T, narrow(g2, 0)),
        (vectors, vector_first, vector_second, narrow(gv, 1)),
    )
    rates = (rate_attention, rate_expand, rate_reduce, rate_vector)
    new = update(rates, arrays, out_tokens, input_grad)
    return new[-2:] + new[0:6] + tuple(value.T for value in new[6:9]) + new[9:12]


def solution(mesh):
    sub = mesh.shape["batch"] // GROUPS
    sequences = P("batch", "blk", None)
    attention = P(None, "blk", "batch")
    matrix = P("blk", "batch")
    return jax.shard_map(
        functools.partial(local, sub),
        mesh=mesh,
        in_specs=(sequences, sequences, P("batch", "blk"), attention, matrix, matrix, matrix)
        + (attention,) * 2
        + (matrix,) * 6,
        out_specs=(sequences,) * 2 + (attention,) * 3 + (matrix,) * 9,
        check_vma=False,
    )
```

```python
import functools
import math

import jax
import jax.numpy as jnp
from jax import lax
from jax.experimental import pallas as pl
from jax.experimental.pallas import tpu as pltpu
from jax.sharding import PartitionSpec as P

HEADS = 12
HEAD = 64
STEP = 10
GROUPS = 8

norm_epsilon = 1e-05
beta_one = 0.9
beta_two = 0.999
adam_epsilon = 1e-08
decay_weight = 0.1
rate_attention = 0.05
rate_expand = 0.03
rate_reduce = 0.015
rate_vector = 0.4

F32 = jnp.float32
BF16 = jnp.bfloat16
MESH = pl.DeviceIdType.MESH
GELU_SCALE = math.sqrt(2.0 / math.pi)
GELU_CUBE = 0.044715


def adamw(weight, moment_one, moment_two, gradient, step_rate):
    moment_one = beta_one * moment_one + (1.0 - beta_one) * gradient
    moment_two = beta_two * moment_two + (1.0 - beta_two) * gradient * gradient
    corrected_one = moment_one / (1.0 - beta_one**STEP)
    corrected_two = moment_two / (1.0 - beta_two**STEP)
    updated = weight - step_rate * (
        corrected_one / (jnp.sqrt(corrected_two) + adam_epsilon) + decay_weight * weight
    )
    return (updated, moment_one, moment_two)


def dot_nn(left, right):
    return lax.dot_general(left, right, (((1,), (0,)), ((), ())), preferred_element_type=F32)


def dot_nt(left, right):
    return lax.dot_general(left, right, (((1,), (1,)), ((), ())), preferred_element_type=F32)


X, Y, Z = 1, 2, 4
(N_QKA, N_QKB, N_VOA, N_VOB, N_W10A, N_W10B, N_W11A, N_W11B, N_W20, N_W21A, N_W21B) = range(11)
(N_AQKA, N_AQKB, N_AVO, N_G10, N_G11, N_G20, N_G21) = range(7)
QK, VO = (N_QKA, N_QKB), (N_VOA, N_VOB)
AQK, AVO = (N_AQKA, N_AQKB), (N_AVO, N_AVO)
SEND, GOT, WHOLE, SUM, VEC, SMALL, DO = range(7)
(TOK, COT, OUT, IG, TOK_HERE, COT_HERE, OUT_HERE,
 IG_HERE, SWAP_HERE, N2S_HERE, COTS_HERE, BACKS_HERE, AHEADS_HERE) = range(13)
GATHER_ROUTES = (
    ((Z, Y, X), (Z, Y, X),),
    ((Z, X, Y), (Z, X, Y),),
    ((Y, Z, X), (Z, Y, X),),
    ((X, Y, Z), (Z, Y, X),),
    ((Z, X, Y),),
    ((Z, Y, X), (Y, X, Z),),
)
SUM_ROUTES = (
    ((X, Z, Y), (X, Z, Y),),
    ((Y, X, Z),),
    ((X, Z, Y),),
    ((Y, X, Z),),
    ((Y, Z, X),),
    ((X, Y, Z),),
)
PLAN = dict(
    own1=(
        (SEND, N_QKA, 0, Z),
    ),
    ownff=(
        (DO, TOK), (SEND, N_QKB, 0, Z), (DO, SWAP_HERE), (VEC, 0), (SEND, N_VOA, 0, Z),
    ),
    mask=(
        (SEND, N_W11A, 0, X), (GOT, N_QKA, Z), (SEND, N_QKA, Z, X), (GOT, N_W11A, X), (VEC, 1),
        (SEND, N_QKA, Z, Y), (GOT, N_QKB, Z), (SEND, N_QKB, Z, X), (SEND, N_W11A, 0, Y), (SEND, N_VOB, 0, Z),
    ),
    ln1=(
        (SEND, N_QKB, Z, Y), (VEC, 2), (SEND, N_W10B, 0, Z), (GOT, N_VOA, Z), (SEND, N_W11B, 0, Z),
        (SEND, N_VOA, Z, Y), (SEND, N_W10A, 0, Y), (SEND, N_VOA, Z, X), (GOT, N_QKA, Z | Y),
        (SEND, N_QKA, Z | Y, X), (GOT, N_QKB, Z | X), (GOT, N_QKB, Z | Y), (SEND, N_QKB, Z | Y, X),
        (SEND, N_W10A, 0, Z), (GOT, N_VOB, Z), (SEND, N_VOB, Z, X), (SEND, N_VOB, Z, Y), (GOT, N_QKA, Z | X),
        (GOT, N_W10A, Y), (GOT, N_VOA, Z | X), (DO, TOK_HERE), (SEND, N_W10A, Y, Z), (SEND, N_W11A, X, Y),
        (SEND, N_W20, 0, Z), (GOT, N_QKA, Z | Y | X), (GOT, N_W11B, Z), (SEND, N_W11B, Z, Y),
        (SEND, N_W11A, X, Z), (SEND, N_W11B, Z, X), (VEC, 3), (GOT, N_QKB, Z | Y | X), (GOT, N_VOA, Z | Y),
        (GOT, N_W10B, Z),
    ),
    unp0=(
        (GOT, N_W10A, Z), (GOT, N_W11A, Y), (GOT, N_VOB, Z | Y), (SEND, N_VOA, Z | X, Y),
        (SEND, N_W21B, 0, X), (SEND, N_W10A, Z, X), (SEND, N_W10B, Z, X), (SEND, N_W11A, 0, Z),
        (WHOLE, N_QKA), (WHOLE, N_QKB),
    ),
    projq=(
        (GOT, N_VOB, Z | X), (SEND, N_W21B, 0, Y),
    ),
    attend0=(
        (GOT, N_W11A, X | Y), (SEND, N_VOB, Z | X, Y), (GOT, N_W11B, Z | Y), (GOT, N_W10A, Y | Z),
        (SEND, N_W10B, Z, Y),
    ),
    attend1=(
        (SEND, N_W11B, Z | Y, X), (SEND, N_W11A, Y, Z),
    ),
    attend2=(
        (DO, COT),
    ),
    attend3=(
        (GOT, N_VOA, Z | X | Y),
    ),
    attend4=(
        (GOT, N_VOB, Z | X | Y),
    ),
    attend5=(
        (SEND, N_W10A, Y | Z, X), (SEND, N_W11A, X | Y, Z),
    ),
    unp1=(
        (GOT, N_W10B, Z | Y), (SEND, N_W10B, Z | Y, X), (WHOLE, N_VOA), (WHOLE, N_VOB), (GOT, N_W11B, Z | X),
    ),
    projv=(
        (GOT, N_W21B, Y), (GOT, N_W21B, X), (SEND, N_W21A, 0, Z),
    ),
    mix0=(
        (GOT, N_W11A, Z), (SEND, N_W21B, Y, Z), (GOT, N_W20, Z),
    ),
    mix2=(
        (SEND, N_W21B, 0, Z),
    ),
    mix3=(
        (GOT, N_W11B, Z | Y | X),
    ),
    mix5=(
        (SEND, N_W21B, Y, X), (GOT, N_W10A, Z | X), (GOT, N_W11A, X | Z), (SEND, N_W20, Z, Y),
    ),
    ao=(
        (SEND, N_W21B, X, Z), (SEND, N_W20, Z, X),
    ),
    ln2=(
        (GOT, N_W10A, Y | Z | X), (GOT, N_W10B, Z | X), (GOT, N_W11A, Y | Z),
    ),
    exp0=(
        (GOT, N_W10B, Z | Y | X), (GOT, N_W11A, X | Y | Z),
    ),
    exp1=(
        (DO, COT_HERE),
    ),
    exp2=(
        (GOT, N_W21A, Z), (SEND, N_W21A, Z, Y), (GOT, N_W21B, Y | X), (SEND, N_W21A, Z, X), (DO, N2S_HERE),
    ),
    exp3=(
        (GOT, N_W20, Z | X), (SEND, N_W21B, Y | X, Z), (SEND, N_W20, Z | X, Y), (DO, COTS_HERE),
    ),
    gw2_0=(
        (GOT, N_W21A, Z | Y), (SEND, N_W21A, Z | Y, X),
    ),
    inn0=(
        (SUM, N_G21, 0), (GOT, N_W20, Z | Y), (SUM, N_G20, 0), (GOT, N_W21B, Y | X | Z), (GOT, N_W21A, Z | X),
        (GOT, N_W21B, X | Z), (GOT, N_W21B, Z), (GOT, N_W21B, Y | Z), (GOT, N_W20, Z | X | Y),
        (GOT, N_W21A, Z | Y | X),
    ),
    hid=(
        (SUM, N_G10, 0), (SUM, N_G21, 1), (SUM, N_G20, 1), (DO, BACKS_HERE),
    ),
    av0=(
        (SUM, N_G11, 0),
    ),
    av5=(
        (SUM, N_G21, 2),
    ),
    ab3=(
        (SUM, N_G10, 1),
    ),
    ab4=(
        (SUM, N_AVO, 0),
    ),
    ab5=(
        (SUM, N_G11, 1),
    ),
    red0=(
        (SUM, N_G20, 2), (SUM, N_AQKA, 0),
    ),
    red1=(
        (SUM, N_G11, 2), (SUM, N_G10, 2), (SUM, N_AQKB, 0), (SUM, N_AVO, 1),
    ),
    outst=(
        (SUM, N_G21, 3), (DO, AHEADS_HERE),
    ),
    dn1=(
        (SUM, N_AQKA, 1), (SUM, N_G10, 3), (DO, OUT),
    ),
    inb=(
        (SUM, N_G11, 3), (SUM, N_G20, 3), (SUM, N_AQKB, 1),
    ),
    end=(
        (DO, IG), (SMALL, 0), (SUM, N_AVO, 2), (SMALL, 1), (SUM, N_AQKA, 2), (SMALL, 2), (SUM, N_AQKB, 2),
        (DO, IG_HERE), (DO, OUT_HERE), (SUM, N_AQKA, 3), (SUM, N_AVO, 3), (SUM, N_AQKB, 3), (SMALL, 3),
    ),
)


def lane_tiles(ref, count=6):
    return jnp.concatenate([ref[t] for t in range(count)], axis=1)


class Unit:
    def __init__(self, index, route, rows, u, other):
        self.index, self.route, self.rows, self.u, self.other = index, route, rows, u, other


class Gradient:
    def __init__(self, index, route, rows, u, other, core_in, got, total):
        self.index, self.route, self.rows, self.u, self.other = index, route, rows, u, other
        self.core_in, self.got, self.total = core_in, got, total


def kernel(sub, zs, *refs):
    (tok, cot, mask_hbm, vec_hbm, a_hbm, w1_hbm, w2_hbm,
     out, ig, ga, g1, g2, gv,
     mask_in, vec_in, a_in, w1_in, w2_in, ua, uw1, uw2, gw1, gw2, core_in, got,
     x_in, cots, stage, vec, gvec, vin, gin, narrow_rows,
     at, n1, heads, pt, h1, acc, normed, act, gp, turned, d6,
     w1_other, w2_other, back_in, ahead_in,
     lines, b1, gb1, totals, turned1, got1, got2,
     local_sem, ag_send, ag_recv, core_send, core_recv, rs_send, rs_recv,
     a2a_send, a2a_recv, v_send, v_recv, pair_send, pair_recv) = refs

    q6, k6, v6, o6 = (heads.at[m] for m in range(4))
    ta, tb, tc = (turned.at[m] for m in range(3))
    n2, n2_other, cot_in, cot_other = normed.at[0], normed.at[1], cots.at[0], cots.at[1]
    i = lax.axis_index("blk")
    b = lax.axis_index("batch")
    c, y = lax.rem(i, 2), lax.div(i, 2)
    g, r = lax.div(b, sub), lax.rem(b, sub)
    x, z = lax.rem(g, 2), lax.div(g, 2)

    def device(c_=c, y_=y, x_=x, z_=z):
        return {"blk": 2 * y_ + c_, "batch": (2 * z_ + x_) * sub + r}

    def z_at(k):
        return lax.rem(z + k, zs)

    def block_at(k):
        return lax.rem(i + k, 4)

    def copy(src, dst, send, recv, to):
        return pltpu.make_async_remote_copy(
            src_ref=src, dst_ref=dst, send_sem=send, recv_sem=recv, device_id=to, device_id_type=MESH
        )

    def loop(count, body, hooks=()):
        def step(s, carry):
            body(s)
            for k, f in hooks:
                pl.when(s == k)(f)
            return carry

        lax.fori_loop(0, count, step, 0)

    partners = [device(z_=z_at(k)) for k in range(1, zs)]
    partners += [device(x_=1 - x), device(y_=1 - y), device(c_=1 - c), device(c_=1 - c, y_=1 - y)]
    barrier = pltpu.get_barrier_semaphore()
    for partner in partners:
        pl.semaphore_signal(barrier, inc=1, device_id=partner, device_id_type=MESH)

    ME = {"y": y, "x": x, "z": z}

    def before(n, axis, other):
        return n.route.index(axis) < n.route.index(other)

    def side(n, axes, all_z):
        where = (1 - y if "y" in axes else y, 1 - x if "x" in axes else x, slice(None) if all_z else z)
        return n.u.at[where + (n.rows,)]

    def neighbour(axis):
        return device(y_=1 - y) if axis == "y" else device(x_=1 - x)

    def ag_copy(n, ref, axes, k, to):
        slot = (("y" in axes) * 2 + ("x" in axes)) * zs + k
        return copy(ref, ref, ag_send.at[n.index, slot], ag_recv.at[n.index, slot], to)

    def core_copy(n, ref):
        return copy(ref, ref, core_send.at[n.index], core_recv.at[n.index], device(c_=1 - c))

    def ag_sends(n, axes, axis):
        axes = axes.replace("z", "")
        if axis == "z":
            ref = side(n, axes, False)
            return [ag_copy(n, ref, axes, k, device(z_=z_at(k))) for k in range(1, zs)]
        ref = side(n, axes, before(n, "z", axis))
        return [ag_copy(n, ref, axes + axis, 0, neighbour(axis))]

    def ag_send_part(n, axes, axis):
        for moved in ag_sends(n, axes, axis):
            moved.start()

    def ag_wait_part(n, axes):
        last = max(axes, key=n.route.index)
        axes = axes.replace("z", "")
        if last == "z":
            yy, xx = (1 - y if "y" in axes else y), (1 - x if "x" in axes else x)
            for k in range(1, zs):
                ag_copy(n, n.u.at[yy, xx, z_at(zs - k), n.rows], axes, k, device()).wait_recv()
        else:
            ag_copy(n, side(n, axes, before(n, "z", last)), axes, 0, device()).wait_recv()
        if n.other is not None and (last == "z" or before(n, "z", last)):
            core_copy(n, side(n, axes, True)).start()

    def ag_done(n):
        if n.other is not None:
            core_copy(n, n.other.at[:, :, :, n.rows]).wait_recv()

    def ag_drain(n):
        for axis in n.route:
            earlier = [other for other in "yx" if before(n, other, axis)]
            for some in range(2 ** len(earlier)):
                axes = "".join(other for bit, other in enumerate(earlier) if some >> bit & 1)
                for moved in ag_sends(n, axes, axis):
                    moved.wait_send()
        if n.other is not None:
            core_copy(n, n.u.at[:, :, :, n.rows]).wait_send()

    AXES = "yxz"

    def rs_groups(n, step):
        axis = n.route[step]
        if axis == "z":
            return [(k, 1 + k, device(z_=z_at(zs - k))) for k in range(1, zs)]
        return [(1, "yx".index(axis), neighbour(axis))]

    def rs_where(n, step, k):
        axis, out, land = n.route[step], [], []
        for other in AXES:
            if other == axis:
                out.append(z_at(zs - k) if axis == "z" else 1 - ME[axis])
                land.append(k)
            elif before(n, other, axis):
                out.append(ME[other])
                land.append(0)
            else:
                out.append(slice(None))
                land.append(slice(None))
        return tuple(out) + (n.rows,), tuple(land) + (n.rows,)

    def rs_copy(n, step, k, slot, to):
        out, land = rs_where(n, step, k)
        return copy(n.u.at[out], n.got.at[land], rs_send.at[n.index, slot], rs_recv.at[n.index, slot], to)

    def rs_core(n):
        return copy(n.other.at[:, :, :, n.rows], n.core_in.at[:, :, :, n.rows], rs_send.at[n.index, zs + 1],
                    rs_recv.at[n.index, zs + 1], device(c_=1 - c))

    def add_terms(n, place, step):
        value = n.u[tuple(place) + (n.rows,)].astype(F32)
        if n.other is not None:
            value = value + n.core_in[tuple(place) + (n.rows,)].astype(F32)
        for axis in n.route[:step]:
            for k in range(1, zs) if axis == "z" else (1,):
                where = [k if other == axis else (0 if before(n, other, axis) else at_place)
                         for other, at_place in zip(AXES, place)]
                value = value + n.got[tuple(where) + (n.rows,)].astype(F32)
        return value

    def rs_start(n):
        rs_core(n).start()

    def rs_step(n, step):
        if step == 0 and n.other is not None:
            rs_core(n).wait_recv()
        if step > 0:
            for group in rs_groups(n, step - 1):
                rs_copy(n, step - 1, *group).wait_recv()
        if step == 3:
            n.total[n.rows, :] = add_terms(n, (y, x, z), 3)
            return
        for k, slot, to in rs_groups(n, step):
            out, _ = rs_where(n, step, k)
            if step > 0 or n.other is not None:
                spans = [range(2) if isinstance(at_place, slice) else (at_place,) for at_place in out[:2]]

                def body(zz):
                    for yy in spans[0]:
                        for xx in spans[1]:
                            n.u[yy, xx, zz, n.rows] = add_terms(n, (yy, xx, zz), step).astype(BF16)

                if isinstance(out[2], slice):
                    loop(zs, body)
                else:
                    body(out[2])
            rs_copy(n, step, k, slot, to).start()

    def rs_drain(n):
        if n.other is not None:
            rs_core(n).wait_send()
        for step in range(3):
            for group in rs_groups(n, step):
                rs_copy(n, step, *group).wait_send()

    def small_sum(ref, slots, which):
        to = (device(y_=1 - y), device(c_=1 - c), device(x_=1 - x))
        to += tuple(device(z_=z_at(k)) for k in range(1, zs))

        def moved(slot):
            return copy(ref, slots.at[slot], v_send.at[which, slot], v_recv.at[which, slot], to[slot])

        def land(last):
            moved(last).wait()
            ref[...] = ref[...] + slots[last]

        def step(n):
            def run():
                if n > 0:
                    land(n - 1)
                moved(n).start()

            return run

        def line():
            land(2)
            for k in range(1, zs):
                moved(2 + k).start()

        def finish():
            for k in range(1, zs):
                moved(2 + k).wait()
            value = ref[...]
            for k in range(1, zs):
                value = value + slots[2 + k]
            ref[...] = value

        return [step(0), step(1), step(2), line, finish]

    def rows_of(s):
        return pl.ds(pl.multiple_of(s * 128, 128), 128)

    def exchange(src, dst, which):
        return [copy(src.at[block_at(k)], dst.at[i], a2a_send.at[which, k - 1],
                     a2a_recv.at[which, k - 1], {"blk": block_at(k), "batch": b})
                for k in range(1, 4)]

    def exchange_landed(dst, which):
        return [copy(dst.at[block_at(4 - k)], dst.at[block_at(4 - k)], a2a_send.at[which, k - 1],
                     a2a_recv.at[which, k - 1], {"blk": block_at(4 - k), "batch": b})
                for k in range(1, 4)]

    def axes_of(mask):
        return "".join(axis for axis, bit in (("y", Y), ("x", X), ("z", Z)) if mask & bit)

    def rows_in(part, count):
        return pl.ds(part * (288 // count), 288 // count)

    units = []
    for unit, routes in enumerate(GATHER_ROUTES):
        half = unit % 2
        ref = (ua, uw1, uw2)[unit // 2]
        pieces = (ref.at[half, c], ref.at[half, 1 - c]) if unit < 2 else (ref.at[half], None)
        for part, route in enumerate(routes):
            units.append(Unit(len(units), "".join(map(axes_of, route)), rows_in(part, len(routes)), *pieces))

    def pair(slot, src, dst):
        return copy(src, dst, pair_send.at[slot], pair_recv.at[slot], device(c_=1 - c))

    w1_swap, w2_swap = pair(0, w1_in, w1_other), pair(1, w2_in, w2_other)

    def each_core(f):
        for q in range(2):
            pl.when(c == q)(functools.partial(f, q))

    def rest_rows(matrix):
        return a_in[matrix, pl.ds(pl.multiple_of(128 * (1 - c), 64), 64), :]

    def own_attention(p):
        mine = ua.at[p, c, y, x, z]
        for m in range(2):
            main = a_in[2 * p + m, pl.ds(pl.multiple_of(64 * c, 64), 128), :]
            mine[96 * m : 96 * m + 96, :] = main.T.astype(BF16)
        rest = jnp.concatenate([rest_rows(2 * p + c), rest_rows(2 * p + 1 - c)], axis=0)
        mine[192:288, :] = rest.T.astype(BF16)

    def own_expand(q):
        both = (w1_in, w1_other) if q == 0 else (w1_other, w1_in)
        cols = slice(192 * q, 192 * q + 192)
        blocks = (
            both[0][0:128, cols],
            jnp.concatenate([both[0][128:192, cols], both[1][0:64, cols]], axis=0),
            both[1][64:192, cols],
        )
        for t, block in enumerate(blocks):
            value = block.T.astype(BF16)
            for h in range(2):
                uw1[h, y, x, z, 96 * t : 96 * t + 96, :] = value[96 * h : 96 * h + 96, :]

    def own_reduce(q):
        both = (w2_in, w2_other) if q == 0 else (w2_other, w2_in)
        for cc in range(2):
            for part_of in range(2):
                start = 384 * part_of + 192 * q
                lines[:, 192 * part_of : 192 * part_of + 192] = both[cc][:, start : start + 192]
            for t in range(3):
                uw2[cc, y, x, z, 96 * t : 96 * t + 96, :] = lines[:, 128 * t : 128 * t + 128].astype(BF16)

    def own_hidden_bias(q):
        for zz in range(zs):
            for xx in range(2):
                col = 384 * (zz % 2) + 192 * xx
                start = 384 * xx + 192 * q
                b1[zz // 2 : zz // 2 + 1, col : col + 192] = vec[8 + zz : 9 + zz, start : start + 192]

    def hidden_bias_gradient(q):
        for zz in range(zs):
            for xx in range(2):
                col = 384 * (zz % 2) + 192 * xx
                start = 384 * xx + 192 * q
                gvec[8 + zz : 9 + zz, start : start + 192] = gb1[zz // 2 : zz // 2 + 1, col : col + 192]

    columns = a_in.shape[2]
    placed = lax.broadcasted_iota(jnp.int32, (columns, 768), 1) == (
        lax.broadcasted_iota(jnp.int32, (columns, 768), 0) + columns * g
    )

    def own_vectors():
        vec[...] = jnp.zeros_like(vec)
        rows = dot_nn(vec_in[...].astype(BF16), jnp.where(placed, 1.0, 0.0).astype(BF16))
        for j in range(3):
            vec[pl.ds(3 * i + j, 1), :] = rows[j : j + 1, :]

    loads = [pltpu.make_async_copy(src, dst, local_sem.at[4 + n]) for n, (src, dst) in enumerate((
        (a_hbm, a_in), (vec_hbm, vec_in), (w1_hbm, w1_in), (w2_hbm, w2_in), (cot, stage), (mask_hbm, mask_in)
    ))]
    load_a, load_vec, load_w1, load_w2, load_cot, load_mask = loads
    for load in loads:
        load.start()

    def masked_cotangent():
        load_cot.wait()
        load_mask.wait()
        eye = lax.broadcasted_iota(jnp.int32, (128, 128), 0) == lax.broadcasted_iota(jnp.int32, (128, 128), 1)
        for s in range(4):
            row = jnp.broadcast_to(mask_in[s : s + 1, :].astype(F32), (128, 128))
            column = jnp.sum(jnp.where(eye, row, 0.0), axis=1, keepdims=True)
            stage[s] = (stage[s].astype(F32) * column).astype(BF16)

    def finish_attention(p):
        value = totals.at[p]
        for m in range(2):
            ga[2 * p + m, pl.ds(pl.multiple_of(64 * c, 64), 128), :] = value[96 * m : 96 * m + 96, :].T
        rest = value[192:288, :].T
        rows = pl.ds(pl.multiple_of(128 * (1 - c), 64), 64)
        ga[2 * p + c, rows, :] = rest[0:64, :]
        ga[2 * p + 1 - c, rows, :] = rest[64:128, :]

    w1_back = pair(6, turned1.at[pl.ds(pl.multiple_of(192 * (1 - c), 64), 192)], got1)
    w2_back = pair(7, totals.at[5 - c], got2)

    def turn_expand():
        for h in range(2):
            for t in range(3):
                turned1[128 * t : 128 * t + 128, 96 * h : 96 * h + 96] = totals[2 + h, 96 * t : 96 * t + 96, :].T
        w1_back.start()

    def join_expand(q):
        g1[:, 192 * q : 192 * q + 192] = turned1[192 * q : 192 * q + 192, :]
        g1[:, 192 * (1 - q) : 192 * (1 - q) + 192] = got1[...]

    def join_reduce(q):
        for half, value in ((q, totals.at[4 + q]), (1 - q, got2)):
            for t in range(3):
                lines[:, 128 * t : 128 * t + 128] = value[96 * t : 96 * t + 96, :]
            for part_of in range(2):
                start = 384 * part_of + 192 * half
                g2[:, start : start + 192] = lines[:, 192 * part_of : 192 * part_of + 192]

    def finish_vectors():
        value, total = gvec[...], 0.0
        for _ in range(3):
            part = value.astype(BF16)
            total = total + dot_nt(part, jnp.where(placed, 1.0, 0.0).astype(BF16))
            value = value - part.astype(F32)
        narrow_rows[...] = total
        for j in range(3):
            gv[j : j + 1, :] = narrow_rows[pl.ds(3 * i + j, 1), :]

    grads, owners = [], []
    for unit, routes in enumerate(SUM_ROUTES):
        half = unit % 2
        ref = (ua, gw1, gw2)[unit // 2]
        pieces = (ref.at[half, c], ref.at[half, 1 - c], core_in.at[half]) if unit < 2 else (ref.at[half], None, None)
        for part, route in enumerate(routes):
            grads.append(Gradient(len(grads), "".join(map(axes_of, route)), rows_in(part, len(routes)), *pieces,
                                  got.at[unit], totals.at[unit]))
            owners.append(unit)

    def summed(unit):
        if unit < 2:
            finish_attention(unit)
        elif unit < 4 and {2, 3} <= set(whole):
            turn_expand()
        elif unit >= 4 and {4, 5} <= set(whole):
            w2_back.start()

    seen, whole = set(), []

    def event(kind, *rest):
        if kind == SEND:
            ag_send_part(units[rest[0]], axes_of(rest[1]), axes_of(rest[2]))
        elif kind == GOT:
            ag_wait_part(units[rest[0]], axes_of(rest[1]))
        elif kind == WHOLE:
            ag_done(units[rest[0]])
        elif kind == SUM:
            rs_step(grads[rest[0]], rest[1])
            if rest[1] == 3:
                seen.add(rest[0])
                unit = owners[rest[0]]
                if all(k in seen for k in range(len(grads)) if owners[k] == unit):
                    whole.append(unit)
                    summed(unit)
        elif kind == DO:
            actions[rest[0]]()
        else:
            (vec_steps if kind == VEC else gvec_steps)[rest[0] + 1]()

    def run(part):
        for todo in PLAN.get(part, ()):
            event(*todo)

    def parts(name, count, body):
        run(name + "0")
        hooks = [(k - 1, functools.partial(run, name + str(k))) for k in range(1, count) if name + str(k) in PLAN]
        loop(count, body, hooks)

    def started(copies):
        for moved in copies:
            moved.start()
        return copies

    def arrived(*copies):
        for moved in copies:
            moved.wait_recv()

    own_tokens = pltpu.make_async_copy(tok.at[i], x_in.at[i], local_sem.at[0])
    own_tokens.start()
    own_cot = pltpu.make_async_copy(stage.at[i], cot_in.at[i], local_sem.at[1])
    tokens_out, cot_out = exchange(tok, x_in, 0), exchange(stage, cot_in, 1)
    result_out = exchange(stage, out, 2)
    grad_out = [copy(n1.at[rows_of(block_at(k))], ig.at[i], a2a_send.at[3, k - 1], a2a_recv.at[3, k - 1],
                     {"blk": block_at(k), "batch": b}) for k in range(1, 4)]
    own_out = pltpu.make_async_copy(stage.at[i], out.at[i], local_sem.at[2])
    own_grad = pltpu.make_async_copy(n1.at[rows_of(i)], ig.at[i], local_sem.at[3])
    n2_swap, cot_swap = pair(2, n2, n2_other), pair(3, cot_in, cot_other)
    back_swap, ahead_swap = pair(4, d6, back_in), pair(5, n2, ahead_in)
    vec_steps, gvec_steps = small_sum(vec, vin, 0), small_sum(gvec, gin, 1)

    def tokens_here():
        arrived(*exchange_landed(x_in, 0))
        own_tokens.wait()

    def cotangent_here():
        arrived(*exchange_landed(cot_in, 1))
        own_cot.wait()
        cot_swap.start()

    def swaps_here():
        w1_swap.wait()
        w2_swap.wait()

    actions = {
        TOK: lambda: started(tokens_out),
        COT: lambda: started(cot_out),
        OUT: lambda: started(result_out),
        IG: lambda: started(grad_out),
        TOK_HERE: tokens_here,
        COT_HERE: cotangent_here,
        OUT_HERE: lambda: arrived(*exchange_landed(out, 2)),
        IG_HERE: lambda: arrived(*exchange_landed(ig, 3)),
        SWAP_HERE: swaps_here,
        N2S_HERE: lambda: n2_swap.wait(),
        COTS_HERE: lambda: cot_swap.wait(),
        BACKS_HERE: lambda: back_swap.wait(),
        AHEADS_HERE: lambda: ahead_swap.wait(),
    }

    load_a.wait()
    own_attention(0)
    load_vec.wait()
    own_vectors()
    load_w1.wait()
    load_w2.wait()
    pl.semaphore_wait(barrier, len(partners))
    vec_steps[0]()
    w1_swap.start()
    w2_swap.start()
    run("own1")
    own_attention(1)
    run("ownff")
    each_core(own_expand)
    each_core(own_reduce)
    run("mask")
    masked_cotangent()
    own_cot.start()
    run("ln1")
    each_core(own_hidden_bias)

    def normalise(value):
        centered = value - jnp.mean(value, axis=-1, keepdims=True)
        scale = lax.rsqrt(jnp.mean(centered * centered, axis=-1, keepdims=True) + norm_epsilon)
        return centered * scale, scale

    def first_norm(s):
        unit, _ = normalise(x_in[s].astype(F32))
        n1[rows_of(s), :] = (unit * vec[0:1, :] + vec[1:2, :]).astype(BF16)

    loop(4, first_norm)
    run("unp0")

    lanes = lax.broadcasted_iota(jnp.int32, (96, 128), 1)

    def unpack(p, s):
        for xx in range(2):
            rows = pl.ds(pl.multiple_of((2 * s + xx) * 96, 96), 96)
            for yy in range(2):
                first, second = ua.at[p, 0, yy, xx, s], ua.at[p, 1, yy, xx, s]
                lo, hi = 384 * yy, 384 * yy + 256
                for m in range(2):
                    at[2 * p + m, rows, lo : lo + 128] = first[96 * m : 96 * m + 96, :]
                    at[2 * p + m, rows, hi : hi + 128] = second[96 * m : 96 * m + 96, :]
                rest_first = first[192:288, :].astype(F32)
                rest_second = second[192:288, :].astype(F32)
                even = jnp.where(lanes < 64, rest_first, rest_second)
                odd = pltpu.roll(jnp.where(lanes < 64, rest_second, rest_first), 64, 1)
                at[2 * p, rows, lo + 128 : lo + 256] = even.astype(BF16)
                at[2 * p + 1, rows, lo + 128 : lo + 256] = odd.astype(BF16)

    def project(m, factor, bias):
        for n in range(3):
            value = dot_nt(n1[...], at[m, 256 * n : 256 * n + 256, :]) + bias[:, 256 * n : 256 * n + 256]
            value = value.astype(BF16) * factor.astype(BF16)
            heads[m, 2 * n] = value[:, 0:128]
            heads[m, 2 * n + 1] = value[:, 128:256]

    def project_scores(m):
        first = jnp.where(m == 0, 1.0, 0.0)
        project(m, 1.0 - (1.0 - HEAD ** (-0.5)) * first, vec[2:3, :] * first)

    loop(zs, functools.partial(unpack, 0))
    run("projq")
    loop(2, project_scores)

    half_lane = lax.broadcasted_iota(jnp.int32, (512, 128), 1) // HEAD

    def half_of(value, which):
        return jnp.where(half_lane == which, value, jnp.zeros_like(value))

    def turn(value):
        return value.astype(F32).T.astype(BF16)

    def attend(p):
        queries, keys = q6[p], k6[p]
        for which in range(2):
            scores = dot_nt(half_of(keys, which), queries)
            expo = jnp.exp(scores - jnp.max(scores, axis=0, keepdims=True))
            probs = (expo * (1.0 / jnp.sum(expo, axis=0, keepdims=True))).astype(BF16)
            pt[2 * p + which] = probs

    def mix(p):
        values_t = turn(v6[p])
        mixed = [dot_nn(values_t[64 * which : 64 * which + 64, :], pt[2 * p + which]) for which in range(2)]
        o6[p] = jnp.concatenate(mixed, axis=0).T.astype(BF16)

    parts("attend", 6, attend)
    run("unp1")
    loop(zs, functools.partial(unpack, 1))
    run("projv")
    project(2, jnp.float32(1.0), vec[3:4, :])
    parts("mix", 6, mix)

    run("ao")
    for n in range(3):
        cols = slice(256 * n, 256 * n + 256)
        value = dot_nt(lane_tiles(o6), at[3, cols, :]) + vec[4:5, cols]
        for s in range(4):
            h1[128 * s : 128 * s + 128, cols] = x_in[s, :, cols].astype(F32) + value[128 * s : 128 * s + 128]

    def second_norm(s):
        unit, _ = normalise(h1[rows_of(s), :])
        n2[rows_of(s), :] = (unit * vec[5:6, :] + vec[6:7, :]).astype(BF16)

    run("ln2")
    loop(4, second_norm)
    n2_swap.start()

    def expand_block(s):
        def piece(ref):
            return jnp.concatenate([ref[96 * t : 96 * t + 96, :] for t in range(3)], axis=1)

        return jnp.concatenate(
            [jnp.concatenate([piece(uw1.at[h, yy, xx, 2 * s + zz]) for yy in range(2)], axis=1)
             for zz in range(2) for xx in range(2) for h in range(2)],
            axis=0,
        )

    def reduce_block(s):
        def piece(ref):
            return jnp.concatenate([ref[96 * t : 96 * t + 96, :] for t in range(3)], axis=1)

        return jnp.concatenate(
            [jnp.concatenate([piece(uw2.at[cc, s, xx, zz]) for cc in range(2)], axis=1)
             for zz in range(zs) for xx in range(2)],
            axis=0,
        )

    def block_rows(owner, s):
        return pl.ds(pl.multiple_of((2 * owner + s) * 512, 512), 512)

    def expand(e):
        owner, s = lax.div(e, 2), lax.rem(e, 2)
        rows = block_rows(owner, s)
        inner = dot_nt(normed[owner], expand_block(s)) + b1[pl.ds(s, 1), :]
        square = inner * inner
        tanh = jnp.tanh(GELU_SCALE * inner * (1.0 + GELU_CUBE * square))
        act[rows, :] = (0.5 * inner * (1.0 + tanh)).astype(BF16)
        slope = 0.5 * (1.0 + tanh) + 0.5 * inner * (1.0 - tanh * tanh) * (
            GELU_SCALE * (1.0 + 3.0 * GELU_CUBE * square)
        )
        gp[rows, :] = slope.astype(BF16)

    parts("exp", 4, expand)

    gvec[...] = jnp.zeros_like(gvec)

    def transpose_rows(dst, s, value):
        dst[:, 128 * s : 128 * s + 128] = turn(value)

    run("trY")
    total = jnp.zeros((1, 768), F32)
    for s in range(4):
        transpose_rows(ta, s, cot_in[s])
        total = total + jnp.sum(cot_in[s].astype(F32), axis=0, keepdims=True)
    gvec[7:8, :] = total
    for s in range(4):
        transpose_rows(tb, s, cot_other[s])

    def both_rows(ref, s):
        return jnp.concatenate([ref[block_rows(0, s), :], ref[block_rows(1, s), :]], axis=0)

    def reduce_back(s):
        grad = dot_nn(jnp.concatenate([ta[...], tb[...]], axis=1), both_rows(act, s)).astype(BF16)
        for zz in range(zs):
            for xx in range(2):
                row = 96 * (2 * zz + xx)
                for cc in range(2):
                    for t in range(3):
                        col = 384 * cc + 128 * t
                        gw2[cc, s, xx, zz, 96 * t : 96 * t + 96, :] = grad[row : row + 96, col : col + 128]

    parts("gw2_", 2, reduce_back)

    def rows_together(ref):
        return jnp.concatenate([ref[s] for s in range(4)], axis=0)

    def inner_back(e):
        owner, s = 1 - lax.div(e, 2), lax.rem(e, 2)
        rows = block_rows(owner, s)
        grad = dot_nn(rows_together(cots.at[owner]), reduce_block(s)) * gp[rows, :].astype(F32)
        low = grad.astype(BF16)
        gp[rows, :] = low
        gb1[pl.ds(s, 1), :] += jnp.sum(low.astype(F32), axis=0, keepdims=True)

    def norm_back(e):
        owner = 1 - e
        acc[...] = dot_nn(gp[block_rows(owner, 0), :], expand_block(0))
        acc[...] += dot_nn(gp[block_rows(owner, 1), :], expand_block(1))

        @pl.when(e == 0)
        def _():
            for t in range(6):
                d6[t] = acc[:, 128 * t : 128 * t + 128].astype(BF16)
            back_swap.start()

    gb1[...] = jnp.zeros_like(gb1)
    parts("inn", 4, inner_back)
    each_core(hidden_bias_gradient)
    parts("dnb", 2, norm_back)

    def expand_back(s):
        turned = jnp.concatenate([turn(gp[block_rows(owner, s), :]) for owner in range(2)], axis=1)
        normed = jnp.concatenate([n2[...], n2_other[...]], axis=0)
        grad = dot_nn(turned, normed).astype(BF16)
        for zz in range(2):
            for xx in range(2):
                for h in range(2):
                    row = 384 * zz + 192 * xx + 96 * h
                    for yy in range(2):
                        for t in range(3):
                            col = 384 * yy + 128 * t
                            gw1[h, yy, xx, 2 * s + zz, 96 * t : 96 * t + 96, :] = grad[
                                row : row + 96, col : col + 128
                            ]

    parts("gw1_", 2, expand_back)
    run("hid")

    def norm_gradient(value, scale_row, grad):
        unit, scale = normalise(value)
        gain_sum = jnp.sum(grad * unit, axis=0, keepdims=True)
        bias_sum = jnp.sum(grad, axis=0, keepdims=True)
        inner = grad * scale_row
        mean = jnp.mean(inner, axis=-1, keepdims=True)
        along = jnp.mean(inner * unit, axis=-1, keepdims=True)
        return scale * (inner - mean - unit * along), gain_sum, bias_sum

    def hidden_back(s):
        rows = rows_of(s)
        grad_in = jnp.concatenate([back_in[t, rows, :] for t in range(6)], axis=1)
        grad_in = acc[rows, :] + grad_in.astype(F32)
        grad, gain_sum, bias_sum = norm_gradient(h1[rows, :], vec[5:6, :], grad_in)
        grad = grad + cot_in[s].astype(F32)
        acc[rows, :] = grad
        low = grad.astype(BF16)
        n2[rows, :] = low
        gvec[5:6, :] += gain_sum
        gvec[6:7, :] += bias_sum
        gvec[4:5, :] += jnp.sum(low.astype(F32), axis=0, keepdims=True)

    loop(4, hidden_back)

    run("dO")
    for n in range(3):
        value = dot_nn(n2[...], at[3, :, 256 * n : 256 * n + 256]).astype(BF16)
        d6[2 * n] = value[:, 0:128]
        d6[2 * n + 1] = value[:, 128:256]
    run("gao")
    for s in range(4):
        transpose_rows(tc, s, n2[128 * s : 128 * s + 128, :])
    gp[768:1536, :] = dot_nn(tc[...], lane_tiles(o6)).astype(BF16)

    def value_back(p):
        grads_in, grad_value = d6[p], 0.0
        for which in range(2):
            grad_value = grad_value + dot_nn(pt[2 * p + which], half_of(grads_in, which))
        tc[rows_of(p), :] = grad_value.T.astype(BF16)
        o6[p] = grad_value.astype(BF16)

    def attend_back(p):
        rows = rows_of(p)
        queries, keys, values, grads_in = q6[p], k6[p], v6[p], d6[p]
        keys_t = turn(keys)
        grad_query, grad_key = [], 0.0
        for which in range(2):
            wide = pt[2 * p + which].astype(F32)
            grad_probs = dot_nt(half_of(values, which), grads_in)
            inner = jnp.sum(wide * grad_probs, axis=0, keepdims=True)
            grad_scores = (wide * (grad_probs - inner)).astype(BF16)
            grad_query.append(dot_nn(keys_t[64 * which : 64 * which + 64, :], grad_scores))
            grad_key = grad_key + dot_nn(grad_scores, half_of(queries, which))
        grad_query = jnp.concatenate(grad_query, axis=0) * HEAD ** (-0.5)
        ta[rows, :] = grad_query.astype(BF16)
        tb[rows, :] = grad_key.T.astype(BF16)
        q6[p] = grad_query.T.astype(BF16)
        k6[p] = grad_key.astype(BF16)

    def pack(p, first_row, second_row):
        def body(s):
            for xx in range(2):
                offset = (2 * s + xx) * 96
                rows = [pl.ds(pl.multiple_of(first_row + offset, 96), 96),
                        pl.ds(pl.multiple_of(second_row + offset, 96), 96)]
                first, second = ua.at[p, 0, :, xx, s], ua.at[p, 1, :, xx, s]
                for yy in range(2):
                    lo, mid, hi = 384 * yy, 384 * yy + 128, 384 * yy + 256
                    for m in range(2):
                        first[yy, 96 * m : 96 * m + 96, :] = gp[rows[m], lo : lo + 128]
                        second[yy, 96 * m : 96 * m + 96, :] = gp[rows[m], hi : hi + 128]
                    even = gp[rows[0], mid : mid + 128].astype(F32)
                    odd = pltpu.roll(gp[rows[1], mid : mid + 128].astype(F32), 64, 1)
                    first[yy, 192:288, :] = jnp.where(lanes < 64, even, odd).astype(BF16)
                    second[yy, 192:288, :] = jnp.where(lanes < 64, odd, even).astype(BF16)

        loop(zs, body)

    parts("av", 6, value_back)
    run("gav")
    for n in units[VO[0] : VO[1] + 1]:
        ag_drain(n)
    gp[0:768, :] = dot_nn(tc[...], n1[...]).astype(BF16)
    pack(1, 0, 768)
    for n in grads[AVO[0] : AVO[1] + 1]:
        rs_start(n)
    parts("ab", 6, attend_back)
    run("gaqk")
    for n in units[QK[0] : QK[1] + 1]:
        ag_drain(n)

    def score_weights(m):
        gp[pl.ds(pl.multiple_of(768 * m, 256), 768), :] = dot_nn(turned[m], n1[...]).astype(BF16)

    loop(2, score_weights)
    pack(0, 0, 768)
    for n in grads[AQK[0] : AQK[1] + 1]:
        rs_start(n)

    def reduce(e):
        owner = 1 - e
        value = dot_nt(act[block_rows(owner, 0), :], reduce_block(0))
        value = value + dot_nt(act[block_rows(owner, 1), :], reduce_block(1))

        @pl.when(e == 0)
        def _():
            n2[...] = value.astype(BF16)
            ahead_swap.start()

        @pl.when(e == 1)
        def _():
            h1[...] = h1[...] + vec[7:8, :] + value

    def layer_output():
        parts("red", 2, reduce)
        run("outst")
        for moved in cot_out:
            moved.wait_send()
        for s in range(4):
            rows = slice(128 * s, 128 * s + 128)
            stage[s] = (h1[rows, :] + ahead_in[rows, :].astype(F32)).astype(BF16)
        own_out.start()

    layer_output()
    run("dn1")
    h1[...] = jnp.zeros_like(h1)

    def project_back(m):
        h1[...] += dot_nn(lane_tiles(heads.at[m + lax.div(m, 2)]), at[m])

    loop(3, project_back)
    gvec[2:3, :] = jnp.sum(lane_tiles(q6).astype(F32), axis=0, keepdims=True)
    gvec[3:4, :] = jnp.sum(lane_tiles(o6).astype(F32), axis=0, keepdims=True)

    run("inb")

    def input_back(s):
        rows = rows_of(s)
        grad, gain_sum, bias_sum = norm_gradient(x_in[s].astype(F32), vec[0:1, :], h1[rows, :])
        n1[rows, :] = (grad + acc[rows, :]).astype(BF16)
        gvec[0:1, :] += gain_sum
        gvec[1:2, :] += bias_sum

    loop(4, input_back)
    gvec_steps[0]()
    own_grad.start()
    run("end")
    finish_vectors()
    w1_back.wait()
    each_core(join_expand)
    w2_back.wait()
    each_core(join_reduce)

    own_out.wait()
    own_grad.wait()
    for moved in tokens_out + result_out + grad_out:
        moved.wait_send()
    for n in units[VO[1] + 1 :]:
        ag_drain(n)
    for n in grads:
        rs_drain(n)


def layer(sub, tokens, cotangent, span_mask, vectors, attention, expand, reduce_t):
    zs = GROUPS // 2
    seqs, block, width = tokens.shape
    rows = seqs * block
    columns = attention.shape[2]
    piece = (3 * columns, 128)
    vmem = lambda shape, dtype: pltpu.VMEM(shape, dtype)
    half = (2, 2, 2, zs) + piece
    scratch = [vmem(value.shape, value.dtype) for value in (span_mask, vectors, attention, expand, reduce_t)]
    scratch += [vmem((2,) + half, BF16)] + [vmem(half, BF16)] * 4
    scratch += [vmem((2, 2, 2, zs) + piece, BF16), vmem((6, 2, 2, zs) + piece, BF16)]
    scratch += [vmem(tokens.shape, BF16), vmem((2,) + tokens.shape, BF16), vmem(tokens.shape, BF16)]
    scratch += [vmem((16, width), F32)] * 2
    scratch += [vmem((zs + 2, 16, width), F32)] * 2
    scratch += [vmem((16, columns), F32)]
    tiles = vmem((width // 128, rows, 128), BF16)
    flat = vmem((rows, width), BF16)
    wide = vmem((rows, width), F32)
    scratch += [vmem((4, width, width), BF16), flat, vmem((4, width // 128, rows, 128), BF16)]
    scratch += [vmem((HEADS, rows, rows), BF16), wide, wide, vmem((2, rows, width), BF16)]
    scratch += [vmem((4 * rows, width), BF16)] * 2 + [vmem((3, width, rows), BF16), tiles]
    scratch += [vmem(expand.shape, F32), vmem(reduce_t.shape, F32)]
    scratch += [tiles, flat, vmem((columns, width // 2), F32), vmem((2, width), F32), vmem((2, width), F32)]
    scratch += [vmem((6,) + piece, F32), vmem((width // 2, 2 * columns), F32)]
    scratch += [vmem((2 * columns, 2 * columns), F32), vmem(piece, F32)]
    scratch += [pltpu.SemaphoreType.DMA((10,))]
    gathered, summed = sum(map(len, GATHER_ROUTES)), sum(map(len, SUM_ROUTES))
    scratch += [pltpu.SemaphoreType.DMA((gathered, 4 * zs))] * 2
    scratch += [pltpu.SemaphoreType.DMA((gathered,))] * 2
    scratch += [pltpu.SemaphoreType.DMA((summed, zs + 2))] * 2
    scratch += [pltpu.SemaphoreType.DMA((4, 3))] * 2
    scratch += [pltpu.SemaphoreType.DMA((2, zs + 2))] * 2
    scratch += [pltpu.SemaphoreType.DMA((8,))] * 2
    in_vmem = pl.BlockSpec(memory_space=pltpu.VMEM)
    anywhere = pl.BlockSpec(memory_space=pl.ANY)
    return pl.pallas_call(
        functools.partial(kernel, sub, zs),
        out_shape=(
            jax.ShapeDtypeStruct(tokens.shape, BF16),
            jax.ShapeDtypeStruct(tokens.shape, BF16),
            jax.ShapeDtypeStruct(attention.shape, F32),
            jax.ShapeDtypeStruct(expand.shape, F32),
            jax.ShapeDtypeStruct(reduce_t.shape, F32),
            jax.ShapeDtypeStruct(vectors.shape, F32),
        ),
        in_specs=[anywhere] * 7,
        out_specs=(anywhere, anywhere) + (in_vmem,) * 4,
        scratch_shapes=scratch,
        compiler_params=pltpu.CompilerParams(
            collective_id=0, has_side_effects=True, vmem_limit_bytes=65400 * 1024
        ),
    )(tokens, cotangent, span_mask, vectors, attention, expand, reduce_t)


def update_kernel(rates, *refs):
    count = len(rates)
    ins, (result, grad) = refs[: 4 * count], refs[4 * count : 4 * count + 2]
    outs, (result_out, grad_out) = refs[4 * count + 2 : 7 * count + 2], refs[7 * count + 2 : 7 * count + 4]
    held, (low, wide, passed) = refs[7 * count + 4 : 11 * count + 4], refs[11 * count + 4 : 11 * count + 7]
    in_sems, out_sems = refs[11 * count + 7 :]
    loads = [pltpu.make_async_copy(ins[n], held[n], in_sems.at[n]) for n in range(4 * count)]
    stores = [pltpu.make_async_copy(held[4 * n + m], outs[3 * n + m], out_sems.at[3 * n + m])
              for n in range(count) for m in range(3)]
    load_grad = pltpu.make_async_copy(grad, low, in_sems.at[4 * count])
    store_grad = pltpu.make_async_copy(wide, grad_out, out_sems.at[3 * count])
    load_result = pltpu.make_async_copy(result, passed, in_sems.at[4 * count + 1])
    store_result = pltpu.make_async_copy(passed, result_out, out_sems.at[3 * count + 1])
    load_grad.start()
    load_result.start()
    for copy in loads:
        copy.start()
    load_result.wait()
    store_result.start()
    load_grad.wait()

    def widen(s, carry):
        wide[s] = low[s].astype(F32)
        return carry

    lax.fori_loop(0, low.shape[0], widen, 0)
    store_grad.start()
    for n in range(count):
        for m in range(4):
            loads[4 * n + m].wait()
        weight, one, two, gradient = held[4 * n : 4 * n + 4]
        values = adamw(weight[...], one[...], two[...], gradient[...], rates[n])
        for ref, value in zip((weight, one, two), values):
            ref[...] = value
        for m in range(3):
            stores[3 * n + m].start()
    for copy in stores + [store_grad, store_result]:
        copy.wait()


def update(rates, arrays, result, grad):
    flat = [value for group in arrays for value in group]
    new = [jax.ShapeDtypeStruct(value.shape, F32) for group in arrays for value in group[:3]]
    new += [jax.ShapeDtypeStruct(result.shape, BF16), jax.ShapeDtypeStruct(grad.shape, F32)]
    anywhere = pl.BlockSpec(memory_space=pl.ANY)
    scratch = [pltpu.VMEM(value.shape, F32) for value in flat]
    scratch += [pltpu.VMEM(grad.shape, BF16), pltpu.VMEM(grad.shape, F32), pltpu.VMEM(result.shape, BF16)]
    scratch += [pltpu.SemaphoreType.DMA((len(flat) + 2,)), pltpu.SemaphoreType.DMA((len(new),))]
    return pl.pallas_call(
        functools.partial(update_kernel, rates),
        out_shape=tuple(new),
        in_specs=[anywhere] * (len(flat) + 2),
        out_specs=(anywhere,) * len(new),
        scratch_shapes=scratch,
        compiler_params=pltpu.CompilerParams(vmem_limit_bytes=63 * 1024 * 1024),
    )(*flat, result, grad)


def local(
    sub,
    tokens,
    cotangent,
    span_mask,
    attention_weight,
    expand_weight,
    reduce_weight,
    vectors,
    attention_first,
    attention_second,
    expand_first,
    expand_second,
    reduce_first,
    reduce_second,
    vector_first,
    vector_second,
):
    together = [[n * sub + m for m in range(sub)] for n in range(GROUPS)]

    def widen(value, axis):
        if sub == 1:
            return value
        low = lax.all_gather(
            value.astype(BF16), "batch", axis=axis, tiled=True, axis_index_groups=together
        )
        return low.astype(F32)

    def narrow(value, axis):
        if sub == 1:
            return value
        return lax.psum_scatter(
            value, "batch", scatter_dimension=axis, tiled=True, axis_index_groups=together
        )

    out_tokens, input_grad, ga, g1, g2, gv = layer(
        sub,
        tokens,
        cotangent,
        span_mask,
        widen(vectors, 1),
        widen(attention_weight, 2),
        widen(expand_weight, 1),
        widen(reduce_weight.T, 0),
    )
    arrays = (
        (attention_weight, attention_first, attention_second, narrow(ga, 2)),
        (expand_weight, expand_first, expand_second, narrow(g1, 1)),
        (reduce_weight.T, reduce_first.T, reduce_second.T, narrow(g2, 0)),
        (vectors, vector_first, vector_second, narrow(gv, 1)),
    )
    rates = (rate_attention, rate_expand, rate_reduce, rate_vector)
    new = update(rates, arrays, out_tokens, input_grad)
    return new[-2:] + new[0:6] + tuple(value.T for value in new[6:9]) + new[9:12]


def solution(mesh):
    sub = mesh.shape["batch"] // GROUPS
    sequences = P("batch", "blk", None)
    attention = P(None, "blk", "batch")
    matrix = P("blk", "batch")
    return jax.shard_map(
        functools.partial(local, sub),
        mesh=mesh,
        in_specs=(sequences, sequences, P("batch", "blk"), attention, matrix, matrix, matrix)
        + (attention,) * 2
        + (matrix,) * 6,
        out_specs=(sequences,) * 2 + (attention,) * 3 + (matrix,) * 9,
        check_vma=False,
    )
```

```python
import functools
import math

import jax
import jax.numpy as jnp
from jax import lax
from jax.experimental import pallas as pl
from jax.experimental.pallas import tpu as pltpu
from jax.sharding import PartitionSpec as P

HEADS = 12
HEAD = 64
STEP = 10
GROUPS = 8

norm_epsilon = 1e-05
beta_one = 0.9
beta_two = 0.999
adam_epsilon = 1e-08
decay_weight = 0.1
rate_attention = 0.05
rate_expand = 0.03
rate_reduce = 0.015
rate_vector = 0.4

F32 = jnp.float32
BF16 = jnp.bfloat16
MESH = pl.DeviceIdType.MESH
GELU_SCALE = math.sqrt(2.0 / math.pi)
GELU_CUBE = 0.044715


def adamw(weight, moment_one, moment_two, gradient, step_rate):
    moment_one = beta_one * moment_one + (1.0 - beta_one) * gradient
    moment_two = beta_two * moment_two + (1.0 - beta_two) * gradient * gradient
    corrected_one = moment_one / (1.0 - beta_one**STEP)
    corrected_two = moment_two / (1.0 - beta_two**STEP)
    updated = weight - step_rate * (
        corrected_one / (jnp.sqrt(corrected_two) + adam_epsilon) + decay_weight * weight
    )
    return (updated, moment_one, moment_two)


def dot_nn(left, right):
    return lax.dot_general(left, right, (((1,), (0,)), ((), ())), preferred_element_type=F32)


def dot_nt(left, right):
    return lax.dot_general(left, right, (((1,), (1,)), ((), ())), preferred_element_type=F32)


X, Y, Z = 1, 2, 4
(N_QKA, N_QKB, N_VOA, N_VOB, N_W10A, N_W10B, N_W11A, N_W11B, N_W20A, N_W20B, N_W21A, N_W21B) = range(12)
(N_AQKA, N_AQKB, N_AVO, N_G10, N_G11A, N_G11B, N_G20, N_G21) = range(8)
QK, VO = (N_QKA, N_QKB), (N_VOA, N_VOB)
AQK, AVO = (N_AQKA, N_AQKB), (N_AVO, N_AVO)
SEND, GOT, WHOLE, SUM, VEC, SMALL, DO = range(7)
(TOK, COT, OUT, IG, TOK_HERE, COT_HERE, OUT_HERE,
 IG_HERE, SWAP_HERE, N2S_HERE, COTS_HERE, BACKS_HERE, AHEADS_HERE) = range(13)
GATHER_ROUTES = (
    ((Z, Y, X), (Z, Y, X),),
    ((Z, Y, X), (Z, Y, X),),
    ((Y, Z, X), (X, Z, Y),),
    ((Z, X, Y), (Y, Z, X),),
    ((X, Z, Y), (Z, X, Y),),
    ((Y, Z, X), (Z, Y, X),),
)
SUM_ROUTES = (
    ((Y, X, Z), (X, Z, Y),),
    ((Y, X, Z),),
    ((Y, X, Z),),
    ((X, Z, Y), (X, Z, Y),),
    ((Y, X, Z),),
    ((Z, X, Y),),
)
PLAN = dict(
    own1=(
        (SEND, N_QKA, 0, Z), (SEND, N_QKB, 0, Z),
    ),
    ownff=(
        (DO, TOK), (SEND, N_VOA, 0, Z), (VEC, 0), (DO, SWAP_HERE),
    ),
    mask=(
        (SEND, N_W10B, 0, X), (SEND, N_W20A, 0, X),
    ),
    ln1=(
        (VEC, 1), (GOT, N_QKA, Z), (SEND, N_QKA, Z, X), (SEND, N_QKA, Z, Y), (SEND, N_VOB, 0, Z),
        (GOT, N_W10B, X), (GOT, N_W20A, X), (GOT, N_QKB, Z), (SEND, N_QKB, Z, X), (SEND, N_QKB, Z, Y),
        (SEND, N_W11A, 0, Z), (GOT, N_QKA, Z | X), (DO, TOK_HERE), (GOT, N_VOA, Z), (SEND, N_VOA, Z, X),
        (SEND, N_VOA, Z, Y), (SEND, N_W11B, 0, Z), (GOT, N_QKB, Z | X), (GOT, N_QKA, Z | Y),
        (SEND, N_QKA, Z | Y, X), (VEC, 2), (GOT, N_VOB, Z), (SEND, N_VOB, Z, Y), (SEND, N_W10A, 0, Z),
        (GOT, N_QKB, Z | Y), (SEND, N_QKB, Z | Y, X), (GOT, N_VOA, Z | X), (SEND, N_W11B, 0, Y),
        (GOT, N_W11A, Z), (SEND, N_VOB, Z, X), (SEND, N_W10A, 0, Y), (VEC, 3),
    ),
    unp0=(
        (SEND, N_W10B, 0, Z), (SEND, N_W11A, Z, Y), (GOT, N_VOA, Z | Y), (GOT, N_QKA, Z | Y | X),
        (SEND, N_VOA, Z | Y, X), (GOT, N_W11B, Z), (SEND, N_W10B, X, Z), (DO, COT), (GOT, N_VOB, Z | Y),
        (GOT, N_QKB, Z | Y | X), (SEND, N_VOB, Z | Y, X), (GOT, N_W11B, Y), (GOT, N_W10A, Z),
        (GOT, N_W10A, Y), (SEND, N_W11B, Y, Z), (WHOLE, N_QKA), (WHOLE, N_QKB),
    ),
    projq=(
        (GOT, N_VOB, Z | X),
    ),
    attend0=(
        (SEND, N_W11A, Z, X), (GOT, N_W10B, Z), (GOT, N_W11A, Z | Y), (SEND, N_W10A, Y, Z),
    ),
    attend1=(
        (GOT, N_VOA, Z | Y | X), (SEND, N_W11B, Z, X),
    ),
    attend2=(
        (SEND, N_W10B, Z, Y), (GOT, N_W10B, X | Z), (SEND, N_W21B, 0, Z),
    ),
    attend3=(
        (GOT, N_VOB, Z | Y | X),
    ),
    attend4=(
        (SEND, N_W10A, Z, X), (SEND, N_W10B, X | Z, Y), (GOT, N_W11B, Y | Z),
    ),
    attend5=(
        (SEND, N_W20B, 0, Z), (WHOLE, N_VOA), (WHOLE, N_VOB),
    ),
    unp1=(
        (GOT, N_W11A, Z | X), (SEND, N_W11B, Y | Z, X), (DO, COT_HERE), (SEND, N_W11A, Z | X, Y),
    ),
    projv=(
        (GOT, N_W10A, Y | Z), (SEND, N_W21A, 0, Z),
    ),
    mix1=(
        (GOT, N_W11B, Z | X),
    ),
    mix3=(
        (SEND, N_W10A, Y | Z, X), (GOT, N_W10B, Z | Y),
    ),
    mix4=(
        (DO, COTS_HERE), (SEND, N_W21A, 0, Y),
    ),
    ao=(
        (GOT, N_W21B, Z),
    ),
    ln2=(
        (SEND, N_W21B, Z, Y), (SEND, N_W20A, 0, Z),
    ),
    exp0=(
        (GOT, N_W10A, Z | X), (GOT, N_W10B, X | Z | Y), (GOT, N_W20B, Z), (SEND, N_W20B, Z, X),
        (SEND, N_W20B, Z, Y), (SEND, N_W20A, X, Z), (GOT, N_W11B, Y | Z | X), (SEND, N_W21B, Z, X),
        (GOT, N_W11A, Z | X | Y), (DO, N2S_HERE), (GOT, N_W21A, Y), (GOT, N_W21A, Z), (SEND, N_W21A, Y, Z),
        (GOT, N_W10A, Y | Z | X),
    ),
    exp1=(
        (SEND, N_W21A, Z, X), (GOT, N_W21B, Z | Y), (GOT, N_W20A, Z), (SEND, N_W20A, Z, Y),
    ),
    exp2=(
        (GOT, N_W20B, Z | X), (SEND, N_W20B, Z | X, Y), (SEND, N_W21B, Z | Y, X), (GOT, N_W20B, Z | Y),
        (GOT, N_W20A, X | Z), (SEND, N_W20A, X | Z, Y),
    ),
    exp3=(
        (GOT, N_W21B, Z | X),
    ),
    trY=(
        (GOT, N_W20A, Z | Y), (GOT, N_W21A, Y | Z), (SEND, N_W21A, Y | Z, X), (GOT, N_W21A, Z | X),
    ),
    gw2_0=(
        (GOT, N_W20B, Z | X | Y),
    ),
    gw2_1=(
        (GOT, N_W21B, Z | Y | X),
    ),
    inn0=(
        (GOT, N_W20A, X | Z | Y), (SUM, N_G20, 0), (SUM, N_G21, 0), (GOT, N_W21A, Y | Z | X),
    ),
    gw1_1=(
        (DO, BACKS_HERE),
    ),
    hid=(
        (SUM, N_G10, 0), (SUM, N_G11A, 0), (SUM, N_G11B, 0), (SUM, N_G20, 1),
    ),
    av5=(
        (SUM, N_G11A, 1),
    ),
    ab2=(
        (SUM, N_G21, 1), (SUM, N_AVO, 0),
    ),
    ab3=(
        (SUM, N_G11B, 1), (SUM, N_G10, 1),
    ),
    ab5=(
        (SUM, N_G11A, 2),
    ),
    gaqk=(
        (SUM, N_G20, 2),
    ),
    red1=(
        (SUM, N_G11B, 2),
    ),
    outst=(
        (SUM, N_G10, 2), (SUM, N_AQKB, 0), (SUM, N_AQKA, 0), (SUM, N_AVO, 1), (SUM, N_G11A, 3),
        (DO, AHEADS_HERE),
    ),
    dn1=(
        (SUM, N_G21, 2), (SUM, N_G11B, 3),
    ),
    inb=(
        (DO, OUT), (SUM, N_G20, 3),
    ),
    end=(
        (SUM, N_AQKB, 1), (SUM, N_AQKA, 1), (SUM, N_G10, 3), (DO, IG), (SUM, N_AVO, 2), (SUM, N_AQKB, 2),
        (DO, OUT_HERE), (SUM, N_AQKA, 2), (SUM, N_AVO, 3), (DO, IG_HERE), (SMALL, 0), (SUM, N_AQKA, 3),
        (SUM, N_G21, 3), (SMALL, 1), (SUM, N_AQKB, 3), (SMALL, 2), (SMALL, 3),
    ),
)


def lane_tiles(ref, count=6):
    return jnp.concatenate([ref[t] for t in range(count)], axis=1)


class Unit:
    def __init__(self, index, route, rows, u, other):
        self.index, self.route, self.rows, self.u, self.other = index, route, rows, u, other


class Gradient:
    def __init__(self, index, route, rows, u, other, core_in, got, total):
        self.index, self.route, self.rows, self.u, self.other = index, route, rows, u, other
        self.core_in, self.got, self.total = core_in, got, total


def kernel(sub, zs, *refs):
    (tok, cot, mask_hbm, vec_hbm, a_hbm, w1_hbm, w2_hbm,
     out, ig, ga, g1, g2, gv,
     mask_in, vec_in, a_in, w1_in, w2_in, ua, uw1, uw2, gw1, gw2, core_in, got,
     x_in, cots, stage, vec, gvec, vin, gin, narrow_rows,
     at, n1, heads, pt, h1, acc, normed, act, gp, turned, d6,
     w1_other, w2_other, back_in, ahead_in,
     lines, b1, gb1, totals, turned1, got1, got2,
     local_sem, ag_send, ag_recv, core_send, core_recv, rs_send, rs_recv,
     a2a_send, a2a_recv, v_send, v_recv, pair_send, pair_recv) = refs

    q6, k6, v6, o6 = (heads.at[m] for m in range(4))
    ta, tb, tc = (turned.at[m] for m in range(3))
    n2, n2_other, cot_in, cot_other = normed.at[0], normed.at[1], cots.at[0], cots.at[1]
    i = lax.axis_index("blk")
    b = lax.axis_index("batch")
    c, y = lax.rem(i, 2), lax.div(i, 2)
    g, r = lax.div(b, sub), lax.rem(b, sub)
    x, z = lax.rem(g, 2), lax.div(g, 2)

    def device(c_=c, y_=y, x_=x, z_=z):
        return {"blk": 2 * y_ + c_, "batch": (2 * z_ + x_) * sub + r}

    def z_at(k):
        return lax.rem(z + k, zs)

    def block_at(k):
        return lax.rem(i + k, 4)

    def copy(src, dst, send, recv, to):
        return pltpu.make_async_remote_copy(
            src_ref=src, dst_ref=dst, send_sem=send, recv_sem=recv, device_id=to, device_id_type=MESH
        )

    def loop(count, body, hooks=()):
        def step(s, carry):
            body(s)
            for k, f in hooks:
                pl.when(s == k)(f)
            return carry

        lax.fori_loop(0, count, step, 0)

    partners = [device(z_=z_at(k)) for k in range(1, zs)]
    partners += [device(x_=1 - x), device(y_=1 - y), device(c_=1 - c), device(c_=1 - c, y_=1 - y)]
    barrier = pltpu.get_barrier_semaphore()
    for partner in partners:
        pl.semaphore_signal(barrier, inc=1, device_id=partner, device_id_type=MESH)

    ME = {"y": y, "x": x, "z": z}

    def before(n, axis, other):
        return n.route.index(axis) < n.route.index(other)

    def side(n, axes, all_z):
        where = (1 - y if "y" in axes else y, 1 - x if "x" in axes else x, slice(None) if all_z else z)
        return n.u.at[where + (n.rows,)]

    def neighbour(axis):
        return device(y_=1 - y) if axis == "y" else device(x_=1 - x)

    def ag_copy(n, ref, axes, k, to):
        slot = (("y" in axes) * 2 + ("x" in axes)) * zs + k
        return copy(ref, ref, ag_send.at[n.index, slot], ag_recv.at[n.index, slot], to)

    def core_copy(n, ref):
        return copy(ref, ref, core_send.at[n.index], core_recv.at[n.index], device(c_=1 - c))

    def ag_sends(n, axes, axis):
        axes = axes.replace("z", "")
        if axis == "z":
            ref = side(n, axes, False)
            return [ag_copy(n, ref, axes, k, device(z_=z_at(k))) for k in range(1, zs)]
        ref = side(n, axes, before(n, "z", axis))
        return [ag_copy(n, ref, axes + axis, 0, neighbour(axis))]

    def ag_send_part(n, axes, axis):
        for moved in ag_sends(n, axes, axis):
            moved.start()

    def ag_wait_part(n, axes):
        last = max(axes, key=n.route.index)
        axes = axes.replace("z", "")
        if last == "z":
            yy, xx = (1 - y if "y" in axes else y), (1 - x if "x" in axes else x)
            for k in range(1, zs):
                ag_copy(n, n.u.at[yy, xx, z_at(zs - k), n.rows], axes, k, device()).wait_recv()
        else:
            ag_copy(n, side(n, axes, before(n, "z", last)), axes, 0, device()).wait_recv()
        if n.other is not None and (last == "z" or before(n, "z", last)):
            core_copy(n, side(n, axes, True)).start()

    def ag_done(n):
        if n.other is not None:
            core_copy(n, n.other.at[:, :, :, n.rows]).wait_recv()

    def ag_drain(n):
        for axis in n.route:
            earlier = [other for other in "yx" if before(n, other, axis)]
            for some in range(2 ** len(earlier)):
                axes = "".join(other for bit, other in enumerate(earlier) if some >> bit & 1)
                for moved in ag_sends(n, axes, axis):
                    moved.wait_send()
        if n.other is not None:
            core_copy(n, n.u.at[:, :, :, n.rows]).wait_send()

    AXES = "yxz"

    def rs_groups(n, step):
        axis = n.route[step]
        if axis == "z":
            return [(k, 1 + k, device(z_=z_at(zs - k))) for k in range(1, zs)]
        return [(1, "yx".index(axis), neighbour(axis))]

    def rs_where(n, step, k):
        axis, out, land = n.route[step], [], []
        for other in AXES:
            if other == axis:
                out.append(z_at(zs - k) if axis == "z" else 1 - ME[axis])
                land.append(k)
            elif before(n, other, axis):
                out.append(ME[other])
                land.append(0)
            else:
                out.append(slice(None))
                land.append(slice(None))
        return tuple(out) + (n.rows,), tuple(land) + (n.rows,)

    def rs_copy(n, step, k, slot, to):
        out, land = rs_where(n, step, k)
        return copy(n.u.at[out], n.got.at[land], rs_send.at[n.index, slot], rs_recv.at[n.index, slot], to)

    def rs_core(n):
        return copy(n.other.at[:, :, :, n.rows], n.core_in.at[:, :, :, n.rows], rs_send.at[n.index, zs + 1],
                    rs_recv.at[n.index, zs + 1], device(c_=1 - c))

    def add_terms(n, place, step):
        value = n.u[tuple(place) + (n.rows,)].astype(F32)
        if n.other is not None:
            value = value + n.core_in[tuple(place) + (n.rows,)].astype(F32)
        for axis in n.route[:step]:
            for k in range(1, zs) if axis == "z" else (1,):
                where = [k if other == axis else (0 if before(n, other, axis) else at_place)
                         for other, at_place in zip(AXES, place)]
                value = value + n.got[tuple(where) + (n.rows,)].astype(F32)
        return value

    def rs_start(n):
        rs_core(n).start()

    def rs_step(n, step):
        if step == 0 and n.other is not None:
            rs_core(n).wait_recv()
        if step > 0:
            for group in rs_groups(n, step - 1):
                rs_copy(n, step - 1, *group).wait_recv()
        if step == 3:
            n.total[n.rows, :] = add_terms(n, (y, x, z), 3)
            return
        for k, slot, to in rs_groups(n, step):
            out, _ = rs_where(n, step, k)
            if step > 0 or n.other is not None:
                spans = [range(2) if isinstance(at_place, slice) else (at_place,) for at_place in out[:2]]

                def body(zz):
                    for yy in spans[0]:
                        for xx in spans[1]:
                            n.u[yy, xx, zz, n.rows] = add_terms(n, (yy, xx, zz), step).astype(BF16)

                if isinstance(out[2], slice):
                    loop(zs, body)
                else:
                    body(out[2])
            rs_copy(n, step, k, slot, to).start()

    def rs_drain(n):
        if n.other is not None:
            rs_core(n).wait_send()
        for step in range(3):
            for group in rs_groups(n, step):
                rs_copy(n, step, *group).wait_send()

    def small_sum(ref, slots, which):
        to = (device(y_=1 - y), device(c_=1 - c), device(x_=1 - x))
        to += tuple(device(z_=z_at(k)) for k in range(1, zs))

        def moved(slot):
            return copy(ref, slots.at[slot], v_send.at[which, slot], v_recv.at[which, slot], to[slot])

        def land(last):
            moved(last).wait()
            ref[...] = ref[...] + slots[last]

        def step(n):
            def run():
                if n > 0:
                    land(n - 1)
                moved(n).start()

            return run

        def line():
            land(2)
            for k in range(1, zs):
                moved(2 + k).start()

        def finish():
            for k in range(1, zs):
                moved(2 + k).wait()
            value = ref[...]
            for k in range(1, zs):
                value = value + slots[2 + k]
            ref[...] = value

        return [step(0), step(1), step(2), line, finish]

    def rows_of(s):
        return pl.ds(pl.multiple_of(s * 128, 128), 128)

    def exchange(src, dst, which):
        return [copy(src.at[block_at(k)], dst.at[i], a2a_send.at[which, k - 1],
                     a2a_recv.at[which, k - 1], {"blk": block_at(k), "batch": b})
                for k in range(1, 4)]

    def exchange_landed(dst, which):
        return [copy(dst.at[block_at(4 - k)], dst.at[block_at(4 - k)], a2a_send.at[which, k - 1],
                     a2a_recv.at[which, k - 1], {"blk": block_at(4 - k), "batch": b})
                for k in range(1, 4)]

    def axes_of(mask):
        return "".join(axis for axis, bit in (("y", Y), ("x", X), ("z", Z)) if mask & bit)

    def rows_in(part, count):
        return pl.ds(part * (288 // count), 288 // count)

    units = []
    for unit, routes in enumerate(GATHER_ROUTES):
        half = unit % 2
        ref = (ua, uw1, uw2)[unit // 2]
        pieces = (ref.at[half, c], ref.at[half, 1 - c]) if unit < 2 else (ref.at[half], None)
        for part, route in enumerate(routes):
            units.append(Unit(len(units), "".join(map(axes_of, route)), rows_in(part, len(routes)), *pieces))

    def pair(slot, src, dst):
        return copy(src, dst, pair_send.at[slot], pair_recv.at[slot], device(c_=1 - c))

    w1_swap, w2_swap = pair(0, w1_in, w1_other), pair(1, w2_in, w2_other)

    def each_core(f):
        for q in range(2):
            pl.when(c == q)(functools.partial(f, q))

    def rest_rows(matrix):
        return a_in[matrix, pl.ds(pl.multiple_of(128 * (1 - c), 64), 64), :]

    def own_attention(p):
        mine = ua.at[p, c, y, x, z]
        for m in range(2):
            main = a_in[2 * p + m, pl.ds(pl.multiple_of(64 * c, 64), 128), :]
            mine[96 * m : 96 * m + 96, :] = main.T.astype(BF16)
        rest = jnp.concatenate([rest_rows(2 * p + c), rest_rows(2 * p + 1 - c)], axis=0)
        mine[192:288, :] = rest.T.astype(BF16)

    def own_expand(q):
        both = (w1_in, w1_other) if q == 0 else (w1_other, w1_in)
        cols = slice(192 * q, 192 * q + 192)
        blocks = (
            both[0][0:128, cols],
            jnp.concatenate([both[0][128:192, cols], both[1][0:64, cols]], axis=0),
            both[1][64:192, cols],
        )
        for t, block in enumerate(blocks):
            value = block.T.astype(BF16)
            for h in range(2):
                uw1[h, y, x, z, 96 * t : 96 * t + 96, :] = value[96 * h : 96 * h + 96, :]

    def own_reduce(q):
        both = (w2_in, w2_other) if q == 0 else (w2_other, w2_in)
        for cc in range(2):
            for part_of in range(2):
                start = 384 * part_of + 192 * q
                lines[:, 192 * part_of : 192 * part_of + 192] = both[cc][:, start : start + 192]
            for t in range(3):
                uw2[cc, y, x, z, 96 * t : 96 * t + 96, :] = lines[:, 128 * t : 128 * t + 128].astype(BF16)

    def own_hidden_bias(q):
        for zz in range(zs):
            for xx in range(2):
                col = 384 * (zz % 2) + 192 * xx
                start = 384 * xx + 192 * q
                b1[zz // 2 : zz // 2 + 1, col : col + 192] = vec[8 + zz : 9 + zz, start : start + 192]

    def hidden_bias_gradient(q):
        for zz in range(zs):
            for xx in range(2):
                col = 384 * (zz % 2) + 192 * xx
                start = 384 * xx + 192 * q
                gvec[8 + zz : 9 + zz, start : start + 192] = gb1[zz // 2 : zz // 2 + 1, col : col + 192]

    columns = a_in.shape[2]
    placed = lax.broadcasted_iota(jnp.int32, (columns, 768), 1) == (
        lax.broadcasted_iota(jnp.int32, (columns, 768), 0) + columns * g
    )

    def own_vectors():
        vec[...] = jnp.zeros_like(vec)
        rows = dot_nn(vec_in[...].astype(BF16), jnp.where(placed, 1.0, 0.0).astype(BF16))
        for j in range(3):
            vec[pl.ds(3 * i + j, 1), :] = rows[j : j + 1, :]

    loads = [pltpu.make_async_copy(src, dst, local_sem.at[4 + n]) for n, (src, dst) in enumerate((
        (a_hbm, a_in), (vec_hbm, vec_in), (w1_hbm, w1_in), (w2_hbm, w2_in), (cot, stage), (mask_hbm, mask_in)
    ))]
    load_a, load_vec, load_w1, load_w2, load_cot, load_mask = loads
    for load in loads:
        load.start()

    def masked_cotangent():
        load_cot.wait()
        load_mask.wait()
        eye = lax.broadcasted_iota(jnp.int32, (128, 128), 0) == lax.broadcasted_iota(jnp.int32, (128, 128), 1)
        for s in range(4):
            row = jnp.broadcast_to(mask_in[s : s + 1, :].astype(F32), (128, 128))
            column = jnp.sum(jnp.where(eye, row, 0.0), axis=1, keepdims=True)
            stage[s] = (stage[s].astype(F32) * column).astype(BF16)

    def finish_attention(p):
        value = totals.at[p]
        for m in range(2):
            ga[2 * p + m, pl.ds(pl.multiple_of(64 * c, 64), 128), :] = value[96 * m : 96 * m + 96, :].T
        rest = value[192:288, :].T
        rows = pl.ds(pl.multiple_of(128 * (1 - c), 64), 64)
        ga[2 * p + c, rows, :] = rest[0:64, :]
        ga[2 * p + 1 - c, rows, :] = rest[64:128, :]

    w1_back = pair(6, turned1.at[pl.ds(pl.multiple_of(192 * (1 - c), 64), 192)], got1)
    w2_back = pair(7, totals.at[5 - c], got2)

    def turn_expand():
        for h in range(2):
            for t in range(3):
                turned1[128 * t : 128 * t + 128, 96 * h : 96 * h + 96] = totals[2 + h, 96 * t : 96 * t + 96, :].T
        w1_back.start()

    def join_expand(q):
        g1[:, 192 * q : 192 * q + 192] = turned1[192 * q : 192 * q + 192, :]
        g1[:, 192 * (1 - q) : 192 * (1 - q) + 192] = got1[...]

    def join_reduce(q):
        for half, value in ((q, totals.at[4 + q]), (1 - q, got2)):
            for t in range(3):
                lines[:, 128 * t : 128 * t + 128] = value[96 * t : 96 * t + 96, :]
            for part_of in range(2):
                start = 384 * part_of + 192 * half
                g2[:, start : start + 192] = lines[:, 192 * part_of : 192 * part_of + 192]

    def finish_vectors():
        value, total = gvec[...], 0.0
        for _ in range(3):
            part = value.astype(BF16)
            total = total + dot_nt(part, jnp.where(placed, 1.0, 0.0).astype(BF16))
            value = value - part.astype(F32)
        narrow_rows[...] = total
        for j in range(3):
            gv[j : j + 1, :] = narrow_rows[pl.ds(3 * i + j, 1), :]

    grads, owners = [], []
    for unit, routes in enumerate(SUM_ROUTES):
        half = unit % 2
        ref = (ua, gw1, gw2)[unit // 2]
        pieces = (ref.at[half, c], ref.at[half, 1 - c], core_in.at[half]) if unit < 2 else (ref.at[half], None, None)
        for part, route in enumerate(routes):
            grads.append(Gradient(len(grads), "".join(map(axes_of, route)), rows_in(part, len(routes)), *pieces,
                                  got.at[unit], totals.at[unit]))
            owners.append(unit)

    def summed(unit):
        if unit < 2:
            finish_attention(unit)
        elif unit < 4 and {2, 3} <= set(whole):
            turn_expand()
        elif unit >= 4 and {4, 5} <= set(whole):
            w2_back.start()

    seen, whole = set(), []

    def event(kind, *rest):
        if kind == SEND:
            ag_send_part(units[rest[0]], axes_of(rest[1]), axes_of(rest[2]))
        elif kind == GOT:
            ag_wait_part(units[rest[0]], axes_of(rest[1]))
        elif kind == WHOLE:
            ag_done(units[rest[0]])
        elif kind == SUM:
            rs_step(grads[rest[0]], rest[1])
            if rest[1] == 3:
                seen.add(rest[0])
                unit = owners[rest[0]]
                if all(k in seen for k in range(len(grads)) if owners[k] == unit):
                    whole.append(unit)
                    summed(unit)
        elif kind == DO:
            actions[rest[0]]()
        else:
            (vec_steps if kind == VEC else gvec_steps)[rest[0] + 1]()

    def run(part):
        for todo in PLAN.get(part, ()):
            event(*todo)

    def parts(name, count, body):
        run(name + "0")
        hooks = [(k - 1, functools.partial(run, name + str(k))) for k in range(1, count) if name + str(k) in PLAN]
        loop(count, body, hooks)

    def started(copies):
        for moved in copies:
            moved.start()
        return copies

    def arrived(*copies):
        for moved in copies:
            moved.wait_recv()

    own_tokens = pltpu.make_async_copy(tok.at[i], x_in.at[i], local_sem.at[0])
    own_tokens.start()
    own_cot = pltpu.make_async_copy(stage.at[i], cot_in.at[i], local_sem.at[1])
    tokens_out, cot_out = exchange(tok, x_in, 0), exchange(stage, cot_in, 1)
    result_out = exchange(stage, out, 2)
    grad_out = [copy(n1.at[rows_of(block_at(k))], ig.at[i], a2a_send.at[3, k - 1], a2a_recv.at[3, k - 1],
                     {"blk": block_at(k), "batch": b}) for k in range(1, 4)]
    own_out = pltpu.make_async_copy(stage.at[i], out.at[i], local_sem.at[2])
    own_grad = pltpu.make_async_copy(n1.at[rows_of(i)], ig.at[i], local_sem.at[3])
    n2_swap, cot_swap = pair(2, n2, n2_other), pair(3, cot_in, cot_other)
    back_swap, ahead_swap = pair(4, d6, back_in), pair(5, n2, ahead_in)
    vec_steps, gvec_steps = small_sum(vec, vin, 0), small_sum(gvec, gin, 1)

    def tokens_here():
        arrived(*exchange_landed(x_in, 0))
        own_tokens.wait()

    def cotangent_here():
        arrived(*exchange_landed(cot_in, 1))
        own_cot.wait()
        cot_swap.start()

    def swaps_here():
        w1_swap.wait()
        w2_swap.wait()

    actions = {
        TOK: lambda: started(tokens_out),
        COT: lambda: started(cot_out),
        OUT: lambda: started(result_out),
        IG: lambda: started(grad_out),
        TOK_HERE: tokens_here,
        COT_HERE: cotangent_here,
        OUT_HERE: lambda: arrived(*exchange_landed(out, 2)),
        IG_HERE: lambda: arrived(*exchange_landed(ig, 3)),
        SWAP_HERE: swaps_here,
        N2S_HERE: lambda: n2_swap.wait(),
        COTS_HERE: lambda: cot_swap.wait(),
        BACKS_HERE: lambda: back_swap.wait(),
        AHEADS_HERE: lambda: ahead_swap.wait(),
    }

    load_a.wait()
    own_attention(0)
    load_vec.wait()
    own_vectors()
    load_w1.wait()
    load_w2.wait()
    pl.semaphore_wait(barrier, len(partners))
    vec_steps[0]()
    w1_swap.start()
    w2_swap.start()
    run("own1")
    own_attention(1)
    run("ownff")
    each_core(own_expand)
    each_core(own_reduce)
    run("mask")
    masked_cotangent()
    own_cot.start()
    run("ln1")
    each_core(own_hidden_bias)

    def normalise(value):
        centered = value - jnp.mean(value, axis=-1, keepdims=True)
        scale = lax.rsqrt(jnp.mean(centered * centered, axis=-1, keepdims=True) + norm_epsilon)
        return centered * scale, scale

    def first_norm(s):
        unit, _ = normalise(x_in[s].astype(F32))
        n1[rows_of(s), :] = (unit * vec[0:1, :] + vec[1:2, :]).astype(BF16)

    loop(4, first_norm)
    run("unp0")

    lanes = lax.broadcasted_iota(jnp.int32, (96, 128), 1)

    def unpack(p, s):
        for xx in range(2):
            rows = pl.ds(pl.multiple_of((2 * s + xx) * 96, 96), 96)
            for yy in range(2):
                first, second = ua.at[p, 0, yy, xx, s], ua.at[p, 1, yy, xx, s]
                lo, hi = 384 * yy, 384 * yy + 256
                for m in range(2):
                    at[2 * p + m, rows, lo : lo + 128] = first[96 * m : 96 * m + 96, :]
                    at[2 * p + m, rows, hi : hi + 128] = second[96 * m : 96 * m + 96, :]
                rest_first = first[192:288, :].astype(F32)
                rest_second = second[192:288, :].astype(F32)
                even = jnp.where(lanes < 64, rest_first, rest_second)
                odd = pltpu.roll(jnp.where(lanes < 64, rest_second, rest_first), 64, 1)
                at[2 * p, rows, lo + 128 : lo + 256] = even.astype(BF16)
                at[2 * p + 1, rows, lo + 128 : lo + 256] = odd.astype(BF16)

    def project(m, factor, bias):
        for n in range(3):
            value = dot_nt(n1[...], at[m, 256 * n : 256 * n + 256, :]) + bias[:, 256 * n : 256 * n + 256]
            value = value.astype(BF16) * factor.astype(BF16)
            heads[m, 2 * n] = value[:, 0:128]
            heads[m, 2 * n + 1] = value[:, 128:256]

    def project_scores(m):
        first = jnp.where(m == 0, 1.0, 0.0)
        project(m, 1.0 - (1.0 - HEAD ** (-0.5)) * first, vec[2:3, :] * first)

    loop(zs, functools.partial(unpack, 0))
    run("projq")
    loop(2, project_scores)

    half_lane = lax.broadcasted_iota(jnp.int32, (512, 128), 1) // HEAD

    def half_of(value, which):
        return jnp.where(half_lane == which, value, jnp.zeros_like(value))

    def turn(value):
        return value.astype(F32).T.astype(BF16)

    def attend(p):
        queries, keys = q6[p], k6[p]
        for which in range(2):
            scores = dot_nt(half_of(keys, which), queries)
            expo = jnp.exp(scores - jnp.max(scores, axis=0, keepdims=True))
            probs = (expo * (1.0 / jnp.sum(expo, axis=0, keepdims=True))).astype(BF16)
            pt[2 * p + which] = probs

    def mix(p):
        values_t = turn(v6[p])
        mixed = [dot_nn(values_t[64 * which : 64 * which + 64, :], pt[2 * p + which]) for which in range(2)]
        o6[p] = jnp.concatenate(mixed, axis=0).T.astype(BF16)

    parts("attend", 6, attend)
    run("unp1")
    loop(zs, functools.partial(unpack, 1))
    run("projv")
    project(2, jnp.float32(1.0), vec[3:4, :])
    parts("mix", 6, mix)

    run("ao")
    for n in range(3):
        cols = slice(256 * n, 256 * n + 256)
        value = dot_nt(lane_tiles(o6), at[3, cols, :]) + vec[4:5, cols]
        for s in range(4):
            h1[128 * s : 128 * s + 128, cols] = x_in[s, :, cols].astype(F32) + value[128 * s : 128 * s + 128]

    def second_norm(s):
        unit, _ = normalise(h1[rows_of(s), :])
        n2[rows_of(s), :] = (unit * vec[5:6, :] + vec[6:7, :]).astype(BF16)

    run("ln2")
    loop(4, second_norm)
    n2_swap.start()

    def expand_block(s):
        def piece(ref):
            return jnp.concatenate([ref[96 * t : 96 * t + 96, :] for t in range(3)], axis=1)

        return jnp.concatenate(
            [jnp.concatenate([piece(uw1.at[h, yy, xx, 2 * s + zz]) for yy in range(2)], axis=1)
             for zz in range(2) for xx in range(2) for h in range(2)],
            axis=0,
        )

    def reduce_block(s):
        def piece(ref):
            return jnp.concatenate([ref[96 * t : 96 * t + 96, :] for t in range(3)], axis=1)

        return jnp.concatenate(
            [jnp.concatenate([piece(uw2.at[cc, s, xx, zz]) for cc in range(2)], axis=1)
             for zz in range(zs) for xx in range(2)],
            axis=0,
        )

    def block_rows(owner, s):
        return pl.ds(pl.multiple_of((2 * owner + s) * 512, 512), 512)

    def expand(e):
        owner, s = lax.div(e, 2), lax.rem(e, 2)
        rows = block_rows(owner, s)
        inner = dot_nt(normed[owner], expand_block(s)) + b1[pl.ds(s, 1), :]
        square = inner * inner
        tanh = jnp.tanh(GELU_SCALE * inner * (1.0 + GELU_CUBE * square))
        act[rows, :] = (0.5 * inner * (1.0 + tanh)).astype(BF16)
        slope = 0.5 * (1.0 + tanh) + 0.5 * inner * (1.0 - tanh * tanh) * (
            GELU_SCALE * (1.0 + 3.0 * GELU_CUBE * square)
        )
        gp[rows, :] = slope.astype(BF16)

    parts("exp", 4, expand)

    gvec[...] = jnp.zeros_like(gvec)

    def transpose_rows(dst, s, value):
        dst[:, 128 * s : 128 * s + 128] = turn(value)

    run("trY")
    total = jnp.zeros((1, 768), F32)
    for s in range(4):
        transpose_rows(ta, s, cot_in[s])
        total = total + jnp.sum(cot_in[s].astype(F32), axis=0, keepdims=True)
    gvec[7:8, :] = total
    for s in range(4):
        transpose_rows(tb, s, cot_other[s])

    def both_rows(ref, s):
        return jnp.concatenate([ref[block_rows(0, s), :], ref[block_rows(1, s), :]], axis=0)

    def reduce_back(s):
        grad = dot_nn(jnp.concatenate([ta[...], tb[...]], axis=1), both_rows(act, s)).astype(BF16)
        for zz in range(zs):
            for xx in range(2):
                row = 96 * (2 * zz + xx)
                for cc in range(2):
                    for t in range(3):
                        col = 384 * cc + 128 * t
                        gw2[cc, s, xx, zz, 96 * t : 96 * t + 96, :] = grad[row : row + 96, col : col + 128]

    parts("gw2_", 2, reduce_back)

    def rows_together(ref):
        return jnp.concatenate([ref[s] for s in range(4)], axis=0)

    def inner_back(e):
        owner, s = 1 - lax.div(e, 2), lax.rem(e, 2)
        rows = block_rows(owner, s)
        grad = dot_nn(rows_together(cots.at[owner]), reduce_block(s)) * gp[rows, :].astype(F32)
        low = grad.astype(BF16)
        gp[rows, :] = low
        gb1[pl.ds(s, 1), :] += jnp.sum(low.astype(F32), axis=0, keepdims=True)

    def norm_back(e):
        owner = 1 - e
        acc[...] = dot_nn(gp[block_rows(owner, 0), :], expand_block(0))
        acc[...] += dot_nn(gp[block_rows(owner, 1), :], expand_block(1))

        @pl.when(e == 0)
        def _():
            for t in range(6):
                d6[t] = acc[:, 128 * t : 128 * t + 128].astype(BF16)
            back_swap.start()

    gb1[...] = jnp.zeros_like(gb1)
    parts("inn", 4, inner_back)
    each_core(hidden_bias_gradient)
    parts("dnb", 2, norm_back)

    def expand_back(s):
        turned = jnp.concatenate([turn(gp[block_rows(owner, s), :]) for owner in range(2)], axis=1)
        normed = jnp.concatenate([n2[...], n2_other[...]], axis=0)
        grad = dot_nn(turned, normed).astype(BF16)
        for zz in range(2):
            for xx in range(2):
                for h in range(2):
                    row = 384 * zz + 192 * xx + 96 * h
                    for yy in range(2):
                        for t in range(3):
                            col = 384 * yy + 128 * t
                            gw1[h, yy, xx, 2 * s + zz, 96 * t : 96 * t + 96, :] = grad[
                                row : row + 96, col : col + 128
                            ]

    parts("gw1_", 2, expand_back)
    run("hid")

    def norm_gradient(value, scale_row, grad):
        unit, scale = normalise(value)
        gain_sum = jnp.sum(grad * unit, axis=0, keepdims=True)
        bias_sum = jnp.sum(grad, axis=0, keepdims=True)
        inner = grad * scale_row
        mean = jnp.mean(inner, axis=-1, keepdims=True)
        along = jnp.mean(inner * unit, axis=-1, keepdims=True)
        return scale * (inner - mean - unit * along), gain_sum, bias_sum

    def hidden_back(s):
        rows = rows_of(s)
        grad_in = jnp.concatenate([back_in[t, rows, :] for t in range(6)], axis=1)
        grad_in = acc[rows, :] + grad_in.astype(F32)
        grad, gain_sum, bias_sum = norm_gradient(h1[rows, :], vec[5:6, :], grad_in)
        grad = grad + cot_in[s].astype(F32)
        acc[rows, :] = grad
        low = grad.astype(BF16)
        n2[rows, :] = low
        gvec[5:6, :] += gain_sum
        gvec[6:7, :] += bias_sum
        gvec[4:5, :] += jnp.sum(low.astype(F32), axis=0, keepdims=True)

    loop(4, hidden_back)

    run("dO")
    for n in range(3):
        value = dot_nn(n2[...], at[3, :, 256 * n : 256 * n + 256]).astype(BF16)
        d6[2 * n] = value[:, 0:128]
        d6[2 * n + 1] = value[:, 128:256]
    run("gao")
    for s in range(4):
        transpose_rows(tc, s, n2[128 * s : 128 * s + 128, :])
    gp[768:1536, :] = dot_nn(tc[...], lane_tiles(o6)).astype(BF16)

    def value_back(p):
        grads_in, grad_value = d6[p], 0.0
        for which in range(2):
            grad_value = grad_value + dot_nn(pt[2 * p + which], half_of(grads_in, which))
        tc[rows_of(p), :] = grad_value.T.astype(BF16)
        o6[p] = grad_value.astype(BF16)

    def attend_back(p):
        rows = rows_of(p)
        queries, keys, values, grads_in = q6[p], k6[p], v6[p], d6[p]
        keys_t = turn(keys)
        grad_query, grad_key = [], 0.0
        for which in range(2):
            wide = pt[2 * p + which].astype(F32)
            grad_probs = dot_nt(half_of(values, which), grads_in)
            inner = jnp.sum(wide * grad_probs, axis=0, keepdims=True)
            grad_scores = (wide * (grad_probs - inner)).astype(BF16)
            grad_query.append(dot_nn(keys_t[64 * which : 64 * which + 64, :], grad_scores))
            grad_key = grad_key + dot_nn(grad_scores, half_of(queries, which))
        grad_query = jnp.concatenate(grad_query, axis=0) * HEAD ** (-0.5)
        ta[rows, :] = grad_query.astype(BF16)
        tb[rows, :] = grad_key.T.astype(BF16)
        q6[p] = grad_query.T.astype(BF16)
        k6[p] = grad_key.astype(BF16)

    def pack(p, first_row, second_row):
        def body(s):
            for xx in range(2):
                offset = (2 * s + xx) * 96
                rows = [pl.ds(pl.multiple_of(first_row + offset, 96), 96),
                        pl.ds(pl.multiple_of(second_row + offset, 96), 96)]
                first, second = ua.at[p, 0, :, xx, s], ua.at[p, 1, :, xx, s]
                for yy in range(2):
                    lo, mid, hi = 384 * yy, 384 * yy + 128, 384 * yy + 256
                    for m in range(2):
                        first[yy, 96 * m : 96 * m + 96, :] = gp[rows[m], lo : lo + 128]
                        second[yy, 96 * m : 96 * m + 96, :] = gp[rows[m], hi : hi + 128]
                    even = gp[rows[0], mid : mid + 128].astype(F32)
                    odd = pltpu.roll(gp[rows[1], mid : mid + 128].astype(F32), 64, 1)
                    first[yy, 192:288, :] = jnp.where(lanes < 64, even, odd).astype(BF16)
                    second[yy, 192:288, :] = jnp.where(lanes < 64, odd, even).astype(BF16)

        loop(zs, body)

    parts("av", 6, value_back)
    run("gav")
    for n in units[VO[0] : VO[1] + 1]:
        ag_drain(n)
    gp[0:768, :] = dot_nn(tc[...], n1[...]).astype(BF16)
    pack(1, 0, 768)
    for n in grads[AVO[0] : AVO[1] + 1]:
        rs_start(n)
    parts("ab", 6, attend_back)
    run("gaqk")
    for n in units[QK[0] : QK[1] + 1]:
        ag_drain(n)

    def score_weights(m):
        gp[pl.ds(pl.multiple_of(768 * m, 256), 768), :] = dot_nn(turned[m], n1[...]).astype(BF16)

    loop(2, score_weights)
    pack(0, 0, 768)
    for n in grads[AQK[0] : AQK[1] + 1]:
        rs_start(n)

    def reduce(e):
        owner = 1 - e
        value = dot_nt(act[block_rows(owner, 0), :], reduce_block(0))
        value = value + dot_nt(act[block_rows(owner, 1), :], reduce_block(1))

        @pl.when(e == 0)
        def _():
            n2[...] = value.astype(BF16)
            ahead_swap.start()

        @pl.when(e == 1)
        def _():
            h1[...] = h1[...] + vec[7:8, :] + value

    def layer_output():
        parts("red", 2, reduce)
        run("outst")
        for moved in cot_out:
            moved.wait_send()
        for s in range(4):
            rows = slice(128 * s, 128 * s + 128)
            stage[s] = (h1[rows, :] + ahead_in[rows, :].astype(F32)).astype(BF16)
        own_out.start()

    layer_output()
    run("dn1")
    h1[...] = jnp.zeros_like(h1)

    def project_back(m):
        h1[...] += dot_nn(lane_tiles(heads.at[m + lax.div(m, 2)]), at[m])

    loop(3, project_back)
    gvec[2:3, :] = jnp.sum(lane_tiles(q6).astype(F32), axis=0, keepdims=True)
    gvec[3:4, :] = jnp.sum(lane_tiles(o6).astype(F32), axis=0, keepdims=True)

    run("inb")

    def input_back(s):
        rows = rows_of(s)
        grad, gain_sum, bias_sum = norm_gradient(x_in[s].astype(F32), vec[0:1, :], h1[rows, :])
        n1[rows, :] = (grad + acc[rows, :]).astype(BF16)
        gvec[0:1, :] += gain_sum
        gvec[1:2, :] += bias_sum

    loop(4, input_back)
    gvec_steps[0]()
    own_grad.start()
    run("end")
    finish_vectors()
    w1_back.wait()
    each_core(join_expand)
    w2_back.wait()
    each_core(join_reduce)

    own_out.wait()
    own_grad.wait()
    for moved in tokens_out + result_out + grad_out:
        moved.wait_send()
    for n in units[VO[1] + 1 :]:
        ag_drain(n)
    for n in grads:
        rs_drain(n)


def layer(sub, tokens, cotangent, span_mask, vectors, attention, expand, reduce_t):
    zs = GROUPS // 2
    seqs, block, width = tokens.shape
    rows = seqs * block
    columns = attention.shape[2]
    piece = (3 * columns, 128)
    vmem = lambda shape, dtype: pltpu.VMEM(shape, dtype)
    half = (2, 2, 2, zs) + piece
    scratch = [vmem(value.shape, value.dtype) for value in (span_mask, vectors, attention, expand, reduce_t)]
    scratch += [vmem((2,) + half, BF16)] + [vmem(half, BF16)] * 4
    scratch += [vmem((2, 2, 2, zs) + piece, BF16), vmem((6, 2, 2, zs) + piece, BF16)]
    scratch += [vmem(tokens.shape, BF16), vmem((2,) + tokens.shape, BF16), vmem(tokens.shape, BF16)]
    scratch += [vmem((16, width), F32)] * 2
    scratch += [vmem((zs + 2, 16, width), F32)] * 2
    scratch += [vmem((16, columns), F32)]
    tiles = vmem((width // 128, rows, 128), BF16)
    flat = vmem((rows, width), BF16)
    wide = vmem((rows, width), F32)
    scratch += [vmem((4, width, width), BF16), flat, vmem((4, width // 128, rows, 128), BF16)]
    scratch += [vmem((HEADS, rows, rows), BF16), wide, wide, vmem((2, rows, width), BF16)]
    scratch += [vmem((4 * rows, width), BF16)] * 2 + [vmem((3, width, rows), BF16), tiles]
    scratch += [vmem(expand.shape, F32), vmem(reduce_t.shape, F32)]
    scratch += [tiles, flat, vmem((columns, width // 2), F32), vmem((2, width), F32), vmem((2, width), F32)]
    scratch += [vmem((6,) + piece, F32), vmem((width // 2, 2 * columns), F32)]
    scratch += [vmem((2 * columns, 2 * columns), F32), vmem(piece, F32)]
    scratch += [pltpu.SemaphoreType.DMA((10,))]
    gathered, summed = sum(map(len, GATHER_ROUTES)), sum(map(len, SUM_ROUTES))
    scratch += [pltpu.SemaphoreType.DMA((gathered, 4 * zs))] * 2
    scratch += [pltpu.SemaphoreType.DMA((gathered,))] * 2
    scratch += [pltpu.SemaphoreType.DMA((summed, zs + 2))] * 2
    scratch += [pltpu.SemaphoreType.DMA((4, 3))] * 2
    scratch += [pltpu.SemaphoreType.DMA((2, zs + 2))] * 2
    scratch += [pltpu.SemaphoreType.DMA((8,))] * 2
    in_vmem = pl.BlockSpec(memory_space=pltpu.VMEM)
    anywhere = pl.BlockSpec(memory_space=pl.ANY)
    return pl.pallas_call(
        functools.partial(kernel, sub, zs),
        out_shape=(
            jax.ShapeDtypeStruct(tokens.shape, BF16),
            jax.ShapeDtypeStruct(tokens.shape, BF16),
            jax.ShapeDtypeStruct(attention.shape, F32),
            jax.ShapeDtypeStruct(expand.shape, F32),
            jax.ShapeDtypeStruct(reduce_t.shape, F32),
            jax.ShapeDtypeStruct(vectors.shape, F32),
        ),
        in_specs=[anywhere] * 7,
        out_specs=(anywhere, anywhere) + (in_vmem,) * 4,
        scratch_shapes=scratch,
        compiler_params=pltpu.CompilerParams(
            collective_id=0, has_side_effects=True, vmem_limit_bytes=65400 * 1024
        ),
    )(tokens, cotangent, span_mask, vectors, attention, expand, reduce_t)


def update_kernel(rates, *refs):
    count = len(rates)
    ins, (result, grad) = refs[: 4 * count], refs[4 * count : 4 * count + 2]
    outs, (result_out, grad_out) = refs[4 * count + 2 : 7 * count + 2], refs[7 * count + 2 : 7 * count + 4]
    held, (low, wide, passed) = refs[7 * count + 4 : 11 * count + 4], refs[11 * count + 4 : 11 * count + 7]
    in_sems, out_sems = refs[11 * count + 7 :]
    loads = [pltpu.make_async_copy(ins[n], held[n], in_sems.at[n]) for n in range(4 * count)]
    stores = [pltpu.make_async_copy(held[4 * n + m], outs[3 * n + m], out_sems.at[3 * n + m])
              for n in range(count) for m in range(3)]
    load_grad = pltpu.make_async_copy(grad, low, in_sems.at[4 * count])
    store_grad = pltpu.make_async_copy(wide, grad_out, out_sems.at[3 * count])
    load_result = pltpu.make_async_copy(result, passed, in_sems.at[4 * count + 1])
    store_result = pltpu.make_async_copy(passed, result_out, out_sems.at[3 * count + 1])
    load_grad.start()
    load_result.start()
    for copy in loads:
        copy.start()
    load_result.wait()
    store_result.start()
    load_grad.wait()

    def widen(s, carry):
        wide[s] = low[s].astype(F32)
        return carry

    lax.fori_loop(0, low.shape[0], widen, 0)
    store_grad.start()
    for n in range(count):
        for m in range(4):
            loads[4 * n + m].wait()
        weight, one, two, gradient = held[4 * n : 4 * n + 4]
        values = adamw(weight[...], one[...], two[...], gradient[...], rates[n])
        for ref, value in zip((weight, one, two), values):
            ref[...] = value
        for m in range(3):
            stores[3 * n + m].start()
    for copy in stores + [store_grad, store_result]:
        copy.wait()


def update(rates, arrays, result, grad):
    flat = [value for group in arrays for value in group]
    new = [jax.ShapeDtypeStruct(value.shape, F32) for group in arrays for value in group[:3]]
    new += [jax.ShapeDtypeStruct(result.shape, BF16), jax.ShapeDtypeStruct(grad.shape, F32)]
    anywhere = pl.BlockSpec(memory_space=pl.ANY)
    scratch = [pltpu.VMEM(value.shape, F32) for value in flat]
    scratch += [pltpu.VMEM(grad.shape, BF16), pltpu.VMEM(grad.shape, F32), pltpu.VMEM(result.shape, BF16)]
    scratch += [pltpu.SemaphoreType.DMA((len(flat) + 2,)), pltpu.SemaphoreType.DMA((len(new),))]
    return pl.pallas_call(
        functools.partial(update_kernel, rates),
        out_shape=tuple(new),
        in_specs=[anywhere] * (len(flat) + 2),
        out_specs=(anywhere,) * len(new),
        scratch_shapes=scratch,
        compiler_params=pltpu.CompilerParams(vmem_limit_bytes=63 * 1024 * 1024),
    )(*flat, result, grad)


def local(
    sub,
    tokens,
    cotangent,
    span_mask,
    attention_weight,
    expand_weight,
    reduce_weight,
    vectors,
    attention_first,
    attention_second,
    expand_first,
    expand_second,
    reduce_first,
    reduce_second,
    vector_first,
    vector_second,
):
    together = [[n * sub + m for m in range(sub)] for n in range(GROUPS)]

    def widen(value, axis):
        if sub == 1:
            return value
        low = lax.all_gather(
            value.astype(BF16), "batch", axis=axis, tiled=True, axis_index_groups=together
        )
        return low.astype(F32)

    def narrow(value, axis):
        if sub == 1:
            return value
        return lax.psum_scatter(
            value, "batch", scatter_dimension=axis, tiled=True, axis_index_groups=together
        )

    out_tokens, input_grad, ga, g1, g2, gv = layer(
        sub,
        tokens,
        cotangent,
        span_mask,
        widen(vectors, 1),
        widen(attention_weight, 2),
        widen(expand_weight, 1),
        widen(reduce_weight.T, 0),
    )
    arrays = (
        (attention_weight, attention_first, attention_second, narrow(ga, 2)),
        (expand_weight, expand_first, expand_second, narrow(g1, 1)),
        (reduce_weight.T, reduce_first.T, reduce_second.T, narrow(g2, 0)),
        (vectors, vector_first, vector_second, narrow(gv, 1)),
    )
    rates = (rate_attention, rate_expand, rate_reduce, rate_vector)
    new = update(rates, arrays, out_tokens, input_grad)
    return new[-2:] + new[0:6] + tuple(value.T for value in new[6:9]) + new[9:12]


def solution(mesh):
    sub = mesh.shape["batch"] // GROUPS
    sequences = P("batch", "blk", None)
    attention = P(None, "blk", "batch")
    matrix = P("blk", "batch")
    return jax.shard_map(
        functools.partial(local, sub),
        mesh=mesh,
        in_specs=(sequences, sequences, P("batch", "blk"), attention, matrix, matrix, matrix)
        + (attention,) * 2
        + (matrix,) * 6,
        out_specs=(sequences,) * 2 + (attention,) * 3 + (matrix,) * 9,
        check_vma=False,
    )
```

```python
import functools
import math

import jax
import jax.numpy as jnp
from jax import lax
from jax.experimental import pallas as pl
from jax.experimental.pallas import tpu as pltpu
from jax.sharding import PartitionSpec as P

HEADS = 12
HEAD = 64
STEP = 10
GROUPS = 8

norm_epsilon = 1e-05
beta_one = 0.9
beta_two = 0.999
adam_epsilon = 1e-08
decay_weight = 0.1
rate_attention = 0.05
rate_expand = 0.03
rate_reduce = 0.015
rate_vector = 0.4

F32 = jnp.float32
BF16 = jnp.bfloat16
MESH = pl.DeviceIdType.MESH
GELU_SCALE = math.sqrt(2.0 / math.pi)
GELU_CUBE = 0.044715


def adamw(weight, moment_one, moment_two, gradient, step_rate):
    moment_one = beta_one * moment_one + (1.0 - beta_one) * gradient
    moment_two = beta_two * moment_two + (1.0 - beta_two) * gradient * gradient
    corrected_one = moment_one / (1.0 - beta_one**STEP)
    corrected_two = moment_two / (1.0 - beta_two**STEP)
    updated = weight - step_rate * (
        corrected_one / (jnp.sqrt(corrected_two) + adam_epsilon) + decay_weight * weight
    )
    return (updated, moment_one, moment_two)


def dot_nn(left, right):
    return lax.dot_general(left, right, (((1,), (0,)), ((), ())), preferred_element_type=F32)


def dot_nt(left, right):
    return lax.dot_general(left, right, (((1,), (1,)), ((), ())), preferred_element_type=F32)


X, Y, Z = 1, 2, 4
(N_QKA, N_QKB, N_VOA, N_VOB, N_W10A, N_W10B, N_W11A, N_W11B, N_W20A, N_W20B, N_W21A, N_W21B) = range(12)
(N_AQKA, N_AQKB, N_AVOA, N_AVOB, N_G10, N_G11A, N_G11B, N_G20, N_G21) = range(9)
QK, VO = (N_QKA, N_QKB), (N_VOA, N_VOB)
AQK, AVO = (N_AQKA, N_AQKB), (N_AVOA, N_AVOB)
SEND, GOT, WHOLE, SUM, VEC, SMALL, DO = range(7)
(TOK, COT, OUT, IG, TOK_HERE, COT_HERE, OUT_HERE,
 IG_HERE, SWAP_HERE, N2S_HERE, COTS_HERE, BACKS_HERE, AHEADS_HERE) = range(13)
GATHER_ROUTES = (
    ((Z, Y, X), (Z, Y, X),),
    ((Z, Y, X), (Y, Z, X),),
    ((X, Z, Y), (Z, X, Y),),
    ((Z, Y, X), (Y, Z, X),),
    ((Y, X, Z), (X, Z, Y),),
    ((Z, Y, X), (Z, X, Y),),
)
SUM_ROUTES = (
    ((X, Z, Y), (X, Z, Y),),
    ((Y, X, Z), (Y, X, Z),),
    ((Y, X, Z),),
    ((X, Z, Y), (Y, Z, X),),
    ((Z, X, Y),),
    ((Y, X, Z),),
)
PLAN = dict(
    own1=(
        (SEND, N_QKA, 0, Z),
    ),
    ownff=(
        (DO, TOK), (SEND, N_QKB, 0, Z), (SEND, N_VOB, 0, Y), (DO, SWAP_HERE),
    ),
    mask=(
        (SEND, N_W20B, 0, X), (SEND, N_W10A, 0, X), (VEC, 0), (GOT, N_QKA, Z), (SEND, N_QKA, Z, Y),
        (SEND, N_QKA, Z, X), (SEND, N_VOA, 0, Z), (VEC, 1), (GOT, N_QKB, Z), (SEND, N_W10B, 0, Z),
        (SEND, N_QKB, Z, X), (SEND, N_QKB, Z, Y), (GOT, N_VOA, Z), (VEC, 2), (GOT, N_VOB, Y),
        (SEND, N_VOA, Z, X), (SEND, N_VOB, Y, Z), (SEND, N_VOB, 0, Z),
    ),
    ln1=(
        (SEND, N_W11A, 0, Z), (GOT, N_QKA, Z | Y), (SEND, N_QKA, Z | Y, X), (SEND, N_W20A, 0, Y), (VEC, 3),
        (SEND, N_W11B, 0, Z), (SEND, N_VOA, Z, Y), (GOT, N_W10B, Z), (GOT, N_W10A, X), (SEND, N_W10A, 0, Z),
        (DO, TOK_HERE), (GOT, N_QKB, Z | X), (GOT, N_QKB, Z | Y), (SEND, N_QKB, Z | Y, X),
        (SEND, N_W11B, 0, Y),
    ),
    unp0=(
        (SEND, N_W10B, Z, X), (GOT, N_W20B, X), (GOT, N_QKA, Z | X), (DO, COT), (GOT, N_VOB, Y | Z),
        (GOT, N_W11B, Y), (SEND, N_W10A, X, Z), (GOT, N_QKA, Z | Y | X), (GOT, N_VOB, Z), (SEND, N_VOB, Z, X),
        (GOT, N_QKB, Z | Y | X), (SEND, N_W11B, Y, Z), (SEND, N_VOB, Y | Z, X), (GOT, N_VOA, Z | Y),
        (GOT, N_W11A, Z), (SEND, N_VOA, Z | Y, X), (GOT, N_W20A, Y), (SEND, N_W11A, Z, X),
        (SEND, N_W11A, Z, Y), (WHOLE, N_QKA), (WHOLE, N_QKB), (SEND, N_W21A, 0, Z),
    ),
    projk=(
        (GOT, N_W10B, Z | X), (GOT, N_W11B, Z),
    ),
    attend0=(
        (SEND, N_W21B, 0, Z), (SEND, N_W10B, Z | X, Y), (SEND, N_W11B, Z, X), (SEND, N_W20B, 0, Z),
    ),
    attend1=(
        (GOT, N_VOB, Z | X), (SEND, N_W10B, Z, Y), (GOT, N_VOA, Z | X),
    ),
    attend3=(
        (GOT, N_VOB, Y | Z | X),
    ),
    attend4=(
        (GOT, N_W11A, Z | Y), (GOT, N_VOA, Z | Y | X), (SEND, N_W20B, X, Z), (DO, COT_HERE),
    ),
    attend5=(
        (GOT, N_W10A, Z), (GOT, N_W10A, X | Z), (GOT, N_W11B, Y | Z), (SEND, N_W11B, Y | Z, X),
        (SEND, N_W10A, X | Z, Y), (SEND, N_W20A, 0, Z), (WHOLE, N_VOA), (WHOLE, N_VOB),
    ),
    unp1=(
        (SEND, N_W11A, Z | Y, X), (SEND, N_W10A, Z, Y),
    ),
    projv=(
        (SEND, N_W20A, Y, X),
    ),
    mix1=(
        (SEND, N_W20A, Y, Z),
    ),
    mix2=(
        (GOT, N_W11B, Z | X), (GOT, N_W21B, Z), (DO, COTS_HERE), (GOT, N_W10B, Z | Y),
    ),
    mix3=(
        (GOT, N_W21A, Z), (SEND, N_W21A, Z, Y),
    ),
    mix4=(
        (SEND, N_W21B, Z, X), (GOT, N_W10B, Z | X | Y), (SEND, N_W21B, Z, Y), (SEND, N_W20A, 0, X),
        (GOT, N_W11A, Z | X),
    ),
    ao=(
        (SEND, N_W21A, Z, X), (GOT, N_W11B, Y | Z | X),
    ),
    expa0=(
        (GOT, N_W20B, Z), (GOT, N_W10A, Z | Y), (GOT, N_W10A, X | Z | Y), (SEND, N_W20B, Z, Y),
        (GOT, N_W11A, Z | Y | X),
    ),
    expa1=(
        (GOT, N_W20B, X | Z), (SEND, N_W20B, X | Z, Y), (GOT, N_W21A, Z | Y),
    ),
    expb0=(
        (GOT, N_W21B, Z | X), (GOT, N_W20A, Y | X), (DO, N2S_HERE),
    ),
    expb1=(
        (SEND, N_W20A, Y | X, Z), (GOT, N_W20A, X),
    ),
    trY=(
        (SEND, N_W21B, Z | X, Y), (SEND, N_W21A, Z | Y, X), (SEND, N_W20A, X, Z),
    ),
    innb0=(
        (SUM, N_G20, 0), (SUM, N_G21, 0), (GOT, N_W21A, Z | X), (GOT, N_W21B, Z | Y),
        (GOT, N_W21B, Z | X | Y), (GOT, N_W20A, X | Z), (GOT, N_W20B, Z | Y), (GOT, N_W20A, Z),
        (GOT, N_W21A, Z | Y | X), (GOT, N_W20A, Y | Z), (GOT, N_W20B, X | Z | Y), (GOT, N_W20A, Y | X | Z),
    ),
    gw1_0=(
        (DO, BACKS_HERE),
    ),
    hid=(
        (SUM, N_G10, 0), (SUM, N_G21, 1),
    ),
    dO=(
        (SUM, N_G11A, 0),
    ),
    av4=(
        (SUM, N_G11B, 0),
    ),
    av5=(
        (SUM, N_G21, 2),
    ),
    ab1=(
        (SUM, N_G20, 1),
    ),
    ab2=(
        (SUM, N_G10, 1), (SUM, N_AVOA, 0), (SUM, N_G11A, 1),
    ),
    ab5=(
        (SUM, N_G11B, 1),
    ),
    redb=(
        (SUM, N_AVOA, 1), (SUM, N_AVOB, 0), (SUM, N_G10, 2),
    ),
    reda=(
        (SUM, N_AQKA, 0),
    ),
    outst=(
        (SUM, N_AVOA, 2), (SUM, N_G11A, 2), (SUM, N_AQKB, 0), (DO, AHEADS_HERE),
    ),
    dn1=(
        (DO, OUT), (SUM, N_G20, 2),
    ),
    inb=(
        (SUM, N_AQKA, 1), (SUM, N_G21, 3), (SUM, N_AVOB, 1),
    ),
    end=(
        (DO, IG), (SUM, N_AQKB, 1), (SUM, N_G11A, 3), (SUM, N_G20, 3), (SMALL, 0), (SUM, N_G11B, 2),
        (SUM, N_AQKA, 2), (SMALL, 1), (SUM, N_AVOB, 2), (SMALL, 2), (SUM, N_G11B, 3), (SUM, N_AVOA, 3),
        (DO, OUT_HERE), (SUM, N_G10, 3), (SUM, N_AQKB, 2), (SUM, N_AQKA, 3), (SUM, N_AVOB, 3), (DO, IG_HERE),
        (SUM, N_AQKB, 3), (SMALL, 3),
    ),
)


def lane_tiles(ref, count=6):
    return jnp.concatenate([ref[t] for t in range(count)], axis=1)


class Unit:
    def __init__(self, index, route, rows, u, other):
        self.index, self.route, self.rows, self.u, self.other = index, route, rows, u, other


class Gradient:
    def __init__(self, index, route, rows, u, other, core_in, got, total):
        self.index, self.route, self.rows, self.u, self.other = index, route, rows, u, other
        self.core_in, self.got, self.total = core_in, got, total


def kernel(sub, zs, *refs):
    (tok, cot, mask_in, vec_in, a_in, w1_in, w2_in,
     out, ig, ga, g1, g2, gv,
     ua, uw1, uw2, gw1, gw2, core_in, got,
     x_in, cot_in, stage, vec, gvec, vin, gin, narrow_rows,
     at, n1, q6, k6, v6, o6, pt, h1, acc, n2, act, gp, ta, tb, tc, d6,
     w1_other, w2_other, n2_other, cot_other, back_in, ahead_in,
     lines, b1, gb1, totals, turned1, got1, got2,
     local_sem, ag_send, ag_recv, core_send, core_recv, rs_send, rs_recv,
     a2a_send, a2a_recv, v_send, v_recv, pair_send, pair_recv) = refs

    i = lax.axis_index("blk")
    b = lax.axis_index("batch")
    c, y = lax.rem(i, 2), lax.div(i, 2)
    g, r = lax.div(b, sub), lax.rem(b, sub)
    x, z = lax.rem(g, 2), lax.div(g, 2)

    def device(c_=c, y_=y, x_=x, z_=z):
        return {"blk": 2 * y_ + c_, "batch": (2 * z_ + x_) * sub + r}

    def z_at(k):
        return lax.rem(z + k, zs)

    def block_at(k):
        return lax.rem(i + k, 4)

    def copy(src, dst, send, recv, to):
        return pltpu.make_async_remote_copy(
            src_ref=src, dst_ref=dst, send_sem=send, recv_sem=recv, device_id=to, device_id_type=MESH
        )

    def loop(count, body, hooks=()):
        def step(s, carry):
            body(s)
            for k, f in hooks:
                pl.when(s == k)(f)
            return carry

        lax.fori_loop(0, count, step, 0)

    partners = [device(z_=z_at(k)) for k in range(1, zs)]
    partners += [device(x_=1 - x), device(y_=1 - y), device(c_=1 - c), device(c_=1 - c, y_=1 - y)]
    barrier = pltpu.get_barrier_semaphore()
    for partner in partners:
        pl.semaphore_signal(barrier, inc=1, device_id=partner, device_id_type=MESH)
    pl.semaphore_wait(barrier, len(partners))

    ME = {"y": y, "x": x, "z": z}

    def before(n, axis, other):
        return n.route.index(axis) < n.route.index(other)

    def side(n, axes, all_z):
        where = (1 - y if "y" in axes else y, 1 - x if "x" in axes else x, slice(None) if all_z else z)
        return n.u.at[where + (n.rows,)]

    def neighbour(axis):
        return device(y_=1 - y) if axis == "y" else device(x_=1 - x)

    def ag_copy(n, ref, axes, k, to):
        slot = (("y" in axes) * 2 + ("x" in axes)) * zs + k
        return copy(ref, ref, ag_send.at[n.index, slot], ag_recv.at[n.index, slot], to)

    def core_copy(n, ref):
        return copy(ref, ref, core_send.at[n.index], core_recv.at[n.index], device(c_=1 - c))

    def ag_sends(n, axes, axis):
        axes = axes.replace("z", "")
        if axis == "z":
            ref = side(n, axes, False)
            return [ag_copy(n, ref, axes, k, device(z_=z_at(k))) for k in range(1, zs)]
        ref = side(n, axes, before(n, "z", axis))
        return [ag_copy(n, ref, axes + axis, 0, neighbour(axis))]

    def ag_send_part(n, axes, axis):
        for moved in ag_sends(n, axes, axis):
            moved.start()

    def ag_wait_part(n, axes):
        last = max(axes, key=n.route.index)
        axes = axes.replace("z", "")
        if last == "z":
            yy, xx = (1 - y if "y" in axes else y), (1 - x if "x" in axes else x)
            for k in range(1, zs):
                ag_copy(n, n.u.at[yy, xx, z_at(zs - k), n.rows], axes, k, device()).wait_recv()
        else:
            ag_copy(n, side(n, axes, before(n, "z", last)), axes, 0, device()).wait_recv()
        if n.other is not None and (last == "z" or before(n, "z", last)):
            core_copy(n, side(n, axes, True)).start()

    def ag_done(n):
        if n.other is not None:
            core_copy(n, n.other.at[:, :, :, n.rows]).wait_recv()

    def ag_drain(n):
        for axis in n.route:
            earlier = [other for other in "yx" if before(n, other, axis)]
            for some in range(2 ** len(earlier)):
                axes = "".join(other for bit, other in enumerate(earlier) if some >> bit & 1)
                for moved in ag_sends(n, axes, axis):
                    moved.wait_send()
        if n.other is not None:
            core_copy(n, n.u.at[:, :, :, n.rows]).wait_send()

    AXES = "yxz"

    def rs_groups(n, step):
        axis = n.route[step]
        if axis == "z":
            return [(k, 1 + k, device(z_=z_at(zs - k))) for k in range(1, zs)]
        return [(1, "yx".index(axis), neighbour(axis))]

    def rs_where(n, step, k):
        axis, out, land = n.route[step], [], []
        for other in AXES:
            if other == axis:
                out.append(z_at(zs - k) if axis == "z" else 1 - ME[axis])
                land.append(k)
            elif before(n, other, axis):
                out.append(ME[other])
                land.append(0)
            else:
                out.append(slice(None))
                land.append(slice(None))
        return tuple(out) + (n.rows,), tuple(land) + (n.rows,)

    def rs_copy(n, step, k, slot, to):
        out, land = rs_where(n, step, k)
        return copy(n.u.at[out], n.got.at[land], rs_send.at[n.index, slot], rs_recv.at[n.index, slot], to)

    def rs_core(n):
        return copy(n.other.at[:, :, :, n.rows], n.core_in.at[:, :, :, n.rows], rs_send.at[n.index, zs + 1],
                    rs_recv.at[n.index, zs + 1], device(c_=1 - c))

    def add_terms(n, place, step):
        value = n.u[tuple(place) + (n.rows,)].astype(F32)
        if n.other is not None:
            value = value + n.core_in[tuple(place) + (n.rows,)].astype(F32)
        for axis in n.route[:step]:
            for k in range(1, zs) if axis == "z" else (1,):
                where = [k if other == axis else (0 if before(n, other, axis) else at_place)
                         for other, at_place in zip(AXES, place)]
                value = value + n.got[tuple(where) + (n.rows,)].astype(F32)
        return value

    def rs_start(n):
        rs_core(n).start()

    def rs_step(n, step):
        if step == 0 and n.other is not None:
            rs_core(n).wait_recv()
        if step > 0:
            for group in rs_groups(n, step - 1):
                rs_copy(n, step - 1, *group).wait_recv()
        if step == 3:
            n.total[n.rows, :] = add_terms(n, (y, x, z), 3)
            return
        for k, slot, to in rs_groups(n, step):
            out, _ = rs_where(n, step, k)
            if step > 0 or n.other is not None:
                spans = [range(2) if isinstance(at_place, slice) else (at_place,) for at_place in out[:2]]

                def body(zz):
                    for yy in spans[0]:
                        for xx in spans[1]:
                            n.u[yy, xx, zz, n.rows] = add_terms(n, (yy, xx, zz), step).astype(BF16)

                if isinstance(out[2], slice):
                    loop(zs, body)
                else:
                    body(out[2])
            rs_copy(n, step, k, slot, to).start()

    def rs_drain(n):
        if n.other is not None:
            rs_core(n).wait_send()
        for step in range(3):
            for group in rs_groups(n, step):
                rs_copy(n, step, *group).wait_send()

    def small_sum(ref, slots, which):
        to = (device(y_=1 - y), device(c_=1 - c), device(x_=1 - x))
        to += tuple(device(z_=z_at(k)) for k in range(1, zs))

        def moved(slot):
            return copy(ref, slots.at[slot], v_send.at[which, slot], v_recv.at[which, slot], to[slot])

        def land(last):
            moved(last).wait()
            ref[...] = ref[...] + slots[last]

        def step(n):
            def run():
                if n > 0:
                    land(n - 1)
                moved(n).start()

            return run

        def line():
            land(2)
            for k in range(1, zs):
                moved(2 + k).start()

        def finish():
            for k in range(1, zs):
                moved(2 + k).wait()
            value = ref[...]
            for k in range(1, zs):
                value = value + slots[2 + k]
            ref[...] = value

        return [step(0), step(1), step(2), line, finish]

    def rows_of(s):
        return pl.ds(pl.multiple_of(s * 128, 128), 128)

    def exchange(src, dst, which):
        return [copy(src.at[block_at(k)], dst.at[i], a2a_send.at[which, k - 1],
                     a2a_recv.at[which, k - 1], {"blk": block_at(k), "batch": b})
                for k in range(1, 4)]

    def exchange_landed(dst, which):
        return [copy(dst.at[block_at(4 - k)], dst.at[block_at(4 - k)], a2a_send.at[which, k - 1],
                     a2a_recv.at[which, k - 1], {"blk": block_at(4 - k), "batch": b})
                for k in range(1, 4)]

    def axes_of(mask):
        return "".join(axis for axis, bit in (("y", Y), ("x", X), ("z", Z)) if mask & bit)

    def rows_in(part, count):
        return pl.ds(part * (288 // count), 288 // count)

    units = []
    for unit, routes in enumerate(GATHER_ROUTES):
        half = unit % 2
        ref = (ua, uw1, uw2)[unit // 2]
        pieces = (ref.at[half, c], ref.at[half, 1 - c]) if unit < 2 else (ref.at[half], None)
        for part, route in enumerate(routes):
            units.append(Unit(len(units), "".join(map(axes_of, route)), rows_in(part, len(routes)), *pieces))

    def pair(slot, src, dst):
        return copy(src, dst, pair_send.at[slot], pair_recv.at[slot], device(c_=1 - c))

    w1_swap, w2_swap = pair(0, w1_in, w1_other), pair(1, w2_in, w2_other)

    def each_core(f):
        for q in range(2):
            pl.when(c == q)(functools.partial(f, q))

    def rest_rows(matrix):
        return a_in[matrix, pl.ds(pl.multiple_of(128 * (1 - c), 64), 64), :]

    def own_attention(p):
        mine = ua.at[p, c, y, x, z]
        for m in range(2):
            main = a_in[2 * p + m, pl.ds(pl.multiple_of(64 * c, 64), 128), :]
            mine[96 * m : 96 * m + 96, :] = main.T.astype(BF16)
        rest = jnp.concatenate([rest_rows(2 * p + c), rest_rows(2 * p + 1 - c)], axis=0)
        mine[192:288, :] = rest.T.astype(BF16)

    def own_expand(q):
        both = (w1_in, w1_other) if q == 0 else (w1_other, w1_in)
        cols = slice(192 * q, 192 * q + 192)
        blocks = (
            both[0][0:128, cols],
            jnp.concatenate([both[0][128:192, cols], both[1][0:64, cols]], axis=0),
            both[1][64:192, cols],
        )
        for t, block in enumerate(blocks):
            value = block.T.astype(BF16)
            for h in range(2):
                uw1[h, y, x, z, 96 * t : 96 * t + 96, :] = value[96 * h : 96 * h + 96, :]

    def own_reduce(q):
        both = (w2_in, w2_other) if q == 0 else (w2_other, w2_in)
        for cc in range(2):
            for part_of in range(2):
                start = 384 * part_of + 192 * q
                lines[:, 192 * part_of : 192 * part_of + 192] = both[cc][:, start : start + 192]
            for t in range(3):
                uw2[cc, y, x, z, 96 * t : 96 * t + 96, :] = lines[:, 128 * t : 128 * t + 128].astype(BF16)

    def own_hidden_bias(q):
        for zz in range(zs):
            for xx in range(2):
                col = 384 * (zz % 2) + 192 * xx
                start = 384 * xx + 192 * q
                b1[zz // 2 : zz // 2 + 1, col : col + 192] = vec[8 + zz : 9 + zz, start : start + 192]

    def hidden_bias_gradient(q):
        for zz in range(zs):
            for xx in range(2):
                col = 384 * (zz % 2) + 192 * xx
                start = 384 * xx + 192 * q
                gvec[8 + zz : 9 + zz, start : start + 192] = gb1[zz // 2 : zz // 2 + 1, col : col + 192]

    columns = a_in.shape[2]
    placed = lax.broadcasted_iota(jnp.int32, (columns, 768), 1) == (
        lax.broadcasted_iota(jnp.int32, (columns, 768), 0) + columns * g
    )

    def own_vectors():
        vec[...] = jnp.zeros_like(vec)
        rows = dot_nn(vec_in[...].astype(BF16), jnp.where(placed, 1.0, 0.0).astype(BF16))
        for j in range(3):
            vec[pl.ds(3 * i + j, 1), :] = rows[j : j + 1, :]

    load_cot = pltpu.make_async_copy(cot, stage, local_sem.at[4])

    def masked_cotangent():
        load_cot.wait()
        eye = lax.broadcasted_iota(jnp.int32, (128, 128), 0) == lax.broadcasted_iota(jnp.int32, (128, 128), 1)
        for s in range(4):
            row = jnp.broadcast_to(mask_in[s : s + 1, :].astype(F32), (128, 128))
            column = jnp.sum(jnp.where(eye, row, 0.0), axis=1, keepdims=True)
            stage[s] = (stage[s].astype(F32) * column).astype(BF16)

    def finish_attention(p):
        value = totals.at[p]
        for m in range(2):
            ga[2 * p + m, pl.ds(pl.multiple_of(64 * c, 64), 128), :] = value[96 * m : 96 * m + 96, :].T
        rest = value[192:288, :].T
        rows = pl.ds(pl.multiple_of(128 * (1 - c), 64), 64)
        ga[2 * p + c, rows, :] = rest[0:64, :]
        ga[2 * p + 1 - c, rows, :] = rest[64:128, :]

    w1_back = pair(6, turned1.at[pl.ds(pl.multiple_of(192 * (1 - c), 64), 192)], got1)
    w2_back = pair(7, totals.at[5 - c], got2)

    def turn_expand():
        for h in range(2):
            for t in range(3):
                turned1[128 * t : 128 * t + 128, 96 * h : 96 * h + 96] = totals[2 + h, 96 * t : 96 * t + 96, :].T
        w1_back.start()

    def join_expand(q):
        g1[:, 192 * q : 192 * q + 192] = turned1[192 * q : 192 * q + 192, :]
        g1[:, 192 * (1 - q) : 192 * (1 - q) + 192] = got1[...]

    def join_reduce(q):
        for half, value in ((q, totals.at[4 + q]), (1 - q, got2)):
            for t in range(3):
                lines[:, 128 * t : 128 * t + 128] = value[96 * t : 96 * t + 96, :]
            for part_of in range(2):
                start = 384 * part_of + 192 * half
                g2[:, start : start + 192] = lines[:, 192 * part_of : 192 * part_of + 192]

    def finish_vectors():
        value, total = gvec[...], 0.0
        for _ in range(3):
            part = value.astype(BF16)
            total = total + dot_nt(part, jnp.where(placed, 1.0, 0.0).astype(BF16))
            value = value - part.astype(F32)
        narrow_rows[...] = total
        for j in range(3):
            gv[j : j + 1, :] = narrow_rows[pl.ds(3 * i + j, 1), :]

    grads, owners = [], []
    for unit, routes in enumerate(SUM_ROUTES):
        half = unit % 2
        ref = (ua, gw1, gw2)[unit // 2]
        pieces = (ref.at[half, c], ref.at[half, 1 - c], core_in.at[half]) if unit < 2 else (ref.at[half], None, None)
        for part, route in enumerate(routes):
            grads.append(Gradient(len(grads), "".join(map(axes_of, route)), rows_in(part, len(routes)), *pieces,
                                  got.at[unit], totals.at[unit]))
            owners.append(unit)

    def summed(unit):
        if unit < 2:
            finish_attention(unit)
        elif unit < 4 and {2, 3} <= set(whole):
            turn_expand()
        elif unit >= 4 and {4, 5} <= set(whole):
            w2_back.start()

    seen, whole = set(), []

    def event(kind, *rest):
        if kind == SEND:
            ag_send_part(units[rest[0]], axes_of(rest[1]), axes_of(rest[2]))
        elif kind == GOT:
            ag_wait_part(units[rest[0]], axes_of(rest[1]))
        elif kind == WHOLE:
            ag_done(units[rest[0]])
        elif kind == SUM:
            rs_step(grads[rest[0]], rest[1])
            if rest[1] == 3:
                seen.add(rest[0])
                unit = owners[rest[0]]
                if all(k in seen for k in range(len(grads)) if owners[k] == unit):
                    whole.append(unit)
                    summed(unit)
        elif kind == DO:
            actions[rest[0]]()
        else:
            (vec_steps if kind == VEC else gvec_steps)[rest[0] + 1]()

    def run(part):
        for todo in PLAN.get(part, ()):
            event(*todo)

    def parts(name, count, body):
        run(name + "0")
        hooks = [(k - 1, functools.partial(run, name + str(k))) for k in range(1, count) if name + str(k) in PLAN]
        loop(count, body, hooks)

    def started(copies):
        for moved in copies:
            moved.start()
        return copies

    def arrived(*copies):
        for moved in copies:
            moved.wait_recv()

    load_cot.start()
    own_tokens = pltpu.make_async_copy(tok.at[i], x_in.at[i], local_sem.at[0])
    own_tokens.start()
    own_cot = pltpu.make_async_copy(stage.at[i], cot_in.at[i], local_sem.at[1])
    tokens_out, cot_out = exchange(tok, x_in, 0), exchange(stage, cot_in, 1)
    result_out = exchange(stage, out, 2)
    grad_out = [copy(n1.at[rows_of(block_at(k))], ig.at[i], a2a_send.at[3, k - 1], a2a_recv.at[3, k - 1],
                     {"blk": block_at(k), "batch": b}) for k in range(1, 4)]
    own_out = pltpu.make_async_copy(stage.at[i], out.at[i], local_sem.at[2])
    own_grad = pltpu.make_async_copy(n1.at[rows_of(i)], ig.at[i], local_sem.at[3])
    n2_swap, cot_swap = pair(2, n2, n2_other), pair(3, cot_in, cot_other)
    back_swap, ahead_swap = pair(4, d6, back_in), pair(5, n2, ahead_in)
    vec_steps, gvec_steps = small_sum(vec, vin, 0), small_sum(gvec, gin, 1)

    def tokens_here():
        arrived(*exchange_landed(x_in, 0))
        own_tokens.wait()

    def cotangent_here():
        arrived(*exchange_landed(cot_in, 1))
        own_cot.wait()
        cot_swap.start()

    def swaps_here():
        w1_swap.wait()
        w2_swap.wait()

    actions = {
        TOK: lambda: started(tokens_out),
        COT: lambda: started(cot_out),
        OUT: lambda: started(result_out),
        IG: lambda: started(grad_out),
        TOK_HERE: tokens_here,
        COT_HERE: cotangent_here,
        OUT_HERE: lambda: arrived(*exchange_landed(out, 2)),
        IG_HERE: lambda: arrived(*exchange_landed(ig, 3)),
        SWAP_HERE: swaps_here,
        N2S_HERE: lambda: n2_swap.wait(),
        COTS_HERE: lambda: cot_swap.wait(),
        BACKS_HERE: lambda: back_swap.wait(),
        AHEADS_HERE: lambda: ahead_swap.wait(),
    }

    own_attention(0)
    w1_swap.start()
    w2_swap.start()
    own_vectors()
    vec_steps[0]()
    run("own1")
    own_attention(1)
    run("ownff")
    each_core(own_expand)
    each_core(own_reduce)
    run("mask")
    masked_cotangent()
    own_cot.start()
    run("ln1")
    each_core(own_hidden_bias)

    def normalise(value):
        centered = value - jnp.mean(value, axis=-1, keepdims=True)
        scale = lax.rsqrt(jnp.mean(centered * centered, axis=-1, keepdims=True) + norm_epsilon)
        return centered * scale, scale

    def first_norm(s):
        unit, _ = normalise(x_in[s].astype(F32))
        n1[rows_of(s), :] = (unit * vec[0:1, :] + vec[1:2, :]).astype(BF16)

    loop(4, first_norm)
    run("unp0")

    lanes = lax.broadcasted_iota(jnp.int32, (96, 128), 1)

    def unpack(p, s):
        for xx in range(2):
            rows = pl.ds(pl.multiple_of((2 * s + xx) * 96, 96), 96)
            for yy in range(2):
                first, second = ua.at[p, 0, yy, xx, s], ua.at[p, 1, yy, xx, s]
                lo, hi = 384 * yy, 384 * yy + 256
                for m in range(2):
                    at[2 * p + m, rows, lo : lo + 128] = first[96 * m : 96 * m + 96, :]
                    at[2 * p + m, rows, hi : hi + 128] = second[96 * m : 96 * m + 96, :]
                rest_first = first[192:288, :].astype(F32)
                rest_second = second[192:288, :].astype(F32)
                even = jnp.where(lanes < 64, rest_first, rest_second)
                odd = pltpu.roll(jnp.where(lanes < 64, rest_second, rest_first), 64, 1)
                at[2 * p, rows, lo + 128 : lo + 256] = even.astype(BF16)
                at[2 * p + 1, rows, lo + 128 : lo + 256] = odd.astype(BF16)

    def project(m, dst, bias):
        for n in range(3):
            value = dot_nt(n1[...], at[m, 256 * n : 256 * n + 256, :])
            if bias is not None:
                value = value + vec[bias : bias + 1, 256 * n : 256 * n + 256]
            value = value.astype(BF16)
            if m == 0:
                value = value * jnp.asarray(HEAD ** (-0.5), BF16)
            dst[2 * n] = value[:, 0:128]
            dst[2 * n + 1] = value[:, 128:256]

    loop(zs, functools.partial(unpack, 0))
    run("projq")
    project(0, q6, 2)
    run("projk")
    project(1, k6, None)

    half_lane = lax.broadcasted_iota(jnp.int32, (512, 128), 1) // HEAD

    def half_of(value, which):
        return jnp.where(half_lane == which, value, jnp.zeros_like(value))

    def turn(value):
        return value.astype(F32).T.astype(BF16)

    def attend(p):
        queries, keys = q6[p], k6[p]
        for which in range(2):
            scores = dot_nt(half_of(keys, which), queries)
            expo = jnp.exp(scores - jnp.max(scores, axis=0, keepdims=True))
            probs = (expo * (1.0 / jnp.sum(expo, axis=0, keepdims=True))).astype(BF16)
            pt[2 * p + which] = probs

    def mix(p):
        values_t = turn(v6[p])
        mixed = [dot_nn(values_t[64 * which : 64 * which + 64, :], pt[2 * p + which]) for which in range(2)]
        o6[p] = jnp.concatenate(mixed, axis=0).T.astype(BF16)

    parts("attend", 6, attend)
    run("unp1")
    loop(zs, functools.partial(unpack, 1))
    run("projv")
    project(2, v6, 3)
    parts("mix", 6, mix)

    run("ao")
    for n in range(3):
        cols = slice(256 * n, 256 * n + 256)
        value = dot_nt(lane_tiles(o6), at[3, cols, :]) + vec[4:5, cols]
        for s in range(4):
            h1[128 * s : 128 * s + 128, cols] = x_in[s, :, cols].astype(F32) + value[128 * s : 128 * s + 128]

    def second_norm(s):
        unit, _ = normalise(h1[rows_of(s), :])
        n2[rows_of(s), :] = (unit * vec[5:6, :] + vec[6:7, :]).astype(BF16)

    run("ln2")
    loop(4, second_norm)
    n2_swap.start()

    def expand_block(s):
        def piece(ref):
            return jnp.concatenate([ref[96 * t : 96 * t + 96, :] for t in range(3)], axis=1)

        return jnp.concatenate(
            [jnp.concatenate([piece(uw1.at[h, yy, xx, 2 * s + zz]) for yy in range(2)], axis=1)
             for zz in range(2) for xx in range(2) for h in range(2)],
            axis=0,
        )

    def reduce_block(s):
        def piece(ref):
            return jnp.concatenate([ref[96 * t : 96 * t + 96, :] for t in range(3)], axis=1)

        return jnp.concatenate(
            [jnp.concatenate([piece(uw2.at[cc, s, xx, zz]) for cc in range(2)], axis=1)
             for zz in range(zs) for xx in range(2)],
            axis=0,
        )

    def block_rows(owner, s):
        return pl.ds(pl.multiple_of((2 * owner + s) * 512, 512), 512)

    def expand(owner, normed, s):
        rows = block_rows(owner, s)
        inner = dot_nt(normed[...], expand_block(s)) + b1[pl.ds(s, 1), :]
        square = inner * inner
        tanh = jnp.tanh(GELU_SCALE * inner * (1.0 + GELU_CUBE * square))
        act[rows, :] = (0.5 * inner * (1.0 + tanh)).astype(BF16)
        slope = 0.5 * (1.0 + tanh) + 0.5 * inner * (1.0 - tanh * tanh) * (
            GELU_SCALE * (1.0 + 3.0 * GELU_CUBE * square)
        )
        gp[rows, :] = slope.astype(BF16)

    parts("expa", 2, functools.partial(expand, 0, n2))
    parts("expb", 2, functools.partial(expand, 1, n2_other))

    gvec[...] = jnp.zeros_like(gvec)

    def transpose_rows(dst, s, value):
        dst[:, 128 * s : 128 * s + 128] = turn(value)

    run("trY")
    total = jnp.zeros((1, 768), F32)
    for s in range(4):
        transpose_rows(ta, s, cot_in[s])
        total = total + jnp.sum(cot_in[s].astype(F32), axis=0, keepdims=True)
    gvec[7:8, :] = total
    for s in range(4):
        transpose_rows(tb, s, cot_other[s])

    def both_rows(ref, s):
        return jnp.concatenate([ref[block_rows(0, s), :], ref[block_rows(1, s), :]], axis=0)

    def reduce_back(s):
        grad = dot_nn(jnp.concatenate([ta[...], tb[...]], axis=1), both_rows(act, s)).astype(BF16)
        for zz in range(zs):
            for xx in range(2):
                row = 96 * (2 * zz + xx)
                for cc in range(2):
                    for t in range(3):
                        col = 384 * cc + 128 * t
                        gw2[cc, s, xx, zz, 96 * t : 96 * t + 96, :] = grad[row : row + 96, col : col + 128]

    parts("gw2_", 2, reduce_back)

    def rows_together(ref):
        return jnp.concatenate([ref[s] for s in range(4)], axis=0)

    def inner_back(owner, cotangent_rows, s):
        rows = block_rows(owner, s)
        grad = dot_nn(rows_together(cotangent_rows), reduce_block(s)) * gp[rows, :].astype(F32)
        low = grad.astype(BF16)
        gp[rows, :] = low
        sums = jnp.sum(low.astype(F32), axis=0, keepdims=True)
        gb1[pl.ds(s, 1), :] = sums if owner == 1 else gb1[pl.ds(s, 1), :] + sums

    def norm_back(owner):
        acc[...] = dot_nn(gp[block_rows(owner, 0), :], expand_block(0))
        acc[...] += dot_nn(gp[block_rows(owner, 1), :], expand_block(1))

    parts("innb", 2, functools.partial(inner_back, 1, cot_other))
    run("dn2b")
    norm_back(1)
    for t in range(6):
        d6[t] = acc[:, 128 * t : 128 * t + 128].astype(BF16)
    back_swap.start()
    parts("inna", 2, functools.partial(inner_back, 0, cot_in))
    each_core(hidden_bias_gradient)
    run("dn2a")
    norm_back(0)

    def expand_back(s):
        turned = jnp.concatenate([turn(gp[block_rows(owner, s), :]) for owner in range(2)], axis=1)
        normed = jnp.concatenate([n2[...], n2_other[...]], axis=0)
        grad = dot_nn(turned, normed).astype(BF16)
        for zz in range(2):
            for xx in range(2):
                for h in range(2):
                    row = 384 * zz + 192 * xx + 96 * h
                    for yy in range(2):
                        for t in range(3):
                            col = 384 * yy + 128 * t
                            gw1[h, yy, xx, 2 * s + zz, 96 * t : 96 * t + 96, :] = grad[
                                row : row + 96, col : col + 128
                            ]

    parts("gw1_", 2, expand_back)
    run("hid")

    def norm_gradient(value, scale_row, grad):
        unit, scale = normalise(value)
        gain_sum = jnp.sum(grad * unit, axis=0, keepdims=True)
        bias_sum = jnp.sum(grad, axis=0, keepdims=True)
        inner = grad * scale_row
        mean = jnp.mean(inner, axis=-1, keepdims=True)
        along = jnp.mean(inner * unit, axis=-1, keepdims=True)
        return scale * (inner - mean - unit * along), gain_sum, bias_sum

    def hidden_back(s):
        rows = rows_of(s)
        grad_in = jnp.concatenate([back_in[t, rows, :] for t in range(6)], axis=1)
        grad_in = acc[rows, :] + grad_in.astype(F32)
        grad, gain_sum, bias_sum = norm_gradient(h1[rows, :], vec[5:6, :], grad_in)
        grad = grad + cot_in[s].astype(F32)
        acc[rows, :] = grad
        low = grad.astype(BF16)
        n2[rows, :] = low
        gvec[5:6, :] += gain_sum
        gvec[6:7, :] += bias_sum
        gvec[4:5, :] += jnp.sum(low.astype(F32), axis=0, keepdims=True)

    loop(4, hidden_back)

    run("dO")
    for n in range(3):
        value = dot_nn(n2[...], at[3, :, 256 * n : 256 * n + 256]).astype(BF16)
        d6[2 * n] = value[:, 0:128]
        d6[2 * n + 1] = value[:, 128:256]
    run("gao")
    for s in range(4):
        transpose_rows(tc, s, n2[128 * s : 128 * s + 128, :])
    gp[768:1536, :] = dot_nn(tc[...], lane_tiles(o6)).astype(BF16)

    def value_back(p):
        grads_in, grad_value = d6[p], 0.0
        for which in range(2):
            grad_value = grad_value + dot_nn(pt[2 * p + which], half_of(grads_in, which))
        tc[rows_of(p), :] = grad_value.T.astype(BF16)
        o6[p] = grad_value.astype(BF16)

    def attend_back(p):
        rows = rows_of(p)
        queries, keys, values, grads_in = q6[p], k6[p], v6[p], d6[p]
        keys_t = turn(keys)
        grad_query, grad_key = [], 0.0
        for which in range(2):
            wide = pt[2 * p + which].astype(F32)
            grad_probs = dot_nt(half_of(values, which), grads_in)
            inner = jnp.sum(wide * grad_probs, axis=0, keepdims=True)
            grad_scores = (wide * (grad_probs - inner)).astype(BF16)
            grad_query.append(dot_nn(keys_t[64 * which : 64 * which + 64, :], grad_scores))
            grad_key = grad_key + dot_nn(grad_scores, half_of(queries, which))
        grad_query = jnp.concatenate(grad_query, axis=0) * HEAD ** (-0.5)
        ta[rows, :] = grad_query.astype(BF16)
        tb[rows, :] = grad_key.T.astype(BF16)
        q6[p] = grad_query.T.astype(BF16)
        k6[p] = grad_key.astype(BF16)

    def pack(p, first_row, second_row):
        def body(s):
            for xx in range(2):
                offset = (2 * s + xx) * 96
                rows = [pl.ds(pl.multiple_of(first_row + offset, 96), 96),
                        pl.ds(pl.multiple_of(second_row + offset, 96), 96)]
                first, second = ua.at[p, 0, :, xx, s], ua.at[p, 1, :, xx, s]
                for yy in range(2):
                    lo, mid, hi = 384 * yy, 384 * yy + 128, 384 * yy + 256
                    for m in range(2):
                        first[yy, 96 * m : 96 * m + 96, :] = gp[rows[m], lo : lo + 128]
                        second[yy, 96 * m : 96 * m + 96, :] = gp[rows[m], hi : hi + 128]
                    even = gp[rows[0], mid : mid + 128].astype(F32)
                    odd = pltpu.roll(gp[rows[1], mid : mid + 128].astype(F32), 64, 1)
                    first[yy, 192:288, :] = jnp.where(lanes < 64, even, odd).astype(BF16)
                    second[yy, 192:288, :] = jnp.where(lanes < 64, odd, even).astype(BF16)

        loop(zs, body)

    parts("av", 6, value_back)
    run("gav")
    for n in units[VO[0] : VO[1] + 1]:
        ag_drain(n)
    gp[0:768, :] = dot_nn(tc[...], n1[...]).astype(BF16)
    pack(1, 0, 768)
    for n in grads[AVO[0] : AVO[1] + 1]:
        rs_start(n)
    parts("ab", 6, attend_back)
    run("gaqk")
    for n in units[QK[0] : QK[1] + 1]:
        ag_drain(n)
    gp[0:768, :] = dot_nn(ta[...], n1[...]).astype(BF16)
    gp[768:1536, :] = dot_nn(tb[...], n1[...]).astype(BF16)
    pack(0, 0, 768)
    for n in grads[AQK[0] : AQK[1] + 1]:
        rs_start(n)

    def reduce(owner):
        value = dot_nt(act[block_rows(owner, 0), :], reduce_block(0))
        return value + dot_nt(act[block_rows(owner, 1), :], reduce_block(1))

    def layer_output():
        run("redb")
        n2[...] = reduce(1).astype(BF16)
        ahead_swap.start()
        run("reda")
        h1[...] = h1[...] + vec[7:8, :] + reduce(0)
        run("outst")
        for moved in cot_out:
            moved.wait_send()
        for s in range(4):
            rows = slice(128 * s, 128 * s + 128)
            stage[s] = (h1[rows, :] + ahead_in[rows, :].astype(F32)).astype(BF16)
        own_out.start()

    layer_output()
    run("dn1")
    h1[...] = dot_nn(lane_tiles(q6), at[0])
    h1[...] += dot_nn(lane_tiles(k6), at[1])
    h1[...] += dot_nn(lane_tiles(o6), at[2])
    gvec[2:3, :] = jnp.sum(lane_tiles(q6).astype(F32), axis=0, keepdims=True)
    gvec[3:4, :] = jnp.sum(lane_tiles(o6).astype(F32), axis=0, keepdims=True)

    run("inb")

    def input_back(s):
        rows = rows_of(s)
        grad, gain_sum, bias_sum = norm_gradient(x_in[s].astype(F32), vec[0:1, :], h1[rows, :])
        n1[rows, :] = (grad + acc[rows, :]).astype(BF16)
        gvec[0:1, :] += gain_sum
        gvec[1:2, :] += bias_sum

    loop(4, input_back)
    gvec_steps[0]()
    own_grad.start()
    run("end")
    finish_vectors()
    w1_back.wait()
    each_core(join_expand)
    w2_back.wait()
    each_core(join_reduce)

    own_out.wait()
    own_grad.wait()
    for moved in tokens_out + result_out + grad_out:
        moved.wait_send()
    for n in units[VO[1] + 1 :]:
        ag_drain(n)
    for n in grads:
        rs_drain(n)


def layer(sub, tokens, cotangent, span_mask, vectors, attention, expand, reduce_t):
    zs = GROUPS // 2
    seqs, block, width = tokens.shape
    rows = seqs * block
    columns = attention.shape[2]
    piece = (3 * columns, 128)
    vmem = lambda shape, dtype: pltpu.VMEM(shape, dtype)
    half = (2, 2, 2, zs) + piece
    scratch = [vmem((2,) + half, BF16)] + [vmem(half, BF16)] * 4
    scratch += [vmem((2, 2, 2, zs) + piece, BF16), vmem((6, 2, 2, zs) + piece, BF16)]
    scratch += [vmem(tokens.shape, BF16)] * 3
    scratch += [vmem((16, width), F32)] * 2
    scratch += [vmem((zs + 2, 16, width), F32)] * 2
    scratch += [vmem((16, columns), F32)]
    tiles = vmem((width // 128, rows, 128), BF16)
    flat = vmem((rows, width), BF16)
    turned = vmem((width, rows), BF16)
    scratch += [vmem((4, width, width), BF16), flat, tiles, tiles, tiles, tiles]
    scratch += [vmem((HEADS, rows, rows), BF16), vmem((rows, width), F32), vmem((rows, width), F32)]
    scratch += [flat, vmem((4 * rows, width), BF16), vmem((4 * rows, width), BF16)]
    scratch += [turned, turned, turned, tiles]
    scratch += [vmem(expand.shape, F32), vmem(reduce_t.shape, F32), flat, vmem(tokens.shape, BF16)]
    scratch += [tiles, flat, vmem((columns, width // 2), F32), vmem((2, width), F32), vmem((2, width), F32)]
    scratch += [vmem((6,) + piece, F32), vmem((width // 2, 2 * columns), F32)]
    scratch += [vmem((2 * columns, 2 * columns), F32), vmem(piece, F32)]
    scratch += [pltpu.SemaphoreType.DMA((5,))]
    gathered, summed = sum(map(len, GATHER_ROUTES)), sum(map(len, SUM_ROUTES))
    scratch += [pltpu.SemaphoreType.DMA((gathered, 4 * zs))] * 2
    scratch += [pltpu.SemaphoreType.DMA((gathered,))] * 2
    scratch += [pltpu.SemaphoreType.DMA((summed, zs + 2))] * 2
    scratch += [pltpu.SemaphoreType.DMA((4, 3))] * 2
    scratch += [pltpu.SemaphoreType.DMA((2, zs + 2))] * 2
    scratch += [pltpu.SemaphoreType.DMA((8,))] * 2
    in_vmem = pl.BlockSpec(memory_space=pltpu.VMEM)
    anywhere = pl.BlockSpec(memory_space=pl.ANY)
    return pl.pallas_call(
        functools.partial(kernel, sub, zs),
        out_shape=(
            jax.ShapeDtypeStruct(tokens.shape, BF16),
            jax.ShapeDtypeStruct(tokens.shape, BF16),
            jax.ShapeDtypeStruct(attention.shape, F32),
            jax.ShapeDtypeStruct(expand.shape, F32),
            jax.ShapeDtypeStruct(reduce_t.shape, F32),
            jax.ShapeDtypeStruct(vectors.shape, F32),
        ),
        in_specs=[anywhere] * 2 + [in_vmem] * 5,
        out_specs=(anywhere, anywhere) + (in_vmem,) * 4,
        scratch_shapes=scratch,
        compiler_params=pltpu.CompilerParams(
            collective_id=0, has_side_effects=True, vmem_limit_bytes=65400 * 1024
        ),
    )(tokens, cotangent, span_mask, vectors, attention, expand, reduce_t)


def update_kernel(rates, *refs):
    count = len(rates)
    ins, (result, grad) = refs[: 4 * count], refs[4 * count : 4 * count + 2]
    outs, (result_out, grad_out) = refs[4 * count + 2 : 7 * count + 2], refs[7 * count + 2 : 7 * count + 4]
    held, (low, wide, passed) = refs[7 * count + 4 : 11 * count + 4], refs[11 * count + 4 : 11 * count + 7]
    in_sems, out_sems = refs[11 * count + 7 :]
    loads = [pltpu.make_async_copy(ins[n], held[n], in_sems.at[n]) for n in range(4 * count)]
    stores = [pltpu.make_async_copy(held[4 * n + m], outs[3 * n + m], out_sems.at[3 * n + m])
              for n in range(count) for m in range(3)]
    load_grad = pltpu.make_async_copy(grad, low, in_sems.at[4 * count])
    store_grad = pltpu.make_async_copy(wide, grad_out, out_sems.at[3 * count])
    load_result = pltpu.make_async_copy(result, passed, in_sems.at[4 * count + 1])
    store_result = pltpu.make_async_copy(passed, result_out, out_sems.at[3 * count + 1])
    load_grad.start()
    load_result.start()
    for copy in loads:
        copy.start()
    load_result.wait()
    store_result.start()
    load_grad.wait()

    def widen(s, carry):
        wide[s] = low[s].astype(F32)
        return carry

    lax.fori_loop(0, low.shape[0], widen, 0)
    store_grad.start()
    for n in range(count):
        for m in range(4):
            loads[4 * n + m].wait()
        weight, one, two, gradient = held[4 * n : 4 * n + 4]
        values = adamw(weight[...], one[...], two[...], gradient[...], rates[n])
        for ref, value in zip((weight, one, two), values):
            ref[...] = value
        for m in range(3):
            stores[3 * n + m].start()
    for copy in stores + [store_grad, store_result]:
        copy.wait()


def update(rates, arrays, result, grad):
    flat = [value for group in arrays for value in group]
    new = [jax.ShapeDtypeStruct(value.shape, F32) for group in arrays for value in group[:3]]
    new += [jax.ShapeDtypeStruct(result.shape, BF16), jax.ShapeDtypeStruct(grad.shape, F32)]
    anywhere = pl.BlockSpec(memory_space=pl.ANY)
    scratch = [pltpu.VMEM(value.shape, F32) for value in flat]
    scratch += [pltpu.VMEM(grad.shape, BF16), pltpu.VMEM(grad.shape, F32), pltpu.VMEM(result.shape, BF16)]
    scratch += [pltpu.SemaphoreType.DMA((len(flat) + 2,)), pltpu.SemaphoreType.DMA((len(new),))]
    return pl.pallas_call(
        functools.partial(update_kernel, rates),
        out_shape=tuple(new),
        in_specs=[anywhere] * (len(flat) + 2),
        out_specs=(anywhere,) * len(new),
        scratch_shapes=scratch,
        compiler_params=pltpu.CompilerParams(vmem_limit_bytes=63 * 1024 * 1024),
    )(*flat, result, grad)


def local(
    sub,
    tokens,
    cotangent,
    span_mask,
    attention_weight,
    expand_weight,
    reduce_weight,
    vectors,
    attention_first,
    attention_second,
    expand_first,
    expand_second,
    reduce_first,
    reduce_second,
    vector_first,
    vector_second,
):
    together = [[n * sub + m for m in range(sub)] for n in range(GROUPS)]

    def widen(value, axis):
        if sub == 1:
            return value
        low = lax.all_gather(
            value.astype(BF16), "batch", axis=axis, tiled=True, axis_index_groups=together
        )
        return low.astype(F32)

    def narrow(value, axis):
        if sub == 1:
            return value
        return lax.psum_scatter(
            value, "batch", scatter_dimension=axis, tiled=True, axis_index_groups=together
        )

    out_tokens, input_grad, ga, g1, g2, gv = layer(
        sub,
        tokens,
        cotangent,
        span_mask,
        widen(vectors, 1),
        widen(attention_weight, 2),
        widen(expand_weight, 1),
        widen(reduce_weight.T, 0),
    )
    arrays = (
        (attention_weight, attention_first, attention_second, narrow(ga, 2)),
        (expand_weight, expand_first, expand_second, narrow(g1, 1)),
        (reduce_weight.T, reduce_first.T, reduce_second.T, narrow(g2, 0)),
        (vectors, vector_first, vector_second, narrow(gv, 1)),
    )
    rates = (rate_attention, rate_expand, rate_reduce, rate_vector)
    new = update(rates, arrays, out_tokens, input_grad)
    return new[-2:] + new[0:6] + tuple(value.T for value in new[6:9]) + new[9:12]


def solution(mesh):
    sub = mesh.shape["batch"] // GROUPS
    sequences = P("batch", "blk", None)
    attention = P(None, "blk", "batch")
    matrix = P("blk", "batch")
    return jax.shard_map(
        functools.partial(local, sub),
        mesh=mesh,
        in_specs=(sequences, sequences, P("batch", "blk"), attention, matrix, matrix, matrix)
        + (attention,) * 2
        + (matrix,) * 6,
        out_specs=(sequences,) * 2 + (attention,) * 3 + (matrix,) * 9,
        check_vma=False,
    )
```

```python
import functools
import math

import jax
import jax.numpy as jnp
from jax import lax
from jax.experimental import pallas as pl
from jax.experimental.pallas import tpu as pltpu
from jax.sharding import PartitionSpec as P

HEADS = 12
HEAD = 64
STEP = 10
GROUPS = 8

norm_epsilon = 1e-05
beta_one = 0.9
beta_two = 0.999
adam_epsilon = 1e-08
decay_weight = 0.1
rate_attention = 0.05
rate_expand = 0.03
rate_reduce = 0.015
rate_vector = 0.4

F32 = jnp.float32
BF16 = jnp.bfloat16
MESH = pl.DeviceIdType.MESH
GELU_SCALE = math.sqrt(2.0 / math.pi)
GELU_CUBE = 0.044715


def adamw(weight, moment_one, moment_two, gradient, step_rate):
    moment_one = beta_one * moment_one + (1.0 - beta_one) * gradient
    moment_two = beta_two * moment_two + (1.0 - beta_two) * gradient * gradient
    corrected_one = moment_one / (1.0 - beta_one**STEP)
    corrected_two = moment_two / (1.0 - beta_two**STEP)
    updated = weight - step_rate * (
        corrected_one / (jnp.sqrt(corrected_two) + adam_epsilon) + decay_weight * weight
    )
    return (updated, moment_one, moment_two)


def dot_nn(left, right):
    return lax.dot_general(left, right, (((1,), (0,)), ((), ())), preferred_element_type=F32)


def dot_nt(left, right):
    return lax.dot_general(left, right, (((1,), (1,)), ((), ())), preferred_element_type=F32)


X, Y, Z = 1, 2, 4
(N_QKA, N_QKB, N_VOA, N_VOB, N_W10A, N_W10B, N_W11A, N_W11B, N_W20A, N_W20B, N_W21A, N_W21B) = range(12)
(N_AQKA, N_AQKB, N_AVO, N_G10A, N_G10B, N_G11A, N_G11B, N_G20A, N_G20B, N_G21A, N_G21B) = range(11)
QK, VO = (N_QKA, N_QKB), (N_VOA, N_VOB)
AQK, AVO = (N_AQKA, N_AQKB), (N_AVO, N_AVO)
SEND, GOT, WHOLE, SUM, VEC, SMALL, DO = range(7)
(TOK, COT, OUT, IG, TOK_HERE, COT_HERE, OUT_HERE,
 IG_HERE, SWAP_HERE, N2S_HERE, COTS_HERE, BACKS_HERE, AHEADS_HERE) = range(13)
GATHER_ROUTES = (
    ((Z, Y, X), (Z, X, Y),),
    ((Y, Z, X), (Z, X, Y),),
    ((Z, X, Y), (Z, Y, X),),
    ((Z, Y, X), (Y, Z, X),),
    ((Z, X, Y), (Z, Y, X),),
    ((Y, Z, X), (X, Y, Z),),
)
SUM_ROUTES = (
    ((X, Z, Y), (X, Z, Y),),
    ((Y, X, Z),),
    ((Y, X, Z), (X, Z, Y),),
    ((X, Z, Y), (Y, X, Z),),
    ((X, Z, Y), (Z, X, Y),),
    ((Y, X, Z), (Y, X, Z),),
)
PLAN = dict(
    own1=(
        (SEND, N_QKA, 0, Z), (SEND, N_QKB, 0, Z),
    ),
    ownff=(
        (SEND, N_VOA, 0, Y), (DO, TOK), (SEND, N_VOB, 0, Z), (DO, SWAP_HERE),
    ),
    mask=(
        (SEND, N_VOA, 0, Z), (SEND, N_W21B, 0, X), (GOT, N_QKA, Z), (SEND, N_QKA, Z, X), (VEC, 0),
        (SEND, N_QKA, Z, Y), (SEND, N_W11B, 0, Y), (SEND, N_W11A, 0, Z), (GOT, N_VOA, Y), (VEC, 1),
        (GOT, N_QKB, Z),
    ),
    ln1=(
        (SEND, N_QKB, Z, X), (GOT, N_VOB, Z), (SEND, N_QKB, Z, Y), (SEND, N_VOA, Y, Z), (VEC, 2),
        (SEND, N_VOB, Z, X), (GOT, N_QKB, Z | X), (GOT, N_VOA, Z), (SEND, N_QKB, Z | X, Y),
        (GOT, N_QKA, Z | Y), (GOT, N_QKA, Z | X), (SEND, N_QKA, Z | Y, X), (SEND, N_VOB, Z, Y),
        (SEND, N_VOA, Z, X), (SEND, N_W10A, 0, Z), (GOT, N_W11A, Z), (SEND, N_W10B, 0, Z),
        (GOT, N_VOA, Y | Z), (DO, TOK_HERE), (GOT, N_QKB, Z | Y), (SEND, N_W11A, Z, Y), (SEND, N_W11A, Z, X),
        (SEND, N_VOA, Y | Z, X), (VEC, 3), (SEND, N_W11B, 0, Z),
    ),
    unp0=(
        (GOT, N_QKA, Z | Y | X), (GOT, N_QKB, Z | X | Y), (GOT, N_VOB, Z | X), (GOT, N_W10A, Z),
        (SEND, N_W10A, Z, Y), (SEND, N_W10A, Z, X), (WHOLE, N_QKA), (WHOLE, N_QKB),
    ),
    projq=(
        (GOT, N_VOA, Z | X),
    ),
    projk=(
        (GOT, N_W11A, Z | Y),
    ),
    attend0=(
        (SEND, N_W20A, 0, Z), (SEND, N_W20B, 0, Z), (SEND, N_W11A, Z | Y, X), (SEND, N_VOB, Z | X, Y),
        (GOT, N_VOB, Z | Y), (GOT, N_W10B, Z), (SEND, N_W10B, Z, X), (GOT, N_VOA, Y | Z | X),
    ),
    attend2=(
        (GOT, N_W21B, X), (GOT, N_W11B, Z), (GOT, N_W11B, Y),
    ),
    attend3=(
        (SEND, N_W10B, Z, Y), (SEND, N_W21B, X, Y), (SEND, N_W11B, Z, X), (GOT, N_VOB, Z | X | Y),
    ),
    attend4=(
        (GOT, N_W10A, Z | X), (DO, COT), (SEND, N_W11B, Y, Z), (GOT, N_W21B, X | Y), (GOT, N_W10B, Z | Y),
        (SEND, N_W10B, Z | Y, X), (WHOLE, N_VOA), (WHOLE, N_VOB),
    ),
    attend5=(
        (GOT, N_W10B, Z | X),
    ),
    unp1=(
        (GOT, N_W20B, Z), (SEND, N_W21A, 0, Z), (GOT, N_W11A, Z | Y | X), (SEND, N_W21B, X | Y, Z),
    ),
    projv=(
        (SEND, N_W10A, Z | X, Y), (SEND, N_W21A, 0, Y), (SEND, N_W21B, 0, Z), (GOT, N_W11B, Y | Z),
    ),
    mix0=(
        (SEND, N_W11B, Y | Z, X), (GOT, N_W10B, Z | Y | X), (GOT, N_W20A, Z), (SEND, N_W21B, X, Z),
    ),
    mix2=(
        (SEND, N_W21B, 0, Y),
    ),
    mix4=(
        (SEND, N_W20A, Z, X), (SEND, N_W20B, Z, Y),
    ),
    mix5=(
        (DO, COT_HERE), (GOT, N_W11B, Z | X),
    ),
    ao=(
        (GOT, N_W11B, Y | Z | X),
    ),
    ln2=(
        (GOT, N_W11A, Z | X), (SEND, N_W20B, Z, X), (GOT, N_W10A, Z | Y),
    ),
    expa0=(
        (GOT, N_W21A, Z), (GOT, N_W21B, X | Y | Z), (SEND, N_W21A, Z, X), (GOT, N_W10A, Z | X | Y),
    ),
    expa1=(
        (DO, COTS_HERE), (GOT, N_W21B, Z),
    ),
    expb0=(
        (GOT, N_W20A, Z | X), (GOT, N_W21A, Y), (SEND, N_W20A, Z, Y), (SEND, N_W21A, Y, Z), (DO, N2S_HERE),
    ),
    expb1=(
        (GOT, N_W21B, Y),
    ),
    trY=(
        (GOT, N_W20B, Z | Y), (SEND, N_W20B, Z | Y, X), (GOT, N_W21B, X | Z),
    ),
    gw2_0=(
        (SEND, N_W20A, Z | X, Y), (SEND, N_W21B, Y, Z),
    ),
    gw2_1=(
        (GOT, N_W21A, Y | Z), (GOT, N_W21A, Z | X), (SEND, N_W21A, Y | Z, X),
    ),
    innb0=(
        (SUM, N_G20B, 0), (GOT, N_W20B, Z | X), (GOT, N_W20A, Z | Y), (SUM, N_G21A, 0),
        (GOT, N_W20B, Z | Y | X), (SUM, N_G20A, 0), (GOT, N_W20A, Z | X | Y), (GOT, N_W21B, Y | Z),
        (SUM, N_G21B, 0), (GOT, N_W21A, Y | Z | X),
    ),
    gw1_0=(
        (SUM, N_G21A, 1),
    ),
    hid=(
        (SUM, N_G10B, 0), (SUM, N_G20A, 1), (DO, BACKS_HERE), (SUM, N_G10A, 0),
    ),
    reda=(
        (SUM, N_G11A, 0), (SUM, N_G21A, 2),
    ),
    outst=(
        (SUM, N_G11B, 0), (SUM, N_G21B, 1), (SUM, N_G10B, 1), (SUM, N_G10A, 1), (DO, AHEADS_HERE),
    ),
    ab0=(
        (DO, OUT),
    ),
    ab3=(
        (SUM, N_G11A, 1),
    ),
    gaqk=(
        (SUM, N_G11B, 1),
    ),
    dn1=(
        (SUM, N_G21B, 2), (SUM, N_G20B, 1), (SUM, N_AVO, 0),
    ),
    inb=(
        (SUM, N_AQKA, 0), (SUM, N_G10A, 2), (SUM, N_G11B, 2), (SUM, N_G10B, 2), (DO, OUT_HERE),
        (SUM, N_G11A, 2), (SUM, N_AQKB, 0),
    ),
    end=(
        (SUM, N_G20B, 2), (SUM, N_AQKA, 1), (SUM, N_AVO, 1), (SUM, N_AQKB, 1), (SUM, N_G20B, 3), (DO, IG),
        (SUM, N_AVO, 2), (SMALL, 0), (SUM, N_G21A, 3), (SUM, N_G21B, 3), (SMALL, 1), (SUM, N_G11A, 3),
        (SUM, N_AQKA, 2), (SUM, N_G11B, 3), (SUM, N_G10B, 3), (SUM, N_G10A, 3), (SUM, N_G20A, 2),
        (DO, IG_HERE), (SUM, N_AQKB, 2), (SUM, N_AQKA, 3), (SMALL, 2), (SUM, N_AVO, 3), (SUM, N_AQKB, 3),
        (SUM, N_G20A, 3), (SMALL, 3),
    ),
)


def lane_tiles(ref, count=6):
    return jnp.concatenate([ref[t] for t in range(count)], axis=1)


class Unit:
    def __init__(self, index, route, rows, u, other):
        self.index, self.route, self.rows, self.u, self.other = index, route, rows, u, other


class Gradient:
    def __init__(self, index, route, rows, u, other, core_in, got, total):
        self.index, self.route, self.rows, self.u, self.other = index, route, rows, u, other
        self.core_in, self.got, self.total = core_in, got, total


def kernel(sub, zs, *refs):
    (tok, cot, mask_in, vec_in, a_in, w1_in, w2_in,
     out, ig, ga, g1, g2, gv,
     ua, uw1, uw2, gw1, gw2, core_in, got,
     x_in, cot_in, stage, vec, gvec, vin, gin, narrow_rows,
     at, n1, q6, k6, v6, o6, pt, h1, acc, n2, act, gp, ta, tb, tc, d6,
     w1_other, w2_other, n2_other, cot_other, back_in, ahead_in,
     lines, b1, gb1, totals, turned1, got1, got2,
     local_sem, ag_send, ag_recv, core_send, core_recv, rs_send, rs_recv,
     a2a_send, a2a_recv, v_send, v_recv, pair_send, pair_recv) = refs

    i = lax.axis_index("blk")
    b = lax.axis_index("batch")
    c, y = lax.rem(i, 2), lax.div(i, 2)
    g, r = lax.div(b, sub), lax.rem(b, sub)
    x, z = lax.rem(g, 2), lax.div(g, 2)

    def device(c_=c, y_=y, x_=x, z_=z):
        return {"blk": 2 * y_ + c_, "batch": (2 * z_ + x_) * sub + r}

    def z_at(k):
        return lax.rem(z + k, zs)

    def block_at(k):
        return lax.rem(i + k, 4)

    def copy(src, dst, send, recv, to):
        return pltpu.make_async_remote_copy(
            src_ref=src, dst_ref=dst, send_sem=send, recv_sem=recv, device_id=to, device_id_type=MESH
        )

    def loop(count, body, hooks=()):
        def step(s, carry):
            body(s)
            for k, f in hooks:
                pl.when(s == k)(f)
            return carry

        lax.fori_loop(0, count, step, 0)

    partners = [device(z_=z_at(k)) for k in range(1, zs)]
    partners += [device(x_=1 - x), device(y_=1 - y), device(c_=1 - c), device(c_=1 - c, y_=1 - y)]
    barrier = pltpu.get_barrier_semaphore()
    for partner in partners:
        pl.semaphore_signal(barrier, inc=1, device_id=partner, device_id_type=MESH)
    pl.semaphore_wait(barrier, len(partners))

    ME = {"y": y, "x": x, "z": z}

    def before(n, axis, other):
        return n.route.index(axis) < n.route.index(other)

    def side(n, axes, all_z):
        where = (1 - y if "y" in axes else y, 1 - x if "x" in axes else x, slice(None) if all_z else z)
        return n.u.at[where + (n.rows,)]

    def neighbour(axis):
        return device(y_=1 - y) if axis == "y" else device(x_=1 - x)

    def ag_copy(n, ref, axes, k, to):
        slot = (("y" in axes) * 2 + ("x" in axes)) * zs + k
        return copy(ref, ref, ag_send.at[n.index, slot], ag_recv.at[n.index, slot], to)

    def core_copy(n, ref):
        return copy(ref, ref, core_send.at[n.index], core_recv.at[n.index], device(c_=1 - c))

    def ag_sends(n, axes, axis):
        axes = axes.replace("z", "")
        if axis == "z":
            ref = side(n, axes, False)
            return [ag_copy(n, ref, axes, k, device(z_=z_at(k))) for k in range(1, zs)]
        ref = side(n, axes, before(n, "z", axis))
        return [ag_copy(n, ref, axes + axis, 0, neighbour(axis))]

    def ag_send_part(n, axes, axis):
        for moved in ag_sends(n, axes, axis):
            moved.start()

    def ag_wait_part(n, axes):
        last = max(axes, key=n.route.index)
        axes = axes.replace("z", "")
        if last == "z":
            yy, xx = (1 - y if "y" in axes else y), (1 - x if "x" in axes else x)
            for k in range(1, zs):
                ag_copy(n, n.u.at[yy, xx, z_at(zs - k), n.rows], axes, k, device()).wait_recv()
        else:
            ag_copy(n, side(n, axes, before(n, "z", last)), axes, 0, device()).wait_recv()
        if n.other is not None and (last == "z" or before(n, "z", last)):
            core_copy(n, side(n, axes, True)).start()

    def ag_done(n):
        if n.other is not None:
            core_copy(n, n.other.at[:, :, :, n.rows]).wait_recv()

    def ag_drain(n):
        for axis in n.route:
            earlier = [other for other in "yx" if before(n, other, axis)]
            for some in range(2 ** len(earlier)):
                axes = "".join(other for bit, other in enumerate(earlier) if some >> bit & 1)
                for moved in ag_sends(n, axes, axis):
                    moved.wait_send()
        if n.other is not None:
            core_copy(n, n.u.at[:, :, :, n.rows]).wait_send()

    AXES = "yxz"

    def rs_groups(n, step):
        axis = n.route[step]
        if axis == "z":
            return [(k, 1 + k, device(z_=z_at(zs - k))) for k in range(1, zs)]
        return [(1, "yx".index(axis), neighbour(axis))]

    def rs_where(n, step, k):
        axis, out, land = n.route[step], [], []
        for other in AXES:
            if other == axis:
                out.append(z_at(zs - k) if axis == "z" else 1 - ME[axis])
                land.append(k)
            elif before(n, other, axis):
                out.append(ME[other])
                land.append(0)
            else:
                out.append(slice(None))
                land.append(slice(None))
        return tuple(out) + (n.rows,), tuple(land) + (n.rows,)

    def rs_copy(n, step, k, slot, to):
        out, land = rs_where(n, step, k)
        return copy(n.u.at[out], n.got.at[land], rs_send.at[n.index, slot], rs_recv.at[n.index, slot], to)

    def rs_core(n):
        return copy(n.other.at[:, :, :, n.rows], n.core_in.at[:, :, :, n.rows], rs_send.at[n.index, zs + 1],
                    rs_recv.at[n.index, zs + 1], device(c_=1 - c))

    def add_terms(n, place, step):
        value = n.u[tuple(place) + (n.rows,)].astype(F32)
        if n.other is not None:
            value = value + n.core_in[tuple(place) + (n.rows,)].astype(F32)
        for axis in n.route[:step]:
            for k in range(1, zs) if axis == "z" else (1,):
                where = [k if other == axis else (0 if before(n, other, axis) else at_place)
                         for other, at_place in zip(AXES, place)]
                value = value + n.got[tuple(where) + (n.rows,)].astype(F32)
        return value

    def rs_start(n):
        rs_core(n).start()

    def rs_step(n, step):
        if step == 0 and n.other is not None:
            rs_core(n).wait_recv()
        if step > 0:
            for group in rs_groups(n, step - 1):
                rs_copy(n, step - 1, *group).wait_recv()
        if step == 3:
            n.total[n.rows, :] = add_terms(n, (y, x, z), 3)
            return
        for k, slot, to in rs_groups(n, step):
            out, _ = rs_where(n, step, k)
            if step > 0 or n.other is not None:
                spans = [range(2) if isinstance(at_place, slice) else (at_place,) for at_place in out[:2]]

                def body(zz):
                    for yy in spans[0]:
                        for xx in spans[1]:
                            n.u[yy, xx, zz, n.rows] = add_terms(n, (yy, xx, zz), step).astype(BF16)

                if isinstance(out[2], slice):
                    loop(zs, body)
                else:
                    body(out[2])
            rs_copy(n, step, k, slot, to).start()

    def rs_drain(n):
        if n.other is not None:
            rs_core(n).wait_send()
        for step in range(3):
            for group in rs_groups(n, step):
                rs_copy(n, step, *group).wait_send()

    def small_sum(ref, slots, which):
        to = (device(y_=1 - y), device(c_=1 - c), device(x_=1 - x))
        to += tuple(device(z_=z_at(k)) for k in range(1, zs))

        def moved(slot):
            return copy(ref, slots.at[slot], v_send.at[which, slot], v_recv.at[which, slot], to[slot])

        def land(last):
            moved(last).wait()
            ref[...] = ref[...] + slots[last]

        def step(n):
            def run():
                if n > 0:
                    land(n - 1)
                moved(n).start()

            return run

        def line():
            land(2)
            for k in range(1, zs):
                moved(2 + k).start()

        def finish():
            for k in range(1, zs):
                moved(2 + k).wait()
            value = ref[...]
            for k in range(1, zs):
                value = value + slots[2 + k]
            ref[...] = value

        return [step(0), step(1), step(2), line, finish]

    def rows_of(s):
        return pl.ds(pl.multiple_of(s * 128, 128), 128)

    def exchange(src, dst, which):
        return [copy(src.at[block_at(k)], dst.at[i], a2a_send.at[which, k - 1],
                     a2a_recv.at[which, k - 1], {"blk": block_at(k), "batch": b})
                for k in range(1, 4)]

    def exchange_landed(dst, which):
        return [copy(dst.at[block_at(4 - k)], dst.at[block_at(4 - k)], a2a_send.at[which, k - 1],
                     a2a_recv.at[which, k - 1], {"blk": block_at(4 - k), "batch": b})
                for k in range(1, 4)]

    def axes_of(mask):
        return "".join(axis for axis, bit in (("y", Y), ("x", X), ("z", Z)) if mask & bit)

    def rows_in(part, count):
        return pl.ds(part * (288 // count), 288 // count)

    units = []
    for unit, routes in enumerate(GATHER_ROUTES):
        half = unit % 2
        ref = (ua, uw1, uw2)[unit // 2]
        pieces = (ref.at[half, c], ref.at[half, 1 - c]) if unit < 2 else (ref.at[half], None)
        for part, route in enumerate(routes):
            units.append(Unit(len(units), "".join(map(axes_of, route)), rows_in(part, len(routes)), *pieces))

    def pair(slot, src, dst):
        return copy(src, dst, pair_send.at[slot], pair_recv.at[slot], device(c_=1 - c))

    w1_swap, w2_swap = pair(0, w1_in, w1_other), pair(1, w2_in, w2_other)

    def each_core(f):
        for q in range(2):
            pl.when(c == q)(functools.partial(f, q))

    def rest_rows(matrix):
        return a_in[matrix, pl.ds(pl.multiple_of(128 * (1 - c), 64), 64), :]

    def own_attention(p):
        mine = ua.at[p, c, y, x, z]
        for m in range(2):
            main = a_in[2 * p + m, pl.ds(pl.multiple_of(64 * c, 64), 128), :]
            mine[96 * m : 96 * m + 96, :] = main.T.astype(BF16)
        rest = jnp.concatenate([rest_rows(2 * p + c), rest_rows(2 * p + 1 - c)], axis=0)
        mine[192:288, :] = rest.T.astype(BF16)

    def own_expand(q):
        both = (w1_in, w1_other) if q == 0 else (w1_other, w1_in)
        cols = slice(192 * q, 192 * q + 192)
        blocks = (
            both[0][0:128, cols],
            jnp.concatenate([both[0][128:192, cols], both[1][0:64, cols]], axis=0),
            both[1][64:192, cols],
        )
        for t, block in enumerate(blocks):
            value = block.T.astype(BF16)
            for h in range(2):
                uw1[h, y, x, z, 96 * t : 96 * t + 96, :] = value[96 * h : 96 * h + 96, :]

    def own_reduce(q):
        both = (w2_in, w2_other) if q == 0 else (w2_other, w2_in)
        for cc in range(2):
            for part_of in range(2):
                start = 384 * part_of + 192 * q
                lines[:, 192 * part_of : 192 * part_of + 192] = both[cc][:, start : start + 192]
            for t in range(3):
                uw2[cc, y, x, z, 96 * t : 96 * t + 96, :] = lines[:, 128 * t : 128 * t + 128].astype(BF16)

    def own_hidden_bias(q):
        for zz in range(zs):
            for xx in range(2):
                col = 384 * (zz % 2) + 192 * xx
                start = 384 * xx + 192 * q
                b1[zz // 2 : zz // 2 + 1, col : col + 192] = vec[8 + zz : 9 + zz, start : start + 192]

    def hidden_bias_gradient(q):
        for zz in range(zs):
            for xx in range(2):
                col = 384 * (zz % 2) + 192 * xx
                start = 384 * xx + 192 * q
                gvec[8 + zz : 9 + zz, start : start + 192] = gb1[zz // 2 : zz // 2 + 1, col : col + 192]

    columns = a_in.shape[2]
    placed = lax.broadcasted_iota(jnp.int32, (columns, 768), 1) == (
        lax.broadcasted_iota(jnp.int32, (columns, 768), 0) + columns * g
    )

    def own_vectors():
        vec[...] = jnp.zeros_like(vec)
        rows = dot_nn(vec_in[...].astype(BF16), jnp.where(placed, 1.0, 0.0).astype(BF16))
        for j in range(3):
            vec[pl.ds(3 * i + j, 1), :] = rows[j : j + 1, :]

    load_cot = pltpu.make_async_copy(cot, stage, local_sem.at[4])

    def masked_cotangent():
        load_cot.wait()
        eye = lax.broadcasted_iota(jnp.int32, (128, 128), 0) == lax.broadcasted_iota(jnp.int32, (128, 128), 1)
        for s in range(4):
            row = jnp.broadcast_to(mask_in[s : s + 1, :].astype(F32), (128, 128))
            column = jnp.sum(jnp.where(eye, row, 0.0), axis=1, keepdims=True)
            stage[s] = (stage[s].astype(F32) * column).astype(BF16)

    def finish_attention(p):
        value = totals.at[p]
        for m in range(2):
            ga[2 * p + m, pl.ds(pl.multiple_of(64 * c, 64), 128), :] = value[96 * m : 96 * m + 96, :].T
        rest = value[192:288, :].T
        rows = pl.ds(pl.multiple_of(128 * (1 - c), 64), 64)
        ga[2 * p + c, rows, :] = rest[0:64, :]
        ga[2 * p + 1 - c, rows, :] = rest[64:128, :]

    w1_back = pair(6, turned1.at[pl.ds(pl.multiple_of(192 * (1 - c), 64), 192)], got1)
    w2_back = pair(7, totals.at[5 - c], got2)

    def turn_expand():
        for h in range(2):
            for t in range(3):
                turned1[128 * t : 128 * t + 128, 96 * h : 96 * h + 96] = totals[2 + h, 96 * t : 96 * t + 96, :].T
        w1_back.start()

    def join_expand(q):
        g1[:, 192 * q : 192 * q + 192] = turned1[192 * q : 192 * q + 192, :]
        g1[:, 192 * (1 - q) : 192 * (1 - q) + 192] = got1[...]

    def join_reduce(q):
        for half, value in ((q, totals.at[4 + q]), (1 - q, got2)):
            for t in range(3):
                lines[:, 128 * t : 128 * t + 128] = value[96 * t : 96 * t + 96, :]
            for part_of in range(2):
                start = 384 * part_of + 192 * half
                g2[:, start : start + 192] = lines[:, 192 * part_of : 192 * part_of + 192]

    def finish_vectors():
        value, total = gvec[...], 0.0
        for _ in range(3):
            part = value.astype(BF16)
            total = total + dot_nt(part, jnp.where(placed, 1.0, 0.0).astype(BF16))
            value = value - part.astype(F32)
        narrow_rows[...] = total
        for j in range(3):
            gv[j : j + 1, :] = narrow_rows[pl.ds(3 * i + j, 1), :]

    grads, owners = [], []
    for unit, routes in enumerate(SUM_ROUTES):
        half = unit % 2
        ref = (ua, gw1, gw2)[unit // 2]
        pieces = (ref.at[half, c], ref.at[half, 1 - c], core_in.at[half]) if unit < 2 else (ref.at[half], None, None)
        for part, route in enumerate(routes):
            grads.append(Gradient(len(grads), "".join(map(axes_of, route)), rows_in(part, len(routes)), *pieces,
                                  got.at[unit], totals.at[unit]))
            owners.append(unit)

    def summed(unit):
        if unit < 2:
            finish_attention(unit)
        elif unit < 4 and {2, 3} <= set(whole):
            turn_expand()
        elif unit >= 4 and {4, 5} <= set(whole):
            w2_back.start()

    seen, whole = set(), []

    def event(kind, *rest):
        if kind == SEND:
            ag_send_part(units[rest[0]], axes_of(rest[1]), axes_of(rest[2]))
        elif kind == GOT:
            ag_wait_part(units[rest[0]], axes_of(rest[1]))
        elif kind == WHOLE:
            ag_done(units[rest[0]])
        elif kind == SUM:
            rs_step(grads[rest[0]], rest[1])
            if rest[1] == 3:
                seen.add(rest[0])
                unit = owners[rest[0]]
                if all(k in seen for k in range(len(grads)) if owners[k] == unit):
                    whole.append(unit)
                    summed(unit)
        elif kind == DO:
            actions[rest[0]]()
        else:
            (vec_steps if kind == VEC else gvec_steps)[rest[0] + 1]()

    def run(part):
        for todo in PLAN.get(part, ()):
            event(*todo)

    def parts(name, count, body):
        run(name + "0")
        hooks = [(k - 1, functools.partial(run, name + str(k))) for k in range(1, count) if name + str(k) in PLAN]
        loop(count, body, hooks)

    def started(copies):
        for moved in copies:
            moved.start()
        return copies

    def arrived(*copies):
        for moved in copies:
            moved.wait_recv()

    load_cot.start()
    own_tokens = pltpu.make_async_copy(tok.at[i], x_in.at[i], local_sem.at[0])
    own_tokens.start()
    own_cot = pltpu.make_async_copy(stage.at[i], cot_in.at[i], local_sem.at[1])
    tokens_out, cot_out = exchange(tok, x_in, 0), exchange(stage, cot_in, 1)
    result_out = exchange(stage, out, 2)
    grad_out = [copy(n1.at[rows_of(block_at(k))], ig.at[i], a2a_send.at[3, k - 1], a2a_recv.at[3, k - 1],
                     {"blk": block_at(k), "batch": b}) for k in range(1, 4)]
    own_out = pltpu.make_async_copy(stage.at[i], out.at[i], local_sem.at[2])
    own_grad = pltpu.make_async_copy(n1.at[rows_of(i)], ig.at[i], local_sem.at[3])
    n2_swap, cot_swap = pair(2, n2, n2_other), pair(3, cot_in, cot_other)
    back_swap, ahead_swap = pair(4, d6, back_in), pair(5, n2, ahead_in)
    vec_steps, gvec_steps = small_sum(vec, vin, 0), small_sum(gvec, gin, 1)

    def tokens_here():
        arrived(*exchange_landed(x_in, 0))
        own_tokens.wait()

    def cotangent_here():
        arrived(*exchange_landed(cot_in, 1))
        own_cot.wait()
        cot_swap.start()

    def swaps_here():
        w1_swap.wait()
        w2_swap.wait()

    actions = {
        TOK: lambda: started(tokens_out),
        COT: lambda: started(cot_out),
        OUT: lambda: started(result_out),
        IG: lambda: started(grad_out),
        TOK_HERE: tokens_here,
        COT_HERE: cotangent_here,
        OUT_HERE: lambda: arrived(*exchange_landed(out, 2)),
        IG_HERE: lambda: arrived(*exchange_landed(ig, 3)),
        SWAP_HERE: swaps_here,
        N2S_HERE: lambda: n2_swap.wait(),
        COTS_HERE: lambda: cot_swap.wait(),
        BACKS_HERE: lambda: back_swap.wait(),
        AHEADS_HERE: lambda: ahead_swap.wait(),
    }

    own_attention(0)
    w1_swap.start()
    w2_swap.start()
    own_vectors()
    vec_steps[0]()
    run("own1")
    own_attention(1)
    run("ownff")
    each_core(own_expand)
    each_core(own_reduce)
    run("mask")
    masked_cotangent()
    own_cot.start()
    run("ln1")
    each_core(own_hidden_bias)

    def normalise(value):
        centered = value - jnp.mean(value, axis=-1, keepdims=True)
        scale = lax.rsqrt(jnp.mean(centered * centered, axis=-1, keepdims=True) + norm_epsilon)
        return centered * scale, scale

    def first_norm(s):
        unit, _ = normalise(x_in[s].astype(F32))
        n1[rows_of(s), :] = (unit * vec[0:1, :] + vec[1:2, :]).astype(BF16)

    loop(4, first_norm)
    run("unp0")

    lanes = lax.broadcasted_iota(jnp.int32, (96, 128), 1)

    def unpack(p, s):
        for xx in range(2):
            rows = pl.ds(pl.multiple_of((2 * s + xx) * 96, 96), 96)
            for yy in range(2):
                first, second = ua.at[p, 0, yy, xx, s], ua.at[p, 1, yy, xx, s]
                lo, hi = 384 * yy, 384 * yy + 256
                for m in range(2):
                    at[2 * p + m, rows, lo : lo + 128] = first[96 * m : 96 * m + 96, :]
                    at[2 * p + m, rows, hi : hi + 128] = second[96 * m : 96 * m + 96, :]
                rest_first = first[192:288, :].astype(F32)
                rest_second = second[192:288, :].astype(F32)
                even = jnp.where(lanes < 64, rest_first, rest_second)
                odd = pltpu.roll(jnp.where(lanes < 64, rest_second, rest_first), 64, 1)
                at[2 * p, rows, lo + 128 : lo + 256] = even.astype(BF16)
                at[2 * p + 1, rows, lo + 128 : lo + 256] = odd.astype(BF16)

    def project(m, dst, bias):
        for n in range(3):
            value = dot_nt(n1[...], at[m, 256 * n : 256 * n + 256, :])
            if bias is not None:
                value = value + vec[bias : bias + 1, 256 * n : 256 * n + 256]
            value = value.astype(BF16)
            if m == 0:
                value = value * jnp.asarray(HEAD ** (-0.5), BF16)
            dst[2 * n] = value[:, 0:128]
            dst[2 * n + 1] = value[:, 128:256]

    loop(zs, functools.partial(unpack, 0))
    run("projq")
    project(0, q6, 2)
    run("projk")
    project(1, k6, None)

    half_lane = lax.broadcasted_iota(jnp.int32, (512, 128), 1) // HEAD

    def half_of(value, which):
        return jnp.where(half_lane == which, value, jnp.zeros_like(value))

    def turn(value):
        return value.astype(F32).T.astype(BF16)

    def attend(p):
        queries, keys = q6[p], k6[p]
        for which in range(2):
            scores = dot_nt(half_of(keys, which), queries)
            expo = jnp.exp(scores - jnp.max(scores, axis=0, keepdims=True))
            probs = (expo * (1.0 / jnp.sum(expo, axis=0, keepdims=True))).astype(BF16)
            pt[2 * p + which] = probs

    def mix(p):
        values_t = turn(v6[p])
        mixed = [dot_nn(values_t[64 * which : 64 * which + 64, :], pt[2 * p + which]) for which in range(2)]
        o6[p] = jnp.concatenate(mixed, axis=0).T.astype(BF16)

    parts("attend", 6, attend)
    run("unp1")
    loop(zs, functools.partial(unpack, 1))
    run("projv")
    project(2, v6, 3)
    parts("mix", 6, mix)

    run("ao")
    for n in range(3):
        cols = slice(256 * n, 256 * n + 256)
        value = dot_nt(lane_tiles(o6), at[3, cols, :]) + vec[4:5, cols]
        for s in range(4):
            h1[128 * s : 128 * s + 128, cols] = x_in[s, :, cols].astype(F32) + value[128 * s : 128 * s + 128]

    def second_norm(s):
        unit, _ = normalise(h1[rows_of(s), :])
        n2[rows_of(s), :] = (unit * vec[5:6, :] + vec[6:7, :]).astype(BF16)

    run("ln2")
    loop(4, second_norm)
    n2_swap.start()

    def expand_block(s):
        def piece(ref):
            return jnp.concatenate([ref[96 * t : 96 * t + 96, :] for t in range(3)], axis=1)

        return jnp.concatenate(
            [jnp.concatenate([piece(uw1.at[h, yy, xx, 2 * s + zz]) for yy in range(2)], axis=1)
             for zz in range(2) for xx in range(2) for h in range(2)],
            axis=0,
        )

    def reduce_block(s):
        def piece(ref):
            return jnp.concatenate([ref[96 * t : 96 * t + 96, :] for t in range(3)], axis=1)

        return jnp.concatenate(
            [jnp.concatenate([piece(uw2.at[cc, s, xx, zz]) for cc in range(2)], axis=1)
             for zz in range(zs) for xx in range(2)],
            axis=0,
        )

    def block_rows(owner, s):
        return pl.ds(pl.multiple_of((2 * owner + s) * 512, 512), 512)

    def expand(owner, normed, s):
        rows = block_rows(owner, s)
        inner = dot_nt(normed[...], expand_block(s)) + b1[pl.ds(s, 1), :]
        square = inner * inner
        tanh = jnp.tanh(GELU_SCALE * inner * (1.0 + GELU_CUBE * square))
        act[rows, :] = (0.5 * inner * (1.0 + tanh)).astype(BF16)
        slope = 0.5 * (1.0 + tanh) + 0.5 * inner * (1.0 - tanh * tanh) * (
            GELU_SCALE * (1.0 + 3.0 * GELU_CUBE * square)
        )
        gp[rows, :] = slope.astype(BF16)

    parts("expa", 2, functools.partial(expand, 0, n2))
    parts("expb", 2, functools.partial(expand, 1, n2_other))

    gvec[...] = jnp.zeros_like(gvec)

    def transpose_rows(dst, s, value):
        dst[:, 128 * s : 128 * s + 128] = turn(value)

    run("trY")
    total = jnp.zeros((1, 768), F32)
    for s in range(4):
        transpose_rows(ta, s, cot_in[s])
        total = total + jnp.sum(cot_in[s].astype(F32), axis=0, keepdims=True)
    gvec[7:8, :] = total
    for s in range(4):
        transpose_rows(tb, s, cot_other[s])

    def both_rows(ref, s):
        return jnp.concatenate([ref[block_rows(0, s), :], ref[block_rows(1, s), :]], axis=0)

    def reduce_back(s):
        grad = dot_nn(jnp.concatenate([ta[...], tb[...]], axis=1), both_rows(act, s)).astype(BF16)
        for zz in range(zs):
            for xx in range(2):
                row = 96 * (2 * zz + xx)
                for cc in range(2):
                    for t in range(3):
                        col = 384 * cc + 128 * t
                        gw2[cc, s, xx, zz, 96 * t : 96 * t + 96, :] = grad[row : row + 96, col : col + 128]

    parts("gw2_", 2, reduce_back)

    def rows_together(ref):
        return jnp.concatenate([ref[s] for s in range(4)], axis=0)

    def inner_back(owner, cotangent_rows, s):
        rows = block_rows(owner, s)
        grad = dot_nn(rows_together(cotangent_rows), reduce_block(s)) * gp[rows, :].astype(F32)
        low = grad.astype(BF16)
        gp[rows, :] = low
        sums = jnp.sum(low.astype(F32), axis=0, keepdims=True)
        gb1[pl.ds(s, 1), :] = sums if owner == 1 else gb1[pl.ds(s, 1), :] + sums

    def norm_back(owner):
        acc[...] = dot_nn(gp[block_rows(owner, 0), :], expand_block(0))
        acc[...] += dot_nn(gp[block_rows(owner, 1), :], expand_block(1))

    parts("innb", 2, functools.partial(inner_back, 1, cot_other))
    run("dn2b")
    norm_back(1)
    for t in range(6):
        d6[t] = acc[:, 128 * t : 128 * t + 128].astype(BF16)
    back_swap.start()
    parts("inna", 2, functools.partial(inner_back, 0, cot_in))
    each_core(hidden_bias_gradient)
    run("dn2a")
    norm_back(0)

    def expand_back(s):
        turned = jnp.concatenate([turn(gp[block_rows(owner, s), :]) for owner in range(2)], axis=1)
        normed = jnp.concatenate([n2[...], n2_other[...]], axis=0)
        grad = dot_nn(turned, normed).astype(BF16)
        for zz in range(2):
            for xx in range(2):
                for h in range(2):
                    row = 384 * zz + 192 * xx + 96 * h
                    for yy in range(2):
                        for t in range(3):
                            col = 384 * yy + 128 * t
                            gw1[h, yy, xx, 2 * s + zz, 96 * t : 96 * t + 96, :] = grad[
                                row : row + 96, col : col + 128
                            ]

    parts("gw1_", 2, expand_back)
    run("hid")

    def norm_gradient(value, scale_row, grad):
        unit, scale = normalise(value)
        gain_sum = jnp.sum(grad * unit, axis=0, keepdims=True)
        bias_sum = jnp.sum(grad, axis=0, keepdims=True)
        inner = grad * scale_row
        mean = jnp.mean(inner, axis=-1, keepdims=True)
        along = jnp.mean(inner * unit, axis=-1, keepdims=True)
        return scale * (inner - mean - unit * along), gain_sum, bias_sum

    def hidden_back(s):
        rows = rows_of(s)
        grad_in = jnp.concatenate([back_in[t, rows, :] for t in range(6)], axis=1)
        grad_in = acc[rows, :] + grad_in.astype(F32)
        grad, gain_sum, bias_sum = norm_gradient(h1[rows, :], vec[5:6, :], grad_in)
        grad = grad + cot_in[s].astype(F32)
        acc[rows, :] = grad
        low = grad.astype(BF16)
        n2[rows, :] = low
        gvec[5:6, :] += gain_sum
        gvec[6:7, :] += bias_sum
        gvec[4:5, :] += jnp.sum(low.astype(F32), axis=0, keepdims=True)

    loop(4, hidden_back)

    run("dO")
    for n in range(3):
        value = dot_nn(n2[...], at[3, :, 256 * n : 256 * n + 256]).astype(BF16)
        d6[2 * n] = value[:, 0:128]
        d6[2 * n + 1] = value[:, 128:256]
    run("gao")
    for s in range(4):
        transpose_rows(tc, s, n2[128 * s : 128 * s + 128, :])
    gp[768:1536, :] = dot_nn(tc[...], lane_tiles(o6)).astype(BF16)

    def reduce(owner):
        value = dot_nt(act[block_rows(owner, 0), :], reduce_block(0))
        return value + dot_nt(act[block_rows(owner, 1), :], reduce_block(1))

    def layer_output():
        run("redb")
        n2[...] = reduce(1).astype(BF16)
        ahead_swap.start()
        run("reda")
        h1[...] = h1[...] + vec[7:8, :] + reduce(0)
        run("outst")
        for moved in cot_out:
            moved.wait_send()
        for s in range(4):
            rows = slice(128 * s, 128 * s + 128)
            stage[s] = (h1[rows, :] + ahead_in[rows, :].astype(F32)).astype(BF16)
        own_out.start()

    layer_output()

    def value_back(p):
        grads_in, grad_value = d6[p], 0.0
        for which in range(2):
            grad_value = grad_value + dot_nn(pt[2 * p + which], half_of(grads_in, which))
        tc[rows_of(p), :] = grad_value.T.astype(BF16)
        o6[p] = grad_value.astype(BF16)

    def attend_back(p):
        rows = rows_of(p)
        queries, keys, values, grads_in = q6[p], k6[p], v6[p], d6[p]
        keys_t = turn(keys)
        grad_query, grad_key = [], 0.0
        for which in range(2):
            wide = pt[2 * p + which].astype(F32)
            grad_probs = dot_nt(half_of(values, which), grads_in)
            inner = jnp.sum(wide * grad_probs, axis=0, keepdims=True)
            grad_scores = (wide * (grad_probs - inner)).astype(BF16)
            grad_query.append(dot_nn(keys_t[64 * which : 64 * which + 64, :], grad_scores))
            grad_key = grad_key + dot_nn(grad_scores, half_of(queries, which))
        grad_query = jnp.concatenate(grad_query, axis=0) * HEAD ** (-0.5)
        ta[rows, :] = grad_query.astype(BF16)
        tb[rows, :] = grad_key.T.astype(BF16)
        q6[p] = grad_query.T.astype(BF16)
        k6[p] = grad_key.astype(BF16)

    def pack(p, first_row, second_row):
        def body(s):
            for xx in range(2):
                offset = (2 * s + xx) * 96
                rows = [pl.ds(pl.multiple_of(first_row + offset, 96), 96),
                        pl.ds(pl.multiple_of(second_row + offset, 96), 96)]
                first, second = ua.at[p, 0, :, xx, s], ua.at[p, 1, :, xx, s]
                for yy in range(2):
                    lo, mid, hi = 384 * yy, 384 * yy + 128, 384 * yy + 256
                    for m in range(2):
                        first[yy, 96 * m : 96 * m + 96, :] = gp[rows[m], lo : lo + 128]
                        second[yy, 96 * m : 96 * m + 96, :] = gp[rows[m], hi : hi + 128]
                    even = gp[rows[0], mid : mid + 128].astype(F32)
                    odd = pltpu.roll(gp[rows[1], mid : mid + 128].astype(F32), 64, 1)
                    first[yy, 192:288, :] = jnp.where(lanes < 64, even, odd).astype(BF16)
                    second[yy, 192:288, :] = jnp.where(lanes < 64, odd, even).astype(BF16)

        loop(zs, body)

    parts("av", 6, value_back)
    run("gav")
    for n in units[VO[0] : VO[1] + 1]:
        ag_drain(n)
    gp[0:768, :] = dot_nn(tc[...], n1[...]).astype(BF16)
    pack(1, 0, 768)
    for n in grads[AVO[0] : AVO[1] + 1]:
        rs_start(n)
    parts("ab", 6, attend_back)
    run("gaqk")
    for n in units[QK[0] : QK[1] + 1]:
        ag_drain(n)
    gp[0:768, :] = dot_nn(ta[...], n1[...]).astype(BF16)
    gp[768:1536, :] = dot_nn(tb[...], n1[...]).astype(BF16)
    pack(0, 0, 768)
    for n in grads[AQK[0] : AQK[1] + 1]:
        rs_start(n)

    run("dn1")
    h1[...] = dot_nn(lane_tiles(q6), at[0])
    h1[...] += dot_nn(lane_tiles(k6), at[1])
    h1[...] += dot_nn(lane_tiles(o6), at[2])
    gvec[2:3, :] = jnp.sum(lane_tiles(q6).astype(F32), axis=0, keepdims=True)
    gvec[3:4, :] = jnp.sum(lane_tiles(o6).astype(F32), axis=0, keepdims=True)

    run("inb")

    def input_back(s):
        rows = rows_of(s)
        grad, gain_sum, bias_sum = norm_gradient(x_in[s].astype(F32), vec[0:1, :], h1[rows, :])
        n1[rows, :] = (grad + acc[rows, :]).astype(BF16)
        gvec[0:1, :] += gain_sum
        gvec[1:2, :] += bias_sum

    loop(4, input_back)
    gvec_steps[0]()
    own_grad.start()
    run("end")
    finish_vectors()
    w1_back.wait()
    each_core(join_expand)
    w2_back.wait()
    each_core(join_reduce)

    own_out.wait()
    own_grad.wait()
    for moved in tokens_out + result_out + grad_out:
        moved.wait_send()
    for n in units[VO[1] + 1 :]:
        ag_drain(n)
    for n in grads:
        rs_drain(n)


def layer(sub, tokens, cotangent, span_mask, vectors, attention, expand, reduce_t):
    zs = GROUPS // 2
    seqs, block, width = tokens.shape
    rows = seqs * block
    columns = attention.shape[2]
    piece = (3 * columns, 128)
    vmem = lambda shape, dtype: pltpu.VMEM(shape, dtype)
    half = (2, 2, 2, zs) + piece
    scratch = [vmem((2,) + half, BF16)] + [vmem(half, BF16)] * 4
    scratch += [vmem((2, 2, 2, zs) + piece, BF16), vmem((6, 2, 2, zs) + piece, BF16)]
    scratch += [vmem(tokens.shape, BF16)] * 3
    scratch += [vmem((16, width), F32)] * 2
    scratch += [vmem((zs + 2, 16, width), F32)] * 2
    scratch += [vmem((16, columns), F32)]
    tiles = vmem((width // 128, rows, 128), BF16)
    flat = vmem((rows, width), BF16)
    turned = vmem((width, rows), BF16)
    scratch += [vmem((4, width, width), BF16), flat, tiles, tiles, tiles, tiles]
    scratch += [vmem((HEADS, rows, rows), BF16), vmem((rows, width), F32), vmem((rows, width), F32)]
    scratch += [flat, vmem((4 * rows, width), BF16), vmem((4 * rows, width), BF16)]
    scratch += [turned, turned, turned, tiles]
    scratch += [vmem(expand.shape, F32), vmem(reduce_t.shape, F32), flat, vmem(tokens.shape, BF16)]
    scratch += [tiles, flat, vmem((columns, width // 2), F32), vmem((2, width), F32), vmem((2, width), F32)]
    scratch += [vmem((6,) + piece, F32), vmem((width // 2, 2 * columns), F32)]
    scratch += [vmem((2 * columns, 2 * columns), F32), vmem(piece, F32)]
    scratch += [pltpu.SemaphoreType.DMA((5,))]
    gathered, summed = sum(map(len, GATHER_ROUTES)), sum(map(len, SUM_ROUTES))
    scratch += [pltpu.SemaphoreType.DMA((gathered, 4 * zs))] * 2
    scratch += [pltpu.SemaphoreType.DMA((gathered,))] * 2
    scratch += [pltpu.SemaphoreType.DMA((summed, zs + 2))] * 2
    scratch += [pltpu.SemaphoreType.DMA((4, 3))] * 2
    scratch += [pltpu.SemaphoreType.DMA((2, zs + 2))] * 2
    scratch += [pltpu.SemaphoreType.DMA((8,))] * 2
    in_vmem = pl.BlockSpec(memory_space=pltpu.VMEM)
    anywhere = pl.BlockSpec(memory_space=pl.ANY)
    return pl.pallas_call(
        functools.partial(kernel, sub, zs),
        out_shape=(
            jax.ShapeDtypeStruct(tokens.shape, BF16),
            jax.ShapeDtypeStruct(tokens.shape, BF16),
            jax.ShapeDtypeStruct(attention.shape, F32),
            jax.ShapeDtypeStruct(expand.shape, F32),
            jax.ShapeDtypeStruct(reduce_t.shape, F32),
            jax.ShapeDtypeStruct(vectors.shape, F32),
        ),
        in_specs=[anywhere] * 2 + [in_vmem] * 5,
        out_specs=(anywhere, anywhere) + (in_vmem,) * 4,
        scratch_shapes=scratch,
        compiler_params=pltpu.CompilerParams(
            collective_id=0, has_side_effects=True, vmem_limit_bytes=65400 * 1024
        ),
    )(tokens, cotangent, span_mask, vectors, attention, expand, reduce_t)


def update_kernel(rates, *refs):
    count = len(rates)
    ins, (result, grad) = refs[: 4 * count], refs[4 * count : 4 * count + 2]
    outs, (result_out, grad_out) = refs[4 * count + 2 : 7 * count + 2], refs[7 * count + 2 : 7 * count + 4]
    held, (low, wide, passed) = refs[7 * count + 4 : 11 * count + 4], refs[11 * count + 4 : 11 * count + 7]
    in_sems, out_sems = refs[11 * count + 7 :]
    loads = [pltpu.make_async_copy(ins[n], held[n], in_sems.at[n]) for n in range(4 * count)]
    stores = [pltpu.make_async_copy(held[4 * n + m], outs[3 * n + m], out_sems.at[3 * n + m])
              for n in range(count) for m in range(3)]
    load_grad = pltpu.make_async_copy(grad, low, in_sems.at[4 * count])
    store_grad = pltpu.make_async_copy(wide, grad_out, out_sems.at[3 * count])
    load_result = pltpu.make_async_copy(result, passed, in_sems.at[4 * count + 1])
    store_result = pltpu.make_async_copy(passed, result_out, out_sems.at[3 * count + 1])
    load_grad.start()
    load_result.start()
    for copy in loads:
        copy.start()
    load_result.wait()
    store_result.start()
    load_grad.wait()

    def widen(s, carry):
        wide[s] = low[s].astype(F32)
        return carry

    lax.fori_loop(0, low.shape[0], widen, 0)
    store_grad.start()
    for n in range(count):
        for m in range(4):
            loads[4 * n + m].wait()
        weight, one, two, gradient = held[4 * n : 4 * n + 4]
        values = adamw(weight[...], one[...], two[...], gradient[...], rates[n])
        for ref, value in zip((weight, one, two), values):
            ref[...] = value
        for m in range(3):
            stores[3 * n + m].start()
    for copy in stores + [store_grad, store_result]:
        copy.wait()


def update(rates, arrays, result, grad):
    flat = [value for group in arrays for value in group]
    new = [jax.ShapeDtypeStruct(value.shape, F32) for group in arrays for value in group[:3]]
    new += [jax.ShapeDtypeStruct(result.shape, BF16), jax.ShapeDtypeStruct(grad.shape, F32)]
    anywhere = pl.BlockSpec(memory_space=pl.ANY)
    scratch = [pltpu.VMEM(value.shape, F32) for value in flat]
    scratch += [pltpu.VMEM(grad.shape, BF16), pltpu.VMEM(grad.shape, F32), pltpu.VMEM(result.shape, BF16)]
    scratch += [pltpu.SemaphoreType.DMA((len(flat) + 2,)), pltpu.SemaphoreType.DMA((len(new),))]
    return pl.pallas_call(
        functools.partial(update_kernel, rates),
        out_shape=tuple(new),
        in_specs=[anywhere] * (len(flat) + 2),
        out_specs=(anywhere,) * len(new),
        scratch_shapes=scratch,
        compiler_params=pltpu.CompilerParams(vmem_limit_bytes=63 * 1024 * 1024),
    )(*flat, result, grad)


def local(
    sub,
    tokens,
    cotangent,
    span_mask,
    attention_weight,
    expand_weight,
    reduce_weight,
    vectors,
    attention_first,
    attention_second,
    expand_first,
    expand_second,
    reduce_first,
    reduce_second,
    vector_first,
    vector_second,
):
    together = [[n * sub + m for m in range(sub)] for n in range(GROUPS)]

    def widen(value, axis):
        if sub == 1:
            return value
        low = lax.all_gather(
            value.astype(BF16), "batch", axis=axis, tiled=True, axis_index_groups=together
        )
        return low.astype(F32)

    def narrow(value, axis):
        if sub == 1:
            return value
        return lax.psum_scatter(
            value, "batch", scatter_dimension=axis, tiled=True, axis_index_groups=together
        )

    out_tokens, input_grad, ga, g1, g2, gv = layer(
        sub,
        tokens,
        cotangent,
        span_mask,
        widen(vectors, 1),
        widen(attention_weight, 2),
        widen(expand_weight, 1),
        widen(reduce_weight.T, 0),
    )
    arrays = (
        (attention_weight, attention_first, attention_second, narrow(ga, 2)),
        (expand_weight, expand_first, expand_second, narrow(g1, 1)),
        (reduce_weight.T, reduce_first.T, reduce_second.T, narrow(g2, 0)),
        (vectors, vector_first, vector_second, narrow(gv, 1)),
    )
    rates = (rate_attention, rate_expand, rate_reduce, rate_vector)
    new = update(rates, arrays, out_tokens, input_grad)
    return new[-2:] + new[0:6] + tuple(value.T for value in new[6:9]) + new[9:12]


def solution(mesh):
    sub = mesh.shape["batch"] // GROUPS
    sequences = P("batch", "blk", None)
    attention = P(None, "blk", "batch")
    matrix = P("blk", "batch")
    return jax.shard_map(
        functools.partial(local, sub),
        mesh=mesh,
        in_specs=(sequences, sequences, P("batch", "blk"), attention, matrix, matrix, matrix)
        + (attention,) * 2
        + (matrix,) * 6,
        out_specs=(sequences,) * 2 + (attention,) * 3 + (matrix,) * 9,
        check_vma=False,
    )
```

```python
import functools
import math

import jax
import jax.numpy as jnp
from jax import lax
from jax.experimental import pallas as pl
from jax.experimental.pallas import tpu as pltpu
from jax.sharding import PartitionSpec as P

HEADS = 12
HEAD = 64
STEP = 10
GROUPS = 8

norm_epsilon = 1e-05
beta_one = 0.9
beta_two = 0.999
adam_epsilon = 1e-08
decay_weight = 0.1
rate_attention = 0.05
rate_expand = 0.03
rate_reduce = 0.015
rate_vector = 0.4

F32 = jnp.float32
BF16 = jnp.bfloat16
MESH = pl.DeviceIdType.MESH
GELU_SCALE = math.sqrt(2.0 / math.pi)
GELU_CUBE = 0.044715


def adamw(weight, moment_one, moment_two, gradient, step_rate):
    moment_one = beta_one * moment_one + (1.0 - beta_one) * gradient
    moment_two = beta_two * moment_two + (1.0 - beta_two) * gradient * gradient
    corrected_one = moment_one / (1.0 - beta_one**STEP)
    corrected_two = moment_two / (1.0 - beta_two**STEP)
    updated = weight - step_rate * (
        corrected_one / (jnp.sqrt(corrected_two) + adam_epsilon) + decay_weight * weight
    )
    return (updated, moment_one, moment_two)


def dot_nn(left, right):
    return lax.dot_general(left, right, (((1,), (0,)), ((), ())), preferred_element_type=F32)


def dot_nt(left, right):
    return lax.dot_general(left, right, (((1,), (1,)), ((), ())), preferred_element_type=F32)


X, Y, Z = 1, 2, 4
(N_QKA, N_QKB, N_VOA, N_VOB, N_W10A, N_W10B, N_W11A, N_W11B, N_W20A, N_W20B, N_W21A, N_W21B) = range(12)
(N_AQKA, N_AQKB, N_AVO, N_G10, N_G11A, N_G11B, N_G20, N_G21) = range(8)
QK, VO = (N_QKA, N_QKB), (N_VOA, N_VOB)
AQK, AVO = (N_AQKA, N_AQKB), (N_AVO, N_AVO)
SEND, GOT, WHOLE, SUM, VEC, SMALL, DO = range(7)
(TOK, COT, OUT, IG, TOK_HERE, COT_HERE, OUT_HERE,
 IG_HERE, SWAP_HERE, N2S_HERE, COTS_HERE, BACKS_HERE, AHEADS_HERE) = range(13)
GATHER_ROUTES = (
    ((Z, Y, X), (Z, Y, X),),
    ((Z, Y, X), (Z, Y, X),),
    ((Y, Z, X), (X, Z, Y),),
    ((Z, X, Y), (Y, Z, X),),
    ((X, Z, Y), (Z, X, Y),),
    ((Y, Z, X), (Z, Y, X),),
)
SUM_ROUTES = (
    ((Y, X, Z), (X, Z, Y),),
    ((Y, X, Z),),
    ((Y, X, Z),),
    ((X, Z, Y), (X, Z, Y),),
    ((Y, X, Z),),
    ((Z, X, Y),),
)
PLAN = dict(
    own1=(
        (SEND, N_QKA, 0, Z), (SEND, N_QKB, 0, Z),
    ),
    ownff=(
        (DO, TOK), (SEND, N_VOA, 0, Z), (VEC, 0), (DO, SWAP_HERE),
    ),
    mask=(
        (SEND, N_W10B, 0, X), (SEND, N_W20A, 0, X),
    ),
    ln1=(
        (VEC, 1), (GOT, N_QKA, Z), (SEND, N_QKA, Z, X), (SEND, N_QKA, Z, Y), (SEND, N_VOB, 0, Z),
        (GOT, N_W10B, X), (GOT, N_W20A, X), (GOT, N_QKB, Z), (SEND, N_QKB, Z, X), (SEND, N_QKB, Z, Y),
        (SEND, N_W11A, 0, Z), (GOT, N_QKA, Z | X), (DO, TOK_HERE), (GOT, N_VOA, Z), (SEND, N_VOA, Z, X),
        (SEND, N_VOA, Z, Y), (SEND, N_W11B, 0, Z), (GOT, N_QKB, Z | X), (VEC, 2), (GOT, N_QKA, Z | Y),
        (SEND, N_QKA, Z | Y, X), (GOT, N_VOB, Z), (SEND, N_VOB, Z, Y), (SEND, N_W10A, 0, Z),
        (GOT, N_VOA, Z | X), (GOT, N_QKB, Z | Y), (SEND, N_QKB, Z | Y, X), (SEND, N_VOB, Z, X),
        (SEND, N_W11B, 0, Y), (GOT, N_W11A, Z), (SEND, N_W10A, 0, Y), (VEC, 3), (SEND, N_W10B, 0, Z),
    ),
    unp0=(
        (DO, COT), (GOT, N_QKA, Z | Y | X), (GOT, N_VOA, Z | Y), (SEND, N_VOA, Z | Y, X), (GOT, N_W11B, Z),
        (SEND, N_W10B, X, Z), (GOT, N_QKB, Z | Y | X), (GOT, N_VOB, Z | Y), (SEND, N_VOB, Z | Y, X),
        (GOT, N_W11B, Y), (GOT, N_W10A, Z), (SEND, N_W11B, Y, Z), (GOT, N_W10A, Y), (WHOLE, N_QKA),
        (WHOLE, N_QKB),
    ),
    projq=(
        (GOT, N_VOB, Z | X), (SEND, N_W11A, Z, X),
    ),
    projk=(
        (SEND, N_W11A, Z, Y),
    ),
    attend0=(
        (GOT, N_W10B, Z), (SEND, N_W10A, Y, Z),
    ),
    attend1=(
        (GOT, N_VOA, Z | Y | X), (SEND, N_W11B, Z, X),
    ),
    attend2=(
        (SEND, N_W10B, Z, Y), (GOT, N_W10B, X | Z),
    ),
    attend3=(
        (SEND, N_W21B, 0, Z),
    ),
    attend4=(
        (GOT, N_VOB, Z | Y | X), (SEND, N_W10A, Z, X), (DO, COT_HERE), (SEND, N_W10B, X | Z, Y),
    ),
    attend5=(
        (GOT, N_W11B, Y | Z), (SEND, N_W20B, 0, Z),
    ),
    unp1=(
        (WHOLE, N_VOA), (WHOLE, N_VOB), (GOT, N_W11A, Z | X), (SEND, N_W11B, Y | Z, X),
    ),
    projv=(
        (GOT, N_W11A, Z | Y), (SEND, N_W11A, Z | X, Y), (DO, COTS_HERE),
    ),
    mix0=(
        (GOT, N_W10A, Y | Z), (SEND, N_W21A, 0, Z),
    ),
    mix5=(
        (GOT, N_W11B, Z | X),
    ),
    ao=(
        (SEND, N_W10A, Y | Z, X),
    ),
    ln2=(
        (GOT, N_W10B, Z | Y), (SEND, N_W21A, 0, Y), (GOT, N_W21B, Z),
    ),
    expa0=(
        (SEND, N_W20A, 0, Z), (SEND, N_W21B, Z, Y), (GOT, N_W10A, Z | X), (GOT, N_W10B, X | Z | Y),
        (GOT, N_W20B, Z), (SEND, N_W20B, Z, X), (SEND, N_W20A, X, Z), (SEND, N_W20B, Z, Y), (DO, N2S_HERE),
        (GOT, N_W11B, Y | Z | X), (SEND, N_W21B, Z, X), (GOT, N_W11A, Z | X | Y), (GOT, N_W21A, Z),
        (GOT, N_W21A, Y), (SEND, N_W21A, Y, Z), (GOT, N_W10A, Y | Z | X), (SEND, N_W21A, Z, X),
    ),
    expa1=(
        (GOT, N_W20A, Z), (SEND, N_W20A, Z, Y), (GOT, N_W21B, Z | Y),
    ),
    expb0=(
        (GOT, N_W20B, Z | X), (SEND, N_W20B, Z | X, Y), (SEND, N_W21B, Z | Y, X), (GOT, N_W20A, X | Z),
        (GOT, N_W20B, Z | Y),
    ),
    expb1=(
        (SEND, N_W20A, X | Z, Y), (GOT, N_W21B, Z | X),
    ),
    trY=(
        (GOT, N_W21A, Y | Z), (SEND, N_W21A, Y | Z, X), (GOT, N_W20A, Z | Y),
    ),
    gw2_0=(
        (GOT, N_W21A, Z | X),
    ),
    gw2_1=(
        (GOT, N_W20B, Z | X | Y),
    ),
    innb0=(
        (GOT, N_W21B, Z | Y | X), (SUM, N_G20, 0), (SUM, N_G21, 0), (GOT, N_W20A, X | Z | Y),
        (GOT, N_W21A, Y | Z | X),
    ),
    gw1_0=(
        (DO, BACKS_HERE),
    ),
    hid=(
        (SUM, N_G10, 0), (SUM, N_G11A, 0), (SUM, N_G11B, 0), (SUM, N_G20, 1),
    ),
    ab0=(
        (SUM, N_G11A, 1),
    ),
    ab2=(
        (SUM, N_G21, 1),
    ),
    ab3=(
        (SUM, N_AVO, 0), (SUM, N_G10, 1), (SUM, N_G11B, 1),
    ),
    gaqk=(
        (SUM, N_G11A, 2),
    ),
    redb=(
        (SUM, N_G20, 2),
    ),
    outst=(
        (SUM, N_G11B, 2), (SUM, N_AQKB, 0), (SUM, N_AQKA, 0), (SUM, N_G10, 2), (DO, AHEADS_HERE),
        (SUM, N_AVO, 1),
    ),
    inb=(
        (SUM, N_G11A, 3), (DO, OUT), (SUM, N_G21, 2), (SUM, N_G20, 3),
    ),
    end=(
        (SUM, N_AQKA, 1), (SUM, N_AQKB, 1), (SUM, N_G10, 3), (DO, IG), (SUM, N_AVO, 2), (DO, OUT_HERE),
        (SMALL, 0), (SUM, N_AQKB, 2), (SUM, N_AQKA, 2), (SMALL, 1), (SMALL, 2), (SUM, N_AVO, 3),
        (DO, IG_HERE), (SUM, N_G21, 3), (SUM, N_AQKA, 3), (SUM, N_G11B, 3), (SMALL, 3), (SUM, N_AQKB, 3),
    ),
)


def lane_tiles(ref, count=6):
    return jnp.concatenate([ref[t] for t in range(count)], axis=1)


class Unit:
    def __init__(self, index, route, rows, u, other):
        self.index, self.route, self.rows, self.u, self.other = index, route, rows, u, other


class Gradient:
    def __init__(self, index, route, rows, u, other, core_in, got, total):
        self.index, self.route, self.rows, self.u, self.other = index, route, rows, u, other
        self.core_in, self.got, self.total = core_in, got, total


def kernel(sub, zs, *refs):
    (tok, cot, mask_hbm, vec_hbm, a_hbm, w1_hbm, w2_hbm,
     out, ig, ga, g1, g2, gv,
     mask_in, vec_in, a_in, w1_in, w2_in, ua, uw1, uw2, gw1, gw2, core_in, got,
     x_in, cot_in, stage, vec, gvec, vin, gin, narrow_rows,
     at, n1, q6, k6, v6, o6, pt, h1, acc, n2, act, gp, ta, tb, tc, d6,
     w1_other, w2_other, n2_other, cot_other, back_in, ahead_in,
     lines, b1, gb1, totals, turned1, got1, got2,
     local_sem, ag_send, ag_recv, core_send, core_recv, rs_send, rs_recv,
     a2a_send, a2a_recv, v_send, v_recv, pair_send, pair_recv) = refs

    i = lax.axis_index("blk")
    b = lax.axis_index("batch")
    c, y = lax.rem(i, 2), lax.div(i, 2)
    g, r = lax.div(b, sub), lax.rem(b, sub)
    x, z = lax.rem(g, 2), lax.div(g, 2)

    def device(c_=c, y_=y, x_=x, z_=z):
        return {"blk": 2 * y_ + c_, "batch": (2 * z_ + x_) * sub + r}

    def z_at(k):
        return lax.rem(z + k, zs)

    def block_at(k):
        return lax.rem(i + k, 4)

    def copy(src, dst, send, recv, to):
        return pltpu.make_async_remote_copy(
            src_ref=src, dst_ref=dst, send_sem=send, recv_sem=recv, device_id=to, device_id_type=MESH
        )

    def loop(count, body, hooks=()):
        def step(s, carry):
            body(s)
            for k, f in hooks:
                pl.when(s == k)(f)
            return carry

        lax.fori_loop(0, count, step, 0)

    partners = [device(z_=z_at(k)) for k in range(1, zs)]
    partners += [device(x_=1 - x), device(y_=1 - y), device(c_=1 - c), device(c_=1 - c, y_=1 - y)]
    barrier = pltpu.get_barrier_semaphore()
    for partner in partners:
        pl.semaphore_signal(barrier, inc=1, device_id=partner, device_id_type=MESH)

    ME = {"y": y, "x": x, "z": z}

    def before(n, axis, other):
        return n.route.index(axis) < n.route.index(other)

    def side(n, axes, all_z):
        where = (1 - y if "y" in axes else y, 1 - x if "x" in axes else x, slice(None) if all_z else z)
        return n.u.at[where + (n.rows,)]

    def neighbour(axis):
        return device(y_=1 - y) if axis == "y" else device(x_=1 - x)

    def ag_copy(n, ref, axes, k, to):
        slot = (("y" in axes) * 2 + ("x" in axes)) * zs + k
        return copy(ref, ref, ag_send.at[n.index, slot], ag_recv.at[n.index, slot], to)

    def core_copy(n, ref):
        return copy(ref, ref, core_send.at[n.index], core_recv.at[n.index], device(c_=1 - c))

    def ag_sends(n, axes, axis):
        axes = axes.replace("z", "")
        if axis == "z":
            ref = side(n, axes, False)
            return [ag_copy(n, ref, axes, k, device(z_=z_at(k))) for k in range(1, zs)]
        ref = side(n, axes, before(n, "z", axis))
        return [ag_copy(n, ref, axes + axis, 0, neighbour(axis))]

    def ag_send_part(n, axes, axis):
        for moved in ag_sends(n, axes, axis):
            moved.start()

    def ag_wait_part(n, axes):
        last = max(axes, key=n.route.index)
        axes = axes.replace("z", "")
        if last == "z":
            yy, xx = (1 - y if "y" in axes else y), (1 - x if "x" in axes else x)
            for k in range(1, zs):
                ag_copy(n, n.u.at[yy, xx, z_at(zs - k), n.rows], axes, k, device()).wait_recv()
        else:
            ag_copy(n, side(n, axes, before(n, "z", last)), axes, 0, device()).wait_recv()
        if n.other is not None and (last == "z" or before(n, "z", last)):
            core_copy(n, side(n, axes, True)).start()

    def ag_done(n):
        if n.other is not None:
            core_copy(n, n.other.at[:, :, :, n.rows]).wait_recv()

    def ag_drain(n):
        for axis in n.route:
            earlier = [other for other in "yx" if before(n, other, axis)]
            for some in range(2 ** len(earlier)):
                axes = "".join(other for bit, other in enumerate(earlier) if some >> bit & 1)
                for moved in ag_sends(n, axes, axis):
                    moved.wait_send()
        if n.other is not None:
            core_copy(n, n.u.at[:, :, :, n.rows]).wait_send()

    AXES = "yxz"

    def rs_groups(n, step):
        axis = n.route[step]
        if axis == "z":
            return [(k, 1 + k, device(z_=z_at(zs - k))) for k in range(1, zs)]
        return [(1, "yx".index(axis), neighbour(axis))]

    def rs_where(n, step, k):
        axis, out, land = n.route[step], [], []
        for other in AXES:
            if other == axis:
                out.append(z_at(zs - k) if axis == "z" else 1 - ME[axis])
                land.append(k)
            elif before(n, other, axis):
                out.append(ME[other])
                land.append(0)
            else:
                out.append(slice(None))
                land.append(slice(None))
        return tuple(out) + (n.rows,), tuple(land) + (n.rows,)

    def rs_copy(n, step, k, slot, to):
        out, land = rs_where(n, step, k)
        return copy(n.u.at[out], n.got.at[land], rs_send.at[n.index, slot], rs_recv.at[n.index, slot], to)

    def rs_core(n):
        return copy(n.other.at[:, :, :, n.rows], n.core_in.at[:, :, :, n.rows], rs_send.at[n.index, zs + 1],
                    rs_recv.at[n.index, zs + 1], device(c_=1 - c))

    def add_terms(n, place, step):
        value = n.u[tuple(place) + (n.rows,)].astype(F32)
        if n.other is not None:
            value = value + n.core_in[tuple(place) + (n.rows,)].astype(F32)
        for axis in n.route[:step]:
            for k in range(1, zs) if axis == "z" else (1,):
                where = [k if other == axis else (0 if before(n, other, axis) else at_place)
                         for other, at_place in zip(AXES, place)]
                value = value + n.got[tuple(where) + (n.rows,)].astype(F32)
        return value

    def rs_start(n):
        rs_core(n).start()

    def rs_step(n, step):
        if step == 0 and n.other is not None:
            rs_core(n).wait_recv()
        if step > 0:
            for group in rs_groups(n, step - 1):
                rs_copy(n, step - 1, *group).wait_recv()
        if step == 3:
            n.total[n.rows, :] = add_terms(n, (y, x, z), 3)
            return
        for k, slot, to in rs_groups(n, step):
            out, _ = rs_where(n, step, k)
            if step > 0 or n.other is not None:
                spans = [range(2) if isinstance(at_place, slice) else (at_place,) for at_place in out[:2]]

                def body(zz):
                    for yy in spans[0]:
                        for xx in spans[1]:
                            n.u[yy, xx, zz, n.rows] = add_terms(n, (yy, xx, zz), step).astype(BF16)

                if isinstance(out[2], slice):
                    loop(zs, body)
                else:
                    body(out[2])
            rs_copy(n, step, k, slot, to).start()

    def rs_drain(n):
        if n.other is not None:
            rs_core(n).wait_send()
        for step in range(3):
            for group in rs_groups(n, step):
                rs_copy(n, step, *group).wait_send()

    def small_sum(ref, slots, which):
        to = (device(y_=1 - y), device(c_=1 - c), device(x_=1 - x))
        to += tuple(device(z_=z_at(k)) for k in range(1, zs))

        def moved(slot):
            return copy(ref, slots.at[slot], v_send.at[which, slot], v_recv.at[which, slot], to[slot])

        def land(last):
            moved(last).wait()
            ref[...] = ref[...] + slots[last]

        def step(n):
            def run():
                if n > 0:
                    land(n - 1)
                moved(n).start()

            return run

        def line():
            land(2)
            for k in range(1, zs):
                moved(2 + k).start()

        def finish():
            for k in range(1, zs):
                moved(2 + k).wait()
            value = ref[...]
            for k in range(1, zs):
                value = value + slots[2 + k]
            ref[...] = value

        return [step(0), step(1), step(2), line, finish]

    def rows_of(s):
        return pl.ds(pl.multiple_of(s * 128, 128), 128)

    def exchange(src, dst, which):
        return [copy(src.at[block_at(k)], dst.at[i], a2a_send.at[which, k - 1],
                     a2a_recv.at[which, k - 1], {"blk": block_at(k), "batch": b})
                for k in range(1, 4)]

    def exchange_landed(dst, which):
        return [copy(dst.at[block_at(4 - k)], dst.at[block_at(4 - k)], a2a_send.at[which, k - 1],
                     a2a_recv.at[which, k - 1], {"blk": block_at(4 - k), "batch": b})
                for k in range(1, 4)]

    def axes_of(mask):
        return "".join(axis for axis, bit in (("y", Y), ("x", X), ("z", Z)) if mask & bit)

    def rows_in(part, count):
        return pl.ds(part * (288 // count), 288 // count)

    units = []
    for unit, routes in enumerate(GATHER_ROUTES):
        half = unit % 2
        ref = (ua, uw1, uw2)[unit // 2]
        pieces = (ref.at[half, c], ref.at[half, 1 - c]) if unit < 2 else (ref.at[half], None)
        for part, route in enumerate(routes):
            units.append(Unit(len(units), "".join(map(axes_of, route)), rows_in(part, len(routes)), *pieces))

    def pair(slot, src, dst):
        return copy(src, dst, pair_send.at[slot], pair_recv.at[slot], device(c_=1 - c))

    w1_swap, w2_swap = pair(0, w1_in, w1_other), pair(1, w2_in, w2_other)

    def each_core(f):
        for q in range(2):
            pl.when(c == q)(functools.partial(f, q))

    def rest_rows(matrix):
        return a_in[matrix, pl.ds(pl.multiple_of(128 * (1 - c), 64), 64), :]

    def own_attention(p):
        mine = ua.at[p, c, y, x, z]
        for m in range(2):
            main = a_in[2 * p + m, pl.ds(pl.multiple_of(64 * c, 64), 128), :]
            mine[96 * m : 96 * m + 96, :] = main.T.astype(BF16)
        rest = jnp.concatenate([rest_rows(2 * p + c), rest_rows(2 * p + 1 - c)], axis=0)
        mine[192:288, :] = rest.T.astype(BF16)

    def own_expand(q):
        both = (w1_in, w1_other) if q == 0 else (w1_other, w1_in)
        cols = slice(192 * q, 192 * q + 192)
        blocks = (
            both[0][0:128, cols],
            jnp.concatenate([both[0][128:192, cols], both[1][0:64, cols]], axis=0),
            both[1][64:192, cols],
        )
        for t, block in enumerate(blocks):
            value = block.T.astype(BF16)
            for h in range(2):
                uw1[h, y, x, z, 96 * t : 96 * t + 96, :] = value[96 * h : 96 * h + 96, :]

    def own_reduce(q):
        both = (w2_in, w2_other) if q == 0 else (w2_other, w2_in)
        for cc in range(2):
            for part_of in range(2):
                start = 384 * part_of + 192 * q
                lines[:, 192 * part_of : 192 * part_of + 192] = both[cc][:, start : start + 192]
            for t in range(3):
                uw2[cc, y, x, z, 96 * t : 96 * t + 96, :] = lines[:, 128 * t : 128 * t + 128].astype(BF16)

    def own_hidden_bias(q):
        for zz in range(zs):
            for xx in range(2):
                col = 384 * (zz % 2) + 192 * xx
                start = 384 * xx + 192 * q
                b1[zz // 2 : zz // 2 + 1, col : col + 192] = vec[8 + zz : 9 + zz, start : start + 192]

    def hidden_bias_gradient(q):
        for zz in range(zs):
            for xx in range(2):
                col = 384 * (zz % 2) + 192 * xx
                start = 384 * xx + 192 * q
                gvec[8 + zz : 9 + zz, start : start + 192] = gb1[zz // 2 : zz // 2 + 1, col : col + 192]

    columns = a_in.shape[2]
    placed = lax.broadcasted_iota(jnp.int32, (columns, 768), 1) == (
        lax.broadcasted_iota(jnp.int32, (columns, 768), 0) + columns * g
    )

    def own_vectors():
        vec[...] = jnp.zeros_like(vec)
        rows = dot_nn(vec_in[...].astype(BF16), jnp.where(placed, 1.0, 0.0).astype(BF16))
        for j in range(3):
            vec[pl.ds(3 * i + j, 1), :] = rows[j : j + 1, :]

    loads = [pltpu.make_async_copy(src, dst, local_sem.at[4 + n]) for n, (src, dst) in enumerate((
        (a_hbm, a_in), (vec_hbm, vec_in), (w1_hbm, w1_in), (w2_hbm, w2_in), (cot, stage), (mask_hbm, mask_in)
    ))]
    load_a, load_vec, load_w1, load_w2, load_cot, load_mask = loads
    for load in loads:
        load.start()

    def masked_cotangent():
        load_cot.wait()
        load_mask.wait()
        eye = lax.broadcasted_iota(jnp.int32, (128, 128), 0) == lax.broadcasted_iota(jnp.int32, (128, 128), 1)
        for s in range(4):
            row = jnp.broadcast_to(mask_in[s : s + 1, :].astype(F32), (128, 128))
            column = jnp.sum(jnp.where(eye, row, 0.0), axis=1, keepdims=True)
            stage[s] = (stage[s].astype(F32) * column).astype(BF16)

    def finish_attention(p):
        value = totals.at[p]
        for m in range(2):
            ga[2 * p + m, pl.ds(pl.multiple_of(64 * c, 64), 128), :] = value[96 * m : 96 * m + 96, :].T
        rest = value[192:288, :].T
        rows = pl.ds(pl.multiple_of(128 * (1 - c), 64), 64)
        ga[2 * p + c, rows, :] = rest[0:64, :]
        ga[2 * p + 1 - c, rows, :] = rest[64:128, :]

    w1_back = pair(6, turned1.at[pl.ds(pl.multiple_of(192 * (1 - c), 64), 192)], got1)
    w2_back = pair(7, totals.at[5 - c], got2)

    def turn_expand():
        for h in range(2):
            for t in range(3):
                turned1[128 * t : 128 * t + 128, 96 * h : 96 * h + 96] = totals[2 + h, 96 * t : 96 * t + 96, :].T
        w1_back.start()

    def join_expand(q):
        g1[:, 192 * q : 192 * q + 192] = turned1[192 * q : 192 * q + 192, :]
        g1[:, 192 * (1 - q) : 192 * (1 - q) + 192] = got1[...]

    def join_reduce(q):
        for half, value in ((q, totals.at[4 + q]), (1 - q, got2)):
            for t in range(3):
                lines[:, 128 * t : 128 * t + 128] = value[96 * t : 96 * t + 96, :]
            for part_of in range(2):
                start = 384 * part_of + 192 * half
                g2[:, start : start + 192] = lines[:, 192 * part_of : 192 * part_of + 192]

    def finish_vectors():
        value, total = gvec[...], 0.0
        for _ in range(3):
            part = value.astype(BF16)
            total = total + dot_nt(part, jnp.where(placed, 1.0, 0.0).astype(BF16))
            value = value - part.astype(F32)
        narrow_rows[...] = total
        for j in range(3):
            gv[j : j + 1, :] = narrow_rows[pl.ds(3 * i + j, 1), :]

    grads, owners = [], []
    for unit, routes in enumerate(SUM_ROUTES):
        half = unit % 2
        ref = (ua, gw1, gw2)[unit // 2]
        pieces = (ref.at[half, c], ref.at[half, 1 - c], core_in.at[half]) if unit < 2 else (ref.at[half], None, None)
        for part, route in enumerate(routes):
            grads.append(Gradient(len(grads), "".join(map(axes_of, route)), rows_in(part, len(routes)), *pieces,
                                  got.at[unit], totals.at[unit]))
            owners.append(unit)

    def summed(unit):
        if unit < 2:
            finish_attention(unit)
        elif unit < 4 and {2, 3} <= set(whole):
            turn_expand()
        elif unit >= 4 and {4, 5} <= set(whole):
            w2_back.start()

    seen, whole = set(), []

    def event(kind, *rest):
        if kind == SEND:
            ag_send_part(units[rest[0]], axes_of(rest[1]), axes_of(rest[2]))
        elif kind == GOT:
            ag_wait_part(units[rest[0]], axes_of(rest[1]))
        elif kind == WHOLE:
            ag_done(units[rest[0]])
        elif kind == SUM:
            rs_step(grads[rest[0]], rest[1])
            if rest[1] == 3:
                seen.add(rest[0])
                unit = owners[rest[0]]
                if all(k in seen for k in range(len(grads)) if owners[k] == unit):
                    whole.append(unit)
                    summed(unit)
        elif kind == DO:
            actions[rest[0]]()
        else:
            (vec_steps if kind == VEC else gvec_steps)[rest[0] + 1]()
            if (kind, rest[0]) == (SMALL, zs - 1):
                finish_vectors()

    def run(part):
        for todo in PLAN.get(part, ()):
            event(*todo)

    def parts(name, count, body):
        run(name + "0")
        hooks = [(k - 1, functools.partial(run, name + str(k))) for k in range(1, count) if name + str(k) in PLAN]
        loop(count, body, hooks)

    def started(copies):
        for moved in copies:
            moved.start()
        return copies

    def arrived(*copies):
        for moved in copies:
            moved.wait_recv()

    own_tokens = pltpu.make_async_copy(tok.at[i], x_in.at[i], local_sem.at[0])
    own_tokens.start()
    own_cot = pltpu.make_async_copy(stage.at[i], cot_in.at[i], local_sem.at[1])
    tokens_out, cot_out = exchange(tok, x_in, 0), exchange(stage, cot_in, 1)
    result_out = exchange(stage, out, 2)
    grad_out = [copy(n1.at[rows_of(block_at(k))], ig.at[i], a2a_send.at[3, k - 1], a2a_recv.at[3, k - 1],
                     {"blk": block_at(k), "batch": b}) for k in range(1, 4)]
    own_out = pltpu.make_async_copy(stage.at[i], out.at[i], local_sem.at[2])
    own_grad = pltpu.make_async_copy(n1.at[rows_of(i)], ig.at[i], local_sem.at[3])
    n2_swap, cot_swap = pair(2, n2, n2_other), pair(3, cot_in, cot_other)
    back_swap, ahead_swap = pair(4, d6, back_in), pair(5, n2, ahead_in)
    vec_steps, gvec_steps = small_sum(vec, vin, 0), small_sum(gvec, gin, 1)

    def tokens_here():
        arrived(*exchange_landed(x_in, 0))
        own_tokens.wait()

    def cotangent_here():
        arrived(*exchange_landed(cot_in, 1))
        own_cot.wait()
        cot_swap.start()

    def swaps_here():
        w1_swap.wait()
        w2_swap.wait()

    actions = {
        TOK: lambda: started(tokens_out),
        COT: lambda: started(cot_out),
        OUT: lambda: started(result_out),
        IG: lambda: started(grad_out),
        TOK_HERE: tokens_here,
        COT_HERE: cotangent_here,
        OUT_HERE: lambda: arrived(*exchange_landed(out, 2)),
        IG_HERE: lambda: arrived(*exchange_landed(ig, 3)),
        SWAP_HERE: swaps_here,
        N2S_HERE: lambda: n2_swap.wait(),
        COTS_HERE: lambda: cot_swap.wait(),
        BACKS_HERE: lambda: back_swap.wait(),
        AHEADS_HERE: lambda: ahead_swap.wait(),
    }

    load_a.wait()
    own_attention(0)
    load_vec.wait()
    own_vectors()
    load_w1.wait()
    load_w2.wait()
    pl.semaphore_wait(barrier, len(partners))
    vec_steps[0]()
    w1_swap.start()
    w2_swap.start()
    run("own1")
    own_attention(1)
    run("ownff")
    each_core(own_expand)
    each_core(own_reduce)
    run("mask")
    masked_cotangent()
    own_cot.start()
    run("ln1")
    each_core(own_hidden_bias)

    def normalise(value):
        centered = value - jnp.mean(value, axis=-1, keepdims=True)
        scale = lax.rsqrt(jnp.mean(centered * centered, axis=-1, keepdims=True) + norm_epsilon)
        return centered * scale, scale

    def first_norm(s):
        unit, _ = normalise(x_in[s].astype(F32))
        n1[rows_of(s), :] = (unit * vec[0:1, :] + vec[1:2, :]).astype(BF16)

    loop(4, first_norm)
    run("unp0")

    lanes = lax.broadcasted_iota(jnp.int32, (96, 128), 1)

    def unpack(p, s):
        for xx in range(2):
            rows = pl.ds(pl.multiple_of((2 * s + xx) * 96, 96), 96)
            for yy in range(2):
                first, second = ua.at[p, 0, yy, xx, s], ua.at[p, 1, yy, xx, s]
                lo, hi = 384 * yy, 384 * yy + 256
                for m in range(2):
                    at[2 * p + m, rows, lo : lo + 128] = first[96 * m : 96 * m + 96, :]
                    at[2 * p + m, rows, hi : hi + 128] = second[96 * m : 96 * m + 96, :]
                rest_first = first[192:288, :].astype(F32)
                rest_second = second[192:288, :].astype(F32)
                even = jnp.where(lanes < 64, rest_first, rest_second)
                odd = pltpu.roll(jnp.where(lanes < 64, rest_second, rest_first), 64, 1)
                at[2 * p, rows, lo + 128 : lo + 256] = even.astype(BF16)
                at[2 * p + 1, rows, lo + 128 : lo + 256] = odd.astype(BF16)

    def project(m, dst, bias):
        for n in range(3):
            value = dot_nt(n1[...], at[m, 256 * n : 256 * n + 256, :])
            if bias is not None:
                value = value + vec[bias : bias + 1, 256 * n : 256 * n + 256]
            value = value.astype(BF16)
            if m == 0:
                value = value * jnp.asarray(HEAD ** (-0.5), BF16)
            dst[2 * n] = value[:, 0:128]
            dst[2 * n + 1] = value[:, 128:256]

    loop(zs, functools.partial(unpack, 0))
    run("projq")
    project(0, q6, 2)
    run("projk")
    project(1, k6, None)

    half_lane = lax.broadcasted_iota(jnp.int32, (512, 128), 1) // HEAD

    def half_of(value, which):
        return jnp.where(half_lane == which, value, jnp.zeros_like(value))

    def turn(value):
        return value.astype(F32).T.astype(BF16)

    def attend(p):
        queries, keys = q6[p], k6[p]
        for which in range(2):
            scores = dot_nt(half_of(keys, which), queries)
            expo = jnp.exp(scores - jnp.max(scores, axis=0, keepdims=True))
            probs = (expo * (1.0 / jnp.sum(expo, axis=0, keepdims=True))).astype(BF16)
            pt[2 * p + which] = probs

    def mix(p):
        values_t = turn(v6[p])
        mixed = [dot_nn(values_t[64 * which : 64 * which + 64, :], pt[2 * p + which]) for which in range(2)]
        o6[p] = jnp.concatenate(mixed, axis=0).T.astype(BF16)

    parts("attend", 6, attend)
    run("unp1")
    loop(zs, functools.partial(unpack, 1))
    run("projv")
    project(2, v6, 3)
    parts("mix", 6, mix)

    run("ao")
    for n in range(3):
        cols = slice(256 * n, 256 * n + 256)
        value = dot_nt(lane_tiles(o6), at[3, cols, :]) + vec[4:5, cols]
        for s in range(4):
            h1[128 * s : 128 * s + 128, cols] = x_in[s, :, cols].astype(F32) + value[128 * s : 128 * s + 128]

    def second_norm(s):
        unit, _ = normalise(h1[rows_of(s), :])
        n2[rows_of(s), :] = (unit * vec[5:6, :] + vec[6:7, :]).astype(BF16)

    run("ln2")
    loop(4, second_norm)
    n2_swap.start()

    def expand_block(s):
        def piece(ref):
            return jnp.concatenate([ref[96 * t : 96 * t + 96, :] for t in range(3)], axis=1)

        return jnp.concatenate(
            [jnp.concatenate([piece(uw1.at[h, yy, xx, 2 * s + zz]) for yy in range(2)], axis=1)
             for zz in range(2) for xx in range(2) for h in range(2)],
            axis=0,
        )

    def reduce_block(s):
        def piece(ref):
            return jnp.concatenate([ref[96 * t : 96 * t + 96, :] for t in range(3)], axis=1)

        return jnp.concatenate(
            [jnp.concatenate([piece(uw2.at[cc, s, xx, zz]) for cc in range(2)], axis=1)
             for zz in range(zs) for xx in range(2)],
            axis=0,
        )

    def block_rows(owner, s):
        return pl.ds(pl.multiple_of((2 * owner + s) * 512, 512), 512)

    def expand(owner, normed, s):
        rows = block_rows(owner, s)
        inner = dot_nt(normed[...], expand_block(s)) + b1[pl.ds(s, 1), :]
        square = inner * inner
        tanh = jnp.tanh(GELU_SCALE * inner * (1.0 + GELU_CUBE * square))
        act[rows, :] = (0.5 * inner * (1.0 + tanh)).astype(BF16)
        slope = 0.5 * (1.0 + tanh) + 0.5 * inner * (1.0 - tanh * tanh) * (
            GELU_SCALE * (1.0 + 3.0 * GELU_CUBE * square)
        )
        gp[rows, :] = slope.astype(BF16)

    parts("expa", 2, functools.partial(expand, 0, n2))
    parts("expb", 2, functools.partial(expand, 1, n2_other))

    gvec[...] = jnp.zeros_like(gvec)

    def transpose_rows(dst, s, value):
        dst[:, 128 * s : 128 * s + 128] = turn(value)

    run("trY")
    total = jnp.zeros((1, 768), F32)
    for s in range(4):
        transpose_rows(ta, s, cot_in[s])
        total = total + jnp.sum(cot_in[s].astype(F32), axis=0, keepdims=True)
    gvec[7:8, :] = total
    for s in range(4):
        transpose_rows(tb, s, cot_other[s])

    def both_rows(ref, s):
        return jnp.concatenate([ref[block_rows(0, s), :], ref[block_rows(1, s), :]], axis=0)

    def reduce_back(s):
        grad = dot_nn(jnp.concatenate([ta[...], tb[...]], axis=1), both_rows(act, s)).astype(BF16)
        for zz in range(zs):
            for xx in range(2):
                row = 96 * (2 * zz + xx)
                for cc in range(2):
                    for t in range(3):
                        col = 384 * cc + 128 * t
                        gw2[cc, s, xx, zz, 96 * t : 96 * t + 96, :] = grad[row : row + 96, col : col + 128]

    parts("gw2_", 2, reduce_back)

    def rows_together(ref):
        return jnp.concatenate([ref[s] for s in range(4)], axis=0)

    def inner_back(owner, cotangent_rows, s):
        rows = block_rows(owner, s)
        grad = dot_nn(rows_together(cotangent_rows), reduce_block(s)) * gp[rows, :].astype(F32)
        low = grad.astype(BF16)
        gp[rows, :] = low
        sums = jnp.sum(low.astype(F32), axis=0, keepdims=True)
        gb1[pl.ds(s, 1), :] = sums if owner == 1 else gb1[pl.ds(s, 1), :] + sums

    def norm_back(owner):
        acc[...] = dot_nn(gp[block_rows(owner, 0), :], expand_block(0))
        acc[...] += dot_nn(gp[block_rows(owner, 1), :], expand_block(1))

    parts("innb", 2, functools.partial(inner_back, 1, cot_other))
    run("dn2b")
    norm_back(1)
    for t in range(6):
        d6[t] = acc[:, 128 * t : 128 * t + 128].astype(BF16)
    back_swap.start()
    parts("inna", 2, functools.partial(inner_back, 0, cot_in))
    each_core(hidden_bias_gradient)
    run("dn2a")
    norm_back(0)

    def expand_back(s):
        turned = jnp.concatenate([turn(gp[block_rows(owner, s), :]) for owner in range(2)], axis=1)
        normed = jnp.concatenate([n2[...], n2_other[...]], axis=0)
        grad = dot_nn(turned, normed).astype(BF16)
        for zz in range(2):
            for xx in range(2):
                for h in range(2):
                    row = 384 * zz + 192 * xx + 96 * h
                    for yy in range(2):
                        for t in range(3):
                            col = 384 * yy + 128 * t
                            gw1[h, yy, xx, 2 * s + zz, 96 * t : 96 * t + 96, :] = grad[
                                row : row + 96, col : col + 128
                            ]

    parts("gw1_", 2, expand_back)
    run("hid")

    def norm_gradient(value, scale_row, grad):
        unit, scale = normalise(value)
        gain_sum = jnp.sum(grad * unit, axis=0, keepdims=True)
        bias_sum = jnp.sum(grad, axis=0, keepdims=True)
        inner = grad * scale_row
        mean = jnp.mean(inner, axis=-1, keepdims=True)
        along = jnp.mean(inner * unit, axis=-1, keepdims=True)
        return scale * (inner - mean - unit * along), gain_sum, bias_sum

    def hidden_back(s):
        rows = rows_of(s)
        grad_in = jnp.concatenate([back_in[t, rows, :] for t in range(6)], axis=1)
        grad_in = acc[rows, :] + grad_in.astype(F32)
        grad, gain_sum, bias_sum = norm_gradient(h1[rows, :], vec[5:6, :], grad_in)
        grad = grad + cot_in[s].astype(F32)
        acc[rows, :] = grad
        low = grad.astype(BF16)
        n2[rows, :] = low
        gvec[5:6, :] += gain_sum
        gvec[6:7, :] += bias_sum
        gvec[4:5, :] += jnp.sum(low.astype(F32), axis=0, keepdims=True)

    loop(4, hidden_back)

    run("dO")
    for n in range(3):
        value = dot_nn(n2[...], at[3, :, 256 * n : 256 * n + 256]).astype(BF16)
        d6[2 * n] = value[:, 0:128]
        d6[2 * n + 1] = value[:, 128:256]
    run("gao")
    for s in range(4):
        transpose_rows(tc, s, n2[128 * s : 128 * s + 128, :])
    gp[768:1536, :] = dot_nn(tc[...], lane_tiles(o6)).astype(BF16)

    def value_back(p):
        grads_in, grad_value = d6[p], 0.0
        for which in range(2):
            grad_value = grad_value + dot_nn(pt[2 * p + which], half_of(grads_in, which))
        tc[rows_of(p), :] = grad_value.T.astype(BF16)
        o6[p] = grad_value.astype(BF16)

    def attend_back(p):
        rows = rows_of(p)
        queries, keys, values, grads_in = q6[p], k6[p], v6[p], d6[p]
        keys_t = turn(keys)
        grad_query, grad_key = [], 0.0
        for which in range(2):
            wide = pt[2 * p + which].astype(F32)
            grad_probs = dot_nt(half_of(values, which), grads_in)
            inner = jnp.sum(wide * grad_probs, axis=0, keepdims=True)
            grad_scores = (wide * (grad_probs - inner)).astype(BF16)
            grad_query.append(dot_nn(keys_t[64 * which : 64 * which + 64, :], grad_scores))
            grad_key = grad_key + dot_nn(grad_scores, half_of(queries, which))
        grad_query = jnp.concatenate(grad_query, axis=0) * HEAD ** (-0.5)
        ta[rows, :] = grad_query.astype(BF16)
        tb[rows, :] = grad_key.T.astype(BF16)
        q6[p] = grad_query.T.astype(BF16)
        k6[p] = grad_key.astype(BF16)

    def pack(p, first_row, second_row):
        def body(s):
            for xx in range(2):
                offset = (2 * s + xx) * 96
                rows = [pl.ds(pl.multiple_of(first_row + offset, 96), 96),
                        pl.ds(pl.multiple_of(second_row + offset, 96), 96)]
                first, second = ua.at[p, 0, :, xx, s], ua.at[p, 1, :, xx, s]
                for yy in range(2):
                    lo, mid, hi = 384 * yy, 384 * yy + 128, 384 * yy + 256
                    for m in range(2):
                        first[yy, 96 * m : 96 * m + 96, :] = gp[rows[m], lo : lo + 128]
                        second[yy, 96 * m : 96 * m + 96, :] = gp[rows[m], hi : hi + 128]
                    even = gp[rows[0], mid : mid + 128].astype(F32)
                    odd = pltpu.roll(gp[rows[1], mid : mid + 128].astype(F32), 64, 1)
                    first[yy, 192:288, :] = jnp.where(lanes < 64, even, odd).astype(BF16)
                    second[yy, 192:288, :] = jnp.where(lanes < 64, odd, even).astype(BF16)

        loop(zs, body)

    parts("av", 6, value_back)
    run("gav")
    for n in units[VO[0] : VO[1] + 1]:
        ag_drain(n)
    gp[0:768, :] = dot_nn(tc[...], n1[...]).astype(BF16)
    pack(1, 0, 768)
    for n in grads[AVO[0] : AVO[1] + 1]:
        rs_start(n)
    parts("ab", 6, attend_back)
    run("gaqk")
    for n in units[QK[0] : QK[1] + 1]:
        ag_drain(n)
    gp[0:768, :] = dot_nn(ta[...], n1[...]).astype(BF16)
    gp[768:1536, :] = dot_nn(tb[...], n1[...]).astype(BF16)
    pack(0, 0, 768)
    for n in grads[AQK[0] : AQK[1] + 1]:
        rs_start(n)

    def reduce(owner):
        value = dot_nt(act[block_rows(owner, 0), :], reduce_block(0))
        return value + dot_nt(act[block_rows(owner, 1), :], reduce_block(1))

    def layer_output():
        run("redb")
        n2[...] = reduce(1).astype(BF16)
        ahead_swap.start()
        run("reda")
        h1[...] = h1[...] + vec[7:8, :] + reduce(0)
        run("outst")
        for moved in cot_out:
            moved.wait_send()
        for s in range(4):
            rows = slice(128 * s, 128 * s + 128)
            stage[s] = (h1[rows, :] + ahead_in[rows, :].astype(F32)).astype(BF16)
        own_out.start()

    layer_output()
    run("dn1")
    h1[...] = dot_nn(lane_tiles(q6), at[0])
    h1[...] += dot_nn(lane_tiles(k6), at[1])
    h1[...] += dot_nn(lane_tiles(o6), at[2])
    gvec[2:3, :] = jnp.sum(lane_tiles(q6).astype(F32), axis=0, keepdims=True)
    gvec[3:4, :] = jnp.sum(lane_tiles(o6).astype(F32), axis=0, keepdims=True)

    run("inb")

    def input_back(s):
        rows = rows_of(s)
        grad, gain_sum, bias_sum = norm_gradient(x_in[s].astype(F32), vec[0:1, :], h1[rows, :])
        n1[rows, :] = (grad + acc[rows, :]).astype(BF16)
        gvec[0:1, :] += gain_sum
        gvec[1:2, :] += bias_sum

    loop(4, input_back)
    gvec_steps[0]()
    own_grad.start()

    def join():
        w1_back.wait()
        each_core(join_expand)
        w2_back.wait()
        each_core(join_reduce)

    joined = False
    for n, todo in enumerate(PLAN["end"]):
        if not joined and n >= len(PLAN["end"]) - 3 and {2, 3, 4, 5} <= set(whole):
            join()
            joined = True
        event(*todo)
    if not joined:
        join()

    own_out.wait()
    own_grad.wait()
    for moved in tokens_out + result_out + grad_out:
        moved.wait_send()
    for n in units[VO[1] + 1 :]:
        ag_drain(n)
    for n in grads:
        rs_drain(n)


def layer(sub, tokens, cotangent, span_mask, vectors, attention, expand, reduce_t):
    zs = GROUPS // 2
    seqs, block, width = tokens.shape
    rows = seqs * block
    columns = attention.shape[2]
    piece = (3 * columns, 128)
    vmem = lambda shape, dtype: pltpu.VMEM(shape, dtype)
    half = (2, 2, 2, zs) + piece
    scratch = [vmem(value.shape, value.dtype) for value in (span_mask, vectors, attention, expand, reduce_t)]
    scratch += [vmem((2,) + half, BF16)] + [vmem(half, BF16)] * 4
    scratch += [vmem((2, 2, 2, zs) + piece, BF16), vmem((6, 2, 2, zs) + piece, BF16)]
    scratch += [vmem(tokens.shape, BF16)] * 3
    scratch += [vmem((16, width), F32)] * 2
    scratch += [vmem((zs + 2, 16, width), F32)] * 2
    scratch += [vmem((16, columns), F32)]
    tiles = vmem((width // 128, rows, 128), BF16)
    flat = vmem((rows, width), BF16)
    turned = vmem((width, rows), BF16)
    scratch += [vmem((4, width, width), BF16), flat, tiles, tiles, tiles, tiles]
    scratch += [vmem((HEADS, rows, rows), BF16), vmem((rows, width), F32), vmem((rows, width), F32)]
    scratch += [flat, vmem((4 * rows, width), BF16), vmem((4 * rows, width), BF16)]
    scratch += [turned, turned, turned, tiles]
    scratch += [vmem(expand.shape, F32), vmem(reduce_t.shape, F32), flat, vmem(tokens.shape, BF16)]
    scratch += [tiles, flat, vmem((columns, width // 2), F32), vmem((2, width), F32), vmem((2, width), F32)]
    scratch += [vmem((6,) + piece, F32), vmem((width // 2, 2 * columns), F32)]
    scratch += [vmem((2 * columns, 2 * columns), F32), vmem(piece, F32)]
    scratch += [pltpu.SemaphoreType.DMA((10,))]
    gathered, summed = sum(map(len, GATHER_ROUTES)), sum(map(len, SUM_ROUTES))
    scratch += [pltpu.SemaphoreType.DMA((gathered, 4 * zs))] * 2
    scratch += [pltpu.SemaphoreType.DMA((gathered,))] * 2
    scratch += [pltpu.SemaphoreType.DMA((summed, zs + 2))] * 2
    scratch += [pltpu.SemaphoreType.DMA((4, 3))] * 2
    scratch += [pltpu.SemaphoreType.DMA((2, zs + 2))] * 2
    scratch += [pltpu.SemaphoreType.DMA((8,))] * 2
    in_vmem = pl.BlockSpec(memory_space=pltpu.VMEM)
    anywhere = pl.BlockSpec(memory_space=pl.ANY)
    return pl.pallas_call(
        functools.partial(kernel, sub, zs),
        out_shape=(
            jax.ShapeDtypeStruct(tokens.shape, BF16),
            jax.ShapeDtypeStruct(tokens.shape, BF16),
            jax.ShapeDtypeStruct(attention.shape, F32),
            jax.ShapeDtypeStruct(expand.shape, F32),
            jax.ShapeDtypeStruct(reduce_t.shape, F32),
            jax.ShapeDtypeStruct(vectors.shape, F32),
        ),
        in_specs=[anywhere] * 7,
        out_specs=(anywhere, anywhere) + (in_vmem,) * 4,
        scratch_shapes=scratch,
        compiler_params=pltpu.CompilerParams(
            collective_id=0, has_side_effects=True, vmem_limit_bytes=65400 * 1024
        ),
    )(tokens, cotangent, span_mask, vectors, attention, expand, reduce_t)


def update_kernel(rates, *refs):
    count = len(rates)
    ins, (result, grad) = refs[: 4 * count], refs[4 * count : 4 * count + 2]
    outs, (result_out, grad_out) = refs[4 * count + 2 : 7 * count + 2], refs[7 * count + 2 : 7 * count + 4]
    held, (low, wide, passed) = refs[7 * count + 4 : 11 * count + 4], refs[11 * count + 4 : 11 * count + 7]
    in_sems, out_sems = refs[11 * count + 7 :]
    loads = [pltpu.make_async_copy(ins[n], held[n], in_sems.at[n]) for n in range(4 * count)]
    stores = [pltpu.make_async_copy(held[4 * n + m], outs[3 * n + m], out_sems.at[3 * n + m])
              for n in range(count) for m in range(3)]
    load_grad = pltpu.make_async_copy(grad, low, in_sems.at[4 * count])
    store_grad = pltpu.make_async_copy(wide, grad_out, out_sems.at[3 * count])
    load_result = pltpu.make_async_copy(result, passed, in_sems.at[4 * count + 1])
    store_result = pltpu.make_async_copy(passed, result_out, out_sems.at[3 * count + 1])
    load_grad.start()
    load_result.start()
    for copy in loads:
        copy.start()
    load_result.wait()
    store_result.start()
    load_grad.wait()

    def widen(s, carry):
        wide[s] = low[s].astype(F32)
        return carry

    lax.fori_loop(0, low.shape[0], widen, 0)
    store_grad.start()
    for n in range(count):
        for m in range(4):
            loads[4 * n + m].wait()
        weight, one, two, gradient = held[4 * n : 4 * n + 4]
        values = adamw(weight[...], one[...], two[...], gradient[...], rates[n])
        for ref, value in zip((weight, one, two), values):
            ref[...] = value
        for m in range(3):
            stores[3 * n + m].start()
    for copy in stores + [store_grad, store_result]:
        copy.wait()


def update(rates, arrays, result, grad):
    flat = [value for group in arrays for value in group]
    new = [jax.ShapeDtypeStruct(value.shape, F32) for group in arrays for value in group[:3]]
    new += [jax.ShapeDtypeStruct(result.shape, BF16), jax.ShapeDtypeStruct(grad.shape, F32)]
    anywhere = pl.BlockSpec(memory_space=pl.ANY)
    scratch = [pltpu.VMEM(value.shape, F32) for value in flat]
    scratch += [pltpu.VMEM(grad.shape, BF16), pltpu.VMEM(grad.shape, F32), pltpu.VMEM(result.shape, BF16)]
    scratch += [pltpu.SemaphoreType.DMA((len(flat) + 2,)), pltpu.SemaphoreType.DMA((len(new),))]
    return pl.pallas_call(
        functools.partial(update_kernel, rates),
        out_shape=tuple(new),
        in_specs=[anywhere] * (len(flat) + 2),
        out_specs=(anywhere,) * len(new),
        scratch_shapes=scratch,
        compiler_params=pltpu.CompilerParams(vmem_limit_bytes=63 * 1024 * 1024),
    )(*flat, result, grad)


def local(
    sub,
    tokens,
    cotangent,
    span_mask,
    attention_weight,
    expand_weight,
    reduce_weight,
    vectors,
    attention_first,
    attention_second,
    expand_first,
    expand_second,
    reduce_first,
    reduce_second,
    vector_first,
    vector_second,
):
    together = [[n * sub + m for m in range(sub)] for n in range(GROUPS)]

    def widen(value, axis):
        if sub == 1:
            return value
        low = lax.all_gather(
            value.astype(BF16), "batch", axis=axis, tiled=True, axis_index_groups=together
        )
        return low.astype(F32)

    def narrow(value, axis):
        if sub == 1:
            return value
        return lax.psum_scatter(
            value, "batch", scatter_dimension=axis, tiled=True, axis_index_groups=together
        )

    out_tokens, input_grad, ga, g1, g2, gv = layer(
        sub,
        tokens,
        cotangent,
        span_mask,
        widen(vectors, 1),
        widen(attention_weight, 2),
        widen(expand_weight, 1),
        widen(reduce_weight.T, 0),
    )
    arrays = (
        (attention_weight, attention_first, attention_second, narrow(ga, 2)),
        (expand_weight, expand_first, expand_second, narrow(g1, 1)),
        (reduce_weight.T, reduce_first.T, reduce_second.T, narrow(g2, 0)),
        (vectors, vector_first, vector_second, narrow(gv, 1)),
    )
    rates = (rate_attention, rate_expand, rate_reduce, rate_vector)
    new = update(rates, arrays, out_tokens, input_grad)
    return new[-2:] + new[0:6] + tuple(value.T for value in new[6:9]) + new[9:12]


def solution(mesh):
    sub = mesh.shape["batch"] // GROUPS
    sequences = P("batch", "blk", None)
    attention = P(None, "blk", "batch")
    matrix = P("blk", "batch")
    return jax.shard_map(
        functools.partial(local, sub),
        mesh=mesh,
        in_specs=(sequences, sequences, P("batch", "blk"), attention, matrix, matrix, matrix)
        + (attention,) * 2
        + (matrix,) * 6,
        out_specs=(sequences,) * 2 + (attention,) * 3 + (matrix,) * 9,
        check_vma=False,
    )
```

```python
import functools
import math

import jax
import jax.numpy as jnp
from jax import lax
from jax.experimental import pallas as pl
from jax.experimental.pallas import tpu as pltpu
from jax.sharding import PartitionSpec as P

HEADS = 12
HEAD = 64
STEP = 10
GROUPS = 8

norm_epsilon = 1e-05
beta_one = 0.9
beta_two = 0.999
adam_epsilon = 1e-08
decay_weight = 0.1
rate_attention = 0.05
rate_expand = 0.03
rate_reduce = 0.015
rate_vector = 0.4

F32 = jnp.float32
BF16 = jnp.bfloat16
MESH = pl.DeviceIdType.MESH
GELU_SCALE = math.sqrt(2.0 / math.pi)
GELU_CUBE = 0.044715


def adamw(weight, moment_one, moment_two, gradient, step_rate):
    moment_one = beta_one * moment_one + (1.0 - beta_one) * gradient
    moment_two = beta_two * moment_two + (1.0 - beta_two) * gradient * gradient
    corrected_one = moment_one / (1.0 - beta_one**STEP)
    corrected_two = moment_two / (1.0 - beta_two**STEP)
    updated = weight - step_rate * (
        corrected_one / (jnp.sqrt(corrected_two) + adam_epsilon) + decay_weight * weight
    )
    return (updated, moment_one, moment_two)


def dot_nn(left, right):
    return lax.dot_general(left, right, (((1,), (0,)), ((), ())), preferred_element_type=F32)


def dot_nt(left, right):
    return lax.dot_general(left, right, (((1,), (1,)), ((), ())), preferred_element_type=F32)


X, Y, Z = 1, 2, 4
(N_QKA, N_QKB, N_VOA, N_VOB, N_W10A, N_W10B, N_W11A, N_W11B, N_W20A, N_W20B, N_W21A, N_W21B) = range(12)
(N_AQKA, N_AQKB, N_AVO, N_G10, N_G11A, N_G11B, N_G20, N_G21A, N_G21B) = range(9)
QK, VO = (N_QKA, N_QKB), (N_VOA, N_VOB)
AQK, AVO = (N_AQKA, N_AQKB), (N_AVO, N_AVO)
SEND, GOT, WHOLE, SUM, VEC, SMALL, DO = range(7)
(TOK, COT, OUT, IG, TOK_HERE, COT_HERE, OUT_HERE,
 IG_HERE, SWAP_HERE, N2S_HERE, COTS_HERE, BACKS_HERE, AHEADS_HERE) = range(13)
GATHER_ROUTES = (
    ((Z, Y, X), (Z, Y, X),),
    ((Z, Y, X), (Z, Y, X),),
    ((Y, Z, X), (X, Z, Y),),
    ((Z, X, Y), (Y, Z, X),),
    ((Z, X, Y), (Z, Y, X),),
    ((Y, X, Z), (Z, X, Y),),
)
SUM_ROUTES = (
    ((Y, X, Z), (X, Z, Y),),
    ((Y, X, Z),),
    ((Y, X, Z),),
    ((Z, X, Y), (X, Z, Y),),
    ((Y, X, Z),),
    ((Z, X, Y), (X, Z, Y),),
)
PLAN = dict(
    own1=(
        (SEND, N_QKA, 0, Z), (SEND, N_QKB, 0, Z),
    ),
    ownff=(
        (DO, TOK), (SEND, N_VOA, 0, Z), (VEC, 0), (DO, SWAP_HERE),
    ),
    mask=(
        (SEND, N_W10B, 0, X), (SEND, N_W21A, 0, X),
    ),
    ln1=(
        (VEC, 1), (GOT, N_QKA, Z), (SEND, N_QKA, Z, X), (SEND, N_QKA, Z, Y), (SEND, N_VOB, 0, Z),
        (GOT, N_W10B, X), (GOT, N_W21A, X), (VEC, 2), (GOT, N_QKB, Z), (SEND, N_QKB, Z, X),
        (SEND, N_QKB, Z, Y), (SEND, N_W11A, 0, Z), (GOT, N_QKA, Z | X), (DO, TOK_HERE), (GOT, N_VOA, Z),
        (SEND, N_VOA, Z, X), (SEND, N_VOA, Z, Y), (SEND, N_W10A, 0, Z), (GOT, N_QKB, Z | X),
        (GOT, N_QKA, Z | Y), (SEND, N_QKA, Z | Y, X), (GOT, N_VOB, Z), (SEND, N_VOB, Z, Y), (VEC, 3),
        (SEND, N_W10B, 0, Z),
    ),
    unp0=(
        (GOT, N_VOA, Z | X), (GOT, N_QKB, Z | Y), (SEND, N_QKB, Z | Y, X), (SEND, N_VOB, Z, X),
        (SEND, N_W10A, 0, Y), (SEND, N_W11B, 0, Y), (GOT, N_W11A, Z), (SEND, N_W11B, 0, Z), (DO, COT),
        (GOT, N_QKA, Z | Y | X), (GOT, N_VOA, Z | Y), (SEND, N_VOA, Z | Y, X), (GOT, N_W10A, Z),
        (SEND, N_W10B, X, Z), (GOT, N_QKB, Z | Y | X), (GOT, N_VOB, Z | Y), (SEND, N_VOB, Z | Y, X),
        (GOT, N_W10A, Y), (GOT, N_W10B, Z), (GOT, N_W11B, Y), (SEND, N_W10A, Y, Z), (WHOLE, N_QKA),
        (WHOLE, N_QKB),
    ),
    projq=(
        (GOT, N_VOB, Z | X),
    ),
    projk=(
        (SEND, N_W11A, Z, X), (SEND, N_W11A, Z, Y),
    ),
    attend0=(
        (GOT, N_W11B, Z),
    ),
    attend1=(
        (SEND, N_W11B, Y, Z),
    ),
    attend2=(
        (GOT, N_VOA, Z | Y | X), (SEND, N_W10A, Z, X),
    ),
    attend3=(
        (SEND, N_W10B, Z, Y), (GOT, N_W10B, X | Z),
    ),
    attend4=(
        (SEND, N_W21B, 0, Z),
    ),
    attend5=(
        (GOT, N_VOB, Z | Y | X), (SEND, N_W11B, Z, X),
    ),
    unp1=(
        (DO, COT_HERE), (SEND, N_W10B, X | Z, Y), (GOT, N_W10A, Y | Z), (SEND, N_W20A, 0, Z), (WHOLE, N_VOA),
        (WHOLE, N_VOB),
    ),
    projv=(
        (GOT, N_W11A, Z | X),
    ),
    mix0=(
        (SEND, N_W10A, Y | Z, X), (GOT, N_W11A, Z | Y), (SEND, N_W11A, Z | X, Y),
    ),
    mix1=(
        (DO, COTS_HERE),
    ),
    mix3=(
        (GOT, N_W11B, Y | Z),
    ),
    mix4=(
        (SEND, N_W20B, 0, Z),
    ),
    ln2=(
        (GOT, N_W10A, Z | X),
    ),
    expa0=(
        (SEND, N_W11B, Y | Z, X), (GOT, N_W10B, Z | Y), (SEND, N_W21A, 0, Y), (GOT, N_W21B, Z),
        (SEND, N_W21B, Z, Y), (SEND, N_W21A, 0, Z), (GOT, N_W11B, Z | X), (SEND, N_W21B, Z, X),
        (GOT, N_W10B, X | Z | Y), (DO, N2S_HERE), (GOT, N_W20A, Z), (SEND, N_W21A, X, Z),
        (GOT, N_W10A, Y | Z | X), (SEND, N_W20A, Z, X), (GOT, N_W11A, Z | X | Y), (GOT, N_W21A, Y),
        (GOT, N_W20B, Z), (SEND, N_W20B, Z, Y), (SEND, N_W20A, Z, Y), (SEND, N_W21A, Y, Z),
        (GOT, N_W11B, Y | Z | X), (SEND, N_W21A, Y, X),
    ),
    expa1=(
        (SEND, N_W20B, Z, X), (GOT, N_W21B, Z | Y), (GOT, N_W21A, Z),
    ),
    expb0=(
        (GOT, N_W21B, Z | X), (SEND, N_W21B, Z | X, Y),
    ),
    expb1=(
        (GOT, N_W20B, Z | Y), (SEND, N_W20B, Z | Y, X), (GOT, N_W21A, X | Z),
    ),
    trY=(
        (GOT, N_W20A, Z | X), (SEND, N_W20A, Z | X, Y), (GOT, N_W21A, Y | X), (SEND, N_W21A, Y | X, Z),
    ),
    gw2_0=(
        (GOT, N_W20A, Z | Y), (GOT, N_W21A, Y | Z),
    ),
    innb0=(
        (GOT, N_W20B, Z | X), (GOT, N_W21B, Z | X | Y), (SUM, N_G20, 0), (SUM, N_G21A, 0), (SUM, N_G21B, 0),
        (GOT, N_W21A, Y | X | Z), (GOT, N_W20B, Z | Y | X), (GOT, N_W20A, Z | X | Y),
    ),
    gw1_0=(
        (SUM, N_G21B, 1),
    ),
    gw1_1=(
        (DO, BACKS_HERE),
    ),
    hid=(
        (SUM, N_G10, 0), (SUM, N_G11A, 0), (SUM, N_G11B, 0),
    ),
    dO=(
        (SUM, N_G21A, 1),
    ),
    gao=(
        (SUM, N_G20, 1),
    ),
    ab0=(
        (SUM, N_G21B, 2),
    ),
    ab1=(
        (SUM, N_G11B, 1),
    ),
    ab3=(
        (SUM, N_AVO, 0),
    ),
    ab5=(
        (SUM, N_G20, 2), (SUM, N_G10, 1),
    ),
    gaqk=(
        (SUM, N_G21A, 2),
    ),
    reda=(
        (SUM, N_G11A, 1),
    ),
    outst=(
        (SUM, N_AQKB, 0), (SUM, N_AQKA, 0), (SUM, N_G10, 2), (DO, AHEADS_HERE),
    ),
    inb=(
        (SUM, N_G11A, 2), (SUM, N_G11B, 2),
    ),
    end=(
        (SUM, N_AVO, 1), (DO, OUT), (SUM, N_AQKB, 1), (SUM, N_G20, 3), (SUM, N_AQKA, 1), (SMALL, 0),
        (SMALL, 1), (DO, IG), (SUM, N_AVO, 2), (SUM, N_G10, 3), (SUM, N_AQKA, 2), (SMALL, 2), (DO, OUT_HERE),
        (SUM, N_AQKB, 2), (DO, IG_HERE), (SUM, N_AVO, 3), (SUM, N_G21B, 3), (SUM, N_G21A, 3),
        (SUM, N_G11A, 3), (SUM, N_G11B, 3), (SUM, N_AQKA, 3), (SUM, N_AQKB, 3), (SMALL, 3),
    ),
)


def lane_tiles(ref, count=6):
    return jnp.concatenate([ref[t] for t in range(count)], axis=1)


class Unit:
    def __init__(self, index, route, rows, u, other):
        self.index, self.route, self.rows, self.u, self.other = index, route, rows, u, other


class Gradient:
    def __init__(self, index, route, rows, u, other, core_in, got, total):
        self.index, self.route, self.rows, self.u, self.other = index, route, rows, u, other
        self.core_in, self.got, self.total = core_in, got, total


def kernel(sub, zs, *refs):
    (tok, cot, mask_hbm, vec_hbm, a_hbm, w1_hbm, w2_hbm,
     out, ig, ga, g1, g2, gv,
     mask_in, vec_in, a_in, w1_in, w2_in, ua, uw1, uw2, gw1, gw2, core_in, got,
     x_in, cot_in, stage, vec, gvec, vin, gin, narrow_rows,
     at, n1, q6, k6, v6, o6, pt, h1, acc, n2, act, gp, ta, tb, tc, d6,
     w1_other, w2_other, n2_other, cot_other, back_in, ahead_in,
     lines, b1, gb1, totals, turned1, got1, got2,
     local_sem, ag_send, ag_recv, core_send, core_recv, rs_send, rs_recv,
     a2a_send, a2a_recv, v_send, v_recv, pair_send, pair_recv) = refs

    i = lax.axis_index("blk")
    b = lax.axis_index("batch")
    c, y = lax.rem(i, 2), lax.div(i, 2)
    g, r = lax.div(b, sub), lax.rem(b, sub)
    x, z = lax.rem(g, 2), lax.div(g, 2)

    def device(c_=c, y_=y, x_=x, z_=z):
        return {"blk": 2 * y_ + c_, "batch": (2 * z_ + x_) * sub + r}

    def z_at(k):
        return lax.rem(z + k, zs)

    def block_at(k):
        return lax.rem(i + k, 4)

    def copy(src, dst, send, recv, to):
        return pltpu.make_async_remote_copy(
            src_ref=src, dst_ref=dst, send_sem=send, recv_sem=recv, device_id=to, device_id_type=MESH
        )

    def loop(count, body, hooks=()):
        def step(s, carry):
            body(s)
            for k, f in hooks:
                pl.when(s == k)(f)
            return carry

        lax.fori_loop(0, count, step, 0)

    partners = [device(z_=z_at(k)) for k in range(1, zs)]
    partners += [device(x_=1 - x), device(y_=1 - y), device(c_=1 - c), device(c_=1 - c, y_=1 - y)]
    barrier = pltpu.get_barrier_semaphore()
    for partner in partners:
        pl.semaphore_signal(barrier, inc=1, device_id=partner, device_id_type=MESH)

    ME = {"y": y, "x": x, "z": z}

    def before(n, axis, other):
        return n.route.index(axis) < n.route.index(other)

    def side(n, axes, all_z):
        where = (1 - y if "y" in axes else y, 1 - x if "x" in axes else x, slice(None) if all_z else z)
        return n.u.at[where + (n.rows,)]

    def neighbour(axis):
        return device(y_=1 - y) if axis == "y" else device(x_=1 - x)

    def ag_copy(n, ref, axes, k, to):
        slot = (("y" in axes) * 2 + ("x" in axes)) * zs + k
        return copy(ref, ref, ag_send.at[n.index, slot], ag_recv.at[n.index, slot], to)

    def core_copy(n, ref):
        return copy(ref, ref, core_send.at[n.index], core_recv.at[n.index], device(c_=1 - c))

    def ag_sends(n, axes, axis):
        axes = axes.replace("z", "")
        if axis == "z":
            ref = side(n, axes, False)
            return [ag_copy(n, ref, axes, k, device(z_=z_at(k))) for k in range(1, zs)]
        ref = side(n, axes, before(n, "z", axis))
        return [ag_copy(n, ref, axes + axis, 0, neighbour(axis))]

    def ag_send_part(n, axes, axis):
        for moved in ag_sends(n, axes, axis):
            moved.start()

    def ag_wait_part(n, axes):
        last = max(axes, key=n.route.index)
        axes = axes.replace("z", "")
        if last == "z":
            yy, xx = (1 - y if "y" in axes else y), (1 - x if "x" in axes else x)
            for k in range(1, zs):
                ag_copy(n, n.u.at[yy, xx, z_at(zs - k), n.rows], axes, k, device()).wait_recv()
        else:
            ag_copy(n, side(n, axes, before(n, "z", last)), axes, 0, device()).wait_recv()
        if n.other is not None and (last == "z" or before(n, "z", last)):
            core_copy(n, side(n, axes, True)).start()

    def ag_done(n):
        if n.other is not None:
            core_copy(n, n.other.at[:, :, :, n.rows]).wait_recv()

    def ag_drain(n):
        for axis in n.route:
            earlier = [other for other in "yx" if before(n, other, axis)]
            for some in range(2 ** len(earlier)):
                axes = "".join(other for bit, other in enumerate(earlier) if some >> bit & 1)
                for moved in ag_sends(n, axes, axis):
                    moved.wait_send()
        if n.other is not None:
            core_copy(n, n.u.at[:, :, :, n.rows]).wait_send()

    AXES = "yxz"

    def rs_groups(n, step):
        axis = n.route[step]
        if axis == "z":
            return [(k, 1 + k, device(z_=z_at(zs - k))) for k in range(1, zs)]
        return [(1, "yx".index(axis), neighbour(axis))]

    def rs_where(n, step, k):
        axis, out, land = n.route[step], [], []
        for other in AXES:
            if other == axis:
                out.append(z_at(zs - k) if axis == "z" else 1 - ME[axis])
                land.append(k)
            elif before(n, other, axis):
                out.append(ME[other])
                land.append(0)
            else:
                out.append(slice(None))
                land.append(slice(None))
        return tuple(out) + (n.rows,), tuple(land) + (n.rows,)

    def rs_copy(n, step, k, slot, to):
        out, land = rs_where(n, step, k)
        return copy(n.u.at[out], n.got.at[land], rs_send.at[n.index, slot], rs_recv.at[n.index, slot], to)

    def rs_core(n):
        return copy(n.other.at[:, :, :, n.rows], n.core_in.at[:, :, :, n.rows], rs_send.at[n.index, zs + 1],
                    rs_recv.at[n.index, zs + 1], device(c_=1 - c))

    def add_terms(n, place, step):
        value = n.u[tuple(place) + (n.rows,)].astype(F32)
        if n.other is not None:
            value = value + n.core_in[tuple(place) + (n.rows,)].astype(F32)
        for axis in n.route[:step]:
            for k in range(1, zs) if axis == "z" else (1,):
                where = [k if other == axis else (0 if before(n, other, axis) else at_place)
                         for other, at_place in zip(AXES, place)]
                value = value + n.got[tuple(where) + (n.rows,)].astype(F32)
        return value

    def rs_start(n):
        rs_core(n).start()

    def rs_step(n, step):
        if step == 0 and n.other is not None:
            rs_core(n).wait_recv()
        if step > 0:
            for group in rs_groups(n, step - 1):
                rs_copy(n, step - 1, *group).wait_recv()
        if step == 3:
            n.total[n.rows, :] = add_terms(n, (y, x, z), 3)
            return
        for k, slot, to in rs_groups(n, step):
            out, _ = rs_where(n, step, k)
            if step > 0 or n.other is not None:
                spans = [range(2) if isinstance(at_place, slice) else (at_place,) for at_place in out[:2]]

                def body(zz):
                    for yy in spans[0]:
                        for xx in spans[1]:
                            n.u[yy, xx, zz, n.rows] = add_terms(n, (yy, xx, zz), step).astype(BF16)

                if isinstance(out[2], slice):
                    loop(zs, body)
                else:
                    body(out[2])
            rs_copy(n, step, k, slot, to).start()

    def rs_drain(n):
        if n.other is not None:
            rs_core(n).wait_send()
        for step in range(3):
            for group in rs_groups(n, step):
                rs_copy(n, step, *group).wait_send()

    def small_sum(ref, slots, which):
        to = (device(y_=1 - y), device(c_=1 - c), device(x_=1 - x))
        to += tuple(device(z_=z_at(k)) for k in range(1, zs))

        def moved(slot):
            return copy(ref, slots.at[slot], v_send.at[which, slot], v_recv.at[which, slot], to[slot])

        def land(last):
            moved(last).wait()
            ref[...] = ref[...] + slots[last]

        def step(n):
            def run():
                if n > 0:
                    land(n - 1)
                moved(n).start()

            return run

        def line():
            land(2)
            for k in range(1, zs):
                moved(2 + k).start()

        def finish():
            for k in range(1, zs):
                moved(2 + k).wait()
            value = ref[...]
            for k in range(1, zs):
                value = value + slots[2 + k]
            ref[...] = value

        return [step(0), step(1), step(2), line, finish]

    def rows_of(s):
        return pl.ds(pl.multiple_of(s * 128, 128), 128)

    def exchange(src, dst, which):
        return [copy(src.at[block_at(k)], dst.at[i], a2a_send.at[which, k - 1],
                     a2a_recv.at[which, k - 1], {"blk": block_at(k), "batch": b})
                for k in range(1, 4)]

    def exchange_landed(dst, which):
        return [copy(dst.at[block_at(4 - k)], dst.at[block_at(4 - k)], a2a_send.at[which, k - 1],
                     a2a_recv.at[which, k - 1], {"blk": block_at(4 - k), "batch": b})
                for k in range(1, 4)]

    def axes_of(mask):
        return "".join(axis for axis, bit in (("y", Y), ("x", X), ("z", Z)) if mask & bit)

    def rows_in(part, count):
        return pl.ds(part * (288 // count), 288 // count)

    units = []
    for unit, routes in enumerate(GATHER_ROUTES):
        half = unit % 2
        ref = (ua, uw1, uw2)[unit // 2]
        pieces = (ref.at[half, c], ref.at[half, 1 - c]) if unit < 2 else (ref.at[half], None)
        for part, route in enumerate(routes):
            units.append(Unit(len(units), "".join(map(axes_of, route)), rows_in(part, len(routes)), *pieces))

    def pair(slot, src, dst):
        return copy(src, dst, pair_send.at[slot], pair_recv.at[slot], device(c_=1 - c))

    w1_swap, w2_swap = pair(0, w1_in, w1_other), pair(1, w2_in, w2_other)

    def each_core(f):
        for q in range(2):
            pl.when(c == q)(functools.partial(f, q))

    def rest_rows(matrix):
        return a_in[matrix, pl.ds(pl.multiple_of(128 * (1 - c), 64), 64), :]

    def own_attention(p):
        mine = ua.at[p, c, y, x, z]
        for m in range(2):
            main = a_in[2 * p + m, pl.ds(pl.multiple_of(64 * c, 64), 128), :]
            mine[96 * m : 96 * m + 96, :] = main.T.astype(BF16)
        rest = jnp.concatenate([rest_rows(2 * p + c), rest_rows(2 * p + 1 - c)], axis=0)
        mine[192:288, :] = rest.T.astype(BF16)

    def own_expand(q):
        both = (w1_in, w1_other) if q == 0 else (w1_other, w1_in)
        cols = slice(192 * q, 192 * q + 192)
        blocks = (
            both[0][0:128, cols],
            jnp.concatenate([both[0][128:192, cols], both[1][0:64, cols]], axis=0),
            both[1][64:192, cols],
        )
        for t, block in enumerate(blocks):
            value = block.T.astype(BF16)
            for h in range(2):
                uw1[h, y, x, z, 96 * t : 96 * t + 96, :] = value[96 * h : 96 * h + 96, :]

    def own_reduce(q):
        both = (w2_in, w2_other) if q == 0 else (w2_other, w2_in)
        for cc in range(2):
            for part_of in range(2):
                start = 384 * part_of + 192 * q
                lines[:, 192 * part_of : 192 * part_of + 192] = both[cc][:, start : start + 192]
            for t in range(3):
                uw2[cc, y, x, z, 96 * t : 96 * t + 96, :] = lines[:, 128 * t : 128 * t + 128].astype(BF16)

    def own_hidden_bias(q):
        for zz in range(zs):
            for xx in range(2):
                col = 384 * (zz % 2) + 192 * xx
                start = 384 * xx + 192 * q
                b1[zz // 2 : zz // 2 + 1, col : col + 192] = vec[8 + zz : 9 + zz, start : start + 192]

    def hidden_bias_gradient(q):
        for zz in range(zs):
            for xx in range(2):
                col = 384 * (zz % 2) + 192 * xx
                start = 384 * xx + 192 * q
                gvec[8 + zz : 9 + zz, start : start + 192] = gb1[zz // 2 : zz // 2 + 1, col : col + 192]

    columns = a_in.shape[2]
    placed = lax.broadcasted_iota(jnp.int32, (columns, 768), 1) == (
        lax.broadcasted_iota(jnp.int32, (columns, 768), 0) + columns * g
    )

    def own_vectors():
        vec[...] = jnp.zeros_like(vec)
        rows = dot_nn(vec_in[...].astype(BF16), jnp.where(placed, 1.0, 0.0).astype(BF16))
        for j in range(3):
            vec[pl.ds(3 * i + j, 1), :] = rows[j : j + 1, :]

    loads = [pltpu.make_async_copy(src, dst, local_sem.at[4 + n]) for n, (src, dst) in enumerate((
        (a_hbm, a_in), (vec_hbm, vec_in), (w1_hbm, w1_in), (w2_hbm, w2_in), (cot, stage), (mask_hbm, mask_in)
    ))]
    load_a, load_vec, load_w1, load_w2, load_cot, load_mask = loads
    for load in loads:
        load.start()

    def masked_cotangent():
        load_cot.wait()
        load_mask.wait()
        eye = lax.broadcasted_iota(jnp.int32, (128, 128), 0) == lax.broadcasted_iota(jnp.int32, (128, 128), 1)
        for s in range(4):
            row = jnp.broadcast_to(mask_in[s : s + 1, :].astype(F32), (128, 128))
            column = jnp.sum(jnp.where(eye, row, 0.0), axis=1, keepdims=True)
            stage[s] = (stage[s].astype(F32) * column).astype(BF16)

    def finish_attention(p):
        value = totals.at[p]
        for m in range(2):
            ga[2 * p + m, pl.ds(pl.multiple_of(64 * c, 64), 128), :] = value[96 * m : 96 * m + 96, :].T
        rest = value[192:288, :].T
        rows = pl.ds(pl.multiple_of(128 * (1 - c), 64), 64)
        ga[2 * p + c, rows, :] = rest[0:64, :]
        ga[2 * p + 1 - c, rows, :] = rest[64:128, :]

    w1_back = pair(6, turned1.at[pl.ds(pl.multiple_of(192 * (1 - c), 64), 192)], got1)
    w2_back = pair(7, totals.at[5 - c], got2)

    def turn_expand():
        for h in range(2):
            for t in range(3):
                turned1[128 * t : 128 * t + 128, 96 * h : 96 * h + 96] = totals[2 + h, 96 * t : 96 * t + 96, :].T
        w1_back.start()

    def join_expand(q):
        g1[:, 192 * q : 192 * q + 192] = turned1[192 * q : 192 * q + 192, :]
        g1[:, 192 * (1 - q) : 192 * (1 - q) + 192] = got1[...]

    def join_reduce(q):
        for half, value in ((q, totals.at[4 + q]), (1 - q, got2)):
            for t in range(3):
                lines[:, 128 * t : 128 * t + 128] = value[96 * t : 96 * t + 96, :]
            for part_of in range(2):
                start = 384 * part_of + 192 * half
                g2[:, start : start + 192] = lines[:, 192 * part_of : 192 * part_of + 192]

    def finish_vectors():
        value, total = gvec[...], 0.0
        for _ in range(3):
            part = value.astype(BF16)
            total = total + dot_nt(part, jnp.where(placed, 1.0, 0.0).astype(BF16))
            value = value - part.astype(F32)
        narrow_rows[...] = total
        for j in range(3):
            gv[j : j + 1, :] = narrow_rows[pl.ds(3 * i + j, 1), :]

    grads, owners = [], []
    for unit, routes in enumerate(SUM_ROUTES):
        half = unit % 2
        ref = (ua, gw1, gw2)[unit // 2]
        pieces = (ref.at[half, c], ref.at[half, 1 - c], core_in.at[half]) if unit < 2 else (ref.at[half], None, None)
        for part, route in enumerate(routes):
            grads.append(Gradient(len(grads), "".join(map(axes_of, route)), rows_in(part, len(routes)), *pieces,
                                  got.at[unit], totals.at[unit]))
            owners.append(unit)

    def summed(unit):
        if unit < 2:
            finish_attention(unit)
        elif unit < 4 and {2, 3} <= set(whole):
            turn_expand()
        elif unit >= 4 and {4, 5} <= set(whole):
            w2_back.start()

    seen, whole = set(), []

    def event(kind, *rest):
        if kind == SEND:
            ag_send_part(units[rest[0]], axes_of(rest[1]), axes_of(rest[2]))
        elif kind == GOT:
            ag_wait_part(units[rest[0]], axes_of(rest[1]))
        elif kind == WHOLE:
            ag_done(units[rest[0]])
        elif kind == SUM:
            rs_step(grads[rest[0]], rest[1])
            if rest[1] == 3:
                seen.add(rest[0])
                unit = owners[rest[0]]
                if all(k in seen for k in range(len(grads)) if owners[k] == unit):
                    whole.append(unit)
                    summed(unit)
        elif kind == DO:
            actions[rest[0]]()
        else:
            (vec_steps if kind == VEC else gvec_steps)[rest[0] + 1]()
            if (kind, rest[0]) == (SMALL, zs - 1):
                finish_vectors()

    def run(part):
        for todo in PLAN.get(part, ()):
            event(*todo)

    def parts(name, count, body):
        run(name + "0")
        hooks = [(k - 1, functools.partial(run, name + str(k))) for k in range(1, count) if name + str(k) in PLAN]
        loop(count, body, hooks)

    def started(copies):
        for moved in copies:
            moved.start()
        return copies

    def arrived(*copies):
        for moved in copies:
            moved.wait_recv()

    own_tokens = pltpu.make_async_copy(tok.at[i], x_in.at[i], local_sem.at[0])
    own_tokens.start()
    own_cot = pltpu.make_async_copy(stage.at[i], cot_in.at[i], local_sem.at[1])
    tokens_out, cot_out = exchange(tok, x_in, 0), exchange(stage, cot_in, 1)
    result_out = exchange(stage, out, 2)
    grad_out = [copy(n1.at[rows_of(block_at(k))], ig.at[i], a2a_send.at[3, k - 1], a2a_recv.at[3, k - 1],
                     {"blk": block_at(k), "batch": b}) for k in range(1, 4)]
    own_out = pltpu.make_async_copy(stage.at[i], out.at[i], local_sem.at[2])
    own_grad = pltpu.make_async_copy(n1.at[rows_of(i)], ig.at[i], local_sem.at[3])
    n2_swap, cot_swap = pair(2, n2, n2_other), pair(3, cot_in, cot_other)
    back_swap, ahead_swap = pair(4, d6, back_in), pair(5, n2, ahead_in)
    vec_steps, gvec_steps = small_sum(vec, vin, 0), small_sum(gvec, gin, 1)

    def tokens_here():
        arrived(*exchange_landed(x_in, 0))
        own_tokens.wait()

    def cotangent_here():
        arrived(*exchange_landed(cot_in, 1))
        own_cot.wait()
        cot_swap.start()

    def swaps_here():
        w1_swap.wait()
        w2_swap.wait()

    actions = {
        TOK: lambda: started(tokens_out),
        COT: lambda: started(cot_out),
        OUT: lambda: started(result_out),
        IG: lambda: started(grad_out),
        TOK_HERE: tokens_here,
        COT_HERE: cotangent_here,
        OUT_HERE: lambda: arrived(*exchange_landed(out, 2)),
        IG_HERE: lambda: arrived(*exchange_landed(ig, 3)),
        SWAP_HERE: swaps_here,
        N2S_HERE: lambda: n2_swap.wait(),
        COTS_HERE: lambda: cot_swap.wait(),
        BACKS_HERE: lambda: back_swap.wait(),
        AHEADS_HERE: lambda: ahead_swap.wait(),
    }

    load_a.wait()
    own_attention(0)
    load_vec.wait()
    own_vectors()
    load_w1.wait()
    load_w2.wait()
    pl.semaphore_wait(barrier, len(partners))
    vec_steps[0]()
    w1_swap.start()
    w2_swap.start()
    run("own1")
    own_attention(1)
    run("ownff")
    each_core(own_expand)
    each_core(own_reduce)
    run("mask")
    masked_cotangent()
    own_cot.start()
    run("ln1")
    each_core(own_hidden_bias)

    def normalise(value):
        centered = value - jnp.mean(value, axis=-1, keepdims=True)
        scale = lax.rsqrt(jnp.mean(centered * centered, axis=-1, keepdims=True) + norm_epsilon)
        return centered * scale, scale

    def first_norm(s):
        unit, _ = normalise(x_in[s].astype(F32))
        n1[rows_of(s), :] = (unit * vec[0:1, :] + vec[1:2, :]).astype(BF16)

    loop(4, first_norm)
    run("unp0")

    lanes = lax.broadcasted_iota(jnp.int32, (96, 128), 1)

    def unpack(p, s):
        for xx in range(2):
            rows = pl.ds(pl.multiple_of((2 * s + xx) * 96, 96), 96)
            for yy in range(2):
                first, second = ua.at[p, 0, yy, xx, s], ua.at[p, 1, yy, xx, s]
                lo, hi = 384 * yy, 384 * yy + 256
                for m in range(2):
                    at[2 * p + m, rows, lo : lo + 128] = first[96 * m : 96 * m + 96, :]
                    at[2 * p + m, rows, hi : hi + 128] = second[96 * m : 96 * m + 96, :]
                rest_first = first[192:288, :].astype(F32)
                rest_second = second[192:288, :].astype(F32)
                even = jnp.where(lanes < 64, rest_first, rest_second)
                odd = pltpu.roll(jnp.where(lanes < 64, rest_second, rest_first), 64, 1)
                at[2 * p, rows, lo + 128 : lo + 256] = even.astype(BF16)
                at[2 * p + 1, rows, lo + 128 : lo + 256] = odd.astype(BF16)

    def project(m, dst, bias):
        for n in range(3):
            value = dot_nt(n1[...], at[m, 256 * n : 256 * n + 256, :])
            if bias is not None:
                value = value + vec[bias : bias + 1, 256 * n : 256 * n + 256]
            value = value.astype(BF16)
            if m == 0:
                value = value * jnp.asarray(HEAD ** (-0.5), BF16)
            dst[2 * n] = value[:, 0:128]
            dst[2 * n + 1] = value[:, 128:256]

    loop(zs, functools.partial(unpack, 0))
    run("projq")
    project(0, q6, 2)
    run("projk")
    project(1, k6, None)

    half_lane = lax.broadcasted_iota(jnp.int32, (512, 128), 1) // HEAD

    def half_of(value, which):
        return jnp.where(half_lane == which, value, jnp.zeros_like(value))

    def turn(value):
        return value.astype(F32).T.astype(BF16)

    def attend(p):
        queries, keys = q6[p], k6[p]
        for which in range(2):
            scores = dot_nt(half_of(keys, which), queries)
            expo = jnp.exp(scores - jnp.max(scores, axis=0, keepdims=True))
            probs = (expo * (1.0 / jnp.sum(expo, axis=0, keepdims=True))).astype(BF16)
            pt[2 * p + which] = probs

    def mix(p):
        values_t = turn(v6[p])
        mixed = [dot_nn(values_t[64 * which : 64 * which + 64, :], pt[2 * p + which]) for which in range(2)]
        o6[p] = jnp.concatenate(mixed, axis=0).T.astype(BF16)

    parts("attend", 6, attend)
    run("unp1")
    loop(zs, functools.partial(unpack, 1))
    run("projv")
    project(2, v6, 3)
    parts("mix", 6, mix)

    run("ao")
    for n in range(3):
        cols = slice(256 * n, 256 * n + 256)
        value = dot_nt(lane_tiles(o6), at[3, cols, :]) + vec[4:5, cols]
        for s in range(4):
            h1[128 * s : 128 * s + 128, cols] = x_in[s, :, cols].astype(F32) + value[128 * s : 128 * s + 128]

    def second_norm(s):
        unit, _ = normalise(h1[rows_of(s), :])
        n2[rows_of(s), :] = (unit * vec[5:6, :] + vec[6:7, :]).astype(BF16)

    run("ln2")
    loop(4, second_norm)
    n2_swap.start()

    def expand_block(s):
        def piece(ref):
            return jnp.concatenate([ref[96 * t : 96 * t + 96, :] for t in range(3)], axis=1)

        return jnp.concatenate(
            [jnp.concatenate([piece(uw1.at[h, yy, xx, 2 * s + zz]) for yy in range(2)], axis=1)
             for zz in range(2) for xx in range(2) for h in range(2)],
            axis=0,
        )

    def reduce_block(s):
        def piece(ref):
            return jnp.concatenate([ref[96 * t : 96 * t + 96, :] for t in range(3)], axis=1)

        return jnp.concatenate(
            [jnp.concatenate([piece(uw2.at[cc, s, xx, zz]) for cc in range(2)], axis=1)
             for zz in range(zs) for xx in range(2)],
            axis=0,
        )

    def block_rows(owner, s):
        return pl.ds(pl.multiple_of((2 * owner + s) * 512, 512), 512)

    def expand(owner, normed, s):
        rows = block_rows(owner, s)
        inner = dot_nt(normed[...], expand_block(s)) + b1[pl.ds(s, 1), :]
        square = inner * inner
        tanh = jnp.tanh(GELU_SCALE * inner * (1.0 + GELU_CUBE * square))
        act[rows, :] = (0.5 * inner * (1.0 + tanh)).astype(BF16)
        slope = 0.5 * (1.0 + tanh) + 0.5 * inner * (1.0 - tanh * tanh) * (
            GELU_SCALE * (1.0 + 3.0 * GELU_CUBE * square)
        )
        gp[rows, :] = slope.astype(BF16)

    parts("expa", 2, functools.partial(expand, 0, n2))
    parts("expb", 2, functools.partial(expand, 1, n2_other))

    gvec[...] = jnp.zeros_like(gvec)

    def transpose_rows(dst, s, value):
        dst[:, 128 * s : 128 * s + 128] = turn(value)

    run("trY")
    total = jnp.zeros((1, 768), F32)
    for s in range(4):
        transpose_rows(ta, s, cot_in[s])
        total = total + jnp.sum(cot_in[s].astype(F32), axis=0, keepdims=True)
    gvec[7:8, :] = total
    for s in range(4):
        transpose_rows(tb, s, cot_other[s])

    def both_rows(ref, s):
        return jnp.concatenate([ref[block_rows(0, s), :], ref[block_rows(1, s), :]], axis=0)

    def reduce_back(s):
        grad = dot_nn(jnp.concatenate([ta[...], tb[...]], axis=1), both_rows(act, s)).astype(BF16)
        for zz in range(zs):
            for xx in range(2):
                row = 96 * (2 * zz + xx)
                for cc in range(2):
                    for t in range(3):
                        col = 384 * cc + 128 * t
                        gw2[cc, s, xx, zz, 96 * t : 96 * t + 96, :] = grad[row : row + 96, col : col + 128]

    parts("gw2_", 2, reduce_back)

    def rows_together(ref):
        return jnp.concatenate([ref[s] for s in range(4)], axis=0)

    def inner_back(owner, cotangent_rows, s):
        rows = block_rows(owner, s)
        grad = dot_nn(rows_together(cotangent_rows), reduce_block(s)) * gp[rows, :].astype(F32)
        low = grad.astype(BF16)
        gp[rows, :] = low
        sums = jnp.sum(low.astype(F32), axis=0, keepdims=True)
        gb1[pl.ds(s, 1), :] = sums if owner == 1 else gb1[pl.ds(s, 1), :] + sums

    def norm_back(owner):
        acc[...] = dot_nn(gp[block_rows(owner, 0), :], expand_block(0))
        acc[...] += dot_nn(gp[block_rows(owner, 1), :], expand_block(1))

    parts("innb", 2, functools.partial(inner_back, 1, cot_other))
    run("dn2b")
    norm_back(1)
    for t in range(6):
        d6[t] = acc[:, 128 * t : 128 * t + 128].astype(BF16)
    back_swap.start()
    parts("inna", 2, functools.partial(inner_back, 0, cot_in))
    each_core(hidden_bias_gradient)
    run("dn2a")
    norm_back(0)

    def expand_back(s):
        turned = jnp.concatenate([turn(gp[block_rows(owner, s), :]) for owner in range(2)], axis=1)
        normed = jnp.concatenate([n2[...], n2_other[...]], axis=0)
        grad = dot_nn(turned, normed).astype(BF16)
        for zz in range(2):
            for xx in range(2):
                for h in range(2):
                    row = 384 * zz + 192 * xx + 96 * h
                    for yy in range(2):
                        for t in range(3):
                            col = 384 * yy + 128 * t
                            gw1[h, yy, xx, 2 * s + zz, 96 * t : 96 * t + 96, :] = grad[
                                row : row + 96, col : col + 128
                            ]

    parts("gw1_", 2, expand_back)
    run("hid")

    def norm_gradient(value, scale_row, grad):
        unit, scale = normalise(value)
        gain_sum = jnp.sum(grad * unit, axis=0, keepdims=True)
        bias_sum = jnp.sum(grad, axis=0, keepdims=True)
        inner = grad * scale_row
        mean = jnp.mean(inner, axis=-1, keepdims=True)
        along = jnp.mean(inner * unit, axis=-1, keepdims=True)
        return scale * (inner - mean - unit * along), gain_sum, bias_sum

    def hidden_back(s):
        rows = rows_of(s)
        grad_in = jnp.concatenate([back_in[t, rows, :] for t in range(6)], axis=1)
        grad_in = acc[rows, :] + grad_in.astype(F32)
        grad, gain_sum, bias_sum = norm_gradient(h1[rows, :], vec[5:6, :], grad_in)
        grad = grad + cot_in[s].astype(F32)
        acc[rows, :] = grad
        low = grad.astype(BF16)
        n2[rows, :] = low
        gvec[5:6, :] += gain_sum
        gvec[6:7, :] += bias_sum
        gvec[4:5, :] += jnp.sum(low.astype(F32), axis=0, keepdims=True)

    loop(4, hidden_back)

    run("dO")
    for n in range(3):
        value = dot_nn(n2[...], at[3, :, 256 * n : 256 * n + 256]).astype(BF16)
        d6[2 * n] = value[:, 0:128]
        d6[2 * n + 1] = value[:, 128:256]
    run("gao")
    for s in range(4):
        transpose_rows(tc, s, n2[128 * s : 128 * s + 128, :])
    gp[768:1536, :] = dot_nn(tc[...], lane_tiles(o6)).astype(BF16)

    def value_back(p):
        grads_in, grad_value = d6[p], 0.0
        for which in range(2):
            grad_value = grad_value + dot_nn(pt[2 * p + which], half_of(grads_in, which))
        tc[rows_of(p), :] = grad_value.T.astype(BF16)
        o6[p] = grad_value.astype(BF16)

    def attend_back(p):
        rows = rows_of(p)
        queries, keys, values, grads_in = q6[p], k6[p], v6[p], d6[p]
        keys_t = turn(keys)
        grad_query, grad_key = [], 0.0
        for which in range(2):
            wide = pt[2 * p + which].astype(F32)
            grad_probs = dot_nt(half_of(values, which), grads_in)
            inner = jnp.sum(wide * grad_probs, axis=0, keepdims=True)
            grad_scores = (wide * (grad_probs - inner)).astype(BF16)
            grad_query.append(dot_nn(keys_t[64 * which : 64 * which + 64, :], grad_scores))
            grad_key = grad_key + dot_nn(grad_scores, half_of(queries, which))
        grad_query = jnp.concatenate(grad_query, axis=0) * HEAD ** (-0.5)
        ta[rows, :] = grad_query.astype(BF16)
        tb[rows, :] = grad_key.T.astype(BF16)
        q6[p] = grad_query.T.astype(BF16)
        k6[p] = grad_key.astype(BF16)

    def pack(p, first_row, second_row):
        def body(s):
            for xx in range(2):
                offset = (2 * s + xx) * 96
                rows = [pl.ds(pl.multiple_of(first_row + offset, 96), 96),
                        pl.ds(pl.multiple_of(second_row + offset, 96), 96)]
                first, second = ua.at[p, 0, :, xx, s], ua.at[p, 1, :, xx, s]
                for yy in range(2):
                    lo, mid, hi = 384 * yy, 384 * yy + 128, 384 * yy + 256
                    for m in range(2):
                        first[yy, 96 * m : 96 * m + 96, :] = gp[rows[m], lo : lo + 128]
                        second[yy, 96 * m : 96 * m + 96, :] = gp[rows[m], hi : hi + 128]
                    even = gp[rows[0], mid : mid + 128].astype(F32)
                    odd = pltpu.roll(gp[rows[1], mid : mid + 128].astype(F32), 64, 1)
                    first[yy, 192:288, :] = jnp.where(lanes < 64, even, odd).astype(BF16)
                    second[yy, 192:288, :] = jnp.where(lanes < 64, odd, even).astype(BF16)

        loop(zs, body)

    parts("av", 6, value_back)
    run("gav")
    for n in units[VO[0] : VO[1] + 1]:
        ag_drain(n)
    gp[0:768, :] = dot_nn(tc[...], n1[...]).astype(BF16)
    pack(1, 0, 768)
    for n in grads[AVO[0] : AVO[1] + 1]:
        rs_start(n)
    parts("ab", 6, attend_back)
    run("gaqk")
    for n in units[QK[0] : QK[1] + 1]:
        ag_drain(n)
    gp[0:768, :] = dot_nn(ta[...], n1[...]).astype(BF16)
    gp[768:1536, :] = dot_nn(tb[...], n1[...]).astype(BF16)
    pack(0, 0, 768)
    for n in grads[AQK[0] : AQK[1] + 1]:
        rs_start(n)

    def reduce(owner):
        value = dot_nt(act[block_rows(owner, 0), :], reduce_block(0))
        return value + dot_nt(act[block_rows(owner, 1), :], reduce_block(1))

    def layer_output():
        run("redb")
        n2[...] = reduce(1).astype(BF16)
        ahead_swap.start()
        run("reda")
        h1[...] = h1[...] + vec[7:8, :] + reduce(0)
        run("outst")
        for moved in cot_out:
            moved.wait_send()
        for s in range(4):
            rows = slice(128 * s, 128 * s + 128)
            stage[s] = (h1[rows, :] + ahead_in[rows, :].astype(F32)).astype(BF16)
        own_out.start()

    layer_output()
    run("dn1")
    h1[...] = dot_nn(lane_tiles(q6), at[0])
    h1[...] += dot_nn(lane_tiles(k6), at[1])
    h1[...] += dot_nn(lane_tiles(o6), at[2])
    gvec[2:3, :] = jnp.sum(lane_tiles(q6).astype(F32), axis=0, keepdims=True)
    gvec[3:4, :] = jnp.sum(lane_tiles(o6).astype(F32), axis=0, keepdims=True)

    run("inb")

    def input_back(s):
        rows = rows_of(s)
        grad, gain_sum, bias_sum = norm_gradient(x_in[s].astype(F32), vec[0:1, :], h1[rows, :])
        n1[rows, :] = (grad + acc[rows, :]).astype(BF16)
        gvec[0:1, :] += gain_sum
        gvec[1:2, :] += bias_sum

    loop(4, input_back)
    gvec_steps[0]()
    own_grad.start()

    def join():
        w1_back.wait()
        each_core(join_expand)
        w2_back.wait()
        each_core(join_reduce)

    joined = False
    for n, todo in enumerate(PLAN["end"]):
        if not joined and n >= len(PLAN["end"]) - 3 and {2, 3, 4, 5} <= set(whole):
            join()
            joined = True
        event(*todo)
    if not joined:
        join()

    own_out.wait()
    own_grad.wait()
    for moved in tokens_out + result_out + grad_out:
        moved.wait_send()
    for n in units[VO[1] + 1 :]:
        ag_drain(n)
    for n in grads:
        rs_drain(n)


def layer(sub, tokens, cotangent, span_mask, vectors, attention, expand, reduce_t):
    zs = GROUPS // 2
    seqs, block, width = tokens.shape
    rows = seqs * block
    columns = attention.shape[2]
    piece = (3 * columns, 128)
    vmem = lambda shape, dtype: pltpu.VMEM(shape, dtype)
    half = (2, 2, 2, zs) + piece
    scratch = [vmem(value.shape, value.dtype) for value in (span_mask, vectors, attention, expand, reduce_t)]
    scratch += [vmem((2,) + half, BF16)] + [vmem(half, BF16)] * 4
    scratch += [vmem((2, 2, 2, zs) + piece, BF16), vmem((6, 2, 2, zs) + piece, BF16)]
    scratch += [vmem(tokens.shape, BF16)] * 3
    scratch += [vmem((16, width), F32)] * 2
    scratch += [vmem((zs + 2, 16, width), F32)] * 2
    scratch += [vmem((16, columns), F32)]
    tiles = vmem((width // 128, rows, 128), BF16)
    flat = vmem((rows, width), BF16)
    turned = vmem((width, rows), BF16)
    scratch += [vmem((4, width, width), BF16), flat, tiles, tiles, tiles, tiles]
    scratch += [vmem((HEADS, rows, rows), BF16), vmem((rows, width), F32), vmem((rows, width), F32)]
    scratch += [flat, vmem((4 * rows, width), BF16), vmem((4 * rows, width), BF16)]
    scratch += [turned, turned, turned, tiles]
    scratch += [vmem(expand.shape, F32), vmem(reduce_t.shape, F32), flat, vmem(tokens.shape, BF16)]
    scratch += [tiles, flat, vmem((columns, width // 2), F32), vmem((2, width), F32), vmem((2, width), F32)]
    scratch += [vmem((6,) + piece, F32), vmem((width // 2, 2 * columns), F32)]
    scratch += [vmem((2 * columns, 2 * columns), F32), vmem(piece, F32)]
    scratch += [pltpu.SemaphoreType.DMA((10,))]
    gathered, summed = sum(map(len, GATHER_ROUTES)), sum(map(len, SUM_ROUTES))
    scratch += [pltpu.SemaphoreType.DMA((gathered, 4 * zs))] * 2
    scratch += [pltpu.SemaphoreType.DMA((gathered,))] * 2
    scratch += [pltpu.SemaphoreType.DMA((summed, zs + 2))] * 2
    scratch += [pltpu.SemaphoreType.DMA((4, 3))] * 2
    scratch += [pltpu.SemaphoreType.DMA((2, zs + 2))] * 2
    scratch += [pltpu.SemaphoreType.DMA((8,))] * 2
    in_vmem = pl.BlockSpec(memory_space=pltpu.VMEM)
    anywhere = pl.BlockSpec(memory_space=pl.ANY)
    return pl.pallas_call(
        functools.partial(kernel, sub, zs),
        out_shape=(
            jax.ShapeDtypeStruct(tokens.shape, BF16),
            jax.ShapeDtypeStruct(tokens.shape, BF16),
            jax.ShapeDtypeStruct(attention.shape, F32),
            jax.ShapeDtypeStruct(expand.shape, F32),
            jax.ShapeDtypeStruct(reduce_t.shape, F32),
            jax.ShapeDtypeStruct(vectors.shape, F32),
        ),
        in_specs=[anywhere] * 7,
        out_specs=(anywhere, anywhere) + (in_vmem,) * 4,
        scratch_shapes=scratch,
        compiler_params=pltpu.CompilerParams(
            collective_id=0, has_side_effects=True, vmem_limit_bytes=65400 * 1024
        ),
    )(tokens, cotangent, span_mask, vectors, attention, expand, reduce_t)


def update_kernel(rates, *refs):
    count = len(rates)
    ins, (result, grad) = refs[: 4 * count], refs[4 * count : 4 * count + 2]
    outs, (result_out, grad_out) = refs[4 * count + 2 : 7 * count + 2], refs[7 * count + 2 : 7 * count + 4]
    held, (low, wide, passed) = refs[7 * count + 4 : 11 * count + 4], refs[11 * count + 4 : 11 * count + 7]
    in_sems, out_sems = refs[11 * count + 7 :]
    loads = [pltpu.make_async_copy(ins[n], held[n], in_sems.at[n]) for n in range(4 * count)]
    stores = [pltpu.make_async_copy(held[4 * n + m], outs[3 * n + m], out_sems.at[3 * n + m])
              for n in range(count) for m in range(3)]
    load_grad = pltpu.make_async_copy(grad, low, in_sems.at[4 * count])
    store_grad = pltpu.make_async_copy(wide, grad_out, out_sems.at[3 * count])
    load_result = pltpu.make_async_copy(result, passed, in_sems.at[4 * count + 1])
    store_result = pltpu.make_async_copy(passed, result_out, out_sems.at[3 * count + 1])
    load_grad.start()
    load_result.start()
    for copy in loads:
        copy.start()
    load_result.wait()
    store_result.start()
    load_grad.wait()

    def widen(s, carry):
        wide[s] = low[s].astype(F32)
        return carry

    lax.fori_loop(0, low.shape[0], widen, 0)
    store_grad.start()
    for n in range(count):
        for m in range(4):
            loads[4 * n + m].wait()
        weight, one, two, gradient = held[4 * n : 4 * n + 4]
        values = adamw(weight[...], one[...], two[...], gradient[...], rates[n])
        for ref, value in zip((weight, one, two), values):
            ref[...] = value
        for m in range(3):
            stores[3 * n + m].start()
    for copy in stores + [store_grad, store_result]:
        copy.wait()


def update(rates, arrays, result, grad):
    flat = [value for group in arrays for value in group]
    new = [jax.ShapeDtypeStruct(value.shape, F32) for group in arrays for value in group[:3]]
    new += [jax.ShapeDtypeStruct(result.shape, BF16), jax.ShapeDtypeStruct(grad.shape, F32)]
    anywhere = pl.BlockSpec(memory_space=pl.ANY)
    scratch = [pltpu.VMEM(value.shape, F32) for value in flat]
    scratch += [pltpu.VMEM(grad.shape, BF16), pltpu.VMEM(grad.shape, F32), pltpu.VMEM(result.shape, BF16)]
    scratch += [pltpu.SemaphoreType.DMA((len(flat) + 2,)), pltpu.SemaphoreType.DMA((len(new),))]
    return pl.pallas_call(
        functools.partial(update_kernel, rates),
        out_shape=tuple(new),
        in_specs=[anywhere] * (len(flat) + 2),
        out_specs=(anywhere,) * len(new),
        scratch_shapes=scratch,
        compiler_params=pltpu.CompilerParams(vmem_limit_bytes=63 * 1024 * 1024),
    )(*flat, result, grad)


def local(
    sub,
    tokens,
    cotangent,
    span_mask,
    attention_weight,
    expand_weight,
    reduce_weight,
    vectors,
    attention_first,
    attention_second,
    expand_first,
    expand_second,
    reduce_first,
    reduce_second,
    vector_first,
    vector_second,
):
    together = [[n * sub + m for m in range(sub)] for n in range(GROUPS)]

    def widen(value, axis):
        if sub == 1:
            return value
        low = lax.all_gather(
            value.astype(BF16), "batch", axis=axis, tiled=True, axis_index_groups=together
        )
        return low.astype(F32)

    def narrow(value, axis):
        if sub == 1:
            return value
        return lax.psum_scatter(
            value, "batch", scatter_dimension=axis, tiled=True, axis_index_groups=together
        )

    out_tokens, input_grad, ga, g1, g2, gv = layer(
        sub,
        tokens,
        cotangent,
        span_mask,
        widen(vectors, 1),
        widen(attention_weight, 2),
        widen(expand_weight, 1),
        widen(reduce_weight.T, 0),
    )
    arrays = (
        (attention_weight, attention_first, attention_second, narrow(ga, 2)),
        (expand_weight, expand_first, expand_second, narrow(g1, 1)),
        (reduce_weight.T, reduce_first.T, reduce_second.T, narrow(g2, 0)),
        (vectors, vector_first, vector_second, narrow(gv, 1)),
    )
    rates = (rate_attention, rate_expand, rate_reduce, rate_vector)
    new = update(rates, arrays, out_tokens, input_grad)
    return new[-2:] + new[0:6] + tuple(value.T for value in new[6:9]) + new[9:12]


def solution(mesh):
    sub = mesh.shape["batch"] // GROUPS
    sequences = P("batch", "blk", None)
    attention = P(None, "blk", "batch")
    matrix = P("blk", "batch")
    return jax.shard_map(
        functools.partial(local, sub),
        mesh=mesh,
        in_specs=(sequences, sequences, P("batch", "blk"), attention, matrix, matrix, matrix)
        + (attention,) * 2
        + (matrix,) * 6,
        out_specs=(sequences,) * 2 + (attention,) * 3 + (matrix,) * 9,
        check_vma=False,
    )
```

```python
import functools
import math

import jax
import jax.numpy as jnp
from jax import lax
from jax.experimental import pallas as pl
from jax.experimental.pallas import tpu as pltpu
from jax.sharding import PartitionSpec as P

HEADS = 12
HEAD = 64
STEP = 10
GROUPS = 8

norm_epsilon = 1e-05
beta_one = 0.9
beta_two = 0.999
adam_epsilon = 1e-08
decay_weight = 0.1
rate_attention = 0.05
rate_expand = 0.03
rate_reduce = 0.015
rate_vector = 0.4

F32 = jnp.float32
BF16 = jnp.bfloat16
MESH = pl.DeviceIdType.MESH
GELU_SCALE = math.sqrt(2.0 / math.pi)
GELU_CUBE = 0.044715


def adamw(weight, moment_one, moment_two, gradient, step_rate):
    moment_one = beta_one * moment_one + (1.0 - beta_one) * gradient
    moment_two = beta_two * moment_two + (1.0 - beta_two) * gradient * gradient
    corrected_one = moment_one / (1.0 - beta_one**STEP)
    corrected_two = moment_two / (1.0 - beta_two**STEP)
    updated = weight - step_rate * (
        corrected_one / (jnp.sqrt(corrected_two) + adam_epsilon) + decay_weight * weight
    )
    return (updated, moment_one, moment_two)


def dot_nn(left, right):
    return lax.dot_general(left, right, (((1,), (0,)), ((), ())), preferred_element_type=F32)


def dot_nt(left, right):
    return lax.dot_general(left, right, (((1,), (1,)), ((), ())), preferred_element_type=F32)


X, Y, Z = 1, 2, 4
(N_QKA, N_QKB, N_VOA, N_VOB, N_W10A, N_W10B, N_W11A, N_W11B, N_W20A, N_W20B, N_W21A, N_W21B) = range(12)
(N_AQKA, N_AQKB, N_AVO, N_G10, N_G11A, N_G11B, N_G20, N_G21A, N_G21B) = range(9)
QK, VO = (N_QKA, N_QKB), (N_VOA, N_VOB)
AQK, AVO = (N_AQKA, N_AQKB), (N_AVO, N_AVO)
SEND, GOT, WHOLE, SUM, VEC, SMALL, DO = range(7)
(TOK, COT, OUT, IG, TOK_HERE, COT_HERE, OUT_HERE,
 IG_HERE, SWAP_HERE, N2S_HERE, COTS_HERE, BACKS_HERE, AHEADS_HERE) = range(13)
GATHER_ROUTES = (
    ((Z, Y, X), (Z, Y, X),),
    ((Z, Y, X), (Z, Y, X),),
    ((Y, Z, X), (X, Z, Y),),
    ((Z, X, Y), (Y, Z, X),),
    ((Z, X, Y), (Z, X, Y),),
    ((Y, X, Z), (Z, Y, X),),
)
SUM_ROUTES = (
    ((Y, X, Z), (X, Z, Y),),
    ((Y, X, Z),),
    ((Y, X, Z),),
    ((X, Z, Y), (X, Z, Y),),
    ((Y, X, Z),),
    ((Z, X, Y), (X, Z, Y),),
)
PLAN = dict(
    own1=(
        (SEND, N_QKA, 0, Z),
    ),
    ownff=(
        (DO, TOK), (SEND, N_QKB, 0, Z), (VEC, 0), (DO, SWAP_HERE),
    ),
    mask=(
        (SEND, N_W10B, 0, X), (SEND, N_W21A, 0, X),
    ),
    ln1=(
        (SEND, N_VOA, 0, Z), (VEC, 1), (GOT, N_QKA, Z), (SEND, N_QKA, Z, X), (GOT, N_W10B, X),
        (SEND, N_QKA, Z, Y), (SEND, N_VOB, 0, Z), (GOT, N_W21A, X), (GOT, N_QKB, Z), (SEND, N_QKB, Z, X),
        (SEND, N_QKB, Z, Y), (SEND, N_W11A, 0, Z), (GOT, N_QKA, Z | X), (DO, TOK_HERE), (GOT, N_VOA, Z),
        (SEND, N_VOA, Z, X), (SEND, N_VOA, Z, Y), (GOT, N_QKB, Z | X), (VEC, 2), (GOT, N_QKA, Z | Y),
        (SEND, N_QKA, Z | Y, X), (SEND, N_W11B, 0, Z), (GOT, N_VOB, Z), (SEND, N_VOB, Z, Y),
        (GOT, N_VOA, Z | X), (GOT, N_QKB, Z | Y), (SEND, N_QKB, Z | Y, X), (SEND, N_W10A, 0, Z),
        (GOT, N_W11A, Z), (VEC, 3),
    ),
    unp0=(
        (SEND, N_VOB, Z, X), (SEND, N_W11B, 0, Y), (SEND, N_W10A, 0, Y), (GOT, N_QKA, Z | Y | X),
        (GOT, N_VOA, Z | Y), (SEND, N_W10B, 0, Z), (DO, COT), (GOT, N_W11B, Z), (SEND, N_VOA, Z | Y, X),
        (GOT, N_QKB, Z | Y | X), (GOT, N_VOB, Z | Y), (SEND, N_W10B, X, Z), (GOT, N_W11B, Y),
        (GOT, N_W10A, Z), (GOT, N_W10A, Y), (SEND, N_VOB, Z | Y, X), (WHOLE, N_QKA), (WHOLE, N_QKB),
    ),
    projk=(
        (GOT, N_VOB, Z | X), (SEND, N_W11B, Y, Z),
    ),
    attend0=(
        (GOT, N_W10B, Z),
    ),
    attend1=(
        (SEND, N_W11A, Z, X), (SEND, N_W11A, Z, Y),
    ),
    attend2=(
        (GOT, N_VOA, Z | Y | X), (SEND, N_W10A, Y, Z),
    ),
    attend3=(
        (GOT, N_W10B, X | Z), (SEND, N_W11B, Z, X),
    ),
    attend4=(
        (SEND, N_W10B, Z, Y), (GOT, N_VOB, Z | Y | X), (SEND, N_W20A, 0, Z),
    ),
    attend5=(
        (DO, COT_HERE), (GOT, N_W11B, Y | Z),
    ),
    unp1=(
        (SEND, N_W10A, Z, X), (WHOLE, N_VOA), (WHOLE, N_VOB), (SEND, N_W10B, X | Z, Y),
    ),
    projv=(
        (GOT, N_W11A, Z | X), (SEND, N_W20B, 0, Z), (GOT, N_W11A, Z | Y),
    ),
    mix0=(
        (DO, COTS_HERE), (GOT, N_W10A, Y | Z),
    ),
    mix2=(
        (SEND, N_W11B, Y | Z, X),
    ),
    mix4=(
        (SEND, N_W11A, Z | X, Y),
    ),
    ao=(
        (GOT, N_W11B, Z | X),
    ),
    ln2=(
        (SEND, N_W21B, 0, Z), (GOT, N_W10B, Z | Y),
    ),
    expa0=(
        (GOT, N_W20A, Z), (SEND, N_W10A, Y | Z, X), (SEND, N_W21A, 0, Y), (GOT, N_W10A, Z | X),
        (SEND, N_W21A, 0, Z), (SEND, N_W20A, Z, Y), (GOT, N_W10B, X | Z | Y), (GOT, N_W20B, Z),
        (SEND, N_W20A, Z, X), (DO, N2S_HERE), (GOT, N_W11B, Y | Z | X), (SEND, N_W21A, X, Z),
        (GOT, N_W11A, Z | X | Y), (GOT, N_W21B, Z), (SEND, N_W21B, Z, Y), (GOT, N_W21A, Y),
        (SEND, N_W20B, Z, X), (GOT, N_W10A, Y | Z | X),
    ),
    expa1=(
        (SEND, N_W21A, Y, Z), (SEND, N_W20B, Z, Y), (GOT, N_W21A, Z), (GOT, N_W20A, Z | Y),
        (SEND, N_W21A, Y, X),
    ),
    expb0=(
        (SEND, N_W21B, Z, X), (GOT, N_W20A, Z | X), (SEND, N_W20A, Z | X, Y),
    ),
    expb1=(
        (GOT, N_W21A, X | Z), (GOT, N_W21B, Z | Y), (SEND, N_W21B, Z | Y, X), (GOT, N_W20B, Z | X),
    ),
    trY=(
        (SEND, N_W20B, Z | X, Y), (GOT, N_W21A, Y | X), (SEND, N_W21A, Y | X, Z), (GOT, N_W21A, Y | Z),
        (GOT, N_W20B, Z | Y),
    ),
    gw2_1=(
        (GOT, N_W21B, Z | X), (GOT, N_W20A, Z | X | Y),
    ),
    innb0=(
        (GOT, N_W21A, Y | X | Z), (GOT, N_W21B, Z | Y | X), (SUM, N_G20, 0), (SUM, N_G21A, 0),
        (SUM, N_G21B, 0), (GOT, N_W20B, Z | X | Y),
    ),
    gw1_0=(
        (DO, BACKS_HERE),
    ),
    gw1_1=(
        (SUM, N_G21B, 1),
    ),
    hid=(
        (SUM, N_G10, 0), (SUM, N_G11A, 0), (SUM, N_G11B, 0),
    ),
    dO=(
        (SUM, N_G20, 1), (SUM, N_G21A, 1),
    ),
    ab0=(
        (SUM, N_G21B, 2), (SUM, N_G11A, 1),
    ),
    ab3=(
        (SUM, N_AVO, 0), (SUM, N_G10, 1), (SUM, N_G11B, 1),
    ),
    ab4=(
        (SUM, N_G21B, 3),
    ),
    ab5=(
        (SUM, N_G11A, 2),
    ),
    redb=(
        (SUM, N_G20, 2),
    ),
    reda=(
        (SUM, N_G11B, 2),
    ),
    outst=(
        (SUM, N_AQKB, 0), (SUM, N_AQKA, 0), (SUM, N_G10, 2), (DO, AHEADS_HERE),
    ),
    dn1=(
        (SUM, N_AVO, 1),
    ),
    inb=(
        (SUM, N_G21A, 2), (SUM, N_G11A, 3), (SUM, N_G20, 3), (DO, OUT),
    ),
    end=(
        (SUM, N_AQKB, 1), (SUM, N_AQKA, 1), (SUM, N_G10, 3), (DO, IG), (SUM, N_AVO, 2), (SUM, N_AQKB, 2),
        (DO, OUT_HERE), (SMALL, 0), (SUM, N_AQKA, 2), (SMALL, 1), (SMALL, 2), (SUM, N_AVO, 3), (DO, IG_HERE),
        (SUM, N_AQKA, 3), (SUM, N_G11B, 3), (SMALL, 3), (SUM, N_G21A, 3), (SUM, N_AQKB, 3),
    ),
)


def lane_tiles(ref, count=6):
    return jnp.concatenate([ref[t] for t in range(count)], axis=1)


class Unit:
    def __init__(self, index, route, rows, u, other):
        self.index, self.route, self.rows, self.u, self.other = index, route, rows, u, other


class Gradient:
    def __init__(self, index, route, rows, u, other, core_in, got, total):
        self.index, self.route, self.rows, self.u, self.other = index, route, rows, u, other
        self.core_in, self.got, self.total = core_in, got, total


def kernel(sub, zs, *refs):
    (tok, cot, mask_hbm, vec_hbm, a_hbm, w1_hbm, w2_hbm,
     out, ig, ga, g1, g2, gv,
     mask_in, vec_in, a_in, w1_in, w2_in, ua, uw1, uw2, gw1, gw2, core_in, got,
     x_in, cot_in, stage, vec, gvec, vin, gin, narrow_rows,
     at, n1, q6, k6, v6, o6, pt, h1, acc, n2, act, gp, ta, tb, tc, d6,
     w1_other, w2_other, n2_other, cot_other, back_in, ahead_in,
     lines, b1, gb1, totals, turned1, got1, got2,
     local_sem, ag_send, ag_recv, core_send, core_recv, rs_send, rs_recv,
     a2a_send, a2a_recv, v_send, v_recv, pair_send, pair_recv) = refs

    i = lax.axis_index("blk")
    b = lax.axis_index("batch")
    c, y = lax.rem(i, 2), lax.div(i, 2)
    g, r = lax.div(b, sub), lax.rem(b, sub)
    x, z = lax.rem(g, 2), lax.div(g, 2)

    def device(c_=c, y_=y, x_=x, z_=z):
        return {"blk": 2 * y_ + c_, "batch": (2 * z_ + x_) * sub + r}

    def z_at(k):
        return lax.rem(z + k, zs)

    def block_at(k):
        return lax.rem(i + k, 4)

    def copy(src, dst, send, recv, to):
        return pltpu.make_async_remote_copy(
            src_ref=src, dst_ref=dst, send_sem=send, recv_sem=recv, device_id=to, device_id_type=MESH
        )

    def loop(count, body, hooks=()):
        def step(s, carry):
            body(s)
            for k, f in hooks:
                pl.when(s == k)(f)
            return carry

        lax.fori_loop(0, count, step, 0)

    partners = [device(z_=z_at(k)) for k in range(1, zs)]
    partners += [device(x_=1 - x), device(y_=1 - y), device(c_=1 - c), device(c_=1 - c, y_=1 - y)]
    barrier = pltpu.get_barrier_semaphore()
    for partner in partners:
        pl.semaphore_signal(barrier, inc=1, device_id=partner, device_id_type=MESH)

    ME = {"y": y, "x": x, "z": z}

    def before(n, axis, other):
        return n.route.index(axis) < n.route.index(other)

    def side(n, axes, all_z):
        where = (1 - y if "y" in axes else y, 1 - x if "x" in axes else x, slice(None) if all_z else z)
        return n.u.at[where + (n.rows,)]

    def neighbour(axis):
        return device(y_=1 - y) if axis == "y" else device(x_=1 - x)

    def ag_copy(n, ref, axes, k, to):
        slot = (("y" in axes) * 2 + ("x" in axes)) * zs + k
        return copy(ref, ref, ag_send.at[n.index, slot], ag_recv.at[n.index, slot], to)

    def core_copy(n, ref):
        return copy(ref, ref, core_send.at[n.index], core_recv.at[n.index], device(c_=1 - c))

    def ag_sends(n, axes, axis):
        axes = axes.replace("z", "")
        if axis == "z":
            ref = side(n, axes, False)
            return [ag_copy(n, ref, axes, k, device(z_=z_at(k))) for k in range(1, zs)]
        ref = side(n, axes, before(n, "z", axis))
        return [ag_copy(n, ref, axes + axis, 0, neighbour(axis))]

    def ag_send_part(n, axes, axis):
        for moved in ag_sends(n, axes, axis):
            moved.start()

    def ag_wait_part(n, axes):
        last = max(axes, key=n.route.index)
        axes = axes.replace("z", "")
        if last == "z":
            yy, xx = (1 - y if "y" in axes else y), (1 - x if "x" in axes else x)
            for k in range(1, zs):
                ag_copy(n, n.u.at[yy, xx, z_at(zs - k), n.rows], axes, k, device()).wait_recv()
        else:
            ag_copy(n, side(n, axes, before(n, "z", last)), axes, 0, device()).wait_recv()
        if n.other is not None and (last == "z" or before(n, "z", last)):
            core_copy(n, side(n, axes, True)).start()

    def ag_done(n):
        if n.other is not None:
            core_copy(n, n.other.at[:, :, :, n.rows]).wait_recv()

    def ag_drain(n):
        for axis in n.route:
            earlier = [other for other in "yx" if before(n, other, axis)]
            for some in range(2 ** len(earlier)):
                axes = "".join(other for bit, other in enumerate(earlier) if some >> bit & 1)
                for moved in ag_sends(n, axes, axis):
                    moved.wait_send()
        if n.other is not None:
            core_copy(n, n.u.at[:, :, :, n.rows]).wait_send()

    AXES = "yxz"

    def rs_groups(n, step):
        axis = n.route[step]
        if axis == "z":
            return [(k, 1 + k, device(z_=z_at(zs - k))) for k in range(1, zs)]
        return [(1, "yx".index(axis), neighbour(axis))]

    def rs_where(n, step, k):
        axis, out, land = n.route[step], [], []
        for other in AXES:
            if other == axis:
                out.append(z_at(zs - k) if axis == "z" else 1 - ME[axis])
                land.append(k)
            elif before(n, other, axis):
                out.append(ME[other])
                land.append(0)
            else:
                out.append(slice(None))
                land.append(slice(None))
        return tuple(out) + (n.rows,), tuple(land) + (n.rows,)

    def rs_copy(n, step, k, slot, to):
        out, land = rs_where(n, step, k)
        return copy(n.u.at[out], n.got.at[land], rs_send.at[n.index, slot], rs_recv.at[n.index, slot], to)

    def rs_core(n):
        return copy(n.other.at[:, :, :, n.rows], n.core_in.at[:, :, :, n.rows], rs_send.at[n.index, zs + 1],
                    rs_recv.at[n.index, zs + 1], device(c_=1 - c))

    def add_terms(n, place, step):
        value = n.u[tuple(place) + (n.rows,)].astype(F32)
        if n.other is not None:
            value = value + n.core_in[tuple(place) + (n.rows,)].astype(F32)
        for axis in n.route[:step]:
            for k in range(1, zs) if axis == "z" else (1,):
                where = [k if other == axis else (0 if before(n, other, axis) else at_place)
                         for other, at_place in zip(AXES, place)]
                value = value + n.got[tuple(where) + (n.rows,)].astype(F32)
        return value

    def rs_start(n):
        rs_core(n).start()

    def rs_step(n, step):
        if step == 0 and n.other is not None:
            rs_core(n).wait_recv()
        if step > 0:
            for group in rs_groups(n, step - 1):
                rs_copy(n, step - 1, *group).wait_recv()
        if step == 3:
            n.total[n.rows, :] = add_terms(n, (y, x, z), 3)
            return
        for k, slot, to in rs_groups(n, step):
            out, _ = rs_where(n, step, k)
            if step > 0 or n.other is not None:
                spans = [range(2) if isinstance(at_place, slice) else (at_place,) for at_place in out[:2]]

                def body(zz):
                    for yy in spans[0]:
                        for xx in spans[1]:
                            n.u[yy, xx, zz, n.rows] = add_terms(n, (yy, xx, zz), step).astype(BF16)

                if isinstance(out[2], slice):
                    loop(zs, body)
                else:
                    body(out[2])
            rs_copy(n, step, k, slot, to).start()

    def rs_drain(n):
        if n.other is not None:
            rs_core(n).wait_send()
        for step in range(3):
            for group in rs_groups(n, step):
                rs_copy(n, step, *group).wait_send()

    def small_sum(ref, slots, which):
        to = (device(y_=1 - y), device(c_=1 - c), device(x_=1 - x))
        to += tuple(device(z_=z_at(k)) for k in range(1, zs))

        def moved(slot):
            return copy(ref, slots.at[slot], v_send.at[which, slot], v_recv.at[which, slot], to[slot])

        def land(last):
            moved(last).wait()
            ref[...] = ref[...] + slots[last]

        def step(n):
            def run():
                if n > 0:
                    land(n - 1)
                moved(n).start()

            return run

        def line():
            land(2)
            for k in range(1, zs):
                moved(2 + k).start()

        def finish():
            for k in range(1, zs):
                moved(2 + k).wait()
            value = ref[...]
            for k in range(1, zs):
                value = value + slots[2 + k]
            ref[...] = value

        return [step(0), step(1), step(2), line, finish]

    def rows_of(s):
        return pl.ds(pl.multiple_of(s * 128, 128), 128)

    def exchange(src, dst, which):
        return [copy(src.at[block_at(k)], dst.at[i], a2a_send.at[which, k - 1],
                     a2a_recv.at[which, k - 1], {"blk": block_at(k), "batch": b})
                for k in range(1, 4)]

    def exchange_landed(dst, which):
        return [copy(dst.at[block_at(4 - k)], dst.at[block_at(4 - k)], a2a_send.at[which, k - 1],
                     a2a_recv.at[which, k - 1], {"blk": block_at(4 - k), "batch": b})
                for k in range(1, 4)]

    def axes_of(mask):
        return "".join(axis for axis, bit in (("y", Y), ("x", X), ("z", Z)) if mask & bit)

    def rows_in(part, count):
        return pl.ds(part * (288 // count), 288 // count)

    units = []
    for unit, routes in enumerate(GATHER_ROUTES):
        half = unit % 2
        ref = (ua, uw1, uw2)[unit // 2]
        pieces = (ref.at[half, c], ref.at[half, 1 - c]) if unit < 2 else (ref.at[half], None)
        for part, route in enumerate(routes):
            units.append(Unit(len(units), "".join(map(axes_of, route)), rows_in(part, len(routes)), *pieces))

    def pair(slot, src, dst):
        return copy(src, dst, pair_send.at[slot], pair_recv.at[slot], device(c_=1 - c))

    w1_swap, w2_swap = pair(0, w1_in, w1_other), pair(1, w2_in, w2_other)

    def each_core(f):
        for q in range(2):
            pl.when(c == q)(functools.partial(f, q))

    def rest_rows(matrix):
        return a_in[matrix, pl.ds(pl.multiple_of(128 * (1 - c), 64), 64), :]

    def own_attention(p):
        mine = ua.at[p, c, y, x, z]
        for m in range(2):
            main = a_in[2 * p + m, pl.ds(pl.multiple_of(64 * c, 64), 128), :]
            mine[96 * m : 96 * m + 96, :] = main.T.astype(BF16)
        rest = jnp.concatenate([rest_rows(2 * p + c), rest_rows(2 * p + 1 - c)], axis=0)
        mine[192:288, :] = rest.T.astype(BF16)

    def own_expand(q):
        both = (w1_in, w1_other) if q == 0 else (w1_other, w1_in)
        cols = slice(192 * q, 192 * q + 192)
        blocks = (
            both[0][0:128, cols],
            jnp.concatenate([both[0][128:192, cols], both[1][0:64, cols]], axis=0),
            both[1][64:192, cols],
        )
        for t, block in enumerate(blocks):
            value = block.T.astype(BF16)
            for h in range(2):
                uw1[h, y, x, z, 96 * t : 96 * t + 96, :] = value[96 * h : 96 * h + 96, :]

    def own_reduce(q):
        both = (w2_in, w2_other) if q == 0 else (w2_other, w2_in)
        for cc in range(2):
            for part_of in range(2):
                start = 384 * part_of + 192 * q
                lines[:, 192 * part_of : 192 * part_of + 192] = both[cc][:, start : start + 192]
            for t in range(3):
                uw2[cc, y, x, z, 96 * t : 96 * t + 96, :] = lines[:, 128 * t : 128 * t + 128].astype(BF16)

    def own_hidden_bias(q):
        for zz in range(zs):
            for xx in range(2):
                col = 384 * (zz % 2) + 192 * xx
                start = 384 * xx + 192 * q
                b1[zz // 2 : zz // 2 + 1, col : col + 192] = vec[8 + zz : 9 + zz, start : start + 192]

    def hidden_bias_gradient(q):
        for zz in range(zs):
            for xx in range(2):
                col = 384 * (zz % 2) + 192 * xx
                start = 384 * xx + 192 * q
                gvec[8 + zz : 9 + zz, start : start + 192] = gb1[zz // 2 : zz // 2 + 1, col : col + 192]

    columns = a_in.shape[2]
    placed = lax.broadcasted_iota(jnp.int32, (columns, 768), 1) == (
        lax.broadcasted_iota(jnp.int32, (columns, 768), 0) + columns * g
    )

    def own_vectors():
        vec[...] = jnp.zeros_like(vec)
        rows = dot_nn(vec_in[...].astype(BF16), jnp.where(placed, 1.0, 0.0).astype(BF16))
        for j in range(3):
            vec[pl.ds(3 * i + j, 1), :] = rows[j : j + 1, :]

    loads = [pltpu.make_async_copy(src, dst, local_sem.at[4 + n]) for n, (src, dst) in enumerate((
        (a_hbm, a_in), (vec_hbm, vec_in), (w1_hbm, w1_in), (w2_hbm, w2_in), (cot, stage), (mask_hbm, mask_in)
    ))]
    load_a, load_vec, load_w1, load_w2, load_cot, load_mask = loads
    for load in loads:
        load.start()

    def masked_cotangent():
        load_cot.wait()
        load_mask.wait()
        eye = lax.broadcasted_iota(jnp.int32, (128, 128), 0) == lax.broadcasted_iota(jnp.int32, (128, 128), 1)
        for s in range(4):
            row = jnp.broadcast_to(mask_in[s : s + 1, :].astype(F32), (128, 128))
            column = jnp.sum(jnp.where(eye, row, 0.0), axis=1, keepdims=True)
            stage[s] = (stage[s].astype(F32) * column).astype(BF16)

    def finish_attention(p):
        value = totals.at[p]
        for m in range(2):
            ga[2 * p + m, pl.ds(pl.multiple_of(64 * c, 64), 128), :] = value[96 * m : 96 * m + 96, :].T
        rest = value[192:288, :].T
        rows = pl.ds(pl.multiple_of(128 * (1 - c), 64), 64)
        ga[2 * p + c, rows, :] = rest[0:64, :]
        ga[2 * p + 1 - c, rows, :] = rest[64:128, :]

    w1_back = pair(6, turned1.at[pl.ds(pl.multiple_of(192 * (1 - c), 64), 192)], got1)
    w2_back = pair(7, totals.at[5 - c], got2)

    def turn_expand():
        for h in range(2):
            for t in range(3):
                turned1[128 * t : 128 * t + 128, 96 * h : 96 * h + 96] = totals[2 + h, 96 * t : 96 * t + 96, :].T
        w1_back.start()

    def join_expand(q):
        g1[:, 192 * q : 192 * q + 192] = turned1[192 * q : 192 * q + 192, :]
        g1[:, 192 * (1 - q) : 192 * (1 - q) + 192] = got1[...]

    def join_reduce(q):
        for half, value in ((q, totals.at[4 + q]), (1 - q, got2)):
            for t in range(3):
                lines[:, 128 * t : 128 * t + 128] = value[96 * t : 96 * t + 96, :]
            for part_of in range(2):
                start = 384 * part_of + 192 * half
                g2[:, start : start + 192] = lines[:, 192 * part_of : 192 * part_of + 192]

    def finish_vectors():
        value, total = gvec[...], 0.0
        for _ in range(3):
            part = value.astype(BF16)
            total = total + dot_nt(part, jnp.where(placed, 1.0, 0.0).astype(BF16))
            value = value - part.astype(F32)
        narrow_rows[...] = total
        for j in range(3):
            gv[j : j + 1, :] = narrow_rows[pl.ds(3 * i + j, 1), :]

    grads, owners = [], []
    for unit, routes in enumerate(SUM_ROUTES):
        half = unit % 2
        ref = (ua, gw1, gw2)[unit // 2]
        pieces = (ref.at[half, c], ref.at[half, 1 - c], core_in.at[half]) if unit < 2 else (ref.at[half], None, None)
        for part, route in enumerate(routes):
            grads.append(Gradient(len(grads), "".join(map(axes_of, route)), rows_in(part, len(routes)), *pieces,
                                  got.at[unit], totals.at[unit]))
            owners.append(unit)

    def summed(unit):
        if unit < 2:
            finish_attention(unit)
        elif unit < 4 and {2, 3} <= set(whole):
            turn_expand()
        elif unit >= 4 and {4, 5} <= set(whole):
            w2_back.start()

    seen, whole = set(), []

    def event(kind, *rest):
        if kind == SEND:
            ag_send_part(units[rest[0]], axes_of(rest[1]), axes_of(rest[2]))
        elif kind == GOT:
            ag_wait_part(units[rest[0]], axes_of(rest[1]))
        elif kind == WHOLE:
            ag_done(units[rest[0]])
        elif kind == SUM:
            rs_step(grads[rest[0]], rest[1])
            if rest[1] == 3:
                seen.add(rest[0])
                unit = owners[rest[0]]
                if all(k in seen for k in range(len(grads)) if owners[k] == unit):
                    whole.append(unit)
                    summed(unit)
        elif kind == DO:
            actions[rest[0]]()
        else:
            (vec_steps if kind == VEC else gvec_steps)[rest[0] + 1]()
            if (kind, rest[0]) == (SMALL, zs - 1):
                finish_vectors()

    def run(part):
        for todo in PLAN.get(part, ()):
            event(*todo)

    def parts(name, count, body):
        run(name + "0")
        hooks = [(k - 1, functools.partial(run, name + str(k))) for k in range(1, count) if name + str(k) in PLAN]
        loop(count, body, hooks)

    def started(copies):
        for moved in copies:
            moved.start()
        return copies

    def arrived(*copies):
        for moved in copies:
            moved.wait_recv()

    own_tokens = pltpu.make_async_copy(tok.at[i], x_in.at[i], local_sem.at[0])
    own_tokens.start()
    own_cot = pltpu.make_async_copy(stage.at[i], cot_in.at[i], local_sem.at[1])
    tokens_out, cot_out = exchange(tok, x_in, 0), exchange(stage, cot_in, 1)
    result_out = exchange(stage, out, 2)
    grad_out = [copy(n1.at[rows_of(block_at(k))], ig.at[i], a2a_send.at[3, k - 1], a2a_recv.at[3, k - 1],
                     {"blk": block_at(k), "batch": b}) for k in range(1, 4)]
    own_out = pltpu.make_async_copy(stage.at[i], out.at[i], local_sem.at[2])
    own_grad = pltpu.make_async_copy(n1.at[rows_of(i)], ig.at[i], local_sem.at[3])
    n2_swap, cot_swap = pair(2, n2, n2_other), pair(3, cot_in, cot_other)
    back_swap, ahead_swap = pair(4, d6, back_in), pair(5, n2, ahead_in)
    vec_steps, gvec_steps = small_sum(vec, vin, 0), small_sum(gvec, gin, 1)

    def tokens_here():
        arrived(*exchange_landed(x_in, 0))
        own_tokens.wait()

    def cotangent_here():
        arrived(*exchange_landed(cot_in, 1))
        own_cot.wait()
        cot_swap.start()

    def swaps_here():
        w1_swap.wait()
        w2_swap.wait()

    actions = {
        TOK: lambda: started(tokens_out),
        COT: lambda: started(cot_out),
        OUT: lambda: started(result_out),
        IG: lambda: started(grad_out),
        TOK_HERE: tokens_here,
        COT_HERE: cotangent_here,
        OUT_HERE: lambda: arrived(*exchange_landed(out, 2)),
        IG_HERE: lambda: arrived(*exchange_landed(ig, 3)),
        SWAP_HERE: swaps_here,
        N2S_HERE: lambda: n2_swap.wait(),
        COTS_HERE: lambda: cot_swap.wait(),
        BACKS_HERE: lambda: back_swap.wait(),
        AHEADS_HERE: lambda: ahead_swap.wait(),
    }

    load_a.wait()
    own_attention(0)
    load_vec.wait()
    own_vectors()
    load_w1.wait()
    load_w2.wait()
    pl.semaphore_wait(barrier, len(partners))
    vec_steps[0]()
    w1_swap.start()
    w2_swap.start()
    run("own1")
    own_attention(1)
    run("ownff")
    each_core(own_expand)
    each_core(own_reduce)
    run("mask")
    masked_cotangent()
    own_cot.start()
    run("ln1")
    each_core(own_hidden_bias)

    def normalise(value):
        centered = value - jnp.mean(value, axis=-1, keepdims=True)
        scale = lax.rsqrt(jnp.mean(centered * centered, axis=-1, keepdims=True) + norm_epsilon)
        return centered * scale, scale

    def first_norm(s):
        unit, _ = normalise(x_in[s].astype(F32))
        n1[rows_of(s), :] = (unit * vec[0:1, :] + vec[1:2, :]).astype(BF16)

    loop(4, first_norm)
    run("unp0")

    lanes = lax.broadcasted_iota(jnp.int32, (96, 128), 1)

    def unpack(p, s):
        for xx in range(2):
            rows = pl.ds(pl.multiple_of((2 * s + xx) * 96, 96), 96)
            for yy in range(2):
                first, second = ua.at[p, 0, yy, xx, s], ua.at[p, 1, yy, xx, s]
                lo, hi = 384 * yy, 384 * yy + 256
                for m in range(2):
                    at[2 * p + m, rows, lo : lo + 128] = first[96 * m : 96 * m + 96, :]
                    at[2 * p + m, rows, hi : hi + 128] = second[96 * m : 96 * m + 96, :]
                rest_first = first[192:288, :].astype(F32)
                rest_second = second[192:288, :].astype(F32)
                even = jnp.where(lanes < 64, rest_first, rest_second)
                odd = pltpu.roll(jnp.where(lanes < 64, rest_second, rest_first), 64, 1)
                at[2 * p, rows, lo + 128 : lo + 256] = even.astype(BF16)
                at[2 * p + 1, rows, lo + 128 : lo + 256] = odd.astype(BF16)

    def project(m, dst, bias):
        for n in range(3):
            value = dot_nt(n1[...], at[m, 256 * n : 256 * n + 256, :])
            if bias is not None:
                value = value + vec[bias : bias + 1, 256 * n : 256 * n + 256]
            value = value.astype(BF16)
            if m == 0:
                value = value * jnp.asarray(HEAD ** (-0.5), BF16)
            dst[2 * n] = value[:, 0:128]
            dst[2 * n + 1] = value[:, 128:256]

    loop(zs, functools.partial(unpack, 0))
    run("projq")
    project(0, q6, 2)
    run("projk")
    project(1, k6, None)

    half_lane = lax.broadcasted_iota(jnp.int32, (512, 128), 1) // HEAD

    def half_of(value, which):
        return jnp.where(half_lane == which, value, jnp.zeros_like(value))

    def turn(value):
        return value.astype(F32).T.astype(BF16)

    def attend(p):
        queries, keys = q6[p], k6[p]
        for which in range(2):
            scores = dot_nt(half_of(keys, which), queries)
            expo = jnp.exp(scores - jnp.max(scores, axis=0, keepdims=True))
            probs = (expo * (1.0 / jnp.sum(expo, axis=0, keepdims=True))).astype(BF16)
            pt[2 * p + which] = probs

    def mix(p):
        values_t = turn(v6[p])
        mixed = [dot_nn(values_t[64 * which : 64 * which + 64, :], pt[2 * p + which]) for which in range(2)]
        o6[p] = jnp.concatenate(mixed, axis=0).T.astype(BF16)

    parts("attend", 6, attend)
    run("unp1")
    loop(zs, functools.partial(unpack, 1))
    run("projv")
    project(2, v6, 3)
    parts("mix", 6, mix)

    run("ao")
    for n in range(3):
        cols = slice(256 * n, 256 * n + 256)
        value = dot_nt(lane_tiles(o6), at[3, cols, :]) + vec[4:5, cols]
        for s in range(4):
            h1[128 * s : 128 * s + 128, cols] = x_in[s, :, cols].astype(F32) + value[128 * s : 128 * s + 128]

    def second_norm(s):
        unit, _ = normalise(h1[rows_of(s), :])
        n2[rows_of(s), :] = (unit * vec[5:6, :] + vec[6:7, :]).astype(BF16)

    run("ln2")
    loop(4, second_norm)
    n2_swap.start()

    def expand_block(s):
        def piece(ref):
            return jnp.concatenate([ref[96 * t : 96 * t + 96, :] for t in range(3)], axis=1)

        return jnp.concatenate(
            [jnp.concatenate([piece(uw1.at[h, yy, xx, 2 * s + zz]) for yy in range(2)], axis=1)
             for zz in range(2) for xx in range(2) for h in range(2)],
            axis=0,
        )

    def reduce_block(s):
        def piece(ref):
            return jnp.concatenate([ref[96 * t : 96 * t + 96, :] for t in range(3)], axis=1)

        return jnp.concatenate(
            [jnp.concatenate([piece(uw2.at[cc, s, xx, zz]) for cc in range(2)], axis=1)
             for zz in range(zs) for xx in range(2)],
            axis=0,
        )

    def block_rows(owner, s):
        return pl.ds(pl.multiple_of((2 * owner + s) * 512, 512), 512)

    def expand(owner, normed, s):
        rows = block_rows(owner, s)
        inner = dot_nt(normed[...], expand_block(s)) + b1[pl.ds(s, 1), :]
        square = inner * inner
        tanh = jnp.tanh(GELU_SCALE * inner * (1.0 + GELU_CUBE * square))
        act[rows, :] = (0.5 * inner * (1.0 + tanh)).astype(BF16)
        slope = 0.5 * (1.0 + tanh) + 0.5 * inner * (1.0 - tanh * tanh) * (
            GELU_SCALE * (1.0 + 3.0 * GELU_CUBE * square)
        )
        gp[rows, :] = slope.astype(BF16)

    parts("expa", 2, functools.partial(expand, 0, n2))
    parts("expb", 2, functools.partial(expand, 1, n2_other))

    gvec[...] = jnp.zeros_like(gvec)

    def transpose_rows(dst, s, value):
        dst[:, 128 * s : 128 * s + 128] = turn(value)

    run("trY")
    total = jnp.zeros((1, 768), F32)
    for s in range(4):
        transpose_rows(ta, s, cot_in[s])
        total = total + jnp.sum(cot_in[s].astype(F32), axis=0, keepdims=True)
    gvec[7:8, :] = total
    for s in range(4):
        transpose_rows(tb, s, cot_other[s])

    def both_rows(ref, s):
        return jnp.concatenate([ref[block_rows(0, s), :], ref[block_rows(1, s), :]], axis=0)

    def reduce_back(s):
        grad = dot_nn(jnp.concatenate([ta[...], tb[...]], axis=1), both_rows(act, s)).astype(BF16)
        for zz in range(zs):
            for xx in range(2):
                row = 96 * (2 * zz + xx)
                for cc in range(2):
                    for t in range(3):
                        col = 384 * cc + 128 * t
                        gw2[cc, s, xx, zz, 96 * t : 96 * t + 96, :] = grad[row : row + 96, col : col + 128]

    parts("gw2_", 2, reduce_back)

    def rows_together(ref):
        return jnp.concatenate([ref[s] for s in range(4)], axis=0)

    def inner_back(owner, cotangent_rows, s):
        rows = block_rows(owner, s)
        grad = dot_nn(rows_together(cotangent_rows), reduce_block(s)) * gp[rows, :].astype(F32)
        low = grad.astype(BF16)
        gp[rows, :] = low
        sums = jnp.sum(low.astype(F32), axis=0, keepdims=True)
        gb1[pl.ds(s, 1), :] = sums if owner == 1 else gb1[pl.ds(s, 1), :] + sums

    def norm_back(owner):
        acc[...] = dot_nn(gp[block_rows(owner, 0), :], expand_block(0))
        acc[...] += dot_nn(gp[block_rows(owner, 1), :], expand_block(1))

    parts("innb", 2, functools.partial(inner_back, 1, cot_other))
    run("dn2b")
    norm_back(1)
    for t in range(6):
        d6[t] = acc[:, 128 * t : 128 * t + 128].astype(BF16)
    back_swap.start()
    parts("inna", 2, functools.partial(inner_back, 0, cot_in))
    each_core(hidden_bias_gradient)
    run("dn2a")
    norm_back(0)

    def expand_back(s):
        turned = jnp.concatenate([turn(gp[block_rows(owner, s), :]) for owner in range(2)], axis=1)
        normed = jnp.concatenate([n2[...], n2_other[...]], axis=0)
        grad = dot_nn(turned, normed).astype(BF16)
        for zz in range(2):
            for xx in range(2):
                for h in range(2):
                    row = 384 * zz + 192 * xx + 96 * h
                    for yy in range(2):
                        for t in range(3):
                            col = 384 * yy + 128 * t
                            gw1[h, yy, xx, 2 * s + zz, 96 * t : 96 * t + 96, :] = grad[
                                row : row + 96, col : col + 128
                            ]

    parts("gw1_", 2, expand_back)
    run("hid")

    def norm_gradient(value, scale_row, grad):
        unit, scale = normalise(value)
        gain_sum = jnp.sum(grad * unit, axis=0, keepdims=True)
        bias_sum = jnp.sum(grad, axis=0, keepdims=True)
        inner = grad * scale_row
        mean = jnp.mean(inner, axis=-1, keepdims=True)
        along = jnp.mean(inner * unit, axis=-1, keepdims=True)
        return scale * (inner - mean - unit * along), gain_sum, bias_sum

    def hidden_back(s):
        rows = rows_of(s)
        grad_in = jnp.concatenate([back_in[t, rows, :] for t in range(6)], axis=1)
        grad_in = acc[rows, :] + grad_in.astype(F32)
        grad, gain_sum, bias_sum = norm_gradient(h1[rows, :], vec[5:6, :], grad_in)
        grad = grad + cot_in[s].astype(F32)
        acc[rows, :] = grad
        low = grad.astype(BF16)
        n2[rows, :] = low
        gvec[5:6, :] += gain_sum
        gvec[6:7, :] += bias_sum
        gvec[4:5, :] += jnp.sum(low.astype(F32), axis=0, keepdims=True)

    loop(4, hidden_back)

    run("dO")
    for n in range(3):
        value = dot_nn(n2[...], at[3, :, 256 * n : 256 * n + 256]).astype(BF16)
        d6[2 * n] = value[:, 0:128]
        d6[2 * n + 1] = value[:, 128:256]
    run("gao")
    for s in range(4):
        transpose_rows(tc, s, n2[128 * s : 128 * s + 128, :])
    gp[768:1536, :] = dot_nn(tc[...], lane_tiles(o6)).astype(BF16)

    def value_back(p):
        grads_in, grad_value = d6[p], 0.0
        for which in range(2):
            grad_value = grad_value + dot_nn(pt[2 * p + which], half_of(grads_in, which))
        tc[rows_of(p), :] = grad_value.T.astype(BF16)
        o6[p] = grad_value.astype(BF16)

    def attend_back(p):
        rows = rows_of(p)
        queries, keys, values, grads_in = q6[p], k6[p], v6[p], d6[p]
        keys_t = turn(keys)
        grad_query, grad_key = [], 0.0
        for which in range(2):
            wide = pt[2 * p + which].astype(F32)
            grad_probs = dot_nt(half_of(values, which), grads_in)
            inner = jnp.sum(wide * grad_probs, axis=0, keepdims=True)
            grad_scores = (wide * (grad_probs - inner)).astype(BF16)
            grad_query.append(dot_nn(keys_t[64 * which : 64 * which + 64, :], grad_scores))
            grad_key = grad_key + dot_nn(grad_scores, half_of(queries, which))
        grad_query = jnp.concatenate(grad_query, axis=0) * HEAD ** (-0.5)
        ta[rows, :] = grad_query.astype(BF16)
        tb[rows, :] = grad_key.T.astype(BF16)
        q6[p] = grad_query.T.astype(BF16)
        k6[p] = grad_key.astype(BF16)

    def pack(p, first_row, second_row):
        def body(s):
            for xx in range(2):
                offset = (2 * s + xx) * 96
                rows = [pl.ds(pl.multiple_of(first_row + offset, 96), 96),
                        pl.ds(pl.multiple_of(second_row + offset, 96), 96)]
                first, second = ua.at[p, 0, :, xx, s], ua.at[p, 1, :, xx, s]
                for yy in range(2):
                    lo, mid, hi = 384 * yy, 384 * yy + 128, 384 * yy + 256
                    for m in range(2):
                        first[yy, 96 * m : 96 * m + 96, :] = gp[rows[m], lo : lo + 128]
                        second[yy, 96 * m : 96 * m + 96, :] = gp[rows[m], hi : hi + 128]
                    even = gp[rows[0], mid : mid + 128].astype(F32)
                    odd = pltpu.roll(gp[rows[1], mid : mid + 128].astype(F32), 64, 1)
                    first[yy, 192:288, :] = jnp.where(lanes < 64, even, odd).astype(BF16)
                    second[yy, 192:288, :] = jnp.where(lanes < 64, odd, even).astype(BF16)

        loop(zs, body)

    parts("av", 6, value_back)
    run("gav")
    for n in units[VO[0] : VO[1] + 1]:
        ag_drain(n)
    gp[0:768, :] = dot_nn(tc[...], n1[...]).astype(BF16)
    pack(1, 0, 768)
    for n in grads[AVO[0] : AVO[1] + 1]:
        rs_start(n)
    parts("ab", 6, attend_back)
    run("gaqk")
    for n in units[QK[0] : QK[1] + 1]:
        ag_drain(n)
    gp[0:768, :] = dot_nn(ta[...], n1[...]).astype(BF16)
    gp[768:1536, :] = dot_nn(tb[...], n1[...]).astype(BF16)
    pack(0, 0, 768)
    for n in grads[AQK[0] : AQK[1] + 1]:
        rs_start(n)

    def reduce(owner):
        value = dot_nt(act[block_rows(owner, 0), :], reduce_block(0))
        return value + dot_nt(act[block_rows(owner, 1), :], reduce_block(1))

    def layer_output():
        run("redb")
        n2[...] = reduce(1).astype(BF16)
        ahead_swap.start()
        run("reda")
        h1[...] = h1[...] + vec[7:8, :] + reduce(0)
        run("outst")
        for moved in cot_out:
            moved.wait_send()
        for s in range(4):
            rows = slice(128 * s, 128 * s + 128)
            stage[s] = (h1[rows, :] + ahead_in[rows, :].astype(F32)).astype(BF16)
        own_out.start()

    layer_output()
    run("dn1")
    h1[...] = dot_nn(lane_tiles(q6), at[0])
    h1[...] += dot_nn(lane_tiles(k6), at[1])
    h1[...] += dot_nn(lane_tiles(o6), at[2])
    gvec[2:3, :] = jnp.sum(lane_tiles(q6).astype(F32), axis=0, keepdims=True)
    gvec[3:4, :] = jnp.sum(lane_tiles(o6).astype(F32), axis=0, keepdims=True)

    run("inb")

    def input_back(s):
        rows = rows_of(s)
        grad, gain_sum, bias_sum = norm_gradient(x_in[s].astype(F32), vec[0:1, :], h1[rows, :])
        n1[rows, :] = (grad + acc[rows, :]).astype(BF16)
        gvec[0:1, :] += gain_sum
        gvec[1:2, :] += bias_sum

    loop(4, input_back)
    gvec_steps[0]()
    own_grad.start()

    def join():
        w1_back.wait()
        each_core(join_expand)
        w2_back.wait()
        each_core(join_reduce)

    joined = False
    for n, todo in enumerate(PLAN["end"]):
        if not joined and n >= len(PLAN["end"]) - 3 and {2, 3, 4, 5} <= set(whole):
            join()
            joined = True
        event(*todo)
    if not joined:
        join()

    own_out.wait()
    own_grad.wait()
    for moved in tokens_out + result_out + grad_out:
        moved.wait_send()
    for n in units[VO[1] + 1 :]:
        ag_drain(n)
    for n in grads:
        rs_drain(n)


def layer(sub, tokens, cotangent, span_mask, vectors, attention, expand, reduce_t):
    zs = GROUPS // 2
    seqs, block, width = tokens.shape
    rows = seqs * block
    columns = attention.shape[2]
    piece = (3 * columns, 128)
    vmem = lambda shape, dtype: pltpu.VMEM(shape, dtype)
    half = (2, 2, 2, zs) + piece
    scratch = [vmem(value.shape, value.dtype) for value in (span_mask, vectors, attention, expand, reduce_t)]
    scratch += [vmem((2,) + half, BF16)] + [vmem(half, BF16)] * 4
    scratch += [vmem((2, 2, 2, zs) + piece, BF16), vmem((6, 2, 2, zs) + piece, BF16)]
    scratch += [vmem(tokens.shape, BF16)] * 3
    scratch += [vmem((16, width), F32)] * 2
    scratch += [vmem((zs + 2, 16, width), F32)] * 2
    scratch += [vmem((16, columns), F32)]
    tiles = vmem((width // 128, rows, 128), BF16)
    flat = vmem((rows, width), BF16)
    turned = vmem((width, rows), BF16)
    scratch += [vmem((4, width, width), BF16), flat, tiles, tiles, tiles, tiles]
    scratch += [vmem((HEADS, rows, rows), BF16), vmem((rows, width), F32), vmem((rows, width), F32)]
    scratch += [flat, vmem((4 * rows, width), BF16), vmem((4 * rows, width), BF16)]
    scratch += [turned, turned, turned, tiles]
    scratch += [vmem(expand.shape, F32), vmem(reduce_t.shape, F32), flat, vmem(tokens.shape, BF16)]
    scratch += [tiles, flat, vmem((columns, width // 2), F32), vmem((2, width), F32), vmem((2, width), F32)]
    scratch += [vmem((6,) + piece, F32), vmem((width // 2, 2 * columns), F32)]
    scratch += [vmem((2 * columns, 2 * columns), F32), vmem(piece, F32)]
    scratch += [pltpu.SemaphoreType.DMA((10,))]
    gathered, summed = sum(map(len, GATHER_ROUTES)), sum(map(len, SUM_ROUTES))
    scratch += [pltpu.SemaphoreType.DMA((gathered, 4 * zs))] * 2
    scratch += [pltpu.SemaphoreType.DMA((gathered,))] * 2
    scratch += [pltpu.SemaphoreType.DMA((summed, zs + 2))] * 2
    scratch += [pltpu.SemaphoreType.DMA((4, 3))] * 2
    scratch += [pltpu.SemaphoreType.DMA((2, zs + 2))] * 2
    scratch += [pltpu.SemaphoreType.DMA((8,))] * 2
    in_vmem = pl.BlockSpec(memory_space=pltpu.VMEM)
    anywhere = pl.BlockSpec(memory_space=pl.ANY)
    return pl.pallas_call(
        functools.partial(kernel, sub, zs),
        out_shape=(
            jax.ShapeDtypeStruct(tokens.shape, BF16),
            jax.ShapeDtypeStruct(tokens.shape, BF16),
            jax.ShapeDtypeStruct(attention.shape, F32),
            jax.ShapeDtypeStruct(expand.shape, F32),
            jax.ShapeDtypeStruct(reduce_t.shape, F32),
            jax.ShapeDtypeStruct(vectors.shape, F32),
        ),
        in_specs=[anywhere] * 7,
        out_specs=(anywhere, anywhere) + (in_vmem,) * 4,
        scratch_shapes=scratch,
        compiler_params=pltpu.CompilerParams(
            collective_id=0, has_side_effects=True, vmem_limit_bytes=65400 * 1024
        ),
    )(tokens, cotangent, span_mask, vectors, attention, expand, reduce_t)


def update_kernel(rates, *refs):
    count = len(rates)
    ins, (result, grad) = refs[: 4 * count], refs[4 * count : 4 * count + 2]
    outs, (result_out, grad_out) = refs[4 * count + 2 : 7 * count + 2], refs[7 * count + 2 : 7 * count + 4]
    held, (low, wide, passed) = refs[7 * count + 4 : 11 * count + 4], refs[11 * count + 4 : 11 * count + 7]
    in_sems, out_sems = refs[11 * count + 7 :]
    loads = [pltpu.make_async_copy(ins[n], held[n], in_sems.at[n]) for n in range(4 * count)]
    stores = [pltpu.make_async_copy(held[4 * n + m], outs[3 * n + m], out_sems.at[3 * n + m])
              for n in range(count) for m in range(3)]
    load_grad = pltpu.make_async_copy(grad, low, in_sems.at[4 * count])
    store_grad = pltpu.make_async_copy(wide, grad_out, out_sems.at[3 * count])
    load_result = pltpu.make_async_copy(result, passed, in_sems.at[4 * count + 1])
    store_result = pltpu.make_async_copy(passed, result_out, out_sems.at[3 * count + 1])
    load_grad.start()
    load_result.start()
    for copy in loads:
        copy.start()
    load_result.wait()
    store_result.start()
    load_grad.wait()

    def widen(s, carry):
        wide[s] = low[s].astype(F32)
        return carry

    lax.fori_loop(0, low.shape[0], widen, 0)
    store_grad.start()
    for n in range(count):
        for m in range(4):
            loads[4 * n + m].wait()
        weight, one, two, gradient = held[4 * n : 4 * n + 4]
        values = adamw(weight[...], one[...], two[...], gradient[...], rates[n])
        for ref, value in zip((weight, one, two), values):
            ref[...] = value
        for m in range(3):
            stores[3 * n + m].start()
    for copy in stores + [store_grad, store_result]:
        copy.wait()


def update(rates, arrays, result, grad):
    flat = [value for group in arrays for value in group]
    new = [jax.ShapeDtypeStruct(value.shape, F32) for group in arrays for value in group[:3]]
    new += [jax.ShapeDtypeStruct(result.shape, BF16), jax.ShapeDtypeStruct(grad.shape, F32)]
    anywhere = pl.BlockSpec(memory_space=pl.ANY)
    scratch = [pltpu.VMEM(value.shape, F32) for value in flat]
    scratch += [pltpu.VMEM(grad.shape, BF16), pltpu.VMEM(grad.shape, F32), pltpu.VMEM(result.shape, BF16)]
    scratch += [pltpu.SemaphoreType.DMA((len(flat) + 2,)), pltpu.SemaphoreType.DMA((len(new),))]
    return pl.pallas_call(
        functools.partial(update_kernel, rates),
        out_shape=tuple(new),
        in_specs=[anywhere] * (len(flat) + 2),
        out_specs=(anywhere,) * len(new),
        scratch_shapes=scratch,
        compiler_params=pltpu.CompilerParams(vmem_limit_bytes=63 * 1024 * 1024),
    )(*flat, result, grad)


def local(
    sub,
    tokens,
    cotangent,
    span_mask,
    attention_weight,
    expand_weight,
    reduce_weight,
    vectors,
    attention_first,
    attention_second,
    expand_first,
    expand_second,
    reduce_first,
    reduce_second,
    vector_first,
    vector_second,
):
    together = [[n * sub + m for m in range(sub)] for n in range(GROUPS)]

    def widen(value, axis):
        if sub == 1:
            return value
        low = lax.all_gather(
            value.astype(BF16), "batch", axis=axis, tiled=True, axis_index_groups=together
        )
        return low.astype(F32)

    def narrow(value, axis):
        if sub == 1:
            return value
        return lax.psum_scatter(
            value, "batch", scatter_dimension=axis, tiled=True, axis_index_groups=together
        )

    out_tokens, input_grad, ga, g1, g2, gv = layer(
        sub,
        tokens,
        cotangent,
        span_mask,
        widen(vectors, 1),
        widen(attention_weight, 2),
        widen(expand_weight, 1),
        widen(reduce_weight.T, 0),
    )
    arrays = (
        (attention_weight, attention_first, attention_second, narrow(ga, 2)),
        (expand_weight, expand_first, expand_second, narrow(g1, 1)),
        (reduce_weight.T, reduce_first.T, reduce_second.T, narrow(g2, 0)),
        (vectors, vector_first, vector_second, narrow(gv, 1)),
    )
    rates = (rate_attention, rate_expand, rate_reduce, rate_vector)
    new = update(rates, arrays, out_tokens, input_grad)
    return new[-2:] + new[0:6] + tuple(value.T for value in new[6:9]) + new[9:12]


def solution(mesh):
    sub = mesh.shape["batch"] // GROUPS
    sequences = P("batch", "blk", None)
    attention = P(None, "blk", "batch")
    matrix = P("blk", "batch")
    return jax.shard_map(
        functools.partial(local, sub),
        mesh=mesh,
        in_specs=(sequences, sequences, P("batch", "blk"), attention, matrix, matrix, matrix)
        + (attention,) * 2
        + (matrix,) * 6,
        out_specs=(sequences,) * 2 + (attention,) * 3 + (matrix,) * 9,
        check_vma=False,
    )
```
